32 devices in a mesh: dp: 8 (over z, core), tensor: 4 (over y, x).
Axes of the slice: x: 2, y: 2, z: 4, core: 2. Of those that a mesh axis runs over, the one named last changes fastest.
Arguments:
- tokens: bfloat16 [8192, 2560], P(('dp', 'tensor')), may hold values from -6 to 6
- segments: int32 [8192], P(('dp', 'tensor')), may hold values from 0 to 15, never falling along the last dimension, each value on 1 to 2048 neighbouring positions
- cotangent: bfloat16 [8192, 2560], P(('dp', 'tensor')), may hold values from -6 to 6
- norm_gain: float32 [2560], replicated, may hold values from 0.25 to 1.75
- w_y: bfloat16 [2560, 2560], P('dp', 'tensor'), may hold values from -0.125 to 0.125
- w_x: bfloat16 [2560, 2560], P('dp', 'tensor'), may hold values from -0.125 to 0.125
- conv_w: float32 [4, 2560], replicated, may hold values from -3 to 3
- gate_w: bfloat16 [2, 10, 256, 256], replicated, may hold values from -0.375 to 0.375
- decay_param: float32 [2560], replicated, may hold values from -8.5 to 0.5
- w_out: bfloat16 [2560, 2560], P('dp', 'tensor'), may hold values from -0.125 to 0.125
- mlp_gain: float32 [2560], replicated, may hold values from 0.25 to 1.75
- w_gate: bfloat16 [2560, 7680], P('dp', 'tensor'), may hold values from -0.125 to 0.125
- w_up: bfloat16 [2560, 7680], P('dp', 'tensor'), may hold values from -0.125 to 0.125
- w_down: bfloat16 [2560, 7680], P('dp', 'tensor'), may hold values from -0.0625 to 0.0625
Outputs:
- mixed: bfloat16 [8192, 2560], P(('dp', 'tensor'))
- grad_input: float32 [8192, 2560], P(('dp', 'tensor'))
- grad_norm_gain: float32 [2560], replicated
- grad_w_y: float32 [2560, 2560], P('dp', 'tensor')
- grad_w_x: float32 [2560, 2560], P('dp', 'tensor')
- grad_conv_w: float32 [4, 2560], replicated
- grad_gate_w: float32 [2, 10, 256, 256], replicated
- grad_decay_param: float32 [2560], replicated
- grad_w_out: float32 [2560, 2560], P('dp', 'tensor')
- grad_mlp_gain: float32 [2560], replicated
- grad_w_gate: float32 [2560, 7680], P('dp', 'tensor')
- grad_w_up: float32 [2560, 7680], P('dp', 'tensor')
- grad_w_down: float32 [2560, 7680], P('dp', 'tensor')
The draws below stay inside these ranges and needn't reach their ends.
Inputs may be any that keep to these rules, and one draw needn't show every extreme that they name: `segments`: segment numbers never fall along the tokens and a document holds at most 2048 tokens; the recurrence and the convolution also start afresh every 1024 tokens.
All inputs are finite; a program needn't handle non-finite values.
Results may differ from the reference program's by a relative error of at most 0.0095.
Values may be sent and summed in bfloat16 or wider, within the bound.
A program may use at most 384 MiB of HBM per device.

```python
import math
import jax
import jax.numpy as jnp
import numpy as np
from jax import lax

D = 2560
FF = 7680
NB = 10
BS = 256
CONV = 4
LEN = 1024
L = 2560
TOKENS = 8192
N_DP = 8


def block_levels(stream_key, dims, pieces, least, top_value):
    factor_of, own = 1.0, jax.random.fold_in(stream_key, 6)
    for position, shards_of in pieces:
        heights = jnp.exp(jax.random.uniform(jax.random.fold_in(own, position), (shards_of,), jnp.float32, least / len(pieces), top_value / len(pieces)))
        factor_of = factor_of * jnp.repeat(heights, dims[position] // shards_of).reshape([-1 if axis == position else 1 for axis in range(len(dims))])
    return factor_of


def profile(amount, total, limit, lean):
    weights = [(1 << 20) // math.isqrt(rank ** lean) + 1 for rank in range(2, amount + 1)]
    spare, given = total - limit - (amount - 1), [1] * (amount - 1)
    while spare > 0:
        free = [i for i in range(amount - 1) if given[i] < limit]
        mass, remaining = sum([weights[i] for i in free]), spare
        for i in free:
            extra = min(limit - given[i], max(1, remaining * weights[i] // mass), spare)
            given[i] = given[i] + extra
            spare = spare - extra
    return np.array([limit] + given)


def ragged_sizes(stream_key, amount, total, limit, slope):
    if amount == 2:
        one = jax.random.randint(stream_key, (), max(1, total - limit), min(limit, total - 1) + 1)
        return jnp.stack([one, total - one])
    tallies = jnp.asarray(profile(amount, total, limit, slope), jnp.int32)
    couples = (amount - 1) // 2
    giver, receiver = tallies[1:1 + 2 * couples:2], tallies[2:2 + 2 * couples:2]
    slack = jnp.minimum(giver - 1, limit - receiver)
    shifted = jax.random.randint(jax.random.fold_in(stream_key, 1), (couples,), 0, 1 << 20) % (slack + 1)
    tallies = tallies.at[1:1 + 2 * couples:2].set(giver - shifted).at[2:2 + 2 * couples:2].set(receiver + shifted)
    return tallies[jax.random.permutation(jax.random.fold_in(stream_key, 2), amount)]


def bell_draw(rng, dims, spread, bound, pieces=(), kind=jnp.bfloat16):
    level = block_levels(rng, dims, pieces, -0.22, 0.18) if pieces else 1.0
    drawn = jax.random.normal(rng, dims, jnp.float32) * spread * level
    return jnp.minimum(jnp.maximum(drawn, -bound), bound).astype(kind)


def setup_inputs(seed: int = 0) -> dict:
    keys = jax.random.split(jax.random.key(seed), 15)
    return {
        "tokens": bell_draw(keys[0], (TOKENS, D), 1.0, 6.0, ((0, 32),)),
        "segments": jnp.searchsorted(jnp.cumsum(ragged_sizes(keys[1], 2 * TOKENS // LEN, TOKENS, 2 * LEN, 1)), jnp.arange(TOKENS), side="right").astype(jnp.int32),
        "cotangent": bell_draw(keys[2], (TOKENS, D), 1.0, 6.0, ((0, 32),)),
        "norm_gain": jnp.clip(1.0 + 0.15 * jax.random.normal(keys[3], (D,), jnp.float32), 0.25, 1.75),
        "w_y": bell_draw(keys[4], (D, L), D ** -0.5, 0.125, ((0, 8), (1, 4))),
        "w_x": bell_draw(keys[5], (D, L), D ** -0.5, 0.125, ((0, 8), (1, 4))),
        "conv_w": bell_draw(keys[6], (CONV, L), CONV ** -0.5, 3.0, (), jnp.float32),
        "gate_w": bell_draw(keys[7], (2, NB, BS, BS), BS ** -0.5, 0.375),
        "decay_param": jnp.clip(jax.random.uniform(keys[8], (L,), jnp.float32, -8.5, 0.5), -8.5, 0.5),
        "w_out": bell_draw(keys[9], (D, L), L ** -0.5, 0.125, ((0, 8), (1, 4))),
        "mlp_gain": jnp.clip(1.0 + 0.15 * jax.random.normal(keys[10], (D,), jnp.float32), 0.25, 1.75),
        "w_gate": bell_draw(keys[11], (D, FF), D ** -0.5, 0.125, ((0, 8), (1, 4))),
        "w_up": bell_draw(keys[12], (D, FF), D ** -0.5, 0.125, ((0, 8), (1, 4))),
        "w_down": bell_draw(keys[13], (D, FF), FF ** -0.5, 0.0625, ((0, 8), (1, 4))),
    }


@jax.custom_vjp
def low(v):
    return lax.optimization_barrier(v.astype(jnp.bfloat16)).astype(jnp.float32)

@jax.custom_vjp
def low_back(v):
    return v

def low_keep(v):
    return (low(v), None)

def low_pass(kept, grad):
    return (grad,)

def back_keep(v):
    return (v, None)

def back_low(kept, grad):
    return (low(grad),)
low.defvjp(low_keep, low_pass)
low_back.defvjp(back_keep, back_low)
EPSILON = 1e-06

def matmul(left, right):
    return jnp.dot(left, right, precision=lax.Precision.HIGHEST, preferred_element_type=jnp.float32)

def rms_norm(values, gain):
    return values * lax.rsqrt(lax.optimization_barrier(jnp.mean(values * values, axis=-1, keepdims=True)) + EPSILON) * gain

def doc_layout(seg_ids, seq_len):
    places = jnp.arange(seg_ids.shape[0], dtype=jnp.int32)
    before = jnp.concatenate([seg_ids[:1], seg_ids[:-1]])
    resets = (places % seq_len == 0) | (seg_ids != before)
    starts = lax.cummax(jnp.where(resets, places, jnp.zeros_like(places)), axis=0)
    return (resets, starts)

def causal_conv(values, kernel, starts):
    places = jnp.arange(values.shape[0], dtype=jnp.int32)
    total = values * kernel[0]
    for offset_k in range(1, kernel.shape[0]):
        moved = jnp.concatenate([jnp.zeros((offset_k, values.shape[1]), values.dtype), values[:-offset_k]], axis=0)
        valid = (places - offset_k >= starts)[:, None]
        total = total + jnp.where(valid, moved, jnp.zeros_like(moved)) * kernel[offset_k]
    return total

def linear_scan(decays, inputs):

    def advance(state, pair):
        state = pair[0] * state + pair[1]
        return (state, state)
    _, states = lax.scan(advance, jnp.zeros(decays.shape[1:], decays.dtype), (decays, inputs))
    return states

def recurrence(conv_out, gate_a, gate_x, branch_y, decay_param, resets):
    sig_a = jax.nn.sigmoid(gate_a)
    sig_x = jax.nn.sigmoid(gate_x)
    log_decay = -8.0 * sig_a * jax.nn.softplus(decay_param)
    fresh = resets[:, None]
    decays = jnp.where(fresh, jnp.zeros_like(log_decay), jnp.exp(log_decay))
    scale = jnp.where(fresh, jnp.ones_like(log_decay), jnp.sqrt(-jnp.expm1(2.0 * log_decay)))
    states = linear_scan(decays, conv_out * sig_x * scale)
    return states * jax.nn.gelu(branch_y, approximate=True)

def layer(resid, norm_gain, w_y, w_x, conv_w, gate_w, decay_param, w_out, mlp_gain, w_gate, w_up, w_down, resets, starts):
    row_count = resid.shape[0]
    normed = low(rms_norm(resid, norm_gain))
    branch_y = low_back(matmul(normed, w_y))
    branch_x = low_back(matmul(normed, w_x))
    conv_out = low(causal_conv(branch_x, conv_w, starts))
    grouped = conv_out.reshape(row_count, gate_w.shape[1], gate_w.shape[2])
    gate_pre = jnp.einsum('tnk,snkj->stnj', grouped, gate_w, precision=lax.Precision.HIGHEST)
    gate_pre = low_back(gate_pre.reshape(2, row_count, gate_w.shape[1] * gate_w.shape[3]))
    mixed_in = low(recurrence(conv_out, gate_pre[0], gate_pre[1], branch_y, decay_param, resets))
    mixer = low_back(matmul(mixed_in, w_out.T))
    middle = resid + mixer
    normed_mid = low(rms_norm(middle, mlp_gain))
    gate_val = low_back(matmul(normed_mid, w_gate))
    up_val = low_back(matmul(normed_mid, w_up))
    hidden = low(jax.nn.gelu(gate_val, approximate=True) * up_val)
    return middle + low_back(matmul(hidden, w_down.T))

def reference(tokens, segments, cotangent, norm_gain, w_y, w_x, conv_w, gate_w, decay_param, w_out, mlp_gain, w_gate, w_up, w_down):
    params = tuple((weight.astype(jnp.float32) for weight in (norm_gain, w_y, w_x, conv_w, gate_w, decay_param, w_out, mlp_gain, w_gate, w_up, w_down)))
    group_rows = TOKENS // N_DP
    tok_groups = tokens.reshape(N_DP, group_rows, D)
    seg_groups = segments.reshape(N_DP, group_rows)
    cot_groups = cotangent.reshape(N_DP, group_rows, D)

    def one_group(totals, item):
        resid, seg_ids, cot_rows = item
        resets, starts = doc_layout(seg_ids, LEN)

        def forward(resid_in, *weights):
            return layer(resid_in, *weights, resets, starts)
        result, pullback = jax.vjp(forward, resid.astype(jnp.float32), *params)
        grads = pullback(cot_rows.astype(jnp.float32))
        totals = tuple((acc + part for acc, part in zip(totals, grads[1:])))
        return (totals, (result.astype(jnp.bfloat16), grads[0]))
    zeros = tuple((jnp.zeros(weight.shape, jnp.float32) for weight in params))
    totals, outputs = lax.scan(one_group, zeros, (tok_groups, seg_groups, cot_groups))
    mixed = outputs[0].reshape(TOKENS, D)
    grad_input = outputs[1].reshape(TOKENS, D)
    return (mixed, grad_input, totals[0], totals[1], totals[2], totals[3], totals[4], totals[5], totals[6], totals[7], totals[8], totals[9], totals[10])
```

```python
from functools import partial

import jax
import jax.numpy as jnp
from jax import lax
from jax.experimental import pallas as pl
from jax.experimental.pallas import tpu as pltpu
from jax.sharding import PartitionSpec as P

EPSILON = 1e-06
MESH = pl.DeviceIdType.MESH
VMEM_BYTES = 56 * 1024 * 1024
CHUNK = 16
F32 = jnp.float32
BF16 = jnp.bfloat16


def subsets(bits):
    found = [()]
    for bit in bits:
        found = found + [chosen + (bit,) for chosen in found]
    return found


def flipped(index, bits):
    for bit in bits:
        mine = (index // (1 << bit)) % 2
        index = index + (1 - 2 * mine) * (1 << bit)
    return index


def log2_of(count):
    assert count & (count - 1) == 0
    return count.bit_length() - 1


def greet(axis_bits):
    barrier = pltpu.get_barrier_semaphore()
    for axis, bit in axis_bits:
        peer = flipped(lax.axis_index(axis), (bit,))
        pl.semaphore_signal(barrier, inc=1, device_id={axis: peer}, device_id_type=MESH)
    pl.semaphore_wait(barrier, len(axis_bits))


def halves_of(nbits, columns):
    half = columns // 2
    ups = tuple(range(nbits))
    return ((ups, 0, half), (ups[::-1], half, half))


class Gather:
    def __init__(self, ref, rows, nbits, send_sems, recv_sems):
        self.ref, self.rows, self.nbits = ref, rows, nbits
        self.sems = (send_sems, recv_sems)
        self.me = lax.axis_index("tensor")
        self.plan = []
        number = 0
        for half, (order, at, width) in enumerate(halves_of(nbits, ref.shape[1])):
            for step, bit in enumerate(order):
                for known in subsets(order[:step]):
                    self.plan.append((half, step, known, bit, at, width, number))
                    number += 1
        self.count = number

    def copy(self, item):
        half, step, known, bit, at, width, number = item
        row = pl.multiple_of(flipped(self.me, known) * self.rows, self.rows)
        piece = self.ref.at[pl.ds(row, self.rows), pl.ds(at, width)]
        return pltpu.make_async_remote_copy(
            src_ref=piece,
            dst_ref=piece,
            send_sem=self.sems[0].at[number],
            recv_sem=self.sems[1].at[number],
            device_id={"tensor": flipped(self.me, (bit,))},
            device_id_type=MESH,
        )

    def ready(self, known_of):
        pass

    def begin(self):
        for item in sorted(self.plan, key=lambda it: it[1]):
            if item[2] == ():
                self.copy(item).start()

    def finish(self):
        arrived = sorted(self.plan, key=lambda it: (it[1], it[0]))
        for item in arrived:
            half, step, known, bit, at, width, number = item
            self.copy(item).wait_recv()
            block = known + (bit,)
            for later in self.plan:
                if later[0] == half and set(later[2]) == set(block):
                    self.copy(later).start()
        for item in self.plan:
            self.copy(item).wait_send()


def gather_copies(nbits):
    return 2 * ((1 << nbits) - 1)


class Scatter:
    def __init__(self, ref, landed, staged, rows, nbits, send_sems, recv_sems):
        self.ref, self.landed, self.staged = ref, landed, staged
        self.rows, self.nbits = rows, nbits
        self.sems = (send_sems, recv_sems)
        self.me = lax.axis_index("tensor")
        self.plan = []
        number = 0
        for half, (order, at, width) in enumerate(halves_of(nbits, ref.shape[1])):
            for step, bit in enumerate(order):
                for rest in subsets(order[step + 1 :])[::-1]:
                    self.plan.append((half, step, rest, bit, at, width, number))
                    number += 1

    def copy(self, item):
        half, step, rest, bit, at, width, number = item
        if step == 0:
            row = pl.multiple_of(flipped(self.me, rest + (bit,)) * self.rows, self.rows)
            source = self.ref.at[pl.ds(row, self.rows), pl.ds(at, width)]
        else:
            source = self.staged.at[number]
        return pltpu.make_async_remote_copy(
            src_ref=source,
            dst_ref=self.landed.at[number],
            send_sem=self.sems[0].at[number],
            recv_sem=self.sems[1].at[number],
            device_id={"tensor": flipped(self.me, (bit,))},
            device_id_type=MESH,
        )

    def begin(self):
        for item in sorted(self.plan, key=lambda it: (len(it[2]) == 0)):
            if item[1] == 0:
                self.copy(item).start()

    def parts_of(self, half, block, before):
        return [
            it[6]
            for it in self.plan
            if it[0] == half and it[1] < before and set(it[2]) == set(block)
        ]

    def partial_sum(self, half, block, before, row, size):
        at, width = [(o[1], o[2]) for o in halves_of(self.nbits, self.ref.shape[1])][half]
        base = pl.multiple_of(flipped(self.me, block) * self.rows + row, size)
        total = self.ref[pl.ds(base, size), pl.ds(at, width)].astype(F32)
        for number in self.parts_of(half, block, before):
            total = total + self.landed[number, pl.ds(row, size), :].astype(F32)
        return total

    def run(self):
        for step in range(self.nbits):
            for half in range(2):
                mine = [it for it in self.plan if it[0] == half and it[1] == step]
                for item in mine:
                    self.copy(item).wait_recv()
                for item in self.plan:
                    if item[0] == half and item[1] == step + 1:
                        block = item[2] + (item[3],)

                        def fill(i, carry, item=item, block=block, half=half):
                            row = pl.multiple_of(i * CHUNK, CHUNK)
                            value = self.partial_sum(half, block, item[1], row, CHUNK)
                            self.staged[item[6], pl.ds(row, CHUNK), :] = value.astype(BF16)
                            return carry

                        lax.fori_loop(0, self.rows // CHUNK, fill, 0)
                        self.copy(item).start()

    def total(self, row, size):
        return jnp.concatenate(
            [self.partial_sum(half, (), self.nbits, row, size) for half in range(2)], axis=1
        )

    def drain(self):
        for item in self.plan:
            self.copy(item).wait_send()


def scatter_scratch(rows, columns, nbits):
    copies = gather_copies(nbits)
    return [
        pltpu.VMEM((copies, rows, columns // 2), BF16),
        pltpu.VMEM((copies, rows, columns // 2), BF16),
        pltpu.SemaphoreType.DMA((copies,)),
        pltpu.SemaphoreType.DMA((copies,)),
    ]


def gather_sems(nbits):
    copies = gather_copies(nbits)
    return [pltpu.SemaphoreType.DMA((copies,)), pltpu.SemaphoreType.DMA((copies,))]


def tensor_bits(nbits):
    return [("tensor", bit) for bit in range(nbits)]


def rms_scale_of(values):
    return lax.rsqrt(jnp.mean(values * values, axis=-1, keepdims=True) + EPSILON)


def chunks(rows, body):
    def step(i, carry):
        body(pl.multiple_of(i * CHUNK, CHUNK))
        return carry

    lax.fori_loop(0, rows // CHUNK, step, 0)


def own_row(row, rows):
    return pl.multiple_of(lax.axis_index("tensor") * rows + row, CHUNK)


def enter_kernel(
    nbits, tokens, cot, seg, gain, normed_all, cot_all, seg_all, s0, r0, s1, r1, s2, r2, l0
):
    rows = tokens.shape[0]
    me = lax.axis_index("tensor")
    peers = [chosen for chosen in subsets(tuple(range(nbits))) if chosen]
    barrier = pltpu.get_barrier_semaphore()
    for chosen in peers:
        pl.semaphore_signal(
            barrier, inc=1, device_id={"tensor": flipped(me, chosen)}, device_id_type=MESH
        )

    def norm(row):
        values = tokens[pl.ds(row, CHUNK), :].astype(F32)
        scaled = values * rms_scale_of(values) * gain[...]
        normed_all[pl.ds(own_row(row, rows), CHUNK), :] = scaled.astype(BF16)

    chunks(rows, norm)
    cot_own = cot_all.at[pl.ds(pl.multiple_of(me * rows, rows), rows), :]
    local = pltpu.make_async_copy(cot, cot_own, l0.at[0])
    local.start()
    seg_own = pltpu.make_async_copy(seg, seg_all.at[me], l0.at[1])
    seg_own.start()
    pl.semaphore_wait(barrier, len(peers))
    seg_copies = [
        pltpu.make_async_remote_copy(
            src_ref=seg,
            dst_ref=seg_all.at[me],
            send_sem=s2.at[number],
            recv_sem=r2.at[number],
            device_id={"tensor": flipped(me, chosen)},
            device_id_type=MESH,
        )
        for number, chosen in enumerate(peers)
    ]
    for copy in seg_copies:
        copy.start()
    first = Gather(normed_all, rows, nbits, s0, r0)
    second = Gather(cot_all, rows, nbits, s1, r1)
    first.begin()
    local.wait()
    second.begin()
    first.finish()
    second.finish()
    for copy in seg_copies:
        copy.wait()
    seg_own.wait()


def middle_kernel(
    nbits, mixer, tokens, gain, middle, mid_all, landed, staged, s0, r0, s1, r1
):
    rows = tokens.shape[0]
    greet(tensor_bits(nbits))
    scatter = Scatter(mixer, landed, staged, rows, nbits, s0, r0)
    scatter.begin()
    scatter.run()

    def norm(row):
        values = tokens[pl.ds(row, CHUNK), :].astype(F32) + scatter.total(row, CHUNK)
        middle[pl.ds(row, CHUNK), :] = values
        scaled = values * rms_scale_of(values) * gain[...]
        mid_all[pl.ds(own_row(row, rows), CHUNK), :] = scaled.astype(BF16)

    chunks(rows, norm)
    gather = Gather(mid_all, rows, nbits, s1, r1)
    gather.begin()
    gather.finish()
    scatter.drain()


def result_kernel(nbits, ffn, middle, mixed, landed, staged, s0, r0):
    rows = middle.shape[0]
    greet(tensor_bits(nbits))
    scatter = Scatter(ffn, landed, staged, rows, nbits, s0, r0)
    scatter.begin()
    scatter.run()

    def add(row):
        values = middle[pl.ds(row, CHUNK), :] + scatter.total(row, CHUNK)
        mixed[pl.ds(row, CHUNK), :] = values.astype(BF16)

    chunks(rows, add)
    scatter.drain()


def norm_pull(values, gain, cotangent):
    scale = rms_scale_of(values)
    unit = values * scale
    inner = cotangent * gain
    back = scale * (inner - unit * jnp.mean(inner * unit, axis=-1, keepdims=True))
    return back, cotangent * unit


def eight_rows(values):
    total = values[0:8]
    for at in range(8, CHUNK, 8):
        total = total + values[at : at + 8]
    return total


def turn_kernel(
    nbits, d_norm, cot, middle, gain, d_middle, d_mixer, d_gain, landed, staged, s0, r0, s1, r1
):
    rows = middle.shape[0]
    greet(tensor_bits(nbits))
    scatter = Scatter(d_norm, landed, staged, rows, nbits, s0, r0)
    scatter.begin()
    d_gain[...] = jnp.zeros_like(d_gain)
    scatter.run()

    def pull(row):
        span = pl.ds(row, CHUNK)
        back, gains = norm_pull(middle[span, :], gain[...], scatter.total(row, CHUNK))
        values = cot[span, :].astype(F32) + back
        d_middle[span, :] = values
        d_mixer[pl.ds(own_row(row, rows), CHUNK), :] = values.astype(BF16)
        d_gain[...] += eight_rows(gains)

    chunks(rows, pull)
    gather = Gather(d_mixer, rows, nbits, s1, r1)
    gather.begin()
    gather.finish()
    scatter.drain()


def leave_kernel(
    nbits, d_norm, tokens, d_middle, gain, grad_input, d_gain, landed, staged, s0, r0
):
    rows = tokens.shape[0]
    greet(tensor_bits(nbits))
    scatter = Scatter(d_norm, landed, staged, rows, nbits, s0, r0)
    scatter.begin()
    d_gain[...] = jnp.zeros_like(d_gain)
    scatter.run()

    def pull(row):
        span = pl.ds(row, CHUNK)
        values = tokens[span, :].astype(F32)
        back, gains = norm_pull(values, gain[...], scatter.total(row, CHUNK))
        grad_input[span, :] = d_middle[span, :] + back
        d_gain[...] += eight_rows(gains)

    chunks(rows, pull)
    scatter.drain()


def sum_kernel(axis_bits, values, total, landed, send_sems, recv_sems):
    greet(axis_bits)
    total[...] = values[...]
    for number, (axis, bit) in enumerate(axis_bits):
        copy = pltpu.make_async_remote_copy(
            src_ref=total,
            dst_ref=landed.at[number],
            send_sem=send_sems.at[number],
            recv_sem=recv_sems.at[number],
            device_id={axis: flipped(lax.axis_index(axis), (bit,))},
            device_id_type=MESH,
        )
        copy.start()
        copy.wait()
        total[...] += landed[number]


def in_vmem(count):
    return [pl.BlockSpec(memory_space=pltpu.VMEM)] * count


def call_kernel(kernel, outs, scratch, number, *operands):
    return pl.pallas_call(
        kernel,
        out_shape=outs,
        in_specs=in_vmem(len(operands)),
        out_specs=tuple(in_vmem(len(outs))),
        scratch_shapes=scratch,
        compiler_params=pltpu.CompilerParams(
            collective_id=number, has_side_effects=True, vmem_limit_bytes=VMEM_BYTES
        ),
    )(*operands)


def sigmoid(values):
    return 1.0 / (1.0 + jnp.exp(-values))


def one_minus_exp(values):
    series = values / 7.0 + 1.0
    for order in (6.0, 5.0, 4.0, 3.0, 2.0):
        series = 1.0 + series * values / order
    return jnp.where(values > -0.3, -values * series, 1.0 - jnp.exp(values))


GELU_K = 0.7978845608028654
GELU_C = 0.044715


def gelu_parts(values):
    square = values * values
    bent = jnp.tanh(GELU_K * values * (1.0 + GELU_C * square))
    gelu = 0.5 * values * (1.0 + bent)
    slope = 0.5 * (1.0 + bent) + 0.5 * values * (1.0 - bent * bent) * GELU_K * (
        1.0 + 3.0 * GELU_C * square
    )
    return gelu, slope


def gate_terms(gate_a, gate_x, soft, fresh):
    sig_a = sigmoid(gate_a)
    sig_x = sigmoid(gate_x)
    log_decay = -8.0 * sig_a * soft
    decay = jnp.exp(log_decay)
    scale = jnp.sqrt(one_minus_exp(2.0 * log_decay))
    keep = fresh < 0.5
    return sig_a, sig_x, decay, jnp.where(keep, scale, 1.0), keep


def scan_down(decay, value, carry):
    place = lax.broadcasted_iota(jnp.int32, decay.shape, 0)
    for shift in (1, 2, 4):
        past = place >= shift
        moved = pltpu.roll(value, shift, 0)
        value = jnp.where(past, decay * moved + value, value)
        if True:
            decay = jnp.where(past, decay * pltpu.roll(decay, shift, 0), decay)
    return decay * carry + value


def scan_up(decay, value, carry):
    place = lax.broadcasted_iota(jnp.int32, decay.shape, 0)
    factor = jnp.where(place < 7, pltpu.roll(decay, 7, 0), 1.0)
    for shift in (1, 2, 4):
        past = place < 8 - shift
        moved = pltpu.roll(value, 8 - shift, 0)
        value = jnp.where(past, factor * moved + value, value)
        factor = jnp.where(past, factor * pltpu.roll(factor, 8 - shift, 0), factor)
    return factor * carry + value


def forward_scan_kernel(conv, gates, branch_y, soft, fresh, mixed, states):
    total_rows = conv.shape[0]

    def step(i, carry):
        row = pl.multiple_of(i * CHUNK, CHUNK)
        span = pl.ds(row, CHUNK)
        values = conv[span, :].astype(F32)
        kept = []
        for at in range(0, CHUNK, 8):
            tile = pl.ds(row + at, 8)
            sig_a, sig_x, decay, scale, keep = gate_terms(
                gates[0, tile, :], gates[1, tile, :], soft[...], fresh[tile, :]
            )
            given = values[at : at + 8] * sig_x * scale
            state = scan_down(jnp.where(keep, decay, 0.0), given, carry)
            carry = state[7:8]
            states[tile, :] = state
            kept.append(state * gelu_parts(branch_y[tile, :])[0])
        mixed[span, :] = jnp.concatenate(kept, axis=0).astype(BF16)
        return carry

    lax.fori_loop(0, total_rows // CHUNK, step, jnp.zeros((1, conv.shape[1]), F32))


def backward_scan_kernel(
    d_mixed, conv, gates, branch_y, states, soft, slope_soft, fresh, d_conv, d_gates, d_branch, d_decay
):
    total_rows = conv.shape[0]
    d_decay[...] = jnp.zeros_like(d_decay)

    def step(i, carry):
        row = pl.multiple_of(total_rows - CHUNK - i * CHUNK, CHUNK)
        span = pl.ds(row, CHUNK)
        values = conv[span, :].astype(F32)
        kept = []
        for at in range(CHUNK - 8, -1, -8):
            tile = pl.ds(row + at, 8)
            soft_row = soft[...]
            sig_a, sig_x, decay, scale, keep = gate_terms(
                gates[0, tile, :], gates[1, tile, :], soft_row, fresh[tile, :]
            )
            value = values[at : at + 8]
            gelu, slope = gelu_parts(branch_y[tile, :])
            state = states[tile, :]
            upper = d_mixed[tile, :]
            held = jnp.where(keep, decay, 0.0)
            lam = scan_up(held, upper * gelu, carry)
            carry = held[0:1] * lam[0:1]
            d_conv[tile, :] = lam * sig_x * scale
            d_x = lam * value * scale * sig_x * (1.0 - sig_x)
            given = value * sig_x
            d_log = lam * (state - given * scale - given * decay * decay / scale)
            d_log = jnp.where(keep, d_log, 0.0)
            d_a = d_log * (-8.0 * soft_row) * sig_a * (1.0 - sig_a)
            d_decay[...] += d_log * (-8.0 * sig_a) * slope_soft[...]
            kept.append((d_a, d_x, upper * state * slope))
        kept = kept[::-1]
        d_gates[0, span, :] = jnp.concatenate([k[0] for k in kept], axis=0).astype(BF16)
        d_gates[1, span, :] = jnp.concatenate([k[1] for k in kept], axis=0).astype(BF16)
        d_branch[span, :] = jnp.concatenate([k[2] for k in kept], axis=0).astype(BF16)
        return carry

    lax.fori_loop(0, total_rows // CHUNK, step, jnp.zeros((1, conv.shape[1]), F32))


def scan_call(kernel, outs, *operands):
    return pl.pallas_call(
        kernel,
        out_shape=outs,
        in_specs=in_vmem(len(operands)),
        out_specs=tuple(in_vmem(len(outs))),
        compiler_params=pltpu.CompilerParams(vmem_limit_bytes=VMEM_BYTES),
    )(*operands)


def shifted(block, axis, distance):
    devices = range(lax.axis_size(axis))
    route = [(i - distance, i) for i in devices if i - distance in devices]
    return lax.ppermute(block, axis, route)


def doc_layout(seg_ids, seq_len):
    places = jnp.arange(seg_ids.shape[0], dtype=jnp.int32)
    before = jnp.concatenate([seg_ids[:1], seg_ids[:-1]])
    resets = (places % seq_len == 0) | (seg_ids != before)
    starts = lax.cummax(jnp.where(resets, places, jnp.zeros_like(places)), axis=0)
    return (resets, starts)


def causal_conv(starts, values, kernel):
    places = jnp.arange(values.shape[0], dtype=jnp.int32)
    total = values * kernel[0]
    for offset_k in range(1, kernel.shape[0]):
        moved = jnp.concatenate(
            [jnp.zeros((offset_k, values.shape[1]), values.dtype), values[:-offset_k]], axis=0
        )
        valid = (places - offset_k >= starts)[:, None]
        total = total + jnp.where(valid, moved, jnp.zeros_like(moved)) * kernel[offset_k]
    return total


def geglu(gate_val, up_val):
    return jax.nn.gelu(gate_val, approximate=True) * up_val


def rows_times(left, right):
    return lax.dot_general(left, right, (((1,), (1,)), ((), ())), preferred_element_type=F32)


def rows_back(lefts, rights):
    total = rows_times(lefts[0], rights[0])
    return total + rows_times(lefts[1], rights[1])


def inner_rows(left, right):
    return lax.dot_general(left, right, (((0,), (0,)), ((), ())), preferred_element_type=F32)


def body(
    tokens,
    segments,
    cotangent,
    norm_gain,
    w_y,
    w_x,
    conv_w,
    gate_w,
    decay_param,
    w_out,
    mlp_gain,
    w_gate,
    w_up,
    w_down,
):
    ntensor = lax.axis_size("tensor")
    ndp = lax.axis_size("dp")
    nbits = log2_of(ntensor)
    tindex = lax.axis_index("tensor")
    own_rows, width = tokens.shape
    group_rows = own_rows * ntensor
    block_size = gate_w.shape[2]
    nblocks = gate_w.shape[1]
    channels = w_y.shape[1]
    shape = jax.ShapeDtypeStruct
    gain_in = norm_gain.reshape(1, width)
    gain_mid = mlp_gain.reshape(1, width)
    wyx_loc = lax.all_gather(jnp.concatenate([w_y, w_x], axis=1), "dp", axis=0, tiled=True)
    wout_loc = lax.all_gather(w_out, "dp", axis=0, tiled=True)
    wg_loc = lax.all_gather(w_gate, "dp", axis=0, tiled=True)
    wu_loc = lax.all_gather(w_up, "dp", axis=0, tiled=True)
    wd_loc = lax.all_gather(w_down, "dp", axis=0, tiled=True)

    seg_rows_of = own_rows // 128
    normed_rows, cot_rows, seg_all = call_kernel(
        partial(enter_kernel, nbits),
        (
            shape((group_rows, width), BF16),
            shape((group_rows, width), BF16),
            shape((ntensor, seg_rows_of, 128), jnp.int32),
        ),
        gather_sems(nbits)
        + gather_sems(nbits)
        + [pltpu.SemaphoreType.DMA((ntensor - 1,)), pltpu.SemaphoreType.DMA((ntensor - 1,))]
        + [pltpu.SemaphoreType.DMA((2,))],
        0,
        tokens,
        cotangent,
        segments.reshape(seg_rows_of, 128),
        gain_in,
    )
    seg_rows = seg_all.reshape(group_rows)
    resets, starts = doc_layout(seg_rows, group_rows)
    fresh = resets.astype(F32)[:, None]
    branches = jnp.dot(normed_rows, wyx_loc, preferred_element_type=F32)
    branch_y, branch_x = branches[:, :channels], branches[:, channels:]
    offset = tindex * channels
    conv_loc = lax.dynamic_slice_in_dim(conv_w, offset, channels, 1)
    conv_out, conv_pull = jax.vjp(partial(causal_conv, starts), branch_x, conv_loc)
    conv_low = conv_out.astype(BF16)
    lower_rim = shifted(conv_low[:, channels - block_size :], "tensor", 1)
    upper_rim = shifted(conv_low[:, :block_size], "tensor", -1)
    rim_cells = jnp.concatenate([lower_rim, conv_low, upper_rim], axis=1)
    span_blocks = max(
        (
            -(-(channels + channels * index_t % block_size) // block_size)
            for index_t in range(ntensor)
        )
    )
    first_block = jnp.minimum(offset // block_size, nblocks - span_blocks)
    window_start = block_size * first_block - offset + block_size
    own_offset = offset - block_size * first_block
    window = lax.dynamic_slice_in_dim(rim_cells, window_start, span_blocks * block_size, 1)
    window = window.reshape(group_rows, span_blocks, block_size)
    w_window = lax.dynamic_slice_in_dim(gate_w, first_block, span_blocks, 1)
    gate_all = jnp.einsum("tnk,snkj->stnj", window, w_window, preferred_element_type=F32)
    gate_all = gate_all.reshape(2, group_rows, span_blocks * block_size)
    gate_pre = lax.dynamic_slice_in_dim(gate_all, own_offset, channels, 2)
    decay_loc = lax.dynamic_slice_in_dim(decay_param, offset, channels, 0).reshape(1, channels)
    soft = jax.nn.softplus(decay_loc)
    mixed_low, states = scan_call(
        forward_scan_kernel,
        (shape((group_rows, channels), BF16), shape((group_rows, channels), F32)),
        conv_low,
        gate_pre,
        branch_y,
        soft,
        fresh,
    )
    middle, mid_rows = call_kernel(
        partial(middle_kernel, nbits),
        (shape((own_rows, width), F32), shape((group_rows, width), BF16)),
        scatter_scratch(own_rows, width, nbits) + gather_sems(nbits),
        1,
        rows_times(mixed_low, wout_loc).astype(BF16),
        tokens,
        gain_mid,
    )
    gate_val = jnp.dot(mid_rows, wg_loc, preferred_element_type=F32)
    up_val = jnp.dot(mid_rows, wu_loc, preferred_element_type=F32)
    hidden, act_pull = jax.vjp(geglu, gate_val, up_val)
    hidden_low = hidden.astype(BF16)
    grad_wd = inner_rows(cot_rows, hidden_low).astype(BF16)
    sum_wd = lax.psum_scatter(grad_wd, "dp", scatter_dimension=0, tiled=True)
    d_hidden = jnp.dot(cot_rows, wd_loc, preferred_element_type=F32)
    d_gate, d_up = act_pull(d_hidden)
    d_gate = d_gate.astype(BF16)
    d_up = d_up.astype(BF16)
    grad_wg = inner_rows(mid_rows, d_gate).astype(BF16)
    sum_wg = lax.psum_scatter(grad_wg, "dp", scatter_dimension=0, tiled=True)
    grad_wu = inner_rows(mid_rows, d_up).astype(BF16)
    sum_wu = lax.psum_scatter(grad_wu, "dp", scatter_dimension=0, tiled=True)
    d_middle, d_mixer, d_gain_mid = call_kernel(
        partial(turn_kernel, nbits),
        (
            shape((own_rows, width), F32),
            shape((group_rows, width), BF16),
            shape((8, width), F32),
        ),
        scatter_scratch(own_rows, width, nbits) + gather_sems(nbits),
        2,
        rows_back((d_gate, d_up), (wg_loc, wu_loc)).astype(BF16),
        cotangent,
        middle,
        gain_mid,
    )
    grad_wout = inner_rows(d_mixer, mixed_low).astype(BF16)
    sum_wout = lax.psum_scatter(grad_wout, "dp", scatter_dimension=0, tiled=True)
    d_mixed_in = jnp.dot(d_mixer, wout_loc, preferred_element_type=F32)
    d_conv_direct, d_gate_low, d_branch_y, d_decay = scan_call(
        backward_scan_kernel,
        (
            shape((group_rows, channels), F32),
            shape((2, group_rows, channels), BF16),
            shape((group_rows, channels), BF16),
            shape((8, channels), F32),
        ),
        d_mixed_in,
        conv_low,
        gate_pre,
        branch_y,
        states,
        soft,
        jax.nn.sigmoid(decay_loc),
        fresh,
    )
    lower_back = shifted(d_gate_low[:, :, channels - block_size :], "tensor", 1)
    upper_back = shifted(d_gate_low[:, :, :block_size], "tensor", -1)
    back_rim = jnp.concatenate([lower_back, d_gate_low, upper_back], axis=2)
    d_window = lax.dynamic_slice_in_dim(back_rim, window_start, span_blocks * block_size, 2)
    d_window = d_window.reshape(2, group_rows, span_blocks, block_size)
    d_from_gate = jnp.einsum("stnj,snkj->tnk", d_window, w_window, preferred_element_type=F32)
    d_from_gate = d_from_gate.reshape(group_rows, span_blocks * block_size)
    d_conv_out = d_conv_direct + lax.dynamic_slice_in_dim(d_from_gate, own_offset, channels, 1)
    d_branch_x, grad_conv_loc = conv_pull(d_conv_out)
    d_branches = jnp.concatenate([d_branch_y, d_branch_x.astype(BF16)], axis=1)
    grad_wyx = inner_rows(normed_rows, d_branches).astype(BF16)
    sum_wyx = lax.psum_scatter(grad_wyx, "dp", scatter_dimension=0, tiled=True)
    grad_input, d_gain_in = call_kernel(
        partial(leave_kernel, nbits),
        (shape((own_rows, width), F32), shape((8, width), F32)),
        scatter_scratch(own_rows, width, nbits),
        3,
        rows_times(d_branches, wyx_loc).astype(BF16),
        tokens,
        d_middle,
        gain_in,
    )
    ffn_part = rows_times(hidden_low, wd_loc).astype(BF16)
    (mixed,) = call_kernel(
        partial(result_kernel, nbits),
        (shape((own_rows, width), BF16),),
        scatter_scratch(own_rows, width, nbits),
        4,
        ffn_part,
        middle,
    )
    gate_grad = jnp.einsum("tnk,stnj->sknj", window, d_window, preferred_element_type=F32)
    gate_grad = gate_grad.reshape(2, block_size, span_blocks * block_size)
    gate_grad = lax.dynamic_slice_in_dim(gate_grad, own_offset, channels, 2).astype(BF16)
    gate_grad = lax.psum(gate_grad.reshape(2 * block_size, channels), "dp")
    gate_grad = lax.all_gather(gate_grad, "tensor", axis=1, tiled=True)
    sum_gate = gate_grad.astype(F32).reshape(2, block_size, nblocks, block_size)
    sum_gate = sum_gate.transpose(0, 2, 1, 3)
    taps = conv_w.shape[0]
    own_small = jnp.concatenate([grad_conv_loc, jnp.sum(d_decay, axis=0, keepdims=True)], axis=0)
    own_small = lax.dynamic_update_slice(
        jnp.zeros((taps + 1, width), F32), own_small, (jnp.int32(0), offset)
    )
    small = jnp.concatenate(
        [
            own_small,
            jnp.sum(d_gain_in, axis=0, keepdims=True),
            jnp.sum(d_gain_mid, axis=0, keepdims=True),
        ],
        axis=0,
    )
    axis_bits = [("dp", bit) for bit in range(log2_of(ndp))] + tensor_bits(nbits)
    (summed,) = call_kernel(
        partial(sum_kernel, axis_bits),
        (shape(small.shape, F32),),
        [
            pltpu.VMEM((len(axis_bits),) + small.shape, F32),
            pltpu.SemaphoreType.DMA((len(axis_bits),)),
            pltpu.SemaphoreType.DMA((len(axis_bits),)),
        ],
        5,
        small,
    )
    sum_wyx = sum_wyx.astype(F32)
    return (
        mixed,
        grad_input,
        summed[taps + 1],
        sum_wyx[:, :channels],
        sum_wyx[:, channels:],
        summed[:taps],
        sum_gate,
        summed[taps],
        sum_wout.astype(F32),
        summed[taps + 2],
        sum_wg.astype(F32),
        sum_wu.astype(F32),
        sum_wd.astype(F32),
    )


def solution(mesh):
    split = P(("dp", "tensor"), None)
    weight = P("dp", "tensor")
    return jax.shard_map(
        body,
        mesh=mesh,
        in_specs=(
            split,
            P(("dp", "tensor")),
            split,
            P(),
            weight,
            weight,
            P(),
            P(),
            P(),
            weight,
            P(),
            weight,
            weight,
            weight,
        ),
        out_specs=(
            split,
            split,
            P(),
            weight,
            weight,
            P(),
            P(),
            P(),
            weight,
            P(),
            weight,
            weight,
            weight,
        ),
        check_vma=False,
    )
```

```python
import math
from functools import partial

import jax
import jax.numpy as jnp
from jax import lax
from jax.experimental import pallas as pl
from jax.experimental.pallas import tpu as pltpu
from jax.sharding import PartitionSpec as P

EPSILON = 1e-06
MESH = pl.DeviceIdType.MESH
VMEM_BYTES = 56 * 1024 * 1024
CHUNK = 16
F32 = jnp.float32
BF16 = jnp.bfloat16


def subsets(bits):
    found = [()]
    for bit in bits:
        found = found + [chosen + (bit,) for chosen in found]
    return found


def flipped(index, bits):
    for bit in bits:
        mine = (index // (1 << bit)) % 2
        index = index + (1 - 2 * mine) * (1 << bit)
    return index


def log2_of(count):
    assert count & (count - 1) == 0
    return count.bit_length() - 1


def greet(axis_bits):
    barrier = pltpu.get_barrier_semaphore()
    for axis, bit in axis_bits:
        peer = flipped(lax.axis_index(axis), (bit,))
        pl.semaphore_signal(barrier, inc=1, device_id={axis: peer}, device_id_type=MESH)
    pl.semaphore_wait(barrier, len(axis_bits))


def halves_of(nbits, columns):
    half = columns // 2
    ups = tuple(range(nbits))
    return ((ups, 0, half), (ups[::-1], half, half))


class Gather:
    def __init__(self, ref, rows, nbits, send_sems, recv_sems):
        self.ref, self.rows, self.nbits = ref, rows, nbits
        self.sems = (send_sems, recv_sems)
        self.me = lax.axis_index("tensor")
        self.plan = []
        number = 0
        for half, (order, at, width) in enumerate(halves_of(nbits, ref.shape[1])):
            for step, bit in enumerate(order):
                for known in subsets(order[:step]):
                    self.plan.append((half, step, known, bit, at, width, number))
                    number += 1
        self.count = number

    def copy(self, item):
        half, step, known, bit, at, width, number = item
        row = pl.multiple_of(flipped(self.me, known) * self.rows, self.rows)
        piece = self.ref.at[pl.ds(row, self.rows), pl.ds(at, width)]
        return pltpu.make_async_remote_copy(
            src_ref=piece,
            dst_ref=piece,
            send_sem=self.sems[0].at[number],
            recv_sem=self.sems[1].at[number],
            device_id={"tensor": flipped(self.me, (bit,))},
            device_id_type=MESH,
        )

    def begin(self):
        for item in sorted(self.plan, key=lambda it: it[1]):
            if item[2] == ():
                self.copy(item).start()

    def finish(self):
        arrived = sorted(self.plan, key=lambda it: (it[1], it[0]))
        for item in arrived:
            half, step, known, bit, at, width, number = item
            self.copy(item).wait_recv()
            block = known + (bit,)
            for later in self.plan:
                if later[0] == half and set(later[2]) == set(block):
                    self.copy(later).start()
        for item in self.plan:
            self.copy(item).wait_send()


def gather_copies(nbits):
    return 2 * ((1 << nbits) - 1)


class Scatter:
    def __init__(self, ref, landed, staged, rows, nbits, send_sems, recv_sems):
        self.ref, self.landed, self.staged = ref, landed, staged
        self.rows, self.nbits = rows, nbits
        self.sems = (send_sems, recv_sems)
        self.me = lax.axis_index("tensor")
        self.plan, self.slot = [], {}
        number = 0
        for half, (order, at, width) in enumerate(halves_of(nbits, ref.shape[1])):
            for step, bit in enumerate(order):
                for rest in subsets(order[step + 1 :])[::-1]:
                    self.plan.append((half, step, rest, bit, at, width, number))
                    if step > 0:
                        self.slot[number] = len(self.slot)
                    number += 1

    def copy(self, item):
        half, step, rest, bit, at, width, number = item
        if step == 0:
            row = pl.multiple_of(flipped(self.me, rest + (bit,)) * self.rows, self.rows)
            source = self.ref.at[pl.ds(row, self.rows), pl.ds(at, width)]
        else:
            source = self.staged.at[self.slot[number]]
        return pltpu.make_async_remote_copy(
            src_ref=source,
            dst_ref=self.landed.at[number],
            send_sem=self.sems[0].at[number],
            recv_sem=self.sems[1].at[number],
            device_id={"tensor": flipped(self.me, (bit,))},
            device_id_type=MESH,
        )

    def begin(self):
        for item in sorted(self.plan, key=lambda it: (len(it[2]) == 0)):
            if item[1] == 0:
                self.copy(item).start()

    def partial_sum(self, half, block, before, row, size):
        at, width = halves_of(self.nbits, self.ref.shape[1])[half][1:]
        base = pl.multiple_of(flipped(self.me, block) * self.rows + row, size)
        total = self.ref[pl.ds(base, size), pl.ds(at, width)].astype(F32)
        for it in self.plan:
            if it[0] == half and it[1] < before and set(it[2]) == set(block):
                total = total + self.landed[it[6], pl.ds(row, size), :].astype(F32)
        return total

    def advance(self, step):
        for half in range(2):
            for item in self.plan:
                if item[0] == half and item[1] == step:
                    self.copy(item).wait_recv()
            for item in self.plan:
                if item[0] == half and item[1] == step + 1:

                    def fill(row, item=item):
                        value = self.partial_sum(
                            item[0], item[2] + (item[3],), item[1], row, CHUNK
                        )
                        where = (self.slot[item[6]], pl.ds(row, CHUNK))
                        self.staged[where + (slice(None),)] = value.astype(BF16)

                    chunks(self.rows, fill)
                    self.copy(item).start()

    def run(self):
        for step in range(self.nbits):
            self.advance(step)

    def total(self, row, size):
        return jnp.concatenate(
            [self.partial_sum(half, (), self.nbits, row, size) for half in range(2)], axis=1
        )

    def drain(self):
        for item in self.plan:
            self.copy(item).wait_send()


def scatter_scratch(rows, columns, nbits):
    copies = gather_copies(nbits)
    later = max(1, copies - (1 << nbits))
    return [
        pltpu.VMEM((copies, rows, columns // 2), BF16),
        pltpu.VMEM((later, rows, columns // 2), BF16),
        pltpu.SemaphoreType.DMA((copies,)),
        pltpu.SemaphoreType.DMA((copies,)),
    ]


def gather_sems(nbits):
    copies = gather_copies(nbits)
    return [pltpu.SemaphoreType.DMA((copies,)), pltpu.SemaphoreType.DMA((copies,))]


def tensor_bits(nbits):
    return [("tensor", bit) for bit in range(nbits)]


def rms_scale_of(values):
    return lax.rsqrt(jnp.mean(values * values, axis=-1, keepdims=True) + EPSILON)


def chunks(rows, body):
    def step(i, carry):
        body(pl.multiple_of(i * CHUNK, CHUNK))
        return carry

    lax.fori_loop(0, rows // CHUNK, step, 0)


def own_row(row, rows):
    return pl.multiple_of(lax.axis_index("tensor") * rows + row, CHUNK)


def dp_place():
    me = lax.axis_index("dp")
    return me // 2, me % 2, lax.axis_size("dp") // 2


def dp_index(chip, core):
    return chip * 2 + core


def shift_order(count):
    return sorted(range(1, count), key=lambda shift: min(shift, count - shift))


class LineGather:
    def __init__(self, own, whole, send_sems, recv_sems):
        self.own, self.whole = own, whole
        self.sems = (send_sems, recv_sems)
        self.chip, self.core, self.chips = dp_place()
        self.rows = own.shape[0]

    def block(self, chip, core):
        row = pl.multiple_of(dp_index(chip, core) * self.rows, self.rows)
        return self.whole.at[pl.ds(row, self.rows), :]

    def along(self, shift):
        return pltpu.make_async_remote_copy(
            src_ref=self.own,
            dst_ref=self.block(self.chip, self.core),
            send_sem=self.sems[0].at[shift],
            recv_sem=self.sems[1].at[shift],
            device_id={"dp": dp_index((self.chip + shift) % self.chips, self.core)},
            device_id_type=MESH,
        )

    def across(self, shift):
        block = self.block((self.chip + self.chips - shift) % self.chips, self.core)
        number = self.chips + shift
        return pltpu.make_async_remote_copy(
            src_ref=self.own if shift == 0 else block,
            dst_ref=block,
            send_sem=self.sems[0].at[number],
            recv_sem=self.sems[1].at[number],
            device_id={"dp": dp_index(self.chip, 1 - self.core)},
            device_id_type=MESH,
        )

    def local(self):
        return pltpu.make_async_copy(
            self.own, self.block(self.chip, self.core), self.sems[0].at[2 * self.chips]
        )

    def begin(self):
        for shift in shift_order(self.chips):
            self.along(shift).start()
        self.across(0).start()
        self.local().start()

    def pass_on(self):
        for shift in shift_order(self.chips):
            self.along(shift).wait_recv()
            self.across(shift).start()

    def finish(self):
        for shift in range(self.chips):
            self.across(shift).wait()
        for shift in range(1, self.chips):
            self.along(shift).wait_send()
        self.local().wait()


def line_sems(ndp):
    return [pltpu.SemaphoreType.DMA((ndp + 1,)), pltpu.SemaphoreType.DMA((ndp + 1,))]


def greet_peers(nbits, whole_dp):
    me = lax.axis_index("tensor")
    chip, core, chips = dp_place()
    barrier = pltpu.get_barrier_semaphore()
    met = 0
    for chosen in subsets(tuple(range(nbits))):
        if chosen:
            pl.semaphore_signal(
                barrier, inc=1, device_id={"tensor": flipped(me, chosen)}, device_id_type=MESH
            )
            met += 1
    for shift in range(chips):
        for turn in range(2):
            if (shift, turn) == (0, 0) or (shift and turn and not whole_dp):
                continue
            other = dp_index((chip + shift) % chips, core + turn * (1 - 2 * core))
            pl.semaphore_signal(
                barrier, inc=1, device_id={"dp": other}, device_id_type=MESH
            )
            met += 1
    pl.semaphore_wait(barrier, met)


def enter_kernel(
    nbits,
    tokens,
    cot,
    seg,
    gain,
    w_y,
    w_x,
    w_out,
    normed_all,
    cot_all,
    seg_all,
    wy_all,
    wx_all,
    wout_all,
    s0,
    r0,
    s1,
    r1,
    s2,
    r2,
    l0,
    *line,
):
    rows = tokens.shape[0]
    me = lax.axis_index("tensor")
    peers = [chosen for chosen in subsets(tuple(range(nbits))) if chosen]
    greet_peers(nbits, False)
    lines = [
        LineGather(own, whole, line[2 * number], line[2 * number + 1])
        for number, (own, whole) in enumerate(((w_y, wy_all), (w_x, wx_all), (w_out, wout_all)))
    ]
    lines[0].begin()
    lines[1].begin()

    def norm(row):
        values = tokens[pl.ds(row, CHUNK), :].astype(F32)
        scaled = values * rms_scale_of(values) * gain[...]
        normed_all[pl.ds(own_row(row, rows), CHUNK), :] = scaled.astype(BF16)

    chunks(rows, norm)
    first = Gather(normed_all, rows, nbits, s0, r0)
    first.begin()
    cot_own = cot_all.at[pl.ds(pl.multiple_of(me * rows, rows), rows), :]
    local = pltpu.make_async_copy(cot, cot_own, l0.at[0])
    local.start()
    seg_own = pltpu.make_async_copy(seg, seg_all.at[me], l0.at[1])
    seg_own.start()
    seg_copies = [
        pltpu.make_async_remote_copy(
            src_ref=seg,
            dst_ref=seg_all.at[me],
            send_sem=s2.at[number],
            recv_sem=r2.at[number],
            device_id={"tensor": flipped(me, chosen)},
            device_id_type=MESH,
        )
        for number, chosen in enumerate(peers)
    ]
    for copy in seg_copies:
        copy.start()
    local.wait()
    second = Gather(cot_all, rows, nbits, s1, r1)
    second.begin()
    first.finish()
    lines[0].pass_on()
    lines[1].pass_on()
    lines[2].begin()
    second.finish()
    lines[2].pass_on()
    for item in lines:
        item.finish()
    for copy in seg_copies:
        copy.wait()
    seg_own.wait()


def middle_kernel(
    nbits, mixer, tokens, gain, middle, mid_all, landed, staged, s0, r0, s1, r1
):
    rows = tokens.shape[0]
    greet(tensor_bits(nbits))
    scatter = Scatter(mixer, landed, staged, rows, nbits, s0, r0)
    scatter.begin()
    scatter.run()

    def norm(row):
        values = tokens[pl.ds(row, CHUNK), :].astype(F32) + scatter.total(row, CHUNK)
        middle[pl.ds(row, CHUNK), :] = values
        scaled = values * rms_scale_of(values) * gain[...]
        mid_all[pl.ds(own_row(row, rows), CHUNK), :] = scaled.astype(BF16)

    chunks(rows, norm)
    gather = Gather(mid_all, rows, nbits, s1, r1)
    gather.begin()
    gather.finish()
    scatter.drain()


def result_kernel(nbits, ffn, middle, mixed, landed, staged, s0, r0):
    rows = middle.shape[0]
    greet(tensor_bits(nbits))
    scatter = Scatter(ffn, landed, staged, rows, nbits, s0, r0)
    scatter.begin()
    scatter.run()

    def add(row):
        values = middle[pl.ds(row, CHUNK), :] + scatter.total(row, CHUNK)
        mixed[pl.ds(row, CHUNK), :] = values.astype(BF16)

    chunks(rows, add)
    scatter.drain()


def norm_pull(values, gain, cotangent):
    scale = rms_scale_of(values)
    unit = values * scale
    inner = cotangent * gain
    back = scale * (inner - unit * jnp.mean(inner * unit, axis=-1, keepdims=True))
    return back, cotangent * unit


def eight_rows(values):
    total = values[0:8]
    for at in range(8, CHUNK, 8):
        total = total + values[at : at + 8]
    return total


def turn_kernel(
    nbits, d_norm, cot, middle, gain, d_middle, d_mixer, d_gain, landed, staged, s0, r0, s1, r1
):
    rows = middle.shape[0]
    greet(tensor_bits(nbits))
    scatter = Scatter(d_norm, landed, staged, rows, nbits, s0, r0)
    scatter.begin()
    d_gain[...] = jnp.zeros_like(d_gain)
    scatter.run()

    def pull(row):
        span = pl.ds(row, CHUNK)
        back, gains = norm_pull(middle[span, :], gain[...], scatter.total(row, CHUNK))
        values = cot[span, :].astype(F32) + back
        d_middle[span, :] = values
        d_mixer[pl.ds(own_row(row, rows), CHUNK), :] = values.astype(BF16)
        d_gain[...] += eight_rows(gains)

    chunks(rows, pull)
    gather = Gather(d_mixer, rows, nbits, s1, r1)
    gather.begin()
    gather.finish()
    scatter.drain()


class LineRing:
    def __init__(self, whole, kept, swapped, staged, landed, send_sems, recv_sems):
        self.whole, self.kept, self.swapped = whole, kept, swapped
        self.staged, self.landed = staged, landed
        self.sems = (send_sems, recv_sems)
        self.chip, self.core, self.chips = dp_place()
        self.rows = whole.shape[2]

    def local(self):
        return pltpu.make_async_copy(
            self.whole.at[:, self.core], self.kept, self.sems[0].at[self.chips]
        )

    def swap(self):
        return pltpu.make_async_remote_copy(
            src_ref=self.whole.at[:, 1 - self.core],
            dst_ref=self.swapped,
            send_sem=self.sems[0].at[0],
            recv_sem=self.sems[1].at[0],
            device_id={"dp": dp_index(self.chip, 1 - self.core)},
            device_id_type=MESH,
        )

    def hop(self, step):
        return pltpu.make_async_remote_copy(
            src_ref=self.staged.at[step - 1],
            dst_ref=self.landed.at[step - 1],
            send_sem=self.sems[0].at[step],
            recv_sem=self.sems[1].at[step],
            device_id={"dp": dp_index((self.chip + 1) % self.chips, self.core)},
            device_id_type=MESH,
        )

    def begin(self):
        self.local().start()
        self.swap().start()

    def value(self, step, span):
        chip = (self.chip + self.chips - step) % self.chips
        total = self.kept[chip, span, :].astype(F32) + self.swapped[chip, span, :].astype(F32)
        if step != 1:
            before = (step if step else self.chips) - 2
            total = total + self.landed[before, span, :].astype(F32)
        return total

    def advance(self, step):
        if step == 1:
            self.local().wait()
            self.swap().wait_recv()
        else:
            self.hop(step - 1).wait_recv()

        def fill(row):
            span = pl.ds(row, CHUNK)
            self.staged[step - 1, span, :] = self.value(step, span).astype(BF16)

        chunks(self.rows, fill)
        self.hop(step).start()

    def finish(self, store):
        self.hop(self.chips - 1).wait_recv()

        def fill(row):
            span = pl.ds(row, CHUNK)
            store(span, self.value(0, span))

        chunks(self.rows, fill)

    def drain(self):
        self.swap().wait_send()
        for step in range(1, self.chips):
            self.hop(step).wait_send()


def ring_scratch(ndp, rows, columns):
    chips = ndp // 2
    return [
        pltpu.VMEM((chips, rows, columns), BF16),
        pltpu.VMEM((chips, rows, columns), BF16),
        pltpu.VMEM((chips - 1, rows, columns), BF16),
        pltpu.VMEM((chips - 1, rows, columns), BF16),
        pltpu.SemaphoreType.DMA((chips + 1,)),
        pltpu.SemaphoreType.DMA((chips + 1,)),
    ]


RING = 6


def leave_kernel(nbits, with_ffn, *refs):
    refs = list(refs)

    def take(count):
        taken = refs[:count]
        del refs[:count]
        return taken

    d_norm, tokens, d_middle, gain, own_small, d_gain_mid = take(6)
    pieces = take(4)
    ffn, middle = take(2) if with_ffn else (None, None)
    grad_input, sum_out, sum_y, sum_x, gate_all, small_all = take(6)
    mixed = take(1)[0] if with_ffn else None
    landed, staged, s0, r0 = take(4)
    rings = [LineRing(piece, *take(RING)) for piece in pieces]
    d_gain, gains, gains_landed, small, small_landed = take(5)
    gain_s, gain_r, vec_s, vec_r, join_s, join_r, gate_s, gate_r = take(8)
    rows = tokens.shape[0]
    me = lax.axis_index("tensor")
    chip, core, chips = dp_place()
    place = dp_index(chip, core)
    peers = [chosen for chosen in subsets(tuple(range(nbits))) if chosen]
    others = [(shift, turn) for shift in range(chips) for turn in range(2)][1:]
    greet_peers(nbits, True)
    for ring in rings:
        ring.begin()
    scatter = Scatter(d_norm, landed, staged, rows, nbits, s0, r0)
    scatter.begin()
    if with_ffn:
        second = Scatter(ffn, *take(2), rows, nbits, *take(2))
        second.begin()
    d_gain[...] = jnp.zeros_like(d_gain)
    for ring in rings:
        ring.advance(1)
    scatter.advance(0)
    if chips > 2:
        for ring in rings:
            ring.advance(2)
    for step in range(1, nbits):
        scatter.advance(step)

    def pull(row):
        span = pl.ds(row, CHUNK)
        back, parts = norm_pull(
            tokens[span, :].astype(F32), gain[...], scatter.total(row, CHUNK)
        )
        grad_input[span, :] = d_middle[span, :] + back
        d_gain[...] += eight_rows(parts)

    chunks(rows, pull)
    share = gains.shape[2]
    top = jnp.sum(d_gain[...], axis=0, keepdims=True)
    low = jnp.sum(d_gain_mid[...], axis=0, keepdims=True)
    place8 = lax.broadcasted_iota(jnp.int32, (8, share), 0)
    for index in range(1 << nbits):
        span = slice(index * share, (index + 1) * share)
        gains[index] = jnp.where(
            place8 == 6, top[:, span], jnp.where(place8 == 7, low[:, span], 0.0)
        )

    def gain_copy(number, chosen):
        peer = flipped(me, chosen)
        return pltpu.make_async_remote_copy(
            src_ref=gains.at[peer],
            dst_ref=gains_landed.at[number],
            send_sem=gain_s.at[number],
            recv_sem=gain_r.at[number],
            device_id={"tensor": peer},
            device_id_type=MESH,
        )

    for number, chosen in enumerate(peers):
        gain_copy(number, chosen).start()
    for step in range(3, chips):
        for ring in rings:
            ring.advance(step)
    if with_ffn:
        second.advance(0)
    total = own_small[...] + gains[me]
    for number, chosen in enumerate(peers):
        gain_copy(number, chosen).wait_recv()
        total = total + gains_landed[number]
    small[...] = total

    def vec_copy(number, shift, turn):
        other = dp_index((chip + shift) % chips, core + turn * (1 - 2 * core))
        return pltpu.make_async_remote_copy(
            src_ref=small,
            dst_ref=small_landed.at[number],
            send_sem=vec_s.at[number],
            recv_sem=vec_r.at[number],
            device_id={"dp": other},
            device_id_type=MESH,
        )

    for number, (shift, turn) in enumerate(others):
        vec_copy(number, shift, turn).start()

    def store_gate(span, value):
        gate_all[place, me, span, :] = value.astype(BF16)

    rings[0].finish(store_gate)

    def gate_copy(number, chip_from, ref, target):
        return pltpu.make_async_remote_copy(
            src_ref=ref,
            dst_ref=ref,
            send_sem=gate_s.at[number],
            recv_sem=gate_r.at[number],
            device_id=target,
            device_id_type=MESH,
        )

    def gate_tensor(number, chosen):
        ref = gate_all.at[place, me]
        return gate_copy(number, chip, ref, {"tensor": flipped(me, chosen)})

    def gate_line(shift):
        target = {"dp": dp_index((chip + shift) % chips, core)}
        return gate_copy(len(peers) + shift - 1, chip, gate_all.at[place], target)

    def gate_core(shift):
        ref = gate_all.at[dp_index((chip + chips - shift) % chips, core)]
        target = {"dp": dp_index(chip, 1 - core)}
        return gate_copy(len(peers) + chips - 1 + shift, chip, ref, target)

    for number, chosen in enumerate(peers):
        gate_tensor(number, chosen).start()
    if with_ffn:
        for step in range(1, nbits):
            second.advance(step)
    total = small[...]
    for number, (shift, turn) in enumerate(others):
        vec_copy(number, shift, turn).wait_recv()
        total = total + small_landed[number]
    small_all[me] = total

    def join_copy(number, chosen):
        return pltpu.make_async_remote_copy(
            src_ref=small_all.at[me],
            dst_ref=small_all.at[me],
            send_sem=join_s.at[number],
            recv_sem=join_r.at[number],
            device_id={"tensor": flipped(me, chosen)},
            device_id_type=MESH,
        )

    for number, chosen in enumerate(peers):
        join_copy(number, chosen).start()
    for number, chosen in enumerate(peers):
        gate_tensor(number, chosen).wait_recv()
    for shift in range(1, chips):
        gate_line(shift).start()
    gate_core(0).start()
    if with_ffn:

        def add(row):
            span = pl.ds(row, CHUNK)
            mixed[span, :] = (middle[span, :] + second.total(row, CHUNK)).astype(BF16)

        chunks(rows, add)
    for shift in shift_order(chips):
        gate_line(shift).wait_recv()
        gate_core(shift).start()

    def store_in(ref):
        def store(span, value):
            ref[span, :] = value

        return store

    for ring, ref in zip(rings[1:], (sum_out, sum_y, sum_x)):
        ring.finish(store_in(ref))
    for shift in range(chips):
        gate_core(shift).wait()
    for shift in range(1, chips):
        gate_line(shift).wait_send()
    for number, chosen in enumerate(peers):
        gate_tensor(number, chosen).wait_send()
        gain_copy(number, chosen).wait_send()
        join_copy(number, chosen).wait()
    for number, (shift, turn) in enumerate(others):
        vec_copy(number, shift, turn).wait_send()
    scatter.drain()
    if with_ffn:
        second.drain()
    for ring in rings:
        ring.drain()


def in_vmem(count):
    return [pl.BlockSpec(memory_space=pltpu.VMEM)] * count


def call_kernel(kernel, outs, scratch, number, *operands, far_in=(), far_out=(), cost_us=1):
    vmem = pl.BlockSpec(memory_space=pltpu.VMEM)
    far = pl.BlockSpec(memory_space=pl.ANY)
    return pl.pallas_call(
        kernel,
        out_shape=outs,
        in_specs=[far if i in far_in else vmem for i in range(len(operands))],
        out_specs=tuple(far if i in far_out else vmem for i in range(len(outs))),
        scratch_shapes=scratch,
        cost_estimate=pl.CostEstimate(
            flops=0, bytes_accessed=cost_us * 1_000_000, transcendentals=0
        ),
        compiler_params=pltpu.CompilerParams(
            collective_id=number, has_side_effects=True, vmem_limit_bytes=VMEM_BYTES
        ),
    )(*operands)


def sigmoid(values):
    return 1.0 / (1.0 + jnp.exp(-values))


def one_minus_exp(values):
    series = values / 7.0 + 1.0
    for order in (6.0, 5.0, 4.0, 3.0, 2.0):
        series = 1.0 + series * values / order
    return jnp.where(values > -0.3, -values * series, 1.0 - jnp.exp(values))


GELU_K = 0.7978845608028654
GELU_C = 0.044715


def gelu_parts(values):
    square = values * values
    bent = jnp.tanh(GELU_K * values * (1.0 + GELU_C * square))
    gelu = 0.5 * values * (1.0 + bent)
    slope = 0.5 * (1.0 + bent) + 0.5 * values * (1.0 - bent * bent) * GELU_K * (
        1.0 + 3.0 * GELU_C * square
    )
    return gelu, slope


def gate_terms(gate_a, gate_x, soft, fresh):
    sig_a = sigmoid(gate_a)
    sig_x = sigmoid(gate_x)
    log_decay = -8.0 * sig_a * soft
    decay = jnp.exp(log_decay)
    scale = jnp.sqrt(one_minus_exp(2.0 * log_decay))
    keep = fresh < 0.5
    return sig_a, sig_x, decay, jnp.where(keep, scale, 1.0), keep


def scan_down(decay, value, carry):
    place = lax.broadcasted_iota(jnp.int32, decay.shape, 0)
    for shift in (1, 2, 4):
        past = place >= shift
        moved = pltpu.roll(value, shift, 0)
        value = jnp.where(past, decay * moved + value, value)
        decay = jnp.where(past, decay * pltpu.roll(decay, shift, 0), decay)
    return decay * carry + value


def scan_up(decay, value, carry):
    place = lax.broadcasted_iota(jnp.int32, decay.shape, 0)
    factor = jnp.where(place < 7, pltpu.roll(decay, 7, 0), 1.0)
    for shift in (1, 2, 4):
        past = place < 8 - shift
        moved = pltpu.roll(value, 8 - shift, 0)
        value = jnp.where(past, factor * moved + value, value)
        factor = jnp.where(past, factor * pltpu.roll(factor, 8 - shift, 0), factor)
    return factor * carry + value


def forward_scan_kernel(conv, gates, branch_y, soft, fresh, mixed, states):
    total_rows, width = conv.shape

    def step(i, carry):
        row = pl.multiple_of(i * CHUNK, CHUNK)
        span = pl.ds(row, CHUNK)
        values = conv[span, :].astype(F32)
        kept = []
        for at in range(0, CHUNK, 8):
            tile = pl.ds(row + at, 8)
            sig_a, sig_x, decay, scale, keep = gate_terms(
                gates[tile, :width], gates[tile, width:], soft[...], fresh[tile, :]
            )
            given = values[at : at + 8] * sig_x * scale
            state = scan_down(jnp.where(keep, decay, 0.0), given, carry)
            carry = state[7:8]
            states[tile, :] = state
            kept.append(state * gelu_parts(branch_y[tile, :])[0])
        mixed[span, :] = jnp.concatenate(kept, axis=0).astype(BF16)
        return carry

    lax.fori_loop(0, total_rows // CHUNK, step, jnp.zeros((1, conv.shape[1]), F32))


def backward_scan_kernel(
    d_mixed, conv, gates, branch_y, states, soft, slope_soft, fresh, d_conv, d_gates, d_branch, d_decay
):
    total_rows, width = conv.shape
    d_decay[...] = jnp.zeros_like(d_decay)

    def step(i, carry):
        row = pl.multiple_of(total_rows - CHUNK - i * CHUNK, CHUNK)
        span = pl.ds(row, CHUNK)
        values = conv[span, :].astype(F32)
        kept = []
        for at in range(CHUNK - 8, -1, -8):
            tile = pl.ds(row + at, 8)
            soft_row = soft[...]
            sig_a, sig_x, decay, scale, keep = gate_terms(
                gates[tile, :width], gates[tile, width:], soft_row, fresh[tile, :]
            )
            value = values[at : at + 8]
            gelu, slope = gelu_parts(branch_y[tile, :])
            state = states[tile, :]
            upper = d_mixed[tile, :]
            held = jnp.where(keep, decay, 0.0)
            lam = scan_up(held, upper * gelu, carry)
            carry = held[0:1] * lam[0:1]
            d_conv[tile, :] = lam * sig_x * scale
            d_x = lam * value * scale * sig_x * (1.0 - sig_x)
            given = value * sig_x
            d_log = lam * (state - given * scale - given * decay * decay / scale)
            d_log = jnp.where(keep, d_log, 0.0)
            d_a = d_log * (-8.0 * soft_row) * sig_a * (1.0 - sig_a)
            d_decay[...] += d_log * (-8.0 * sig_a) * slope_soft[...]
            kept.append((d_a, d_x, upper * state * slope))
        kept = kept[::-1]
        d_gates[span, :width] = jnp.concatenate([k[0] for k in kept], axis=0).astype(BF16)
        d_gates[span, width:] = jnp.concatenate([k[1] for k in kept], axis=0).astype(BF16)
        d_branch[span, :] = jnp.concatenate([k[2] for k in kept], axis=0).astype(BF16)
        return carry

    lax.fori_loop(0, total_rows // CHUNK, step, jnp.zeros((1, conv.shape[1]), F32))


def scan_call(kernel, outs, *operands):
    return pl.pallas_call(
        kernel,
        out_shape=outs,
        in_specs=in_vmem(len(operands)),
        out_specs=tuple(in_vmem(len(outs))),
        compiler_params=pltpu.CompilerParams(vmem_limit_bytes=VMEM_BYTES),
    )(*operands)


class Rim:
    def __init__(self, route, back, source, first, width, room):
        self.route, self.back = route, back
        self.source, self.first, self.width = source, first, width
        self.room = room

    def fetch(self, values):
        part = lax.dynamic_slice_in_dim(values, self.source, self.width, 1)
        return lax.ppermute(part, "tensor", self.route)

    def give(self, part):
        return lax.ppermute(part, "tensor", self.back)

    def add(self, values, part):
        zeros = jnp.zeros(values.shape, F32)
        return values + lax.dynamic_update_slice_in_dim(
            zeros, part.astype(F32), self.source, 1
        )

    def window(self, channels):
        if self.room:
            return (channels // self.width + 4) * self.width
        return channels + self.width


def gate_rims(channels, block_size, ntensor, offset, tindex):
    if channels % block_size == block_size // 2 and ntensor % 2 == 0:
        half = block_size // 2
        even = tindex % 2 == 0
        route = [(i, i + 1 - 2 * (i % 2)) for i in range(ntensor)]
        source = jnp.where(even, channels - half, 0)
        first = jnp.where(even, offset + channels, offset - half)
        return [Rim(route, route, source, first, half, 0)]
    up = [(i, i + 1) for i in range(ntensor - 1)]
    down = [(i + 1, i) for i in range(ntensor - 1)]
    last = jnp.int32(channels - block_size)
    return [
        Rim(up, down, last, offset - block_size, block_size, block_size),
        Rim(down, up, jnp.int32(0), offset + channels, block_size, block_size),
    ]


def same_block(first, count, offset, channels, block_size):
    rows = (first + jnp.arange(count, dtype=jnp.int32))[:, None]
    columns = (offset + jnp.arange(channels, dtype=jnp.int32))[None, :]
    return (rows + block_size) // block_size == (columns + block_size) // block_size


def gate_dense(gate_w, offset, first, count):
    block_size = gate_w.shape[2]
    total = gate_w.shape[1] * block_size
    channels = total // lax.axis_size("tensor")
    columns = gate_w.transpose(2, 0, 1, 3).reshape(block_size, 2, total)
    columns = lax.dynamic_slice_in_dim(columns, offset, channels, 2)
    copies = -(-count // block_size) + 1
    tall = jnp.concatenate([columns] * copies, axis=0)
    tall = lax.dynamic_slice_in_dim(tall, (first + block_size) % block_size, count, 0)
    same = same_block(first, count, offset, channels, block_size)
    dense = jnp.where(same[:, None, :], tall, jnp.zeros_like(tall))
    return dense.reshape(count, 2 * channels)


def doc_layout(seg_ids, seq_len):
    places = jnp.arange(seg_ids.shape[0], dtype=jnp.int32)
    before = jnp.concatenate([seg_ids[:1], seg_ids[:-1]])
    resets = (places % seq_len == 0) | (seg_ids != before)
    starts = lax.cummax(jnp.where(resets, places, jnp.zeros_like(places)), axis=0)
    return (resets, starts)


def causal_conv(starts, values, kernel):
    places = jnp.arange(values.shape[0], dtype=jnp.int32)
    total = values * kernel[0]
    for offset_k in range(1, kernel.shape[0]):
        moved = jnp.concatenate(
            [jnp.zeros((offset_k, values.shape[1]), values.dtype), values[:-offset_k]], axis=0
        )
        valid = (places - offset_k >= starts)[:, None]
        total = total + jnp.where(valid, moved, jnp.zeros_like(moved)) * kernel[offset_k]
    return total


def geglu(gate_val, up_val):
    return jax.nn.gelu(gate_val, approximate=True) * up_val


def rows_times(left, right):
    return lax.dot_general(left, right, (((1,), (1,)), ((), ())), preferred_element_type=F32)


def rows_back(lefts, rights):
    total = rows_times(lefts[0], rights[0])
    return total + rows_times(lefts[1], rights[1])


def inner_rows(left, right):
    return lax.dot_general(left, right, (((0,), (0,)), ((), ())), preferred_element_type=F32)


def body(
    tokens,
    segments,
    cotangent,
    norm_gain,
    w_y,
    w_x,
    conv_w,
    gate_w,
    decay_param,
    w_out,
    mlp_gain,
    w_gate,
    w_up,
    w_down,
):
    ntensor = lax.axis_size("tensor")
    ndp = lax.axis_size("dp")
    nbits = log2_of(ntensor)
    tindex = lax.axis_index("tensor")
    own_rows, width = tokens.shape
    group_rows = own_rows * ntensor
    block_size = gate_w.shape[2]
    nblocks = gate_w.shape[1]
    dp_rows, channels = w_y.shape
    taps = conv_w.shape[0]
    offset = tindex * channels
    shape = jax.ShapeDtypeStruct
    gain_in = norm_gain.reshape(1, width)
    gain_mid = mlp_gain.reshape(1, width)
    wg_loc = lax.all_gather(w_gate, "dp", axis=0, tiled=True)
    wu_loc = lax.all_gather(w_up, "dp", axis=0, tiled=True)
    wd_loc = lax.all_gather(w_down, "dp", axis=0, tiled=True)

    seg_rows_of = own_rows // 128
    normed_rows, cot_rows, seg_all, wy_loc, wx_loc, wout_loc = call_kernel(
        partial(enter_kernel, nbits),
        (
            shape((group_rows, width), BF16),
            shape((group_rows, width), BF16),
            shape((ntensor, seg_rows_of, 128), jnp.int32),
        )
        + (shape((dp_rows * ndp, channels), BF16),) * 3,
        gather_sems(nbits)
        + gather_sems(nbits)
        + [pltpu.SemaphoreType.DMA((ntensor - 1,)), pltpu.SemaphoreType.DMA((ntensor - 1,))]
        + [pltpu.SemaphoreType.DMA((2,))]
        + line_sems(ndp) * 3,
        0,
        tokens,
        cotangent,
        segments.reshape(seg_rows_of, 128),
        gain_in,
        w_y,
        w_x,
        w_out,
        far_in=(4, 5, 6),
        far_out=(3, 4, 5),
    )
    seg_rows = seg_all.reshape(group_rows)
    resets, starts = doc_layout(seg_rows, group_rows)
    fresh = resets.astype(F32)[:, None]
    conv_loc = lax.dynamic_slice_in_dim(conv_w, offset, channels, 1)
    decay_loc = lax.dynamic_slice_in_dim(decay_param, offset, channels, 0).reshape(1, channels)
    soft = jax.nn.softplus(decay_loc)
    slope_soft = jax.nn.sigmoid(decay_loc)
    rims = gate_rims(channels, block_size, ntensor, offset, tindex)
    own_dense = gate_dense(gate_w, offset, offset, channels)
    rim_dense = [gate_dense(gate_w, offset, rim.first, rim.width) for rim in rims]

    branch_x = jnp.dot(normed_rows, wx_loc, preferred_element_type=F32)
    branch_y = jnp.dot(normed_rows, wy_loc, preferred_element_type=F32)
    conv_out, conv_pull = jax.vjp(partial(causal_conv, starts), branch_x, conv_loc)
    conv_low = conv_out.astype(BF16)
    rim_cells = [rim.fetch(conv_low) for rim in rims]
    gate_pre = jnp.dot(conv_low, own_dense, preferred_element_type=F32)
    for cells, dense in zip(rim_cells, rim_dense):
        gate_pre = gate_pre + jnp.dot(cells, dense, preferred_element_type=F32)
    mixed_low, states = scan_call(
        forward_scan_kernel,
        (shape((group_rows, channels), BF16), shape((group_rows, channels), F32)),
        conv_low,
        gate_pre,
        branch_y,
        soft,
        fresh,
    )
    middle, mid_rows = call_kernel(
        partial(middle_kernel, nbits),
        (shape((own_rows, width), F32), shape((group_rows, width), BF16)),
        scatter_scratch(own_rows, width, nbits) + gather_sems(nbits),
        1,
        rows_times(mixed_low, wout_loc).astype(BF16),
        tokens,
        gain_mid,
    )
    gate_val = jnp.dot(mid_rows, wg_loc, preferred_element_type=F32)
    up_val = jnp.dot(mid_rows, wu_loc, preferred_element_type=F32)
    hidden, act_pull = jax.vjp(geglu, gate_val, up_val)
    hidden_low = hidden.astype(BF16)
    grad_wd = inner_rows(cot_rows, hidden_low).astype(BF16)
    sum_wd = lax.psum_scatter(grad_wd, "dp", scatter_dimension=0, tiled=True)
    grad_wd, wd_loc = lax.optimization_barrier((grad_wd, wd_loc))
    d_hidden = jnp.dot(cot_rows, wd_loc, preferred_element_type=F32)
    d_gate, d_up = act_pull(d_hidden)
    d_gate = d_gate.astype(BF16)
    d_up = d_up.astype(BF16)
    grad_wg = inner_rows(mid_rows, d_gate).astype(BF16)
    sum_wg = lax.psum_scatter(grad_wg, "dp", scatter_dimension=0, tiled=True)
    d_mid_part = rows_back((d_gate, d_up), (wg_loc, wu_loc)).astype(BF16)
    d_mid_part, grad_wg = lax.optimization_barrier((d_mid_part, grad_wg))
    d_middle, d_mixer, d_gain_mid = call_kernel(
        partial(turn_kernel, nbits),
        (
            shape((own_rows, width), F32),
            shape((group_rows, width), BF16),
            shape((8, width), F32),
        ),
        scatter_scratch(own_rows, width, nbits) + gather_sems(nbits),
        2,
        d_mid_part,
        cotangent,
        middle,
        gain_mid,
    )
    d_mixer, sum_wd = lax.optimization_barrier((d_mixer, sum_wd))
    d_mixed_in = jnp.dot(d_mixer, wout_loc, preferred_element_type=F32)
    mid_again, d_mixed_in = lax.optimization_barrier((mid_rows, d_mixed_in))
    grad_wu = inner_rows(mid_again, d_up).astype(BF16)
    sum_wu = lax.psum_scatter(grad_wu, "dp", scatter_dimension=0, tiled=True)
    d_mixed_in, grad_wu = lax.optimization_barrier((d_mixed_in, grad_wu))
    d_conv, d_gate_low, d_branch_y, d_decay = scan_call(
        backward_scan_kernel,
        (
            shape((group_rows, channels), F32),
            shape((group_rows, 2 * channels), BF16),
            shape((group_rows, channels), BF16),
            shape((8, channels), F32),
        ),
        d_mixed_in,
        conv_low,
        gate_pre,
        branch_y,
        states,
        soft,
        slope_soft,
        fresh,
    )
    d_gate_low, sum_wg = lax.optimization_barrier((d_gate_low, sum_wg))
    given = [rows_times(d_gate_low, dense).astype(BF16) for dense in rim_dense]
    taken = [rim.give(part) for rim, part in zip(rims, given)]
    d_conv_out = d_conv + rows_times(d_gate_low, own_dense)
    for rim, part in zip(rims, taken):
        d_conv_out = rim.add(d_conv_out, part)
    d_branch_x, grad_conv_loc = conv_pull(d_conv_out)
    d_branch_x = d_branch_x.astype(BF16)
    unit = math.gcd(channels, block_size)
    base = offset // block_size * block_size - rims[0].room
    window_rows = rims[0].window(channels)
    picked = jnp.zeros((window_rows, 2 * channels), F32)
    for first, cells in [(offset, conv_low)] + [(r.first, c) for r, c in zip(rims, rim_cells)]:
        part = inner_rows(cells, d_gate_low)
        same = same_block(first, cells.shape[1], offset, channels, block_size)
        part = jnp.where(jnp.concatenate([same, same], axis=1), part, 0.0)
        picked = lax.dynamic_update_slice(picked, part, (first - base, jnp.int32(0)))
    picked = picked.reshape(window_rows // block_size, block_size, 2, channels // unit, unit)
    gate_grad = picked.sum(axis=0).astype(BF16).transpose(2, 1, 0, 3)
    gate_grad = gate_grad.reshape(channels // unit * 2 * block_size, unit)

    own_small = jnp.concatenate(
        [
            grad_conv_loc,
            jnp.sum(d_decay, axis=0, keepdims=True),
            jnp.zeros((7 - taps, channels), F32),
        ],
        axis=0,
    )
    grad_wout = inner_rows(d_mixer, mixed_low).astype(BF16)
    grad_wy = inner_rows(normed_rows, d_branch_y).astype(BF16)
    grad_wx = inner_rows(normed_rows, d_branch_x).astype(BF16)
    ffn_part = rows_times(hidden_low, wd_loc).astype(BF16)
    d_normed = rows_back((d_branch_y, d_branch_x), (wy_loc, wx_loc)).astype(BF16)
    merged = nbits <= 2

    def halved(grad):
        return grad.reshape(ndp // 2, 2, grad.shape[0] // ndp, grad.shape[1])

    pieces = [halved(grad) for grad in (gate_grad, grad_wout, grad_wy, grad_wx)]
    peers = ntensor - 1
    gate_rows = gate_grad.shape[0] // ndp
    dma = pltpu.SemaphoreType.DMA
    scratch = scatter_scratch(own_rows, width, nbits)
    for piece in pieces:
        scratch += ring_scratch(ndp, piece.shape[2], piece.shape[3])
    scratch += [
        pltpu.VMEM((8, width), F32),
        pltpu.VMEM((ntensor, 8, channels), F32),
        pltpu.VMEM((peers, 8, channels), F32),
        pltpu.VMEM((8, channels), F32),
        pltpu.VMEM((ndp - 1, 8, channels), F32),
    ]
    scratch += [dma((peers,)), dma((peers,)), dma((ndp - 1,)), dma((ndp - 1,))]
    scratch += [dma((peers,)), dma((peers,)), dma((peers + ndp,)), dma((peers + ndp,))]
    if merged:
        scratch += scatter_scratch(own_rows, width, nbits)
    found = call_kernel(
        partial(leave_kernel, nbits, merged),
        (shape((own_rows, width), F32),)
        + (shape((dp_rows, channels), F32),) * 3
        + (
            shape((ndp, ntensor, gate_rows, unit), BF16),
            shape((ntensor, 8, channels), F32),
        )
        + ((shape((own_rows, width), BF16),) if merged else ()),
        scratch,
        3,
        d_normed,
        tokens,
        d_middle,
        gain_in,
        own_small,
        d_gain_mid,
        *pieces,
        *((ffn_part, middle) if merged else ()),
        far_in=(6, 7, 8, 9),
    )
    grad_input, sum_wout, sum_wy, sum_wx, gate_all, small_all = found[:6]
    if merged:
        mixed = found[6]
    else:
        (mixed,) = call_kernel(
            partial(result_kernel, nbits),
            (shape((own_rows, width), BF16),),
            scatter_scratch(own_rows, width, nbits),
            4,
            ffn_part,
            middle,
        )
    per_block = block_size // unit
    sum_gate = gate_all.transpose(1, 0, 2, 3).reshape(nblocks, per_block, 2, block_size, unit)
    sum_gate = sum_gate.transpose(2, 0, 3, 1, 4).reshape(gate_w.shape).astype(F32)
    summed = small_all.transpose(1, 0, 2).reshape(8, width)
    return (
        mixed,
        grad_input,
        summed[6],
        sum_wy,
        sum_wx,
        summed[:taps],
        sum_gate,
        summed[taps],
        sum_wout,
        summed[7],
        sum_wg.astype(F32),
        sum_wu.astype(F32),
        sum_wd.astype(F32),
    )


def solution(mesh):
    split = P(("dp", "tensor"), None)
    weight = P("dp", "tensor")
    return jax.shard_map(
        body,
        mesh=mesh,
        in_specs=(
            split,
            P(("dp", "tensor")),
            split,
            P(),
            weight,
            weight,
            P(),
            P(),
            P(),
            weight,
            P(),
            weight,
            weight,
            weight,
        ),
        out_specs=(
            split,
            split,
            P(),
            weight,
            weight,
            P(),
            P(),
            P(),
            weight,
            P(),
            weight,
            weight,
            weight,
        ),
        check_vma=False,
    )
```

```python
import math
from functools import partial

import jax
import jax.numpy as jnp
from jax import lax
from jax.experimental import pallas as pl
from jax.experimental.pallas import tpu as pltpu
from jax.sharding import PartitionSpec as P

EPSILON = 1e-06
MESH = pl.DeviceIdType.MESH
VMEM_BYTES = 56 * 1024 * 1024
CHUNK = 16
F32 = jnp.float32
BF16 = jnp.bfloat16


def subsets(bits):
    found = [()]
    for bit in bits:
        found = found + [chosen + (bit,) for chosen in found]
    return found


def flipped(index, bits):
    for bit in bits:
        mine = (index // (1 << bit)) % 2
        index = index + (1 - 2 * mine) * (1 << bit)
    return index


def log2_of(count):
    assert count & (count - 1) == 0
    return count.bit_length() - 1


def greet(axis_bits):
    barrier = pltpu.get_barrier_semaphore()
    for axis, bit in axis_bits:
        peer = flipped(lax.axis_index(axis), (bit,))
        pl.semaphore_signal(barrier, inc=1, device_id={axis: peer}, device_id_type=MESH)
    pl.semaphore_wait(barrier, len(axis_bits))


def halves_of(nbits, columns):
    half = columns // 2
    ups = tuple(range(nbits))
    return ((ups, 0, half), (ups[::-1], half, half))


class Gather:
    def __init__(self, ref, rows, nbits, send_sems, recv_sems):
        self.ref, self.rows, self.nbits = ref, rows, nbits
        self.sems = (send_sems, recv_sems)
        self.me = lax.axis_index("tensor")
        self.plan = []
        number = 0
        for half, (order, at, width) in enumerate(halves_of(nbits, ref.shape[1])):
            for step, bit in enumerate(order):
                for known in subsets(order[:step]):
                    self.plan.append((half, step, known, bit, at, width, number))
                    number += 1
        self.count = number

    def copy(self, item):
        half, step, known, bit, at, width, number = item
        row = pl.multiple_of(flipped(self.me, known) * self.rows, self.rows)
        piece = self.ref.at[pl.ds(row, self.rows), pl.ds(at, width)]
        return pltpu.make_async_remote_copy(
            src_ref=piece,
            dst_ref=piece,
            send_sem=self.sems[0].at[number],
            recv_sem=self.sems[1].at[number],
            device_id={"tensor": flipped(self.me, (bit,))},
            device_id_type=MESH,
        )

    def begin(self):
        for item in sorted(self.plan, key=lambda it: it[1]):
            if item[2] == ():
                self.copy(item).start()

    def finish(self):
        arrived = sorted(self.plan, key=lambda it: (it[1], it[0]))
        for item in arrived:
            half, step, known, bit, at, width, number = item
            self.copy(item).wait_recv()
            block = known + (bit,)
            for later in self.plan:
                if later[0] == half and set(later[2]) == set(block):
                    self.copy(later).start()
        for item in self.plan:
            self.copy(item).wait_send()


def gather_copies(nbits):
    return 2 * ((1 << nbits) - 1)


class Scatter:
    def __init__(self, ref, landed, staged, rows, nbits, send_sems, recv_sems):
        self.ref, self.landed, self.staged = ref, landed, staged
        self.rows, self.nbits = rows, nbits
        self.sems = (send_sems, recv_sems)
        self.me = lax.axis_index("tensor")
        self.plan, self.slot = [], {}
        number = 0
        for half, (order, at, width) in enumerate(halves_of(nbits, ref.shape[1])):
            for step, bit in enumerate(order):
                for rest in subsets(order[step + 1 :])[::-1]:
                    self.plan.append((half, step, rest, bit, at, width, number))
                    if step > 0:
                        self.slot[number] = len(self.slot)
                    number += 1

    def copy(self, item):
        half, step, rest, bit, at, width, number = item
        if step == 0:
            row = pl.multiple_of(flipped(self.me, rest + (bit,)) * self.rows, self.rows)
            source = self.ref.at[pl.ds(row, self.rows), pl.ds(at, width)]
        else:
            source = self.staged.at[self.slot[number]]
        return pltpu.make_async_remote_copy(
            src_ref=source,
            dst_ref=self.landed.at[number],
            send_sem=self.sems[0].at[number],
            recv_sem=self.sems[1].at[number],
            device_id={"tensor": flipped(self.me, (bit,))},
            device_id_type=MESH,
        )

    def begin(self):
        for item in sorted(self.plan, key=lambda it: (len(it[2]) == 0)):
            if item[1] == 0:
                self.copy(item).start()

    def partial_sum(self, half, block, before, row, size):
        at, width = halves_of(self.nbits, self.ref.shape[1])[half][1:]
        base = pl.multiple_of(flipped(self.me, block) * self.rows + row, size)
        total = self.ref[pl.ds(base, size), pl.ds(at, width)].astype(F32)
        for it in self.plan:
            if it[0] == half and it[1] < before and set(it[2]) == set(block):
                total = total + self.landed[it[6], pl.ds(row, size), :].astype(F32)
        return total

    def advance(self, step):
        for half in range(2):
            for item in self.plan:
                if item[0] == half and item[1] == step:
                    self.copy(item).wait_recv()
            for item in self.plan:
                if item[0] == half and item[1] == step + 1:

                    def fill(row, item=item):
                        value = self.partial_sum(
                            item[0], item[2] + (item[3],), item[1], row, CHUNK
                        )
                        where = (self.slot[item[6]], pl.ds(row, CHUNK))
                        self.staged[where + (slice(None),)] = value.astype(BF16)

                    chunks(self.rows, fill)
                    self.copy(item).start()

    def run(self):
        for step in range(self.nbits):
            self.advance(step)

    def total(self, row, size):
        return jnp.concatenate(
            [self.partial_sum(half, (), self.nbits, row, size) for half in range(2)], axis=1
        )

    def drain(self):
        for item in self.plan:
            self.copy(item).wait_send()


def scatter_scratch(rows, columns, nbits):
    copies = gather_copies(nbits)
    later = max(1, copies - (1 << nbits))
    return [
        pltpu.VMEM((copies, rows, columns // 2), BF16),
        pltpu.VMEM((later, rows, columns // 2), BF16),
        pltpu.SemaphoreType.DMA((copies,)),
        pltpu.SemaphoreType.DMA((copies,)),
    ]


def gather_sems(nbits):
    copies = gather_copies(nbits)
    return [pltpu.SemaphoreType.DMA((copies,)), pltpu.SemaphoreType.DMA((copies,))]


def tensor_bits(nbits):
    return [("tensor", bit) for bit in range(nbits)]


def rms_scale_of(values):
    return lax.rsqrt(jnp.mean(values * values, axis=-1, keepdims=True) + EPSILON)


def chunks(rows, body):
    def step(i, carry):
        body(pl.multiple_of(i * CHUNK, CHUNK))
        return carry

    lax.fori_loop(0, rows // CHUNK, step, 0)


def own_row(row, rows):
    return pl.multiple_of(lax.axis_index("tensor") * rows + row, CHUNK)


def dp_place():
    me = lax.axis_index("dp")
    return me // 2, me % 2, lax.axis_size("dp") // 2


def dp_index(chip, core):
    return chip * 2 + core


def shift_order(count):
    return sorted(range(1, count), key=lambda shift: min(shift, count - shift))


class LineGather:
    def __init__(self, own, whole, send_sems, recv_sems):
        self.own, self.whole = own, whole
        self.sems = (send_sems, recv_sems)
        self.chip, self.core, self.chips = dp_place()
        self.rows = own.shape[0]

    def block(self, chip, core):
        row = pl.multiple_of(dp_index(chip, core) * self.rows, self.rows)
        return self.whole.at[pl.ds(row, self.rows), :]

    def along(self, shift):
        return pltpu.make_async_remote_copy(
            src_ref=self.own,
            dst_ref=self.block(self.chip, self.core),
            send_sem=self.sems[0].at[shift],
            recv_sem=self.sems[1].at[shift],
            device_id={"dp": dp_index((self.chip + shift) % self.chips, self.core)},
            device_id_type=MESH,
        )

    def across(self, shift):
        block = self.block((self.chip + self.chips - shift) % self.chips, self.core)
        number = self.chips + shift
        return pltpu.make_async_remote_copy(
            src_ref=self.own if shift == 0 else block,
            dst_ref=block,
            send_sem=self.sems[0].at[number],
            recv_sem=self.sems[1].at[number],
            device_id={"dp": dp_index(self.chip, 1 - self.core)},
            device_id_type=MESH,
        )

    def local(self):
        return pltpu.make_async_copy(
            self.own, self.block(self.chip, self.core), self.sems[0].at[2 * self.chips]
        )

    def begin(self):
        for shift in shift_order(self.chips):
            self.along(shift).start()
        self.across(0).start()
        self.local().start()

    def pass_on(self):
        for shift in shift_order(self.chips):
            self.along(shift).wait_recv()
            self.across(shift).start()

    def finish(self):
        for shift in range(self.chips):
            self.across(shift).wait()
        for shift in range(1, self.chips):
            self.along(shift).wait_send()
        self.local().wait()


def line_sems(ndp):
    return [pltpu.SemaphoreType.DMA((ndp + 1,)), pltpu.SemaphoreType.DMA((ndp + 1,))]


def greet_peers(nbits, whole_dp):
    me = lax.axis_index("tensor")
    chip, core, chips = dp_place()
    barrier = pltpu.get_barrier_semaphore()
    met = 0
    for chosen in subsets(tuple(range(nbits))):
        if chosen:
            pl.semaphore_signal(
                barrier, inc=1, device_id={"tensor": flipped(me, chosen)}, device_id_type=MESH
            )
            met += 1
    for shift in range(chips):
        for turn in range(2):
            if (shift, turn) == (0, 0) or (shift and turn and not whole_dp):
                continue
            other = dp_index((chip + shift) % chips, core + turn * (1 - 2 * core))
            pl.semaphore_signal(
                barrier, inc=1, device_id={"dp": other}, device_id_type=MESH
            )
            met += 1
    pl.semaphore_wait(barrier, met)


def enter_kernel(
    nbits,
    tokens,
    cot,
    seg,
    gain,
    w_y,
    w_x,
    w_out,
    normed_all,
    cot_all,
    seg_all,
    wy_all,
    wx_all,
    wout_all,
    s0,
    r0,
    s1,
    r1,
    s2,
    r2,
    l0,
    *line,
):
    rows = tokens.shape[0]
    me = lax.axis_index("tensor")
    peers = [chosen for chosen in subsets(tuple(range(nbits))) if chosen]
    greet_peers(nbits, False)
    lines = [
        LineGather(own, whole, line[2 * number], line[2 * number + 1])
        for number, (own, whole) in enumerate(((w_y, wy_all), (w_x, wx_all), (w_out, wout_all)))
    ]
    lines[0].begin()
    lines[1].begin()

    def norm(row):
        values = tokens[pl.ds(row, CHUNK), :].astype(F32)
        scaled = values * rms_scale_of(values) * gain[...]
        normed_all[pl.ds(own_row(row, rows), CHUNK), :] = scaled.astype(BF16)

    chunks(rows, norm)
    first = Gather(normed_all, rows, nbits, s0, r0)
    first.begin()
    cot_own = cot_all.at[pl.ds(pl.multiple_of(me * rows, rows), rows), :]
    local = pltpu.make_async_copy(cot, cot_own, l0.at[0])
    local.start()
    seg_own = pltpu.make_async_copy(seg, seg_all.at[me], l0.at[1])
    seg_own.start()
    seg_copies = [
        pltpu.make_async_remote_copy(
            src_ref=seg,
            dst_ref=seg_all.at[me],
            send_sem=s2.at[number],
            recv_sem=r2.at[number],
            device_id={"tensor": flipped(me, chosen)},
            device_id_type=MESH,
        )
        for number, chosen in enumerate(peers)
    ]
    for copy in seg_copies:
        copy.start()
    local.wait()
    second = Gather(cot_all, rows, nbits, s1, r1)
    second.begin()
    first.finish()
    lines[0].pass_on()
    lines[1].pass_on()
    lines[2].begin()
    second.finish()
    lines[2].pass_on()
    for item in lines:
        item.finish()
    for copy in seg_copies:
        copy.wait()
    seg_own.wait()


def middle_kernel(
    nbits, mixer, tokens, gain, middle, mid_all, landed, staged, s0, r0, s1, r1
):
    rows = tokens.shape[0]
    greet(tensor_bits(nbits))
    scatter = Scatter(mixer, landed, staged, rows, nbits, s0, r0)
    scatter.begin()
    scatter.run()

    def norm(row):
        values = tokens[pl.ds(row, CHUNK), :].astype(F32) + scatter.total(row, CHUNK)
        middle[pl.ds(row, CHUNK), :] = values
        scaled = values * rms_scale_of(values) * gain[...]
        mid_all[pl.ds(own_row(row, rows), CHUNK), :] = scaled.astype(BF16)

    chunks(rows, norm)
    gather = Gather(mid_all, rows, nbits, s1, r1)
    gather.begin()
    gather.finish()
    scatter.drain()


def result_kernel(nbits, ffn, middle, mixed, landed, staged, s0, r0):
    rows = middle.shape[0]
    greet(tensor_bits(nbits))
    scatter = Scatter(ffn, landed, staged, rows, nbits, s0, r0)
    scatter.begin()
    scatter.run()

    def add(row):
        values = middle[pl.ds(row, CHUNK), :] + scatter.total(row, CHUNK)
        mixed[pl.ds(row, CHUNK), :] = values.astype(BF16)

    chunks(rows, add)
    scatter.drain()


def norm_pull(values, gain, cotangent):
    scale = rms_scale_of(values)
    unit = values * scale
    inner = cotangent * gain
    back = scale * (inner - unit * jnp.mean(inner * unit, axis=-1, keepdims=True))
    return back, cotangent * unit


def eight_rows(values):
    total = values[0:8]
    for at in range(8, CHUNK, 8):
        total = total + values[at : at + 8]
    return total


def turn_kernel(
    nbits, d_norm, cot, middle, gain, d_middle, d_mixer, d_gain, landed, staged, s0, r0, s1, r1
):
    rows = middle.shape[0]
    greet(tensor_bits(nbits))
    scatter = Scatter(d_norm, landed, staged, rows, nbits, s0, r0)
    scatter.begin()
    d_gain[...] = jnp.zeros_like(d_gain)
    scatter.run()

    def pull(row):
        span = pl.ds(row, CHUNK)
        back, gains = norm_pull(middle[span, :], gain[...], scatter.total(row, CHUNK))
        values = cot[span, :].astype(F32) + back
        d_middle[span, :] = values
        d_mixer[pl.ds(own_row(row, rows), CHUNK), :] = values.astype(BF16)
        d_gain[...] += eight_rows(gains)

    chunks(rows, pull)
    gather = Gather(d_mixer, rows, nbits, s1, r1)
    gather.begin()
    gather.finish()
    scatter.drain()


class LineRing:
    def __init__(self, whole, kept, swapped, staged, landed, send_sems, recv_sems):
        self.whole, self.kept, self.swapped = whole, kept, swapped
        self.staged, self.landed = staged, landed
        self.sems = (send_sems, recv_sems)
        self.chip, self.core, self.chips = dp_place()
        self.rows = whole.shape[2]

    def local(self):
        return pltpu.make_async_copy(
            self.whole.at[:, self.core], self.kept, self.sems[0].at[self.chips]
        )

    def swap(self):
        return pltpu.make_async_remote_copy(
            src_ref=self.whole.at[:, 1 - self.core],
            dst_ref=self.swapped,
            send_sem=self.sems[0].at[0],
            recv_sem=self.sems[1].at[0],
            device_id={"dp": dp_index(self.chip, 1 - self.core)},
            device_id_type=MESH,
        )

    def hop(self, step):
        return pltpu.make_async_remote_copy(
            src_ref=self.staged.at[step - 1],
            dst_ref=self.landed.at[step - 1],
            send_sem=self.sems[0].at[step],
            recv_sem=self.sems[1].at[step],
            device_id={"dp": dp_index((self.chip + 1) % self.chips, self.core)},
            device_id_type=MESH,
        )

    def begin(self):
        self.local().start()
        self.swap().start()

    def value(self, step, span):
        chip = (self.chip + self.chips - step) % self.chips
        total = self.kept[chip, span, :].astype(F32) + self.swapped[chip, span, :].astype(F32)
        if step != 1:
            before = (step if step else self.chips) - 2
            total = total + self.landed[before, span, :].astype(F32)
        return total

    def advance(self, step):
        if step == 1:
            self.local().wait()
            self.swap().wait_recv()
        else:
            self.hop(step - 1).wait_recv()

        def fill(row):
            span = pl.ds(row, CHUNK)
            self.staged[step - 1, span, :] = self.value(step, span).astype(BF16)

        chunks(self.rows, fill)
        self.hop(step).start()

    def finish(self, store):
        self.hop(self.chips - 1).wait_recv()

        def fill(row):
            span = pl.ds(row, CHUNK)
            store(span, self.value(0, span))

        chunks(self.rows, fill)

    def drain(self):
        self.swap().wait_send()
        for step in range(1, self.chips):
            self.hop(step).wait_send()


def ring_scratch(ndp, rows, columns):
    chips = ndp // 2
    return [
        pltpu.VMEM((chips, rows, columns), BF16),
        pltpu.VMEM((chips, rows, columns), BF16),
        pltpu.VMEM((chips - 1, rows, columns), BF16),
        pltpu.VMEM((chips - 1, rows, columns), BF16),
        pltpu.SemaphoreType.DMA((chips + 1,)),
        pltpu.SemaphoreType.DMA((chips + 1,)),
    ]


RING = 6


def leave_kernel(nbits, with_ffn, *refs):
    refs = list(refs)

    def take(count):
        taken = refs[:count]
        del refs[:count]
        return taken

    d_norm, tokens, d_middle, gain, own_small, d_gain_mid = take(6)
    pieces = take(3)
    ffn, middle = take(2) if with_ffn else (None, None)
    grad_input, sum_y, sum_x, gate_all, small_all = take(5)
    mixed = take(1)[0] if with_ffn else None
    landed, staged, s0, r0 = take(4)
    rings = [LineRing(piece, *take(RING)) for piece in pieces]
    d_gain, gains, gains_landed, small, small_landed = take(5)
    gain_s, gain_r, vec_s, vec_r, join_s, join_r, gate_s, gate_r = take(8)
    rows = tokens.shape[0]
    me = lax.axis_index("tensor")
    chip, core, chips = dp_place()
    place = dp_index(chip, core)
    peers = [chosen for chosen in subsets(tuple(range(nbits))) if chosen]
    others = [(shift, turn) for shift in range(chips) for turn in range(2)][1:]
    greet_peers(nbits, True)
    for ring in rings:
        ring.begin()
    scatter = Scatter(d_norm, landed, staged, rows, nbits, s0, r0)
    scatter.begin()
    if with_ffn:
        second = Scatter(ffn, *take(2), rows, nbits, *take(2))
    d_gain[...] = jnp.zeros_like(d_gain)
    for ring in rings:
        ring.advance(1)
    if chips > 2:
        rings[0].advance(2)
    scatter.advance(0)
    if with_ffn:
        second.begin()
    if chips > 2:
        for ring in rings[1:]:
            ring.advance(2)
    for step in range(3, chips):
        rings[0].advance(step)
    for step in range(1, nbits):
        scatter.advance(step)

    def pull(row):
        span = pl.ds(row, CHUNK)
        back, parts = norm_pull(
            tokens[span, :].astype(F32), gain[...], scatter.total(row, CHUNK)
        )
        grad_input[span, :] = d_middle[span, :] + back
        d_gain[...] += eight_rows(parts)

    chunks(rows, pull)
    share = gains.shape[2]
    top = jnp.sum(d_gain[...], axis=0, keepdims=True)
    low = jnp.sum(d_gain_mid[...], axis=0, keepdims=True)
    place8 = lax.broadcasted_iota(jnp.int32, (8, share), 0)
    for index in range(1 << nbits):
        span = slice(index * share, (index + 1) * share)
        gains[index] = jnp.where(
            place8 == 6, top[:, span], jnp.where(place8 == 7, low[:, span], 0.0)
        )

    def gain_copy(number, chosen):
        peer = flipped(me, chosen)
        return pltpu.make_async_remote_copy(
            src_ref=gains.at[peer],
            dst_ref=gains_landed.at[number],
            send_sem=gain_s.at[number],
            recv_sem=gain_r.at[number],
            device_id={"tensor": peer},
            device_id_type=MESH,
        )

    for number, chosen in enumerate(peers):
        gain_copy(number, chosen).start()
    for step in range(3, chips):
        for ring in rings[1:]:
            ring.advance(step)
    total = own_small[...] + gains[me]
    for number, chosen in enumerate(peers):
        gain_copy(number, chosen).wait_recv()
        total = total + gains_landed[number]
    small[...] = total

    def vec_copy(number, shift, turn):
        other = dp_index((chip + shift) % chips, core + turn * (1 - 2 * core))
        return pltpu.make_async_remote_copy(
            src_ref=small,
            dst_ref=small_landed.at[number],
            send_sem=vec_s.at[number],
            recv_sem=vec_r.at[number],
            device_id={"dp": other},
            device_id_type=MESH,
        )

    for number, (shift, turn) in enumerate(others):
        vec_copy(number, shift, turn).start()

    def store_gate(span, value):
        gate_all[me, place, span, :] = value.astype(BF16)

    rings[0].finish(store_gate)

    def gate_copy(number, chip_from, ref, target):
        return pltpu.make_async_remote_copy(
            src_ref=ref,
            dst_ref=ref,
            send_sem=gate_s.at[number],
            recv_sem=gate_r.at[number],
            device_id=target,
            device_id_type=MESH,
        )

    def gate_tensor(number, chosen):
        ref = gate_all.at[me, place]
        return gate_copy(number, chip, ref, {"tensor": flipped(me, chosen)})

    def gate_line(shift):
        target = {"dp": dp_index((chip + shift) % chips, core)}
        return gate_copy(len(peers) + shift - 1, chip, gate_all.at[:, place], target)

    def gate_core(shift):
        ref = gate_all.at[:, dp_index((chip + chips - shift) % chips, core)]
        target = {"dp": dp_index(chip, 1 - core)}
        return gate_copy(len(peers) + chips - 1 + shift, chip, ref, target)

    for number, chosen in enumerate(peers):
        gate_tensor(number, chosen).start()
    if with_ffn:
        second.advance(0)
    total = small[...]
    for number, (shift, turn) in enumerate(others):
        vec_copy(number, shift, turn).wait_recv()
        total = total + small_landed[number]
    small_all[me] = total

    def join_copy(number, chosen):
        return pltpu.make_async_remote_copy(
            src_ref=small_all.at[me],
            dst_ref=small_all.at[me],
            send_sem=join_s.at[number],
            recv_sem=join_r.at[number],
            device_id={"tensor": flipped(me, chosen)},
            device_id_type=MESH,
        )

    for number, chosen in enumerate(peers):
        join_copy(number, chosen).start()
    for number, chosen in enumerate(peers):
        gate_tensor(number, chosen).wait_recv()
    for shift in range(1, chips):
        gate_line(shift).start()
    gate_core(0).start()
    if with_ffn:
        for step in range(1, nbits):
            second.advance(step)

        def add(row):
            span = pl.ds(row, CHUNK)
            mixed[span, :] = (middle[span, :] + second.total(row, CHUNK)).astype(BF16)

        chunks(rows, add)
    for shift in shift_order(chips):
        gate_line(shift).wait_recv()
        gate_core(shift).start()

    def store_in(ref):
        def store(span, value):
            ref[span, :] = value

        return store

    for ring, ref in zip(rings[1:], (sum_y, sum_x)):
        ring.finish(store_in(ref))
    for shift in range(chips):
        gate_core(shift).wait()
    for shift in range(1, chips):
        gate_line(shift).wait_send()
    for number, chosen in enumerate(peers):
        gate_tensor(number, chosen).wait_send()
        gain_copy(number, chosen).wait_send()
        join_copy(number, chosen).wait()
    for number, (shift, turn) in enumerate(others):
        vec_copy(number, shift, turn).wait_send()
    scatter.drain()
    if with_ffn:
        second.drain()
    for ring in rings:
        ring.drain()


def in_vmem(count):
    return [pl.BlockSpec(memory_space=pltpu.VMEM)] * count


def call_kernel(kernel, outs, scratch, number, *operands, far_in=(), far_out=(), cost_us=1):
    vmem = pl.BlockSpec(memory_space=pltpu.VMEM)
    far = pl.BlockSpec(memory_space=pl.ANY)
    return pl.pallas_call(
        kernel,
        out_shape=outs,
        in_specs=[far if i in far_in else vmem for i in range(len(operands))],
        out_specs=tuple(far if i in far_out else vmem for i in range(len(outs))),
        scratch_shapes=scratch,
        cost_estimate=pl.CostEstimate(
            flops=0, bytes_accessed=cost_us * 1_000_000, transcendentals=0
        ),
        compiler_params=pltpu.CompilerParams(
            collective_id=number, has_side_effects=True, vmem_limit_bytes=VMEM_BYTES
        ),
    )(*operands)


def sigmoid(values):
    return 1.0 / (1.0 + jnp.exp(-values))


def one_minus_exp(values):
    series = values / 7.0 + 1.0
    for order in (6.0, 5.0, 4.0, 3.0, 2.0):
        series = 1.0 + series * values / order
    return jnp.where(values > -0.3, -values * series, 1.0 - jnp.exp(values))


GELU_K = 0.7978845608028654
GELU_C = 0.044715


def gelu_parts(values):
    square = values * values
    bent = jnp.tanh(GELU_K * values * (1.0 + GELU_C * square))
    gelu = 0.5 * values * (1.0 + bent)
    slope = 0.5 * (1.0 + bent) + 0.5 * values * (1.0 - bent * bent) * GELU_K * (
        1.0 + 3.0 * GELU_C * square
    )
    return gelu, slope


def gate_terms(gate_a, gate_x, soft, since):
    sig_a = sigmoid(gate_a)
    sig_x = sigmoid(gate_x)
    log_decay = -8.0 * sig_a * soft
    decay = jnp.exp(log_decay)
    scale = jnp.sqrt(one_minus_exp(2.0 * log_decay))
    keep = since > 0.5
    return sig_a, sig_x, decay, jnp.where(keep, scale, 1.0), keep


def scan_down(decay, value, carry):
    place = lax.broadcasted_iota(jnp.int32, decay.shape, 0)
    for shift in (1, 2, 4):
        past = place >= shift
        moved = pltpu.roll(value, shift, 0)
        value = jnp.where(past, decay * moved + value, value)
        decay = jnp.where(past, decay * pltpu.roll(decay, shift, 0), decay)
    return decay * carry + value


def scan_up(decay, value, carry):
    place = lax.broadcasted_iota(jnp.int32, decay.shape, 0)
    factor = jnp.where(place < 7, pltpu.roll(decay, 7, 0), 1.0)
    for shift in (1, 2, 4):
        past = place < 8 - shift
        moved = pltpu.roll(value, 8 - shift, 0)
        value = jnp.where(past, factor * moved + value, value)
        factor = jnp.where(past, factor * pltpu.roll(factor, 8 - shift, 0), factor)
    return factor * carry + value


def forward_scan(conv_rows, gates, branch_y, soft, since, mixed, states):
    total_rows, width = states.shape

    def step(i, carry):
        row = pl.multiple_of(i * CHUNK, CHUNK)
        span = pl.ds(row, CHUNK)
        values = conv_rows(span).astype(F32)
        kept = []
        for at in range(0, CHUNK, 8):
            tile = pl.ds(row + at, 8)
            sig_a, sig_x, decay, scale, keep = gate_terms(
                gates[tile, :width], gates[tile, width:], soft[...], since[tile, :]
            )
            given = values[at : at + 8] * sig_x * scale
            state = scan_down(jnp.where(keep, decay, 0.0), given, carry)
            carry = state[7:8]
            states[tile, :] = state
            kept.append(state * gelu_parts(branch_y[tile, :])[0])
        mixed[span, :] = jnp.concatenate(kept, axis=0).astype(BF16)
        return carry

    lax.fori_loop(0, total_rows // CHUNK, step, jnp.zeros((1, width), F32))


def forward_scan_kernel(conv, gates, branch_y, soft, since, mixed, states):
    forward_scan(lambda span: conv[span, :], gates, branch_y, soft, since, mixed, states)


def backward_scan(
    d_mixed, conv_rows, gates, branch_y, states, soft, slope_soft, since, d_conv, d_gates, d_branch, d_decay
):
    total_rows, width = states.shape
    d_decay[...] = jnp.zeros_like(d_decay)

    def step(i, carry):
        row = pl.multiple_of(total_rows - CHUNK - i * CHUNK, CHUNK)
        span = pl.ds(row, CHUNK)
        values = conv_rows(span).astype(F32)
        kept = []
        for at in range(CHUNK - 8, -1, -8):
            tile = pl.ds(row + at, 8)
            soft_row = soft[...]
            sig_a, sig_x, decay, scale, keep = gate_terms(
                gates[tile, :width], gates[tile, width:], soft_row, since[tile, :]
            )
            value = values[at : at + 8]
            gelu, slope = gelu_parts(branch_y[tile, :])
            state = states[tile, :]
            upper = d_mixed[tile, :]
            held = jnp.where(keep, decay, 0.0)
            lam = scan_up(held, upper * gelu, carry)
            carry = held[0:1] * lam[0:1]
            d_conv[tile, :] = lam * sig_x * scale
            d_x = lam * value * scale * sig_x * (1.0 - sig_x)
            given = value * sig_x
            d_log = lam * (state - given * scale - given * decay * decay / scale)
            d_log = jnp.where(keep, d_log, 0.0)
            d_a = d_log * (-8.0 * soft_row) * sig_a * (1.0 - sig_a)
            d_decay[...] += d_log * (-8.0 * sig_a) * slope_soft[...]
            kept.append((d_a, d_x, upper * state * slope))
        kept = kept[::-1]
        d_gates[span, :width] = jnp.concatenate([k[0] for k in kept], axis=0).astype(BF16)
        d_gates[span, width:] = jnp.concatenate([k[1] for k in kept], axis=0).astype(BF16)
        d_branch[span, :] = jnp.concatenate([k[2] for k in kept], axis=0).astype(BF16)
        return carry

    lax.fori_loop(0, total_rows // CHUNK, step, jnp.zeros((1, width), F32))


def backward_scan_kernel(
    d_mixed, conv, gates, branch_y, states, soft, slope_soft, since, d_conv, d_gates, d_branch, d_decay
):
    backward_scan(
        d_mixed,
        lambda span: conv[span, :],
        gates,
        branch_y,
        states,
        soft,
        slope_soft,
        since,
        d_conv,
        d_gates,
        d_branch,
        d_decay,
    )


def times_transposed(left, right):
    return lax.dot_general(left, right, (((1,), (1,)), ((), ())), preferred_element_type=F32)


class HalfBlocks:
    def __init__(self, channels, block):
        self.odd = lax.axis_index("tensor") % 2
        self.half = block // 2
        self.block = block
        self.count = channels // block + 1
        self.channels = channels
        self.own = pl.multiple_of(self.odd * self.half, self.half)
        self.shared = (1 - self.odd) * (self.count - 1)
        self.mine_in_block = pl.multiple_of(self.odd * self.half, self.half)
        self.other_in_block = pl.multiple_of((1 - self.odd) * self.half, self.half)
        self.mine = pl.multiple_of((1 - self.odd) * (channels - self.half), self.half)
        self.pair = {"tensor": lax.axis_index("tensor") + 1 - 2 * self.odd}

    def full(self, index):
        block = index + self.odd
        return block, pl.multiple_of(index * self.block + self.odd * self.half, self.half)

    def span(self, block):
        return pl.ds(pl.multiple_of(block * self.block, self.block), self.block)

    def shared_part(self, start):
        return pl.ds(pl.multiple_of(self.shared * self.block + start, self.half), self.half)


PART = 256


def parts(rows, body):
    def step(i, carry):
        body(pl.ds(pl.multiple_of(i * PART, PART), PART))
        return carry

    lax.fori_loop(0, rows // PART, step, 0)


def recurrence_kernel(
    taps, branch_x, branch_y, tap_rows, soft, since, weights, mixed, states, window, gates, send, recv
):
    total_rows, width = states.shape
    block = weights.shape[2]
    place = HalfBlocks(width, block)
    barrier = pltpu.get_barrier_semaphore()
    pl.semaphore_signal(barrier, inc=1, device_id=place.pair, device_id_type=MESH)

    def conv(i, before):
        row = pl.multiple_of(i * CHUNK, CHUNK)
        kept = []
        for at in range(0, CHUNK, 8):
            tile = pl.ds(row + at, 8)
            values = branch_x[tile, :]
            line = lax.broadcasted_iota(jnp.int32, values.shape, 0)
            total = values * tap_rows[0:1, :]
            for tap in range(1, taps):
                moved = jnp.where(
                    line < tap, pltpu.roll(before, tap, 0), pltpu.roll(values, tap, 0)
                )
                moved = jnp.where(since[tile, :] > tap - 0.5, moved, 0.0)
                total = total + moved * tap_rows[tap : tap + 1, :]
            kept.append(total)
            before = values
        window[pl.ds(row, CHUNK), pl.ds(place.own, width)] = jnp.concatenate(
            kept, axis=0
        ).astype(BF16)
        return before

    lax.fori_loop(0, total_rows // CHUNK, conv, jnp.zeros((8, width), F32))
    pl.semaphore_wait(barrier, 1)
    source = window.at[:, place.shared_part(place.mine_in_block)]
    away = pl.multiple_of(place.odd * (place.count - 1) * block + place.mine_in_block, place.half)
    rim = pltpu.make_async_remote_copy(
        src_ref=source,
        dst_ref=window.at[:, pl.ds(away, place.half)],
        send_sem=send.at[0],
        recv_sem=recv.at[0],
        device_id=place.pair,
        device_id_type=MESH,
    )
    rim.start()

    def full(span):
        for index in range(place.count - 1):
            number, at = place.full(index)
            cells = window[span, place.span(number)]
            for s in range(2):
                gates[span, pl.ds(s * width + at, block)] = jnp.dot(
                    cells, weights[s, number], preferred_element_type=F32
                )

    parts(total_rows, full)
    rim.wait()

    def shared(span):
        cells = window[span, place.span(place.shared)]
        for s in range(2):
            gates[span, pl.ds(s * width + place.mine, place.half)] = jnp.dot(
                cells,
                weights[s, place.shared, :, pl.ds(place.mine_in_block, place.half)],
                preferred_element_type=F32,
            )

    parts(total_rows, shared)
    forward_scan(
        lambda span: window[span, pl.ds(place.own, width)],
        gates,
        branch_y,
        soft,
        since,
        mixed,
        states,
    )


def recurrence_back_kernel(
    taps,
    d_mixed,
    window,
    gates,
    branch_y,
    branch_x,
    states,
    tap_rows,
    soft,
    slope_soft,
    since,
    weights,
    d_branch_y,
    d_branch_x,
    gate_grad,
    own_small,
    d_conv,
    d_gates,
    given,
    taken,
    sums,
    send,
    recv,
):
    total_rows, width = states.shape
    block = weights.shape[2]
    place = HalfBlocks(width, block)
    half = place.half
    barrier = pltpu.get_barrier_semaphore()
    pl.semaphore_signal(barrier, inc=1, device_id=place.pair, device_id_type=MESH)
    backward_scan(
        d_mixed,
        lambda span: window[span, pl.ds(place.own, width)],
        gates,
        branch_y,
        states,
        soft,
        slope_soft,
        since,
        d_conv,
        d_gates,
        d_branch_y,
        sums.at[taps],
    )

    def to_pair(span):
        total = jnp.zeros((PART, half), F32)
        for s in range(2):
            total = total + times_transposed(
                d_gates[span, pl.ds(s * width + place.mine, half)],
                weights[
                    s,
                    place.shared,
                    pl.ds(place.other_in_block, half),
                    pl.ds(place.mine_in_block, half),
                ],
            )
        given[span, :] = total.astype(BF16)

    parts(total_rows, to_pair)
    pl.semaphore_wait(barrier, 1)
    rim = pltpu.make_async_remote_copy(
        src_ref=given,
        dst_ref=taken,
        send_sem=send.at[0],
        recv_sem=recv.at[0],
        device_id=place.pair,
        device_id_type=MESH,
    )
    rim.start()

    def full(span):
        for index in range(place.count - 1):
            number, at = place.full(index)
            total = d_conv[span, pl.ds(at, block)]
            for s in range(2):
                total = total + times_transposed(
                    d_gates[span, pl.ds(s * width + at, block)], weights[s, number]
                )
            d_conv[span, pl.ds(at, block)] = total
        total = d_conv[span, pl.ds(place.mine, half)]
        for s in range(2):
            total = total + times_transposed(
                d_gates[span, pl.ds(s * width + place.mine, half)],
                weights[
                    s,
                    place.shared,
                    pl.ds(place.mine_in_block, half),
                    pl.ds(place.mine_in_block, half),
                ],
            )
        d_conv[span, pl.ds(place.mine, half)] = total

    parts(total_rows, full)
    units = width // half
    for index in range(units):
        number = (index + place.odd) // 2
        cells = window[:, place.span(number)]
        both = jnp.concatenate(
            [d_gates[:, s * width + index * half : s * width + (index + 1) * half] for s in range(2)],
            axis=1,
        )
        found = lax.dot_general(
            cells, both, (((0,), (0,)), ((), ())), preferred_element_type=F32
        ).astype(BF16)
        gate_grad[2 * index] = found[:, :half]
        gate_grad[2 * index + 1] = found[:, half:]
    rim.wait()

    def add(span):
        d_conv[span, pl.ds(place.mine, half)] += taken[span, :].astype(F32)

    parts(total_rows, add)
    for tap in range(taps):
        sums[tap] = jnp.zeros((8, width), F32)

    def conv(i, after):
        row = pl.multiple_of(total_rows - CHUNK - i * CHUNK, CHUNK)
        kept = []
        for at in range(CHUNK - 8, -1, -8):
            tile = pl.ds(row + at, 8)
            values = d_conv[tile, :]
            line = lax.broadcasted_iota(jnp.int32, values.shape, 0)
            below = branch_x[tile, :]
            higher = pl.multiple_of((row + at - 8 + total_rows) % total_rows, 8)
            above = branch_x[pl.ds(higher, 8), :]
            total = values * tap_rows[0:1, :]
            sums[0] += values * below
            masked = []
            for tap in range(1, taps):
                here = jnp.where(since[tile, :] > tap - 0.5, values, 0.0)
                masked.append(here)
                moved = jnp.where(
                    line < 8 - tap,
                    pltpu.roll(here, 8 - tap, 0),
                    pltpu.roll(after[tap - 1], 8 - tap, 0),
                )
                total = total + moved * tap_rows[tap : tap + 1, :]
                source = jnp.where(
                    line < tap, pltpu.roll(above, tap, 0), pltpu.roll(below, tap, 0)
                )
                sums[tap] += here * source
            after = tuple(masked)
            kept.append(total)
        d_branch_x[pl.ds(row, CHUNK), :] = jnp.concatenate(kept[::-1], axis=0).astype(BF16)
        return after

    none = jnp.zeros((8, width), F32)
    lax.fori_loop(0, total_rows // CHUNK, conv, (none,) * (taps - 1))
    line = lax.broadcasted_iota(jnp.int32, (8, width), 0)
    total = jnp.zeros((8, width), F32)
    for tap in range(taps + 1):
        row = jnp.sum(sums[tap], axis=0, keepdims=True)
        total = jnp.where(line == tap, row, total)
    own_small[...] = total


def gate_layout_kernel(parts_in, whole):
    for piece in range(parts_in.shape[1]):
        for s in range(2):
            whole[s, 0, :, piece * 128 : (piece + 1) * 128] = parts_in[0, piece, s].astype(F32)


def gate_layout(parts_in):
    blocks, pieces, _, block, unit = parts_in.shape
    if unit != 128:
        whole = parts_in.transpose(2, 0, 3, 1, 4).reshape(2, blocks, block, block)
        return whole.astype(F32)
    return pl.pallas_call(
        gate_layout_kernel,
        grid=(blocks,),
        out_shape=jax.ShapeDtypeStruct((2, blocks, block, block), F32),
        in_specs=[pl.BlockSpec((1, pieces, 2, block, unit), lambda n: (n, 0, 0, 0, 0))],
        out_specs=pl.BlockSpec((2, 1, block, block), lambda n: (0, n, 0, 0)),
    )(parts_in)


def scan_call(kernel, outs, *operands):
    return pl.pallas_call(
        kernel,
        out_shape=outs,
        in_specs=in_vmem(len(operands)),
        out_specs=tuple(in_vmem(len(outs))),
        compiler_params=pltpu.CompilerParams(vmem_limit_bytes=VMEM_BYTES),
    )(*operands)


class Rim:
    def __init__(self, route, back, source, first, width, room):
        self.route, self.back = route, back
        self.source, self.first, self.width = source, first, width
        self.room = room

    def fetch(self, values):
        part = lax.dynamic_slice_in_dim(values, self.source, self.width, 1)
        return lax.ppermute(part, "tensor", self.route)

    def give(self, part):
        return lax.ppermute(part, "tensor", self.back)

    def add(self, values, part):
        zeros = jnp.zeros(values.shape, F32)
        return values + lax.dynamic_update_slice_in_dim(
            zeros, part.astype(F32), self.source, 1
        )

    def window(self, channels):
        return (channels // self.width + 4) * self.width


def gate_rims(channels, block_size, ntensor, offset):
    up = [(i, i + 1) for i in range(ntensor - 1)]
    down = [(i + 1, i) for i in range(ntensor - 1)]
    last = jnp.int32(channels - block_size)
    return [
        Rim(up, down, last, offset - block_size, block_size, block_size),
        Rim(down, up, jnp.int32(0), offset + channels, block_size, block_size),
    ]


def same_block(first, count, offset, channels, block_size):
    rows = (first + jnp.arange(count, dtype=jnp.int32))[:, None]
    columns = (offset + jnp.arange(channels, dtype=jnp.int32))[None, :]
    return (rows + block_size) // block_size == (columns + block_size) // block_size


def gate_dense(gate_w, offset, first, count):
    block_size = gate_w.shape[2]
    total = gate_w.shape[1] * block_size
    channels = total // lax.axis_size("tensor")
    columns = gate_w.transpose(2, 0, 1, 3).reshape(block_size, 2, total)
    columns = lax.dynamic_slice_in_dim(columns, offset, channels, 2)
    copies = -(-count // block_size) + 1
    tall = jnp.concatenate([columns] * copies, axis=0)
    tall = lax.dynamic_slice_in_dim(tall, (first + block_size) % block_size, count, 0)
    same = same_block(first, count, offset, channels, block_size)
    dense = jnp.where(same[:, None, :], tall, jnp.zeros_like(tall))
    return dense.reshape(count, 2 * channels)


def doc_starts(seg_ids, seq_len):
    places = jnp.arange(seg_ids.shape[0], dtype=jnp.int32)
    before = jnp.concatenate([seg_ids[:1], seg_ids[:-1]])
    resets = (places % seq_len == 0) | (seg_ids != before)
    starts = lax.cummax(jnp.where(resets, places, jnp.zeros_like(places)), axis=0)
    return starts


def causal_conv(starts, values, kernel):
    places = jnp.arange(values.shape[0], dtype=jnp.int32)
    total = values * kernel[0]
    for offset_k in range(1, kernel.shape[0]):
        moved = jnp.concatenate(
            [jnp.zeros((offset_k, values.shape[1]), values.dtype), values[:-offset_k]], axis=0
        )
        valid = (places - offset_k >= starts)[:, None]
        total = total + jnp.where(valid, moved, jnp.zeros_like(moved)) * kernel[offset_k]
    return total


def geglu(gate_val, up_val):
    return jax.nn.gelu(gate_val, approximate=True) * up_val


def rows_times(left, right):
    return lax.dot_general(left, right, (((1,), (1,)), ((), ())), preferred_element_type=F32)


def rows_back(lefts, rights):
    total = rows_times(lefts[0], rights[0])
    return total + rows_times(lefts[1], rights[1])


def inner_rows(left, right):
    return lax.dot_general(left, right, (((0,), (0,)), ((), ())), preferred_element_type=F32)


def body(
    tokens,
    segments,
    cotangent,
    norm_gain,
    w_y,
    w_x,
    conv_w,
    gate_w,
    decay_param,
    w_out,
    mlp_gain,
    w_gate,
    w_up,
    w_down,
):
    ntensor = lax.axis_size("tensor")
    ndp = lax.axis_size("dp")
    nbits = log2_of(ntensor)
    tindex = lax.axis_index("tensor")
    own_rows, width = tokens.shape
    group_rows = own_rows * ntensor
    block_size = gate_w.shape[2]
    nblocks = gate_w.shape[1]
    dp_rows, channels = w_y.shape
    taps = conv_w.shape[0]
    offset = tindex * channels
    shape = jax.ShapeDtypeStruct
    gain_in = norm_gain.reshape(1, width)
    gain_mid = mlp_gain.reshape(1, width)
    seg_rows_of = own_rows // 128
    normed_rows, cot_rows, seg_all, wy_loc, wx_loc, wout_loc = call_kernel(
        partial(enter_kernel, nbits),
        (
            shape((group_rows, width), BF16),
            shape((group_rows, width), BF16),
            shape((ntensor, seg_rows_of, 128), jnp.int32),
        )
        + (shape((dp_rows * ndp, channels), BF16),) * 3,
        gather_sems(nbits)
        + gather_sems(nbits)
        + [pltpu.SemaphoreType.DMA((ntensor - 1,)), pltpu.SemaphoreType.DMA((ntensor - 1,))]
        + [pltpu.SemaphoreType.DMA((2,))]
        + line_sems(ndp) * 3,
        0,
        tokens,
        cotangent,
        segments.reshape(seg_rows_of, 128),
        gain_in,
        w_y,
        w_x,
        w_out,
        far_in=(4, 5, 6),
        far_out=(3, 4, 5),
    )
    w_gate, w_up, w_down, normed_rows = lax.optimization_barrier(
        (w_gate, w_up, w_down, normed_rows)
    )
    wg_loc = lax.all_gather(w_gate, "dp", axis=0, tiled=True)
    wu_loc = lax.all_gather(w_up, "dp", axis=0, tiled=True)
    wd_loc = lax.all_gather(w_down, "dp", axis=0, tiled=True)
    seg_rows = seg_all.reshape(group_rows)
    starts = doc_starts(seg_rows, group_rows)
    conv_loc = lax.dynamic_slice_in_dim(conv_w, offset, channels, 1)
    decay_loc = lax.dynamic_slice_in_dim(decay_param, offset, channels, 0).reshape(1, channels)
    soft = jax.nn.softplus(decay_loc)
    slope_soft = jax.nn.sigmoid(decay_loc)
    half_blocks = (
        channels % block_size == block_size // 2 and ntensor % 2 == 0 and block_size % 256 == 0
    )
    since = (jnp.arange(group_rows, dtype=jnp.int32) - starts).astype(F32)[:, None]
    branch_x = jnp.dot(normed_rows, wx_loc, preferred_element_type=F32)
    branch_y = jnp.dot(normed_rows, wy_loc, preferred_element_type=F32)
    if half_blocks:
        span_blocks = channels // block_size + 1
        w_window = lax.dynamic_slice_in_dim(gate_w, offset // block_size, span_blocks, 1)
        taps_pad = jnp.concatenate([conv_loc, jnp.zeros((8 - taps, channels), F32)], axis=0)
        mixed_low, states, window, gate_pre = call_kernel(
            partial(recurrence_kernel, taps),
            (
                shape((group_rows, channels), BF16),
                shape((group_rows, channels), F32),
                shape((group_rows, span_blocks * block_size), BF16),
                shape((group_rows, 2 * channels), F32),
            ),
            [pltpu.SemaphoreType.DMA((1,)), pltpu.SemaphoreType.DMA((1,))],
            5,
            branch_x,
            branch_y,
            taps_pad,
            soft,
            since,
            w_window,
        )
    else:
        rims = gate_rims(channels, block_size, ntensor, offset)
        own_dense = gate_dense(gate_w, offset, offset, channels)
        rim_dense = [gate_dense(gate_w, offset, rim.first, rim.width) for rim in rims]
        conv_out, conv_pull = jax.vjp(partial(causal_conv, starts), branch_x, conv_loc)
        conv_low = conv_out.astype(BF16)
        rim_cells = [rim.fetch(conv_low) for rim in rims]
        gate_pre = jnp.dot(conv_low, own_dense, preferred_element_type=F32)
        for cells, dense in zip(rim_cells, rim_dense):
            gate_pre = gate_pre + jnp.dot(cells, dense, preferred_element_type=F32)
        mixed_low, states = scan_call(
            forward_scan_kernel,
            (shape((group_rows, channels), BF16), shape((group_rows, channels), F32)),
            conv_low,
            gate_pre,
            branch_y,
            soft,
            since,
        )
    middle, mid_rows = call_kernel(
        partial(middle_kernel, nbits),
        (shape((own_rows, width), F32), shape((group_rows, width), BF16)),
        scatter_scratch(own_rows, width, nbits) + gather_sems(nbits),
        1,
        rows_times(mixed_low, wout_loc).astype(BF16),
        tokens,
        gain_mid,
    )
    gate_val = jnp.dot(mid_rows, wg_loc, preferred_element_type=F32)
    up_val = jnp.dot(mid_rows, wu_loc, preferred_element_type=F32)
    hidden, act_pull = jax.vjp(geglu, gate_val, up_val)
    hidden_low = hidden.astype(BF16)
    grad_wd = inner_rows(cot_rows, hidden_low).astype(BF16)
    sum_wd = lax.psum_scatter(grad_wd, "dp", scatter_dimension=0, tiled=True)
    grad_wd, wd_loc = lax.optimization_barrier((grad_wd, wd_loc))
    d_hidden = jnp.dot(cot_rows, wd_loc, preferred_element_type=F32)
    d_gate, d_up = act_pull(d_hidden)
    d_gate = d_gate.astype(BF16)
    d_up = d_up.astype(BF16)
    grad_wg = inner_rows(mid_rows, d_gate).astype(BF16)
    sum_wg = lax.psum_scatter(grad_wg, "dp", scatter_dimension=0, tiled=True)
    d_mid_part = rows_back((d_gate, d_up), (wg_loc, wu_loc)).astype(BF16)
    d_mid_part, grad_wg = lax.optimization_barrier((d_mid_part, grad_wg))
    d_middle, d_mixer, d_gain_mid = call_kernel(
        partial(turn_kernel, nbits),
        (
            shape((own_rows, width), F32),
            shape((group_rows, width), BF16),
            shape((8, width), F32),
        ),
        scatter_scratch(own_rows, width, nbits) + gather_sems(nbits),
        2,
        d_mid_part,
        cotangent,
        middle,
        gain_mid,
    )
    d_mixer, sum_wd = lax.optimization_barrier((d_mixer, sum_wd))
    d_mixed_in = jnp.dot(d_mixer, wout_loc, preferred_element_type=F32)
    mid_again, d_mixed_in = lax.optimization_barrier((mid_rows, d_mixed_in))
    grad_wu = inner_rows(mid_again, d_up).astype(BF16)
    sum_wu = lax.psum_scatter(grad_wu, "dp", scatter_dimension=0, tiled=True)
    d_mixed_in, grad_wu = lax.optimization_barrier((d_mixed_in, grad_wu))
    unit = math.gcd(channels, block_size)
    if half_blocks:
        d_branch_y, d_branch_x, gate_grad, own_small = call_kernel(
            partial(recurrence_back_kernel, taps),
            (
                shape((group_rows, channels), BF16),
                shape((group_rows, channels), BF16),
                shape((channels // unit * 2, block_size, unit), BF16),
                shape((8, channels), F32),
            ),
            [
                pltpu.VMEM((group_rows, channels), F32),
                pltpu.VMEM((group_rows, 2 * channels), BF16),
                pltpu.VMEM((group_rows, unit), BF16),
                pltpu.VMEM((group_rows, unit), BF16),
                pltpu.VMEM((taps + 1, 8, channels), F32),
                pltpu.SemaphoreType.DMA((1,)),
                pltpu.SemaphoreType.DMA((1,)),
            ],
            6,
            d_mixed_in,
            window,
            gate_pre,
            branch_y,
            branch_x,
            states,
            taps_pad,
            soft,
            slope_soft,
            since,
            w_window,
        )
        gate_grad, d_branch_y, sum_wg = lax.optimization_barrier((gate_grad, d_branch_y, sum_wg))
        gate_grad = gate_grad.reshape(channels // unit * 2 * block_size, unit)
    else:
        d_conv, d_gate_low, d_branch_y, d_decay = scan_call(
            backward_scan_kernel,
            (
                shape((group_rows, channels), F32),
                shape((group_rows, 2 * channels), BF16),
                shape((group_rows, channels), BF16),
                shape((8, channels), F32),
            ),
            d_mixed_in,
            conv_low,
            gate_pre,
            branch_y,
            states,
            soft,
            slope_soft,
            since,
        )
        given = [rows_times(d_gate_low, dense).astype(BF16) for dense in rim_dense]
        taken = [rim.give(part) for rim, part in zip(rims, given)]
        d_conv_out = d_conv + rows_times(d_gate_low, own_dense)
        for rim, part in zip(rims, taken):
            d_conv_out = rim.add(d_conv_out, part)
        d_branch_x, grad_conv_loc = conv_pull(d_conv_out)
        d_branch_x = d_branch_x.astype(BF16)
        base = offset // block_size * block_size - rims[0].room
        window_rows = rims[0].window(channels)
        picked = jnp.zeros((window_rows, 2 * channels), F32)
        for first, cells in [(offset, conv_low)] + [(r.first, c) for r, c in zip(rims, rim_cells)]:
            part = inner_rows(cells, d_gate_low)
            same = same_block(first, cells.shape[1], offset, channels, block_size)
            part = jnp.where(jnp.concatenate([same, same], axis=1), part, 0.0)
            picked = lax.dynamic_update_slice(picked, part, (first - base, jnp.int32(0)))
        picked = picked.reshape(window_rows // block_size, block_size, 2, channels // unit, unit)
        gate_grad = picked.sum(axis=0).astype(BF16).transpose(2, 1, 0, 3)
        gate_grad = gate_grad.reshape(channels // unit * 2 * block_size, unit)
        own_small = jnp.concatenate(
            [
                grad_conv_loc,
                jnp.sum(d_decay, axis=0, keepdims=True),
                jnp.zeros((7 - taps, channels), F32),
            ],
            axis=0,
        )

    grad_wout = inner_rows(d_mixer, mixed_low).astype(BF16)
    sum_wout = lax.psum_scatter(grad_wout, "dp", scatter_dimension=0, tiled=True)
    grad_wy = inner_rows(normed_rows, d_branch_y).astype(BF16)
    grad_wx = inner_rows(normed_rows, d_branch_x).astype(BF16)
    ffn_part = rows_times(hidden_low, wd_loc).astype(BF16)
    d_normed = rows_back((d_branch_y, d_branch_x), (wy_loc, wx_loc)).astype(BF16)
    merged = nbits <= 2

    def halved(grad):
        return grad.reshape(ndp // 2, 2, grad.shape[0] // ndp, grad.shape[1])

    pieces = [halved(grad) for grad in (gate_grad, grad_wy, grad_wx)]
    peers = ntensor - 1
    gate_rows = gate_grad.shape[0] // ndp
    dma = pltpu.SemaphoreType.DMA
    scratch = scatter_scratch(own_rows, width, nbits)
    for piece in pieces:
        scratch += ring_scratch(ndp, piece.shape[2], piece.shape[3])
    scratch += [
        pltpu.VMEM((8, width), F32),
        pltpu.VMEM((ntensor, 8, channels), F32),
        pltpu.VMEM((peers, 8, channels), F32),
        pltpu.VMEM((8, channels), F32),
        pltpu.VMEM((ndp - 1, 8, channels), F32),
    ]
    scratch += [dma((peers,)), dma((peers,)), dma((ndp - 1,)), dma((ndp - 1,))]
    scratch += [dma((peers,)), dma((peers,)), dma((peers + ndp,)), dma((peers + ndp,))]
    if merged:
        scratch += scatter_scratch(own_rows, width, nbits)
    found = call_kernel(
        partial(leave_kernel, nbits, merged),
        (shape((own_rows, width), F32),)
        + (shape((dp_rows, channels), F32),) * 2
        + (
            shape((ntensor, ndp, gate_rows, unit), BF16),
            shape((ntensor, 8, channels), F32),
        )
        + ((shape((own_rows, width), BF16),) if merged else ()),
        scratch,
        3,
        d_normed,
        tokens,
        d_middle,
        gain_in,
        own_small,
        d_gain_mid,
        *pieces,
        *((ffn_part, middle) if merged else ()),
        far_in=(6, 7, 8),
    )
    grad_input, sum_wy, sum_wx, gate_all, small_all = found[:5]
    if merged:
        mixed = found[5]
    else:
        (mixed,) = call_kernel(
            partial(result_kernel, nbits),
            (shape((own_rows, width), BF16),),
            scatter_scratch(own_rows, width, nbits),
            4,
            ffn_part,
            middle,
        )
    per_block = block_size // unit
    sum_gate = gate_all.reshape(nblocks, per_block, 2, block_size, unit)
    sum_gate = gate_layout(sum_gate)
    summed = small_all.transpose(1, 0, 2).reshape(8, width)
    return (
        mixed,
        grad_input,
        summed[6],
        sum_wy,
        sum_wx,
        summed[:taps],
        sum_gate,
        summed[taps],
        sum_wout.astype(F32),
        summed[7],
        sum_wg.astype(F32),
        sum_wu.astype(F32),
        sum_wd.astype(F32),
    )


def solution(mesh):
    split = P(("dp", "tensor"), None)
    weight = P("dp", "tensor")
    return jax.shard_map(
        body,
        mesh=mesh,
        in_specs=(
            split,
            P(("dp", "tensor")),
            split,
            P(),
            weight,
            weight,
            P(),
            P(),
            P(),
            weight,
            P(),
            weight,
            weight,
            weight,
        ),
        out_specs=(
            split,
            split,
            P(),
            weight,
            weight,
            P(),
            P(),
            P(),
            weight,
            P(),
            weight,
            weight,
            weight,
        ),
        check_vma=False,
    )
```

```python
import math
from functools import partial

import jax
import jax.numpy as jnp
from jax import lax
from jax.experimental import pallas as pl
from jax.experimental.pallas import tpu as pltpu
from jax.sharding import PartitionSpec as P

EPSILON = 1e-06
MESH = pl.DeviceIdType.MESH
VMEM_BYTES = 56 * 1024 * 1024
CHUNK = 16
F32 = jnp.float32
BF16 = jnp.bfloat16


def subsets(bits):
    found = [()]
    for bit in bits:
        found = found + [chosen + (bit,) for chosen in found]
    return found


def flipped(index, bits):
    for bit in bits:
        mine = (index // (1 << bit)) % 2
        index = index + (1 - 2 * mine) * (1 << bit)
    return index


def log2_of(count):
    assert count & (count - 1) == 0
    return count.bit_length() - 1


def greet(axis_bits):
    barrier = pltpu.get_barrier_semaphore()
    for axis, bit in axis_bits:
        peer = flipped(lax.axis_index(axis), (bit,))
        pl.semaphore_signal(barrier, inc=1, device_id={axis: peer}, device_id_type=MESH)
    pl.semaphore_wait(barrier, len(axis_bits))


def halves_of(nbits, columns):
    half = columns // 2
    ups = tuple(range(nbits))
    return ((ups, 0, half), (ups[::-1], half, half))


class Gather:
    def __init__(self, ref, rows, nbits, send_sems, recv_sems):
        self.ref, self.rows, self.nbits = ref, rows, nbits
        self.sems = (send_sems, recv_sems)
        self.me = lax.axis_index("tensor")
        self.plan = []
        number = 0
        for half, (order, at, width) in enumerate(halves_of(nbits, ref.shape[1])):
            for step, bit in enumerate(order):
                for known in subsets(order[:step]):
                    self.plan.append((half, step, known, bit, at, width, number))
                    number += 1
        self.count = number

    def copy(self, item):
        half, step, known, bit, at, width, number = item
        row = pl.multiple_of(flipped(self.me, known) * self.rows, self.rows)
        piece = self.ref.at[pl.ds(row, self.rows), pl.ds(at, width)]
        return pltpu.make_async_remote_copy(
            src_ref=piece,
            dst_ref=piece,
            send_sem=self.sems[0].at[number],
            recv_sem=self.sems[1].at[number],
            device_id={"tensor": flipped(self.me, (bit,))},
            device_id_type=MESH,
        )

    def begin(self):
        for item in sorted(self.plan, key=lambda it: it[1]):
            if item[2] == ():
                self.copy(item).start()

    def advance(self, step):
        for item in self.plan:
            half, at_step, known, bit, at, width, number = item
            if at_step == step:
                self.copy(item).wait_recv()
                block = known + (bit,)
                for later in self.plan:
                    if later[0] == half and set(later[2]) == set(block):
                        self.copy(later).start()

    def finish(self, step=0):
        for at_step in range(step, self.nbits):
            self.advance(at_step)
        for item in self.plan:
            self.copy(item).wait_send()


def gather_copies(nbits):
    return 2 * ((1 << nbits) - 1)


class Scatter:
    def __init__(self, ref, landed, staged, rows, nbits, send_sems, recv_sems):
        self.ref, self.landed, self.staged = ref, landed, staged
        self.rows, self.nbits = rows, nbits
        self.sems = (send_sems, recv_sems)
        self.me = lax.axis_index("tensor")
        self.plan, self.slot = [], {}
        number = 0
        for half, (order, at, width) in enumerate(halves_of(nbits, ref.shape[1])):
            for step, bit in enumerate(order):
                for rest in subsets(order[step + 1 :])[::-1]:
                    self.plan.append((half, step, rest, bit, at, width, number))
                    if step > 0:
                        self.slot[number] = len(self.slot)
                    number += 1

    def copy(self, item):
        half, step, rest, bit, at, width, number = item
        if step == 0:
            row = pl.multiple_of(flipped(self.me, rest + (bit,)) * self.rows, self.rows)
            source = self.ref.at[pl.ds(row, self.rows), pl.ds(at, width)]
        else:
            source = self.staged.at[self.slot[number]]
        return pltpu.make_async_remote_copy(
            src_ref=source,
            dst_ref=self.landed.at[number],
            send_sem=self.sems[0].at[number],
            recv_sem=self.sems[1].at[number],
            device_id={"tensor": flipped(self.me, (bit,))},
            device_id_type=MESH,
        )

    def begin(self):
        for item in sorted(self.plan, key=lambda it: (len(it[2]) == 0)):
            if item[1] == 0:
                self.copy(item).start()

    def partial_sum(self, half, block, before, row, size):
        at, width = halves_of(self.nbits, self.ref.shape[1])[half][1:]
        base = pl.multiple_of(flipped(self.me, block) * self.rows + row, size)
        total = self.ref[pl.ds(base, size), pl.ds(at, width)].astype(F32)
        for it in self.plan:
            if it[0] == half and it[1] < before and set(it[2]) == set(block):
                total = total + self.landed[it[6], pl.ds(row, size), :].astype(F32)
        return total

    def advance(self, step):
        for half in range(2):
            for item in self.plan:
                if item[0] == half and item[1] == step:
                    self.copy(item).wait_recv()
            for item in self.plan:
                if item[0] == half and item[1] == step + 1:

                    def fill(row, item=item):
                        value = self.partial_sum(
                            item[0], item[2] + (item[3],), item[1], row, CHUNK
                        )
                        where = (self.slot[item[6]], pl.ds(row, CHUNK))
                        self.staged[where + (slice(None),)] = value.astype(BF16)

                    chunks(self.rows, fill)
                    self.copy(item).start()

    def run(self):
        for step in range(self.nbits):
            self.advance(step)

    def total(self, row, size):
        return jnp.concatenate(
            [self.partial_sum(half, (), self.nbits, row, size) for half in range(2)], axis=1
        )

    def drain(self):
        for item in self.plan:
            self.copy(item).wait_send()


def scatter_scratch(rows, columns, nbits):
    copies = gather_copies(nbits)
    later = max(1, copies - (1 << nbits))
    return [
        pltpu.VMEM((copies, rows, columns // 2), BF16),
        pltpu.VMEM((later, rows, columns // 2), BF16),
        pltpu.SemaphoreType.DMA((copies,)),
        pltpu.SemaphoreType.DMA((copies,)),
    ]


def gather_sems(nbits):
    copies = gather_copies(nbits)
    return [pltpu.SemaphoreType.DMA((copies,)), pltpu.SemaphoreType.DMA((copies,))]


def tensor_bits(nbits):
    return [("tensor", bit) for bit in range(nbits)]


def rms_scale_of(values):
    return lax.rsqrt(jnp.mean(values * values, axis=-1, keepdims=True) + EPSILON)


def chunks(rows, body):
    def step(i, carry):
        body(pl.multiple_of(i * CHUNK, CHUNK))
        return carry

    lax.fori_loop(0, rows // CHUNK, step, 0)


def own_row(row, rows):
    return pl.multiple_of(lax.axis_index("tensor") * rows + row, CHUNK)


def dp_place():
    me = lax.axis_index("dp")
    return me // 2, me % 2, lax.axis_size("dp") // 2


def dp_index(chip, core):
    return chip * 2 + core


def shift_order(count):
    return sorted(range(1, count), key=lambda shift: min(shift, count - shift))


class LineGather:
    def __init__(self, own, whole, send_sems, recv_sems):
        self.own, self.whole = own, whole
        self.sems = (send_sems, recv_sems)
        self.chip, self.core, self.chips = dp_place()
        self.rows = own.shape[0]

    def block(self, chip, core):
        row = pl.multiple_of(dp_index(chip, core) * self.rows, self.rows)
        return self.whole.at[pl.ds(row, self.rows), :]

    def along(self, shift):
        return pltpu.make_async_remote_copy(
            src_ref=self.own,
            dst_ref=self.block(self.chip, self.core),
            send_sem=self.sems[0].at[shift],
            recv_sem=self.sems[1].at[shift],
            device_id={"dp": dp_index((self.chip + shift) % self.chips, self.core)},
            device_id_type=MESH,
        )

    def across(self, shift):
        block = self.block((self.chip + self.chips - shift) % self.chips, self.core)
        number = self.chips + shift
        return pltpu.make_async_remote_copy(
            src_ref=self.own if shift == 0 else block,
            dst_ref=block,
            send_sem=self.sems[0].at[number],
            recv_sem=self.sems[1].at[number],
            device_id={"dp": dp_index(self.chip, 1 - self.core)},
            device_id_type=MESH,
        )

    def local(self):
        return pltpu.make_async_copy(
            self.own, self.block(self.chip, self.core), self.sems[0].at[2 * self.chips]
        )

    def begin(self):
        for shift in shift_order(self.chips):
            self.along(shift).start()
        self.across(0).start()
        self.local().start()

    def pass_on(self):
        for shift in shift_order(self.chips):
            self.along(shift).wait_recv()
            self.across(shift).start()

    def finish(self):
        for shift in range(self.chips):
            self.across(shift).wait()
        for shift in range(1, self.chips):
            self.along(shift).wait_send()
        self.local().wait()


def line_sems(ndp):
    return [pltpu.SemaphoreType.DMA((ndp + 1,)), pltpu.SemaphoreType.DMA((ndp + 1,))]


def greet_peers(nbits, whole_dp):
    me = lax.axis_index("tensor")
    chip, core, chips = dp_place()
    barrier = pltpu.get_barrier_semaphore()
    met = 0
    for chosen in subsets(tuple(range(nbits))):
        if chosen:
            pl.semaphore_signal(
                barrier, inc=1, device_id={"tensor": flipped(me, chosen)}, device_id_type=MESH
            )
            met += 1
    for shift in range(chips):
        for turn in range(2):
            if (shift, turn) == (0, 0) or (shift and turn and not whole_dp):
                continue
            other = dp_index((chip + shift) % chips, core + turn * (1 - 2 * core))
            pl.semaphore_signal(
                barrier, inc=1, device_id={"dp": other}, device_id_type=MESH
            )
            met += 1
    pl.semaphore_wait(barrier, met)


def enter_kernel(
    nbits,
    tokens,
    cot,
    seg,
    gain,
    w_y,
    w_x,
    w_out,
    normed_all,
    cot_all,
    seg_all,
    wy_all,
    wx_all,
    wout_all,
    s0,
    r0,
    s1,
    r1,
    s2,
    r2,
    l0,
    *line,
):
    rows = tokens.shape[0]
    me = lax.axis_index("tensor")
    peers = [chosen for chosen in subsets(tuple(range(nbits))) if chosen]
    greet_peers(nbits, False)
    lines = [
        LineGather(own, whole, line[2 * number], line[2 * number + 1])
        for number, (own, whole) in enumerate(((w_y, wy_all), (w_x, wx_all), (w_out, wout_all)))
    ]
    for item in lines:
        item.begin()

    def norm(row):
        values = tokens[pl.ds(row, CHUNK), :].astype(F32)
        scaled = values * rms_scale_of(values) * gain[...]
        normed_all[pl.ds(own_row(row, rows), CHUNK), :] = scaled.astype(BF16)

    chunks(rows, norm)
    first = Gather(normed_all, rows, nbits, s0, r0)
    first.begin()
    cot_own = cot_all.at[pl.ds(pl.multiple_of(me * rows, rows), rows), :]
    local = pltpu.make_async_copy(cot, cot_own, l0.at[0])
    local.start()
    seg_own = pltpu.make_async_copy(seg, seg_all.at[me], l0.at[1])
    seg_own.start()
    seg_copies = [
        pltpu.make_async_remote_copy(
            src_ref=seg,
            dst_ref=seg_all.at[me],
            send_sem=s2.at[number],
            recv_sem=r2.at[number],
            device_id={"tensor": flipped(me, chosen)},
            device_id_type=MESH,
        )
        for number, chosen in enumerate(peers)
    ]
    for copy in seg_copies:
        copy.start()
    local.wait()
    second = Gather(cot_all, rows, nbits, s1, r1)
    first.advance(0)
    second.begin()
    first.finish(1)
    lines[0].pass_on()
    lines[1].pass_on()
    second.finish()
    lines[2].pass_on()
    for item in lines:
        item.finish()
    for copy in seg_copies:
        copy.wait()
    seg_own.wait()


def middle_kernel(
    nbits, mixer, tokens, gain, middle, mid_all, landed, staged, s0, r0, s1, r1
):
    rows = tokens.shape[0]
    greet(tensor_bits(nbits))
    scatter = Scatter(mixer, landed, staged, rows, nbits, s0, r0)
    scatter.begin()
    scatter.run()

    def norm(row):
        values = tokens[pl.ds(row, CHUNK), :].astype(F32) + scatter.total(row, CHUNK)
        middle[pl.ds(row, CHUNK), :] = values
        scaled = values * rms_scale_of(values) * gain[...]
        mid_all[pl.ds(own_row(row, rows), CHUNK), :] = scaled.astype(BF16)

    chunks(rows, norm)
    gather = Gather(mid_all, rows, nbits, s1, r1)
    gather.begin()
    gather.finish()
    scatter.drain()


def result_kernel(nbits, ffn, middle, mixed, landed, staged, s0, r0):
    rows = middle.shape[0]
    greet(tensor_bits(nbits))
    scatter = Scatter(ffn, landed, staged, rows, nbits, s0, r0)
    scatter.begin()
    scatter.run()

    def add(row):
        values = middle[pl.ds(row, CHUNK), :] + scatter.total(row, CHUNK)
        mixed[pl.ds(row, CHUNK), :] = values.astype(BF16)

    chunks(rows, add)
    scatter.drain()


def norm_pull(values, gain, cotangent):
    scale = rms_scale_of(values)
    unit = values * scale
    inner = cotangent * gain
    back = scale * (inner - unit * jnp.mean(inner * unit, axis=-1, keepdims=True))
    return back, cotangent * unit


def eight_rows(values):
    total = values[0:8]
    for at in range(8, CHUNK, 8):
        total = total + values[at : at + 8]
    return total


def turn_kernel(
    nbits, d_norm, cot, middle, gain, d_middle, d_mixer, d_gain, landed, staged, s0, r0, s1, r1
):
    rows = middle.shape[0]
    greet(tensor_bits(nbits))
    scatter = Scatter(d_norm, landed, staged, rows, nbits, s0, r0)
    scatter.begin()
    d_gain[...] = jnp.zeros_like(d_gain)
    scatter.run()

    def pull(row):
        span = pl.ds(row, CHUNK)
        back, gains = norm_pull(middle[span, :], gain[...], scatter.total(row, CHUNK))
        values = cot[span, :].astype(F32) + back
        d_middle[span, :] = values
        d_mixer[pl.ds(own_row(row, rows), CHUNK), :] = values.astype(BF16)
        d_gain[...] += eight_rows(gains)

    chunks(rows, pull)
    gather = Gather(d_mixer, rows, nbits, s1, r1)
    gather.begin()
    gather.finish()
    scatter.drain()


class LineRing:
    def __init__(self, whole, kept, swapped, staged, landed, send_sems, recv_sems):
        self.whole, self.kept, self.swapped = whole, kept, swapped
        self.staged, self.landed = staged, landed
        self.sems = (send_sems, recv_sems)
        self.chip, self.core, self.chips = dp_place()
        self.rows = whole.shape[2]

    def local(self):
        return pltpu.make_async_copy(
            self.whole.at[:, self.core], self.kept, self.sems[0].at[self.chips]
        )

    def swap(self):
        return pltpu.make_async_remote_copy(
            src_ref=self.whole.at[:, 1 - self.core],
            dst_ref=self.swapped,
            send_sem=self.sems[0].at[0],
            recv_sem=self.sems[1].at[0],
            device_id={"dp": dp_index(self.chip, 1 - self.core)},
            device_id_type=MESH,
        )

    def hop(self, step):
        return pltpu.make_async_remote_copy(
            src_ref=self.staged.at[step - 1],
            dst_ref=self.landed.at[step - 1],
            send_sem=self.sems[0].at[step],
            recv_sem=self.sems[1].at[step],
            device_id={"dp": dp_index((self.chip + 1) % self.chips, self.core)},
            device_id_type=MESH,
        )

    def begin(self):
        self.local().start()
        self.swap().start()

    def value(self, step, span):
        chip = (self.chip + self.chips - step) % self.chips
        total = self.kept[chip, span, :].astype(F32) + self.swapped[chip, span, :].astype(F32)
        if step != 1:
            before = (step if step else self.chips) - 2
            total = total + self.landed[before, span, :].astype(F32)
        return total

    def advance(self, step):
        if step == 1:
            self.local().wait()
            self.swap().wait_recv()
        else:
            self.hop(step - 1).wait_recv()

        def fill(row):
            span = pl.ds(row, CHUNK)
            self.staged[step - 1, span, :] = self.value(step, span).astype(BF16)

        chunks(self.rows, fill)
        self.hop(step).start()

    def finish(self, store):
        self.hop(self.chips - 1).wait_recv()

        def fill(row):
            span = pl.ds(row, CHUNK)
            store(span, self.value(0, span))

        chunks(self.rows, fill)

    def drain(self):
        self.swap().wait_send()
        for step in range(1, self.chips):
            self.hop(step).wait_send()


def ring_scratch(ndp, rows, columns):
    chips = ndp // 2
    return [
        pltpu.VMEM((chips, rows, columns), BF16),
        pltpu.VMEM((chips, rows, columns), BF16),
        pltpu.VMEM((chips - 1, rows, columns), BF16),
        pltpu.VMEM((chips - 1, rows, columns), BF16),
        pltpu.SemaphoreType.DMA((chips + 1,)),
        pltpu.SemaphoreType.DMA((chips + 1,)),
    ]


RING = 6


def leave_kernel(nbits, with_ffn, *refs):
    refs = list(refs)

    def take(count):
        taken = refs[:count]
        del refs[:count]
        return taken

    d_norm, tokens, d_middle, gain, own_small, d_gain_mid = take(6)
    pieces = take(3)
    ffn, middle = take(2) if with_ffn else (None, None)
    grad_input, sum_y, sum_x, gate_all, small_all = take(5)
    mixed = take(1)[0] if with_ffn else None
    landed, staged, s0, r0 = take(4)
    rings = [LineRing(piece, *take(RING)) for piece in pieces]
    d_gain, gains, gains_landed, small, small_landed = take(5)
    gain_s, gain_r, vec_s, vec_r, join_s, join_r, gate_s, gate_r = take(8)
    rows = tokens.shape[0]
    me = lax.axis_index("tensor")
    chip, core, chips = dp_place()
    place = dp_index(chip, core)
    peers = [chosen for chosen in subsets(tuple(range(nbits))) if chosen]
    others = [(shift, turn) for shift in range(chips) for turn in range(2)][1:]
    greet_peers(nbits, True)
    for ring in rings:
        ring.begin()
    scatter = Scatter(d_norm, landed, staged, rows, nbits, s0, r0)
    scatter.begin()
    if with_ffn:
        second = Scatter(ffn, *take(2), rows, nbits, *take(2))
    d_gain[...] = jnp.zeros_like(d_gain)
    for ring in rings:
        ring.advance(1)
    if chips > 2:
        rings[0].advance(2)
    scatter.advance(0)
    if with_ffn:
        second.begin()
    if chips > 2:
        for ring in rings[1:]:
            ring.advance(2)
    for step in range(3, chips):
        rings[0].advance(step)
    for step in range(1, nbits):
        scatter.advance(step)

    def pull(row):
        span = pl.ds(row, CHUNK)
        back, parts = norm_pull(
            tokens[span, :].astype(F32), gain[...], scatter.total(row, CHUNK)
        )
        grad_input[span, :] = d_middle[span, :] + back
        d_gain[...] += eight_rows(parts)

    chunks(rows, pull)
    share = gains.shape[2]
    top = jnp.sum(d_gain[...], axis=0, keepdims=True)
    low = jnp.sum(d_gain_mid[...], axis=0, keepdims=True)
    place8 = lax.broadcasted_iota(jnp.int32, (8, share), 0)
    for index in range(1 << nbits):
        span = slice(index * share, (index + 1) * share)
        gains[index] = jnp.where(
            place8 == 6, top[:, span], jnp.where(place8 == 7, low[:, span], 0.0)
        )

    def gain_copy(number, chosen):
        peer = flipped(me, chosen)
        return pltpu.make_async_remote_copy(
            src_ref=gains.at[peer],
            dst_ref=gains_landed.at[number],
            send_sem=gain_s.at[number],
            recv_sem=gain_r.at[number],
            device_id={"tensor": peer},
            device_id_type=MESH,
        )

    for number, chosen in enumerate(peers):
        gain_copy(number, chosen).start()
    for step in range(3, chips):
        for ring in rings[1:]:
            ring.advance(step)
    total = own_small[...] + gains[me]
    for number, chosen in enumerate(peers):
        gain_copy(number, chosen).wait_recv()
        total = total + gains_landed[number]
    small[...] = total

    def vec_copy(number, shift, turn):
        other = dp_index((chip + shift) % chips, core + turn * (1 - 2 * core))
        return pltpu.make_async_remote_copy(
            src_ref=small,
            dst_ref=small_landed.at[number],
            send_sem=vec_s.at[number],
            recv_sem=vec_r.at[number],
            device_id={"dp": other},
            device_id_type=MESH,
        )

    for number, (shift, turn) in enumerate(others):
        vec_copy(number, shift, turn).start()

    def store_gate(span, value):
        gate_all[me, place, span, :] = value.astype(BF16)

    rings[0].finish(store_gate)

    def gate_copy(number, chip_from, ref, target):
        return pltpu.make_async_remote_copy(
            src_ref=ref,
            dst_ref=ref,
            send_sem=gate_s.at[number],
            recv_sem=gate_r.at[number],
            device_id=target,
            device_id_type=MESH,
        )

    def gate_tensor(number, chosen):
        ref = gate_all.at[me, place]
        return gate_copy(number, chip, ref, {"tensor": flipped(me, chosen)})

    def gate_line(shift):
        target = {"dp": dp_index((chip + shift) % chips, core)}
        return gate_copy(len(peers) + shift - 1, chip, gate_all.at[:, place], target)

    def gate_core(shift):
        ref = gate_all.at[:, dp_index((chip + chips - shift) % chips, core)]
        target = {"dp": dp_index(chip, 1 - core)}
        return gate_copy(len(peers) + chips - 1 + shift, chip, ref, target)

    for number, chosen in enumerate(peers):
        gate_tensor(number, chosen).start()
    if with_ffn:
        second.advance(0)
    total = small[...]
    for number, (shift, turn) in enumerate(others):
        vec_copy(number, shift, turn).wait_recv()
        total = total + small_landed[number]
    small_all[me] = total

    def join_copy(number, chosen):
        return pltpu.make_async_remote_copy(
            src_ref=small_all.at[me],
            dst_ref=small_all.at[me],
            send_sem=join_s.at[number],
            recv_sem=join_r.at[number],
            device_id={"tensor": flipped(me, chosen)},
            device_id_type=MESH,
        )

    for number, chosen in enumerate(peers):
        join_copy(number, chosen).start()
    for number, chosen in enumerate(peers):
        gate_tensor(number, chosen).wait_recv()
    for shift in range(1, chips):
        gate_line(shift).start()
    gate_core(0).start()
    if with_ffn:
        for step in range(1, nbits):
            second.advance(step)

        def add(row):
            span = pl.ds(row, CHUNK)
            mixed[span, :] = (middle[span, :] + second.total(row, CHUNK)).astype(BF16)

        chunks(rows, add)
    for shift in shift_order(chips):
        gate_line(shift).wait_recv()
        gate_core(shift).start()

    def store_in(ref):
        def store(span, value):
            ref[span, :] = value

        return store

    for ring, ref in zip(rings[1:], (sum_y, sum_x)):
        ring.finish(store_in(ref))
    for shift in range(chips):
        gate_core(shift).wait()
    for shift in range(1, chips):
        gate_line(shift).wait_send()
    for number, chosen in enumerate(peers):
        gate_tensor(number, chosen).wait_send()
        gain_copy(number, chosen).wait_send()
        join_copy(number, chosen).wait()
    for number, (shift, turn) in enumerate(others):
        vec_copy(number, shift, turn).wait_send()
    scatter.drain()
    if with_ffn:
        second.drain()
    for ring in rings:
        ring.drain()


def in_vmem(count):
    return [pl.BlockSpec(memory_space=pltpu.VMEM)] * count


def call_kernel(kernel, outs, scratch, number, *operands, far_in=(), far_out=(), cost_us=1):
    vmem = pl.BlockSpec(memory_space=pltpu.VMEM)
    far = pl.BlockSpec(memory_space=pl.ANY)
    return pl.pallas_call(
        kernel,
        out_shape=outs,
        in_specs=[far if i in far_in else vmem for i in range(len(operands))],
        out_specs=tuple(far if i in far_out else vmem for i in range(len(outs))),
        scratch_shapes=scratch,
        cost_estimate=pl.CostEstimate(
            flops=0, bytes_accessed=cost_us * 1_000_000, transcendentals=0
        ),
        compiler_params=pltpu.CompilerParams(
            collective_id=number, has_side_effects=True, vmem_limit_bytes=VMEM_BYTES
        ),
    )(*operands)


def sigmoid(values):
    return 1.0 / (1.0 + jnp.exp(-values))


def one_minus_exp(values):
    series = values / 7.0 + 1.0
    for order in (6.0, 5.0, 4.0, 3.0, 2.0):
        series = 1.0 + series * values / order
    return jnp.where(values > -0.3, -values * series, 1.0 - jnp.exp(values))


GELU_K = 0.7978845608028654
GELU_C = 0.044715


def gelu_parts(values):
    square = values * values
    bent = jnp.tanh(GELU_K * values * (1.0 + GELU_C * square))
    gelu = 0.5 * values * (1.0 + bent)
    slope = 0.5 * (1.0 + bent) + 0.5 * values * (1.0 - bent * bent) * GELU_K * (
        1.0 + 3.0 * GELU_C * square
    )
    return gelu, slope


def gate_terms(gate_a, gate_x, soft, since):
    sig_a = sigmoid(gate_a)
    sig_x = sigmoid(gate_x)
    log_decay = -8.0 * sig_a * soft
    decay = jnp.exp(log_decay)
    scale = jnp.sqrt(one_minus_exp(2.0 * log_decay))
    keep = since > 0.5
    return sig_a, sig_x, decay, jnp.where(keep, scale, 1.0), keep


def scan_down(decay, value, carry):
    place = lax.broadcasted_iota(jnp.int32, decay.shape, 0)
    for shift in (1, 2, 4):
        past = place >= shift
        moved = pltpu.roll(value, shift, 0)
        value = jnp.where(past, decay * moved + value, value)
        decay = jnp.where(past, decay * pltpu.roll(decay, shift, 0), decay)
    return decay * carry + value


def scan_up(decay, value, carry):
    place = lax.broadcasted_iota(jnp.int32, decay.shape, 0)
    factor = jnp.where(place < 7, pltpu.roll(decay, 7, 0), 1.0)
    for shift in (1, 2, 4):
        past = place < 8 - shift
        moved = pltpu.roll(value, 8 - shift, 0)
        value = jnp.where(past, factor * moved + value, value)
        factor = jnp.where(past, factor * pltpu.roll(factor, 8 - shift, 0), factor)
    return factor * carry + value


def forward_scan(conv_rows, gates, branch_y, soft, since, mixed, states):
    total_rows, width = states.shape

    def step(i, carry):
        row = pl.multiple_of(i * CHUNK, CHUNK)
        span = pl.ds(row, CHUNK)
        values = conv_rows(span).astype(F32)
        kept = []
        for at in range(0, CHUNK, 8):
            tile = pl.ds(row + at, 8)
            sig_a, sig_x, decay, scale, keep = gate_terms(
                gates[tile, :width], gates[tile, width:], soft[...], since[tile, :]
            )
            given = values[at : at + 8] * sig_x * scale
            state = scan_down(jnp.where(keep, decay, 0.0), given, carry)
            carry = state[7:8]
            states[tile, :] = state
            kept.append(state * gelu_parts(branch_y[tile, :])[0])
        mixed[span, :] = jnp.concatenate(kept, axis=0).astype(BF16)
        return carry

    lax.fori_loop(0, total_rows // CHUNK, step, jnp.zeros((1, width), F32))


def forward_scan_kernel(conv, gates, branch_y, soft, since, mixed, states):
    forward_scan(lambda span: conv[span, :], gates, branch_y, soft, since, mixed, states)


def backward_scan(
    d_mixed, conv_rows, gates, branch_y, states, soft, slope_soft, since, d_conv, d_gates, d_branch, d_decay
):
    total_rows, width = states.shape
    d_decay[...] = jnp.zeros_like(d_decay)

    def step(i, carry):
        row = pl.multiple_of(total_rows - CHUNK - i * CHUNK, CHUNK)
        span = pl.ds(row, CHUNK)
        values = conv_rows(span).astype(F32)
        kept = []
        for at in range(CHUNK - 8, -1, -8):
            tile = pl.ds(row + at, 8)
            soft_row = soft[...]
            sig_a, sig_x, decay, scale, keep = gate_terms(
                gates[tile, :width], gates[tile, width:], soft_row, since[tile, :]
            )
            value = values[at : at + 8]
            gelu, slope = gelu_parts(branch_y[tile, :])
            state = states[tile, :]
            upper = d_mixed[tile, :]
            held = jnp.where(keep, decay, 0.0)
            lam = scan_up(held, upper * gelu, carry)
            carry = held[0:1] * lam[0:1]
            d_conv[tile, :] = lam * sig_x * scale
            d_x = lam * value * scale * sig_x * (1.0 - sig_x)
            given = value * sig_x
            d_log = lam * (state - given * scale - given * decay * decay / scale)
            d_log = jnp.where(keep, d_log, 0.0)
            d_a = d_log * (-8.0 * soft_row) * sig_a * (1.0 - sig_a)
            d_decay[...] += d_log * (-8.0 * sig_a) * slope_soft[...]
            kept.append((d_a, d_x, upper * state * slope))
        kept = kept[::-1]
        d_gates[span, :width] = jnp.concatenate([k[0] for k in kept], axis=0).astype(BF16)
        d_gates[span, width:] = jnp.concatenate([k[1] for k in kept], axis=0).astype(BF16)
        d_branch[span, :] = jnp.concatenate([k[2] for k in kept], axis=0).astype(BF16)
        return carry

    lax.fori_loop(0, total_rows // CHUNK, step, jnp.zeros((1, width), F32))


def backward_scan_kernel(
    d_mixed, conv, gates, branch_y, states, soft, slope_soft, since, d_conv, d_gates, d_branch, d_decay
):
    backward_scan(
        d_mixed,
        lambda span: conv[span, :],
        gates,
        branch_y,
        states,
        soft,
        slope_soft,
        since,
        d_conv,
        d_gates,
        d_branch,
        d_decay,
    )


def times_transposed(left, right):
    return lax.dot_general(left, right, (((1,), (1,)), ((), ())), preferred_element_type=F32)


class HalfBlocks:
    def __init__(self, channels, block):
        self.odd = lax.axis_index("tensor") % 2
        self.half = block // 2
        self.block = block
        self.count = channels // block + 1
        self.channels = channels
        self.own = pl.multiple_of(self.odd * self.half, self.half)
        self.shared = (1 - self.odd) * (self.count - 1)
        self.mine_in_block = pl.multiple_of(self.odd * self.half, self.half)
        self.other_in_block = pl.multiple_of((1 - self.odd) * self.half, self.half)
        self.mine = pl.multiple_of((1 - self.odd) * (channels - self.half), self.half)
        self.pair = {"tensor": lax.axis_index("tensor") + 1 - 2 * self.odd}

    def full(self, index):
        block = index + self.odd
        return block, pl.multiple_of(index * self.block + self.odd * self.half, self.half)

    def span(self, block):
        return pl.ds(pl.multiple_of(block * self.block, self.block), self.block)

    def shared_part(self, start):
        return pl.ds(pl.multiple_of(self.shared * self.block + start, self.half), self.half)


PART = 256


def parts(rows, body):
    def step(i, carry):
        body(pl.ds(pl.multiple_of(i * PART, PART), PART))
        return carry

    lax.fori_loop(0, rows // PART, step, 0)


def recurrence_kernel(
    taps, branch_x, branch_y, tap_rows, soft, since, weights, mixed, states, window, gates, send, recv
):
    total_rows, width = states.shape
    block = weights.shape[2]
    place = HalfBlocks(width, block)
    barrier = pltpu.get_barrier_semaphore()
    pl.semaphore_signal(barrier, inc=1, device_id=place.pair, device_id_type=MESH)

    def conv(i, before):
        row = pl.multiple_of(i * CHUNK, CHUNK)
        kept = []
        for at in range(0, CHUNK, 8):
            tile = pl.ds(row + at, 8)
            values = branch_x[tile, :]
            line = lax.broadcasted_iota(jnp.int32, values.shape, 0)
            total = values * tap_rows[0:1, :]
            for tap in range(1, taps):
                moved = jnp.where(
                    line < tap, pltpu.roll(before, tap, 0), pltpu.roll(values, tap, 0)
                )
                moved = jnp.where(since[tile, :] > tap - 0.5, moved, 0.0)
                total = total + moved * tap_rows[tap : tap + 1, :]
            kept.append(total)
            before = values
        window[pl.ds(row, CHUNK), pl.ds(place.own, width)] = jnp.concatenate(
            kept, axis=0
        ).astype(BF16)
        return before

    lax.fori_loop(0, total_rows // CHUNK, conv, jnp.zeros((8, width), F32))
    pl.semaphore_wait(barrier, 1)
    source = window.at[:, place.shared_part(place.mine_in_block)]
    away = pl.multiple_of(place.odd * (place.count - 1) * block + place.mine_in_block, place.half)
    rim = pltpu.make_async_remote_copy(
        src_ref=source,
        dst_ref=window.at[:, pl.ds(away, place.half)],
        send_sem=send.at[0],
        recv_sem=recv.at[0],
        device_id=place.pair,
        device_id_type=MESH,
    )
    rim.start()

    def full(span):
        for index in range(place.count - 1):
            number, at = place.full(index)
            cells = window[span, place.span(number)]
            for s in range(2):
                gates[span, pl.ds(s * width + at, block)] = jnp.dot(
                    cells, weights[s, number], preferred_element_type=F32
                )

    parts(total_rows, full)
    rim.wait()

    def shared(span):
        cells = window[span, place.span(place.shared)]
        for s in range(2):
            gates[span, pl.ds(s * width + place.mine, place.half)] = jnp.dot(
                cells,
                weights[s, place.shared, :, pl.ds(place.mine_in_block, place.half)],
                preferred_element_type=F32,
            )

    parts(total_rows, shared)
    forward_scan(
        lambda span: window[span, pl.ds(place.own, width)],
        gates,
        branch_y,
        soft,
        since,
        mixed,
        states,
    )


def recurrence_back_kernel(
    taps,
    d_mixed,
    window,
    gates,
    branch_y,
    branch_x,
    states,
    tap_rows,
    soft,
    slope_soft,
    since,
    weights,
    d_branch_y,
    d_branch_x,
    gate_grad,
    own_small,
    d_conv,
    d_gates,
    given,
    taken,
    sums,
    send,
    recv,
):
    total_rows, width = states.shape
    block = weights.shape[2]
    place = HalfBlocks(width, block)
    half = place.half
    barrier = pltpu.get_barrier_semaphore()
    pl.semaphore_signal(barrier, inc=1, device_id=place.pair, device_id_type=MESH)
    backward_scan(
        d_mixed,
        lambda span: window[span, pl.ds(place.own, width)],
        gates,
        branch_y,
        states,
        soft,
        slope_soft,
        since,
        d_conv,
        d_gates,
        d_branch_y,
        sums.at[taps],
    )

    def to_pair(span):
        total = jnp.zeros((PART, half), F32)
        for s in range(2):
            total = total + times_transposed(
                d_gates[span, pl.ds(s * width + place.mine, half)],
                weights[
                    s,
                    place.shared,
                    pl.ds(place.other_in_block, half),
                    pl.ds(place.mine_in_block, half),
                ],
            )
        given[span, :] = total.astype(BF16)

    parts(total_rows, to_pair)
    pl.semaphore_wait(barrier, 1)
    rim = pltpu.make_async_remote_copy(
        src_ref=given,
        dst_ref=taken,
        send_sem=send.at[0],
        recv_sem=recv.at[0],
        device_id=place.pair,
        device_id_type=MESH,
    )
    rim.start()

    def full(span):
        for index in range(place.count - 1):
            number, at = place.full(index)
            total = d_conv[span, pl.ds(at, block)]
            for s in range(2):
                total = total + times_transposed(
                    d_gates[span, pl.ds(s * width + at, block)], weights[s, number]
                )
            d_conv[span, pl.ds(at, block)] = total
        total = d_conv[span, pl.ds(place.mine, half)]
        for s in range(2):
            total = total + times_transposed(
                d_gates[span, pl.ds(s * width + place.mine, half)],
                weights[
                    s,
                    place.shared,
                    pl.ds(place.mine_in_block, half),
                    pl.ds(place.mine_in_block, half),
                ],
            )
        d_conv[span, pl.ds(place.mine, half)] = total

    parts(total_rows, full)
    units = width // half
    for index in range(units):
        number = (index + place.odd) // 2
        cells = window[:, place.span(number)]
        both = jnp.concatenate(
            [d_gates[:, s * width + index * half : s * width + (index + 1) * half] for s in range(2)],
            axis=1,
        )
        found = lax.dot_general(
            cells, both, (((0,), (0,)), ((), ())), preferred_element_type=F32
        ).astype(BF16)
        gate_grad[2 * index] = found[:, :half]
        gate_grad[2 * index + 1] = found[:, half:]
    rim.wait()

    def add(span):
        d_conv[span, pl.ds(place.mine, half)] += taken[span, :].astype(F32)

    parts(total_rows, add)
    for tap in range(taps):
        sums[tap] = jnp.zeros((8, width), F32)

    def conv(i, after):
        row = pl.multiple_of(total_rows - CHUNK - i * CHUNK, CHUNK)
        kept = []
        for at in range(CHUNK - 8, -1, -8):
            tile = pl.ds(row + at, 8)
            values = d_conv[tile, :]
            line = lax.broadcasted_iota(jnp.int32, values.shape, 0)
            below = branch_x[tile, :]
            higher = pl.multiple_of((row + at - 8 + total_rows) % total_rows, 8)
            above = branch_x[pl.ds(higher, 8), :]
            total = values * tap_rows[0:1, :]
            sums[0] += values * below
            masked = []
            for tap in range(1, taps):
                here = jnp.where(since[tile, :] > tap - 0.5, values, 0.0)
                masked.append(here)
                moved = jnp.where(
                    line < 8 - tap,
                    pltpu.roll(here, 8 - tap, 0),
                    pltpu.roll(after[tap - 1], 8 - tap, 0),
                )
                total = total + moved * tap_rows[tap : tap + 1, :]
                source = jnp.where(
                    line < tap, pltpu.roll(above, tap, 0), pltpu.roll(below, tap, 0)
                )
                sums[tap] += here * source
            after = tuple(masked)
            kept.append(total)
        d_branch_x[pl.ds(row, CHUNK), :] = jnp.concatenate(kept[::-1], axis=0).astype(BF16)
        return after

    none = jnp.zeros((8, width), F32)
    lax.fori_loop(0, total_rows // CHUNK, conv, (none,) * (taps - 1))
    line = lax.broadcasted_iota(jnp.int32, (8, width), 0)
    total = jnp.zeros((8, width), F32)
    for tap in range(taps + 1):
        row = jnp.sum(sums[tap], axis=0, keepdims=True)
        total = jnp.where(line == tap, row, total)
    own_small[...] = total


def gate_layout_kernel(parts_in, whole):
    for piece in range(parts_in.shape[1]):
        for s in range(2):
            whole[s, 0, :, piece * 128 : (piece + 1) * 128] = parts_in[0, piece, s].astype(F32)


def gate_layout(parts_in):
    blocks, pieces, _, block, unit = parts_in.shape
    if unit != 128:
        whole = parts_in.transpose(2, 0, 3, 1, 4).reshape(2, blocks, block, block)
        return whole.astype(F32)
    return pl.pallas_call(
        gate_layout_kernel,
        grid=(blocks,),
        out_shape=jax.ShapeDtypeStruct((2, blocks, block, block), F32),
        in_specs=[pl.BlockSpec((1, pieces, 2, block, unit), lambda n: (n, 0, 0, 0, 0))],
        out_specs=pl.BlockSpec((2, 1, block, block), lambda n: (0, n, 0, 0)),
    )(parts_in)


def scan_call(kernel, outs, *operands):
    return pl.pallas_call(
        kernel,
        out_shape=outs,
        in_specs=in_vmem(len(operands)),
        out_specs=tuple(in_vmem(len(outs))),
        compiler_params=pltpu.CompilerParams(vmem_limit_bytes=VMEM_BYTES),
    )(*operands)


class Rim:
    def __init__(self, route, back, source, first, width, room):
        self.route, self.back = route, back
        self.source, self.first, self.width = source, first, width
        self.room = room

    def fetch(self, values):
        part = lax.dynamic_slice_in_dim(values, self.source, self.width, 1)
        return lax.ppermute(part, "tensor", self.route)

    def give(self, part):
        return lax.ppermute(part, "tensor", self.back)

    def add(self, values, part):
        zeros = jnp.zeros(values.shape, F32)
        return values + lax.dynamic_update_slice_in_dim(
            zeros, part.astype(F32), self.source, 1
        )

    def window(self, channels):
        return (channels // self.width + 4) * self.width


def gate_rims(channels, block_size, ntensor, offset):
    up = [(i, i + 1) for i in range(ntensor - 1)]
    down = [(i + 1, i) for i in range(ntensor - 1)]
    last = jnp.int32(channels - block_size)
    return [
        Rim(up, down, last, offset - block_size, block_size, block_size),
        Rim(down, up, jnp.int32(0), offset + channels, block_size, block_size),
    ]


def same_block(first, count, offset, channels, block_size):
    rows = (first + jnp.arange(count, dtype=jnp.int32))[:, None]
    columns = (offset + jnp.arange(channels, dtype=jnp.int32))[None, :]
    return (rows + block_size) // block_size == (columns + block_size) // block_size


def gate_dense(gate_w, offset, first, count):
    block_size = gate_w.shape[2]
    total = gate_w.shape[1] * block_size
    channels = total // lax.axis_size("tensor")
    columns = gate_w.transpose(2, 0, 1, 3).reshape(block_size, 2, total)
    columns = lax.dynamic_slice_in_dim(columns, offset, channels, 2)
    copies = -(-count // block_size) + 1
    tall = jnp.concatenate([columns] * copies, axis=0)
    tall = lax.dynamic_slice_in_dim(tall, (first + block_size) % block_size, count, 0)
    same = same_block(first, count, offset, channels, block_size)
    dense = jnp.where(same[:, None, :], tall, jnp.zeros_like(tall))
    return dense.reshape(count, 2 * channels)


def doc_starts(seg_ids, seq_len):
    places = jnp.arange(seg_ids.shape[0], dtype=jnp.int32)
    before = jnp.concatenate([seg_ids[:1], seg_ids[:-1]])
    resets = (places % seq_len == 0) | (seg_ids != before)
    starts = lax.cummax(jnp.where(resets, places, jnp.zeros_like(places)), axis=0)
    return starts


def causal_conv(starts, values, kernel):
    places = jnp.arange(values.shape[0], dtype=jnp.int32)
    total = values * kernel[0]
    for offset_k in range(1, kernel.shape[0]):
        moved = jnp.concatenate(
            [jnp.zeros((offset_k, values.shape[1]), values.dtype), values[:-offset_k]], axis=0
        )
        valid = (places - offset_k >= starts)[:, None]
        total = total + jnp.where(valid, moved, jnp.zeros_like(moved)) * kernel[offset_k]
    return total


def geglu(gate_val, up_val):
    return jax.nn.gelu(gate_val, approximate=True) * up_val


def line_groups():
    ndp = lax.axis_size("dp")
    return [list(range(core, ndp, 2)) for core in range(2)]


def to_sibling(block):
    route = [(i, i + 1 - 2 * (i % 2)) for i in range(lax.axis_size("dp"))]
    return lax.ppermute(block, "dp", route)


def gather_line(own):
    return lax.all_gather(own, "dp", axis=0, axis_index_groups=line_groups())


def join_cores(line):
    core = lax.axis_index("dp") % 2
    chips, rows, columns = line.shape
    other = to_sibling(line)
    first = jnp.where(core == 0, line, other)
    second = jnp.where(core == 0, other, line)
    return jnp.stack([first, second], axis=1).reshape(chips * 2 * rows, columns)


def scatter_two_level(grad):
    core = lax.axis_index("dp") % 2
    chips = lax.axis_size("dp") // 2
    rows, columns = grad.shape[0] // (2 * chips), grad.shape[1]
    split = grad.reshape(chips, 2, rows, columns)
    away = lax.dynamic_index_in_dim(split, 1 - core, 1, keepdims=False)
    kept = lax.dynamic_index_in_dim(split, core, 1, keepdims=False)
    both = kept.astype(F32) + to_sibling(away).astype(F32)
    both = both.astype(BF16).reshape(chips * rows, columns)
    return lax.psum_scatter(
        both, "dp", scatter_dimension=0, axis_index_groups=line_groups(), tiled=True
    )


def rows_times(left, right):
    return lax.dot_general(left, right, (((1,), (1,)), ((), ())), preferred_element_type=F32)


def rows_back(lefts, rights):
    total = rows_times(lefts[0], rights[0])
    return total + rows_times(lefts[1], rights[1])


def inner_rows(left, right):
    return lax.dot_general(left, right, (((0,), (0,)), ((), ())), preferred_element_type=F32)


def body(
    tokens,
    segments,
    cotangent,
    norm_gain,
    w_y,
    w_x,
    conv_w,
    gate_w,
    decay_param,
    w_out,
    mlp_gain,
    w_gate,
    w_up,
    w_down,
):
    ntensor = lax.axis_size("tensor")
    ndp = lax.axis_size("dp")
    nbits = log2_of(ntensor)
    tindex = lax.axis_index("tensor")
    own_rows, width = tokens.shape
    group_rows = own_rows * ntensor
    block_size = gate_w.shape[2]
    nblocks = gate_w.shape[1]
    dp_rows, channels = w_y.shape
    taps = conv_w.shape[0]
    offset = tindex * channels
    shape = jax.ShapeDtypeStruct
    gain_in = norm_gain.reshape(1, width)
    gain_mid = mlp_gain.reshape(1, width)
    seg_rows_of = own_rows // 128
    normed_rows, cot_rows, seg_all, wy_loc, wx_loc, wout_loc = call_kernel(
        partial(enter_kernel, nbits),
        (
            shape((group_rows, width), BF16),
            shape((group_rows, width), BF16),
            shape((ntensor, seg_rows_of, 128), jnp.int32),
        )
        + (shape((dp_rows * ndp, channels), BF16),) * 3,
        gather_sems(nbits)
        + gather_sems(nbits)
        + [pltpu.SemaphoreType.DMA((ntensor - 1,)), pltpu.SemaphoreType.DMA((ntensor - 1,))]
        + [pltpu.SemaphoreType.DMA((2,))]
        + line_sems(ndp) * 3,
        0,
        tokens,
        cotangent,
        segments.reshape(seg_rows_of, 128),
        gain_in,
        w_y,
        w_x,
        w_out,
        far_in=(4, 5, 6),
        far_out=(3, 4, 5),
    )
    w_gate, w_up, w_down, normed_rows = lax.optimization_barrier(
        (w_gate, w_up, w_down, normed_rows)
    )
    wg_loc = lax.all_gather(w_gate, "dp", axis=0, tiled=True)
    wu_loc = lax.all_gather(w_up, "dp", axis=0, tiled=True)
    seg_rows = seg_all.reshape(group_rows)
    starts = doc_starts(seg_rows, group_rows)
    conv_loc = lax.dynamic_slice_in_dim(conv_w, offset, channels, 1)
    decay_loc = lax.dynamic_slice_in_dim(decay_param, offset, channels, 0).reshape(1, channels)
    soft = jax.nn.softplus(decay_loc)
    slope_soft = jax.nn.sigmoid(decay_loc)
    half_blocks = (
        channels % block_size == block_size // 2 and ntensor % 2 == 0 and block_size % 256 == 0
    )
    since = (jnp.arange(group_rows, dtype=jnp.int32) - starts).astype(F32)[:, None]
    branch_x = jnp.dot(normed_rows, wx_loc, preferred_element_type=F32)
    branch_y = jnp.dot(normed_rows, wy_loc, preferred_element_type=F32)
    if half_blocks:
        span_blocks = channels // block_size + 1
        w_window = lax.dynamic_slice_in_dim(gate_w, offset // block_size, span_blocks, 1)
        taps_pad = jnp.concatenate([conv_loc, jnp.zeros((8 - taps, channels), F32)], axis=0)
        mixed_low, states, window, gate_pre = call_kernel(
            partial(recurrence_kernel, taps),
            (
                shape((group_rows, channels), BF16),
                shape((group_rows, channels), F32),
                shape((group_rows, span_blocks * block_size), BF16),
                shape((group_rows, 2 * channels), F32),
            ),
            [pltpu.SemaphoreType.DMA((1,)), pltpu.SemaphoreType.DMA((1,))],
            5,
            branch_x,
            branch_y,
            taps_pad,
            soft,
            since,
            w_window,
        )
    else:
        rims = gate_rims(channels, block_size, ntensor, offset)
        own_dense = gate_dense(gate_w, offset, offset, channels)
        rim_dense = [gate_dense(gate_w, offset, rim.first, rim.width) for rim in rims]
        conv_out, conv_pull = jax.vjp(partial(causal_conv, starts), branch_x, conv_loc)
        conv_low = conv_out.astype(BF16)
        rim_cells = [rim.fetch(conv_low) for rim in rims]
        gate_pre = jnp.dot(conv_low, own_dense, preferred_element_type=F32)
        for cells, dense in zip(rim_cells, rim_dense):
            gate_pre = gate_pre + jnp.dot(cells, dense, preferred_element_type=F32)
        mixed_low, states = scan_call(
            forward_scan_kernel,
            (shape((group_rows, channels), BF16), shape((group_rows, channels), F32)),
            conv_low,
            gate_pre,
            branch_y,
            soft,
            since,
        )
    middle, mid_rows = call_kernel(
        partial(middle_kernel, nbits),
        (shape((own_rows, width), F32), shape((group_rows, width), BF16)),
        scatter_scratch(own_rows, width, nbits) + gather_sems(nbits),
        1,
        rows_times(mixed_low, wout_loc).astype(BF16),
        tokens,
        gain_mid,
    )
    wg_loc, w_down = lax.optimization_barrier((wg_loc, w_down))
    wd_line = gather_line(w_down)
    gate_val = jnp.dot(mid_rows, wg_loc, preferred_element_type=F32)
    up_val = jnp.dot(mid_rows, wu_loc, preferred_element_type=F32)
    hidden, act_pull = jax.vjp(geglu, gate_val, up_val)
    hidden_low = hidden.astype(BF16)
    grad_wd = inner_rows(cot_rows, hidden_low).astype(BF16)
    sum_wd = scatter_two_level(grad_wd)
    grad_wd, wd_line = lax.optimization_barrier((grad_wd, wd_line))
    wd_loc = join_cores(wd_line)
    d_hidden = jnp.dot(cot_rows, wd_loc, preferred_element_type=F32)
    d_gate, d_up = act_pull(d_hidden)
    d_gate = d_gate.astype(BF16)
    d_up = d_up.astype(BF16)
    grad_wg = inner_rows(mid_rows, d_gate).astype(BF16)
    sum_wg = lax.psum_scatter(grad_wg, "dp", scatter_dimension=0, tiled=True)
    d_mid_part = rows_back((d_gate, d_up), (wg_loc, wu_loc)).astype(BF16)
    d_mid_part, grad_wg = lax.optimization_barrier((d_mid_part, grad_wg))
    d_middle, d_mixer, d_gain_mid = call_kernel(
        partial(turn_kernel, nbits),
        (
            shape((own_rows, width), F32),
            shape((group_rows, width), BF16),
            shape((8, width), F32),
        ),
        scatter_scratch(own_rows, width, nbits) + gather_sems(nbits),
        2,
        d_mid_part,
        cotangent,
        middle,
        gain_mid,
    )
    d_mixer, sum_wd = lax.optimization_barrier((d_mixer, sum_wd))
    d_mixed_in = jnp.dot(d_mixer, wout_loc, preferred_element_type=F32)
    mid_again, d_mixed_in = lax.optimization_barrier((mid_rows, d_mixed_in))
    grad_wu = inner_rows(mid_again, d_up).astype(BF16)
    sum_wu = lax.psum_scatter(grad_wu, "dp", scatter_dimension=0, tiled=True)
    d_mixed_in, grad_wu = lax.optimization_barrier((d_mixed_in, grad_wu))
    unit = math.gcd(channels, block_size)
    if half_blocks:
        d_branch_y, d_branch_x, gate_grad, own_small = call_kernel(
            partial(recurrence_back_kernel, taps),
            (
                shape((group_rows, channels), BF16),
                shape((group_rows, channels), BF16),
                shape((channels // unit * 2, block_size, unit), BF16),
                shape((8, channels), F32),
            ),
            [
                pltpu.VMEM((group_rows, channels), F32),
                pltpu.VMEM((group_rows, 2 * channels), BF16),
                pltpu.VMEM((group_rows, unit), BF16),
                pltpu.VMEM((group_rows, unit), BF16),
                pltpu.VMEM((taps + 1, 8, channels), F32),
                pltpu.SemaphoreType.DMA((1,)),
                pltpu.SemaphoreType.DMA((1,)),
            ],
            6,
            d_mixed_in,
            window,
            gate_pre,
            branch_y,
            branch_x,
            states,
            taps_pad,
            soft,
            slope_soft,
            since,
            w_window,
        )
        gate_grad, d_branch_y, sum_wg = lax.optimization_barrier((gate_grad, d_branch_y, sum_wg))
        gate_grad = gate_grad.reshape(channels // unit * 2 * block_size, unit)
    else:
        d_conv, d_gate_low, d_branch_y, d_decay = scan_call(
            backward_scan_kernel,
            (
                shape((group_rows, channels), F32),
                shape((group_rows, 2 * channels), BF16),
                shape((group_rows, channels), BF16),
                shape((8, channels), F32),
            ),
            d_mixed_in,
            conv_low,
            gate_pre,
            branch_y,
            states,
            soft,
            slope_soft,
            since,
        )
        d_gate_low, sum_wg = lax.optimization_barrier((d_gate_low, sum_wg))
        given = [rows_times(d_gate_low, dense).astype(BF16) for dense in rim_dense]
        taken = [rim.give(part) for rim, part in zip(rims, given)]
        d_conv_out = d_conv + rows_times(d_gate_low, own_dense)
        for rim, part in zip(rims, taken):
            d_conv_out = rim.add(d_conv_out, part)
        d_branch_x, grad_conv_loc = conv_pull(d_conv_out)
        d_branch_x = d_branch_x.astype(BF16)
        base = offset // block_size * block_size - rims[0].room
        window_rows = rims[0].window(channels)
        picked = jnp.zeros((window_rows, 2 * channels), F32)
        for first, cells in [(offset, conv_low)] + [(r.first, c) for r, c in zip(rims, rim_cells)]:
            part = inner_rows(cells, d_gate_low)
            same = same_block(first, cells.shape[1], offset, channels, block_size)
            part = jnp.where(jnp.concatenate([same, same], axis=1), part, 0.0)
            picked = lax.dynamic_update_slice(picked, part, (first - base, jnp.int32(0)))
        picked = picked.reshape(window_rows // block_size, block_size, 2, channels // unit, unit)
        gate_grad = picked.sum(axis=0).astype(BF16).transpose(2, 1, 0, 3)
        gate_grad = gate_grad.reshape(channels // unit * 2 * block_size, unit)
        own_small = jnp.concatenate(
            [
                grad_conv_loc,
                jnp.sum(d_decay, axis=0, keepdims=True),
                jnp.zeros((7 - taps, channels), F32),
            ],
            axis=0,
        )

    grad_wout = inner_rows(d_mixer, mixed_low).astype(BF16)
    sum_wout = lax.psum_scatter(grad_wout, "dp", scatter_dimension=0, tiled=True)
    grad_wy = inner_rows(normed_rows, d_branch_y).astype(BF16)
    grad_wx = inner_rows(normed_rows, d_branch_x).astype(BF16)
    ffn_part = rows_times(hidden_low, wd_loc).astype(BF16)
    d_normed = rows_back((d_branch_y, d_branch_x), (wy_loc, wx_loc)).astype(BF16)
    merged = nbits <= 2

    def halved(grad):
        return grad.reshape(ndp // 2, 2, grad.shape[0] // ndp, grad.shape[1])

    pieces = [halved(grad) for grad in (gate_grad, grad_wy, grad_wx)]
    peers = ntensor - 1
    gate_rows = gate_grad.shape[0] // ndp
    dma = pltpu.SemaphoreType.DMA
    scratch = scatter_scratch(own_rows, width, nbits)
    for piece in pieces:
        scratch += ring_scratch(ndp, piece.shape[2], piece.shape[3])
    scratch += [
        pltpu.VMEM((8, width), F32),
        pltpu.VMEM((ntensor, 8, channels), F32),
        pltpu.VMEM((peers, 8, channels), F32),
        pltpu.VMEM((8, channels), F32),
        pltpu.VMEM((ndp - 1, 8, channels), F32),
    ]
    scratch += [dma((peers,)), dma((peers,)), dma((ndp - 1,)), dma((ndp - 1,))]
    scratch += [dma((peers,)), dma((peers,)), dma((peers + ndp,)), dma((peers + ndp,))]
    if merged:
        scratch += scatter_scratch(own_rows, width, nbits)
    found = call_kernel(
        partial(leave_kernel, nbits, merged),
        (shape((own_rows, width), F32),)
        + (shape((dp_rows, channels), F32),) * 2
        + (
            shape((ntensor, ndp, gate_rows, unit), BF16),
            shape((ntensor, 8, channels), F32),
        )
        + ((shape((own_rows, width), BF16),) if merged else ()),
        scratch,
        3,
        d_normed,
        tokens,
        d_middle,
        gain_in,
        own_small,
        d_gain_mid,
        *pieces,
        *((ffn_part, middle) if merged else ()),
        far_in=(6, 7, 8),
    )
    grad_input, sum_wy, sum_wx, gate_all, small_all = found[:5]
    if merged:
        mixed = found[5]
    else:
        (mixed,) = call_kernel(
            partial(result_kernel, nbits),
            (shape((own_rows, width), BF16),),
            scatter_scratch(own_rows, width, nbits),
            4,
            ffn_part,
            middle,
        )
    per_block = block_size // unit
    sum_gate = gate_all.reshape(nblocks, per_block, 2, block_size, unit)
    sum_gate = gate_layout(sum_gate)
    summed = small_all.transpose(1, 0, 2).reshape(8, width)
    return (
        mixed,
        grad_input,
        summed[6],
        sum_wy,
        sum_wx,
        summed[:taps],
        sum_gate,
        summed[taps],
        sum_wout.astype(F32),
        summed[7],
        sum_wg.astype(F32),
        sum_wu.astype(F32),
        sum_wd.astype(F32),
    )


def solution(mesh):
    split = P(("dp", "tensor"), None)
    weight = P("dp", "tensor")
    return jax.shard_map(
        body,
        mesh=mesh,
        in_specs=(
            split,
            P(("dp", "tensor")),
            split,
            P(),
            weight,
            weight,
            P(),
            P(),
            P(),
            weight,
            P(),
            weight,
            weight,
            weight,
        ),
        out_specs=(
            split,
            split,
            P(),
            weight,
            weight,
            P(),
            P(),
            P(),
            weight,
            P(),
            weight,
            weight,
            weight,
        ),
        check_vma=False,
    )
```

```python
import math
from functools import partial

import jax
import jax.numpy as jnp
from jax import lax
from jax.experimental import pallas as pl
from jax.experimental.pallas import tpu as pltpu
from jax.sharding import PartitionSpec as P

EPSILON = 1e-06
MESH = pl.DeviceIdType.MESH
VMEM_BYTES = 56 * 1024 * 1024
CHUNK = 16
F32 = jnp.float32
BF16 = jnp.bfloat16


def subsets(bits):
    found = [()]
    for bit in bits:
        found = found + [chosen + (bit,) for chosen in found]
    return found


def flipped(index, bits):
    for bit in bits:
        mine = (index // (1 << bit)) % 2
        index = index + (1 - 2 * mine) * (1 << bit)
    return index


def log2_of(count):
    assert count & (count - 1) == 0
    return count.bit_length() - 1


def greet(axis_bits):
    barrier = pltpu.get_barrier_semaphore()
    for axis, bit in axis_bits:
        peer = flipped(lax.axis_index(axis), (bit,))
        pl.semaphore_signal(barrier, inc=1, device_id={axis: peer}, device_id_type=MESH)
    pl.semaphore_wait(barrier, len(axis_bits))


def halves_of(nbits, columns):
    half = columns // 2
    ups = tuple(range(nbits))
    return ((ups, 0, half), (ups[::-1], half, half))


class Gather:
    def __init__(self, ref, rows, nbits, send_sems, recv_sems):
        self.ref, self.rows, self.nbits = ref, rows, nbits
        self.sems = (send_sems, recv_sems)
        self.me = lax.axis_index("tensor")
        self.plan = []
        number = 0
        for half, (order, at, width) in enumerate(halves_of(nbits, ref.shape[1])):
            for step, bit in enumerate(order):
                for known in subsets(order[:step]):
                    self.plan.append((half, step, known, bit, at, width, number))
                    number += 1
        self.count = number

    def copy(self, item):
        half, step, known, bit, at, width, number = item
        row = pl.multiple_of(flipped(self.me, known) * self.rows, self.rows)
        piece = self.ref.at[pl.ds(row, self.rows), pl.ds(at, width)]
        return pltpu.make_async_remote_copy(
            src_ref=piece,
            dst_ref=piece,
            send_sem=self.sems[0].at[number],
            recv_sem=self.sems[1].at[number],
            device_id={"tensor": flipped(self.me, (bit,))},
            device_id_type=MESH,
        )

    def begin(self):
        for item in sorted(self.plan, key=lambda it: it[1]):
            if item[2] == ():
                self.copy(item).start()

    def advance(self, step):
        for item in self.plan:
            half, at_step, known, bit, at, width, number = item
            if at_step == step:
                self.copy(item).wait_recv()
                block = known + (bit,)
                for later in self.plan:
                    if later[0] == half and set(later[2]) == set(block):
                        self.copy(later).start()

    def finish(self, step=0):
        for at_step in range(step, self.nbits):
            self.advance(at_step)
        for item in self.plan:
            self.copy(item).wait_send()


def gather_copies(nbits):
    return 2 * ((1 << nbits) - 1)


class Scatter:
    def __init__(self, ref, landed, staged, rows, nbits, send_sems, recv_sems):
        self.ref, self.landed, self.staged = ref, landed, staged
        self.rows, self.nbits = rows, nbits
        self.sems = (send_sems, recv_sems)
        self.me = lax.axis_index("tensor")
        self.plan, self.slot = [], {}
        number = 0
        for half, (order, at, width) in enumerate(halves_of(nbits, ref.shape[1])):
            for step, bit in enumerate(order):
                for rest in subsets(order[step + 1 :])[::-1]:
                    self.plan.append((half, step, rest, bit, at, width, number))
                    if step > 0:
                        self.slot[number] = len(self.slot)
                    number += 1

    def copy(self, item):
        half, step, rest, bit, at, width, number = item
        if step == 0:
            row = pl.multiple_of(flipped(self.me, rest + (bit,)) * self.rows, self.rows)
            source = self.ref.at[pl.ds(row, self.rows), pl.ds(at, width)]
        else:
            source = self.staged.at[self.slot[number]]
        return pltpu.make_async_remote_copy(
            src_ref=source,
            dst_ref=self.landed.at[number],
            send_sem=self.sems[0].at[number],
            recv_sem=self.sems[1].at[number],
            device_id={"tensor": flipped(self.me, (bit,))},
            device_id_type=MESH,
        )

    def begin(self):
        for item in sorted(self.plan, key=lambda it: (len(it[2]) == 0)):
            if item[1] == 0:
                self.copy(item).start()

    def partial_sum(self, half, block, before, row, size):
        at, width = halves_of(self.nbits, self.ref.shape[1])[half][1:]
        base = pl.multiple_of(flipped(self.me, block) * self.rows + row, size)
        total = self.ref[pl.ds(base, size), pl.ds(at, width)].astype(F32)
        for it in self.plan:
            if it[0] == half and it[1] < before and set(it[2]) == set(block):
                total = total + self.landed[it[6], pl.ds(row, size), :].astype(F32)
        return total

    def advance(self, step):
        for half in range(2):
            for item in self.plan:
                if item[0] == half and item[1] == step:
                    self.copy(item).wait_recv()
            for item in self.plan:
                if item[0] == half and item[1] == step + 1:

                    def fill(row, item=item):
                        value = self.partial_sum(
                            item[0], item[2] + (item[3],), item[1], row, CHUNK
                        )
                        where = (self.slot[item[6]], pl.ds(row, CHUNK))
                        self.staged[where + (slice(None),)] = value.astype(BF16)

                    chunks(self.rows, fill)
                    self.copy(item).start()

    def run(self):
        for step in range(self.nbits):
            self.advance(step)

    def total(self, row, size):
        return jnp.concatenate(
            [self.partial_sum(half, (), self.nbits, row, size) for half in range(2)], axis=1
        )

    def drain(self):
        for item in self.plan:
            self.copy(item).wait_send()


def scatter_scratch(rows, columns, nbits):
    copies = gather_copies(nbits)
    later = max(1, copies - (1 << nbits))
    return [
        pltpu.VMEM((copies, rows, columns // 2), BF16),
        pltpu.VMEM((later, rows, columns // 2), BF16),
        pltpu.SemaphoreType.DMA((copies,)),
        pltpu.SemaphoreType.DMA((copies,)),
    ]


def gather_sems(nbits):
    copies = gather_copies(nbits)
    return [pltpu.SemaphoreType.DMA((copies,)), pltpu.SemaphoreType.DMA((copies,))]


def tensor_bits(nbits):
    return [("tensor", bit) for bit in range(nbits)]


def rms_scale_of(values):
    return lax.rsqrt(jnp.mean(values * values, axis=-1, keepdims=True) + EPSILON)


def chunks(rows, body):
    def step(i, carry):
        body(pl.multiple_of(i * CHUNK, CHUNK))
        return carry

    lax.fori_loop(0, rows // CHUNK, step, 0)


def own_row(row, rows):
    return pl.multiple_of(lax.axis_index("tensor") * rows + row, CHUNK)


def dp_place():
    me = lax.axis_index("dp")
    return me // 2, me % 2, lax.axis_size("dp") // 2


def dp_index(chip, core):
    return chip * 2 + core


UP, DOWN = 1, -1


class LineGather:
    def __init__(self, own, whole, send_sems, recv_sems):
        self.own, self.whole = own, whole
        self.sems = (send_sems, recv_sems)
        self.chip, self.core, self.chips = dp_place()
        self.rows = own.shape[0]

    def block(self, chip):
        row = pl.multiple_of(dp_index(chip, self.core) * self.rows, self.rows)
        return self.whole.at[pl.ds(row, self.rows), :]

    def has(self, way, distance):
        return self.chip >= distance if way == UP else self.chip + distance < self.chips

    def number(self, way, distance):
        return (0 if way == UP else self.chips) + distance

    def along(self, way, distance):
        block = self.block(self.chip - way * distance)
        return pltpu.make_async_remote_copy(
            src_ref=self.own if distance == 0 else block,
            dst_ref=block,
            send_sem=self.sems[0].at[self.number(way, distance)],
            recv_sem=self.sems[1].at[self.number(way, distance + 1)],
            device_id={"dp": dp_index(self.chip + way, self.core)},
            device_id_type=MESH,
        )

    def arrival(self, way, distance):
        block = self.block(self.chip - way * distance)
        return pltpu.make_async_remote_copy(
            src_ref=block,
            dst_ref=block,
            send_sem=self.sems[0].at[self.number(way, distance)],
            recv_sem=self.sems[1].at[self.number(way, distance)],
            device_id={"dp": dp_index(self.chip + way, self.core)},
            device_id_type=MESH,
        )

    def across(self, way, distance):
        block = self.block(self.chip - way * distance)
        number = 2 * self.chips + self.number(way, distance)
        return pltpu.make_async_remote_copy(
            src_ref=self.own if distance == 0 else block,
            dst_ref=block,
            send_sem=self.sems[0].at[number],
            recv_sem=self.sems[1].at[number],
            device_id={"dp": dp_index(self.chip, 1 - self.core)},
            device_id_type=MESH,
        )

    def local(self):
        return pltpu.make_async_copy(
            self.own, self.block(self.chip), self.sems[0].at[4 * self.chips]
        )

    def begin(self):
        for way in (UP, DOWN):

            @pl.when(self.has(-way, 1))
            def _(way=way):
                self.along(way, 0).start()

        self.across(UP, 0).start()
        self.local().start()

    def pass_on(self, distance):
        for way in (UP, DOWN):

            @pl.when(self.has(way, distance))
            def _(way=way):
                self.arrival(way, distance).wait_recv()

                @pl.when(self.has(-way, 1))
                def _():
                    self.along(way, distance).start()

                self.across(way, distance).start()

    def finish(self):
        self.across(UP, 0).wait()
        self.local().wait()
        for way in (UP, DOWN):
            for distance in range(self.chips):

                @pl.when(self.has(way, distance) & self.has(-way, 1))
                def _(way=way, distance=distance):
                    self.along(way, distance).wait_send()

                if distance:

                    @pl.when(self.has(way, distance))
                    def _(way=way, distance=distance):
                        self.across(way, distance).wait()


def line_sems(ndp):
    chips = ndp // 2
    return [pltpu.SemaphoreType.DMA((4 * chips + 1,)), pltpu.SemaphoreType.DMA((4 * chips + 1,))]


def greet_peers(nbits, all_tensor, whole_dp):
    me = lax.axis_index("tensor")
    chip, core, chips = dp_place()
    barrier = pltpu.get_barrier_semaphore()

    def signal(target):
        pl.semaphore_signal(barrier, inc=1, device_id=target, device_id_type=MESH)

    met = 0
    for chosen in subsets(tuple(range(nbits))):
        if chosen and (all_tensor or len(chosen) == 1):
            signal({"tensor": flipped(me, chosen)})
            met += 1
    if whole_dp:
        for shift in range(chips):
            for turn in range(2):
                if (shift, turn) != (0, 0):
                    other = dp_index((chip + shift) % chips, core + turn * (1 - 2 * core))
                    signal({"dp": other})
                    met += 1
    else:
        signal({"dp": dp_index(chip, 1 - core)})
        met += 1

        for shift in sorted({1 % chips, chips - 1} - {0}):
            signal({"dp": dp_index((chip + shift) % chips, core)})
            met += 1

    pl.semaphore_wait(barrier, met)


def enter_kernel(
    nbits, tokens, seg, gain, w_y, w_x, normed_all, seg_all, wy_all, wx_all, s0, r0, s2, r2, l0, *line
):
    rows = tokens.shape[0]
    me = lax.axis_index("tensor")
    peers = [chosen for chosen in subsets(tuple(range(nbits))) if chosen]
    greet_peers(nbits, True, False)
    lines = [
        LineGather(own, whole, line[2 * number], line[2 * number + 1])
        for number, (own, whole) in enumerate(((w_y, wy_all), (w_x, wx_all)))
    ]
    for item in lines:
        item.begin()

    def norm(row):
        values = tokens[pl.ds(row, CHUNK), :].astype(F32)
        scaled = values * rms_scale_of(values) * gain[...]
        normed_all[pl.ds(own_row(row, rows), CHUNK), :] = scaled.astype(BF16)

    chunks(rows, norm)
    gather = Gather(normed_all, rows, nbits, s0, r0)
    gather.begin()
    seg_own = pltpu.make_async_copy(seg, seg_all.at[me], l0.at[0])
    seg_own.start()
    seg_copies = [
        pltpu.make_async_remote_copy(
            src_ref=seg,
            dst_ref=seg_all.at[me],
            send_sem=s2.at[number],
            recv_sem=r2.at[number],
            device_id={"tensor": flipped(me, chosen)},
            device_id_type=MESH,
        )
        for number, chosen in enumerate(peers)
    ]
    for copy in seg_copies:
        copy.start()
    chips = lines[0].chips
    for item in lines:
        item.pass_on(1)
    gather.advance(0)
    for distance in range(2, chips):
        for item in lines:
            item.pass_on(distance)
    gather.finish(1)
    for item in lines:
        item.finish()
    for copy in seg_copies:
        copy.wait()
    seg_own.wait()


class Fetch:
    def __init__(self, nbits, cot, w_out, cot_all, wout_all, s0, r0, l0, s1, r1):
        rows = cot.shape[0]
        own = pl.multiple_of(lax.axis_index("tensor") * rows, rows)
        self.local = pltpu.make_async_copy(cot, cot_all.at[pl.ds(own, rows), :], l0.at[0])
        self.gather = Gather(cot_all, rows, nbits, s0, r0)
        self.line = LineGather(w_out, wout_all, s1, r1)

    def begin(self):
        self.line.begin()
        self.local.start()
        self.local.wait()
        self.gather.begin()

    def advance(self, part):
        if part == 0:
            self.line.pass_on(1)
        elif part == 1:
            self.gather.advance(0)
            for distance in range(2, self.line.chips - 1):
                self.line.pass_on(distance)
        else:
            if self.line.chips > 2:
                self.line.pass_on(self.line.chips - 1)

    def finish(self):
        self.gather.finish(1)
        self.line.finish()


def fetch_scratch(nbits, ndp):
    return gather_sems(nbits) + [pltpu.SemaphoreType.DMA((1,))] + line_sems(ndp)


def fetch_kernel(nbits, cot, w_out, cot_all, wout_all, *sems):
    greet_peers(nbits, False, False)
    fetch = Fetch(nbits, cot, w_out, cot_all, wout_all, *sems)
    fetch.begin()
    for part in range(3):
        fetch.advance(part)
    fetch.finish()


def middle_kernel(
    nbits, mixer, tokens, gain, middle, mid_all, landed, staged, s0, r0, s1, r1
):
    rows = tokens.shape[0]
    greet(tensor_bits(nbits))
    scatter = Scatter(mixer, landed, staged, rows, nbits, s0, r0)
    scatter.begin()
    scatter.run()

    def norm(row):
        values = tokens[pl.ds(row, CHUNK), :].astype(F32) + scatter.total(row, CHUNK)
        middle[pl.ds(row, CHUNK), :] = values
        scaled = values * rms_scale_of(values) * gain[...]
        mid_all[pl.ds(own_row(row, rows), CHUNK), :] = scaled.astype(BF16)

    chunks(rows, norm)
    gather = Gather(mid_all, rows, nbits, s1, r1)
    gather.begin()
    gather.finish()
    scatter.drain()


def result_kernel(nbits, ffn, middle, mixed, landed, staged, s0, r0):
    rows = middle.shape[0]
    greet(tensor_bits(nbits))
    scatter = Scatter(ffn, landed, staged, rows, nbits, s0, r0)
    scatter.begin()
    scatter.run()

    def add(row):
        values = middle[pl.ds(row, CHUNK), :] + scatter.total(row, CHUNK)
        mixed[pl.ds(row, CHUNK), :] = values.astype(BF16)

    chunks(rows, add)
    scatter.drain()


def norm_pull(values, gain, cotangent):
    scale = rms_scale_of(values)
    unit = values * scale
    inner = cotangent * gain
    back = scale * (inner - unit * jnp.mean(inner * unit, axis=-1, keepdims=True))
    return back, cotangent * unit


def eight_rows(values):
    total = values[0:8]
    for at in range(8, CHUNK, 8):
        total = total + values[at : at + 8]
    return total


def turn_kernel(
    nbits, d_norm, cot, middle, gain, d_middle, d_mixer, d_gain, landed, staged, s0, r0, s1, r1
):
    rows = middle.shape[0]
    greet(tensor_bits(nbits))
    scatter = Scatter(d_norm, landed, staged, rows, nbits, s0, r0)
    scatter.begin()
    d_gain[...] = jnp.zeros_like(d_gain)
    scatter.run()

    def pull(row):
        span = pl.ds(row, CHUNK)
        back, gains = norm_pull(middle[span, :], gain[...], scatter.total(row, CHUNK))
        values = cot[span, :].astype(F32) + back
        d_middle[span, :] = values
        d_mixer[pl.ds(own_row(row, rows), CHUNK), :] = values.astype(BF16)
        d_gain[...] += eight_rows(gains)

    chunks(rows, pull)
    gather = Gather(d_mixer, rows, nbits, s1, r1)
    gather.begin()
    gather.finish()
    scatter.drain()


class LineSum:
    def __init__(self, whole, kept, swapped, staged, landed, send_sems, recv_sems, columns=None):
        self.whole, self.kept, self.swapped = whole, kept, swapped
        self.staged, self.landed = staged, landed
        self.sems = (send_sems, recv_sems)
        self.columns = columns
        self.chip, self.core, self.chips = dp_place()
        self.rows = whole.shape[2]

    def half(self, core):
        if self.columns is None:
            return self.whole.at[:, core]
        return self.whole.at[:, core, :, self.columns]

    def local(self):
        return pltpu.make_async_copy(
            self.half(self.core), self.kept, self.sems[0].at[2 * self.chips]
        )

    def swap(self):
        return pltpu.make_async_remote_copy(
            src_ref=self.half(1 - self.core),
            dst_ref=self.swapped,
            send_sem=self.sems[0].at[0],
            recv_sem=self.sems[1].at[0],
            device_id={"dp": dp_index(self.chip, 1 - self.core)},
            device_id_type=MESH,
        )

    def has(self, way, distance):
        return self.chip + distance < self.chips if way == UP else self.chip >= distance

    def slot(self, way, distance):
        return (0 if way == UP else self.chips - 1) + distance

    def hop(self, way, distance):
        return pltpu.make_async_remote_copy(
            src_ref=self.staged.at[self.slot(way, distance - 1)],
            dst_ref=self.landed.at[self.slot(way, distance - 1)],
            send_sem=self.sems[0].at[1 + self.slot(way, distance - 1)],
            recv_sem=self.sems[1].at[1 + self.slot(way, distance - 1)],
            device_id={"dp": dp_index(self.chip + way, self.core)},
            device_id_type=MESH,
        )

    def arrival(self, way, distance):
        number = self.slot(way, distance)
        return pltpu.make_async_remote_copy(
            src_ref=self.landed.at[number],
            dst_ref=self.landed.at[number],
            send_sem=self.sems[0].at[1 + number],
            recv_sem=self.sems[1].at[1 + number],
            device_id={"dp": dp_index(self.chip - way, self.core)},
            device_id_type=MESH,
        )

    def begin(self):
        self.swap().start()
        self.local().start()

    def both(self, chip, span):
        return self.kept[chip, span, :].astype(F32) + self.swapped[chip, span, :].astype(F32)

    def send(self, distance):
        if distance == self.chips - 1:
            self.local().wait()
            self.swap().wait_recv()
        for way in (UP, DOWN):

            @pl.when(self.has(way, distance))
            def _(way=way):
                chip = self.chip + way * distance
                slot = self.slot(way, distance - 1)

                def first(row):
                    span = pl.ds(row, CHUNK)
                    self.staged[slot, span, :] = self.both(chip, span).astype(BF16)

                def later(row):
                    span = pl.ds(row, CHUNK)
                    total = self.both(chip, span) + self.landed[
                        self.slot(way, distance), span, :
                    ].astype(F32)
                    self.staged[slot, span, :] = total.astype(BF16)

                if distance == self.chips - 1:
                    chunks(self.rows, first)
                else:

                    @pl.when(self.has(-way, 1))
                    def _():
                        self.arrival(way, distance).wait_recv()
                        chunks(self.rows, later)

                    @pl.when(jnp.logical_not(self.has(-way, 1)))
                    def _():
                        chunks(self.rows, first)

                self.hop(way, distance).start()

    def finish(self, store):
        below, above = self.has(DOWN, 1), self.has(UP, 1)

        def fill(slots):
            for way in slots:
                self.arrival(way, 0).wait_recv()

            def one(row):
                span = pl.ds(row, CHUNK)
                total = self.both(self.chip, span)
                for way in slots:
                    total = total + self.landed[self.slot(way, 0), span, :].astype(F32)
                store(span, total)

            chunks(self.rows, one)

        @pl.when(below & above)
        def _():
            fill((UP, DOWN))

        @pl.when(jnp.logical_not(above))
        def _():
            fill((UP,))

        @pl.when(jnp.logical_not(below))
        def _():
            fill((DOWN,))

    def drain(self):
        self.swap().wait_send()
        for way in (UP, DOWN):
            for distance in range(1, self.chips):

                @pl.when(self.has(way, distance))
                def _(way=way, distance=distance):
                    self.hop(way, distance).wait_send()


def line_scratch(ndp, rows, columns):
    chips = ndp // 2
    return [
        pltpu.VMEM((chips, rows, columns), BF16),
        pltpu.VMEM((chips, rows, columns), BF16),
        pltpu.VMEM((2 * chips - 2, rows, columns), BF16),
        pltpu.VMEM((2 * chips - 2, rows, columns), BF16),
        pltpu.SemaphoreType.DMA((2 * chips + 1,)),
        pltpu.SemaphoreType.DMA((2 * chips + 1,)),
    ]


def sum_kernel(count, whole, total, *scratch):
    greet_peers(0, False, False)
    width = total.shape[1] // count
    pieces = [
        LineSum(
            whole, *scratch[RING * piece : RING * (piece + 1)], pl.ds(piece * width, width)
        )
        for piece in range(count)
    ]
    for piece in pieces:
        piece.begin()
    for distance in range(pieces[0].chips - 1, 0, -1):
        for piece in pieces:
            piece.send(distance)
    for number, piece in enumerate(pieces):

        def store(span, value, number=number):
            total[span, number * width : (number + 1) * width] = value

        piece.finish(store)
    for piece in pieces:
        piece.drain()


RING = 6


def leave_kernel(nbits, with_ffn, *refs):
    refs = list(refs)

    def take(count):
        taken = refs[:count]
        del refs[:count]
        return taken

    d_norm, tokens, d_middle, gain, own_small, d_gain_mid = take(6)
    pieces = take(3)
    ffn, middle = take(2) if with_ffn else (None, None)
    grad_input, sum_y, sum_x, gate_all, small_all = take(5)
    mixed = take(1)[0] if with_ffn else None
    landed, staged, s0, r0 = take(4)
    rings = [LineSum(piece, *take(RING)) for piece in pieces]
    d_gain, gains, gains_landed, small, small_landed = take(5)
    gain_s, gain_r, vec_s, vec_r, join_s, join_r, gate_s, gate_r = take(8)
    rows = tokens.shape[0]
    me = lax.axis_index("tensor")
    chip, core, chips = dp_place()
    place = dp_index(chip, core)
    peers = [chosen for chosen in subsets(tuple(range(nbits))) if chosen]
    others = [(shift, turn) for shift in range(chips) for turn in range(2)][1:]
    greet_peers(nbits, True, True)
    for ring in rings:
        ring.begin()
    scatter = Scatter(d_norm, landed, staged, rows, nbits, s0, r0)
    scatter.begin()
    if with_ffn:
        second = Scatter(ffn, *take(2), rows, nbits, *take(2))
    d_gain[...] = jnp.zeros_like(d_gain)
    far = list(range(chips - 1, 0, -1))
    for ring in rings:
        ring.send(far[0])
    if len(far) > 1:
        rings[0].send(far[1])
    scatter.advance(0)
    if with_ffn:
        second.begin()
    if len(far) > 1:
        for ring in rings[1:]:
            ring.send(far[1])
    for distance in far[2:]:
        rings[0].send(distance)
    for step in range(1, nbits):
        scatter.advance(step)

    def pull(row):
        span = pl.ds(row, CHUNK)
        back, parts = norm_pull(
            tokens[span, :].astype(F32), gain[...], scatter.total(row, CHUNK)
        )
        grad_input[span, :] = d_middle[span, :] + back
        d_gain[...] += eight_rows(parts)

    chunks(rows, pull)
    share = gains.shape[2]
    top = jnp.sum(d_gain[...], axis=0, keepdims=True)
    low = jnp.sum(d_gain_mid[...], axis=0, keepdims=True)
    place8 = lax.broadcasted_iota(jnp.int32, (8, share), 0)
    for index in range(1 << nbits):
        span = slice(index * share, (index + 1) * share)
        gains[index] = jnp.where(
            place8 == 6, top[:, span], jnp.where(place8 == 7, low[:, span], 0.0)
        )

    def gain_copy(number, chosen):
        peer = flipped(me, chosen)
        return pltpu.make_async_remote_copy(
            src_ref=gains.at[peer],
            dst_ref=gains_landed.at[number],
            send_sem=gain_s.at[number],
            recv_sem=gain_r.at[number],
            device_id={"tensor": peer},
            device_id_type=MESH,
        )

    for number, chosen in enumerate(peers):
        gain_copy(number, chosen).start()
    for distance in far[2:]:
        for ring in rings[1:]:
            ring.send(distance)
    total = own_small[...] + gains[me]
    for number, chosen in enumerate(peers):
        gain_copy(number, chosen).wait_recv()
        total = total + gains_landed[number]
    small[...] = total

    def vec_copy(number, shift, turn):
        other = dp_index((chip + shift) % chips, core + turn * (1 - 2 * core))
        return pltpu.make_async_remote_copy(
            src_ref=small,
            dst_ref=small_landed.at[number],
            send_sem=vec_s.at[number],
            recv_sem=vec_r.at[number],
            device_id={"dp": other},
            device_id_type=MESH,
        )

    for number, (shift, turn) in enumerate(others):
        vec_copy(number, shift, turn).start()

    def store_gate(span, value):
        gate_all[me, place, span, :] = value.astype(BF16)

    rings[0].finish(store_gate)

    def gate_copy(number, chip_from, ref, target):
        return pltpu.make_async_remote_copy(
            src_ref=ref,
            dst_ref=ref,
            send_sem=gate_s.at[number],
            recv_sem=gate_r.at[number],
            device_id=target,
            device_id_type=MESH,
        )

    def gate_tensor(number, chosen):
        ref = gate_all.at[me, place]
        return gate_copy(number, chip, ref, {"tensor": flipped(me, chosen)})

    def gate_line(shift):
        target = {"dp": dp_index((chip + shift) % chips, core)}
        return gate_copy(len(peers) + shift - 1, chip, gate_all.at[:, place], target)

    def gate_core(shift):
        ref = gate_all.at[:, dp_index((chip + chips - shift) % chips, core)]
        target = {"dp": dp_index(chip, 1 - core)}
        return gate_copy(len(peers) + chips - 1 + shift, chip, ref, target)

    for number, chosen in enumerate(peers):
        gate_tensor(number, chosen).start()
    if with_ffn:
        second.advance(0)
    total = small[...]
    for number, (shift, turn) in enumerate(others):
        vec_copy(number, shift, turn).wait_recv()
        total = total + small_landed[number]
    small_all[me] = total

    def join_copy(number, chosen):
        return pltpu.make_async_remote_copy(
            src_ref=small_all.at[me],
            dst_ref=small_all.at[me],
            send_sem=join_s.at[number],
            recv_sem=join_r.at[number],
            device_id={"tensor": flipped(me, chosen)},
            device_id_type=MESH,
        )

    for number, chosen in enumerate(peers):
        join_copy(number, chosen).start()
    for number, chosen in enumerate(peers):
        gate_tensor(number, chosen).wait_recv()
    for shift in range(1, chips):
        gate_line(shift).start()
    gate_core(0).start()
    if with_ffn:
        for step in range(1, nbits):
            second.advance(step)

        def add(row):
            span = pl.ds(row, CHUNK)
            mixed[span, :] = (middle[span, :] + second.total(row, CHUNK)).astype(BF16)

        chunks(rows, add)
    for shift in range(1, chips):
        gate_line(shift).wait_recv()
        gate_core(shift).start()

    def store_in(ref):
        def store(span, value):
            ref[span, :] = value

        return store

    for ring, ref in zip(rings[1:], (sum_y, sum_x)):
        ring.finish(store_in(ref))
    for shift in range(chips):
        gate_core(shift).wait()
    for shift in range(1, chips):
        gate_line(shift).wait_send()
    for number, chosen in enumerate(peers):
        gate_tensor(number, chosen).wait_send()
        gain_copy(number, chosen).wait_send()
        join_copy(number, chosen).wait()
    for number, (shift, turn) in enumerate(others):
        vec_copy(number, shift, turn).wait_send()
    scatter.drain()
    if with_ffn:
        second.drain()
    for ring in rings:
        ring.drain()


def in_vmem(count):
    return [pl.BlockSpec(memory_space=pltpu.VMEM)] * count


def call_kernel(kernel, outs, scratch, number, *operands, far_in=(), far_out=(), cost_us=1):
    vmem = pl.BlockSpec(memory_space=pltpu.VMEM)
    far = pl.BlockSpec(memory_space=pl.ANY)
    return pl.pallas_call(
        kernel,
        out_shape=outs,
        in_specs=[far if i in far_in else vmem for i in range(len(operands))],
        out_specs=tuple(far if i in far_out else vmem for i in range(len(outs))),
        scratch_shapes=scratch,
        cost_estimate=pl.CostEstimate(
            flops=0, bytes_accessed=cost_us * 1_000_000, transcendentals=0
        ),
        compiler_params=pltpu.CompilerParams(
            collective_id=number, has_side_effects=True, vmem_limit_bytes=VMEM_BYTES
        ),
    )(*operands)


def sigmoid(values):
    return 1.0 / (1.0 + jnp.exp(-values))


def one_minus_exp(values):
    series = values / 7.0 + 1.0
    for order in (6.0, 5.0, 4.0, 3.0, 2.0):
        series = 1.0 + series * values / order
    return jnp.where(values > -0.3, -values * series, 1.0 - jnp.exp(values))


GELU_K = 0.7978845608028654
GELU_C = 0.044715


def gelu_parts(values):
    square = values * values
    bent = jnp.tanh(GELU_K * values * (1.0 + GELU_C * square))
    gelu = 0.5 * values * (1.0 + bent)
    slope = 0.5 * (1.0 + bent) + 0.5 * values * (1.0 - bent * bent) * GELU_K * (
        1.0 + 3.0 * GELU_C * square
    )
    return gelu, slope


def gate_terms(gate_a, gate_x, soft, since):
    sig_a = sigmoid(gate_a)
    sig_x = sigmoid(gate_x)
    log_decay = -8.0 * sig_a * soft
    decay = jnp.exp(log_decay)
    scale = jnp.sqrt(one_minus_exp(2.0 * log_decay))
    keep = since > 0.5
    return sig_a, sig_x, decay, jnp.where(keep, scale, 1.0), keep


def scan_down(decay, value, carry):
    place = lax.broadcasted_iota(jnp.int32, decay.shape, 0)
    for shift in (1, 2, 4):
        past = place >= shift
        moved = pltpu.roll(value, shift, 0)
        value = jnp.where(past, decay * moved + value, value)
        decay = jnp.where(past, decay * pltpu.roll(decay, shift, 0), decay)
    return decay * carry + value


def scan_up(decay, value, carry):
    place = lax.broadcasted_iota(jnp.int32, decay.shape, 0)
    factor = jnp.where(place < 7, pltpu.roll(decay, 7, 0), 1.0)
    for shift in (1, 2, 4):
        past = place < 8 - shift
        moved = pltpu.roll(value, 8 - shift, 0)
        value = jnp.where(past, factor * moved + value, value)
        factor = jnp.where(past, factor * pltpu.roll(factor, 8 - shift, 0), factor)
    return factor * carry + value


def forward_scan(conv_rows, gates, branch_y, soft, since, mixed, states, between=()):
    total_rows, width = states.shape

    def step(i, carry):
        row = pl.multiple_of(i * CHUNK, CHUNK)
        span = pl.ds(row, CHUNK)
        values = conv_rows(span).astype(F32)
        kept = []
        for at in range(0, CHUNK, 8):
            tile = pl.ds(row + at, 8)
            sig_a, sig_x, decay, scale, keep = gate_terms(
                gates[tile, :width], gates[tile, width:], soft[...], since[tile, :]
            )
            given = values[at : at + 8] * sig_x * scale
            state = scan_down(jnp.where(keep, decay, 0.0), given, carry)
            carry = state[7:8]
            states[tile, :] = state
            kept.append(state * gelu_parts(branch_y[tile, :])[0])
        mixed[span, :] = jnp.concatenate(kept, axis=0).astype(BF16)
        return carry

    steps, stretches = total_rows // CHUNK, len(between) + 1
    carry = jnp.zeros((1, width), F32)
    for stretch in range(stretches):
        first, last = stretch * steps // stretches, (stretch + 1) * steps // stretches
        carry = lax.fori_loop(first, last, step, carry)
        if stretch < len(between):
            between[stretch]()


def forward_scan_kernel(conv, gates, branch_y, soft, since, mixed, states):
    forward_scan(lambda span: conv[span, :], gates, branch_y, soft, since, mixed, states)


def backward_scan(
    d_mixed, conv_rows, gates, branch_y, states, soft, slope_soft, since, d_conv, d_gates, d_branch, d_decay
):
    total_rows, width = states.shape
    d_decay[...] = jnp.zeros_like(d_decay)

    def step(i, carry):
        row = pl.multiple_of(total_rows - CHUNK - i * CHUNK, CHUNK)
        span = pl.ds(row, CHUNK)
        values = conv_rows(span).astype(F32)
        kept = []
        for at in range(CHUNK - 8, -1, -8):
            tile = pl.ds(row + at, 8)
            soft_row = soft[...]
            sig_a, sig_x, decay, scale, keep = gate_terms(
                gates[tile, :width], gates[tile, width:], soft_row, since[tile, :]
            )
            value = values[at : at + 8]
            gelu, slope = gelu_parts(branch_y[tile, :])
            state = states[tile, :]
            upper = d_mixed[tile, :]
            held = jnp.where(keep, decay, 0.0)
            lam = scan_up(held, upper * gelu, carry)
            carry = held[0:1] * lam[0:1]
            d_conv[tile, :] = lam * sig_x * scale
            d_x = lam * value * scale * sig_x * (1.0 - sig_x)
            given = value * sig_x
            d_log = lam * (state - given * scale - given * decay * decay / scale)
            d_log = jnp.where(keep, d_log, 0.0)
            d_a = d_log * (-8.0 * soft_row) * sig_a * (1.0 - sig_a)
            d_decay[...] += d_log * (-8.0 * sig_a) * slope_soft[...]
            kept.append((d_a, d_x, upper * state * slope))
        kept = kept[::-1]
        d_gates[span, :width] = jnp.concatenate([k[0] for k in kept], axis=0).astype(BF16)
        d_gates[span, width:] = jnp.concatenate([k[1] for k in kept], axis=0).astype(BF16)
        d_branch[span, :] = jnp.concatenate([k[2] for k in kept], axis=0).astype(BF16)
        return carry

    lax.fori_loop(0, total_rows // CHUNK, step, jnp.zeros((1, width), F32))


def backward_scan_kernel(
    d_mixed, conv, gates, branch_y, states, soft, slope_soft, since, d_conv, d_gates, d_branch, d_decay
):
    backward_scan(
        d_mixed,
        lambda span: conv[span, :],
        gates,
        branch_y,
        states,
        soft,
        slope_soft,
        since,
        d_conv,
        d_gates,
        d_branch,
        d_decay,
    )


def times_transposed(left, right):
    return lax.dot_general(left, right, (((1,), (1,)), ((), ())), preferred_element_type=F32)


class HalfBlocks:
    def __init__(self, channels, block):
        self.odd = lax.axis_index("tensor") % 2
        self.half = block // 2
        self.block = block
        self.count = channels // block + 1
        self.channels = channels
        self.own = pl.multiple_of(self.odd * self.half, self.half)
        self.shared = (1 - self.odd) * (self.count - 1)
        self.mine_in_block = pl.multiple_of(self.odd * self.half, self.half)
        self.other_in_block = pl.multiple_of((1 - self.odd) * self.half, self.half)
        self.mine = pl.multiple_of((1 - self.odd) * (channels - self.half), self.half)
        self.pair = {"tensor": lax.axis_index("tensor") + 1 - 2 * self.odd}

    def full(self, index):
        block = index + self.odd
        return block, pl.multiple_of(index * self.block + self.odd * self.half, self.half)

    def span(self, block):
        return pl.ds(pl.multiple_of(block * self.block, self.block), self.block)

    def shared_part(self, start):
        return pl.ds(pl.multiple_of(self.shared * self.block + start, self.half), self.half)


PART = 256


def parts(rows, body):
    def step(i, carry):
        body(pl.ds(pl.multiple_of(i * PART, PART), PART))
        return carry

    lax.fori_loop(0, rows // PART, step, 0)


def recurrence_kernel(
    taps,
    nbits,
    branch_x,
    branch_y,
    tap_rows,
    soft,
    since,
    weights,
    cot,
    w_out,
    mixed,
    states,
    window,
    gates,
    cot_all,
    wout_all,
    send,
    recv,
    *sems,
):
    total_rows, width = states.shape
    block = weights.shape[2]
    place = HalfBlocks(width, block)
    greet_peers(nbits, False, False)
    fetch = Fetch(nbits, cot, w_out, cot_all, wout_all, *sems)
    fetch.begin()

    def conv(i, before):
        row = pl.multiple_of(i * CHUNK, CHUNK)
        kept = []
        for at in range(0, CHUNK, 8):
            tile = pl.ds(row + at, 8)
            values = branch_x[tile, :]
            line = lax.broadcasted_iota(jnp.int32, values.shape, 0)
            total = values * tap_rows[0:1, :]
            for tap in range(1, taps):
                moved = jnp.where(
                    line < tap, pltpu.roll(before, tap, 0), pltpu.roll(values, tap, 0)
                )
                moved = jnp.where(since[tile, :] > tap - 0.5, moved, 0.0)
                total = total + moved * tap_rows[tap : tap + 1, :]
            kept.append(total)
            before = values
        window[pl.ds(row, CHUNK), pl.ds(place.own, width)] = jnp.concatenate(
            kept, axis=0
        ).astype(BF16)
        return before

    lax.fori_loop(0, total_rows // CHUNK, conv, jnp.zeros((8, width), F32))
    source = window.at[:, place.shared_part(place.mine_in_block)]
    away = pl.multiple_of(place.odd * (place.count - 1) * block + place.mine_in_block, place.half)
    rim = pltpu.make_async_remote_copy(
        src_ref=source,
        dst_ref=window.at[:, pl.ds(away, place.half)],
        send_sem=send.at[0],
        recv_sem=recv.at[0],
        device_id=place.pair,
        device_id_type=MESH,
    )
    rim.start()

    def full(span):
        for index in range(place.count - 1):
            number, at = place.full(index)
            cells = window[span, place.span(number)]
            for s in range(2):
                gates[span, pl.ds(s * width + at, block)] = jnp.dot(
                    cells, weights[s, number], preferred_element_type=F32
                )

    parts(total_rows, full)
    rim.wait()

    def shared(span):
        cells = window[span, place.span(place.shared)]
        for s in range(2):
            gates[span, pl.ds(s * width + place.mine, place.half)] = jnp.dot(
                cells,
                weights[s, place.shared, :, pl.ds(place.mine_in_block, place.half)],
                preferred_element_type=F32,
            )

    parts(total_rows, shared)
    forward_scan(
        lambda span: window[span, pl.ds(place.own, width)],
        gates,
        branch_y,
        soft,
        since,
        mixed,
        states,
        [partial(fetch.advance, part) for part in range(3)],
    )
    fetch.finish()


def recurrence_back_kernel(
    taps,
    d_mixed,
    window,
    gates,
    branch_y,
    branch_x,
    states,
    tap_rows,
    soft,
    slope_soft,
    since,
    weights,
    d_branch_y,
    d_branch_x,
    gate_grad,
    own_small,
    d_conv,
    d_gates,
    given,
    taken,
    sums,
    send,
    recv,
):
    total_rows, width = states.shape
    block = weights.shape[2]
    place = HalfBlocks(width, block)
    half = place.half
    barrier = pltpu.get_barrier_semaphore()
    pl.semaphore_signal(barrier, inc=1, device_id=place.pair, device_id_type=MESH)
    backward_scan(
        d_mixed,
        lambda span: window[span, pl.ds(place.own, width)],
        gates,
        branch_y,
        states,
        soft,
        slope_soft,
        since,
        d_conv,
        d_gates,
        d_branch_y,
        sums.at[taps],
    )

    def to_pair(span):
        total = jnp.zeros((PART, half), F32)
        for s in range(2):
            total = total + times_transposed(
                d_gates[span, pl.ds(s * width + place.mine, half)],
                weights[
                    s,
                    place.shared,
                    pl.ds(place.other_in_block, half),
                    pl.ds(place.mine_in_block, half),
                ],
            )
        given[span, :] = total.astype(BF16)

    parts(total_rows, to_pair)
    pl.semaphore_wait(barrier, 1)
    rim = pltpu.make_async_remote_copy(
        src_ref=given,
        dst_ref=taken,
        send_sem=send.at[0],
        recv_sem=recv.at[0],
        device_id=place.pair,
        device_id_type=MESH,
    )
    rim.start()

    def full(span):
        for index in range(place.count - 1):
            number, at = place.full(index)
            total = d_conv[span, pl.ds(at, block)]
            for s in range(2):
                total = total + times_transposed(
                    d_gates[span, pl.ds(s * width + at, block)], weights[s, number]
                )
            d_conv[span, pl.ds(at, block)] = total
        total = d_conv[span, pl.ds(place.mine, half)]
        for s in range(2):
            total = total + times_transposed(
                d_gates[span, pl.ds(s * width + place.mine, half)],
                weights[
                    s,
                    place.shared,
                    pl.ds(place.mine_in_block, half),
                    pl.ds(place.mine_in_block, half),
                ],
            )
        d_conv[span, pl.ds(place.mine, half)] = total

    parts(total_rows, full)
    units = width // half
    for index in range(units):
        number = (index + place.odd) // 2
        cells = window[:, place.span(number)]
        both = jnp.concatenate(
            [d_gates[:, s * width + index * half : s * width + (index + 1) * half] for s in range(2)],
            axis=1,
        )
        found = lax.dot_general(
            cells, both, (((0,), (0,)), ((), ())), preferred_element_type=F32
        ).astype(BF16)
        gate_grad[2 * index] = found[:, :half]
        gate_grad[2 * index + 1] = found[:, half:]
    rim.wait()

    def add(span):
        d_conv[span, pl.ds(place.mine, half)] += taken[span, :].astype(F32)

    parts(total_rows, add)
    for tap in range(taps):
        sums[tap] = jnp.zeros((8, width), F32)

    def conv(i, after):
        row = pl.multiple_of(total_rows - CHUNK - i * CHUNK, CHUNK)
        kept = []
        for at in range(CHUNK - 8, -1, -8):
            tile = pl.ds(row + at, 8)
            values = d_conv[tile, :]
            line = lax.broadcasted_iota(jnp.int32, values.shape, 0)
            below = branch_x[tile, :]
            higher = pl.multiple_of((row + at - 8 + total_rows) % total_rows, 8)
            above = branch_x[pl.ds(higher, 8), :]
            total = values * tap_rows[0:1, :]
            sums[0] += values * below
            masked = []
            for tap in range(1, taps):
                here = jnp.where(since[tile, :] > tap - 0.5, values, 0.0)
                masked.append(here)
                moved = jnp.where(
                    line < 8 - tap,
                    pltpu.roll(here, 8 - tap, 0),
                    pltpu.roll(after[tap - 1], 8 - tap, 0),
                )
                total = total + moved * tap_rows[tap : tap + 1, :]
                source = jnp.where(
                    line < tap, pltpu.roll(above, tap, 0), pltpu.roll(below, tap, 0)
                )
                sums[tap] += here * source
            after = tuple(masked)
            kept.append(total)
        d_branch_x[pl.ds(row, CHUNK), :] = jnp.concatenate(kept[::-1], axis=0).astype(BF16)
        return after

    none = jnp.zeros((8, width), F32)
    lax.fori_loop(0, total_rows // CHUNK, conv, (none,) * (taps - 1))
    line = lax.broadcasted_iota(jnp.int32, (8, width), 0)
    total = jnp.zeros((8, width), F32)
    for tap in range(taps + 1):
        row = jnp.sum(sums[tap], axis=0, keepdims=True)
        total = jnp.where(line == tap, row, total)
    own_small[...] = total


def gate_layout_kernel(parts_in, whole):
    for piece in range(parts_in.shape[1]):
        for s in range(2):
            whole[s, 0, :, piece * 128 : (piece + 1) * 128] = parts_in[0, piece, s].astype(F32)


def gate_layout(parts_in):
    blocks, pieces, _, block, unit = parts_in.shape
    if unit != 128:
        whole = parts_in.transpose(2, 0, 3, 1, 4).reshape(2, blocks, block, block)
        return whole.astype(F32)
    return pl.pallas_call(
        gate_layout_kernel,
        grid=(blocks,),
        out_shape=jax.ShapeDtypeStruct((2, blocks, block, block), F32),
        in_specs=[pl.BlockSpec((1, pieces, 2, block, unit), lambda n: (n, 0, 0, 0, 0))],
        out_specs=pl.BlockSpec((2, 1, block, block), lambda n: (0, n, 0, 0)),
    )(parts_in)


def scan_call(kernel, outs, *operands):
    return pl.pallas_call(
        kernel,
        out_shape=outs,
        in_specs=in_vmem(len(operands)),
        out_specs=tuple(in_vmem(len(outs))),
        compiler_params=pltpu.CompilerParams(vmem_limit_bytes=VMEM_BYTES),
    )(*operands)


class Rim:
    def __init__(self, route, back, source, first, width, room):
        self.route, self.back = route, back
        self.source, self.first, self.width = source, first, width
        self.room = room

    def fetch(self, values):
        part = lax.dynamic_slice_in_dim(values, self.source, self.width, 1)
        return lax.ppermute(part, "tensor", self.route)

    def give(self, part):
        return lax.ppermute(part, "tensor", self.back)

    def add(self, values, part):
        zeros = jnp.zeros(values.shape, F32)
        return values + lax.dynamic_update_slice_in_dim(
            zeros, part.astype(F32), self.source, 1
        )

    def window(self, channels):
        return (channels // self.width + 4) * self.width


def gate_rims(channels, block_size, ntensor, offset):
    up = [(i, i + 1) for i in range(ntensor - 1)]
    down = [(i + 1, i) for i in range(ntensor - 1)]
    last = jnp.int32(channels - block_size)
    return [
        Rim(up, down, last, offset - block_size, block_size, block_size),
        Rim(down, up, jnp.int32(0), offset + channels, block_size, block_size),
    ]


def same_block(first, count, offset, channels, block_size):
    rows = (first + jnp.arange(count, dtype=jnp.int32))[:, None]
    columns = (offset + jnp.arange(channels, dtype=jnp.int32))[None, :]
    return (rows + block_size) // block_size == (columns + block_size) // block_size


def gate_dense(gate_w, offset, first, count):
    block_size = gate_w.shape[2]
    total = gate_w.shape[1] * block_size
    channels = total // lax.axis_size("tensor")
    columns = gate_w.transpose(2, 0, 1, 3).reshape(block_size, 2, total)
    columns = lax.dynamic_slice_in_dim(columns, offset, channels, 2)
    copies = -(-count // block_size) + 1
    tall = jnp.concatenate([columns] * copies, axis=0)
    tall = lax.dynamic_slice_in_dim(tall, (first + block_size) % block_size, count, 0)
    same = same_block(first, count, offset, channels, block_size)
    dense = jnp.where(same[:, None, :], tall, jnp.zeros_like(tall))
    return dense.reshape(count, 2 * channels)


def doc_starts(seg_ids, seq_len):
    places = jnp.arange(seg_ids.shape[0], dtype=jnp.int32)
    before = jnp.concatenate([seg_ids[:1], seg_ids[:-1]])
    resets = (places % seq_len == 0) | (seg_ids != before)
    starts = lax.cummax(jnp.where(resets, places, jnp.zeros_like(places)), axis=0)
    return starts


def causal_conv(starts, values, kernel):
    places = jnp.arange(values.shape[0], dtype=jnp.int32)
    total = values * kernel[0]
    for offset_k in range(1, kernel.shape[0]):
        moved = jnp.concatenate(
            [jnp.zeros((offset_k, values.shape[1]), values.dtype), values[:-offset_k]], axis=0
        )
        valid = (places - offset_k >= starts)[:, None]
        total = total + jnp.where(valid, moved, jnp.zeros_like(moved)) * kernel[offset_k]
    return total


def geglu(gate_val, up_val):
    return jax.nn.gelu(gate_val, approximate=True) * up_val


def rows_times(left, right):
    return lax.dot_general(left, right, (((1,), (1,)), ((), ())), preferred_element_type=F32)


def rows_back(lefts, rights):
    total = rows_times(lefts[0], rights[0])
    return total + rows_times(lefts[1], rights[1])


def inner_rows(left, right):
    return lax.dot_general(left, right, (((0,), (0,)), ((), ())), preferred_element_type=F32)


def halved(grad, ndp):
    return grad.reshape(ndp // 2, 2, grad.shape[0] // ndp, grad.shape[1])


def body(
    tokens,
    segments,
    cotangent,
    norm_gain,
    w_y,
    w_x,
    conv_w,
    gate_w,
    decay_param,
    w_out,
    mlp_gain,
    w_gate,
    w_up,
    w_down,
):
    ntensor = lax.axis_size("tensor")
    ndp = lax.axis_size("dp")
    nbits = log2_of(ntensor)
    tindex = lax.axis_index("tensor")
    own_rows, width = tokens.shape
    group_rows = own_rows * ntensor
    block_size = gate_w.shape[2]
    nblocks = gate_w.shape[1]
    dp_rows, channels = w_y.shape
    taps = conv_w.shape[0]
    offset = tindex * channels
    shape = jax.ShapeDtypeStruct
    gain_in = norm_gain.reshape(1, width)
    gain_mid = mlp_gain.reshape(1, width)
    seg_rows_of = own_rows // 128
    normed_rows, seg_all, wy_loc, wx_loc = call_kernel(
        partial(enter_kernel, nbits),
        (
            shape((group_rows, width), BF16),
            shape((ntensor, seg_rows_of, 128), jnp.int32),
        )
        + (shape((dp_rows * ndp, channels), BF16),) * 2,
        gather_sems(nbits)
        + [pltpu.SemaphoreType.DMA((ntensor - 1,)), pltpu.SemaphoreType.DMA((ntensor - 1,))]
        + [pltpu.SemaphoreType.DMA((1,))]
        + line_sems(ndp) * 2,
        0,
        tokens,
        segments.reshape(seg_rows_of, 128),
        gain_in,
        w_y,
        w_x,
        far_in=(3, 4),
        far_out=(2, 3),
    )
    w_gate, w_up, w_down, normed_rows = lax.optimization_barrier(
        (w_gate, w_up, w_down, normed_rows)
    )
    wg_loc = lax.all_gather(w_gate, "dp", axis=0, tiled=True)
    wu_loc = lax.all_gather(w_up, "dp", axis=0, tiled=True)
    wd_loc = lax.all_gather(w_down, "dp", axis=0, tiled=True)
    seg_rows = seg_all.reshape(group_rows)
    starts = doc_starts(seg_rows, group_rows)
    conv_loc = lax.dynamic_slice_in_dim(conv_w, offset, channels, 1)
    decay_loc = lax.dynamic_slice_in_dim(decay_param, offset, channels, 0).reshape(1, channels)
    soft = jax.nn.softplus(decay_loc)
    slope_soft = jax.nn.sigmoid(decay_loc)
    half_blocks = (
        channels % block_size == block_size // 2 and ntensor % 2 == 0 and block_size % 256 == 0
    )
    since = (jnp.arange(group_rows, dtype=jnp.int32) - starts).astype(F32)[:, None]
    branch_x = jnp.dot(normed_rows, wx_loc, preferred_element_type=F32)
    branch_y = jnp.dot(normed_rows, wy_loc, preferred_element_type=F32)
    if half_blocks:
        span_blocks = channels // block_size + 1
        w_window = lax.dynamic_slice_in_dim(gate_w, offset // block_size, span_blocks, 1)
        taps_pad = jnp.concatenate([conv_loc, jnp.zeros((8 - taps, channels), F32)], axis=0)
        mixed_low, states, window, gate_pre, cot_rows, wout_loc = call_kernel(
            partial(recurrence_kernel, taps, nbits),
            (
                shape((group_rows, channels), BF16),
                shape((group_rows, channels), F32),
                shape((group_rows, span_blocks * block_size), BF16),
                shape((group_rows, 2 * channels), F32),
                shape((group_rows, width), BF16),
                shape((dp_rows * ndp, channels), BF16),
            ),
            [pltpu.SemaphoreType.DMA((1,)), pltpu.SemaphoreType.DMA((1,))]
            + fetch_scratch(nbits, ndp),
            5,
            branch_x,
            branch_y,
            taps_pad,
            soft,
            since,
            w_window,
            cotangent,
            w_out,
            far_in=(7,),
            far_out=(5,),
        )
    else:
        cot_rows, wout_loc = call_kernel(
            partial(fetch_kernel, nbits),
            (
                shape((group_rows, width), BF16),
                shape((dp_rows * ndp, channels), BF16),
            ),
            fetch_scratch(nbits, ndp),
            5,
            cotangent,
            w_out,
            far_in=(1,),
            far_out=(1,),
        )
        rims = gate_rims(channels, block_size, ntensor, offset)
        own_dense = gate_dense(gate_w, offset, offset, channels)
        rim_dense = [gate_dense(gate_w, offset, rim.first, rim.width) for rim in rims]
        conv_out, conv_pull = jax.vjp(partial(causal_conv, starts), branch_x, conv_loc)
        conv_low = conv_out.astype(BF16)
        rim_cells = [rim.fetch(conv_low) for rim in rims]
        gate_pre = jnp.dot(conv_low, own_dense, preferred_element_type=F32)
        for cells, dense in zip(rim_cells, rim_dense):
            gate_pre = gate_pre + jnp.dot(cells, dense, preferred_element_type=F32)
        mixed_low, states = scan_call(
            forward_scan_kernel,
            (shape((group_rows, channels), BF16), shape((group_rows, channels), F32)),
            conv_low,
            gate_pre,
            branch_y,
            soft,
            since,
        )
    middle, mid_rows = call_kernel(
        partial(middle_kernel, nbits),
        (shape((own_rows, width), F32), shape((group_rows, width), BF16)),
        scatter_scratch(own_rows, width, nbits) + gather_sems(nbits),
        1,
        rows_times(mixed_low, wout_loc).astype(BF16),
        tokens,
        gain_mid,
    )
    gate_val = jnp.dot(mid_rows, wg_loc, preferred_element_type=F32)
    up_val = jnp.dot(mid_rows, wu_loc, preferred_element_type=F32)
    hidden, act_pull = jax.vjp(geglu, gate_val, up_val)
    hidden_low = hidden.astype(BF16)
    grad_wd = inner_rows(cot_rows, hidden_low).astype(BF16)
    units = w_down.shape[1]
    pieces = 3 if units % 384 == 0 else 1
    (sum_wd,) = call_kernel(
        partial(sum_kernel, pieces),
        (shape((dp_rows, units), F32),),
        line_scratch(ndp, dp_rows, units // pieces) * pieces,
        7,
        halved(grad_wd, ndp),
        far_in=(0,),
    )
    sum_wd, wd_loc = lax.optimization_barrier((sum_wd, wd_loc))
    d_hidden = jnp.dot(cot_rows, wd_loc, preferred_element_type=F32)
    d_gate, d_up = act_pull(d_hidden)
    d_gate = d_gate.astype(BF16)
    d_up = d_up.astype(BF16)
    grad_wg = inner_rows(mid_rows, d_gate).astype(BF16)
    sum_wg = lax.psum_scatter(grad_wg, "dp", scatter_dimension=0, tiled=True)
    grad_wu = inner_rows(mid_rows, d_up).astype(BF16)
    sum_wu = lax.psum_scatter(grad_wu, "dp", scatter_dimension=0, tiled=True)
    d_gate, d_up, grad_wg, grad_wu = lax.optimization_barrier((d_gate, d_up, grad_wg, grad_wu))
    d_mid_part = rows_back((d_gate, d_up), (wg_loc, wu_loc)).astype(BF16)
    d_middle, d_mixer, d_gain_mid = call_kernel(
        partial(turn_kernel, nbits),
        (
            shape((own_rows, width), F32),
            shape((group_rows, width), BF16),
            shape((8, width), F32),
        ),
        scatter_scratch(own_rows, width, nbits) + gather_sems(nbits),
        2,
        d_mid_part,
        cotangent,
        middle,
        gain_mid,
    )
    d_mixer, sum_wg = lax.optimization_barrier((d_mixer, sum_wg))
    d_mixed_in = jnp.dot(d_mixer, wout_loc, preferred_element_type=F32)
    unit = math.gcd(channels, block_size)
    if half_blocks:
        d_branch_y, d_branch_x, gate_grad, own_small = call_kernel(
            partial(recurrence_back_kernel, taps),
            (
                shape((group_rows, channels), BF16),
                shape((group_rows, channels), BF16),
                shape((channels // unit * 2, block_size, unit), BF16),
                shape((8, channels), F32),
            ),
            [
                pltpu.VMEM((group_rows, channels), F32),
                pltpu.VMEM((group_rows, 2 * channels), BF16),
                pltpu.VMEM((group_rows, unit), BF16),
                pltpu.VMEM((group_rows, unit), BF16),
                pltpu.VMEM((taps + 1, 8, channels), F32),
                pltpu.SemaphoreType.DMA((1,)),
                pltpu.SemaphoreType.DMA((1,)),
            ],
            6,
            d_mixed_in,
            window,
            gate_pre,
            branch_y,
            branch_x,
            states,
            taps_pad,
            soft,
            slope_soft,
            since,
            w_window,
        )
        gate_grad = gate_grad.reshape(channels // unit * 2 * block_size, unit)
    else:
        d_conv, d_gate_low, d_branch_y, d_decay = scan_call(
            backward_scan_kernel,
            (
                shape((group_rows, channels), F32),
                shape((group_rows, 2 * channels), BF16),
                shape((group_rows, channels), BF16),
                shape((8, channels), F32),
            ),
            d_mixed_in,
            conv_low,
            gate_pre,
            branch_y,
            states,
            soft,
            slope_soft,
            since,
        )
        given = [rows_times(d_gate_low, dense).astype(BF16) for dense in rim_dense]
        taken = [rim.give(part) for rim, part in zip(rims, given)]
        d_conv_out = d_conv + rows_times(d_gate_low, own_dense)
        for rim, part in zip(rims, taken):
            d_conv_out = rim.add(d_conv_out, part)
        d_branch_x, grad_conv_loc = conv_pull(d_conv_out)
        d_branch_x = d_branch_x.astype(BF16)
        base = offset // block_size * block_size - rims[0].room
        window_rows = rims[0].window(channels)
        picked = jnp.zeros((window_rows, 2 * channels), F32)
        for first, cells in [(offset, conv_low)] + [(r.first, c) for r, c in zip(rims, rim_cells)]:
            part = inner_rows(cells, d_gate_low)
            same = same_block(first, cells.shape[1], offset, channels, block_size)
            part = jnp.where(jnp.concatenate([same, same], axis=1), part, 0.0)
            picked = lax.dynamic_update_slice(picked, part, (first - base, jnp.int32(0)))
        picked = picked.reshape(window_rows // block_size, block_size, 2, channels // unit, unit)
        gate_grad = picked.sum(axis=0).astype(BF16).transpose(2, 1, 0, 3)
        gate_grad = gate_grad.reshape(channels // unit * 2 * block_size, unit)
        own_small = jnp.concatenate(
            [
                grad_conv_loc,
                jnp.sum(d_decay, axis=0, keepdims=True),
                jnp.zeros((7 - taps, channels), F32),
            ],
            axis=0,
        )

    grad_wout = inner_rows(d_mixer, mixed_low).astype(BF16)
    sum_wout = lax.psum_scatter(grad_wout, "dp", scatter_dimension=0, tiled=True)
    grad_wy = inner_rows(normed_rows, d_branch_y).astype(BF16)
    grad_wx = inner_rows(normed_rows, d_branch_x).astype(BF16)
    ffn_part = rows_times(hidden_low, wd_loc).astype(BF16)
    d_normed = rows_back((d_branch_y, d_branch_x), (wy_loc, wx_loc)).astype(BF16)
    d_normed, sum_wu = lax.optimization_barrier((d_normed, sum_wu))
    merged = nbits <= 2

    pieces = [halved(grad, ndp) for grad in (gate_grad, grad_wy, grad_wx)]
    peers = ntensor - 1
    gate_rows = gate_grad.shape[0] // ndp
    dma = pltpu.SemaphoreType.DMA
    scratch = scatter_scratch(own_rows, width, nbits)
    for piece in pieces:
        scratch += line_scratch(ndp, piece.shape[2], piece.shape[3])
    scratch += [
        pltpu.VMEM((8, width), F32),
        pltpu.VMEM((ntensor, 8, channels), F32),
        pltpu.VMEM((peers, 8, channels), F32),
        pltpu.VMEM((8, channels), F32),
        pltpu.VMEM((ndp - 1, 8, channels), F32),
    ]
    scratch += [dma((peers,)), dma((peers,)), dma((ndp - 1,)), dma((ndp - 1,))]
    scratch += [dma((peers,)), dma((peers,)), dma((peers + ndp,)), dma((peers + ndp,))]
    if merged:
        scratch += scatter_scratch(own_rows, width, nbits)
    found = call_kernel(
        partial(leave_kernel, nbits, merged),
        (shape((own_rows, width), F32),)
        + (shape((dp_rows, channels), F32),) * 2
        + (
            shape((ntensor, ndp, gate_rows, unit), BF16),
            shape((ntensor, 8, channels), F32),
        )
        + ((shape((own_rows, width), BF16),) if merged else ()),
        scratch,
        3,
        d_normed,
        tokens,
        d_middle,
        gain_in,
        own_small,
        d_gain_mid,
        *pieces,
        *((ffn_part, middle) if merged else ()),
        far_in=(6, 7, 8),
    )
    grad_input, sum_wy, sum_wx, gate_all, small_all = found[:5]
    if merged:
        mixed = found[5]
    else:
        (mixed,) = call_kernel(
            partial(result_kernel, nbits),
            (shape((own_rows, width), BF16),),
            scatter_scratch(own_rows, width, nbits),
            4,
            ffn_part,
            middle,
        )
    per_block = block_size // unit
    sum_gate = gate_all.reshape(nblocks, per_block, 2, block_size, unit)
    sum_gate = gate_layout(sum_gate)
    summed = small_all.transpose(1, 0, 2).reshape(8, width)
    return (
        mixed,
        grad_input,
        summed[6],
        sum_wy,
        sum_wx,
        summed[:taps],
        sum_gate,
        summed[taps],
        sum_wout.astype(F32),
        summed[7],
        sum_wg.astype(F32),
        sum_wu.astype(F32),
        sum_wd,
    )


def solution(mesh):
    split = P(("dp", "tensor"), None)
    weight = P("dp", "tensor")
    return jax.shard_map(
        body,
        mesh=mesh,
        in_specs=(
            split,
            P(("dp", "tensor")),
            split,
            P(),
            weight,
            weight,
            P(),
            P(),
            P(),
            weight,
            P(),
            weight,
            weight,
            weight,
        ),
        out_specs=(
            split,
            split,
            P(),
            weight,
            weight,
            P(),
            P(),
            P(),
            weight,
            P(),
            weight,
            weight,
            weight,
        ),
        check_vma=False,
    )
```

```python
import math
from functools import partial

import jax
import jax.numpy as jnp
from jax import lax
from jax.experimental import pallas as pl
from jax.experimental.pallas import tpu as pltpu
from jax.sharding import PartitionSpec as P

EPSILON = 1e-06
MESH = pl.DeviceIdType.MESH
VMEM_BYTES = 56 * 1024 * 1024
CHUNK = 16
F32 = jnp.float32
BF16 = jnp.bfloat16


def subsets(bits):
    found = [()]
    for bit in bits:
        found = found + [chosen + (bit,) for chosen in found]
    return found


def flipped(index, bits):
    for bit in bits:
        mine = (index // (1 << bit)) % 2
        index = index + (1 - 2 * mine) * (1 << bit)
    return index


def log2_of(count):
    assert count & (count - 1) == 0
    return count.bit_length() - 1


def greet(axis_bits):
    barrier = pltpu.get_barrier_semaphore()
    for axis, bit in axis_bits:
        peer = flipped(lax.axis_index(axis), (bit,))
        pl.semaphore_signal(barrier, inc=1, device_id={axis: peer}, device_id_type=MESH)
    pl.semaphore_wait(barrier, len(axis_bits))


def halves_of(nbits, columns):
    half = columns // 2
    ups = tuple(range(nbits))
    return ((ups, 0, half), (ups[::-1], half, half))


class Gather:
    def __init__(self, ref, rows, nbits, send_sems, recv_sems):
        self.ref, self.rows, self.nbits = ref, rows, nbits
        self.sems = (send_sems, recv_sems)
        self.me = lax.axis_index("tensor")
        self.plan = []
        number = 0
        for half, (order, at, width) in enumerate(halves_of(nbits, ref.shape[1])):
            for step, bit in enumerate(order):
                for known in subsets(order[:step]):
                    self.plan.append((half, step, known, bit, at, width, number))
                    number += 1
        self.count = number

    def copy(self, item):
        half, step, known, bit, at, width, number = item
        row = pl.multiple_of(flipped(self.me, known) * self.rows, self.rows)
        piece = self.ref.at[pl.ds(row, self.rows), pl.ds(at, width)]
        return pltpu.make_async_remote_copy(
            src_ref=piece,
            dst_ref=piece,
            send_sem=self.sems[0].at[number],
            recv_sem=self.sems[1].at[number],
            device_id={"tensor": flipped(self.me, (bit,))},
            device_id_type=MESH,
        )

    def begin(self):
        for item in sorted(self.plan, key=lambda it: it[1]):
            if item[2] == ():
                self.copy(item).start()

    def advance(self, step):
        for item in self.plan:
            half, at_step, known, bit, at, width, number = item
            if at_step == step:
                self.copy(item).wait_recv()
                block = known + (bit,)
                for later in self.plan:
                    if later[0] == half and set(later[2]) == set(block):
                        self.copy(later).start()

    def finish(self, step=0):
        for at_step in range(step, self.nbits):
            self.advance(at_step)
        for item in self.plan:
            self.copy(item).wait_send()


def gather_copies(nbits):
    return 2 * ((1 << nbits) - 1)


class Scatter:
    def __init__(self, ref, landed, staged, rows, nbits, send_sems, recv_sems):
        self.ref, self.landed, self.staged = ref, landed, staged
        self.rows, self.nbits = rows, nbits
        self.sems = (send_sems, recv_sems)
        self.me = lax.axis_index("tensor")
        self.plan, self.slot = [], {}
        number = 0
        for half, (order, at, width) in enumerate(halves_of(nbits, ref.shape[1])):
            for step, bit in enumerate(order):
                for rest in subsets(order[step + 1 :])[::-1]:
                    self.plan.append((half, step, rest, bit, at, width, number))
                    if step > 0:
                        self.slot[number] = len(self.slot)
                    number += 1

    def copy(self, item):
        half, step, rest, bit, at, width, number = item
        if step == 0:
            row = pl.multiple_of(flipped(self.me, rest + (bit,)) * self.rows, self.rows)
            source = self.ref.at[pl.ds(row, self.rows), pl.ds(at, width)]
        else:
            source = self.staged.at[self.slot[number]]
        return pltpu.make_async_remote_copy(
            src_ref=source,
            dst_ref=self.landed.at[number],
            send_sem=self.sems[0].at[number],
            recv_sem=self.sems[1].at[number],
            device_id={"tensor": flipped(self.me, (bit,))},
            device_id_type=MESH,
        )

    def begin(self):
        for item in sorted(self.plan, key=lambda it: (len(it[2]) == 0)):
            if item[1] == 0:
                self.copy(item).start()

    def partial_sum(self, half, block, before, row, size):
        at, width = halves_of(self.nbits, self.ref.shape[1])[half][1:]
        base = pl.multiple_of(flipped(self.me, block) * self.rows + row, size)
        total = self.ref[pl.ds(base, size), pl.ds(at, width)].astype(F32)
        for it in self.plan:
            if it[0] == half and it[1] < before and set(it[2]) == set(block):
                total = total + self.landed[it[6], pl.ds(row, size), :].astype(F32)
        return total

    def advance(self, step):
        for half in range(2):
            for item in self.plan:
                if item[0] == half and item[1] == step:
                    self.copy(item).wait_recv()
            for item in self.plan:
                if item[0] == half and item[1] == step + 1:

                    def fill(row, item=item):
                        value = self.partial_sum(
                            item[0], item[2] + (item[3],), item[1], row, CHUNK
                        )
                        where = (self.slot[item[6]], pl.ds(row, CHUNK))
                        self.staged[where + (slice(None),)] = value.astype(BF16)

                    chunks(self.rows, fill)
                    self.copy(item).start()

    def run(self):
        for step in range(self.nbits):
            self.advance(step)

    def total(self, row, size):
        return jnp.concatenate(
            [self.partial_sum(half, (), self.nbits, row, size) for half in range(2)], axis=1
        )

    def drain(self):
        for item in self.plan:
            self.copy(item).wait_send()


def scatter_scratch(rows, columns, nbits):
    copies = gather_copies(nbits)
    later = max(1, copies - (1 << nbits))
    return [
        pltpu.VMEM((copies, rows, columns // 2), BF16),
        pltpu.VMEM((later, rows, columns // 2), BF16),
        pltpu.SemaphoreType.DMA((copies,)),
        pltpu.SemaphoreType.DMA((copies,)),
    ]


def gather_sems(nbits):
    copies = gather_copies(nbits)
    return [pltpu.SemaphoreType.DMA((copies,)), pltpu.SemaphoreType.DMA((copies,))]


def tensor_bits(nbits):
    return [("tensor", bit) for bit in range(nbits)]


def rms_scale_of(values):
    return lax.rsqrt(jnp.mean(values * values, axis=-1, keepdims=True) + EPSILON)


def chunks(rows, body):
    def step(i, carry):
        body(pl.multiple_of(i * CHUNK, CHUNK))
        return carry

    lax.fori_loop(0, rows // CHUNK, step, 0)


def own_row(row, rows):
    return pl.multiple_of(lax.axis_index("tensor") * rows + row, CHUNK)


def dp_place():
    me = lax.axis_index("dp")
    return me // 2, me % 2, lax.axis_size("dp") // 2


def dp_index(chip, core):
    return chip * 2 + core


UP, DOWN = 1, -1


class LineGather:
    def __init__(self, own, whole, send_sems, recv_sems, columns=None):
        self.own, self.whole = own, whole
        self.sems = (send_sems, recv_sems)
        self.chip, self.core, self.chips = dp_place()
        self.rows = own.shape[0]
        self.columns = slice(None) if columns is None else columns

    def block(self, chip):
        row = pl.multiple_of(dp_index(chip, self.core) * self.rows, self.rows)
        return self.whole.at[pl.ds(row, self.rows), self.columns]

    def has(self, way, distance):
        return self.chip >= distance if way == UP else self.chip + distance < self.chips

    def number(self, way, distance):
        return (0 if way == UP else self.chips) + distance

    def along(self, way, distance):
        block = self.block(self.chip - way * distance)
        return pltpu.make_async_remote_copy(
            src_ref=self.own if distance == 0 else block,
            dst_ref=block,
            send_sem=self.sems[0].at[self.number(way, distance)],
            recv_sem=self.sems[1].at[self.number(way, distance + 1)],
            device_id={"dp": dp_index(self.chip + way, self.core)},
            device_id_type=MESH,
        )

    def arrival(self, way, distance):
        block = self.block(self.chip - way * distance)
        return pltpu.make_async_remote_copy(
            src_ref=block,
            dst_ref=block,
            send_sem=self.sems[0].at[self.number(way, distance)],
            recv_sem=self.sems[1].at[self.number(way, distance)],
            device_id={"dp": dp_index(self.chip + way, self.core)},
            device_id_type=MESH,
        )

    def across(self, way, distance):
        block = self.block(self.chip - way * distance)
        number = 2 * self.chips + self.number(way, distance)
        return pltpu.make_async_remote_copy(
            src_ref=self.own if distance == 0 else block,
            dst_ref=block,
            send_sem=self.sems[0].at[number],
            recv_sem=self.sems[1].at[number],
            device_id={"dp": dp_index(self.chip, 1 - self.core)},
            device_id_type=MESH,
        )

    def local(self):
        return pltpu.make_async_copy(
            self.own, self.block(self.chip), self.sems[0].at[4 * self.chips]
        )

    def begin(self):
        for way in (UP, DOWN):

            @pl.when(self.has(-way, 1))
            def _(way=way):
                self.along(way, 0).start()

        self.across(UP, 0).start()
        self.local().start()

    def pass_on(self, distance):
        for way in (UP, DOWN):

            @pl.when(self.has(way, distance))
            def _(way=way):
                self.arrival(way, distance).wait_recv()

                @pl.when(self.has(-way, 1))
                def _():
                    self.along(way, distance).start()

                self.across(way, distance).start()

    def finish(self):
        self.across(UP, 0).wait()
        self.local().wait()
        for way in (UP, DOWN):
            for distance in range(self.chips):

                @pl.when(self.has(way, distance) & self.has(-way, 1))
                def _(way=way, distance=distance):
                    self.along(way, distance).wait_send()

                if distance:

                    @pl.when(self.has(way, distance))
                    def _(way=way, distance=distance):
                        self.across(way, distance).wait()


def line_sems(ndp):
    chips = ndp // 2
    return [pltpu.SemaphoreType.DMA((4 * chips + 1,)), pltpu.SemaphoreType.DMA((4 * chips + 1,))]


def greet_peers(nbits, all_tensor, whole_dp):
    me = lax.axis_index("tensor")
    chip, core, chips = dp_place()
    barrier = pltpu.get_barrier_semaphore()

    def signal(target):
        pl.semaphore_signal(barrier, inc=1, device_id=target, device_id_type=MESH)

    met = 0
    for chosen in subsets(tuple(range(nbits))):
        if chosen and (all_tensor or len(chosen) == 1):
            signal({"tensor": flipped(me, chosen)})
            met += 1
    if whole_dp:
        for shift in range(chips):
            for turn in range(2):
                if (shift, turn) != (0, 0):
                    other = dp_index((chip + shift) % chips, core + turn * (1 - 2 * core))
                    signal({"dp": other})
                    met += 1
    else:
        signal({"dp": dp_index(chip, 1 - core)})
        met += 1

        for shift in sorted({1 % chips, chips - 1} - {0}):
            signal({"dp": dp_index((chip + shift) % chips, core)})
            met += 1

    pl.semaphore_wait(barrier, met)


def enter_kernel(
    nbits, parts_yx, tokens, seg, gain, *refs
):
    w_yx, w_out = refs[:parts_yx], refs[parts_yx]
    normed_all, seg_all, wyx_all, wout_all, s0, r0, s2, r2, l0, *line = refs[parts_yx + 1 :]
    rows = tokens.shape[0]
    me = lax.axis_index("tensor")
    peers = [chosen for chosen in subsets(tuple(range(nbits))) if chosen]
    greet_peers(nbits, True, False)
    width = wyx_all.shape[1] // parts_yx
    lines = [
        LineGather(
            own,
            wyx_all,
            line[2 * number],
            line[2 * number + 1],
            pl.ds(number * width, width) if parts_yx > 1 else None,
        )
        for number, own in enumerate(w_yx)
    ]
    lines.append(LineGather(w_out, wout_all, *line[2 * parts_yx : 2 * parts_yx + 2]))
    for item in lines:
        item.begin()

    def norm(row):
        values = tokens[pl.ds(row, CHUNK), :].astype(F32)
        scaled = values * rms_scale_of(values) * gain[...]
        normed_all[pl.ds(own_row(row, rows), CHUNK), :] = scaled.astype(BF16)

    chunks(rows, norm)
    gather = Gather(normed_all, rows, nbits, s0, r0)
    gather.begin()
    seg_own = pltpu.make_async_copy(seg, seg_all.at[me], l0.at[0])
    seg_own.start()
    seg_copies = [
        pltpu.make_async_remote_copy(
            src_ref=seg,
            dst_ref=seg_all.at[me],
            send_sem=s2.at[number],
            recv_sem=r2.at[number],
            device_id={"tensor": flipped(me, chosen)},
            device_id_type=MESH,
        )
        for number, chosen in enumerate(peers)
    ]
    for copy in seg_copies:
        copy.start()
    chips = lines[0].chips
    for item in lines:
        item.pass_on(1)
    gather.advance(0)
    for distance in range(2, chips):
        for item in lines:
            item.pass_on(distance)
    gather.finish(1)
    for item in lines:
        item.finish()
    for copy in seg_copies:
        copy.wait()
    seg_own.wait()


class Fetch:
    def __init__(self, nbits, cot, cot_all, s0, r0, l0):
        rows = cot.shape[0]
        own = pl.multiple_of(lax.axis_index("tensor") * rows, rows)
        self.local = pltpu.make_async_copy(cot, cot_all.at[pl.ds(own, rows), :], l0.at[0])
        self.gather = Gather(cot_all, rows, nbits, s0, r0)

    def begin(self):
        self.local.start()
        self.local.wait()
        self.gather.begin()

    def advance(self):
        self.gather.advance(0)

    def finish(self):
        self.gather.finish(1)


def fetch_scratch(nbits):
    return gather_sems(nbits) + [pltpu.SemaphoreType.DMA((1,))]


def fetch_kernel(nbits, cot, cot_all, *sems):
    greet(tensor_bits(nbits))
    fetch = Fetch(nbits, cot, cot_all, *sems)
    fetch.begin()
    fetch.advance()
    fetch.finish()


def middle_kernel(
    nbits, mixer, tokens, gain, middle, mid_all, landed, staged, s0, r0, s1, r1
):
    rows = tokens.shape[0]
    greet(tensor_bits(nbits))
    scatter = Scatter(mixer, landed, staged, rows, nbits, s0, r0)
    scatter.begin()
    scatter.run()

    def norm(row):
        values = tokens[pl.ds(row, CHUNK), :].astype(F32) + scatter.total(row, CHUNK)
        middle[pl.ds(row, CHUNK), :] = values
        scaled = values * rms_scale_of(values) * gain[...]
        mid_all[pl.ds(own_row(row, rows), CHUNK), :] = scaled.astype(BF16)

    chunks(rows, norm)
    gather = Gather(mid_all, rows, nbits, s1, r1)
    gather.begin()
    gather.finish()
    scatter.drain()


def result_kernel(nbits, ffn, middle, mixed, landed, staged, s0, r0):
    rows = middle.shape[0]
    greet(tensor_bits(nbits))
    scatter = Scatter(ffn, landed, staged, rows, nbits, s0, r0)
    scatter.begin()
    scatter.run()

    def add(row):
        values = middle[pl.ds(row, CHUNK), :] + scatter.total(row, CHUNK)
        mixed[pl.ds(row, CHUNK), :] = values.astype(BF16)

    chunks(rows, add)
    scatter.drain()


def norm_pull(values, gain, cotangent):
    scale = rms_scale_of(values)
    unit = values * scale
    inner = cotangent * gain
    back = scale * (inner - unit * jnp.mean(inner * unit, axis=-1, keepdims=True))
    return back, cotangent * unit


def eight_rows(values):
    total = values[0:8]
    for at in range(8, CHUNK, 8):
        total = total + values[at : at + 8]
    return total


def turn_kernel(
    nbits, d_norm, cot, middle, gain, d_middle, d_mixer, d_gain, landed, staged, s0, r0, s1, r1
):
    rows = middle.shape[0]
    greet(tensor_bits(nbits))
    scatter = Scatter(d_norm, landed, staged, rows, nbits, s0, r0)
    scatter.begin()
    d_gain[...] = jnp.zeros_like(d_gain)
    scatter.run()

    def pull(row):
        span = pl.ds(row, CHUNK)
        back, gains = norm_pull(middle[span, :], gain[...], scatter.total(row, CHUNK))
        values = cot[span, :].astype(F32) + back
        d_middle[span, :] = values
        d_mixer[pl.ds(own_row(row, rows), CHUNK), :] = values.astype(BF16)
        d_gain[...] += eight_rows(gains)

    chunks(rows, pull)
    gather = Gather(d_mixer, rows, nbits, s1, r1)
    gather.begin()
    gather.finish()
    scatter.drain()


class LineSum:
    def __init__(self, whole, kept, swapped, staged, landed, send_sems, recv_sems, columns=None):
        self.whole, self.kept, self.swapped = whole, kept, swapped
        self.staged, self.landed = staged, landed
        self.sems = (send_sems, recv_sems)
        self.columns = columns
        self.chip, self.core, self.chips = dp_place()
        self.rows = whole.shape[2]

    def half(self, core):
        if self.columns is None:
            return self.whole.at[:, core]
        return self.whole.at[:, core, :, self.columns]

    def local(self):
        return pltpu.make_async_copy(
            self.half(self.core), self.kept, self.sems[0].at[2 * self.chips]
        )

    def swap(self):
        return pltpu.make_async_remote_copy(
            src_ref=self.half(1 - self.core),
            dst_ref=self.swapped,
            send_sem=self.sems[0].at[0],
            recv_sem=self.sems[1].at[0],
            device_id={"dp": dp_index(self.chip, 1 - self.core)},
            device_id_type=MESH,
        )

    def has(self, way, distance):
        return self.chip + distance < self.chips if way == UP else self.chip >= distance

    def slot(self, way, distance):
        return (0 if way == UP else self.chips - 1) + distance

    def hop(self, way, distance):
        return pltpu.make_async_remote_copy(
            src_ref=self.staged.at[self.slot(way, distance - 1)],
            dst_ref=self.landed.at[self.slot(way, distance - 1)],
            send_sem=self.sems[0].at[1 + self.slot(way, distance - 1)],
            recv_sem=self.sems[1].at[1 + self.slot(way, distance - 1)],
            device_id={"dp": dp_index(self.chip + way, self.core)},
            device_id_type=MESH,
        )

    def arrival(self, way, distance):
        number = self.slot(way, distance)
        return pltpu.make_async_remote_copy(
            src_ref=self.landed.at[number],
            dst_ref=self.landed.at[number],
            send_sem=self.sems[0].at[1 + number],
            recv_sem=self.sems[1].at[1 + number],
            device_id={"dp": dp_index(self.chip - way, self.core)},
            device_id_type=MESH,
        )

    def begin(self):
        self.swap().start()
        self.local().start()

    def both(self, chip, span):
        return self.kept[chip, span, :].astype(F32) + self.swapped[chip, span, :].astype(F32)

    def send(self, distance):
        if distance == self.chips - 1:
            self.local().wait()
            self.swap().wait_recv()
        for way in (UP, DOWN):

            @pl.when(self.has(way, distance))
            def _(way=way):
                chip = self.chip + way * distance
                slot = self.slot(way, distance - 1)

                def first(row):
                    span = pl.ds(row, CHUNK)
                    self.staged[slot, span, :] = self.both(chip, span).astype(BF16)

                def later(row):
                    span = pl.ds(row, CHUNK)
                    total = self.both(chip, span) + self.landed[
                        self.slot(way, distance), span, :
                    ].astype(F32)
                    self.staged[slot, span, :] = total.astype(BF16)

                if distance == self.chips - 1:
                    chunks(self.rows, first)
                else:

                    @pl.when(self.has(-way, 1))
                    def _():
                        self.arrival(way, distance).wait_recv()
                        chunks(self.rows, later)

                    @pl.when(jnp.logical_not(self.has(-way, 1)))
                    def _():
                        chunks(self.rows, first)

                self.hop(way, distance).start()

    def finish(self, store):
        below, above = self.has(DOWN, 1), self.has(UP, 1)

        def fill(slots):
            for way in slots:
                self.arrival(way, 0).wait_recv()

            def one(row):
                span = pl.ds(row, CHUNK)
                total = self.both(self.chip, span)
                for way in slots:
                    total = total + self.landed[self.slot(way, 0), span, :].astype(F32)
                store(span, total)

            chunks(self.rows, one)

        @pl.when(below & above)
        def _():
            fill((UP, DOWN))

        @pl.when(jnp.logical_not(above))
        def _():
            fill((UP,))

        @pl.when(jnp.logical_not(below))
        def _():
            fill((DOWN,))

    def drain(self):
        self.swap().wait_send()
        for way in (UP, DOWN):
            for distance in range(1, self.chips):

                @pl.when(self.has(way, distance))
                def _(way=way, distance=distance):
                    self.hop(way, distance).wait_send()


def line_scratch(ndp, rows, columns):
    chips = ndp // 2
    return [
        pltpu.VMEM((chips, rows, columns), BF16),
        pltpu.VMEM((chips, rows, columns), BF16),
        pltpu.VMEM((2 * chips - 2, rows, columns), BF16),
        pltpu.VMEM((2 * chips - 2, rows, columns), BF16),
        pltpu.SemaphoreType.DMA((2 * chips + 1,)),
        pltpu.SemaphoreType.DMA((2 * chips + 1,)),
    ]


RING = 6


def leave_kernel(nbits, tiled, *refs):
    refs = list(refs)

    def take(count):
        taken = refs[:count]
        del refs[:count]
        return taken

    d_norm, tokens, d_middle, gain, own_small, d_gain_mid = take(6)
    pieces = take(2)
    grad_input, sum_y, sum_x, gate_all, small_all = take(5)
    landed, staged, s0, r0 = take(4)
    share = small_all.shape[2]
    rings = [LineSum(pieces[0], *take(RING))]
    if tiled:
        for at in (0, share):
            rings.append(LineSum(pieces[1], *take(RING), pl.ds(at, share)))
    else:
        rings.append(LineSum(pieces[1], *take(RING)))
    d_gain, gains, gains_landed, small, small_landed = take(5)
    gain_s, gain_r, vec_s, vec_r, join_s, join_r, gate_s, gate_r = take(8)
    rows = tokens.shape[0]
    me = lax.axis_index("tensor")
    chip, core, chips = dp_place()
    place = dp_index(chip, core)
    peers = [chosen for chosen in subsets(tuple(range(nbits))) if chosen]
    others = [(shift, turn) for shift in range(chips) for turn in range(2)][1:]
    greet_peers(nbits, True, True)
    for ring in rings:
        ring.begin()
    scatter = Scatter(d_norm, landed, staged, rows, nbits, s0, r0)
    scatter.begin()
    d_gain[...] = jnp.zeros_like(d_gain)
    far = list(range(chips - 1, 0, -1))
    for ring in rings:
        ring.send(far[0])
    if len(far) > 1:
        rings[0].send(far[1])
    scatter.advance(0)
    if len(far) > 1:
        for ring in rings[1:]:
            ring.send(far[1])
    for distance in far[2:]:
        rings[0].send(distance)
    for step in range(1, nbits):
        scatter.advance(step)

    def pull(row):
        span = pl.ds(row, CHUNK)
        back, parts = norm_pull(
            tokens[span, :].astype(F32), gain[...], scatter.total(row, CHUNK)
        )
        grad_input[span, :] = d_middle[span, :] + back
        d_gain[...] += eight_rows(parts)

    chunks(rows, pull)
    top = jnp.sum(d_gain[...], axis=0, keepdims=True)
    low = jnp.sum(d_gain_mid[...], axis=0, keepdims=True)
    place8 = lax.broadcasted_iota(jnp.int32, (8, share), 0)
    for index in range(1 << nbits):
        span = slice(index * share, (index + 1) * share)
        gains[index] = jnp.where(
            place8 == 6, top[:, span], jnp.where(place8 == 7, low[:, span], 0.0)
        )

    def gain_copy(number, chosen):
        peer = flipped(me, chosen)
        return pltpu.make_async_remote_copy(
            src_ref=gains.at[peer],
            dst_ref=gains_landed.at[number],
            send_sem=gain_s.at[number],
            recv_sem=gain_r.at[number],
            device_id={"tensor": peer},
            device_id_type=MESH,
        )

    for number, chosen in enumerate(peers):
        gain_copy(number, chosen).start()
    for distance in far[2:]:
        for ring in rings[1:]:
            ring.send(distance)
    total = own_small[...] + gains[me]
    for number, chosen in enumerate(peers):
        gain_copy(number, chosen).wait_recv()
        total = total + gains_landed[number]
    small[...] = total

    def vec_copy(number, shift, turn):
        other = dp_index((chip + shift) % chips, core + turn * (1 - 2 * core))
        return pltpu.make_async_remote_copy(
            src_ref=small,
            dst_ref=small_landed.at[number],
            send_sem=vec_s.at[number],
            recv_sem=vec_r.at[number],
            device_id={"dp": other},
            device_id_type=MESH,
        )

    for number, (shift, turn) in enumerate(others):
        vec_copy(number, shift, turn).start()

    def store_gate(span, value):
        gate_all[me, place, span, :] = value.astype(BF16)

    rings[0].finish(store_gate)

    def gate_copy(number, chip_from, ref, target):
        return pltpu.make_async_remote_copy(
            src_ref=ref,
            dst_ref=ref,
            send_sem=gate_s.at[number],
            recv_sem=gate_r.at[number],
            device_id=target,
            device_id_type=MESH,
        )

    def gate_tensor(number, chosen):
        ref = gate_all.at[me, place]
        return gate_copy(number, chip, ref, {"tensor": flipped(me, chosen)})

    def gate_line(shift):
        target = {"dp": dp_index((chip + shift) % chips, core)}
        return gate_copy(len(peers) + shift - 1, chip, gate_all.at[:, place], target)

    def gate_core(shift):
        ref = gate_all.at[:, dp_index((chip + chips - shift) % chips, core)]
        target = {"dp": dp_index(chip, 1 - core)}
        return gate_copy(len(peers) + chips - 1 + shift, chip, ref, target)

    for number, chosen in enumerate(peers):
        gate_tensor(number, chosen).start()
    total = small[...]
    for number, (shift, turn) in enumerate(others):
        vec_copy(number, shift, turn).wait_recv()
        total = total + small_landed[number]
    small_all[me] = total

    def join_copy(number, chosen):
        return pltpu.make_async_remote_copy(
            src_ref=small_all.at[me],
            dst_ref=small_all.at[me],
            send_sem=join_s.at[number],
            recv_sem=join_r.at[number],
            device_id={"tensor": flipped(me, chosen)},
            device_id_type=MESH,
        )

    for number, chosen in enumerate(peers):
        join_copy(number, chosen).start()
    for number, chosen in enumerate(peers):
        gate_tensor(number, chosen).wait_recv()
    for shift in range(1, chips):
        gate_line(shift).start()
    gate_core(0).start()
    for shift in range(1, chips):
        gate_line(shift).wait_recv()
        gate_core(shift).start()

    def store_in(*targets):
        def store(span, value):
            for number, ref in enumerate(targets):
                ref[span, :] = value[:, number * share : (number + 1) * share]

        return store

    if tiled:
        rings[1].finish(store_in(sum_y))
        rings[2].finish(store_in(sum_x))
    else:
        rings[1].finish(store_in(sum_y, sum_x))
    for shift in range(chips):
        gate_core(shift).wait()
    for shift in range(1, chips):
        gate_line(shift).wait_send()
    for number, chosen in enumerate(peers):
        gate_tensor(number, chosen).wait_send()
        gain_copy(number, chosen).wait_send()
        join_copy(number, chosen).wait()
    for number, (shift, turn) in enumerate(others):
        vec_copy(number, shift, turn).wait_send()
    scatter.drain()
    for ring in rings:
        ring.drain()


def in_vmem(count):
    return [pl.BlockSpec(memory_space=pltpu.VMEM)] * count


def call_kernel(kernel, outs, scratch, number, *operands, far_in=(), far_out=(), cost_us=1):
    vmem = pl.BlockSpec(memory_space=pltpu.VMEM)
    far = pl.BlockSpec(memory_space=pl.ANY)
    return pl.pallas_call(
        kernel,
        out_shape=outs,
        in_specs=[far if i in far_in else vmem for i in range(len(operands))],
        out_specs=tuple(far if i in far_out else vmem for i in range(len(outs))),
        scratch_shapes=scratch,
        cost_estimate=pl.CostEstimate(
            flops=0, bytes_accessed=cost_us * 1_000_000, transcendentals=0
        ),
        compiler_params=pltpu.CompilerParams(
            collective_id=number, has_side_effects=True, vmem_limit_bytes=VMEM_BYTES
        ),
    )(*operands)


def sigmoid(values):
    return 1.0 / (1.0 + jnp.exp(-values))


def one_minus_exp(values):
    series = values / 7.0 + 1.0
    for order in (6.0, 5.0, 4.0, 3.0, 2.0):
        series = 1.0 + series * values / order
    return jnp.where(values > -0.3, -values * series, 1.0 - jnp.exp(values))


GELU_K = 0.7978845608028654
GELU_C = 0.044715


def gelu_parts(values):
    square = values * values
    bent = jnp.tanh(GELU_K * values * (1.0 + GELU_C * square))
    gelu = 0.5 * values * (1.0 + bent)
    slope = 0.5 * (1.0 + bent) + 0.5 * values * (1.0 - bent * bent) * GELU_K * (
        1.0 + 3.0 * GELU_C * square
    )
    return gelu, slope


def gate_terms(gate_a, gate_x, soft, since):
    sig_a = sigmoid(gate_a)
    sig_x = sigmoid(gate_x)
    log_decay = -8.0 * sig_a * soft
    decay = jnp.exp(log_decay)
    scale = jnp.sqrt(one_minus_exp(2.0 * log_decay))
    keep = since > 0.5
    return sig_a, sig_x, decay, jnp.where(keep, scale, 1.0), keep


def scan_down(decay, value, carry):
    place = lax.broadcasted_iota(jnp.int32, decay.shape, 0)
    for shift in (1, 2, 4):
        past = place >= shift
        moved = pltpu.roll(value, shift, 0)
        value = jnp.where(past, decay * moved + value, value)
        decay = jnp.where(past, decay * pltpu.roll(decay, shift, 0), decay)
    return decay * carry + value


def scan_up(decay, value, carry):
    place = lax.broadcasted_iota(jnp.int32, decay.shape, 0)
    factor = jnp.where(place < 7, pltpu.roll(decay, 7, 0), 1.0)
    for shift in (1, 2, 4):
        past = place < 8 - shift
        moved = pltpu.roll(value, 8 - shift, 0)
        value = jnp.where(past, factor * moved + value, value)
        factor = jnp.where(past, factor * pltpu.roll(factor, 8 - shift, 0), factor)
    return factor * carry + value


def forward_scan(conv_rows, gates, branch_y, soft, since, mixed, states, between=()):
    total_rows, width = states.shape

    def step(i, carry):
        row = pl.multiple_of(i * CHUNK, CHUNK)
        span = pl.ds(row, CHUNK)
        values = conv_rows(span).astype(F32)
        kept = []
        for at in range(0, CHUNK, 8):
            tile = pl.ds(row + at, 8)
            sig_a, sig_x, decay, scale, keep = gate_terms(
                gates[tile, :width], gates[tile, width:], soft[...], since[tile, :]
            )
            given = values[at : at + 8] * sig_x * scale
            state = scan_down(jnp.where(keep, decay, 0.0), given, carry)
            carry = state[7:8]
            states[tile, :] = state
            kept.append(state * gelu_parts(branch_y[tile, :])[0])
        mixed[span, :] = jnp.concatenate(kept, axis=0).astype(BF16)
        return carry

    steps, stretches = total_rows // CHUNK, len(between) + 1
    carry = jnp.zeros((1, width), F32)
    for stretch in range(stretches):
        first, last = stretch * steps // stretches, (stretch + 1) * steps // stretches
        carry = lax.fori_loop(first, last, step, carry)
        if stretch < len(between):
            between[stretch]()


def forward_scan_kernel(conv, gates, branch_y, soft, since, mixed, states):
    forward_scan(lambda span: conv[span, :], gates, branch_y, soft, since, mixed, states)


def backward_scan(
    d_mixed, conv_rows, gates, branch_y, states, soft, slope_soft, since, d_conv, d_gates, d_branch, d_decay
):
    total_rows, width = states.shape
    d_decay[...] = jnp.zeros_like(d_decay)

    def step(i, carry):
        row = pl.multiple_of(total_rows - CHUNK - i * CHUNK, CHUNK)
        span = pl.ds(row, CHUNK)
        values = conv_rows(span).astype(F32)
        kept = []
        for at in range(CHUNK - 8, -1, -8):
            tile = pl.ds(row + at, 8)
            soft_row = soft[...]
            sig_a, sig_x, decay, scale, keep = gate_terms(
                gates[tile, :width], gates[tile, width:], soft_row, since[tile, :]
            )
            value = values[at : at + 8]
            gelu, slope = gelu_parts(branch_y[tile, :])
            state = states[tile, :]
            upper = d_mixed[tile, :]
            held = jnp.where(keep, decay, 0.0)
            lam = scan_up(held, upper * gelu, carry)
            carry = held[0:1] * lam[0:1]
            d_conv[tile, :] = lam * sig_x * scale
            d_x = lam * value * scale * sig_x * (1.0 - sig_x)
            given = value * sig_x
            d_log = lam * (state - given * scale - given * decay * decay / scale)
            d_log = jnp.where(keep, d_log, 0.0)
            d_a = d_log * (-8.0 * soft_row) * sig_a * (1.0 - sig_a)
            d_decay[...] += d_log * (-8.0 * sig_a) * slope_soft[...]
            kept.append((d_a, d_x, upper * state * slope))
        kept = kept[::-1]
        d_gates[span, :width] = jnp.concatenate([k[0] for k in kept], axis=0).astype(BF16)
        d_gates[span, width:] = jnp.concatenate([k[1] for k in kept], axis=0).astype(BF16)
        d_branch[span, :] = jnp.concatenate([k[2] for k in kept], axis=0).astype(BF16)
        return carry

    lax.fori_loop(0, total_rows // CHUNK, step, jnp.zeros((1, width), F32))


def backward_scan_kernel(
    d_mixed, conv, gates, branch_y, states, soft, slope_soft, since, d_conv, d_gates, d_branch, d_decay
):
    backward_scan(
        d_mixed,
        lambda span: conv[span, :],
        gates,
        branch_y,
        states,
        soft,
        slope_soft,
        since,
        d_conv,
        d_gates,
        d_branch,
        d_decay,
    )


def times_transposed(left, right):
    return lax.dot_general(left, right, (((1,), (1,)), ((), ())), preferred_element_type=F32)


class HalfBlocks:
    def __init__(self, channels, block):
        self.odd = lax.axis_index("tensor") % 2
        self.half = block // 2
        self.block = block
        self.count = channels // block + 1
        self.channels = channels
        self.own = pl.multiple_of(self.odd * self.half, self.half)
        self.shared = (1 - self.odd) * (self.count - 1)
        self.mine_in_block = pl.multiple_of(self.odd * self.half, self.half)
        self.other_in_block = pl.multiple_of((1 - self.odd) * self.half, self.half)
        self.mine = pl.multiple_of((1 - self.odd) * (channels - self.half), self.half)
        self.pair = {"tensor": lax.axis_index("tensor") + 1 - 2 * self.odd}

    def full(self, index):
        block = index + self.odd
        return block, pl.multiple_of(index * self.block + self.odd * self.half, self.half)

    def span(self, block):
        return pl.ds(pl.multiple_of(block * self.block, self.block), self.block)

    def shared_part(self, start):
        return pl.ds(pl.multiple_of(self.shared * self.block + start, self.half), self.half)


PART = 256


def parts(rows, body):
    def step(i, carry):
        body(pl.ds(pl.multiple_of(i * PART, PART), PART))
        return carry

    lax.fori_loop(0, rows // PART, step, 0)


def recurrence_kernel(
    taps,
    nbits,
    branches,
    tap_rows,
    soft,
    since,
    weights,
    cot,
    mixed,
    states,
    window,
    gates,
    cot_all,
    send,
    recv,
    *sems,
):
    total_rows, width = states.shape
    block = weights.shape[2]
    place = HalfBlocks(width, block)
    branch_y, branch_x = branches.at[:, :width], branches.at[:, width:]
    greet(tensor_bits(nbits))
    fetch = Fetch(nbits, cot, cot_all, *sems)
    fetch.begin()

    def conv(i, before):
        row = pl.multiple_of(i * CHUNK, CHUNK)
        kept = []
        for at in range(0, CHUNK, 8):
            tile = pl.ds(row + at, 8)
            values = branch_x[tile, :]
            line = lax.broadcasted_iota(jnp.int32, values.shape, 0)
            total = values * tap_rows[0:1, :]
            for tap in range(1, taps):
                moved = jnp.where(
                    line < tap, pltpu.roll(before, tap, 0), pltpu.roll(values, tap, 0)
                )
                moved = jnp.where(since[tile, :] > tap - 0.5, moved, 0.0)
                total = total + moved * tap_rows[tap : tap + 1, :]
            kept.append(total)
            before = values
        window[pl.ds(row, CHUNK), pl.ds(place.own, width)] = jnp.concatenate(
            kept, axis=0
        ).astype(BF16)
        return before

    lax.fori_loop(0, total_rows // CHUNK, conv, jnp.zeros((8, width), F32))
    source = window.at[:, place.shared_part(place.mine_in_block)]
    away = pl.multiple_of(place.odd * (place.count - 1) * block + place.mine_in_block, place.half)
    rim = pltpu.make_async_remote_copy(
        src_ref=source,
        dst_ref=window.at[:, pl.ds(away, place.half)],
        send_sem=send.at[0],
        recv_sem=recv.at[0],
        device_id=place.pair,
        device_id_type=MESH,
    )
    rim.start()

    def full(span):
        for index in range(place.count - 1):
            number, at = place.full(index)
            cells = window[span, place.span(number)]
            for s in range(2):
                gates[span, pl.ds(s * width + at, block)] = jnp.dot(
                    cells, weights[s, number], preferred_element_type=F32
                )

    parts(total_rows, full)
    rim.wait()

    def shared(span):
        cells = window[span, place.span(place.shared)]
        for s in range(2):
            gates[span, pl.ds(s * width + place.mine, place.half)] = jnp.dot(
                cells,
                weights[s, place.shared, :, pl.ds(place.mine_in_block, place.half)],
                preferred_element_type=F32,
            )

    parts(total_rows, shared)
    forward_scan(
        lambda span: window[span, pl.ds(place.own, width)],
        gates,
        branch_y,
        soft,
        since,
        mixed,
        states,
        [fetch.advance],
    )
    fetch.finish()


def recurrence_back_kernel(
    taps,
    nbits,
    with_ffn,
    d_mixed,
    window,
    gates,
    branches,
    states,
    tap_rows,
    soft,
    slope_soft,
    since,
    weights,
    *refs,
):
    refs = list(refs)

    def take(count):
        taken = refs[:count]
        del refs[:count]
        return taken

    ffn, middle = take(2) if with_ffn else (None, None)
    d_branches, gate_grad, own_small = take(3)
    mixed = take(1)[0] if with_ffn else None
    d_conv, d_gates, given, taken, sums, send, recv = take(7)
    total_rows, width = states.shape
    block = weights.shape[2]
    place = HalfBlocks(width, block)
    half = place.half
    branch_y, branch_x = branches.at[:, :width], branches.at[:, width:]
    d_branch_y, d_branch_x = d_branches.at[:, :width], d_branches.at[:, width:]
    greet(tensor_bits(nbits))
    if with_ffn:
        scatter = Scatter(ffn, *take(2), middle.shape[0], nbits, *take(2))
        scatter.begin()
    backward_scan(
        d_mixed,
        lambda span: window[span, pl.ds(place.own, width)],
        gates,
        branch_y,
        states,
        soft,
        slope_soft,
        since,
        d_conv,
        d_gates,
        d_branch_y,
        sums.at[taps],
    )

    def to_pair(span):
        total = jnp.zeros((PART, half), F32)
        for s in range(2):
            total = total + times_transposed(
                d_gates[span, pl.ds(s * width + place.mine, half)],
                weights[
                    s,
                    place.shared,
                    pl.ds(place.other_in_block, half),
                    pl.ds(place.mine_in_block, half),
                ],
            )
        given[span, :] = total.astype(BF16)

    parts(total_rows, to_pair)
    rim = pltpu.make_async_remote_copy(
        src_ref=given,
        dst_ref=taken,
        send_sem=send.at[0],
        recv_sem=recv.at[0],
        device_id=place.pair,
        device_id_type=MESH,
    )
    rim.start()

    def full(span):
        for index in range(place.count - 1):
            number, at = place.full(index)
            total = d_conv[span, pl.ds(at, block)]
            for s in range(2):
                total = total + times_transposed(
                    d_gates[span, pl.ds(s * width + at, block)], weights[s, number]
                )
            d_conv[span, pl.ds(at, block)] = total
        total = d_conv[span, pl.ds(place.mine, half)]
        for s in range(2):
            total = total + times_transposed(
                d_gates[span, pl.ds(s * width + place.mine, half)],
                weights[
                    s,
                    place.shared,
                    pl.ds(place.mine_in_block, half),
                    pl.ds(place.mine_in_block, half),
                ],
            )
        d_conv[span, pl.ds(place.mine, half)] = total

    parts(total_rows, full)
    if with_ffn:
        scatter.advance(0)
    units = width // half
    for index in range(units):
        number = (index + place.odd) // 2
        cells = window[:, place.span(number)]
        both = jnp.concatenate(
            [d_gates[:, s * width + index * half : s * width + (index + 1) * half] for s in range(2)],
            axis=1,
        )
        found = lax.dot_general(
            cells, both, (((0,), (0,)), ((), ())), preferred_element_type=F32
        ).astype(BF16)
        gate_grad[2 * index] = found[:, :half]
        gate_grad[2 * index + 1] = found[:, half:]
    rim.wait()

    def add(span):
        d_conv[span, pl.ds(place.mine, half)] += taken[span, :].astype(F32)

    parts(total_rows, add)
    for tap in range(taps):
        sums[tap] = jnp.zeros((8, width), F32)

    def conv(i, after):
        row = pl.multiple_of(total_rows - CHUNK - i * CHUNK, CHUNK)
        kept = []
        for at in range(CHUNK - 8, -1, -8):
            tile = pl.ds(row + at, 8)
            values = d_conv[tile, :]
            line = lax.broadcasted_iota(jnp.int32, values.shape, 0)
            below = branch_x[tile, :]
            higher = pl.multiple_of((row + at - 8 + total_rows) % total_rows, 8)
            above = branch_x[pl.ds(higher, 8), :]
            total = values * tap_rows[0:1, :]
            sums[0] += values * below
            masked = []
            for tap in range(1, taps):
                here = jnp.where(since[tile, :] > tap - 0.5, values, 0.0)
                masked.append(here)
                moved = jnp.where(
                    line < 8 - tap,
                    pltpu.roll(here, 8 - tap, 0),
                    pltpu.roll(after[tap - 1], 8 - tap, 0),
                )
                total = total + moved * tap_rows[tap : tap + 1, :]
                source = jnp.where(
                    line < tap, pltpu.roll(above, tap, 0), pltpu.roll(below, tap, 0)
                )
                sums[tap] += here * source
            after = tuple(masked)
            kept.append(total)
        d_branch_x[pl.ds(row, CHUNK), :] = jnp.concatenate(kept[::-1], axis=0).astype(BF16)
        return after

    none = jnp.zeros((8, width), F32)
    lax.fori_loop(0, total_rows // CHUNK, conv, (none,) * (taps - 1))
    line = lax.broadcasted_iota(jnp.int32, (8, width), 0)
    total = jnp.zeros((8, width), F32)
    for tap in range(taps + 1):
        row = jnp.sum(sums[tap], axis=0, keepdims=True)
        total = jnp.where(line == tap, row, total)
    own_small[...] = total
    if with_ffn:
        for step in range(1, nbits):
            scatter.advance(step)

        def result(row):
            span = pl.ds(row, CHUNK)
            mixed[span, :] = (middle[span, :] + scatter.total(row, CHUNK)).astype(BF16)

        chunks(middle.shape[0], result)
        scatter.drain()


def gate_layout_kernel(parts_in, whole):
    for piece in range(parts_in.shape[1]):
        for s in range(2):
            whole[s, 0, :, piece * 128 : (piece + 1) * 128] = parts_in[0, piece, s].astype(F32)


def gate_layout(parts_in):
    blocks, pieces, _, block, unit = parts_in.shape
    if unit != 128:
        whole = parts_in.transpose(2, 0, 3, 1, 4).reshape(2, blocks, block, block)
        return whole.astype(F32)
    return pl.pallas_call(
        gate_layout_kernel,
        grid=(blocks,),
        out_shape=jax.ShapeDtypeStruct((2, blocks, block, block), F32),
        in_specs=[pl.BlockSpec((1, pieces, 2, block, unit), lambda n: (n, 0, 0, 0, 0))],
        out_specs=pl.BlockSpec((2, 1, block, block), lambda n: (0, n, 0, 0)),
    )(parts_in)


def scan_call(kernel, outs, *operands):
    return pl.pallas_call(
        kernel,
        out_shape=outs,
        in_specs=in_vmem(len(operands)),
        out_specs=tuple(in_vmem(len(outs))),
        compiler_params=pltpu.CompilerParams(vmem_limit_bytes=VMEM_BYTES),
    )(*operands)


class Rim:
    def __init__(self, route, back, source, first, width, room):
        self.route, self.back = route, back
        self.source, self.first, self.width = source, first, width
        self.room = room

    def fetch(self, values):
        part = lax.dynamic_slice_in_dim(values, self.source, self.width, 1)
        return lax.ppermute(part, "tensor", self.route)

    def give(self, part):
        return lax.ppermute(part, "tensor", self.back)

    def add(self, values, part):
        zeros = jnp.zeros(values.shape, F32)
        return values + lax.dynamic_update_slice_in_dim(
            zeros, part.astype(F32), self.source, 1
        )

    def window(self, channels):
        return (channels // self.width + 4) * self.width


def gate_rims(channels, block_size, ntensor, offset):
    up = [(i, i + 1) for i in range(ntensor - 1)]
    down = [(i + 1, i) for i in range(ntensor - 1)]
    last = jnp.int32(channels - block_size)
    return [
        Rim(up, down, last, offset - block_size, block_size, block_size),
        Rim(down, up, jnp.int32(0), offset + channels, block_size, block_size),
    ]


def same_block(first, count, offset, channels, block_size):
    rows = (first + jnp.arange(count, dtype=jnp.int32))[:, None]
    columns = (offset + jnp.arange(channels, dtype=jnp.int32))[None, :]
    return (rows + block_size) // block_size == (columns + block_size) // block_size


def gate_dense(gate_w, offset, first, count):
    block_size = gate_w.shape[2]
    total = gate_w.shape[1] * block_size
    channels = total // lax.axis_size("tensor")
    columns = gate_w.transpose(2, 0, 1, 3).reshape(block_size, 2, total)
    columns = lax.dynamic_slice_in_dim(columns, offset, channels, 2)
    copies = -(-count // block_size) + 1
    tall = jnp.concatenate([columns] * copies, axis=0)
    tall = lax.dynamic_slice_in_dim(tall, (first + block_size) % block_size, count, 0)
    same = same_block(first, count, offset, channels, block_size)
    dense = jnp.where(same[:, None, :], tall, jnp.zeros_like(tall))
    return dense.reshape(count, 2 * channels)


def doc_starts(seg_ids, seq_len):
    places = jnp.arange(seg_ids.shape[0], dtype=jnp.int32)
    before = jnp.concatenate([seg_ids[:1], seg_ids[:-1]])
    resets = (places % seq_len == 0) | (seg_ids != before)
    starts = lax.cummax(jnp.where(resets, places, jnp.zeros_like(places)), axis=0)
    return starts


def causal_conv(starts, values, kernel):
    places = jnp.arange(values.shape[0], dtype=jnp.int32)
    total = values * kernel[0]
    for offset_k in range(1, kernel.shape[0]):
        moved = jnp.concatenate(
            [jnp.zeros((offset_k, values.shape[1]), values.dtype), values[:-offset_k]], axis=0
        )
        valid = (places - offset_k >= starts)[:, None]
        total = total + jnp.where(valid, moved, jnp.zeros_like(moved)) * kernel[offset_k]
    return total


def geglu(gate_val, up_val):
    return jax.nn.gelu(gate_val, approximate=True) * up_val


def rows_times(left, right):
    return lax.dot_general(left, right, (((1,), (1,)), ((), ())), preferred_element_type=F32)


def rows_back(lefts, rights):
    total = rows_times(lefts[0], rights[0])
    return total + rows_times(lefts[1], rights[1])


def inner_rows(left, right):
    return lax.dot_general(left, right, (((0,), (0,)), ((), ())), preferred_element_type=F32)


def halved(grad, ndp):
    return grad.reshape(ndp // 2, 2, grad.shape[0] // ndp, grad.shape[1])


def body(
    tokens,
    segments,
    cotangent,
    norm_gain,
    w_y,
    w_x,
    conv_w,
    gate_w,
    decay_param,
    w_out,
    mlp_gain,
    w_gate,
    w_up,
    w_down,
):
    ntensor = lax.axis_size("tensor")
    ndp = lax.axis_size("dp")
    nbits = log2_of(ntensor)
    tindex = lax.axis_index("tensor")
    own_rows, width = tokens.shape
    group_rows = own_rows * ntensor
    block_size = gate_w.shape[2]
    nblocks = gate_w.shape[1]
    dp_rows, channels = w_y.shape
    taps = conv_w.shape[0]
    offset = tindex * channels
    shape = jax.ShapeDtypeStruct
    gain_in = norm_gain.reshape(1, width)
    gain_mid = mlp_gain.reshape(1, width)
    seg_rows_of = own_rows // 128
    tiled = channels % 128 == 0
    w_yx = (w_y, w_x) if tiled else (jnp.concatenate([w_y, w_x], axis=1),)
    normed_rows, seg_all, wyx_loc, wout_loc = call_kernel(
        partial(enter_kernel, nbits, len(w_yx)),
        (
            shape((group_rows, width), BF16),
            shape((ntensor, seg_rows_of, 128), jnp.int32),
            shape((dp_rows * ndp, 2 * channels), BF16),
            shape((dp_rows * ndp, channels), BF16),
        ),
        gather_sems(nbits)
        + [pltpu.SemaphoreType.DMA((ntensor - 1,)), pltpu.SemaphoreType.DMA((ntensor - 1,))]
        + [pltpu.SemaphoreType.DMA((1,))]
        + line_sems(ndp) * (len(w_yx) + 1),
        0,
        tokens,
        segments.reshape(seg_rows_of, 128),
        gain_in,
        *w_yx,
        w_out,
        far_in=tuple(range(3, 4 + len(w_yx))),
        far_out=(2, 3),
    )
    w_gate, w_up, w_down, normed_rows = lax.optimization_barrier(
        (w_gate, w_up, w_down, normed_rows)
    )
    wg_loc = lax.all_gather(w_gate, "dp", axis=0, tiled=True)
    wu_loc = lax.all_gather(w_up, "dp", axis=0, tiled=True)
    wd_loc = lax.all_gather(w_down, "dp", axis=0, tiled=True)
    seg_rows = seg_all.reshape(group_rows)
    starts = doc_starts(seg_rows, group_rows)
    conv_loc = lax.dynamic_slice_in_dim(conv_w, offset, channels, 1)
    decay_loc = lax.dynamic_slice_in_dim(decay_param, offset, channels, 0).reshape(1, channels)
    soft = jax.nn.softplus(decay_loc)
    slope_soft = jax.nn.sigmoid(decay_loc)
    half_blocks = (
        channels % block_size == block_size // 2 and ntensor % 2 == 0 and block_size % 256 == 0
    )
    since = (jnp.arange(group_rows, dtype=jnp.int32) - starts).astype(F32)[:, None]
    branches = jnp.dot(normed_rows, wyx_loc, preferred_element_type=F32)
    if half_blocks:
        span_blocks = channels // block_size + 1
        w_window = lax.dynamic_slice_in_dim(gate_w, offset // block_size, span_blocks, 1)
        taps_pad = jnp.concatenate([conv_loc, jnp.zeros((8 - taps, channels), F32)], axis=0)
        mixed_low, states, window, gate_pre, cot_rows = call_kernel(
            partial(recurrence_kernel, taps, nbits),
            (
                shape((group_rows, channels), BF16),
                shape((group_rows, channels), F32),
                shape((group_rows, span_blocks * block_size), BF16),
                shape((group_rows, 2 * channels), F32),
                shape((group_rows, width), BF16),
            ),
            [pltpu.SemaphoreType.DMA((1,)), pltpu.SemaphoreType.DMA((1,))]
            + fetch_scratch(nbits),
            5,
            branches,
            taps_pad,
            soft,
            since,
            w_window,
            cotangent,
        )
    else:
        branch_y, branch_x = branches[:, :channels], branches[:, channels:]
        (cot_rows,) = call_kernel(
            partial(fetch_kernel, nbits),
            (shape((group_rows, width), BF16),),
            fetch_scratch(nbits),
            5,
            cotangent,
        )
        rims = gate_rims(channels, block_size, ntensor, offset)
        own_dense = gate_dense(gate_w, offset, offset, channels)
        rim_dense = [gate_dense(gate_w, offset, rim.first, rim.width) for rim in rims]
        conv_out, conv_pull = jax.vjp(partial(causal_conv, starts), branch_x, conv_loc)
        conv_low = conv_out.astype(BF16)
        rim_cells = [rim.fetch(conv_low) for rim in rims]
        gate_pre = jnp.dot(conv_low, own_dense, preferred_element_type=F32)
        for cells, dense in zip(rim_cells, rim_dense):
            gate_pre = gate_pre + jnp.dot(cells, dense, preferred_element_type=F32)
        mixed_low, states = scan_call(
            forward_scan_kernel,
            (shape((group_rows, channels), BF16), shape((group_rows, channels), F32)),
            conv_low,
            gate_pre,
            branch_y,
            soft,
            since,
        )
    middle, mid_rows = call_kernel(
        partial(middle_kernel, nbits),
        (shape((own_rows, width), F32), shape((group_rows, width), BF16)),
        scatter_scratch(own_rows, width, nbits) + gather_sems(nbits),
        1,
        rows_times(mixed_low, wout_loc).astype(BF16),
        tokens,
        gain_mid,
    )
    gate_val = jnp.dot(mid_rows, wg_loc, preferred_element_type=F32)
    up_val = jnp.dot(mid_rows, wu_loc, preferred_element_type=F32)
    hidden, act_pull = jax.vjp(geglu, gate_val, up_val)
    hidden_low = hidden.astype(BF16)
    grad_wd = inner_rows(cot_rows, hidden_low).astype(BF16)
    sum_wd = lax.psum_scatter(grad_wd, "dp", scatter_dimension=0, tiled=True)
    grad_wd, wd_loc = lax.optimization_barrier((grad_wd, wd_loc))
    d_hidden = jnp.dot(cot_rows, wd_loc, preferred_element_type=F32)
    d_gate, d_up = act_pull(d_hidden)
    d_gate = d_gate.astype(BF16)
    d_up = d_up.astype(BF16)
    grad_wg = inner_rows(mid_rows, d_gate).astype(BF16)
    sum_wg = lax.psum_scatter(grad_wg, "dp", scatter_dimension=0, tiled=True)
    grad_wu = inner_rows(mid_rows, d_up).astype(BF16)
    sum_wu = lax.psum_scatter(grad_wu, "dp", scatter_dimension=0, tiled=True)
    d_gate, d_up, grad_wg, grad_wu = lax.optimization_barrier((d_gate, d_up, grad_wg, grad_wu))
    d_mid_part = rows_back((d_gate, d_up), (wg_loc, wu_loc)).astype(BF16)
    d_middle, d_mixer, d_gain_mid = call_kernel(
        partial(turn_kernel, nbits),
        (
            shape((own_rows, width), F32),
            shape((group_rows, width), BF16),
            shape((8, width), F32),
        ),
        scatter_scratch(own_rows, width, nbits) + gather_sems(nbits),
        2,
        d_mid_part,
        cotangent,
        middle,
        gain_mid,
    )
    d_mixer, sum_wd = lax.optimization_barrier((d_mixer, sum_wd))
    d_mixed_in = jnp.dot(d_mixer, wout_loc, preferred_element_type=F32)
    unit = math.gcd(channels, block_size)
    ffn_part = rows_times(hidden_low, wd_loc).astype(BF16)
    merged = half_blocks and nbits <= 2
    if half_blocks:
        found = call_kernel(
            partial(recurrence_back_kernel, taps, nbits, merged),
            (
                shape((group_rows, 2 * channels), BF16),
                shape((channels // unit * 2, block_size, unit), BF16),
                shape((8, channels), F32),
            )
            + ((shape((own_rows, width), BF16),) if merged else ()),
            [
                pltpu.VMEM((group_rows, channels), F32),
                pltpu.VMEM((group_rows, 2 * channels), BF16),
                pltpu.VMEM((group_rows, unit), BF16),
                pltpu.VMEM((group_rows, unit), BF16),
                pltpu.VMEM((taps + 1, 8, channels), F32),
                pltpu.SemaphoreType.DMA((1,)),
                pltpu.SemaphoreType.DMA((1,)),
            ]
            + (scatter_scratch(own_rows, width, nbits) if merged else []),
            6,
            d_mixed_in,
            window,
            gate_pre,
            branches,
            states,
            taps_pad,
            soft,
            slope_soft,
            since,
            w_window,
            *((ffn_part, middle) if merged else ()),
        )
        d_branches, gate_grad, own_small = found[:3]
        d_branches, sum_wg = lax.optimization_barrier((d_branches, sum_wg))
        gate_grad = gate_grad.reshape(channels // unit * 2 * block_size, unit)
    else:
        d_conv, d_gate_low, d_branch_y, d_decay = scan_call(
            backward_scan_kernel,
            (
                shape((group_rows, channels), F32),
                shape((group_rows, 2 * channels), BF16),
                shape((group_rows, channels), BF16),
                shape((8, channels), F32),
            ),
            d_mixed_in,
            conv_low,
            gate_pre,
            branch_y,
            states,
            soft,
            slope_soft,
            since,
        )
        given = [rows_times(d_gate_low, dense).astype(BF16) for dense in rim_dense]
        taken = [rim.give(part) for rim, part in zip(rims, given)]
        d_conv_out = d_conv + rows_times(d_gate_low, own_dense)
        for rim, part in zip(rims, taken):
            d_conv_out = rim.add(d_conv_out, part)
        d_branch_x, grad_conv_loc = conv_pull(d_conv_out)
        d_branches = jnp.concatenate([d_branch_y, d_branch_x.astype(BF16)], axis=1)
        base = offset // block_size * block_size - rims[0].room
        window_rows = rims[0].window(channels)
        picked = jnp.zeros((window_rows, 2 * channels), F32)
        for first, cells in [(offset, conv_low)] + [(r.first, c) for r, c in zip(rims, rim_cells)]:
            part = inner_rows(cells, d_gate_low)
            same = same_block(first, cells.shape[1], offset, channels, block_size)
            part = jnp.where(jnp.concatenate([same, same], axis=1), part, 0.0)
            picked = lax.dynamic_update_slice(picked, part, (first - base, jnp.int32(0)))
        picked = picked.reshape(window_rows // block_size, block_size, 2, channels // unit, unit)
        gate_grad = picked.sum(axis=0).astype(BF16).transpose(2, 1, 0, 3)
        gate_grad = gate_grad.reshape(channels // unit * 2 * block_size, unit)
        own_small = jnp.concatenate(
            [
                grad_conv_loc,
                jnp.sum(d_decay, axis=0, keepdims=True),
                jnp.zeros((7 - taps, channels), F32),
            ],
            axis=0,
        )

    grad_wout = inner_rows(d_mixer, mixed_low).astype(BF16)
    sum_wout = lax.psum_scatter(grad_wout, "dp", scatter_dimension=0, tiled=True)
    grad_wyx = inner_rows(normed_rows, d_branches).astype(BF16)
    d_normed = rows_times(d_branches, wyx_loc).astype(BF16)
    d_normed, sum_wu = lax.optimization_barrier((d_normed, sum_wu))

    pieces = [halved(grad, ndp) for grad in (gate_grad, grad_wyx)]
    peers = ntensor - 1
    gate_rows = gate_grad.shape[0] // ndp
    dma = pltpu.SemaphoreType.DMA
    scratch = scatter_scratch(own_rows, width, nbits)
    scratch += line_scratch(ndp, gate_rows, unit)
    if tiled:
        scratch += line_scratch(ndp, dp_rows, channels) * 2
    else:
        scratch += line_scratch(ndp, dp_rows, 2 * channels)
    scratch += [
        pltpu.VMEM((8, width), F32),
        pltpu.VMEM((ntensor, 8, channels), F32),
        pltpu.VMEM((peers, 8, channels), F32),
        pltpu.VMEM((8, channels), F32),
        pltpu.VMEM((ndp - 1, 8, channels), F32),
    ]
    scratch += [dma((peers,)), dma((peers,)), dma((ndp - 1,)), dma((ndp - 1,))]
    scratch += [dma((peers,)), dma((peers,)), dma((peers + ndp,)), dma((peers + ndp,))]
    grad_input, sum_wy, sum_wx, gate_all, small_all = call_kernel(
        partial(leave_kernel, nbits, tiled),
        (shape((own_rows, width), F32),)
        + (shape((dp_rows, channels), F32),) * 2
        + (
            shape((ntensor, ndp, gate_rows, unit), BF16),
            shape((ntensor, 8, channels), F32),
        ),
        scratch,
        3,
        d_normed,
        tokens,
        d_middle,
        gain_in,
        own_small,
        d_gain_mid,
        *pieces,
        far_in=(6, 7),
    )
    if merged:
        mixed = found[3]
    else:
        (mixed,) = call_kernel(
            partial(result_kernel, nbits),
            (shape((own_rows, width), BF16),),
            scatter_scratch(own_rows, width, nbits),
            4,
            ffn_part,
            middle,
        )
    per_block = block_size // unit
    sum_gate = gate_all.reshape(nblocks, per_block, 2, block_size, unit)
    sum_gate = gate_layout(sum_gate)
    summed = small_all.transpose(1, 0, 2).reshape(8, width)
    return (
        mixed,
        grad_input,
        summed[6],
        sum_wy,
        sum_wx,
        summed[:taps],
        sum_gate,
        summed[taps],
        sum_wout.astype(F32),
        summed[7],
        sum_wg.astype(F32),
        sum_wu.astype(F32),
        sum_wd.astype(F32),
    )


def solution(mesh):
    split = P(("dp", "tensor"), None)
    weight = P("dp", "tensor")
    return jax.shard_map(
        body,
        mesh=mesh,
        in_specs=(
            split,
            P(("dp", "tensor")),
            split,
            P(),
            weight,
            weight,
            P(),
            P(),
            P(),
            weight,
            P(),
            weight,
            weight,
            weight,
        ),
        out_specs=(
            split,
            split,
            P(),
            weight,
            weight,
            P(),
            P(),
            P(),
            weight,
            P(),
            weight,
            weight,
            weight,
        ),
        check_vma=False,
    )
```

```python
import math
from functools import partial

import jax
import jax.numpy as jnp
from jax import lax
from jax.experimental import pallas as pl
from jax.experimental.pallas import tpu as pltpu
from jax.sharding import PartitionSpec as P

EPSILON = 1e-06
MESH = pl.DeviceIdType.MESH
VMEM_BYTES = 56 * 1024 * 1024
CHUNK = 16
F32 = jnp.float32
BF16 = jnp.bfloat16


def subsets(bits):
    found = [()]
    for bit in bits:
        found = found + [chosen + (bit,) for chosen in found]
    return found


def flipped(index, bits):
    for bit in bits:
        mine = (index // (1 << bit)) % 2
        index = index + (1 - 2 * mine) * (1 << bit)
    return index


def log2_of(count):
    assert count & (count - 1) == 0
    return count.bit_length() - 1


def greet(axis_bits):
    barrier = pltpu.get_barrier_semaphore()
    for axis, bit in axis_bits:
        peer = flipped(lax.axis_index(axis), (bit,))
        pl.semaphore_signal(barrier, inc=1, device_id={axis: peer}, device_id_type=MESH)
    pl.semaphore_wait(barrier, len(axis_bits))


def halves_of(nbits, columns):
    half = columns // 2
    ups = tuple(range(nbits))
    return ((ups, 0, half), (ups[::-1], half, half))


class Gather:
    def __init__(self, ref, rows, nbits, send_sems, recv_sems):
        self.ref, self.rows, self.nbits = ref, rows, nbits
        self.sems = (send_sems, recv_sems)
        self.me = lax.axis_index("tensor")
        self.plan = []
        number = 0
        for half, (order, at, width) in enumerate(halves_of(nbits, ref.shape[1])):
            for step, bit in enumerate(order):
                for known in subsets(order[:step]):
                    self.plan.append((half, step, known, bit, at, width, number))
                    number += 1
        self.count = number

    def copy(self, item):
        half, step, known, bit, at, width, number = item
        row = pl.multiple_of(flipped(self.me, known) * self.rows, self.rows)
        piece = self.ref.at[pl.ds(row, self.rows), pl.ds(at, width)]
        return pltpu.make_async_remote_copy(
            src_ref=piece,
            dst_ref=piece,
            send_sem=self.sems[0].at[number],
            recv_sem=self.sems[1].at[number],
            device_id={"tensor": flipped(self.me, (bit,))},
            device_id_type=MESH,
        )

    def begin(self):
        for item in sorted(self.plan, key=lambda it: it[1]):
            if item[2] == ():
                self.copy(item).start()

    def advance(self, step):
        for item in self.plan:
            half, at_step, known, bit, at, width, number = item
            if at_step == step:
                self.copy(item).wait_recv()
                block = known + (bit,)
                for later in self.plan:
                    if later[0] == half and set(later[2]) == set(block):
                        self.copy(later).start()

    def finish(self, step=0):
        for at_step in range(step, self.nbits):
            self.advance(at_step)
        for item in self.plan:
            self.copy(item).wait_send()


def gather_copies(nbits):
    return 2 * ((1 << nbits) - 1)


class Scatter:
    def __init__(self, ref, landed, staged, rows, nbits, send_sems, recv_sems):
        self.ref, self.landed, self.staged = ref, landed, staged
        self.rows, self.nbits = rows, nbits
        self.sems = (send_sems, recv_sems)
        self.me = lax.axis_index("tensor")
        self.plan, self.slot = [], {}
        number = 0
        for half, (order, at, width) in enumerate(halves_of(nbits, ref.shape[1])):
            for step, bit in enumerate(order):
                for rest in subsets(order[step + 1 :])[::-1]:
                    self.plan.append((half, step, rest, bit, at, width, number))
                    if step > 0:
                        self.slot[number] = len(self.slot)
                    number += 1

    def copy(self, item):
        half, step, rest, bit, at, width, number = item
        if step == 0:
            row = pl.multiple_of(flipped(self.me, rest + (bit,)) * self.rows, self.rows)
            source = self.ref.at[pl.ds(row, self.rows), pl.ds(at, width)]
        else:
            source = self.staged.at[self.slot[number]]
        return pltpu.make_async_remote_copy(
            src_ref=source,
            dst_ref=self.landed.at[number],
            send_sem=self.sems[0].at[number],
            recv_sem=self.sems[1].at[number],
            device_id={"tensor": flipped(self.me, (bit,))},
            device_id_type=MESH,
        )

    def begin(self):
        for item in sorted(self.plan, key=lambda it: (len(it[2]) == 0)):
            if item[1] == 0:
                self.copy(item).start()

    def partial_sum(self, half, block, before, row, size):
        at, width = halves_of(self.nbits, self.ref.shape[1])[half][1:]
        base = pl.multiple_of(flipped(self.me, block) * self.rows + row, size)
        total = self.ref[pl.ds(base, size), pl.ds(at, width)].astype(F32)
        for it in self.plan:
            if it[0] == half and it[1] < before and set(it[2]) == set(block):
                total = total + self.landed[it[6], pl.ds(row, size), :].astype(F32)
        return total

    def advance(self, step):
        for half in range(2):
            for item in self.plan:
                if item[0] == half and item[1] == step:
                    self.copy(item).wait_recv()
            for item in self.plan:
                if item[0] == half and item[1] == step + 1:

                    def fill(row, item=item):
                        value = self.partial_sum(
                            item[0], item[2] + (item[3],), item[1], row, CHUNK
                        )
                        where = (self.slot[item[6]], pl.ds(row, CHUNK))
                        self.staged[where + (slice(None),)] = value.astype(BF16)

                    chunks(self.rows, fill)
                    self.copy(item).start()

    def run(self):
        for step in range(self.nbits):
            self.advance(step)

    def total(self, row, size):
        return jnp.concatenate(
            [self.partial_sum(half, (), self.nbits, row, size) for half in range(2)], axis=1
        )

    def drain(self):
        for item in self.plan:
            self.copy(item).wait_send()


def scatter_scratch(rows, columns, nbits):
    copies = gather_copies(nbits)
    later = max(1, copies - (1 << nbits))
    return [
        pltpu.VMEM((copies, rows, columns // 2), BF16),
        pltpu.VMEM((later, rows, columns // 2), BF16),
        pltpu.SemaphoreType.DMA((copies,)),
        pltpu.SemaphoreType.DMA((copies,)),
    ]


def gather_sems(nbits):
    copies = gather_copies(nbits)
    return [pltpu.SemaphoreType.DMA((copies,)), pltpu.SemaphoreType.DMA((copies,))]


def tensor_bits(nbits):
    return [("tensor", bit) for bit in range(nbits)]


def rms_scale_of(values):
    return lax.rsqrt(jnp.mean(values * values, axis=-1, keepdims=True) + EPSILON)


def chunks(rows, body):
    def step(i, carry):
        body(pl.multiple_of(i * CHUNK, CHUNK))
        return carry

    lax.fori_loop(0, rows // CHUNK, step, 0)


def own_row(row, rows):
    return pl.multiple_of(lax.axis_index("tensor") * rows + row, CHUNK)


def dp_place():
    me = lax.axis_index("dp")
    return me // 2, me % 2, lax.axis_size("dp") // 2


def dp_index(chip, core):
    return chip * 2 + core


UP, DOWN = 1, -1


class LineGather:
    def __init__(self, own, whole, send_sems, recv_sems, columns=None):
        self.own, self.whole = own, whole
        self.sems = (send_sems, recv_sems)
        self.chip, self.core, self.chips = dp_place()
        self.rows = own.shape[0]
        self.columns = slice(None) if columns is None else columns

    def block(self, chip):
        row = pl.multiple_of(dp_index(chip, self.core) * self.rows, self.rows)
        return self.whole.at[pl.ds(row, self.rows), self.columns]

    def has(self, way, distance):
        return self.chip >= distance if way == UP else self.chip + distance < self.chips

    def number(self, way, distance):
        return (0 if way == UP else self.chips) + distance

    def along(self, way, distance):
        block = self.block(self.chip - way * distance)
        return pltpu.make_async_remote_copy(
            src_ref=self.own if distance == 0 else block,
            dst_ref=block,
            send_sem=self.sems[0].at[self.number(way, distance)],
            recv_sem=self.sems[1].at[self.number(way, distance + 1)],
            device_id={"dp": dp_index(self.chip + way, self.core)},
            device_id_type=MESH,
        )

    def arrival(self, way, distance):
        block = self.block(self.chip - way * distance)
        return pltpu.make_async_remote_copy(
            src_ref=block,
            dst_ref=block,
            send_sem=self.sems[0].at[self.number(way, distance)],
            recv_sem=self.sems[1].at[self.number(way, distance)],
            device_id={"dp": dp_index(self.chip + way, self.core)},
            device_id_type=MESH,
        )

    def across(self, way, distance):
        block = self.block(self.chip - way * distance)
        number = 2 * self.chips + self.number(way, distance)
        return pltpu.make_async_remote_copy(
            src_ref=self.own if distance == 0 else block,
            dst_ref=block,
            send_sem=self.sems[0].at[number],
            recv_sem=self.sems[1].at[number],
            device_id={"dp": dp_index(self.chip, 1 - self.core)},
            device_id_type=MESH,
        )

    def local(self):
        return pltpu.make_async_copy(
            self.own, self.block(self.chip), self.sems[0].at[4 * self.chips]
        )

    def begin(self):
        for way in (UP, DOWN):

            @pl.when(self.has(-way, 1))
            def _(way=way):
                self.along(way, 0).start()

        self.across(UP, 0).start()
        self.local().start()

    def pass_on(self, distance):
        for way in (UP, DOWN):

            @pl.when(self.has(way, distance))
            def _(way=way):
                self.arrival(way, distance).wait_recv()

                @pl.when(self.has(-way, 1))
                def _():
                    self.along(way, distance).start()

                self.across(way, distance).start()

    def finish(self):
        self.across(UP, 0).wait()
        self.local().wait()
        for way in (UP, DOWN):
            for distance in range(self.chips):

                @pl.when(self.has(way, distance) & self.has(-way, 1))
                def _(way=way, distance=distance):
                    self.along(way, distance).wait_send()

                if distance:

                    @pl.when(self.has(way, distance))
                    def _(way=way, distance=distance):
                        self.across(way, distance).wait()


def line_sems(ndp):
    chips = ndp // 2
    return [pltpu.SemaphoreType.DMA((4 * chips + 1,)), pltpu.SemaphoreType.DMA((4 * chips + 1,))]


def greet_peers(nbits, all_tensor, whole_dp):
    me = lax.axis_index("tensor")
    chip, core, chips = dp_place()
    barrier = pltpu.get_barrier_semaphore()

    def signal(target):
        pl.semaphore_signal(barrier, inc=1, device_id=target, device_id_type=MESH)

    met = 0
    for chosen in subsets(tuple(range(nbits))):
        if chosen and (all_tensor or len(chosen) == 1):
            signal({"tensor": flipped(me, chosen)})
            met += 1
    if whole_dp:
        for shift in range(chips):
            for turn in range(2):
                if (shift, turn) != (0, 0):
                    other = dp_index((chip + shift) % chips, core + turn * (1 - 2 * core))
                    signal({"dp": other})
                    met += 1
    else:
        signal({"dp": dp_index(chip, 1 - core)})
        met += 1

        for shift in sorted({1 % chips, chips - 1} - {0}):
            signal({"dp": dp_index((chip + shift) % chips, core)})
            met += 1

    pl.semaphore_wait(barrier, met)


def enter_kernel(
    nbits, parts_yx, tokens, seg, gain, *refs
):
    w_yx, w_out = refs[:parts_yx], refs[parts_yx]
    normed_all, seg_all, wyx_all, wout_all, s0, r0, s2, r2, l0, *line = refs[parts_yx + 1 :]
    rows = tokens.shape[0]
    me = lax.axis_index("tensor")
    peers = [chosen for chosen in subsets(tuple(range(nbits))) if chosen]
    greet_peers(nbits, True, False)
    width = wyx_all.shape[1] // parts_yx
    lines = [
        LineGather(
            own,
            wyx_all,
            line[2 * number],
            line[2 * number + 1],
            pl.ds(number * width, width) if parts_yx > 1 else None,
        )
        for number, own in enumerate(w_yx)
    ]
    lines.append(LineGather(w_out, wout_all, *line[2 * parts_yx : 2 * parts_yx + 2]))
    for item in lines:
        item.begin()

    def norm(row):
        values = tokens[pl.ds(row, CHUNK), :].astype(F32)
        scaled = values * rms_scale_of(values) * gain[...]
        normed_all[pl.ds(own_row(row, rows), CHUNK), :] = scaled.astype(BF16)

    chunks(rows, norm)
    gather = Gather(normed_all, rows, nbits, s0, r0)
    gather.begin()
    seg_own = pltpu.make_async_copy(seg, seg_all.at[me], l0.at[0])
    seg_own.start()
    seg_copies = [
        pltpu.make_async_remote_copy(
            src_ref=seg,
            dst_ref=seg_all.at[me],
            send_sem=s2.at[number],
            recv_sem=r2.at[number],
            device_id={"tensor": flipped(me, chosen)},
            device_id_type=MESH,
        )
        for number, chosen in enumerate(peers)
    ]
    for copy in seg_copies:
        copy.start()
    chips = lines[0].chips
    for item in lines:
        item.pass_on(1)
    gather.advance(0)
    for distance in range(2, chips):
        for item in lines:
            item.pass_on(distance)
    gather.finish(1)
    for item in lines:
        item.finish()
    for copy in seg_copies:
        copy.wait()
    seg_own.wait()


class Fetch:
    def __init__(self, nbits, cot, cot_all, s0, r0, l0):
        rows = cot.shape[0]
        own = pl.multiple_of(lax.axis_index("tensor") * rows, rows)
        self.local = pltpu.make_async_copy(cot, cot_all.at[pl.ds(own, rows), :], l0.at[0])
        self.gather = Gather(cot_all, rows, nbits, s0, r0)

    def begin(self):
        self.local.wait()
        self.gather.begin()

    def advance(self):
        self.gather.advance(0)

    def finish(self):
        self.gather.finish(1)


def fetch_scratch(nbits):
    return gather_sems(nbits) + [pltpu.SemaphoreType.DMA((1,))]


def fetch_kernel(nbits, cot, cot_all, *sems):
    greet(tensor_bits(nbits))
    fetch = Fetch(nbits, cot, cot_all, *sems)
    fetch.local.start()
    fetch.begin()
    fetch.advance()
    fetch.finish()


def middle_kernel(
    nbits, mixer, tokens, gain, middle, mid_all, landed, staged, s0, r0, s1, r1
):
    rows = tokens.shape[0]
    greet(tensor_bits(nbits))
    scatter = Scatter(mixer, landed, staged, rows, nbits, s0, r0)
    scatter.begin()
    scatter.run()

    def norm(row):
        values = tokens[pl.ds(row, CHUNK), :].astype(F32) + scatter.total(row, CHUNK)
        middle[pl.ds(row, CHUNK), :] = values
        scaled = values * rms_scale_of(values) * gain[...]
        mid_all[pl.ds(own_row(row, rows), CHUNK), :] = scaled.astype(BF16)

    chunks(rows, norm)
    gather = Gather(mid_all, rows, nbits, s1, r1)
    gather.begin()
    gather.finish()
    scatter.drain()


def result_kernel(nbits, ffn, middle, mixed, landed, staged, s0, r0):
    rows = middle.shape[0]
    greet(tensor_bits(nbits))
    scatter = Scatter(ffn, landed, staged, rows, nbits, s0, r0)
    scatter.begin()
    scatter.run()

    def add(row):
        values = middle[pl.ds(row, CHUNK), :] + scatter.total(row, CHUNK)
        mixed[pl.ds(row, CHUNK), :] = values.astype(BF16)

    chunks(rows, add)
    scatter.drain()


def norm_pull(values, gain, cotangent):
    scale = rms_scale_of(values)
    unit = values * scale
    inner = cotangent * gain
    back = scale * (inner - unit * jnp.mean(inner * unit, axis=-1, keepdims=True))
    return back, cotangent * unit


def eight_rows(values):
    total = values[0:8]
    for at in range(8, CHUNK, 8):
        total = total + values[at : at + 8]
    return total


def turn_kernel(
    nbits, d_norm, cot, middle, gain, d_middle, d_mixer, d_gain, landed, staged, s0, r0, s1, r1
):
    rows = middle.shape[0]
    greet(tensor_bits(nbits))
    scatter = Scatter(d_norm, landed, staged, rows, nbits, s0, r0)
    scatter.begin()
    d_gain[...] = jnp.zeros_like(d_gain)
    scatter.run()

    def pull(row):
        span = pl.ds(row, CHUNK)
        back, gains = norm_pull(middle[span, :], gain[...], scatter.total(row, CHUNK))
        values = cot[span, :].astype(F32) + back
        d_middle[span, :] = values
        d_mixer[pl.ds(own_row(row, rows), CHUNK), :] = values.astype(BF16)
        d_gain[...] += eight_rows(gains)

    chunks(rows, pull)
    gather = Gather(d_mixer, rows, nbits, s1, r1)
    gather.begin()
    gather.finish()
    scatter.drain()


class LineSum:
    def __init__(self, whole, kept, swapped, staged, landed, send_sems, recv_sems, columns=None):
        self.whole, self.kept, self.swapped = whole, kept, swapped
        self.staged, self.landed = staged, landed
        self.sems = (send_sems, recv_sems)
        self.columns = columns
        self.chip, self.core, self.chips = dp_place()
        self.rows = whole.shape[2]

    def half(self, core):
        if self.columns is None:
            return self.whole.at[:, core]
        return self.whole.at[:, core, :, self.columns]

    def local(self):
        return pltpu.make_async_copy(
            self.half(self.core), self.kept, self.sems[0].at[2 * self.chips]
        )

    def swap(self):
        return pltpu.make_async_remote_copy(
            src_ref=self.half(1 - self.core),
            dst_ref=self.swapped,
            send_sem=self.sems[0].at[0],
            recv_sem=self.sems[1].at[0],
            device_id={"dp": dp_index(self.chip, 1 - self.core)},
            device_id_type=MESH,
        )

    def has(self, way, distance):
        return self.chip + distance < self.chips if way == UP else self.chip >= distance

    def slot(self, way, distance):
        return (0 if way == UP else self.chips - 1) + distance

    def hop(self, way, distance):
        return pltpu.make_async_remote_copy(
            src_ref=self.staged.at[self.slot(way, distance - 1)],
            dst_ref=self.landed.at[self.slot(way, distance - 1)],
            send_sem=self.sems[0].at[1 + self.slot(way, distance - 1)],
            recv_sem=self.sems[1].at[1 + self.slot(way, distance - 1)],
            device_id={"dp": dp_index(self.chip + way, self.core)},
            device_id_type=MESH,
        )

    def arrival(self, way, distance):
        number = self.slot(way, distance)
        return pltpu.make_async_remote_copy(
            src_ref=self.landed.at[number],
            dst_ref=self.landed.at[number],
            send_sem=self.sems[0].at[1 + number],
            recv_sem=self.sems[1].at[1 + number],
            device_id={"dp": dp_index(self.chip - way, self.core)},
            device_id_type=MESH,
        )

    def begin(self):
        self.swap().start()
        self.local().start()

    def both(self, chip, span):
        return self.kept[chip, span, :].astype(F32) + self.swapped[chip, span, :].astype(F32)

    def send(self, distance):
        if distance == self.chips - 1:
            self.local().wait()
            self.swap().wait_recv()
        for way in (UP, DOWN):

            @pl.when(self.has(way, distance))
            def _(way=way):
                chip = self.chip + way * distance
                slot = self.slot(way, distance - 1)

                def first(row):
                    span = pl.ds(row, CHUNK)
                    self.staged[slot, span, :] = self.both(chip, span).astype(BF16)

                def later(row):
                    span = pl.ds(row, CHUNK)
                    total = self.both(chip, span) + self.landed[
                        self.slot(way, distance), span, :
                    ].astype(F32)
                    self.staged[slot, span, :] = total.astype(BF16)

                if distance == self.chips - 1:
                    chunks(self.rows, first)
                else:

                    @pl.when(self.has(-way, 1))
                    def _():
                        self.arrival(way, distance).wait_recv()
                        chunks(self.rows, later)

                    @pl.when(jnp.logical_not(self.has(-way, 1)))
                    def _():
                        chunks(self.rows, first)

                self.hop(way, distance).start()

    def finish(self, store):
        below, above = self.has(DOWN, 1), self.has(UP, 1)

        def fill(slots):
            for way in slots:
                self.arrival(way, 0).wait_recv()

            def one(row):
                span = pl.ds(row, CHUNK)
                total = self.both(self.chip, span)
                for way in slots:
                    total = total + self.landed[self.slot(way, 0), span, :].astype(F32)
                store(span, total)

            chunks(self.rows, one)

        @pl.when(below & above)
        def _():
            fill((UP, DOWN))

        @pl.when(jnp.logical_not(above))
        def _():
            fill((UP,))

        @pl.when(jnp.logical_not(below))
        def _():
            fill((DOWN,))

    def drain(self):
        self.swap().wait_send()
        for way in (UP, DOWN):
            for distance in range(1, self.chips):

                @pl.when(self.has(way, distance))
                def _(way=way, distance=distance):
                    self.hop(way, distance).wait_send()


def line_scratch(ndp, rows, columns):
    chips = ndp // 2
    return [
        pltpu.VMEM((chips, rows, columns), BF16),
        pltpu.VMEM((chips, rows, columns), BF16),
        pltpu.VMEM((2 * chips - 2, rows, columns), BF16),
        pltpu.VMEM((2 * chips - 2, rows, columns), BF16),
        pltpu.SemaphoreType.DMA((2 * chips + 1,)),
        pltpu.SemaphoreType.DMA((2 * chips + 1,)),
    ]


RING = 6


def leave_kernel(nbits, tiled, *refs):
    refs = list(refs)

    def take(count):
        taken = refs[:count]
        del refs[:count]
        return taken

    d_norm, tokens, d_middle, gain, own_small, d_gain_mid = take(6)
    pieces = take(2)
    grad_input, sum_y, sum_x, gate_all, small_all = take(5)
    landed, staged, s0, r0 = take(4)
    share = small_all.shape[2]
    rings = [LineSum(pieces[0], *take(RING))]
    if tiled:
        for at in (0, share):
            rings.append(LineSum(pieces[1], *take(RING), pl.ds(at, share)))
    else:
        rings.append(LineSum(pieces[1], *take(RING)))
    d_gain, gains, gains_landed, small, small_landed = take(5)
    gain_s, gain_r, vec_s, vec_r, join_s, join_r, gate_s, gate_r = take(8)
    rows = tokens.shape[0]
    me = lax.axis_index("tensor")
    chip, core, chips = dp_place()
    peers = [chosen for chosen in subsets(tuple(range(nbits))) if chosen]
    others = [(shift, turn) for shift in range(chips) for turn in range(2)][1:]
    greet_peers(nbits, True, True)
    for ring in rings:
        ring.begin()
    scatter = Scatter(d_norm, landed, staged, rows, nbits, s0, r0)
    scatter.begin()
    d_gain[...] = jnp.zeros_like(d_gain)
    far = list(range(chips - 1, 0, -1))
    for ring in rings:
        ring.send(far[0])
    if len(far) > 1:
        rings[0].send(far[1])
    scatter.advance(0)
    if len(far) > 1:
        for ring in rings[1:]:
            ring.send(far[1])
    for distance in far[2:]:
        rings[0].send(distance)
    for step in range(1, nbits):
        scatter.advance(step)

    def pull(row):
        span = pl.ds(row, CHUNK)
        back, parts = norm_pull(
            tokens[span, :].astype(F32), gain[...], scatter.total(row, CHUNK)
        )
        grad_input[span, :] = d_middle[span, :] + back
        d_gain[...] += eight_rows(parts)

    chunks(rows, pull)
    def store_gate(span, value):
        gate_all[me, chip, core, span, :] = value.astype(BF16)

    def gate_copy(number, ref, target):
        return pltpu.make_async_remote_copy(
            src_ref=ref,
            dst_ref=ref,
            send_sem=gate_s.at[number],
            recv_sem=gate_r.at[number],
            device_id=target,
            device_id_type=MESH,
        )

    def gate_line(shift):
        target = {"dp": dp_index((chip + shift) % chips, core)}
        return gate_copy(shift - 1, gate_all.at[me, chip, core], target)

    def gate_tensor(number, chosen):
        target = {"tensor": flipped(me, chosen)}
        return gate_copy(chips - 1 + number, gate_all.at[me, :, core], target)

    def gate_core():
        target = {"dp": dp_index(chip, 1 - core)}
        return gate_copy(chips - 1 + len(peers), gate_all.at[:, :, core], target)

    def start_gate():
        rings[0].finish(store_gate)
        for shift in range(1, chips):
            gate_line(shift).start()

    top = jnp.sum(d_gain[...], axis=0, keepdims=True)
    low = jnp.sum(d_gain_mid[...], axis=0, keepdims=True)
    place8 = lax.broadcasted_iota(jnp.int32, (8, share), 0)
    for index in range(1 << nbits):
        span = slice(index * share, (index + 1) * share)
        gains[index] = jnp.where(
            place8 == 6, top[:, span], jnp.where(place8 == 7, low[:, span], 0.0)
        )

    def gain_copy(number, chosen):
        peer = flipped(me, chosen)
        return pltpu.make_async_remote_copy(
            src_ref=gains.at[peer],
            dst_ref=gains_landed.at[number],
            send_sem=gain_s.at[number],
            recv_sem=gain_r.at[number],
            device_id={"tensor": peer},
            device_id_type=MESH,
        )

    for number, chosen in enumerate(peers):
        gain_copy(number, chosen).start()
    start_gate()
    for distance in far[2:]:
        for ring in rings[1:]:
            ring.send(distance)
    total = own_small[...] + gains[me]
    for number, chosen in enumerate(peers):
        gain_copy(number, chosen).wait_recv()
        total = total + gains_landed[number]
    small[...] = total

    def vec_copy(number, shift, turn):
        other = dp_index((chip + shift) % chips, core + turn * (1 - 2 * core))
        return pltpu.make_async_remote_copy(
            src_ref=small,
            dst_ref=small_landed.at[number],
            send_sem=vec_s.at[number],
            recv_sem=vec_r.at[number],
            device_id={"dp": other},
            device_id_type=MESH,
        )

    for number, (shift, turn) in enumerate(others):
        vec_copy(number, shift, turn).start()

    for shift in range(1, chips):
        gate_line(shift).wait_recv()
    for number, chosen in enumerate(peers):
        gate_tensor(number, chosen).start()
    total = small[...]
    for number, (shift, turn) in enumerate(others):
        vec_copy(number, shift, turn).wait_recv()
        total = total + small_landed[number]
    small_all[me] = total

    def join_copy(number, chosen):
        return pltpu.make_async_remote_copy(
            src_ref=small_all.at[me],
            dst_ref=small_all.at[me],
            send_sem=join_s.at[number],
            recv_sem=join_r.at[number],
            device_id={"tensor": flipped(me, chosen)},
            device_id_type=MESH,
        )

    for number, chosen in enumerate(peers):
        join_copy(number, chosen).start()
    for number, chosen in enumerate(peers):
        gate_tensor(number, chosen).wait_recv()
    gate_core().start()

    def store_in(*targets):
        def store(span, value):
            for number, ref in enumerate(targets):
                ref[span, :] = value[:, number * share : (number + 1) * share]

        return store

    if tiled:
        rings[1].finish(store_in(sum_y))
        rings[2].finish(store_in(sum_x))
    else:
        rings[1].finish(store_in(sum_y, sum_x))
    gate_core().wait()
    for shift in range(1, chips):
        gate_line(shift).wait_send()
    for number, chosen in enumerate(peers):
        gate_tensor(number, chosen).wait_send()
        gain_copy(number, chosen).wait_send()
        join_copy(number, chosen).wait()
    for number, (shift, turn) in enumerate(others):
        vec_copy(number, shift, turn).wait_send()
    scatter.drain()
    for ring in rings:
        ring.drain()


def in_vmem(count):
    return [pl.BlockSpec(memory_space=pltpu.VMEM)] * count


def call_kernel(kernel, outs, scratch, number, *operands, far_in=(), far_out=(), cost_us=1):
    vmem = pl.BlockSpec(memory_space=pltpu.VMEM)
    far = pl.BlockSpec(memory_space=pl.ANY)
    return pl.pallas_call(
        kernel,
        out_shape=outs,
        in_specs=[far if i in far_in else vmem for i in range(len(operands))],
        out_specs=tuple(far if i in far_out else vmem for i in range(len(outs))),
        scratch_shapes=scratch,
        cost_estimate=pl.CostEstimate(
            flops=0, bytes_accessed=cost_us * 1_000_000, transcendentals=0
        ),
        compiler_params=pltpu.CompilerParams(
            collective_id=number, has_side_effects=True, vmem_limit_bytes=VMEM_BYTES
        ),
    )(*operands)


def sigmoid(values):
    return 1.0 / (1.0 + jnp.exp(-values))


def one_minus_exp(values):
    series = values / 7.0 + 1.0
    for order in (6.0, 5.0, 4.0, 3.0, 2.0):
        series = 1.0 + series * values / order
    return jnp.where(values > -0.3, -values * series, 1.0 - jnp.exp(values))


GELU_K = 0.7978845608028654
GELU_C = 0.044715


def gelu_parts(values):
    square = values * values
    bent = jnp.tanh(GELU_K * values * (1.0 + GELU_C * square))
    gelu = 0.5 * values * (1.0 + bent)
    slope = 0.5 * (1.0 + bent) + 0.5 * values * (1.0 - bent * bent) * GELU_K * (
        1.0 + 3.0 * GELU_C * square
    )
    return gelu, slope


def gate_terms(gate_a, gate_x, soft, since):
    sig_a = sigmoid(gate_a)
    sig_x = sigmoid(gate_x)
    log_decay = -8.0 * sig_a * soft
    decay = jnp.exp(log_decay)
    scale = jnp.sqrt(one_minus_exp(2.0 * log_decay))
    keep = since > 0.5
    return sig_a, sig_x, decay, jnp.where(keep, scale, 1.0), keep


def scan_down(decay, value, carry):
    place = lax.broadcasted_iota(jnp.int32, decay.shape, 0)
    for shift in (1, 2, 4):
        past = place >= shift
        moved = pltpu.roll(value, shift, 0)
        value = jnp.where(past, decay * moved + value, value)
        decay = jnp.where(past, decay * pltpu.roll(decay, shift, 0), decay)
    return decay * carry + value


def scan_up(decay, value, carry):
    place = lax.broadcasted_iota(jnp.int32, decay.shape, 0)
    factor = jnp.where(place < 7, pltpu.roll(decay, 7, 0), 1.0)
    for shift in (1, 2, 4):
        past = place < 8 - shift
        moved = pltpu.roll(value, 8 - shift, 0)
        value = jnp.where(past, factor * moved + value, value)
        factor = jnp.where(past, factor * pltpu.roll(factor, 8 - shift, 0), factor)
    return factor * carry + value


def forward_scan(conv_rows, gates, branch_y, soft, since, mixed, states, between=()):
    total_rows, width = states.shape

    def step(i, carry):
        row = pl.multiple_of(i * CHUNK, CHUNK)
        span = pl.ds(row, CHUNK)
        values = conv_rows(span).astype(F32)
        kept = []
        for at in range(0, CHUNK, 8):
            tile = pl.ds(row + at, 8)
            sig_a, sig_x, decay, scale, keep = gate_terms(
                gates[tile, :width], gates[tile, width:], soft[...], since[tile, :]
            )
            given = values[at : at + 8] * sig_x * scale
            state = scan_down(jnp.where(keep, decay, 0.0), given, carry)
            carry = state[7:8]
            states[tile, :] = state
            kept.append(state * gelu_parts(branch_y[tile, :])[0])
        mixed[span, :] = jnp.concatenate(kept, axis=0).astype(BF16)
        return carry

    steps, stretches = total_rows // CHUNK, len(between) + 1
    carry = jnp.zeros((1, width), F32)
    for stretch in range(stretches):
        first, last = stretch * steps // stretches, (stretch + 1) * steps // stretches
        carry = lax.fori_loop(first, last, step, carry)
        if stretch < len(between):
            between[stretch]()


def forward_scan_kernel(conv, gates, branch_y, soft, since, mixed, states):
    forward_scan(lambda span: conv[span, :], gates, branch_y, soft, since, mixed, states)


def backward_scan(
    d_mixed, conv_rows, gates, branch_y, states, soft, slope_soft, since, d_conv, d_gates, d_branch, d_decay
):
    total_rows, width = states.shape
    d_decay[...] = jnp.zeros_like(d_decay)

    def step(i, carry):
        row = pl.multiple_of(total_rows - CHUNK - i * CHUNK, CHUNK)
        span = pl.ds(row, CHUNK)
        values = conv_rows(span).astype(F32)
        kept = []
        for at in range(CHUNK - 8, -1, -8):
            tile = pl.ds(row + at, 8)
            soft_row = soft[...]
            sig_a, sig_x, decay, scale, keep = gate_terms(
                gates[tile, :width], gates[tile, width:], soft_row, since[tile, :]
            )
            value = values[at : at + 8]
            gelu, slope = gelu_parts(branch_y[tile, :])
            state = states[tile, :]
            upper = d_mixed[tile, :]
            held = jnp.where(keep, decay, 0.0)
            lam = scan_up(held, upper * gelu, carry)
            carry = held[0:1] * lam[0:1]
            d_conv[tile, :] = lam * sig_x * scale
            d_x = lam * value * scale * sig_x * (1.0 - sig_x)
            given = value * sig_x
            d_log = lam * (state - given * scale - given * decay * decay / scale)
            d_log = jnp.where(keep, d_log, 0.0)
            d_a = d_log * (-8.0 * soft_row) * sig_a * (1.0 - sig_a)
            d_decay[...] += d_log * (-8.0 * sig_a) * slope_soft[...]
            kept.append((d_a, d_x, upper * state * slope))
        kept = kept[::-1]
        d_gates[span, :width] = jnp.concatenate([k[0] for k in kept], axis=0).astype(BF16)
        d_gates[span, width:] = jnp.concatenate([k[1] for k in kept], axis=0).astype(BF16)
        d_branch[span, :] = jnp.concatenate([k[2] for k in kept], axis=0).astype(BF16)
        return carry

    lax.fori_loop(0, total_rows // CHUNK, step, jnp.zeros((1, width), F32))


def backward_scan_kernel(
    d_mixed, conv, gates, branch_y, states, soft, slope_soft, since, d_conv, d_gates, d_branch, d_decay
):
    backward_scan(
        d_mixed,
        lambda span: conv[span, :],
        gates,
        branch_y,
        states,
        soft,
        slope_soft,
        since,
        d_conv,
        d_gates,
        d_branch,
        d_decay,
    )


def times_transposed(left, right):
    return lax.dot_general(left, right, (((1,), (1,)), ((), ())), preferred_element_type=F32)


class HalfBlocks:
    def __init__(self, channels, block):
        self.odd = lax.axis_index("tensor") % 2
        self.half = block // 2
        self.block = block
        self.count = channels // block + 1
        self.channels = channels
        self.own = pl.multiple_of(self.odd * self.half, self.half)
        self.shared = (1 - self.odd) * (self.count - 1)
        self.mine_in_block = pl.multiple_of(self.odd * self.half, self.half)
        self.other_in_block = pl.multiple_of((1 - self.odd) * self.half, self.half)
        self.mine = pl.multiple_of((1 - self.odd) * (channels - self.half), self.half)
        self.pair = {"tensor": lax.axis_index("tensor") + 1 - 2 * self.odd}

    def full(self, index):
        block = index + self.odd
        return block, pl.multiple_of(index * self.block + self.odd * self.half, self.half)

    def span(self, block):
        return pl.ds(pl.multiple_of(block * self.block, self.block), self.block)

    def shared_part(self, start):
        return pl.ds(pl.multiple_of(self.shared * self.block + start, self.half), self.half)


PART = 256


def parts(rows, body):
    def step(i, carry):
        body(pl.ds(pl.multiple_of(i * PART, PART), PART))
        return carry

    lax.fori_loop(0, rows // PART, step, 0)


def recurrence_kernel(
    taps,
    nbits,
    branches,
    tap_rows,
    soft,
    since,
    weights,
    cot,
    mixed,
    states,
    window,
    gates,
    cot_all,
    send,
    recv,
    *sems,
):
    total_rows, width = states.shape
    block = weights.shape[2]
    place = HalfBlocks(width, block)
    branch_y, branch_x = branches.at[:, :width], branches.at[:, width:]
    greet(tensor_bits(nbits))
    fetch = Fetch(nbits, cot, cot_all, *sems)
    fetch.local.start()

    def conv(i, before):
        row = pl.multiple_of(i * CHUNK, CHUNK)
        kept = []
        for at in range(0, CHUNK, 8):
            tile = pl.ds(row + at, 8)
            values = branch_x[tile, :]
            line = lax.broadcasted_iota(jnp.int32, values.shape, 0)
            total = values * tap_rows[0:1, :]
            for tap in range(1, taps):
                moved = jnp.where(
                    line < tap, pltpu.roll(before, tap, 0), pltpu.roll(values, tap, 0)
                )
                moved = jnp.where(since[tile, :] > tap - 0.5, moved, 0.0)
                total = total + moved * tap_rows[tap : tap + 1, :]
            kept.append(total)
            before = values
        window[pl.ds(row, CHUNK), pl.ds(place.own, width)] = jnp.concatenate(
            kept, axis=0
        ).astype(BF16)
        return before

    lax.fori_loop(0, total_rows // CHUNK, conv, jnp.zeros((8, width), F32))
    source = window.at[:, place.shared_part(place.mine_in_block)]
    away = pl.multiple_of(place.odd * (place.count - 1) * block + place.mine_in_block, place.half)
    rim = pltpu.make_async_remote_copy(
        src_ref=source,
        dst_ref=window.at[:, pl.ds(away, place.half)],
        send_sem=send.at[0],
        recv_sem=recv.at[0],
        device_id=place.pair,
        device_id_type=MESH,
    )
    rim.start()
    fetch.begin()

    def full(span):
        for index in range(place.count - 1):
            number, at = place.full(index)
            cells = window[span, place.span(number)]
            for s in range(2):
                gates[span, pl.ds(s * width + at, block)] = jnp.dot(
                    cells, weights[s, number], preferred_element_type=F32
                )

    parts(total_rows, full)
    rim.wait()

    def shared(span):
        cells = window[span, place.span(place.shared)]
        for s in range(2):
            gates[span, pl.ds(s * width + place.mine, place.half)] = jnp.dot(
                cells,
                weights[s, place.shared, :, pl.ds(place.mine_in_block, place.half)],
                preferred_element_type=F32,
            )

    parts(total_rows, shared)
    forward_scan(
        lambda span: window[span, pl.ds(place.own, width)],
        gates,
        branch_y,
        soft,
        since,
        mixed,
        states,
        [fetch.advance],
    )
    fetch.finish()


def recurrence_back_kernel(
    taps,
    nbits,
    with_ffn,
    d_mixed,
    window,
    gates,
    branches,
    states,
    tap_rows,
    soft,
    slope_soft,
    since,
    weights,
    *refs,
):
    refs = list(refs)

    def take(count):
        taken = refs[:count]
        del refs[:count]
        return taken

    ffn, middle = take(2) if with_ffn else (None, None)
    d_branches, gate_grad, own_small = take(3)
    mixed = take(1)[0] if with_ffn else None
    d_conv, d_gates, given, taken, sums, send, recv = take(7)
    total_rows, width = states.shape
    block = weights.shape[2]
    place = HalfBlocks(width, block)
    half = place.half
    branch_y, branch_x = branches.at[:, :width], branches.at[:, width:]
    d_branch_y, d_branch_x = d_branches.at[:, :width], d_branches.at[:, width:]
    greet(tensor_bits(nbits))
    if with_ffn:
        scatter = Scatter(ffn, *take(2), middle.shape[0], nbits, *take(2))
        scatter.begin()
    backward_scan(
        d_mixed,
        lambda span: window[span, pl.ds(place.own, width)],
        gates,
        branch_y,
        states,
        soft,
        slope_soft,
        since,
        d_conv,
        d_gates,
        d_branch_y,
        sums.at[taps],
    )

    def to_pair(span):
        total = jnp.zeros((PART, half), F32)
        for s in range(2):
            total = total + times_transposed(
                d_gates[span, pl.ds(s * width + place.mine, half)],
                weights[
                    s,
                    place.shared,
                    pl.ds(place.other_in_block, half),
                    pl.ds(place.mine_in_block, half),
                ],
            )
        given[span, :] = total.astype(BF16)

    parts(total_rows, to_pair)
    rim = pltpu.make_async_remote_copy(
        src_ref=given,
        dst_ref=taken,
        send_sem=send.at[0],
        recv_sem=recv.at[0],
        device_id=place.pair,
        device_id_type=MESH,
    )
    rim.start()

    def full(span):
        for index in range(place.count - 1):
            number, at = place.full(index)
            total = d_conv[span, pl.ds(at, block)]
            for s in range(2):
                total = total + times_transposed(
                    d_gates[span, pl.ds(s * width + at, block)], weights[s, number]
                )
            d_conv[span, pl.ds(at, block)] = total
        total = d_conv[span, pl.ds(place.mine, half)]
        for s in range(2):
            total = total + times_transposed(
                d_gates[span, pl.ds(s * width + place.mine, half)],
                weights[
                    s,
                    place.shared,
                    pl.ds(place.mine_in_block, half),
                    pl.ds(place.mine_in_block, half),
                ],
            )
        d_conv[span, pl.ds(place.mine, half)] = total

    parts(total_rows, full)
    if with_ffn:
        scatter.advance(0)
    units = width // half
    for index in range(units):
        number = (index + place.odd) // 2
        cells = window[:, place.span(number)]
        both = jnp.concatenate(
            [d_gates[:, s * width + index * half : s * width + (index + 1) * half] for s in range(2)],
            axis=1,
        )
        found = lax.dot_general(
            cells, both, (((0,), (0,)), ((), ())), preferred_element_type=F32
        ).astype(BF16)
        gate_grad[2 * index] = found[:, :half]
        gate_grad[2 * index + 1] = found[:, half:]
    rim.wait()

    def add(span):
        d_conv[span, pl.ds(place.mine, half)] += taken[span, :].astype(F32)

    parts(total_rows, add)
    for tap in range(taps):
        sums[tap] = jnp.zeros((8, width), F32)

    def conv(i, after):
        row = pl.multiple_of(total_rows - CHUNK - i * CHUNK, CHUNK)
        kept = []
        for at in range(CHUNK - 8, -1, -8):
            tile = pl.ds(row + at, 8)
            values = d_conv[tile, :]
            line = lax.broadcasted_iota(jnp.int32, values.shape, 0)
            below = branch_x[tile, :]
            higher = pl.multiple_of((row + at - 8 + total_rows) % total_rows, 8)
            above = branch_x[pl.ds(higher, 8), :]
            total = values * tap_rows[0:1, :]
            sums[0] += values * below
            masked = []
            for tap in range(1, taps):
                here = jnp.where(since[tile, :] > tap - 0.5, values, 0.0)
                masked.append(here)
                moved = jnp.where(
                    line < 8 - tap,
                    pltpu.roll(here, 8 - tap, 0),
                    pltpu.roll(after[tap - 1], 8 - tap, 0),
                )
                total = total + moved * tap_rows[tap : tap + 1, :]
                source = jnp.where(
                    line < tap, pltpu.roll(above, tap, 0), pltpu.roll(below, tap, 0)
                )
                sums[tap] += here * source
            after = tuple(masked)
            kept.append(total)
        d_branch_x[pl.ds(row, CHUNK), :] = jnp.concatenate(kept[::-1], axis=0).astype(BF16)
        return after

    none = jnp.zeros((8, width), F32)
    lax.fori_loop(0, total_rows // CHUNK, conv, (none,) * (taps - 1))
    line = lax.broadcasted_iota(jnp.int32, (8, width), 0)
    total = jnp.zeros((8, width), F32)
    for tap in range(taps + 1):
        row = jnp.sum(sums[tap], axis=0, keepdims=True)
        total = jnp.where(line == tap, row, total)
    own_small[...] = total
    if with_ffn:
        for step in range(1, nbits):
            scatter.advance(step)

        def result(row):
            span = pl.ds(row, CHUNK)
            mixed[span, :] = (middle[span, :] + scatter.total(row, CHUNK)).astype(BF16)

        chunks(middle.shape[0], result)
        scatter.drain()


def finish_kernel(taps, gates, small, in_y, in_x, whole, out_y, out_x, conv, decay, gain_in, gain_mid):
    blocks = whole.shape[1]
    pieces = gates.shape[0] // blocks

    def block(n, carry):
        for piece in range(pieces):
            for s in range(2):
                whole[s, n, :, piece * 128 : (piece + 1) * 128] = gates[
                    n * pieces + piece, s
                ].astype(F32)
        return carry

    lax.fori_loop(0, blocks, block, 0)
    out_y[...] = in_y[...]
    out_x[...] = in_x[...]
    share = small.shape[2]
    for index in range(small.shape[0]):
        span = slice(index * share, (index + 1) * share)
        conv[:, span] = small[index, :taps, :]
        decay[:, span] = small[index, taps : taps + 1, :]
        gain_in[:, span] = small[index, 6:7, :]
        gain_mid[:, span] = small[index, 7:8, :]


def finish(gate_all, small_all, sum_y, sum_x, taps, gate_shape):
    _, blocks, block, _ = gate_shape
    unit = gate_all.shape[-1]
    pieces = block // unit
    width = small_all.shape[0] * small_all.shape[2]
    if unit != 128:
        whole = gate_all.reshape(blocks, pieces, 2, block, unit).transpose(2, 0, 3, 1, 4)
        summed = small_all.transpose(1, 0, 2).reshape(8, width)
        whole = whole.reshape(gate_shape).astype(F32)
        rows = (summed[:taps], summed[taps], summed[6], summed[7])
        return (whole, sum_y, sum_x) + rows
    shape = jax.ShapeDtypeStruct
    row = shape((1, width), F32)
    found = scan_call(
        partial(finish_kernel, taps),
        (
            shape(gate_shape, F32),
            shape(sum_y.shape, F32),
            shape(sum_x.shape, F32),
            shape((taps, width), F32),
            row,
            row,
            row,
        ),
        gate_all.reshape(blocks * pieces, 2, block, unit),
        small_all,
        sum_y,
        sum_x,
    )
    return found[:4] + tuple(one.reshape(width) for one in found[4:])


def scan_call(kernel, outs, *operands):
    return pl.pallas_call(
        kernel,
        out_shape=outs,
        in_specs=in_vmem(len(operands)),
        out_specs=tuple(in_vmem(len(outs))),
        compiler_params=pltpu.CompilerParams(vmem_limit_bytes=VMEM_BYTES),
    )(*operands)


class Rim:
    def __init__(self, route, back, source, first, width, room):
        self.route, self.back = route, back
        self.source, self.first, self.width = source, first, width
        self.room = room

    def fetch(self, values):
        part = lax.dynamic_slice_in_dim(values, self.source, self.width, 1)
        return lax.ppermute(part, "tensor", self.route)

    def give(self, part):
        return lax.ppermute(part, "tensor", self.back)

    def add(self, values, part):
        zeros = jnp.zeros(values.shape, F32)
        return values + lax.dynamic_update_slice_in_dim(
            zeros, part.astype(F32), self.source, 1
        )

    def window(self, channels):
        return (channels // self.width + 4) * self.width


def gate_rims(channels, block_size, ntensor, offset):
    up = [(i, i + 1) for i in range(ntensor - 1)]
    down = [(i + 1, i) for i in range(ntensor - 1)]
    last = jnp.int32(channels - block_size)
    return [
        Rim(up, down, last, offset - block_size, block_size, block_size),
        Rim(down, up, jnp.int32(0), offset + channels, block_size, block_size),
    ]


def same_block(first, count, offset, channels, block_size):
    rows = (first + jnp.arange(count, dtype=jnp.int32))[:, None]
    columns = (offset + jnp.arange(channels, dtype=jnp.int32))[None, :]
    return (rows + block_size) // block_size == (columns + block_size) // block_size


def gate_dense(gate_w, offset, first, count):
    block_size = gate_w.shape[2]
    total = gate_w.shape[1] * block_size
    channels = total // lax.axis_size("tensor")
    columns = gate_w.transpose(2, 0, 1, 3).reshape(block_size, 2, total)
    columns = lax.dynamic_slice_in_dim(columns, offset, channels, 2)
    copies = -(-count // block_size) + 1
    tall = jnp.concatenate([columns] * copies, axis=0)
    tall = lax.dynamic_slice_in_dim(tall, (first + block_size) % block_size, count, 0)
    same = same_block(first, count, offset, channels, block_size)
    dense = jnp.where(same[:, None, :], tall, jnp.zeros_like(tall))
    return dense.reshape(count, 2 * channels)


def doc_starts(seg_ids, seq_len):
    places = jnp.arange(seg_ids.shape[0], dtype=jnp.int32)
    before = jnp.concatenate([seg_ids[:1], seg_ids[:-1]])
    resets = (places % seq_len == 0) | (seg_ids != before)
    starts = lax.cummax(jnp.where(resets, places, jnp.zeros_like(places)), axis=0)
    return starts


def causal_conv(starts, values, kernel):
    places = jnp.arange(values.shape[0], dtype=jnp.int32)
    total = values * kernel[0]
    for offset_k in range(1, kernel.shape[0]):
        moved = jnp.concatenate(
            [jnp.zeros((offset_k, values.shape[1]), values.dtype), values[:-offset_k]], axis=0
        )
        valid = (places - offset_k >= starts)[:, None]
        total = total + jnp.where(valid, moved, jnp.zeros_like(moved)) * kernel[offset_k]
    return total


def geglu(gate_val, up_val):
    return jax.nn.gelu(gate_val, approximate=True) * up_val


def rows_times(left, right):
    return lax.dot_general(left, right, (((1,), (1,)), ((), ())), preferred_element_type=F32)


def rows_back(lefts, rights):
    total = rows_times(lefts[0], rights[0])
    return total + rows_times(lefts[1], rights[1])


def inner_rows(left, right):
    return lax.dot_general(left, right, (((0,), (0,)), ((), ())), preferred_element_type=F32)


def halved(grad, ndp):
    return grad.reshape(ndp // 2, 2, grad.shape[0] // ndp, grad.shape[1])


def body(
    tokens,
    segments,
    cotangent,
    norm_gain,
    w_y,
    w_x,
    conv_w,
    gate_w,
    decay_param,
    w_out,
    mlp_gain,
    w_gate,
    w_up,
    w_down,
):
    ntensor = lax.axis_size("tensor")
    ndp = lax.axis_size("dp")
    nbits = log2_of(ntensor)
    tindex = lax.axis_index("tensor")
    own_rows, width = tokens.shape
    group_rows = own_rows * ntensor
    block_size = gate_w.shape[2]
    nblocks = gate_w.shape[1]
    dp_rows, channels = w_y.shape
    taps = conv_w.shape[0]
    offset = tindex * channels
    shape = jax.ShapeDtypeStruct
    gain_in = norm_gain.reshape(1, width)
    gain_mid = mlp_gain.reshape(1, width)
    seg_rows_of = own_rows // 128
    tiled = channels % 128 == 0
    w_yx = (w_y, w_x) if tiled else (jnp.concatenate([w_y, w_x], axis=1),)
    normed_rows, seg_all, wyx_loc, wout_loc = call_kernel(
        partial(enter_kernel, nbits, len(w_yx)),
        (
            shape((group_rows, width), BF16),
            shape((ntensor, seg_rows_of, 128), jnp.int32),
            shape((dp_rows * ndp, 2 * channels), BF16),
            shape((dp_rows * ndp, channels), BF16),
        ),
        gather_sems(nbits)
        + [pltpu.SemaphoreType.DMA((ntensor - 1,)), pltpu.SemaphoreType.DMA((ntensor - 1,))]
        + [pltpu.SemaphoreType.DMA((1,))]
        + line_sems(ndp) * (len(w_yx) + 1),
        0,
        tokens,
        segments.reshape(seg_rows_of, 128),
        gain_in,
        *w_yx,
        w_out,
        far_in=tuple(range(3, 4 + len(w_yx))),
        far_out=(2, 3),
    )
    w_gate, w_up, w_down, normed_rows = lax.optimization_barrier(
        (w_gate, w_up, w_down, normed_rows)
    )
    wg_loc = lax.all_gather(w_gate, "dp", axis=0, tiled=True)
    wu_loc = lax.all_gather(w_up, "dp", axis=0, tiled=True)
    wd_loc = lax.all_gather(w_down, "dp", axis=0, tiled=True)
    seg_rows = seg_all.reshape(group_rows)
    starts = doc_starts(seg_rows, group_rows)
    conv_loc = lax.dynamic_slice_in_dim(conv_w, offset, channels, 1)
    decay_loc = lax.dynamic_slice_in_dim(decay_param, offset, channels, 0).reshape(1, channels)
    soft = jax.nn.softplus(decay_loc)
    slope_soft = jax.nn.sigmoid(decay_loc)
    half_blocks = (
        channels % block_size == block_size // 2 and ntensor % 2 == 0 and block_size % 256 == 0
    )
    since = (jnp.arange(group_rows, dtype=jnp.int32) - starts).astype(F32)[:, None]
    branches = jnp.dot(normed_rows, wyx_loc, preferred_element_type=F32)
    if half_blocks:
        span_blocks = channels // block_size + 1
        w_window = lax.dynamic_slice_in_dim(gate_w, offset // block_size, span_blocks, 1)
        taps_pad = jnp.concatenate([conv_loc, jnp.zeros((8 - taps, channels), F32)], axis=0)
        mixed_low, states, window, gate_pre, cot_rows = call_kernel(
            partial(recurrence_kernel, taps, nbits),
            (
                shape((group_rows, channels), BF16),
                shape((group_rows, channels), F32),
                shape((group_rows, span_blocks * block_size), BF16),
                shape((group_rows, 2 * channels), F32),
                shape((group_rows, width), BF16),
            ),
            [pltpu.SemaphoreType.DMA((1,)), pltpu.SemaphoreType.DMA((1,))]
            + fetch_scratch(nbits),
            5,
            branches,
            taps_pad,
            soft,
            since,
            w_window,
            cotangent,
        )
    else:
        branch_y, branch_x = branches[:, :channels], branches[:, channels:]
        (cot_rows,) = call_kernel(
            partial(fetch_kernel, nbits),
            (shape((group_rows, width), BF16),),
            fetch_scratch(nbits),
            5,
            cotangent,
        )
        rims = gate_rims(channels, block_size, ntensor, offset)
        own_dense = gate_dense(gate_w, offset, offset, channels)
        rim_dense = [gate_dense(gate_w, offset, rim.first, rim.width) for rim in rims]
        conv_out, conv_pull = jax.vjp(partial(causal_conv, starts), branch_x, conv_loc)
        conv_low = conv_out.astype(BF16)
        rim_cells = [rim.fetch(conv_low) for rim in rims]
        gate_pre = jnp.dot(conv_low, own_dense, preferred_element_type=F32)
        for cells, dense in zip(rim_cells, rim_dense):
            gate_pre = gate_pre + jnp.dot(cells, dense, preferred_element_type=F32)
        mixed_low, states = scan_call(
            forward_scan_kernel,
            (shape((group_rows, channels), BF16), shape((group_rows, channels), F32)),
            conv_low,
            gate_pre,
            branch_y,
            soft,
            since,
        )
    middle, mid_rows = call_kernel(
        partial(middle_kernel, nbits),
        (shape((own_rows, width), F32), shape((group_rows, width), BF16)),
        scatter_scratch(own_rows, width, nbits) + gather_sems(nbits),
        1,
        rows_times(mixed_low, wout_loc).astype(BF16),
        tokens,
        gain_mid,
    )
    gate_val = jnp.dot(mid_rows, wg_loc, preferred_element_type=F32)
    up_val = jnp.dot(mid_rows, wu_loc, preferred_element_type=F32)
    hidden, act_pull = jax.vjp(geglu, gate_val, up_val)
    hidden_low = hidden.astype(BF16)
    grad_wd = inner_rows(cot_rows, hidden_low).astype(BF16)
    sum_wd = lax.psum_scatter(grad_wd, "dp", scatter_dimension=0, tiled=True)
    grad_wd, wd_loc = lax.optimization_barrier((grad_wd, wd_loc))
    d_hidden = jnp.dot(cot_rows, wd_loc, preferred_element_type=F32)
    d_gate, d_up = act_pull(d_hidden)
    d_gate = d_gate.astype(BF16)
    d_up = d_up.astype(BF16)
    grad_wg = inner_rows(mid_rows, d_gate).astype(BF16)
    sum_wg = lax.psum_scatter(grad_wg, "dp", scatter_dimension=0, tiled=True)
    grad_wu = inner_rows(mid_rows, d_up).astype(BF16)
    sum_wu = lax.psum_scatter(grad_wu, "dp", scatter_dimension=0, tiled=True)
    d_gate, d_up, grad_wg, grad_wu = lax.optimization_barrier((d_gate, d_up, grad_wg, grad_wu))
    d_mid_part = rows_back((d_gate, d_up), (wg_loc, wu_loc)).astype(BF16)
    d_middle, d_mixer, d_gain_mid = call_kernel(
        partial(turn_kernel, nbits),
        (
            shape((own_rows, width), F32),
            shape((group_rows, width), BF16),
            shape((8, width), F32),
        ),
        scatter_scratch(own_rows, width, nbits) + gather_sems(nbits),
        2,
        d_mid_part,
        cotangent,
        middle,
        gain_mid,
    )
    d_mixer, sum_wd = lax.optimization_barrier((d_mixer, sum_wd))
    d_mixed_in = jnp.dot(d_mixer, wout_loc, preferred_element_type=F32)
    unit = math.gcd(channels, block_size)
    ffn_part = rows_times(hidden_low, wd_loc).astype(BF16)
    merged = half_blocks and nbits <= 2
    if half_blocks:
        found = call_kernel(
            partial(recurrence_back_kernel, taps, nbits, merged),
            (
                shape((group_rows, 2 * channels), BF16),
                shape((channels // unit * 2, block_size, unit), BF16),
                shape((8, channels), F32),
            )
            + ((shape((own_rows, width), BF16),) if merged else ()),
            [
                pltpu.VMEM((group_rows, channels), F32),
                pltpu.VMEM((group_rows, 2 * channels), BF16),
                pltpu.VMEM((group_rows, unit), BF16),
                pltpu.VMEM((group_rows, unit), BF16),
                pltpu.VMEM((taps + 1, 8, channels), F32),
                pltpu.SemaphoreType.DMA((1,)),
                pltpu.SemaphoreType.DMA((1,)),
            ]
            + (scatter_scratch(own_rows, width, nbits) if merged else []),
            6,
            d_mixed_in,
            window,
            gate_pre,
            branches,
            states,
            taps_pad,
            soft,
            slope_soft,
            since,
            w_window,
            *((ffn_part, middle) if merged else ()),
        )
        d_branches, gate_grad, own_small = found[:3]
        d_branches, sum_wg = lax.optimization_barrier((d_branches, sum_wg))
        gate_grad = gate_grad.reshape(channels // unit * 2 * block_size, unit)
    else:
        d_conv, d_gate_low, d_branch_y, d_decay = scan_call(
            backward_scan_kernel,
            (
                shape((group_rows, channels), F32),
                shape((group_rows, 2 * channels), BF16),
                shape((group_rows, channels), BF16),
                shape((8, channels), F32),
            ),
            d_mixed_in,
            conv_low,
            gate_pre,
            branch_y,
            states,
            soft,
            slope_soft,
            since,
        )
        given = [rows_times(d_gate_low, dense).astype(BF16) for dense in rim_dense]
        taken = [rim.give(part) for rim, part in zip(rims, given)]
        d_conv_out = d_conv + rows_times(d_gate_low, own_dense)
        for rim, part in zip(rims, taken):
            d_conv_out = rim.add(d_conv_out, part)
        d_branch_x, grad_conv_loc = conv_pull(d_conv_out)
        d_branches = jnp.concatenate([d_branch_y, d_branch_x.astype(BF16)], axis=1)
        base = offset // block_size * block_size - rims[0].room
        window_rows = rims[0].window(channels)
        picked = jnp.zeros((window_rows, 2 * channels), F32)
        for first, cells in [(offset, conv_low)] + [(r.first, c) for r, c in zip(rims, rim_cells)]:
            part = inner_rows(cells, d_gate_low)
            same = same_block(first, cells.shape[1], offset, channels, block_size)
            part = jnp.where(jnp.concatenate([same, same], axis=1), part, 0.0)
            picked = lax.dynamic_update_slice(picked, part, (first - base, jnp.int32(0)))
        picked = picked.reshape(window_rows // block_size, block_size, 2, channels // unit, unit)
        gate_grad = picked.sum(axis=0).astype(BF16).transpose(2, 1, 0, 3)
        gate_grad = gate_grad.reshape(channels // unit * 2 * block_size, unit)
        own_small = jnp.concatenate(
            [
                grad_conv_loc,
                jnp.sum(d_decay, axis=0, keepdims=True),
                jnp.zeros((7 - taps, channels), F32),
            ],
            axis=0,
        )

    grad_wout = inner_rows(d_mixer, mixed_low).astype(BF16)
    sum_wout = lax.psum_scatter(grad_wout, "dp", scatter_dimension=0, tiled=True)
    grad_wyx = inner_rows(normed_rows, d_branches).astype(BF16)
    d_normed = rows_times(d_branches, wyx_loc).astype(BF16)
    d_normed, sum_wu = lax.optimization_barrier((d_normed, sum_wu))

    pieces = [halved(grad, ndp) for grad in (gate_grad, grad_wyx)]
    peers = ntensor - 1
    gate_rows = gate_grad.shape[0] // ndp
    dma = pltpu.SemaphoreType.DMA
    scratch = scatter_scratch(own_rows, width, nbits)
    scratch += line_scratch(ndp, gate_rows, unit)
    if tiled:
        scratch += line_scratch(ndp, dp_rows, channels) * 2
    else:
        scratch += line_scratch(ndp, dp_rows, 2 * channels)
    scratch += [
        pltpu.VMEM((8, width), F32),
        pltpu.VMEM((ntensor, 8, channels), F32),
        pltpu.VMEM((peers, 8, channels), F32),
        pltpu.VMEM((8, channels), F32),
        pltpu.VMEM((ndp - 1, 8, channels), F32),
    ]
    scratch += [dma((peers,)), dma((peers,)), dma((ndp - 1,)), dma((ndp - 1,))]
    scratch += [dma((peers,)), dma((peers,)), dma((peers + ndp,)), dma((peers + ndp,))]
    grad_input, sum_wy, sum_wx, gate_all, small_all = call_kernel(
        partial(leave_kernel, nbits, tiled),
        (shape((own_rows, width), F32),)
        + (shape((dp_rows, channels), F32),) * 2
        + (
            shape((ntensor, ndp // 2, 2, gate_rows, unit), BF16),
            shape((ntensor, 8, channels), F32),
        ),
        scratch,
        3,
        d_normed,
        tokens,
        d_middle,
        gain_in,
        own_small,
        d_gain_mid,
        *pieces,
        far_in=(6, 7),
    )
    if merged:
        mixed = found[3]
    else:
        (mixed,) = call_kernel(
            partial(result_kernel, nbits),
            (shape((own_rows, width), BF16),),
            scatter_scratch(own_rows, width, nbits),
            4,
            ffn_part,
            middle,
        )
    sum_gate, sum_wy, sum_wx, sum_conv, sum_decay, sum_gain_in, sum_gain_mid = finish(
        gate_all, small_all, sum_wy, sum_wx, taps, gate_w.shape
    )
    return (
        mixed,
        grad_input,
        sum_gain_in,
        sum_wy,
        sum_wx,
        sum_conv,
        sum_gate,
        sum_decay,
        sum_wout.astype(F32),
        sum_gain_mid,
        sum_wg.astype(F32),
        sum_wu.astype(F32),
        sum_wd.astype(F32),
    )


def solution(mesh):
    split = P(("dp", "tensor"), None)
    weight = P("dp", "tensor")
    return jax.shard_map(
        body,
        mesh=mesh,
        in_specs=(
            split,
            P(("dp", "tensor")),
            split,
            P(),
            weight,
            weight,
            P(),
            P(),
            P(),
            weight,
            P(),
            weight,
            weight,
            weight,
        ),
        out_specs=(
            split,
            split,
            P(),
            weight,
            weight,
            P(),
            P(),
            P(),
            weight,
            P(),
            weight,
            weight,
            weight,
        ),
        check_vma=False,
    )
```

```python
import math
from functools import partial

import jax
import jax.numpy as jnp
from jax import lax
from jax.experimental import pallas as pl
from jax.experimental.pallas import tpu as pltpu
from jax.sharding import PartitionSpec as P

EPSILON = 1e-06
MESH = pl.DeviceIdType.MESH
VMEM_BYTES = 56 * 1024 * 1024
CHUNK = 16
F32 = jnp.float32
BF16 = jnp.bfloat16


def subsets(bits):
    found = [()]
    for bit in bits:
        found = found + [chosen + (bit,) for chosen in found]
    return found


def flipped(index, bits):
    for bit in bits:
        mine = (index // (1 << bit)) % 2
        index = index + (1 - 2 * mine) * (1 << bit)
    return index


def log2_of(count):
    assert count & (count - 1) == 0
    return count.bit_length() - 1


def greet(axis_bits):
    barrier = pltpu.get_barrier_semaphore()
    for axis, bit in axis_bits:
        peer = flipped(lax.axis_index(axis), (bit,))
        pl.semaphore_signal(barrier, inc=1, device_id={axis: peer}, device_id_type=MESH)
    pl.semaphore_wait(barrier, len(axis_bits))


def halves_of(nbits, columns):
    half = columns // 2
    ups = tuple(range(nbits))
    return ((ups, 0, half), (ups[::-1], half, half))


class Gather:
    def __init__(self, ref, rows, nbits, send_sems, recv_sems):
        self.ref, self.rows, self.nbits = ref, rows, nbits
        self.sems = (send_sems, recv_sems)
        self.me = lax.axis_index("tensor")
        self.plan = []
        number = 0
        for half, (order, at, width) in enumerate(halves_of(nbits, ref.shape[1])):
            for step, bit in enumerate(order):
                for known in subsets(order[:step]):
                    self.plan.append((half, step, known, bit, at, width, number))
                    number += 1
        self.count = number

    def copy(self, item):
        half, step, known, bit, at, width, number = item
        row = pl.multiple_of(flipped(self.me, known) * self.rows, self.rows)
        piece = self.ref.at[pl.ds(row, self.rows), pl.ds(at, width)]
        return pltpu.make_async_remote_copy(
            src_ref=piece,
            dst_ref=piece,
            send_sem=self.sems[0].at[number],
            recv_sem=self.sems[1].at[number],
            device_id={"tensor": flipped(self.me, (bit,))},
            device_id_type=MESH,
        )

    def begin(self):
        for item in sorted(self.plan, key=lambda it: it[1]):
            if item[2] == ():
                self.copy(item).start()

    def advance(self, step):
        for item in self.plan:
            half, at_step, known, bit, at, width, number = item
            if at_step == step:
                self.copy(item).wait_recv()
                block = known + (bit,)
                for later in self.plan:
                    if later[0] == half and set(later[2]) == set(block):
                        self.copy(later).start()

    def finish(self, step=0):
        for at_step in range(step, self.nbits):
            self.advance(at_step)
        for item in self.plan:
            self.copy(item).wait_send()


def gather_copies(nbits):
    return 2 * ((1 << nbits) - 1)


class Scatter:
    def __init__(self, ref, landed, staged, rows, nbits, send_sems, recv_sems):
        self.ref, self.landed, self.staged = ref, landed, staged
        self.rows, self.nbits = rows, nbits
        self.sems = (send_sems, recv_sems)
        self.me = lax.axis_index("tensor")
        self.plan, self.slot = [], {}
        number = 0
        for half, (order, at, width) in enumerate(halves_of(nbits, ref.shape[1])):
            for step, bit in enumerate(order):
                for rest in subsets(order[step + 1 :])[::-1]:
                    self.plan.append((half, step, rest, bit, at, width, number))
                    if step > 0:
                        self.slot[number] = len(self.slot)
                    number += 1

    def copy(self, item):
        half, step, rest, bit, at, width, number = item
        if step == 0:
            row = pl.multiple_of(flipped(self.me, rest + (bit,)) * self.rows, self.rows)
            source = self.ref.at[pl.ds(row, self.rows), pl.ds(at, width)]
        else:
            source = self.staged.at[self.slot[number]]
        return pltpu.make_async_remote_copy(
            src_ref=source,
            dst_ref=self.landed.at[number],
            send_sem=self.sems[0].at[number],
            recv_sem=self.sems[1].at[number],
            device_id={"tensor": flipped(self.me, (bit,))},
            device_id_type=MESH,
        )

    def begin(self):
        for item in sorted(self.plan, key=lambda it: (len(it[2]) == 0)):
            if item[1] == 0:
                self.copy(item).start()

    def partial_sum(self, half, block, before, row, size):
        at, width = halves_of(self.nbits, self.ref.shape[1])[half][1:]
        base = pl.multiple_of(flipped(self.me, block) * self.rows + row, size)
        total = self.ref[pl.ds(base, size), pl.ds(at, width)].astype(F32)
        for it in self.plan:
            if it[0] == half and it[1] < before and set(it[2]) == set(block):
                total = total + self.landed[it[6], pl.ds(row, size), :].astype(F32)
        return total

    def advance(self, step):
        for half in range(2):
            for item in self.plan:
                if item[0] == half and item[1] == step:
                    self.copy(item).wait_recv()
            for item in self.plan:
                if item[0] == half and item[1] == step + 1:

                    def fill(row, item=item):
                        value = self.partial_sum(
                            item[0], item[2] + (item[3],), item[1], row, CHUNK
                        )
                        where = (self.slot[item[6]], pl.ds(row, CHUNK))
                        self.staged[where + (slice(None),)] = value.astype(BF16)

                    chunks(self.rows, fill)
                    self.copy(item).start()

    def run(self):
        for step in range(self.nbits):
            self.advance(step)

    def total(self, row, size):
        return jnp.concatenate(
            [self.partial_sum(half, (), self.nbits, row, size) for half in range(2)], axis=1
        )

    def drain(self):
        for item in self.plan:
            self.copy(item).wait_send()


def scatter_scratch(rows, columns, nbits):
    copies = gather_copies(nbits)
    later = max(1, copies - (1 << nbits))
    return [
        pltpu.VMEM((copies, rows, columns // 2), BF16),
        pltpu.VMEM((later, rows, columns // 2), BF16),
        pltpu.SemaphoreType.DMA((copies,)),
        pltpu.SemaphoreType.DMA((copies,)),
    ]


def gather_sems(nbits):
    copies = gather_copies(nbits)
    return [pltpu.SemaphoreType.DMA((copies,)), pltpu.SemaphoreType.DMA((copies,))]


def tensor_bits(nbits):
    return [("tensor", bit) for bit in range(nbits)]


def rms_scale_of(values):
    return lax.rsqrt(jnp.mean(values * values, axis=-1, keepdims=True) + EPSILON)


def chunks(rows, body):
    def step(i, carry):
        body(pl.multiple_of(i * CHUNK, CHUNK))
        return carry

    lax.fori_loop(0, rows // CHUNK, step, 0)


def own_row(row, rows):
    return pl.multiple_of(lax.axis_index("tensor") * rows + row, CHUNK)


def dp_place():
    me = lax.axis_index("dp")
    return me // 2, me % 2, lax.axis_size("dp") // 2


def dp_index(chip, core):
    return chip * 2 + core


UP, DOWN = 1, -1


class LineGather:
    def __init__(self, own, whole, send_sems, recv_sems, columns=None):
        self.own, self.whole = own, whole
        self.sems = (send_sems, recv_sems)
        self.chip, self.core, self.chips = dp_place()
        self.rows = own.shape[0]
        self.columns = slice(None) if columns is None else columns

    def block(self, chip):
        row = pl.multiple_of(dp_index(chip, self.core) * self.rows, self.rows)
        return self.whole.at[pl.ds(row, self.rows), self.columns]

    def has(self, way, distance):
        return self.chip >= distance if way == UP else self.chip + distance < self.chips

    def number(self, way, distance):
        return (0 if way == UP else self.chips) + distance

    def along(self, way, distance):
        block = self.block(self.chip - way * distance)
        return pltpu.make_async_remote_copy(
            src_ref=self.own if distance == 0 else block,
            dst_ref=block,
            send_sem=self.sems[0].at[self.number(way, distance)],
            recv_sem=self.sems[1].at[self.number(way, distance + 1)],
            device_id={"dp": dp_index(self.chip + way, self.core)},
            device_id_type=MESH,
        )

    def arrival(self, way, distance):
        block = self.block(self.chip - way * distance)
        return pltpu.make_async_remote_copy(
            src_ref=block,
            dst_ref=block,
            send_sem=self.sems[0].at[self.number(way, distance)],
            recv_sem=self.sems[1].at[self.number(way, distance)],
            device_id={"dp": dp_index(self.chip + way, self.core)},
            device_id_type=MESH,
        )

    def across(self, way, distance):
        block = self.block(self.chip - way * distance)
        number = 2 * self.chips + self.number(way, distance)
        return pltpu.make_async_remote_copy(
            src_ref=self.own if distance == 0 else block,
            dst_ref=block,
            send_sem=self.sems[0].at[number],
            recv_sem=self.sems[1].at[number],
            device_id={"dp": dp_index(self.chip, 1 - self.core)},
            device_id_type=MESH,
        )

    def local(self):
        return pltpu.make_async_copy(
            self.own, self.block(self.chip), self.sems[0].at[4 * self.chips]
        )

    def begin(self):
        for way in (UP, DOWN):

            @pl.when(self.has(-way, 1))
            def _(way=way):
                self.along(way, 0).start()

        self.across(UP, 0).start()
        self.local().start()

    def pass_on(self, distance):
        for way in (UP, DOWN):

            @pl.when(self.has(way, distance))
            def _(way=way):
                self.arrival(way, distance).wait_recv()

                @pl.when(self.has(-way, 1))
                def _():
                    self.along(way, distance).start()

                self.across(way, distance).start()

    def finish(self):
        self.across(UP, 0).wait()
        self.local().wait()
        for way in (UP, DOWN):
            for distance in range(self.chips):

                @pl.when(self.has(way, distance) & self.has(-way, 1))
                def _(way=way, distance=distance):
                    self.along(way, distance).wait_send()

                if distance:

                    @pl.when(self.has(way, distance))
                    def _(way=way, distance=distance):
                        self.across(way, distance).wait()


def line_sems(ndp):
    chips = ndp // 2
    return [pltpu.SemaphoreType.DMA((4 * chips + 1,)), pltpu.SemaphoreType.DMA((4 * chips + 1,))]


def greet_peers(nbits, all_tensor, whole_dp):
    me = lax.axis_index("tensor")
    chip, core, chips = dp_place()
    barrier = pltpu.get_barrier_semaphore()

    def signal(target):
        pl.semaphore_signal(barrier, inc=1, device_id=target, device_id_type=MESH)

    met = 0
    for chosen in subsets(tuple(range(nbits))):
        if chosen and (all_tensor or len(chosen) == 1):
            signal({"tensor": flipped(me, chosen)})
            met += 1
    if whole_dp:
        for shift in range(chips):
            for turn in range(2):
                if (shift, turn) != (0, 0):
                    other = dp_index((chip + shift) % chips, core + turn * (1 - 2 * core))
                    signal({"dp": other})
                    met += 1
    else:
        signal({"dp": dp_index(chip, 1 - core)})
        met += 1

        for shift in sorted({1 % chips, chips - 1} - {0}):
            signal({"dp": dp_index((chip + shift) % chips, core)})
            met += 1

    pl.semaphore_wait(barrier, met)


def enter_kernel(
    nbits, parts_yx, tokens, seg, gain, *refs
):
    w_yx, w_out = refs[:parts_yx], refs[parts_yx]
    normed_all, seg_all, wyx_all, wout_all, s0, r0, s2, r2, l0, *line = refs[parts_yx + 1 :]
    rows = tokens.shape[0]
    me = lax.axis_index("tensor")
    peers = [chosen for chosen in subsets(tuple(range(nbits))) if chosen]
    greet_peers(nbits, True, False)
    width = wyx_all.shape[1] // parts_yx
    lines = [
        LineGather(
            own,
            wyx_all,
            line[2 * number],
            line[2 * number + 1],
            pl.ds(number * width, width) if parts_yx > 1 else None,
        )
        for number, own in enumerate(w_yx)
    ]
    lines.append(LineGather(w_out, wout_all, *line[2 * parts_yx : 2 * parts_yx + 2]))
    for item in lines:
        item.begin()

    def norm(row):
        values = tokens[pl.ds(row, CHUNK), :].astype(F32)
        scaled = values * rms_scale_of(values) * gain[...]
        normed_all[pl.ds(own_row(row, rows), CHUNK), :] = scaled.astype(BF16)

    chunks(rows, norm)
    gather = Gather(normed_all, rows, nbits, s0, r0)
    gather.begin()
    seg_own = pltpu.make_async_copy(seg, seg_all.at[me], l0.at[0])
    seg_own.start()
    seg_copies = [
        pltpu.make_async_remote_copy(
            src_ref=seg,
            dst_ref=seg_all.at[me],
            send_sem=s2.at[number],
            recv_sem=r2.at[number],
            device_id={"tensor": flipped(me, chosen)},
            device_id_type=MESH,
        )
        for number, chosen in enumerate(peers)
    ]
    for copy in seg_copies:
        copy.start()
    chips = lines[0].chips
    for item in lines:
        item.pass_on(1)
    gather.advance(0)
    for distance in range(2, chips):
        for item in lines:
            item.pass_on(distance)
    gather.finish(1)
    for item in lines:
        item.finish()
    for copy in seg_copies:
        copy.wait()
    seg_own.wait()


class Fetch:
    def __init__(self, nbits, cot, cot_all, s0, r0, l0):
        rows = cot.shape[0]
        own = pl.multiple_of(lax.axis_index("tensor") * rows, rows)
        self.local = pltpu.make_async_copy(cot, cot_all.at[pl.ds(own, rows), :], l0.at[0])
        self.gather = Gather(cot_all, rows, nbits, s0, r0)

    def begin(self):
        self.local.wait()
        self.gather.begin()

    def advance(self):
        self.gather.advance(0)

    def finish(self):
        self.gather.finish(1)


def fetch_scratch(nbits):
    return gather_sems(nbits) + [pltpu.SemaphoreType.DMA((1,))]


def fetch_kernel(nbits, cot, cot_all, *sems):
    greet(tensor_bits(nbits))
    fetch = Fetch(nbits, cot, cot_all, *sems)
    fetch.local.start()
    fetch.begin()
    fetch.advance()
    fetch.finish()


def middle_kernel(
    nbits, mixer, tokens, gain, middle, mid_all, landed, staged, s0, r0, s1, r1
):
    rows = tokens.shape[0]
    greet(tensor_bits(nbits))
    scatter = Scatter(mixer, landed, staged, rows, nbits, s0, r0)
    scatter.begin()
    scatter.run()

    def norm(row):
        values = tokens[pl.ds(row, CHUNK), :].astype(F32) + scatter.total(row, CHUNK)
        middle[pl.ds(row, CHUNK), :] = values
        scaled = values * rms_scale_of(values) * gain[...]
        mid_all[pl.ds(own_row(row, rows), CHUNK), :] = scaled.astype(BF16)

    chunks(rows, norm)
    gather = Gather(mid_all, rows, nbits, s1, r1)
    gather.begin()
    gather.finish()
    scatter.drain()


def result_kernel(nbits, ffn, middle, mixed, landed, staged, s0, r0):
    rows = middle.shape[0]
    greet(tensor_bits(nbits))
    scatter = Scatter(ffn, landed, staged, rows, nbits, s0, r0)
    scatter.begin()
    scatter.run()

    def add(row):
        values = middle[pl.ds(row, CHUNK), :] + scatter.total(row, CHUNK)
        mixed[pl.ds(row, CHUNK), :] = values.astype(BF16)

    chunks(rows, add)
    scatter.drain()


def norm_pull(values, gain, cotangent):
    scale = rms_scale_of(values)
    unit = values * scale
    inner = cotangent * gain
    back = scale * (inner - unit * jnp.mean(inner * unit, axis=-1, keepdims=True))
    return back, cotangent * unit


def eight_rows(values):
    total = values[0:8]
    for at in range(8, CHUNK, 8):
        total = total + values[at : at + 8]
    return total


def turn_kernel(
    nbits, d_norm, cot, middle, gain, d_middle, d_mixer, d_gain, landed, staged, s0, r0, s1, r1
):
    rows = middle.shape[0]
    greet(tensor_bits(nbits))
    scatter = Scatter(d_norm, landed, staged, rows, nbits, s0, r0)
    scatter.begin()
    d_gain[...] = jnp.zeros_like(d_gain)
    scatter.run()

    def pull(row):
        span = pl.ds(row, CHUNK)
        back, gains = norm_pull(middle[span, :], gain[...], scatter.total(row, CHUNK))
        values = cot[span, :].astype(F32) + back
        d_middle[span, :] = values
        d_mixer[pl.ds(own_row(row, rows), CHUNK), :] = values.astype(BF16)
        d_gain[...] += eight_rows(gains)

    chunks(rows, pull)
    gather = Gather(d_mixer, rows, nbits, s1, r1)
    gather.begin()
    gather.finish()
    scatter.drain()


class LineSum:
    def __init__(self, whole, kept, swapped, staged, landed, send_sems, recv_sems, columns=None):
        self.whole, self.kept, self.swapped = whole, kept, swapped
        self.staged, self.landed = staged, landed
        self.sems = (send_sems, recv_sems)
        self.columns = columns
        self.chip, self.core, self.chips = dp_place()
        self.rows = whole.shape[2]

    def half(self, core):
        if self.columns is None:
            return self.whole.at[:, core]
        return self.whole.at[:, core, :, self.columns]

    def local(self):
        return pltpu.make_async_copy(
            self.half(self.core), self.kept, self.sems[0].at[2 * self.chips]
        )

    def swap(self):
        return pltpu.make_async_remote_copy(
            src_ref=self.half(1 - self.core),
            dst_ref=self.swapped,
            send_sem=self.sems[0].at[0],
            recv_sem=self.sems[1].at[0],
            device_id={"dp": dp_index(self.chip, 1 - self.core)},
            device_id_type=MESH,
        )

    def has(self, way, distance):
        return self.chip + distance < self.chips if way == UP else self.chip >= distance

    def slot(self, way, distance):
        return (0 if way == UP else self.chips - 1) + distance

    def hop(self, way, distance):
        return pltpu.make_async_remote_copy(
            src_ref=self.staged.at[self.slot(way, distance - 1)],
            dst_ref=self.landed.at[self.slot(way, distance - 1)],
            send_sem=self.sems[0].at[1 + self.slot(way, distance - 1)],
            recv_sem=self.sems[1].at[1 + self.slot(way, distance - 1)],
            device_id={"dp": dp_index(self.chip + way, self.core)},
            device_id_type=MESH,
        )

    def arrival(self, way, distance):
        number = self.slot(way, distance)
        return pltpu.make_async_remote_copy(
            src_ref=self.landed.at[number],
            dst_ref=self.landed.at[number],
            send_sem=self.sems[0].at[1 + number],
            recv_sem=self.sems[1].at[1 + number],
            device_id={"dp": dp_index(self.chip - way, self.core)},
            device_id_type=MESH,
        )

    def begin(self):
        self.swap().start()
        self.local().start()

    def both(self, chip, span):
        return self.kept[chip, span, :].astype(F32) + self.swapped[chip, span, :].astype(F32)

    def send(self, distance):
        if distance == self.chips - 1:
            self.local().wait()
            self.swap().wait_recv()
        for way in (UP, DOWN):

            @pl.when(self.has(way, distance))
            def _(way=way):
                chip = self.chip + way * distance
                slot = self.slot(way, distance - 1)

                def first(row):
                    span = pl.ds(row, CHUNK)
                    self.staged[slot, span, :] = self.both(chip, span).astype(BF16)

                def later(row):
                    span = pl.ds(row, CHUNK)
                    total = self.both(chip, span) + self.landed[
                        self.slot(way, distance), span, :
                    ].astype(F32)
                    self.staged[slot, span, :] = total.astype(BF16)

                if distance == self.chips - 1:
                    chunks(self.rows, first)
                else:

                    @pl.when(self.has(-way, 1))
                    def _():
                        self.arrival(way, distance).wait_recv()
                        chunks(self.rows, later)

                    @pl.when(jnp.logical_not(self.has(-way, 1)))
                    def _():
                        chunks(self.rows, first)

                self.hop(way, distance).start()

    def finish(self, store):
        below, above = self.has(DOWN, 1), self.has(UP, 1)

        def fill(slots):
            for way in slots:
                self.arrival(way, 0).wait_recv()

            def one(row):
                span = pl.ds(row, CHUNK)
                total = self.both(self.chip, span)
                for way in slots:
                    total = total + self.landed[self.slot(way, 0), span, :].astype(F32)
                store(span, total)

            chunks(self.rows, one)

        @pl.when(below & above)
        def _():
            fill((UP, DOWN))

        @pl.when(jnp.logical_not(above))
        def _():
            fill((UP,))

        @pl.when(jnp.logical_not(below))
        def _():
            fill((DOWN,))

    def drain(self):
        self.swap().wait_send()
        for way in (UP, DOWN):
            for distance in range(1, self.chips):

                @pl.when(self.has(way, distance))
                def _(way=way, distance=distance):
                    self.hop(way, distance).wait_send()


def line_scratch(ndp, rows, columns):
    chips = ndp // 2
    return [
        pltpu.VMEM((chips, rows, columns), BF16),
        pltpu.VMEM((chips, rows, columns), BF16),
        pltpu.VMEM((2 * chips - 2, rows, columns), BF16),
        pltpu.VMEM((2 * chips - 2, rows, columns), BF16),
        pltpu.SemaphoreType.DMA((2 * chips + 1,)),
        pltpu.SemaphoreType.DMA((2 * chips + 1,)),
    ]


RING = 6


def leave_kernel(nbits, tiled, *refs):
    refs = list(refs)

    def take(count):
        taken = refs[:count]
        del refs[:count]
        return taken

    d_norm, tokens, d_middle, gain, own_small, d_gain_mid = take(6)
    pieces = take(3)
    grad_input, sum_out, sum_y, sum_x, gate_all, small_all = take(6)
    landed, staged, s0, r0 = take(4)
    share = small_all.shape[2]
    rings = [LineSum(piece, *take(RING)) for piece in pieces[:2]]
    if tiled:
        for at in (0, share):
            rings.append(LineSum(pieces[2], *take(RING), pl.ds(at, share)))
    else:
        rings.append(LineSum(pieces[2], *take(RING)))
    d_gain, gains, gains_landed, small, small_landed = take(5)
    gain_s, gain_r, vec_s, vec_r, join_s, join_r, gate_s, gate_r = take(8)
    rows = tokens.shape[0]
    me = lax.axis_index("tensor")
    chip, core, chips = dp_place()
    peers = [chosen for chosen in subsets(tuple(range(nbits))) if chosen]
    others = [(shift, turn) for shift in range(chips) for turn in range(2)][1:]
    greet_peers(nbits, True, True)
    for ring in rings:
        ring.begin()
    scatter = Scatter(d_norm, landed, staged, rows, nbits, s0, r0)
    scatter.begin()
    d_gain[...] = jnp.zeros_like(d_gain)
    far = list(range(chips - 1, 0, -1))
    for ring in rings:
        ring.send(far[0])
    if len(far) > 1:
        rings[0].send(far[1])
    scatter.advance(0)
    if len(far) > 1:
        for ring in rings[1:]:
            ring.send(far[1])
    for distance in far[2:]:
        rings[0].send(distance)
    for step in range(1, nbits):
        scatter.advance(step)

    def pull(row):
        span = pl.ds(row, CHUNK)
        back, parts = norm_pull(
            tokens[span, :].astype(F32), gain[...], scatter.total(row, CHUNK)
        )
        grad_input[span, :] = d_middle[span, :] + back
        d_gain[...] += eight_rows(parts)

    chunks(rows, pull)
    def store_gate(span, value):
        gate_all[me, chip, core, span, :] = value.astype(BF16)

    def gate_copy(number, ref, target):
        return pltpu.make_async_remote_copy(
            src_ref=ref,
            dst_ref=ref,
            send_sem=gate_s.at[number],
            recv_sem=gate_r.at[number],
            device_id=target,
            device_id_type=MESH,
        )

    def gate_line(shift):
        target = {"dp": dp_index((chip + shift) % chips, core)}
        return gate_copy(shift - 1, gate_all.at[me, chip, core], target)

    def gate_tensor(number, chosen):
        target = {"tensor": flipped(me, chosen)}
        return gate_copy(chips - 1 + number, gate_all.at[me, :, core], target)

    def gate_core():
        target = {"dp": dp_index(chip, 1 - core)}
        return gate_copy(chips - 1 + len(peers), gate_all.at[:, :, core], target)

    def start_gate():
        rings[0].finish(store_gate)
        for shift in range(1, chips):
            gate_line(shift).start()

    top = jnp.sum(d_gain[...], axis=0, keepdims=True)
    low = jnp.sum(d_gain_mid[...], axis=0, keepdims=True)
    place8 = lax.broadcasted_iota(jnp.int32, (8, share), 0)
    for index in range(1 << nbits):
        span = slice(index * share, (index + 1) * share)
        gains[index] = jnp.where(
            place8 == 6, top[:, span], jnp.where(place8 == 7, low[:, span], 0.0)
        )

    def gain_copy(number, chosen):
        peer = flipped(me, chosen)
        return pltpu.make_async_remote_copy(
            src_ref=gains.at[peer],
            dst_ref=gains_landed.at[number],
            send_sem=gain_s.at[number],
            recv_sem=gain_r.at[number],
            device_id={"tensor": peer},
            device_id_type=MESH,
        )

    for number, chosen in enumerate(peers):
        gain_copy(number, chosen).start()
    start_gate()
    for distance in far[2:]:
        for ring in rings[1:]:
            ring.send(distance)
    total = own_small[...] + gains[me]
    for number, chosen in enumerate(peers):
        gain_copy(number, chosen).wait_recv()
        total = total + gains_landed[number]
    small[...] = total

    def vec_copy(number, shift, turn):
        other = dp_index((chip + shift) % chips, core + turn * (1 - 2 * core))
        return pltpu.make_async_remote_copy(
            src_ref=small,
            dst_ref=small_landed.at[number],
            send_sem=vec_s.at[number],
            recv_sem=vec_r.at[number],
            device_id={"dp": other},
            device_id_type=MESH,
        )

    for number, (shift, turn) in enumerate(others):
        vec_copy(number, shift, turn).start()

    for shift in range(1, chips):
        gate_line(shift).wait_recv()
    for number, chosen in enumerate(peers):
        gate_tensor(number, chosen).start()
    total = small[...]
    for number, (shift, turn) in enumerate(others):
        vec_copy(number, shift, turn).wait_recv()
        total = total + small_landed[number]
    small_all[me] = total

    def join_copy(number, chosen):
        return pltpu.make_async_remote_copy(
            src_ref=small_all.at[me],
            dst_ref=small_all.at[me],
            send_sem=join_s.at[number],
            recv_sem=join_r.at[number],
            device_id={"tensor": flipped(me, chosen)},
            device_id_type=MESH,
        )

    for number, chosen in enumerate(peers):
        join_copy(number, chosen).start()
    for number, chosen in enumerate(peers):
        gate_tensor(number, chosen).wait_recv()
    gate_core().start()

    def store_in(*targets):
        def store(span, value):
            for number, ref in enumerate(targets):
                ref[span, :] = value[:, number * share : (number + 1) * share]

        return store

    rings[1].finish(store_in(sum_out))
    if tiled:
        rings[2].finish(store_in(sum_y))
        rings[3].finish(store_in(sum_x))
    else:
        rings[2].finish(store_in(sum_y, sum_x))
    gate_core().wait()
    for shift in range(1, chips):
        gate_line(shift).wait_send()
    for number, chosen in enumerate(peers):
        gate_tensor(number, chosen).wait_send()
        gain_copy(number, chosen).wait_send()
        join_copy(number, chosen).wait()
    for number, (shift, turn) in enumerate(others):
        vec_copy(number, shift, turn).wait_send()
    scatter.drain()
    for ring in rings:
        ring.drain()


def in_vmem(count):
    return [pl.BlockSpec(memory_space=pltpu.VMEM)] * count


def call_kernel(kernel, outs, scratch, number, *operands, far_in=(), far_out=(), cost_us=1):
    vmem = pl.BlockSpec(memory_space=pltpu.VMEM)
    far = pl.BlockSpec(memory_space=pl.ANY)
    return pl.pallas_call(
        kernel,
        out_shape=outs,
        in_specs=[far if i in far_in else vmem for i in range(len(operands))],
        out_specs=tuple(far if i in far_out else vmem for i in range(len(outs))),
        scratch_shapes=scratch,
        cost_estimate=pl.CostEstimate(
            flops=0, bytes_accessed=cost_us * 1_000_000, transcendentals=0
        ),
        compiler_params=pltpu.CompilerParams(
            collective_id=number, has_side_effects=True, vmem_limit_bytes=VMEM_BYTES
        ),
    )(*operands)


def sigmoid(values):
    return 1.0 / (1.0 + jnp.exp(-values))


def one_minus_exp(values):
    series = values / 7.0 + 1.0
    for order in (6.0, 5.0, 4.0, 3.0, 2.0):
        series = 1.0 + series * values / order
    return jnp.where(values > -0.3, -values * series, 1.0 - jnp.exp(values))


GELU_K = 0.7978845608028654
GELU_C = 0.044715


def gelu_parts(values):
    square = values * values
    bent = jnp.tanh(GELU_K * values * (1.0 + GELU_C * square))
    gelu = 0.5 * values * (1.0 + bent)
    slope = 0.5 * (1.0 + bent) + 0.5 * values * (1.0 - bent * bent) * GELU_K * (
        1.0 + 3.0 * GELU_C * square
    )
    return gelu, slope


def gate_terms(gate_a, gate_x, soft, since):
    sig_a = sigmoid(gate_a)
    sig_x = sigmoid(gate_x)
    log_decay = -8.0 * sig_a * soft
    decay = jnp.exp(log_decay)
    scale = jnp.sqrt(one_minus_exp(2.0 * log_decay))
    keep = since > 0.5
    return sig_a, sig_x, decay, jnp.where(keep, scale, 1.0), keep


def scan_down(decay, value, carry):
    place = lax.broadcasted_iota(jnp.int32, decay.shape, 0)
    for shift in (1, 2, 4):
        past = place >= shift
        moved = pltpu.roll(value, shift, 0)
        value = jnp.where(past, decay * moved + value, value)
        decay = jnp.where(past, decay * pltpu.roll(decay, shift, 0), decay)
    return decay * carry + value


def scan_up(decay, value, carry):
    place = lax.broadcasted_iota(jnp.int32, decay.shape, 0)
    factor = jnp.where(place < 7, pltpu.roll(decay, 7, 0), 1.0)
    for shift in (1, 2, 4):
        past = place < 8 - shift
        moved = pltpu.roll(value, 8 - shift, 0)
        value = jnp.where(past, factor * moved + value, value)
        factor = jnp.where(past, factor * pltpu.roll(factor, 8 - shift, 0), factor)
    return factor * carry + value


def forward_scan(conv_rows, gates, branch_y, soft, since, mixed, states, between=()):
    total_rows, width = states.shape

    def step(i, carry):
        row = pl.multiple_of(i * CHUNK, CHUNK)
        span = pl.ds(row, CHUNK)
        values = conv_rows(span).astype(F32)
        kept = []
        for at in range(0, CHUNK, 8):
            tile = pl.ds(row + at, 8)
            sig_a, sig_x, decay, scale, keep = gate_terms(
                gates[tile, :width], gates[tile, width:], soft[...], since[tile, :]
            )
            given = values[at : at + 8] * sig_x * scale
            state = scan_down(jnp.where(keep, decay, 0.0), given, carry)
            carry = state[7:8]
            states[tile, :] = state
            kept.append(state * gelu_parts(branch_y[tile, :])[0])
        mixed[span, :] = jnp.concatenate(kept, axis=0).astype(BF16)
        return carry

    steps, stretches = total_rows // CHUNK, len(between) + 1
    carry = jnp.zeros((1, width), F32)
    for stretch in range(stretches):
        first, last = stretch * steps // stretches, (stretch + 1) * steps // stretches
        carry = lax.fori_loop(first, last, step, carry)
        if stretch < len(between):
            between[stretch]()


def forward_scan_kernel(conv, gates, branch_y, soft, since, mixed, states):
    forward_scan(lambda span: conv[span, :], gates, branch_y, soft, since, mixed, states)


def backward_scan(
    d_mixed, conv_rows, gates, branch_y, states, soft, slope_soft, since, d_conv, d_gates, d_branch, d_decay
):
    total_rows, width = states.shape
    d_decay[...] = jnp.zeros_like(d_decay)

    def step(i, carry):
        row = pl.multiple_of(total_rows - CHUNK - i * CHUNK, CHUNK)
        span = pl.ds(row, CHUNK)
        values = conv_rows(span).astype(F32)
        kept = []
        for at in range(CHUNK - 8, -1, -8):
            tile = pl.ds(row + at, 8)
            soft_row = soft[...]
            sig_a, sig_x, decay, scale, keep = gate_terms(
                gates[tile, :width], gates[tile, width:], soft_row, since[tile, :]
            )
            value = values[at : at + 8]
            gelu, slope = gelu_parts(branch_y[tile, :])
            state = states[tile, :]
            upper = d_mixed[tile, :]
            held = jnp.where(keep, decay, 0.0)
            lam = scan_up(held, upper * gelu, carry)
            carry = held[0:1] * lam[0:1]
            d_conv[tile, :] = lam * sig_x * scale
            d_x = lam * value * scale * sig_x * (1.0 - sig_x)
            given = value * sig_x
            d_log = lam * (state - given * scale - given * decay * decay / scale)
            d_log = jnp.where(keep, d_log, 0.0)
            d_a = d_log * (-8.0 * soft_row) * sig_a * (1.0 - sig_a)
            d_decay[...] += d_log * (-8.0 * sig_a) * slope_soft[...]
            kept.append((d_a, d_x, upper * state * slope))
        kept = kept[::-1]
        d_gates[span, :width] = jnp.concatenate([k[0] for k in kept], axis=0).astype(BF16)
        d_gates[span, width:] = jnp.concatenate([k[1] for k in kept], axis=0).astype(BF16)
        d_branch[span, :] = jnp.concatenate([k[2] for k in kept], axis=0).astype(BF16)
        return carry

    lax.fori_loop(0, total_rows // CHUNK, step, jnp.zeros((1, width), F32))


def backward_scan_kernel(
    d_mixed, conv, gates, branch_y, states, soft, slope_soft, since, d_conv, d_gates, d_branch, d_decay
):
    backward_scan(
        d_mixed,
        lambda span: conv[span, :],
        gates,
        branch_y,
        states,
        soft,
        slope_soft,
        since,
        d_conv,
        d_gates,
        d_branch,
        d_decay,
    )


def times_transposed(left, right):
    return lax.dot_general(left, right, (((1,), (1,)), ((), ())), preferred_element_type=F32)


class HalfBlocks:
    def __init__(self, channels, block):
        self.odd = lax.axis_index("tensor") % 2
        self.half = block // 2
        self.block = block
        self.count = channels // block + 1
        self.channels = channels
        self.own = pl.multiple_of(self.odd * self.half, self.half)
        self.shared = (1 - self.odd) * (self.count - 1)
        self.mine_in_block = pl.multiple_of(self.odd * self.half, self.half)
        self.other_in_block = pl.multiple_of((1 - self.odd) * self.half, self.half)
        self.mine = pl.multiple_of((1 - self.odd) * (channels - self.half), self.half)
        self.pair = {"tensor": lax.axis_index("tensor") + 1 - 2 * self.odd}

    def full(self, index):
        block = index + self.odd
        return block, pl.multiple_of(index * self.block + self.odd * self.half, self.half)

    def span(self, block):
        return pl.ds(pl.multiple_of(block * self.block, self.block), self.block)

    def shared_part(self, start):
        return pl.ds(pl.multiple_of(self.shared * self.block + start, self.half), self.half)


PART = 256


def parts(rows, body):
    def step(i, carry):
        body(pl.ds(pl.multiple_of(i * PART, PART), PART))
        return carry

    lax.fori_loop(0, rows // PART, step, 0)


def recurrence_kernel(
    taps,
    nbits,
    branches,
    tap_rows,
    soft,
    since,
    weights,
    cot,
    mixed,
    states,
    window,
    gates,
    cot_all,
    send,
    recv,
    *sems,
):
    total_rows, width = states.shape
    block = weights.shape[2]
    place = HalfBlocks(width, block)
    branch_y, branch_x = branches.at[:, :width], branches.at[:, width:]
    greet(tensor_bits(nbits))
    fetch = Fetch(nbits, cot, cot_all, *sems)
    fetch.local.start()

    def conv(i, before):
        row = pl.multiple_of(i * CHUNK, CHUNK)
        kept = []
        for at in range(0, CHUNK, 8):
            tile = pl.ds(row + at, 8)
            values = branch_x[tile, :]
            line = lax.broadcasted_iota(jnp.int32, values.shape, 0)
            total = values * tap_rows[0:1, :]
            for tap in range(1, taps):
                moved = jnp.where(
                    line < tap, pltpu.roll(before, tap, 0), pltpu.roll(values, tap, 0)
                )
                moved = jnp.where(since[tile, :] > tap - 0.5, moved, 0.0)
                total = total + moved * tap_rows[tap : tap + 1, :]
            kept.append(total)
            before = values
        window[pl.ds(row, CHUNK), pl.ds(place.own, width)] = jnp.concatenate(
            kept, axis=0
        ).astype(BF16)
        return before

    lax.fori_loop(0, total_rows // CHUNK, conv, jnp.zeros((8, width), F32))
    source = window.at[:, place.shared_part(place.mine_in_block)]
    away = pl.multiple_of(place.odd * (place.count - 1) * block + place.mine_in_block, place.half)
    rim = pltpu.make_async_remote_copy(
        src_ref=source,
        dst_ref=window.at[:, pl.ds(away, place.half)],
        send_sem=send.at[0],
        recv_sem=recv.at[0],
        device_id=place.pair,
        device_id_type=MESH,
    )
    rim.start()
    fetch.begin()

    def full(span):
        for index in range(place.count - 1):
            number, at = place.full(index)
            cells = window[span, place.span(number)]
            for s in range(2):
                gates[span, pl.ds(s * width + at, block)] = jnp.dot(
                    cells, weights[s, number], preferred_element_type=F32
                )

    parts(total_rows, full)
    rim.wait()

    def shared(span):
        cells = window[span, place.span(place.shared)]
        for s in range(2):
            gates[span, pl.ds(s * width + place.mine, place.half)] = jnp.dot(
                cells,
                weights[s, place.shared, :, pl.ds(place.mine_in_block, place.half)],
                preferred_element_type=F32,
            )

    parts(total_rows, shared)
    forward_scan(
        lambda span: window[span, pl.ds(place.own, width)],
        gates,
        branch_y,
        soft,
        since,
        mixed,
        states,
        [fetch.advance],
    )
    fetch.finish()


def recurrence_back_kernel(
    taps,
    nbits,
    with_ffn,
    d_mixed,
    window,
    gates,
    branches,
    states,
    tap_rows,
    soft,
    slope_soft,
    since,
    weights,
    *refs,
):
    refs = list(refs)

    def take(count):
        taken = refs[:count]
        del refs[:count]
        return taken

    ffn, middle = take(2) if with_ffn else (None, None)
    d_branches, gate_grad, own_small = take(3)
    mixed = take(1)[0] if with_ffn else None
    d_conv, d_gates, given, taken, sums, send, recv = take(7)
    total_rows, width = states.shape
    block = weights.shape[2]
    place = HalfBlocks(width, block)
    half = place.half
    branch_y, branch_x = branches.at[:, :width], branches.at[:, width:]
    d_branch_y, d_branch_x = d_branches.at[:, :width], d_branches.at[:, width:]
    greet(tensor_bits(nbits))
    if with_ffn:
        scatter = Scatter(ffn, *take(2), middle.shape[0], nbits, *take(2))
        scatter.begin()
    backward_scan(
        d_mixed,
        lambda span: window[span, pl.ds(place.own, width)],
        gates,
        branch_y,
        states,
        soft,
        slope_soft,
        since,
        d_conv,
        d_gates,
        d_branch_y,
        sums.at[taps],
    )

    def to_pair(span):
        total = jnp.zeros((PART, half), F32)
        for s in range(2):
            total = total + times_transposed(
                d_gates[span, pl.ds(s * width + place.mine, half)],
                weights[
                    s,
                    place.shared,
                    pl.ds(place.other_in_block, half),
                    pl.ds(place.mine_in_block, half),
                ],
            )
        given[span, :] = total.astype(BF16)

    parts(total_rows, to_pair)
    rim = pltpu.make_async_remote_copy(
        src_ref=given,
        dst_ref=taken,
        send_sem=send.at[0],
        recv_sem=recv.at[0],
        device_id=place.pair,
        device_id_type=MESH,
    )
    rim.start()

    def full(span):
        for index in range(place.count - 1):
            number, at = place.full(index)
            total = d_conv[span, pl.ds(at, block)]
            for s in range(2):
                total = total + times_transposed(
                    d_gates[span, pl.ds(s * width + at, block)], weights[s, number]
                )
            d_conv[span, pl.ds(at, block)] = total
        total = d_conv[span, pl.ds(place.mine, half)]
        for s in range(2):
            total = total + times_transposed(
                d_gates[span, pl.ds(s * width + place.mine, half)],
                weights[
                    s,
                    place.shared,
                    pl.ds(place.mine_in_block, half),
                    pl.ds(place.mine_in_block, half),
                ],
            )
        d_conv[span, pl.ds(place.mine, half)] = total

    parts(total_rows, full)
    if with_ffn:
        scatter.advance(0)
    units = width // half
    for index in range(units):
        number = (index + place.odd) // 2
        cells = window[:, place.span(number)]
        both = jnp.concatenate(
            [d_gates[:, s * width + index * half : s * width + (index + 1) * half] for s in range(2)],
            axis=1,
        )
        found = lax.dot_general(
            cells, both, (((0,), (0,)), ((), ())), preferred_element_type=F32
        ).astype(BF16)
        gate_grad[2 * index] = found[:, :half]
        gate_grad[2 * index + 1] = found[:, half:]
    rim.wait()

    def add(span):
        d_conv[span, pl.ds(place.mine, half)] += taken[span, :].astype(F32)

    parts(total_rows, add)
    for tap in range(taps):
        sums[tap] = jnp.zeros((8, width), F32)

    def conv(i, after):
        row = pl.multiple_of(total_rows - CHUNK - i * CHUNK, CHUNK)
        kept = []
        for at in range(CHUNK - 8, -1, -8):
            tile = pl.ds(row + at, 8)
            values = d_conv[tile, :]
            line = lax.broadcasted_iota(jnp.int32, values.shape, 0)
            below = branch_x[tile, :]
            higher = pl.multiple_of((row + at - 8 + total_rows) % total_rows, 8)
            above = branch_x[pl.ds(higher, 8), :]
            total = values * tap_rows[0:1, :]
            sums[0] += values * below
            masked = []
            for tap in range(1, taps):
                here = jnp.where(since[tile, :] > tap - 0.5, values, 0.0)
                masked.append(here)
                moved = jnp.where(
                    line < 8 - tap,
                    pltpu.roll(here, 8 - tap, 0),
                    pltpu.roll(after[tap - 1], 8 - tap, 0),
                )
                total = total + moved * tap_rows[tap : tap + 1, :]
                source = jnp.where(
                    line < tap, pltpu.roll(above, tap, 0), pltpu.roll(below, tap, 0)
                )
                sums[tap] += here * source
            after = tuple(masked)
            kept.append(total)
        d_branch_x[pl.ds(row, CHUNK), :] = jnp.concatenate(kept[::-1], axis=0).astype(BF16)
        return after

    none = jnp.zeros((8, width), F32)
    lax.fori_loop(0, total_rows // CHUNK, conv, (none,) * (taps - 1))
    line = lax.broadcasted_iota(jnp.int32, (8, width), 0)
    total = jnp.zeros((8, width), F32)
    for tap in range(taps + 1):
        row = jnp.sum(sums[tap], axis=0, keepdims=True)
        total = jnp.where(line == tap, row, total)
    own_small[...] = total
    if with_ffn:
        for step in range(1, nbits):
            scatter.advance(step)

        def result(row):
            span = pl.ds(row, CHUNK)
            mixed[span, :] = (middle[span, :] + scatter.total(row, CHUNK)).astype(BF16)

        chunks(middle.shape[0], result)
        scatter.drain()


def finish_kernel(taps, gates, small, in_y, in_x, whole, out_y, out_x, conv, decay, gain_in, gain_mid):
    blocks = whole.shape[1]
    pieces = gates.shape[0] // blocks

    def block(n, carry):
        for piece in range(pieces):
            for s in range(2):
                whole[s, n, :, piece * 128 : (piece + 1) * 128] = gates[
                    n * pieces + piece, s
                ].astype(F32)
        return carry

    lax.fori_loop(0, blocks, block, 0)
    out_y[...] = in_y[...]
    out_x[...] = in_x[...]
    share = small.shape[2]
    for index in range(small.shape[0]):
        span = slice(index * share, (index + 1) * share)
        conv[:, span] = small[index, :taps, :]
        decay[:, span] = small[index, taps : taps + 1, :]
        gain_in[:, span] = small[index, 6:7, :]
        gain_mid[:, span] = small[index, 7:8, :]


def finish(gate_all, small_all, sum_y, sum_x, taps, gate_shape):
    _, blocks, block, _ = gate_shape
    unit = gate_all.shape[-1]
    pieces = block // unit
    width = small_all.shape[0] * small_all.shape[2]
    if unit != 128:
        whole = gate_all.reshape(blocks, pieces, 2, block, unit).transpose(2, 0, 3, 1, 4)
        summed = small_all.transpose(1, 0, 2).reshape(8, width)
        whole = whole.reshape(gate_shape).astype(F32)
        rows = (summed[:taps], summed[taps], summed[6], summed[7])
        return (whole, sum_y, sum_x) + rows
    shape = jax.ShapeDtypeStruct
    row = shape((1, width), F32)
    found = scan_call(
        partial(finish_kernel, taps),
        (
            shape(gate_shape, F32),
            shape(sum_y.shape, F32),
            shape(sum_x.shape, F32),
            shape((taps, width), F32),
            row,
            row,
            row,
        ),
        gate_all.reshape(blocks * pieces, 2, block, unit),
        small_all,
        sum_y,
        sum_x,
    )
    return found[:4] + tuple(one.reshape(width) for one in found[4:])


def scan_call(kernel, outs, *operands):
    return pl.pallas_call(
        kernel,
        out_shape=outs,
        in_specs=in_vmem(len(operands)),
        out_specs=tuple(in_vmem(len(outs))),
        compiler_params=pltpu.CompilerParams(vmem_limit_bytes=VMEM_BYTES),
    )(*operands)


class Rim:
    def __init__(self, route, back, source, first, width, room):
        self.route, self.back = route, back
        self.source, self.first, self.width = source, first, width
        self.room = room

    def fetch(self, values):
        part = lax.dynamic_slice_in_dim(values, self.source, self.width, 1)
        return lax.ppermute(part, "tensor", self.route)

    def give(self, part):
        return lax.ppermute(part, "tensor", self.back)

    def add(self, values, part):
        zeros = jnp.zeros(values.shape, F32)
        return values + lax.dynamic_update_slice_in_dim(
            zeros, part.astype(F32), self.source, 1
        )

    def window(self, channels):
        return (channels // self.width + 4) * self.width


def gate_rims(channels, block_size, ntensor, offset):
    up = [(i, i + 1) for i in range(ntensor - 1)]
    down = [(i + 1, i) for i in range(ntensor - 1)]
    last = jnp.int32(channels - block_size)
    return [
        Rim(up, down, last, offset - block_size, block_size, block_size),
        Rim(down, up, jnp.int32(0), offset + channels, block_size, block_size),
    ]


def same_block(first, count, offset, channels, block_size):
    rows = (first + jnp.arange(count, dtype=jnp.int32))[:, None]
    columns = (offset + jnp.arange(channels, dtype=jnp.int32))[None, :]
    return (rows + block_size) // block_size == (columns + block_size) // block_size


def gate_dense(gate_w, offset, first, count):
    block_size = gate_w.shape[2]
    total = gate_w.shape[1] * block_size
    channels = total // lax.axis_size("tensor")
    columns = gate_w.transpose(2, 0, 1, 3).reshape(block_size, 2, total)
    columns = lax.dynamic_slice_in_dim(columns, offset, channels, 2)
    copies = -(-count // block_size) + 1
    tall = jnp.concatenate([columns] * copies, axis=0)
    tall = lax.dynamic_slice_in_dim(tall, (first + block_size) % block_size, count, 0)
    same = same_block(first, count, offset, channels, block_size)
    dense = jnp.where(same[:, None, :], tall, jnp.zeros_like(tall))
    return dense.reshape(count, 2 * channels)


def doc_starts(seg_ids, seq_len):
    places = jnp.arange(seg_ids.shape[0], dtype=jnp.int32)
    before = jnp.concatenate([seg_ids[:1], seg_ids[:-1]])
    resets = (places % seq_len == 0) | (seg_ids != before)
    starts = lax.cummax(jnp.where(resets, places, jnp.zeros_like(places)), axis=0)
    return starts


def causal_conv(starts, values, kernel):
    places = jnp.arange(values.shape[0], dtype=jnp.int32)
    total = values * kernel[0]
    for offset_k in range(1, kernel.shape[0]):
        moved = jnp.concatenate(
            [jnp.zeros((offset_k, values.shape[1]), values.dtype), values[:-offset_k]], axis=0
        )
        valid = (places - offset_k >= starts)[:, None]
        total = total + jnp.where(valid, moved, jnp.zeros_like(moved)) * kernel[offset_k]
    return total


def geglu(gate_val, up_val):
    return jax.nn.gelu(gate_val, approximate=True) * up_val


def rows_times(left, right):
    return lax.dot_general(left, right, (((1,), (1,)), ((), ())), preferred_element_type=F32)


def rows_back(lefts, rights):
    total = rows_times(lefts[0], rights[0])
    return total + rows_times(lefts[1], rights[1])


def inner_rows(left, right):
    return lax.dot_general(left, right, (((0,), (0,)), ((), ())), preferred_element_type=F32)


def halved(grad, ndp):
    return grad.reshape(ndp // 2, 2, grad.shape[0] // ndp, grad.shape[1])


def body(
    tokens,
    segments,
    cotangent,
    norm_gain,
    w_y,
    w_x,
    conv_w,
    gate_w,
    decay_param,
    w_out,
    mlp_gain,
    w_gate,
    w_up,
    w_down,
):
    ntensor = lax.axis_size("tensor")
    ndp = lax.axis_size("dp")
    nbits = log2_of(ntensor)
    tindex = lax.axis_index("tensor")
    own_rows, width = tokens.shape
    group_rows = own_rows * ntensor
    block_size = gate_w.shape[2]
    nblocks = gate_w.shape[1]
    dp_rows, channels = w_y.shape
    taps = conv_w.shape[0]
    offset = tindex * channels
    shape = jax.ShapeDtypeStruct
    gain_in = norm_gain.reshape(1, width)
    gain_mid = mlp_gain.reshape(1, width)
    seg_rows_of = own_rows // 128
    tiled = channels % 128 == 0
    w_yx = (w_y, w_x) if tiled else (jnp.concatenate([w_y, w_x], axis=1),)
    normed_rows, seg_all, wyx_loc, wout_loc = call_kernel(
        partial(enter_kernel, nbits, len(w_yx)),
        (
            shape((group_rows, width), BF16),
            shape((ntensor, seg_rows_of, 128), jnp.int32),
            shape((dp_rows * ndp, 2 * channels), BF16),
            shape((dp_rows * ndp, channels), BF16),
        ),
        gather_sems(nbits)
        + [pltpu.SemaphoreType.DMA((ntensor - 1,)), pltpu.SemaphoreType.DMA((ntensor - 1,))]
        + [pltpu.SemaphoreType.DMA((1,))]
        + line_sems(ndp) * (len(w_yx) + 1),
        0,
        tokens,
        segments.reshape(seg_rows_of, 128),
        gain_in,
        *w_yx,
        w_out,
        far_in=tuple(range(3, 4 + len(w_yx))),
        far_out=(2, 3),
    )
    units = w_gate.shape[1]
    w_both = jnp.concatenate([w_gate, w_up], axis=1)
    w_both, w_down, normed_rows = lax.optimization_barrier((w_both, w_down, normed_rows))
    both_loc = lax.all_gather(w_both, "dp", axis=0, tiled=True)
    wd_loc = lax.all_gather(w_down, "dp", axis=0, tiled=True)
    seg_rows = seg_all.reshape(group_rows)
    starts = doc_starts(seg_rows, group_rows)
    conv_loc = lax.dynamic_slice_in_dim(conv_w, offset, channels, 1)
    decay_loc = lax.dynamic_slice_in_dim(decay_param, offset, channels, 0).reshape(1, channels)
    soft = jax.nn.softplus(decay_loc)
    slope_soft = jax.nn.sigmoid(decay_loc)
    half_blocks = (
        channels % block_size == block_size // 2 and ntensor % 2 == 0 and block_size % 256 == 0
    )
    since = (jnp.arange(group_rows, dtype=jnp.int32) - starts).astype(F32)[:, None]
    branches = jnp.dot(normed_rows, wyx_loc, preferred_element_type=F32)
    if half_blocks:
        span_blocks = channels // block_size + 1
        w_window = lax.dynamic_slice_in_dim(gate_w, offset // block_size, span_blocks, 1)
        taps_pad = jnp.concatenate([conv_loc, jnp.zeros((8 - taps, channels), F32)], axis=0)
        mixed_low, states, window, gate_pre, cot_rows = call_kernel(
            partial(recurrence_kernel, taps, nbits),
            (
                shape((group_rows, channels), BF16),
                shape((group_rows, channels), F32),
                shape((group_rows, span_blocks * block_size), BF16),
                shape((group_rows, 2 * channels), F32),
                shape((group_rows, width), BF16),
            ),
            [pltpu.SemaphoreType.DMA((1,)), pltpu.SemaphoreType.DMA((1,))]
            + fetch_scratch(nbits),
            5,
            branches,
            taps_pad,
            soft,
            since,
            w_window,
            cotangent,
        )
    else:
        branch_y, branch_x = branches[:, :channels], branches[:, channels:]
        (cot_rows,) = call_kernel(
            partial(fetch_kernel, nbits),
            (shape((group_rows, width), BF16),),
            fetch_scratch(nbits),
            5,
            cotangent,
        )
        rims = gate_rims(channels, block_size, ntensor, offset)
        own_dense = gate_dense(gate_w, offset, offset, channels)
        rim_dense = [gate_dense(gate_w, offset, rim.first, rim.width) for rim in rims]
        conv_out, conv_pull = jax.vjp(partial(causal_conv, starts), branch_x, conv_loc)
        conv_low = conv_out.astype(BF16)
        rim_cells = [rim.fetch(conv_low) for rim in rims]
        gate_pre = jnp.dot(conv_low, own_dense, preferred_element_type=F32)
        for cells, dense in zip(rim_cells, rim_dense):
            gate_pre = gate_pre + jnp.dot(cells, dense, preferred_element_type=F32)
        mixed_low, states = scan_call(
            forward_scan_kernel,
            (shape((group_rows, channels), BF16), shape((group_rows, channels), F32)),
            conv_low,
            gate_pre,
            branch_y,
            soft,
            since,
        )
    middle, mid_rows = call_kernel(
        partial(middle_kernel, nbits),
        (shape((own_rows, width), F32), shape((group_rows, width), BF16)),
        scatter_scratch(own_rows, width, nbits) + gather_sems(nbits),
        1,
        rows_times(mixed_low, wout_loc).astype(BF16),
        tokens,
        gain_mid,
    )
    pre = jnp.dot(mid_rows, both_loc, preferred_element_type=F32)
    hidden, act_pull = jax.vjp(geglu, pre[:, :units], pre[:, units:])
    hidden_low = hidden.astype(BF16)
    grad_wd = inner_rows(cot_rows, hidden_low).astype(BF16)
    sum_wd = lax.psum_scatter(grad_wd, "dp", scatter_dimension=0, tiled=True)
    grad_wd, wd_loc = lax.optimization_barrier((grad_wd, wd_loc))
    d_hidden = jnp.dot(cot_rows, wd_loc, preferred_element_type=F32)
    d_gate, d_up = act_pull(d_hidden)
    d_pre = jnp.concatenate([d_gate.astype(BF16), d_up.astype(BF16)], axis=1)
    grad_both = inner_rows(mid_rows, d_pre).astype(BF16)
    sum_both = lax.psum_scatter(grad_both, "dp", scatter_dimension=0, tiled=True)
    d_pre, grad_both = lax.optimization_barrier((d_pre, grad_both))
    d_mid_part = rows_times(d_pre, both_loc).astype(BF16)
    d_middle, d_mixer, d_gain_mid = call_kernel(
        partial(turn_kernel, nbits),
        (
            shape((own_rows, width), F32),
            shape((group_rows, width), BF16),
            shape((8, width), F32),
        ),
        scatter_scratch(own_rows, width, nbits) + gather_sems(nbits),
        2,
        d_mid_part,
        cotangent,
        middle,
        gain_mid,
    )
    d_mixer, sum_wd = lax.optimization_barrier((d_mixer, sum_wd))
    d_mixed_in = jnp.dot(d_mixer, wout_loc, preferred_element_type=F32)
    unit = math.gcd(channels, block_size)
    ffn_part = rows_times(hidden_low, wd_loc).astype(BF16)
    merged = half_blocks and nbits <= 2
    if half_blocks:
        found = call_kernel(
            partial(recurrence_back_kernel, taps, nbits, merged),
            (
                shape((group_rows, 2 * channels), BF16),
                shape((channels // unit * 2, block_size, unit), BF16),
                shape((8, channels), F32),
            )
            + ((shape((own_rows, width), BF16),) if merged else ()),
            [
                pltpu.VMEM((group_rows, channels), F32),
                pltpu.VMEM((group_rows, 2 * channels), BF16),
                pltpu.VMEM((group_rows, unit), BF16),
                pltpu.VMEM((group_rows, unit), BF16),
                pltpu.VMEM((taps + 1, 8, channels), F32),
                pltpu.SemaphoreType.DMA((1,)),
                pltpu.SemaphoreType.DMA((1,)),
            ]
            + (scatter_scratch(own_rows, width, nbits) if merged else []),
            6,
            d_mixed_in,
            window,
            gate_pre,
            branches,
            states,
            taps_pad,
            soft,
            slope_soft,
            since,
            w_window,
            *((ffn_part, middle) if merged else ()),
        )
        d_branches, gate_grad, own_small = found[:3]
        d_branches, sum_both = lax.optimization_barrier((d_branches, sum_both))
        gate_grad = gate_grad.reshape(channels // unit * 2 * block_size, unit)
    else:
        d_conv, d_gate_low, d_branch_y, d_decay = scan_call(
            backward_scan_kernel,
            (
                shape((group_rows, channels), F32),
                shape((group_rows, 2 * channels), BF16),
                shape((group_rows, channels), BF16),
                shape((8, channels), F32),
            ),
            d_mixed_in,
            conv_low,
            gate_pre,
            branch_y,
            states,
            soft,
            slope_soft,
            since,
        )
        given = [rows_times(d_gate_low, dense).astype(BF16) for dense in rim_dense]
        taken = [rim.give(part) for rim, part in zip(rims, given)]
        d_conv_out = d_conv + rows_times(d_gate_low, own_dense)
        for rim, part in zip(rims, taken):
            d_conv_out = rim.add(d_conv_out, part)
        d_branch_x, grad_conv_loc = conv_pull(d_conv_out)
        d_branches = jnp.concatenate([d_branch_y, d_branch_x.astype(BF16)], axis=1)
        base = offset // block_size * block_size - rims[0].room
        window_rows = rims[0].window(channels)
        picked = jnp.zeros((window_rows, 2 * channels), F32)
        for first, cells in [(offset, conv_low)] + [(r.first, c) for r, c in zip(rims, rim_cells)]:
            part = inner_rows(cells, d_gate_low)
            same = same_block(first, cells.shape[1], offset, channels, block_size)
            part = jnp.where(jnp.concatenate([same, same], axis=1), part, 0.0)
            picked = lax.dynamic_update_slice(picked, part, (first - base, jnp.int32(0)))
        picked = picked.reshape(window_rows // block_size, block_size, 2, channels // unit, unit)
        gate_grad = picked.sum(axis=0).astype(BF16).transpose(2, 1, 0, 3)
        gate_grad = gate_grad.reshape(channels // unit * 2 * block_size, unit)
        own_small = jnp.concatenate(
            [
                grad_conv_loc,
                jnp.sum(d_decay, axis=0, keepdims=True),
                jnp.zeros((7 - taps, channels), F32),
            ],
            axis=0,
        )

    grad_wout = inner_rows(d_mixer, mixed_low).astype(BF16)
    grad_wyx = inner_rows(normed_rows, d_branches).astype(BF16)
    d_normed = rows_times(d_branches, wyx_loc).astype(BF16)

    pieces = [halved(grad, ndp) for grad in (gate_grad, grad_wout, grad_wyx)]
    peers = ntensor - 1
    gate_rows = gate_grad.shape[0] // ndp
    dma = pltpu.SemaphoreType.DMA
    scratch = scatter_scratch(own_rows, width, nbits)
    scratch += line_scratch(ndp, gate_rows, unit) + line_scratch(ndp, dp_rows, channels)
    if tiled:
        scratch += line_scratch(ndp, dp_rows, channels) * 2
    else:
        scratch += line_scratch(ndp, dp_rows, 2 * channels)
    scratch += [
        pltpu.VMEM((8, width), F32),
        pltpu.VMEM((ntensor, 8, channels), F32),
        pltpu.VMEM((peers, 8, channels), F32),
        pltpu.VMEM((8, channels), F32),
        pltpu.VMEM((ndp - 1, 8, channels), F32),
    ]
    scratch += [dma((peers,)), dma((peers,)), dma((ndp - 1,)), dma((ndp - 1,))]
    scratch += [dma((peers,)), dma((peers,)), dma((peers + ndp,)), dma((peers + ndp,))]
    grad_input, sum_wout, sum_wy, sum_wx, gate_all, small_all = call_kernel(
        partial(leave_kernel, nbits, tiled),
        (shape((own_rows, width), F32),)
        + (shape((dp_rows, channels), F32),) * 3
        + (
            shape((ntensor, ndp // 2, 2, gate_rows, unit), BF16),
            shape((ntensor, 8, channels), F32),
        ),
        scratch,
        3,
        d_normed,
        tokens,
        d_middle,
        gain_in,
        own_small,
        d_gain_mid,
        *pieces,
        far_in=(6, 7, 8),
    )
    if merged:
        mixed = found[3]
    else:
        (mixed,) = call_kernel(
            partial(result_kernel, nbits),
            (shape((own_rows, width), BF16),),
            scatter_scratch(own_rows, width, nbits),
            4,
            ffn_part,
            middle,
        )
    sum_gate, sum_wy, sum_wx, sum_conv, sum_decay, sum_gain_in, sum_gain_mid = finish(
        gate_all, small_all, sum_wy, sum_wx, taps, gate_w.shape
    )
    return (
        mixed,
        grad_input,
        sum_gain_in,
        sum_wy,
        sum_wx,
        sum_conv,
        sum_gate,
        sum_decay,
        sum_wout,
        sum_gain_mid,
        sum_both[:, :units].astype(F32),
        sum_both[:, units:].astype(F32),
        sum_wd.astype(F32),
    )


def solution(mesh):
    split = P(("dp", "tensor"), None)
    weight = P("dp", "tensor")
    return jax.shard_map(
        body,
        mesh=mesh,
        in_specs=(
            split,
            P(("dp", "tensor")),
            split,
            P(),
            weight,
            weight,
            P(),
            P(),
            P(),
            weight,
            P(),
            weight,
            weight,
            weight,
        ),
        out_specs=(
            split,
            split,
            P(),
            weight,
            weight,
            P(),
            P(),
            P(),
            weight,
            P(),
            weight,
            weight,
            weight,
        ),
        check_vma=False,
    )
```

```python
import math
from functools import partial

import jax
import jax.numpy as jnp
from jax import lax
from jax.experimental import pallas as pl
from jax.experimental.pallas import tpu as pltpu
from jax.sharding import PartitionSpec as P

EPSILON = 1e-06
MESH = pl.DeviceIdType.MESH
VMEM_BYTES = 56 * 1024 * 1024
CHUNK = 16
F32 = jnp.float32
BF16 = jnp.bfloat16


def subsets(bits):
    found = [()]
    for bit in bits:
        found = found + [chosen + (bit,) for chosen in found]
    return found


def flipped(index, bits):
    for bit in bits:
        mine = (index // (1 << bit)) % 2
        index = index + (1 - 2 * mine) * (1 << bit)
    return index


def log2_of(count):
    assert count & (count - 1) == 0
    return count.bit_length() - 1


def greet(axis_bits):
    barrier = pltpu.get_barrier_semaphore()
    for axis, bit in axis_bits:
        peer = flipped(lax.axis_index(axis), (bit,))
        pl.semaphore_signal(barrier, inc=1, device_id={axis: peer}, device_id_type=MESH)
    pl.semaphore_wait(barrier, len(axis_bits))


def halves_of(nbits, columns):
    half = columns // 2
    ups = tuple(range(nbits))
    return ((ups, 0, half), (ups[::-1], half, half))


class Gather:
    def __init__(self, ref, rows, nbits, send_sems, recv_sems):
        self.ref, self.rows, self.nbits = ref, rows, nbits
        self.sems = (send_sems, recv_sems)
        self.me = lax.axis_index("tensor")
        self.plan = []
        number = 0
        for half, (order, at, width) in enumerate(halves_of(nbits, ref.shape[1])):
            for step, bit in enumerate(order):
                for known in subsets(order[:step]):
                    self.plan.append((half, step, known, bit, at, width, number))
                    number += 1
        self.count = number

    def copy(self, item):
        half, step, known, bit, at, width, number = item
        row = pl.multiple_of(flipped(self.me, known) * self.rows, self.rows)
        piece = self.ref.at[pl.ds(row, self.rows), pl.ds(at, width)]
        return pltpu.make_async_remote_copy(
            src_ref=piece,
            dst_ref=piece,
            send_sem=self.sems[0].at[number],
            recv_sem=self.sems[1].at[number],
            device_id={"tensor": flipped(self.me, (bit,))},
            device_id_type=MESH,
        )

    def begin(self):
        for item in sorted(self.plan, key=lambda it: it[1]):
            if item[2] == ():
                self.copy(item).start()

    def advance(self, step):
        for item in self.plan:
            half, at_step, known, bit, at, width, number = item
            if at_step == step:
                self.copy(item).wait_recv()
                block = known + (bit,)
                for later in self.plan:
                    if later[0] == half and set(later[2]) == set(block):
                        self.copy(later).start()

    def finish(self, step=0):
        for at_step in range(step, self.nbits):
            self.advance(at_step)
        for item in self.plan:
            self.copy(item).wait_send()


def gather_copies(nbits):
    return 2 * ((1 << nbits) - 1)


class Scatter:
    def __init__(self, ref, landed, staged, rows, nbits, send_sems, recv_sems):
        self.ref, self.landed, self.staged = ref, landed, staged
        self.rows, self.nbits = rows, nbits
        self.sems = (send_sems, recv_sems)
        self.me = lax.axis_index("tensor")
        self.plan, self.slot = [], {}
        number = 0
        for half, (order, at, width) in enumerate(halves_of(nbits, ref.shape[1])):
            for step, bit in enumerate(order):
                for rest in subsets(order[step + 1 :])[::-1]:
                    self.plan.append((half, step, rest, bit, at, width, number))
                    if step > 0:
                        self.slot[number] = len(self.slot)
                    number += 1

    def copy(self, item):
        half, step, rest, bit, at, width, number = item
        if step == 0:
            row = pl.multiple_of(flipped(self.me, rest + (bit,)) * self.rows, self.rows)
            source = self.ref.at[pl.ds(row, self.rows), pl.ds(at, width)]
        else:
            source = self.staged.at[self.slot[number]]
        return pltpu.make_async_remote_copy(
            src_ref=source,
            dst_ref=self.landed.at[number],
            send_sem=self.sems[0].at[number],
            recv_sem=self.sems[1].at[number],
            device_id={"tensor": flipped(self.me, (bit,))},
            device_id_type=MESH,
        )

    def begin(self):
        for item in sorted(self.plan, key=lambda it: (len(it[2]) == 0)):
            if item[1] == 0:
                self.copy(item).start()

    def partial_sum(self, half, block, before, row, size):
        at, width = halves_of(self.nbits, self.ref.shape[1])[half][1:]
        base = pl.multiple_of(flipped(self.me, block) * self.rows + row, size)
        total = self.ref[pl.ds(base, size), pl.ds(at, width)].astype(F32)
        for it in self.plan:
            if it[0] == half and it[1] < before and set(it[2]) == set(block):
                total = total + self.landed[it[6], pl.ds(row, size), :].astype(F32)
        return total

    def advance(self, step):
        for half in range(2):
            for item in self.plan:
                if item[0] == half and item[1] == step:
                    self.copy(item).wait_recv()
            for item in self.plan:
                if item[0] == half and item[1] == step + 1:

                    def fill(row, item=item):
                        value = self.partial_sum(
                            item[0], item[2] + (item[3],), item[1], row, CHUNK
                        )
                        where = (self.slot[item[6]], pl.ds(row, CHUNK))
                        self.staged[where + (slice(None),)] = value.astype(BF16)

                    chunks(self.rows, fill)
                    self.copy(item).start()

    def run(self):
        for step in range(self.nbits):
            self.advance(step)

    def total(self, row, size):
        return jnp.concatenate(
            [self.partial_sum(half, (), self.nbits, row, size) for half in range(2)], axis=1
        )

    def drain(self):
        for item in self.plan:
            self.copy(item).wait_send()


def scatter_scratch(rows, columns, nbits):
    copies = gather_copies(nbits)
    later = max(1, copies - (1 << nbits))
    return [
        pltpu.VMEM((copies, rows, columns // 2), BF16),
        pltpu.VMEM((later, rows, columns // 2), BF16),
        pltpu.SemaphoreType.DMA((copies,)),
        pltpu.SemaphoreType.DMA((copies,)),
    ]


def gather_sems(nbits):
    copies = gather_copies(nbits)
    return [pltpu.SemaphoreType.DMA((copies,)), pltpu.SemaphoreType.DMA((copies,))]


def tensor_bits(nbits):
    return [("tensor", bit) for bit in range(nbits)]


def rms_scale_of(values):
    return lax.rsqrt(jnp.mean(values * values, axis=-1, keepdims=True) + EPSILON)


def chunks(rows, body):
    def step(i, carry):
        body(pl.multiple_of(i * CHUNK, CHUNK))
        return carry

    lax.fori_loop(0, rows // CHUNK, step, 0)


def own_row(row, rows):
    return pl.multiple_of(lax.axis_index("tensor") * rows + row, CHUNK)


def dp_place():
    me = lax.axis_index("dp")
    return me // 2, me % 2, lax.axis_size("dp") // 2


def dp_index(chip, core):
    return chip * 2 + core


UP, DOWN = 1, -1


class LineGather:
    def __init__(self, own, whole, send_sems, recv_sems, columns=None):
        self.own, self.whole = own, whole
        self.sems = (send_sems, recv_sems)
        self.chip, self.core, self.chips = dp_place()
        self.rows = own.shape[0]
        self.columns = slice(None) if columns is None else columns

    def block(self, chip):
        row = pl.multiple_of(dp_index(chip, self.core) * self.rows, self.rows)
        return self.whole.at[pl.ds(row, self.rows), self.columns]

    def has(self, way, distance):
        return self.chip >= distance if way == UP else self.chip + distance < self.chips

    def number(self, way, distance):
        return (0 if way == UP else self.chips) + distance

    def along(self, way, distance):
        block = self.block(self.chip - way * distance)
        return pltpu.make_async_remote_copy(
            src_ref=self.own if distance == 0 else block,
            dst_ref=block,
            send_sem=self.sems[0].at[self.number(way, distance)],
            recv_sem=self.sems[1].at[self.number(way, distance + 1)],
            device_id={"dp": dp_index(self.chip + way, self.core)},
            device_id_type=MESH,
        )

    def arrival(self, way, distance):
        block = self.block(self.chip - way * distance)
        return pltpu.make_async_remote_copy(
            src_ref=block,
            dst_ref=block,
            send_sem=self.sems[0].at[self.number(way, distance)],
            recv_sem=self.sems[1].at[self.number(way, distance)],
            device_id={"dp": dp_index(self.chip + way, self.core)},
            device_id_type=MESH,
        )

    def across(self, way, distance):
        block = self.block(self.chip - way * distance)
        number = 2 * self.chips + self.number(way, distance)
        return pltpu.make_async_remote_copy(
            src_ref=self.own if distance == 0 else block,
            dst_ref=block,
            send_sem=self.sems[0].at[number],
            recv_sem=self.sems[1].at[number],
            device_id={"dp": dp_index(self.chip, 1 - self.core)},
            device_id_type=MESH,
        )

    def local(self):
        return pltpu.make_async_copy(
            self.own, self.block(self.chip), self.sems[0].at[4 * self.chips]
        )

    def begin(self):
        for way in (UP, DOWN):

            @pl.when(self.has(-way, 1))
            def _(way=way):
                self.along(way, 0).start()

        self.across(UP, 0).start()
        self.local().start()

    def pass_on(self, distance):
        for way in (UP, DOWN):

            @pl.when(self.has(way, distance))
            def _(way=way):
                self.arrival(way, distance).wait_recv()

                @pl.when(self.has(-way, 1))
                def _():
                    self.along(way, distance).start()

                self.across(way, distance).start()

    def finish(self):
        self.across(UP, 0).wait()
        self.local().wait()
        for way in (UP, DOWN):
            for distance in range(self.chips):

                @pl.when(self.has(way, distance) & self.has(-way, 1))
                def _(way=way, distance=distance):
                    self.along(way, distance).wait_send()

                if distance:

                    @pl.when(self.has(way, distance))
                    def _(way=way, distance=distance):
                        self.across(way, distance).wait()


def line_sems(ndp):
    chips = ndp // 2
    return [pltpu.SemaphoreType.DMA((4 * chips + 1,)), pltpu.SemaphoreType.DMA((4 * chips + 1,))]


def greet_peers(nbits, all_tensor, whole_dp):
    me = lax.axis_index("tensor")
    chip, core, chips = dp_place()
    barrier = pltpu.get_barrier_semaphore()

    def signal(target):
        pl.semaphore_signal(barrier, inc=1, device_id=target, device_id_type=MESH)

    met = 0
    for chosen in subsets(tuple(range(nbits))):
        if chosen and (all_tensor or len(chosen) == 1):
            signal({"tensor": flipped(me, chosen)})
            met += 1
    if whole_dp:
        for shift in range(chips):
            for turn in range(2):
                if (shift, turn) != (0, 0):
                    other = dp_index((chip + shift) % chips, core + turn * (1 - 2 * core))
                    signal({"dp": other})
                    met += 1
    else:
        signal({"dp": dp_index(chip, 1 - core)})
        met += 1

        for shift in sorted({1 % chips, chips - 1} - {0}):
            signal({"dp": dp_index((chip + shift) % chips, core)})
            met += 1

    pl.semaphore_wait(barrier, met)


def enter_kernel(
    nbits, parts_yx, tokens, seg, gain, *refs
):
    w_yx, w_out = refs[:parts_yx], refs[parts_yx]
    normed_all, seg_all, wyx_all, wout_all, s0, r0, s2, r2, l0, *line = refs[parts_yx + 1 :]
    rows = tokens.shape[0]
    me = lax.axis_index("tensor")
    peers = [chosen for chosen in subsets(tuple(range(nbits))) if chosen]
    greet_peers(nbits, True, False)
    width = wyx_all.shape[1] // parts_yx
    lines = [
        LineGather(
            own,
            wyx_all,
            line[2 * number],
            line[2 * number + 1],
            pl.ds(number * width, width) if parts_yx > 1 else None,
        )
        for number, own in enumerate(w_yx)
    ]
    lines.append(LineGather(w_out, wout_all, *line[2 * parts_yx : 2 * parts_yx + 2]))
    for item in lines:
        item.begin()

    def norm(row):
        values = tokens[pl.ds(row, CHUNK), :].astype(F32)
        scaled = values * rms_scale_of(values) * gain[...]
        normed_all[pl.ds(own_row(row, rows), CHUNK), :] = scaled.astype(BF16)

    chunks(rows, norm)
    gather = Gather(normed_all, rows, nbits, s0, r0)
    gather.begin()
    seg_own = pltpu.make_async_copy(seg, seg_all.at[me], l0.at[0])
    seg_own.start()
    seg_copies = [
        pltpu.make_async_remote_copy(
            src_ref=seg,
            dst_ref=seg_all.at[me],
            send_sem=s2.at[number],
            recv_sem=r2.at[number],
            device_id={"tensor": flipped(me, chosen)},
            device_id_type=MESH,
        )
        for number, chosen in enumerate(peers)
    ]
    for copy in seg_copies:
        copy.start()
    chips = lines[0].chips
    for item in lines:
        item.pass_on(1)
    gather.advance(0)
    for distance in range(2, chips):
        for item in lines:
            item.pass_on(distance)
    gather.finish(1)
    for item in lines:
        item.finish()
    for copy in seg_copies:
        copy.wait()
    seg_own.wait()


class Fetch:
    def __init__(self, nbits, cot, cot_all, s0, r0, l0):
        rows = cot.shape[0]
        own = pl.multiple_of(lax.axis_index("tensor") * rows, rows)
        self.local = pltpu.make_async_copy(cot, cot_all.at[pl.ds(own, rows), :], l0.at[0])
        self.gather = Gather(cot_all, rows, nbits, s0, r0)

    def begin(self):
        self.local.wait()
        self.gather.begin()

    def advance(self):
        self.gather.advance(0)

    def finish(self):
        self.gather.finish(1)


def fetch_scratch(nbits):
    return gather_sems(nbits) + [pltpu.SemaphoreType.DMA((1,))]


def fetch_kernel(nbits, cot, cot_all, *sems):
    greet(tensor_bits(nbits))
    fetch = Fetch(nbits, cot, cot_all, *sems)
    fetch.local.start()
    fetch.begin()
    fetch.advance()
    fetch.finish()


def middle_kernel(
    nbits, mixer, tokens, gain, middle, mid_all, landed, staged, s0, r0, s1, r1
):
    rows = tokens.shape[0]
    greet(tensor_bits(nbits))
    scatter = Scatter(mixer, landed, staged, rows, nbits, s0, r0)
    scatter.begin()
    scatter.run()

    def norm(row):
        values = tokens[pl.ds(row, CHUNK), :].astype(F32) + scatter.total(row, CHUNK)
        middle[pl.ds(row, CHUNK), :] = values
        scaled = values * rms_scale_of(values) * gain[...]
        mid_all[pl.ds(own_row(row, rows), CHUNK), :] = scaled.astype(BF16)

    chunks(rows, norm)
    gather = Gather(mid_all, rows, nbits, s1, r1)
    gather.begin()
    gather.finish()
    scatter.drain()


def result_kernel(nbits, ffn, middle, mixed, landed, staged, s0, r0):
    rows = middle.shape[0]
    greet(tensor_bits(nbits))
    scatter = Scatter(ffn, landed, staged, rows, nbits, s0, r0)
    scatter.begin()
    scatter.run()

    def add(row):
        values = middle[pl.ds(row, CHUNK), :] + scatter.total(row, CHUNK)
        mixed[pl.ds(row, CHUNK), :] = values.astype(BF16)

    chunks(rows, add)
    scatter.drain()


def norm_pull(values, gain, cotangent):
    scale = rms_scale_of(values)
    unit = values * scale
    inner = cotangent * gain
    back = scale * (inner - unit * jnp.mean(inner * unit, axis=-1, keepdims=True))
    return back, cotangent * unit


def eight_rows(values):
    total = values[0:8]
    for at in range(8, CHUNK, 8):
        total = total + values[at : at + 8]
    return total


class Product:
    def __init__(self, left, right, out, held, sems):
        self.left, self.right, self.out = left, right, out
        self.held, self.sems = held, sems
        self.width = held.shape[1]
        self.count = right.shape[0] // self.width
        self.done = 0

    def fetch(self, block):
        return pltpu.make_async_copy(
            self.right.at[pl.ds(block * self.width, self.width), :],
            self.held.at[block % 2],
            self.sems.at[block % 2],
        )

    def begin(self):
        self.fetch(0).start()

    def work(self, blocks):
        for block in range(self.done, min(self.done + blocks, self.count)):
            if block + 1 < self.count:
                self.fetch(block + 1).start()
            self.fetch(block).wait()

            def rows(span, block=block):
                found = times_transposed(self.left[span, :], self.held[block % 2])
                at = slice(block * self.width, (block + 1) * self.width)
                self.out[span, at] = found.astype(BF16)

            parts(self.left.shape[0], rows)
        self.done = min(self.done + blocks, self.count)


PRODUCT_BLOCK = 256


def product_scratch(depth):
    return [pltpu.VMEM((2, PRODUCT_BLOCK, depth), BF16), pltpu.SemaphoreType.DMA((2,))]


def turn_kernel(
    nbits,
    d_norm,
    cot,
    middle,
    gain,
    hidden,
    w_down,
    d_middle,
    d_mixer,
    d_gain,
    ffn,
    landed,
    staged,
    s0,
    r0,
    s1,
    r1,
    *product,
):
    rows = middle.shape[0]
    ahead = Product(hidden, w_down, ffn, *product)
    ahead.begin()
    greet(tensor_bits(nbits))
    scatter = Scatter(d_norm, landed, staged, rows, nbits, s0, r0)
    scatter.begin()
    d_gain[...] = jnp.zeros_like(d_gain)
    ahead.work(4)
    for step in range(nbits):
        scatter.advance(step)
        if step + 1 < nbits:
            ahead.work(2)

    def pull(row):
        span = pl.ds(row, CHUNK)
        back, gains = norm_pull(middle[span, :], gain[...], scatter.total(row, CHUNK))
        values = cot[span, :].astype(F32) + back
        d_middle[span, :] = values
        d_mixer[pl.ds(own_row(row, rows), CHUNK), :] = values.astype(BF16)
        d_gain[...] += eight_rows(gains)

    chunks(rows, pull)
    gather = Gather(d_mixer, rows, nbits, s1, r1)
    gather.begin()
    ahead.work(2)
    gather.advance(0)
    ahead.work(ahead.count)
    gather.finish(1)
    scatter.drain()


class LineSum:
    def __init__(self, whole, kept, swapped, staged, landed, send_sems, recv_sems, columns=None):
        self.whole, self.kept, self.swapped = whole, kept, swapped
        self.staged, self.landed = staged, landed
        self.sems = (send_sems, recv_sems)
        self.columns = columns
        self.chip, self.core, self.chips = dp_place()
        self.rows = whole.shape[2]

    def half(self, core):
        if self.columns is None:
            return self.whole.at[:, core]
        return self.whole.at[:, core, :, self.columns]

    def local(self):
        return pltpu.make_async_copy(
            self.half(self.core), self.kept, self.sems[0].at[2 * self.chips]
        )

    def swap(self):
        return pltpu.make_async_remote_copy(
            src_ref=self.half(1 - self.core),
            dst_ref=self.swapped,
            send_sem=self.sems[0].at[0],
            recv_sem=self.sems[1].at[0],
            device_id={"dp": dp_index(self.chip, 1 - self.core)},
            device_id_type=MESH,
        )

    def has(self, way, distance):
        return self.chip + distance < self.chips if way == UP else self.chip >= distance

    def slot(self, way, distance):
        return (0 if way == UP else self.chips - 1) + distance

    def hop(self, way, distance):
        return pltpu.make_async_remote_copy(
            src_ref=self.staged.at[self.slot(way, distance - 1)],
            dst_ref=self.landed.at[self.slot(way, distance - 1)],
            send_sem=self.sems[0].at[1 + self.slot(way, distance - 1)],
            recv_sem=self.sems[1].at[1 + self.slot(way, distance - 1)],
            device_id={"dp": dp_index(self.chip + way, self.core)},
            device_id_type=MESH,
        )

    def arrival(self, way, distance):
        number = self.slot(way, distance)
        return pltpu.make_async_remote_copy(
            src_ref=self.landed.at[number],
            dst_ref=self.landed.at[number],
            send_sem=self.sems[0].at[1 + number],
            recv_sem=self.sems[1].at[1 + number],
            device_id={"dp": dp_index(self.chip - way, self.core)},
            device_id_type=MESH,
        )

    def begin(self):
        self.swap().start()
        self.local().start()

    def both(self, chip, span):
        return self.kept[chip, span, :].astype(F32) + self.swapped[chip, span, :].astype(F32)

    def send(self, distance):
        if distance == self.chips - 1:
            self.local().wait()
            self.swap().wait_recv()
        for way in (UP, DOWN):

            @pl.when(self.has(way, distance))
            def _(way=way):
                chip = self.chip + way * distance
                slot = self.slot(way, distance - 1)

                def first(row):
                    span = pl.ds(row, CHUNK)
                    self.staged[slot, span, :] = self.both(chip, span).astype(BF16)

                def later(row):
                    span = pl.ds(row, CHUNK)
                    total = self.both(chip, span) + self.landed[
                        self.slot(way, distance), span, :
                    ].astype(F32)
                    self.staged[slot, span, :] = total.astype(BF16)

                if distance == self.chips - 1:
                    chunks(self.rows, first)
                else:

                    @pl.when(self.has(-way, 1))
                    def _():
                        self.arrival(way, distance).wait_recv()
                        chunks(self.rows, later)

                    @pl.when(jnp.logical_not(self.has(-way, 1)))
                    def _():
                        chunks(self.rows, first)

                self.hop(way, distance).start()

    def finish(self, store):
        below, above = self.has(DOWN, 1), self.has(UP, 1)

        def fill(slots):
            for way in slots:
                self.arrival(way, 0).wait_recv()

            def one(row):
                span = pl.ds(row, CHUNK)
                total = self.both(self.chip, span)
                for way in slots:
                    total = total + self.landed[self.slot(way, 0), span, :].astype(F32)
                store(span, total)

            chunks(self.rows, one)

        @pl.when(below & above)
        def _():
            fill((UP, DOWN))

        @pl.when(jnp.logical_not(above))
        def _():
            fill((UP,))

        @pl.when(jnp.logical_not(below))
        def _():
            fill((DOWN,))

    def drain(self):
        self.swap().wait_send()
        for way in (UP, DOWN):
            for distance in range(1, self.chips):

                @pl.when(self.has(way, distance))
                def _(way=way, distance=distance):
                    self.hop(way, distance).wait_send()


def line_scratch(ndp, rows, columns):
    chips = ndp // 2
    return [
        pltpu.VMEM((chips, rows, columns), BF16),
        pltpu.VMEM((chips, rows, columns), BF16),
        pltpu.VMEM((2 * chips - 2, rows, columns), BF16),
        pltpu.VMEM((2 * chips - 2, rows, columns), BF16),
        pltpu.SemaphoreType.DMA((2 * chips + 1,)),
        pltpu.SemaphoreType.DMA((2 * chips + 1,)),
    ]


RING = 6


def leave_kernel(nbits, tiled, *refs):
    refs = list(refs)

    def take(count):
        taken = refs[:count]
        del refs[:count]
        return taken

    d_norm, tokens, d_middle, gain, own_small, d_gain_mid = take(6)
    pieces = take(2)
    grad_input, sum_y, sum_x, gate_all, small_all = take(5)
    landed, staged, s0, r0 = take(4)
    share = small_all.shape[2]
    gate = LineSum(pieces[0], *take(RING))
    if tiled:
        lines = [LineSum(pieces[1], *take(RING), pl.ds(at, share)) for at in (0, share)]
    else:
        lines = [LineSum(pieces[1], *take(RING))]
    d_gain, gains, gains_landed, small, small_landed = take(5)
    gain_s, gain_r, vec_s, vec_r, join_s, join_r, gate_s, gate_r = take(8)
    rows = tokens.shape[0]
    me = lax.axis_index("tensor")
    chip, core, chips = dp_place()
    peers = [chosen for chosen in subsets(tuple(range(nbits))) if chosen]
    others = [(shift, turn) for shift in range(chips) for turn in range(2)][1:]
    greet_peers(nbits, True, True)
    for line in [gate] + lines:
        line.begin()
    scatter = Scatter(d_norm, landed, staged, rows, nbits, s0, r0)
    scatter.begin()
    d_gain[...] = jnp.zeros_like(d_gain)
    far = list(range(chips - 1, 0, -1))
    for distance in far:
        gate.send(distance)
    for line in lines:
        line.send(far[0])
    scatter.advance(0)
    for distance in far[1:-1]:
        for line in lines:
            line.send(distance)
    for step in range(1, nbits):
        scatter.advance(step)

    def pull(row):
        span = pl.ds(row, CHUNK)
        back, parts = norm_pull(
            tokens[span, :].astype(F32), gain[...], scatter.total(row, CHUNK)
        )
        grad_input[span, :] = d_middle[span, :] + back
        d_gain[...] += eight_rows(parts)

    chunks(rows, pull)
    def store_gate(span, value):
        gate_all[me, chip, core, span, :] = value.astype(BF16)

    def gate_copy(number, ref, target):
        return pltpu.make_async_remote_copy(
            src_ref=ref,
            dst_ref=ref,
            send_sem=gate_s.at[number],
            recv_sem=gate_r.at[number],
            device_id=target,
            device_id_type=MESH,
        )

    def gate_line(shift):
        target = {"dp": dp_index((chip + shift) % chips, core)}
        return gate_copy(shift - 1, gate_all.at[me, chip, core], target)

    def gate_tensor(number, chosen):
        target = {"tensor": flipped(me, chosen)}
        return gate_copy(chips - 1 + number, gate_all.at[me, :, core], target)

    def gate_core():
        target = {"dp": dp_index(chip, 1 - core)}
        return gate_copy(chips - 1 + len(peers), gate_all.at[:, :, core], target)

    def start_gate():
        gate.finish(store_gate)
        for shift in range(1, chips):
            gate_line(shift).start()

    top = jnp.sum(d_gain[...], axis=0, keepdims=True)
    low = jnp.sum(d_gain_mid[...], axis=0, keepdims=True)
    place8 = lax.broadcasted_iota(jnp.int32, (8, share), 0)
    for index in range(1 << nbits):
        span = slice(index * share, (index + 1) * share)
        gains[index] = jnp.where(
            place8 == 6, top[:, span], jnp.where(place8 == 7, low[:, span], 0.0)
        )

    def gain_copy(number, chosen):
        peer = flipped(me, chosen)
        return pltpu.make_async_remote_copy(
            src_ref=gains.at[peer],
            dst_ref=gains_landed.at[number],
            send_sem=gain_s.at[number],
            recv_sem=gain_r.at[number],
            device_id={"tensor": peer},
            device_id_type=MESH,
        )

    for number, chosen in enumerate(peers):
        gain_copy(number, chosen).start()
    start_gate()
    if len(far) > 1:
        for line in lines:
            line.send(far[-1])
    total = own_small[...] + gains[me]
    for number, chosen in enumerate(peers):
        gain_copy(number, chosen).wait_recv()
        total = total + gains_landed[number]
    small[...] = total

    def vec_copy(number, shift, turn):
        other = dp_index((chip + shift) % chips, core + turn * (1 - 2 * core))
        return pltpu.make_async_remote_copy(
            src_ref=small,
            dst_ref=small_landed.at[number],
            send_sem=vec_s.at[number],
            recv_sem=vec_r.at[number],
            device_id={"dp": other},
            device_id_type=MESH,
        )

    for number, (shift, turn) in enumerate(others):
        vec_copy(number, shift, turn).start()

    for shift in range(1, chips):
        gate_line(shift).wait_recv()
    for number, chosen in enumerate(peers):
        gate_tensor(number, chosen).start()
    total = small[...]
    for number, (shift, turn) in enumerate(others):
        vec_copy(number, shift, turn).wait_recv()
        total = total + small_landed[number]
    small_all[me] = total

    def join_copy(number, chosen):
        return pltpu.make_async_remote_copy(
            src_ref=small_all.at[me],
            dst_ref=small_all.at[me],
            send_sem=join_s.at[number],
            recv_sem=join_r.at[number],
            device_id={"tensor": flipped(me, chosen)},
            device_id_type=MESH,
        )

    for number, chosen in enumerate(peers):
        join_copy(number, chosen).start()
    for number, chosen in enumerate(peers):
        gate_tensor(number, chosen).wait_recv()
    gate_core().start()

    def store_in(*targets):
        def store(span, value):
            for number, ref in enumerate(targets):
                ref[span, :] = value[:, number * share : (number + 1) * share]

        return store

    if tiled:
        lines[0].finish(store_in(sum_y))
        lines[1].finish(store_in(sum_x))
    else:
        lines[0].finish(store_in(sum_y, sum_x))
    gate_core().wait()
    for shift in range(1, chips):
        gate_line(shift).wait_send()
    for number, chosen in enumerate(peers):
        gate_tensor(number, chosen).wait_send()
        gain_copy(number, chosen).wait_send()
        join_copy(number, chosen).wait()
    for number, (shift, turn) in enumerate(others):
        vec_copy(number, shift, turn).wait_send()
    scatter.drain()
    for line in [gate] + lines:
        line.drain()


def in_vmem(count):
    return [pl.BlockSpec(memory_space=pltpu.VMEM)] * count


def call_kernel(kernel, outs, scratch, number, *operands, far_in=(), far_out=(), cost_us=1):
    vmem = pl.BlockSpec(memory_space=pltpu.VMEM)
    far = pl.BlockSpec(memory_space=pl.ANY)
    return pl.pallas_call(
        kernel,
        out_shape=outs,
        in_specs=[far if i in far_in else vmem for i in range(len(operands))],
        out_specs=tuple(far if i in far_out else vmem for i in range(len(outs))),
        scratch_shapes=scratch,
        cost_estimate=pl.CostEstimate(
            flops=0, bytes_accessed=cost_us * 1_000_000, transcendentals=0
        ),
        compiler_params=pltpu.CompilerParams(
            collective_id=number, has_side_effects=True, vmem_limit_bytes=VMEM_BYTES
        ),
    )(*operands)


def sigmoid(values):
    return 1.0 / (1.0 + jnp.exp(-values))


def one_minus_exp(values):
    series = values / 7.0 + 1.0
    for order in (6.0, 5.0, 4.0, 3.0, 2.0):
        series = 1.0 + series * values / order
    return jnp.where(values > -0.3, -values * series, 1.0 - jnp.exp(values))


GELU_K = 0.7978845608028654
GELU_C = 0.044715


def gelu_parts(values):
    square = values * values
    bent = jnp.tanh(GELU_K * values * (1.0 + GELU_C * square))
    gelu = 0.5 * values * (1.0 + bent)
    slope = 0.5 * (1.0 + bent) + 0.5 * values * (1.0 - bent * bent) * GELU_K * (
        1.0 + 3.0 * GELU_C * square
    )
    return gelu, slope


def gate_terms(gate_a, gate_x, soft, since):
    sig_a = sigmoid(gate_a)
    sig_x = sigmoid(gate_x)
    log_decay = -8.0 * sig_a * soft
    decay = jnp.exp(log_decay)
    scale = jnp.sqrt(one_minus_exp(2.0 * log_decay))
    keep = since > 0.5
    return sig_a, sig_x, decay, jnp.where(keep, scale, 1.0), keep


def scan_down(decay, value, carry):
    place = lax.broadcasted_iota(jnp.int32, decay.shape, 0)
    for shift in (1, 2, 4):
        past = place >= shift
        moved = pltpu.roll(value, shift, 0)
        value = jnp.where(past, decay * moved + value, value)
        decay = jnp.where(past, decay * pltpu.roll(decay, shift, 0), decay)
    return decay * carry + value


def scan_up(decay, value, carry):
    place = lax.broadcasted_iota(jnp.int32, decay.shape, 0)
    factor = jnp.where(place < 7, pltpu.roll(decay, 7, 0), 1.0)
    for shift in (1, 2, 4):
        past = place < 8 - shift
        moved = pltpu.roll(value, 8 - shift, 0)
        value = jnp.where(past, factor * moved + value, value)
        factor = jnp.where(past, factor * pltpu.roll(factor, 8 - shift, 0), factor)
    return factor * carry + value


def forward_scan(conv_rows, gates, branch_y, soft, since, mixed, states, between=()):
    total_rows, width = states.shape

    def step(i, carry):
        row = pl.multiple_of(i * CHUNK, CHUNK)
        span = pl.ds(row, CHUNK)
        values = conv_rows(span).astype(F32)
        kept = []
        for at in range(0, CHUNK, 8):
            tile = pl.ds(row + at, 8)
            sig_a, sig_x, decay, scale, keep = gate_terms(
                gates[tile, :width], gates[tile, width:], soft[...], since[tile, :]
            )
            given = values[at : at + 8] * sig_x * scale
            state = scan_down(jnp.where(keep, decay, 0.0), given, carry)
            carry = state[7:8]
            states[tile, :] = state
            kept.append(state * gelu_parts(branch_y[tile, :])[0])
        mixed[span, :] = jnp.concatenate(kept, axis=0).astype(BF16)
        return carry

    steps, stretches = total_rows // CHUNK, len(between) + 1
    carry = jnp.zeros((1, width), F32)
    for stretch in range(stretches):
        first, last = stretch * steps // stretches, (stretch + 1) * steps // stretches
        carry = lax.fori_loop(first, last, step, carry)
        if stretch < len(between):
            between[stretch]()


def forward_scan_kernel(conv, gates, branch_y, soft, since, mixed, states):
    forward_scan(lambda span: conv[span, :], gates, branch_y, soft, since, mixed, states)


def backward_scan(
    d_mixed, conv_rows, gates, branch_y, states, soft, slope_soft, since, d_conv, d_gates, d_branch, d_decay
):
    total_rows, width = states.shape
    d_decay[...] = jnp.zeros_like(d_decay)

    def step(i, carry):
        row = pl.multiple_of(total_rows - CHUNK - i * CHUNK, CHUNK)
        span = pl.ds(row, CHUNK)
        values = conv_rows(span).astype(F32)
        kept = []
        for at in range(CHUNK - 8, -1, -8):
            tile = pl.ds(row + at, 8)
            soft_row = soft[...]
            sig_a, sig_x, decay, scale, keep = gate_terms(
                gates[tile, :width], gates[tile, width:], soft_row, since[tile, :]
            )
            value = values[at : at + 8]
            gelu, slope = gelu_parts(branch_y[tile, :])
            state = states[tile, :]
            upper = d_mixed[tile, :]
            held = jnp.where(keep, decay, 0.0)
            lam = scan_up(held, upper * gelu, carry)
            carry = held[0:1] * lam[0:1]
            d_conv[tile, :] = lam * sig_x * scale
            d_x = lam * value * scale * sig_x * (1.0 - sig_x)
            given = value * sig_x
            d_log = lam * (state - given * scale - given * decay * decay / scale)
            d_log = jnp.where(keep, d_log, 0.0)
            d_a = d_log * (-8.0 * soft_row) * sig_a * (1.0 - sig_a)
            d_decay[...] += d_log * (-8.0 * sig_a) * slope_soft[...]
            kept.append((d_a, d_x, upper * state * slope))
        kept = kept[::-1]
        d_gates[span, :width] = jnp.concatenate([k[0] for k in kept], axis=0).astype(BF16)
        d_gates[span, width:] = jnp.concatenate([k[1] for k in kept], axis=0).astype(BF16)
        d_branch[span, :] = jnp.concatenate([k[2] for k in kept], axis=0).astype(BF16)
        return carry

    lax.fori_loop(0, total_rows // CHUNK, step, jnp.zeros((1, width), F32))


def backward_scan_kernel(
    d_mixed, conv, gates, branch_y, states, soft, slope_soft, since, d_conv, d_gates, d_branch, d_decay
):
    backward_scan(
        d_mixed,
        lambda span: conv[span, :],
        gates,
        branch_y,
        states,
        soft,
        slope_soft,
        since,
        d_conv,
        d_gates,
        d_branch,
        d_decay,
    )


def times_transposed(left, right):
    return lax.dot_general(left, right, (((1,), (1,)), ((), ())), preferred_element_type=F32)


class HalfBlocks:
    def __init__(self, channels, block):
        self.odd = lax.axis_index("tensor") % 2
        self.half = block // 2
        self.block = block
        self.count = channels // block + 1
        self.channels = channels
        self.own = pl.multiple_of(self.odd * self.half, self.half)
        self.shared = (1 - self.odd) * (self.count - 1)
        self.mine_in_block = pl.multiple_of(self.odd * self.half, self.half)
        self.other_in_block = pl.multiple_of((1 - self.odd) * self.half, self.half)
        self.mine = pl.multiple_of((1 - self.odd) * (channels - self.half), self.half)
        self.pair = {"tensor": lax.axis_index("tensor") + 1 - 2 * self.odd}

    def full(self, index):
        block = index + self.odd
        return block, pl.multiple_of(index * self.block + self.odd * self.half, self.half)

    def span(self, block):
        return pl.ds(pl.multiple_of(block * self.block, self.block), self.block)

    def shared_part(self, start):
        return pl.ds(pl.multiple_of(self.shared * self.block + start, self.half), self.half)


PART = 256


def parts(rows, body):
    def step(i, carry):
        body(pl.ds(pl.multiple_of(i * PART, PART), PART))
        return carry

    lax.fori_loop(0, rows // PART, step, 0)


def recurrence_kernel(
    taps,
    nbits,
    branches,
    tap_rows,
    soft,
    since,
    weights,
    cot,
    mixed,
    states,
    window,
    gates,
    cot_all,
    send,
    recv,
    *sems,
):
    total_rows, width = states.shape
    block = weights.shape[2]
    place = HalfBlocks(width, block)
    branch_y, branch_x = branches.at[:, :width], branches.at[:, width:]
    greet(tensor_bits(nbits))
    fetch = Fetch(nbits, cot, cot_all, *sems)
    fetch.local.start()

    def conv(i, before):
        row = pl.multiple_of(i * CHUNK, CHUNK)
        kept = []
        for at in range(0, CHUNK, 8):
            tile = pl.ds(row + at, 8)
            values = branch_x[tile, :]
            line = lax.broadcasted_iota(jnp.int32, values.shape, 0)
            total = values * tap_rows[0:1, :]
            for tap in range(1, taps):
                moved = jnp.where(
                    line < tap, pltpu.roll(before, tap, 0), pltpu.roll(values, tap, 0)
                )
                moved = jnp.where(since[tile, :] > tap - 0.5, moved, 0.0)
                total = total + moved * tap_rows[tap : tap + 1, :]
            kept.append(total)
            before = values
        window[pl.ds(row, CHUNK), pl.ds(place.own, width)] = jnp.concatenate(
            kept, axis=0
        ).astype(BF16)
        return before

    lax.fori_loop(0, total_rows // CHUNK, conv, jnp.zeros((8, width), F32))
    source = window.at[:, place.shared_part(place.mine_in_block)]
    away = pl.multiple_of(place.odd * (place.count - 1) * block + place.mine_in_block, place.half)
    rim = pltpu.make_async_remote_copy(
        src_ref=source,
        dst_ref=window.at[:, pl.ds(away, place.half)],
        send_sem=send.at[0],
        recv_sem=recv.at[0],
        device_id=place.pair,
        device_id_type=MESH,
    )
    rim.start()
    fetch.begin()

    def full(span):
        for index in range(place.count - 1):
            number, at = place.full(index)
            cells = window[span, place.span(number)]
            for s in range(2):
                gates[span, pl.ds(s * width + at, block)] = jnp.dot(
                    cells, weights[s, number], preferred_element_type=F32
                )

    parts(total_rows, full)
    rim.wait()

    def shared(span):
        cells = window[span, place.span(place.shared)]
        for s in range(2):
            gates[span, pl.ds(s * width + place.mine, place.half)] = jnp.dot(
                cells,
                weights[s, place.shared, :, pl.ds(place.mine_in_block, place.half)],
                preferred_element_type=F32,
            )

    parts(total_rows, shared)
    forward_scan(
        lambda span: window[span, pl.ds(place.own, width)],
        gates,
        branch_y,
        soft,
        since,
        mixed,
        states,
        [fetch.advance],
    )
    fetch.finish()


def recurrence_back_kernel(
    taps,
    nbits,
    with_ffn,
    d_mixed,
    window,
    gates,
    branches,
    states,
    tap_rows,
    soft,
    slope_soft,
    since,
    weights,
    *refs,
):
    refs = list(refs)

    def take(count):
        taken = refs[:count]
        del refs[:count]
        return taken

    ffn, middle = take(2) if with_ffn else (None, None)
    d_branches, gate_grad, own_small = take(3)
    mixed = take(1)[0] if with_ffn else None
    d_conv, d_gates, given, taken, sums, send, recv = take(7)
    total_rows, width = states.shape
    block = weights.shape[2]
    place = HalfBlocks(width, block)
    half = place.half
    branch_y, branch_x = branches.at[:, :width], branches.at[:, width:]
    d_branch_y, d_branch_x = d_branches.at[:, :width], d_branches.at[:, width:]
    greet(tensor_bits(nbits))
    if with_ffn:
        scatter = Scatter(ffn, *take(2), middle.shape[0], nbits, *take(2))
        scatter.begin()
    backward_scan(
        d_mixed,
        lambda span: window[span, pl.ds(place.own, width)],
        gates,
        branch_y,
        states,
        soft,
        slope_soft,
        since,
        d_conv,
        d_gates,
        d_branch_y,
        sums.at[taps],
    )

    def to_pair(span):
        total = jnp.zeros((PART, half), F32)
        for s in range(2):
            total = total + times_transposed(
                d_gates[span, pl.ds(s * width + place.mine, half)],
                weights[
                    s,
                    place.shared,
                    pl.ds(place.other_in_block, half),
                    pl.ds(place.mine_in_block, half),
                ],
            )
        given[span, :] = total.astype(BF16)

    parts(total_rows, to_pair)
    rim = pltpu.make_async_remote_copy(
        src_ref=given,
        dst_ref=taken,
        send_sem=send.at[0],
        recv_sem=recv.at[0],
        device_id=place.pair,
        device_id_type=MESH,
    )
    rim.start()

    def full(span):
        for index in range(place.count - 1):
            number, at = place.full(index)
            total = d_conv[span, pl.ds(at, block)]
            for s in range(2):
                total = total + times_transposed(
                    d_gates[span, pl.ds(s * width + at, block)], weights[s, number]
                )
            d_conv[span, pl.ds(at, block)] = total
        total = d_conv[span, pl.ds(place.mine, half)]
        for s in range(2):
            total = total + times_transposed(
                d_gates[span, pl.ds(s * width + place.mine, half)],
                weights[
                    s,
                    place.shared,
                    pl.ds(place.mine_in_block, half),
                    pl.ds(place.mine_in_block, half),
                ],
            )
        d_conv[span, pl.ds(place.mine, half)] = total

    parts(total_rows, full)
    if with_ffn:
        scatter.advance(0)
    units = width // half
    for index in range(units):
        number = (index + place.odd) // 2
        cells = window[:, place.span(number)]
        both = jnp.concatenate(
            [d_gates[:, s * width + index * half : s * width + (index + 1) * half] for s in range(2)],
            axis=1,
        )
        found = lax.dot_general(
            cells, both, (((0,), (0,)), ((), ())), preferred_element_type=F32
        ).astype(BF16)
        gate_grad[2 * index] = found[:, :half]
        gate_grad[2 * index + 1] = found[:, half:]
    rim.wait()

    def add(span):
        d_conv[span, pl.ds(place.mine, half)] += taken[span, :].astype(F32)

    parts(total_rows, add)
    for tap in range(taps):
        sums[tap] = jnp.zeros((8, width), F32)

    def conv(i, after):
        row = pl.multiple_of(total_rows - CHUNK - i * CHUNK, CHUNK)
        kept = []
        for at in range(CHUNK - 8, -1, -8):
            tile = pl.ds(row + at, 8)
            values = d_conv[tile, :]
            line = lax.broadcasted_iota(jnp.int32, values.shape, 0)
            below = branch_x[tile, :]
            higher = pl.multiple_of((row + at - 8 + total_rows) % total_rows, 8)
            above = branch_x[pl.ds(higher, 8), :]
            total = values * tap_rows[0:1, :]
            sums[0] += values * below
            masked = []
            for tap in range(1, taps):
                here = jnp.where(since[tile, :] > tap - 0.5, values, 0.0)
                masked.append(here)
                moved = jnp.where(
                    line < 8 - tap,
                    pltpu.roll(here, 8 - tap, 0),
                    pltpu.roll(after[tap - 1], 8 - tap, 0),
                )
                total = total + moved * tap_rows[tap : tap + 1, :]
                source = jnp.where(
                    line < tap, pltpu.roll(above, tap, 0), pltpu.roll(below, tap, 0)
                )
                sums[tap] += here * source
            after = tuple(masked)
            kept.append(total)
        d_branch_x[pl.ds(row, CHUNK), :] = jnp.concatenate(kept[::-1], axis=0).astype(BF16)
        return after

    none = jnp.zeros((8, width), F32)
    lax.fori_loop(0, total_rows // CHUNK, conv, (none,) * (taps - 1))
    line = lax.broadcasted_iota(jnp.int32, (8, width), 0)
    total = jnp.zeros((8, width), F32)
    for tap in range(taps + 1):
        row = jnp.sum(sums[tap], axis=0, keepdims=True)
        total = jnp.where(line == tap, row, total)
    own_small[...] = total
    if with_ffn:
        for step in range(1, nbits):
            scatter.advance(step)

        def result(row):
            span = pl.ds(row, CHUNK)
            mixed[span, :] = (middle[span, :] + scatter.total(row, CHUNK)).astype(BF16)

        chunks(middle.shape[0], result)
        scatter.drain()


def finish_kernel(
    taps,
    gates,
    small,
    in_y,
    in_x,
    in_grad,
    in_mixed,
    whole,
    out_y,
    out_x,
    out_grad,
    out_mixed,
    conv,
    decay,
    gain_in,
    gain_mid,
):
    blocks = whole.shape[1]
    pieces = gates.shape[0] // blocks

    def block(n, carry):
        for piece in range(pieces):
            for s in range(2):
                whole[s, n, :, piece * 128 : (piece + 1) * 128] = gates[
                    n * pieces + piece, s
                ].astype(F32)
        return carry

    lax.fori_loop(0, blocks, block, 0)
    out_y[...] = in_y[...]
    out_x[...] = in_x[...]

    def copy(row):
        span = pl.ds(row, CHUNK)
        out_grad[span, :] = in_grad[span, :]
        out_mixed[span, :] = in_mixed[span, :]

    chunks(in_grad.shape[0], copy)
    share = small.shape[2]
    for index in range(small.shape[0]):
        span = slice(index * share, (index + 1) * share)
        conv[:, span] = small[index, :taps, :]
        for at in range(0, share, 128):
            row = (index * share + at) // 128
            decay[row : row + 1, :] = small[index, taps : taps + 1, at : at + 128]
            gain_in[row : row + 1, :] = small[index, 6:7, at : at + 128]
            gain_mid[row : row + 1, :] = small[index, 7:8, at : at + 128]


def finish(gate_all, small_all, sum_y, sum_x, grad_input, mixed, taps, gate_shape):
    _, blocks, block, _ = gate_shape
    unit = gate_all.shape[-1]
    pieces = block // unit
    width = small_all.shape[0] * small_all.shape[2]
    if unit != 128:
        whole = gate_all.reshape(blocks, pieces, 2, block, unit).transpose(2, 0, 3, 1, 4)
        summed = small_all.transpose(1, 0, 2).reshape(8, width)
        whole = whole.reshape(gate_shape).astype(F32)
        rows = (summed[:taps], summed[taps], summed[6], summed[7])
        return (whole, sum_y, sum_x, grad_input, mixed) + rows
    shape = jax.ShapeDtypeStruct
    row = shape((width // 128, 128), F32)
    found = scan_call(
        partial(finish_kernel, taps),
        (
            shape(gate_shape, F32),
            shape(sum_y.shape, F32),
            shape(sum_x.shape, F32),
            shape(grad_input.shape, F32),
            shape(mixed.shape, BF16),
            shape((taps, width), F32),
            row,
            row,
            row,
        ),
        gate_all.reshape(blocks * pieces, 2, block, unit),
        small_all,
        sum_y,
        sum_x,
        grad_input,
        mixed,
    )
    return found[:6] + tuple(one.reshape(width) for one in found[6:])


def scan_call(kernel, outs, *operands):
    return pl.pallas_call(
        kernel,
        out_shape=outs,
        in_specs=in_vmem(len(operands)),
        out_specs=tuple(in_vmem(len(outs))),
        compiler_params=pltpu.CompilerParams(vmem_limit_bytes=VMEM_BYTES),
    )(*operands)


class Rim:
    def __init__(self, route, back, source, first, width, room):
        self.route, self.back = route, back
        self.source, self.first, self.width = source, first, width
        self.room = room

    def fetch(self, values):
        part = lax.dynamic_slice_in_dim(values, self.source, self.width, 1)
        return lax.ppermute(part, "tensor", self.route)

    def give(self, part):
        return lax.ppermute(part, "tensor", self.back)

    def add(self, values, part):
        zeros = jnp.zeros(values.shape, F32)
        return values + lax.dynamic_update_slice_in_dim(
            zeros, part.astype(F32), self.source, 1
        )

    def window(self, channels):
        return (channels // self.width + 4) * self.width


def gate_rims(channels, block_size, ntensor, offset):
    up = [(i, i + 1) for i in range(ntensor - 1)]
    down = [(i + 1, i) for i in range(ntensor - 1)]
    last = jnp.int32(channels - block_size)
    return [
        Rim(up, down, last, offset - block_size, block_size, block_size),
        Rim(down, up, jnp.int32(0), offset + channels, block_size, block_size),
    ]


def same_block(first, count, offset, channels, block_size):
    rows = (first + jnp.arange(count, dtype=jnp.int32))[:, None]
    columns = (offset + jnp.arange(channels, dtype=jnp.int32))[None, :]
    return (rows + block_size) // block_size == (columns + block_size) // block_size


def gate_dense(gate_w, offset, first, count):
    block_size = gate_w.shape[2]
    total = gate_w.shape[1] * block_size
    channels = total // lax.axis_size("tensor")
    columns = gate_w.transpose(2, 0, 1, 3).reshape(block_size, 2, total)
    columns = lax.dynamic_slice_in_dim(columns, offset, channels, 2)
    copies = -(-count // block_size) + 1
    tall = jnp.concatenate([columns] * copies, axis=0)
    tall = lax.dynamic_slice_in_dim(tall, (first + block_size) % block_size, count, 0)
    same = same_block(first, count, offset, channels, block_size)
    dense = jnp.where(same[:, None, :], tall, jnp.zeros_like(tall))
    return dense.reshape(count, 2 * channels)


def doc_starts(seg_ids, seq_len):
    places = jnp.arange(seg_ids.shape[0], dtype=jnp.int32)
    before = jnp.concatenate([seg_ids[:1], seg_ids[:-1]])
    resets = (places % seq_len == 0) | (seg_ids != before)
    starts = lax.cummax(jnp.where(resets, places, jnp.zeros_like(places)), axis=0)
    return starts


def causal_conv(starts, values, kernel):
    places = jnp.arange(values.shape[0], dtype=jnp.int32)
    total = values * kernel[0]
    for offset_k in range(1, kernel.shape[0]):
        moved = jnp.concatenate(
            [jnp.zeros((offset_k, values.shape[1]), values.dtype), values[:-offset_k]], axis=0
        )
        valid = (places - offset_k >= starts)[:, None]
        total = total + jnp.where(valid, moved, jnp.zeros_like(moved)) * kernel[offset_k]
    return total


def geglu(gate_val, up_val):
    return jax.nn.gelu(gate_val, approximate=True) * up_val


def rows_times(left, right):
    return lax.dot_general(left, right, (((1,), (1,)), ((), ())), preferred_element_type=F32)


def rows_back(lefts, rights):
    total = rows_times(lefts[0], rights[0])
    return total + rows_times(lefts[1], rights[1])


def inner_rows(left, right):
    return lax.dot_general(left, right, (((0,), (0,)), ((), ())), preferred_element_type=F32)


def halved(grad, ndp):
    return grad.reshape(ndp // 2, 2, grad.shape[0] // ndp, grad.shape[1])


def body(
    tokens,
    segments,
    cotangent,
    norm_gain,
    w_y,
    w_x,
    conv_w,
    gate_w,
    decay_param,
    w_out,
    mlp_gain,
    w_gate,
    w_up,
    w_down,
):
    ntensor = lax.axis_size("tensor")
    ndp = lax.axis_size("dp")
    nbits = log2_of(ntensor)
    tindex = lax.axis_index("tensor")
    own_rows, width = tokens.shape
    group_rows = own_rows * ntensor
    block_size = gate_w.shape[2]
    nblocks = gate_w.shape[1]
    dp_rows, channels = w_y.shape
    taps = conv_w.shape[0]
    offset = tindex * channels
    shape = jax.ShapeDtypeStruct
    gain_in = norm_gain.reshape(1, width)
    gain_mid = mlp_gain.reshape(1, width)
    seg_rows_of = own_rows // 128
    tiled = channels % 128 == 0
    w_yx = (w_y, w_x) if tiled else (jnp.concatenate([w_y, w_x], axis=1),)
    normed_rows, seg_all, wyx_loc, wout_loc = call_kernel(
        partial(enter_kernel, nbits, len(w_yx)),
        (
            shape((group_rows, width), BF16),
            shape((ntensor, seg_rows_of, 128), jnp.int32),
            shape((dp_rows * ndp, 2 * channels), BF16),
            shape((dp_rows * ndp, channels), BF16),
        ),
        gather_sems(nbits)
        + [pltpu.SemaphoreType.DMA((ntensor - 1,)), pltpu.SemaphoreType.DMA((ntensor - 1,))]
        + [pltpu.SemaphoreType.DMA((1,))]
        + line_sems(ndp) * (len(w_yx) + 1),
        0,
        tokens,
        segments.reshape(seg_rows_of, 128),
        gain_in,
        *w_yx,
        w_out,
        far_in=tuple(range(3, 4 + len(w_yx))),
        far_out=(2, 3),
    )
    units = w_gate.shape[1]
    w_both = jnp.concatenate([w_gate, w_up], axis=1)
    w_both, w_down, normed_rows = lax.optimization_barrier((w_both, w_down, normed_rows))
    both_loc = lax.all_gather(w_both, "dp", axis=0, tiled=True)
    wd_loc = lax.all_gather(w_down, "dp", axis=0, tiled=True)
    seg_rows = seg_all.reshape(group_rows)
    starts = doc_starts(seg_rows, group_rows)
    conv_loc = lax.dynamic_slice_in_dim(conv_w, offset, channels, 1)
    decay_loc = lax.dynamic_slice_in_dim(decay_param, offset, channels, 0).reshape(1, channels)
    soft = jax.nn.softplus(decay_loc)
    slope_soft = jax.nn.sigmoid(decay_loc)
    half_blocks = (
        channels % block_size == block_size // 2 and ntensor % 2 == 0 and block_size % 256 == 0
    )
    since = (jnp.arange(group_rows, dtype=jnp.int32) - starts).astype(F32)[:, None]
    branches = jnp.dot(normed_rows, wyx_loc, preferred_element_type=F32)
    if half_blocks:
        span_blocks = channels // block_size + 1
        w_window = lax.dynamic_slice_in_dim(gate_w, offset // block_size, span_blocks, 1)
        taps_pad = jnp.concatenate([conv_loc, jnp.zeros((8 - taps, channels), F32)], axis=0)
        mixed_low, states, window, gate_pre, cot_rows = call_kernel(
            partial(recurrence_kernel, taps, nbits),
            (
                shape((group_rows, channels), BF16),
                shape((group_rows, channels), F32),
                shape((group_rows, span_blocks * block_size), BF16),
                shape((group_rows, 2 * channels), F32),
                shape((group_rows, width), BF16),
            ),
            [pltpu.SemaphoreType.DMA((1,)), pltpu.SemaphoreType.DMA((1,))]
            + fetch_scratch(nbits),
            5,
            branches,
            taps_pad,
            soft,
            since,
            w_window,
            cotangent,
        )
    else:
        branch_y, branch_x = branches[:, :channels], branches[:, channels:]
        (cot_rows,) = call_kernel(
            partial(fetch_kernel, nbits),
            (shape((group_rows, width), BF16),),
            fetch_scratch(nbits),
            5,
            cotangent,
        )
        rims = gate_rims(channels, block_size, ntensor, offset)
        own_dense = gate_dense(gate_w, offset, offset, channels)
        rim_dense = [gate_dense(gate_w, offset, rim.first, rim.width) for rim in rims]
        conv_out, conv_pull = jax.vjp(partial(causal_conv, starts), branch_x, conv_loc)
        conv_low = conv_out.astype(BF16)
        rim_cells = [rim.fetch(conv_low) for rim in rims]
        gate_pre = jnp.dot(conv_low, own_dense, preferred_element_type=F32)
        for cells, dense in zip(rim_cells, rim_dense):
            gate_pre = gate_pre + jnp.dot(cells, dense, preferred_element_type=F32)
        mixed_low, states = scan_call(
            forward_scan_kernel,
            (shape((group_rows, channels), BF16), shape((group_rows, channels), F32)),
            conv_low,
            gate_pre,
            branch_y,
            soft,
            since,
        )
    middle, mid_rows = call_kernel(
        partial(middle_kernel, nbits),
        (shape((own_rows, width), F32), shape((group_rows, width), BF16)),
        scatter_scratch(own_rows, width, nbits) + gather_sems(nbits),
        1,
        rows_times(mixed_low, wout_loc).astype(BF16),
        tokens,
        gain_mid,
    )
    pre = jnp.dot(mid_rows, both_loc, preferred_element_type=F32)
    hidden, act_pull = jax.vjp(geglu, pre[:, :units], pre[:, units:])
    hidden_low = hidden.astype(BF16)
    grad_wd = inner_rows(cot_rows, hidden_low).astype(BF16)
    sum_wd = lax.psum_scatter(grad_wd, "dp", scatter_dimension=0, tiled=True)
    grad_wd, wd_loc = lax.optimization_barrier((grad_wd, wd_loc))
    d_hidden = jnp.dot(cot_rows, wd_loc, preferred_element_type=F32)
    d_gate, d_up = act_pull(d_hidden)
    d_pre = jnp.concatenate([d_gate.astype(BF16), d_up.astype(BF16)], axis=1)
    grad_both = inner_rows(mid_rows, d_pre).astype(BF16)
    sum_both = lax.psum_scatter(grad_both, "dp", scatter_dimension=0, tiled=True)
    d_pre, grad_both = lax.optimization_barrier((d_pre, grad_both))
    d_mid_part = rows_times(d_pre, both_loc).astype(BF16)
    d_middle, d_mixer, d_gain_mid, ffn_part = call_kernel(
        partial(turn_kernel, nbits),
        (
            shape((own_rows, width), F32),
            shape((group_rows, width), BF16),
            shape((8, width), F32),
            shape((group_rows, width), BF16),
        ),
        scatter_scratch(own_rows, width, nbits) + gather_sems(nbits) + product_scratch(units),
        2,
        d_mid_part,
        cotangent,
        middle,
        gain_mid,
        hidden_low,
        wd_loc,
        far_in=(5,),
    )
    d_mixer, sum_wd = lax.optimization_barrier((d_mixer, sum_wd))
    d_mixed_in = jnp.dot(d_mixer, wout_loc, preferred_element_type=F32)
    unit = math.gcd(channels, block_size)
    merged = half_blocks and nbits <= 2
    if half_blocks:
        found = call_kernel(
            partial(recurrence_back_kernel, taps, nbits, merged),
            (
                shape((group_rows, 2 * channels), BF16),
                shape((channels // unit * 2, block_size, unit), BF16),
                shape((8, channels), F32),
            )
            + ((shape((own_rows, width), BF16),) if merged else ()),
            [
                pltpu.VMEM((group_rows, channels), F32),
                pltpu.VMEM((group_rows, 2 * channels), BF16),
                pltpu.VMEM((group_rows, unit), BF16),
                pltpu.VMEM((group_rows, unit), BF16),
                pltpu.VMEM((taps + 1, 8, channels), F32),
                pltpu.SemaphoreType.DMA((1,)),
                pltpu.SemaphoreType.DMA((1,)),
            ]
            + (scatter_scratch(own_rows, width, nbits) if merged else []),
            6,
            d_mixed_in,
            window,
            gate_pre,
            branches,
            states,
            taps_pad,
            soft,
            slope_soft,
            since,
            w_window,
            *((ffn_part, middle) if merged else ()),
        )
        d_branches, gate_grad, own_small = found[:3]
        gate_grad = gate_grad.reshape(channels // unit * 2 * block_size, unit)
    else:
        d_conv, d_gate_low, d_branch_y, d_decay = scan_call(
            backward_scan_kernel,
            (
                shape((group_rows, channels), F32),
                shape((group_rows, 2 * channels), BF16),
                shape((group_rows, channels), BF16),
                shape((8, channels), F32),
            ),
            d_mixed_in,
            conv_low,
            gate_pre,
            branch_y,
            states,
            soft,
            slope_soft,
            since,
        )
        given = [rows_times(d_gate_low, dense).astype(BF16) for dense in rim_dense]
        taken = [rim.give(part) for rim, part in zip(rims, given)]
        d_conv_out = d_conv + rows_times(d_gate_low, own_dense)
        for rim, part in zip(rims, taken):
            d_conv_out = rim.add(d_conv_out, part)
        d_branch_x, grad_conv_loc = conv_pull(d_conv_out)
        d_branches = jnp.concatenate([d_branch_y, d_branch_x.astype(BF16)], axis=1)
        base = offset // block_size * block_size - rims[0].room
        window_rows = rims[0].window(channels)
        picked = jnp.zeros((window_rows, 2 * channels), F32)
        for first, cells in [(offset, conv_low)] + [(r.first, c) for r, c in zip(rims, rim_cells)]:
            part = inner_rows(cells, d_gate_low)
            same = same_block(first, cells.shape[1], offset, channels, block_size)
            part = jnp.where(jnp.concatenate([same, same], axis=1), part, 0.0)
            picked = lax.dynamic_update_slice(picked, part, (first - base, jnp.int32(0)))
        picked = picked.reshape(window_rows // block_size, block_size, 2, channels // unit, unit)
        gate_grad = picked.sum(axis=0).astype(BF16).transpose(2, 1, 0, 3)
        gate_grad = gate_grad.reshape(channels // unit * 2 * block_size, unit)
        own_small = jnp.concatenate(
            [
                grad_conv_loc,
                jnp.sum(d_decay, axis=0, keepdims=True),
                jnp.zeros((7 - taps, channels), F32),
            ],
            axis=0,
        )

    grad_wout = inner_rows(d_mixer, mixed_low).astype(BF16)
    grad_wyx = inner_rows(normed_rows, d_branches).astype(BF16)
    d_normed = rows_times(d_branches, wyx_loc).astype(BF16)
    d_normed, grad_wyx, grad_wout, sum_both = lax.optimization_barrier(
        (d_normed, grad_wyx, grad_wout, sum_both)
    )
    sum_wout = lax.psum_scatter(grad_wout, "dp", scatter_dimension=0, tiled=True)

    pieces = [halved(grad, ndp) for grad in (gate_grad, grad_wyx)]
    peers = ntensor - 1
    gate_rows = gate_grad.shape[0] // ndp
    dma = pltpu.SemaphoreType.DMA
    scratch = scatter_scratch(own_rows, width, nbits)
    scratch += line_scratch(ndp, gate_rows, unit)
    if tiled:
        scratch += line_scratch(ndp, dp_rows, channels) * 2
    else:
        scratch += line_scratch(ndp, dp_rows, 2 * channels)
    scratch += [
        pltpu.VMEM((8, width), F32),
        pltpu.VMEM((ntensor, 8, channels), F32),
        pltpu.VMEM((peers, 8, channels), F32),
        pltpu.VMEM((8, channels), F32),
        pltpu.VMEM((ndp - 1, 8, channels), F32),
    ]
    scratch += [dma((peers,)), dma((peers,)), dma((ndp - 1,)), dma((ndp - 1,))]
    scratch += [dma((peers,)), dma((peers,)), dma((peers + ndp,)), dma((peers + ndp,))]
    grad_input, sum_wy, sum_wx, gate_all, small_all = call_kernel(
        partial(leave_kernel, nbits, tiled),
        (shape((own_rows, width), F32),)
        + (shape((dp_rows, channels), F32),) * 2
        + (
            shape((ntensor, ndp // 2, 2, gate_rows, unit), BF16),
            shape((ntensor, 8, channels), F32),
        ),
        scratch,
        3,
        d_normed,
        tokens,
        d_middle,
        gain_in,
        own_small,
        d_gain_mid,
        *pieces,
        far_in=(6, 7),
    )
    if merged:
        mixed = found[3]
    else:
        (mixed,) = call_kernel(
            partial(result_kernel, nbits),
            (shape((own_rows, width), BF16),),
            scatter_scratch(own_rows, width, nbits),
            4,
            ffn_part,
            middle,
        )
    sum_gate, sum_wy, sum_wx, grad_input, mixed, sum_conv, sum_decay, sum_gain_in, sum_gain_mid = finish(
        gate_all, small_all, sum_wy, sum_wx, grad_input, mixed, taps, gate_w.shape
    )
    return (
        mixed,
        grad_input,
        sum_gain_in,
        sum_wy,
        sum_wx,
        sum_conv,
        sum_gate,
        sum_decay,
        sum_wout.astype(F32),
        sum_gain_mid,
        sum_both[:, :units].astype(F32),
        sum_both[:, units:].astype(F32),
        sum_wd.astype(F32),
    )


def solution(mesh):
    split = P(("dp", "tensor"), None)
    weight = P("dp", "tensor")
    return jax.shard_map(
        body,
        mesh=mesh,
        in_specs=(
            split,
            P(("dp", "tensor")),
            split,
            P(),
            weight,
            weight,
            P(),
            P(),
            P(),
            weight,
            P(),
            weight,
            weight,
            weight,
        ),
        out_specs=(
            split,
            split,
            P(),
            weight,
            weight,
            P(),
            P(),
            P(),
            weight,
            P(),
            weight,
            weight,
            weight,
        ),
        check_vma=False,
    )
```

```python
import math
from functools import partial

import jax
import jax.numpy as jnp
from jax import lax
from jax.experimental import pallas as pl
from jax.experimental.pallas import tpu as pltpu
from jax.sharding import PartitionSpec as P

EPSILON = 1e-06
MESH = pl.DeviceIdType.MESH
VMEM_BYTES = 56 * 1024 * 1024
CHUNK = 16
F32 = jnp.float32
BF16 = jnp.bfloat16


def subsets(bits):
    found = [()]
    for bit in bits:
        found = found + [chosen + (bit,) for chosen in found]
    return found


def flipped(index, bits):
    for bit in bits:
        mine = (index // (1 << bit)) % 2
        index = index + (1 - 2 * mine) * (1 << bit)
    return index


def log2_of(count):
    assert count & (count - 1) == 0
    return count.bit_length() - 1


def greet(axis_bits):
    barrier = pltpu.get_barrier_semaphore()
    for axis, bit in axis_bits:
        peer = flipped(lax.axis_index(axis), (bit,))
        pl.semaphore_signal(barrier, inc=1, device_id={axis: peer}, device_id_type=MESH)
    pl.semaphore_wait(barrier, len(axis_bits))


def halves_of(nbits, columns):
    half = columns // 2
    ups = tuple(range(nbits))
    return ((ups, 0, half), (ups[::-1], half, half))


class Gather:
    def __init__(self, ref, rows, nbits, send_sems, recv_sems):
        self.ref, self.rows, self.nbits = ref, rows, nbits
        self.sems = (send_sems, recv_sems)
        self.me = lax.axis_index("tensor")
        self.plan = []
        number = 0
        for half, (order, at, width) in enumerate(halves_of(nbits, ref.shape[1])):
            for step, bit in enumerate(order):
                for known in subsets(order[:step]):
                    self.plan.append((half, step, known, bit, at, width, number))
                    number += 1
        self.count = number

    def copy(self, item):
        half, step, known, bit, at, width, number = item
        row = pl.multiple_of(flipped(self.me, known) * self.rows, self.rows)
        piece = self.ref.at[pl.ds(row, self.rows), pl.ds(at, width)]
        return pltpu.make_async_remote_copy(
            src_ref=piece,
            dst_ref=piece,
            send_sem=self.sems[0].at[number],
            recv_sem=self.sems[1].at[number],
            device_id={"tensor": flipped(self.me, (bit,))},
            device_id_type=MESH,
        )

    def begin(self):
        for item in sorted(self.plan, key=lambda it: it[1]):
            if item[2] == ():
                self.copy(item).start()

    def advance(self, step):
        for item in self.plan:
            half, at_step, known, bit, at, width, number = item
            if at_step == step:
                self.copy(item).wait_recv()
                block = known + (bit,)
                for later in self.plan:
                    if later[0] == half and set(later[2]) == set(block):
                        self.copy(later).start()

    def finish(self, step=0):
        for at_step in range(step, self.nbits):
            self.advance(at_step)
        for item in self.plan:
            self.copy(item).wait_send()


def gather_copies(nbits):
    return 2 * ((1 << nbits) - 1)


class Scatter:
    def __init__(self, ref, landed, staged, rows, nbits, send_sems, recv_sems):
        self.ref, self.landed, self.staged = ref, landed, staged
        self.rows, self.nbits = rows, nbits
        self.sems = (send_sems, recv_sems)
        self.me = lax.axis_index("tensor")
        self.plan, self.slot = [], {}
        number = 0
        for half, (order, at, width) in enumerate(halves_of(nbits, ref.shape[1])):
            for step, bit in enumerate(order):
                for rest in subsets(order[step + 1 :])[::-1]:
                    self.plan.append((half, step, rest, bit, at, width, number))
                    if step > 0:
                        self.slot[number] = len(self.slot)
                    number += 1

    def copy(self, item):
        half, step, rest, bit, at, width, number = item
        if step == 0:
            row = pl.multiple_of(flipped(self.me, rest + (bit,)) * self.rows, self.rows)
            source = self.ref.at[pl.ds(row, self.rows), pl.ds(at, width)]
        else:
            source = self.staged.at[self.slot[number]]
        return pltpu.make_async_remote_copy(
            src_ref=source,
            dst_ref=self.landed.at[number],
            send_sem=self.sems[0].at[number],
            recv_sem=self.sems[1].at[number],
            device_id={"tensor": flipped(self.me, (bit,))},
            device_id_type=MESH,
        )

    def begin(self):
        for item in sorted(self.plan, key=lambda it: (len(it[2]) == 0)):
            if item[1] == 0:
                self.copy(item).start()

    def partial_sum(self, half, block, before, row, size):
        at, width = halves_of(self.nbits, self.ref.shape[1])[half][1:]
        base = pl.multiple_of(flipped(self.me, block) * self.rows + row, size)
        total = self.ref[pl.ds(base, size), pl.ds(at, width)].astype(F32)
        for it in self.plan:
            if it[0] == half and it[1] < before and set(it[2]) == set(block):
                total = total + self.landed[it[6], pl.ds(row, size), :].astype(F32)
        return total

    def advance(self, step):
        for half in range(2):
            for item in self.plan:
                if item[0] == half and item[1] == step:
                    self.copy(item).wait_recv()
            for item in self.plan:
                if item[0] == half and item[1] == step + 1:

                    def fill(row, item=item):
                        value = self.partial_sum(
                            item[0], item[2] + (item[3],), item[1], row, CHUNK
                        )
                        where = (self.slot[item[6]], pl.ds(row, CHUNK))
                        self.staged[where + (slice(None),)] = value.astype(BF16)

                    chunks(self.rows, fill)
                    self.copy(item).start()

    def run(self):
        for step in range(self.nbits):
            self.advance(step)

    def total(self, row, size):
        return jnp.concatenate(
            [self.partial_sum(half, (), self.nbits, row, size) for half in range(2)], axis=1
        )

    def drain(self):
        for item in self.plan:
            self.copy(item).wait_send()


def scatter_scratch(rows, columns, nbits):
    copies = gather_copies(nbits)
    later = max(1, copies - (1 << nbits))
    return [
        pltpu.VMEM((copies, rows, columns // 2), BF16),
        pltpu.VMEM((later, rows, columns // 2), BF16),
        pltpu.SemaphoreType.DMA((copies,)),
        pltpu.SemaphoreType.DMA((copies,)),
    ]


def gather_sems(nbits):
    copies = gather_copies(nbits)
    return [pltpu.SemaphoreType.DMA((copies,)), pltpu.SemaphoreType.DMA((copies,))]


def tensor_bits(nbits):
    return [("tensor", bit) for bit in range(nbits)]


def rms_scale_of(values):
    return lax.rsqrt(jnp.mean(values * values, axis=-1, keepdims=True) + EPSILON)


def chunks(rows, body):
    def step(i, carry):
        body(pl.multiple_of(i * CHUNK, CHUNK))
        return carry

    lax.fori_loop(0, rows // CHUNK, step, 0)


def own_row(row, rows):
    return pl.multiple_of(lax.axis_index("tensor") * rows + row, CHUNK)


def dp_place():
    me = lax.axis_index("dp")
    return me // 2, me % 2, lax.axis_size("dp") // 2


def dp_index(chip, core):
    return chip * 2 + core


UP, DOWN = 1, -1


class LineGather:
    def __init__(self, own, whole, send_sems, recv_sems, columns=None):
        self.own, self.whole = own, whole
        self.sems = (send_sems, recv_sems)
        self.chip, self.core, self.chips = dp_place()
        self.rows = own.shape[0]
        self.columns = slice(None) if columns is None else columns

    def block(self, chip):
        row = pl.multiple_of(dp_index(chip, self.core) * self.rows, self.rows)
        return self.whole.at[pl.ds(row, self.rows), self.columns]

    def has(self, way, distance):
        return self.chip >= distance if way == UP else self.chip + distance < self.chips

    def number(self, way, distance):
        return (0 if way == UP else self.chips) + distance

    def along(self, way, distance):
        block = self.block(self.chip - way * distance)
        return pltpu.make_async_remote_copy(
            src_ref=self.own if distance == 0 else block,
            dst_ref=block,
            send_sem=self.sems[0].at[self.number(way, distance)],
            recv_sem=self.sems[1].at[self.number(way, distance + 1)],
            device_id={"dp": dp_index(self.chip + way, self.core)},
            device_id_type=MESH,
        )

    def arrival(self, way, distance):
        block = self.block(self.chip - way * distance)
        return pltpu.make_async_remote_copy(
            src_ref=block,
            dst_ref=block,
            send_sem=self.sems[0].at[self.number(way, distance)],
            recv_sem=self.sems[1].at[self.number(way, distance)],
            device_id={"dp": dp_index(self.chip + way, self.core)},
            device_id_type=MESH,
        )

    def across(self, way, distance):
        block = self.block(self.chip - way * distance)
        number = 2 * self.chips + self.number(way, distance)
        return pltpu.make_async_remote_copy(
            src_ref=self.own if distance == 0 else block,
            dst_ref=block,
            send_sem=self.sems[0].at[number],
            recv_sem=self.sems[1].at[number],
            device_id={"dp": dp_index(self.chip, 1 - self.core)},
            device_id_type=MESH,
        )

    def local(self):
        return pltpu.make_async_copy(
            self.own, self.block(self.chip), self.sems[0].at[4 * self.chips]
        )

    def begin(self):
        for way in (UP, DOWN):

            @pl.when(self.has(-way, 1))
            def _(way=way):
                self.along(way, 0).start()

        self.across(UP, 0).start()
        self.local().start()

    def pass_on(self, distance):
        for way in (UP, DOWN):

            @pl.when(self.has(way, distance))
            def _(way=way):
                self.arrival(way, distance).wait_recv()

                @pl.when(self.has(-way, 1))
                def _():
                    self.along(way, distance).start()

                self.across(way, distance).start()

    def finish(self):
        self.across(UP, 0).wait()
        self.local().wait()
        for way in (UP, DOWN):
            for distance in range(self.chips):

                @pl.when(self.has(way, distance) & self.has(-way, 1))
                def _(way=way, distance=distance):
                    self.along(way, distance).wait_send()

                if distance:

                    @pl.when(self.has(way, distance))
                    def _(way=way, distance=distance):
                        self.across(way, distance).wait()


def line_sems(ndp):
    chips = ndp // 2
    return [pltpu.SemaphoreType.DMA((4 * chips + 1,)), pltpu.SemaphoreType.DMA((4 * chips + 1,))]


def greet_peers(nbits, all_tensor, whole_dp):
    me = lax.axis_index("tensor")
    chip, core, chips = dp_place()
    barrier = pltpu.get_barrier_semaphore()

    def signal(target):
        pl.semaphore_signal(barrier, inc=1, device_id=target, device_id_type=MESH)

    met = 0
    for chosen in subsets(tuple(range(nbits))):
        if chosen and (all_tensor or len(chosen) == 1):
            signal({"tensor": flipped(me, chosen)})
            met += 1
    if whole_dp:
        for shift in range(chips):
            for turn in range(2):
                if (shift, turn) != (0, 0):
                    other = dp_index((chip + shift) % chips, core + turn * (1 - 2 * core))
                    signal({"dp": other})
                    met += 1
    else:
        signal({"dp": dp_index(chip, 1 - core)})
        met += 1

        for shift in sorted({1 % chips, chips - 1} - {0}):
            signal({"dp": dp_index((chip + shift) % chips, core)})
            met += 1

    pl.semaphore_wait(barrier, met)


def enter_kernel(
    nbits, parts_yx, tokens, seg, gain, *refs
):
    w_yx, w_out = refs[:parts_yx], refs[parts_yx]
    normed_all, seg_all, wyx_all, wout_all, s0, r0, s2, r2, l0, *line = refs[parts_yx + 1 :]
    rows = tokens.shape[0]
    me = lax.axis_index("tensor")
    peers = [chosen for chosen in subsets(tuple(range(nbits))) if chosen]
    greet_peers(nbits, True, False)
    width = wyx_all.shape[1] // parts_yx
    lines = [
        LineGather(
            own,
            wyx_all,
            line[2 * number],
            line[2 * number + 1],
            pl.ds(number * width, width) if parts_yx > 1 else None,
        )
        for number, own in enumerate(w_yx)
    ]
    lines.append(LineGather(w_out, wout_all, *line[2 * parts_yx : 2 * parts_yx + 2]))
    for item in lines:
        item.begin()

    def norm(row):
        values = tokens[pl.ds(row, CHUNK), :].astype(F32)
        scaled = values * rms_scale_of(values) * gain[...]
        normed_all[pl.ds(own_row(row, rows), CHUNK), :] = scaled.astype(BF16)

    chunks(rows, norm)
    gather = Gather(normed_all, rows, nbits, s0, r0)
    gather.begin()
    seg_own = pltpu.make_async_copy(seg, seg_all.at[me], l0.at[0])
    seg_own.start()
    seg_copies = [
        pltpu.make_async_remote_copy(
            src_ref=seg,
            dst_ref=seg_all.at[me],
            send_sem=s2.at[number],
            recv_sem=r2.at[number],
            device_id={"tensor": flipped(me, chosen)},
            device_id_type=MESH,
        )
        for number, chosen in enumerate(peers)
    ]
    for copy in seg_copies:
        copy.start()
    chips = lines[0].chips
    for item in lines:
        item.pass_on(1)
    gather.advance(0)
    for distance in range(2, chips):
        for item in lines:
            item.pass_on(distance)
    gather.finish(1)
    for item in lines:
        item.finish()
    for copy in seg_copies:
        copy.wait()
    seg_own.wait()


class Fetch:
    def __init__(self, nbits, cot, cot_all, s0, r0, l0):
        rows = cot.shape[0]
        own = pl.multiple_of(lax.axis_index("tensor") * rows, rows)
        self.local = pltpu.make_async_copy(cot, cot_all.at[pl.ds(own, rows), :], l0.at[0])
        self.gather = Gather(cot_all, rows, nbits, s0, r0)

    def begin(self):
        self.local.wait()
        self.gather.begin()

    def advance(self):
        self.gather.advance(0)

    def finish(self):
        self.gather.finish(1)


def fetch_scratch(nbits):
    return gather_sems(nbits) + [pltpu.SemaphoreType.DMA((1,))]


def fetch_kernel(nbits, cot, cot_all, *sems):
    greet(tensor_bits(nbits))
    fetch = Fetch(nbits, cot, cot_all, *sems)
    fetch.local.start()
    fetch.begin()
    fetch.advance()
    fetch.finish()


def middle_kernel(
    nbits, mixer, tokens, gain, middle, mid_all, landed, staged, s0, r0, s1, r1
):
    rows = tokens.shape[0]
    greet(tensor_bits(nbits))
    scatter = Scatter(mixer, landed, staged, rows, nbits, s0, r0)
    scatter.begin()
    scatter.run()

    def norm(row):
        values = tokens[pl.ds(row, CHUNK), :].astype(F32) + scatter.total(row, CHUNK)
        middle[pl.ds(row, CHUNK), :] = values
        scaled = values * rms_scale_of(values) * gain[...]
        mid_all[pl.ds(own_row(row, rows), CHUNK), :] = scaled.astype(BF16)

    chunks(rows, norm)
    gather = Gather(mid_all, rows, nbits, s1, r1)
    gather.begin()
    gather.finish()
    scatter.drain()


def result_kernel(nbits, ffn, middle, mixed, landed, staged, s0, r0):
    rows = middle.shape[0]
    greet(tensor_bits(nbits))
    scatter = Scatter(ffn, landed, staged, rows, nbits, s0, r0)
    scatter.begin()
    scatter.run()

    def add(row):
        values = middle[pl.ds(row, CHUNK), :] + scatter.total(row, CHUNK)
        mixed[pl.ds(row, CHUNK), :] = values.astype(BF16)

    chunks(rows, add)
    scatter.drain()


def norm_pull(values, gain, cotangent):
    scale = rms_scale_of(values)
    unit = values * scale
    inner = cotangent * gain
    back = scale * (inner - unit * jnp.mean(inner * unit, axis=-1, keepdims=True))
    return back, cotangent * unit


def eight_rows(values):
    total = values[0:8]
    for at in range(8, CHUNK, 8):
        total = total + values[at : at + 8]
    return total


class Product:
    def __init__(self, left, right, out, held, sems):
        self.left, self.right, self.out = left, right, out
        self.held, self.sems = held, sems
        self.width = held.shape[1]
        self.count = right.shape[0] // self.width
        self.done = 0

    def fetch(self, block):
        return pltpu.make_async_copy(
            self.right.at[pl.ds(block * self.width, self.width), :],
            self.held.at[block % 2],
            self.sems.at[block % 2],
        )

    def begin(self):
        self.fetch(0).start()

    def work(self, blocks):
        for block in range(self.done, min(self.done + blocks, self.count)):
            if block + 1 < self.count:
                self.fetch(block + 1).start()
            self.fetch(block).wait()

            def rows(span, block=block):
                found = times_transposed(self.left[span, :], self.held[block % 2])
                at = slice(block * self.width, (block + 1) * self.width)
                self.out[span, at] = found.astype(BF16)

            parts(self.left.shape[0], rows)
        self.done = min(self.done + blocks, self.count)


PRODUCT_BLOCK = 256


def product_scratch(depth):
    return [pltpu.VMEM((2, PRODUCT_BLOCK, depth), BF16), pltpu.SemaphoreType.DMA((2,))]


def turn_kernel(
    nbits,
    d_norm,
    cot,
    middle,
    gain,
    hidden,
    w_down,
    d_middle,
    d_mixer,
    d_gain,
    ffn,
    landed,
    staged,
    s0,
    r0,
    s1,
    r1,
    *product,
):
    rows = middle.shape[0]
    ahead = Product(hidden, w_down, ffn, *product)
    ahead.begin()
    greet(tensor_bits(nbits))
    scatter = Scatter(d_norm, landed, staged, rows, nbits, s0, r0)
    scatter.begin()
    d_gain[...] = jnp.zeros_like(d_gain)
    ahead.work(4)
    for step in range(nbits):
        scatter.advance(step)
        if step + 1 < nbits:
            ahead.work(2)

    def pull(row):
        span = pl.ds(row, CHUNK)
        back, gains = norm_pull(middle[span, :], gain[...], scatter.total(row, CHUNK))
        values = cot[span, :].astype(F32) + back
        d_middle[span, :] = values
        d_mixer[pl.ds(own_row(row, rows), CHUNK), :] = values.astype(BF16)
        d_gain[...] += eight_rows(gains)

    chunks(rows, pull)
    gather = Gather(d_mixer, rows, nbits, s1, r1)
    gather.begin()
    ahead.work(2)
    gather.advance(0)
    ahead.work(ahead.count)
    gather.finish(1)
    scatter.drain()


class LineSum:
    def __init__(self, whole, kept, swapped, staged, landed, send_sems, recv_sems, columns=None):
        self.whole, self.kept, self.swapped = whole, kept, swapped
        self.staged, self.landed = staged, landed
        self.sems = (send_sems, recv_sems)
        self.columns = columns
        self.chip, self.core, self.chips = dp_place()
        self.rows = whole.shape[2]

    def half(self, core):
        if self.columns is None:
            return self.whole.at[:, core]
        return self.whole.at[:, core, :, self.columns]

    def local(self):
        return pltpu.make_async_copy(
            self.half(self.core), self.kept, self.sems[0].at[2 * self.chips]
        )

    def swap(self):
        return pltpu.make_async_remote_copy(
            src_ref=self.half(1 - self.core),
            dst_ref=self.swapped,
            send_sem=self.sems[0].at[0],
            recv_sem=self.sems[1].at[0],
            device_id={"dp": dp_index(self.chip, 1 - self.core)},
            device_id_type=MESH,
        )

    def has(self, way, distance):
        return self.chip + distance < self.chips if way == UP else self.chip >= distance

    def slot(self, way, distance):
        return (0 if way == UP else self.chips - 1) + distance

    def hop(self, way, distance):
        return pltpu.make_async_remote_copy(
            src_ref=self.staged.at[self.slot(way, distance - 1)],
            dst_ref=self.landed.at[self.slot(way, distance - 1)],
            send_sem=self.sems[0].at[1 + self.slot(way, distance - 1)],
            recv_sem=self.sems[1].at[1 + self.slot(way, distance - 1)],
            device_id={"dp": dp_index(self.chip + way, self.core)},
            device_id_type=MESH,
        )

    def arrival(self, way, distance):
        number = self.slot(way, distance)
        return pltpu.make_async_remote_copy(
            src_ref=self.landed.at[number],
            dst_ref=self.landed.at[number],
            send_sem=self.sems[0].at[1 + number],
            recv_sem=self.sems[1].at[1 + number],
            device_id={"dp": dp_index(self.chip - way, self.core)},
            device_id_type=MESH,
        )

    def begin(self):
        self.swap().start()
        self.local().start()

    def both(self, chip, span):
        return self.kept[chip, span, :].astype(F32) + self.swapped[chip, span, :].astype(F32)

    def send(self, distance):
        if distance == self.chips - 1:
            self.local().wait()
            self.swap().wait_recv()
        for way in (UP, DOWN):

            @pl.when(self.has(way, distance))
            def _(way=way):
                chip = self.chip + way * distance
                slot = self.slot(way, distance - 1)

                def first(row):
                    span = pl.ds(row, CHUNK)
                    self.staged[slot, span, :] = self.both(chip, span).astype(BF16)

                def later(row):
                    span = pl.ds(row, CHUNK)
                    total = self.both(chip, span) + self.landed[
                        self.slot(way, distance), span, :
                    ].astype(F32)
                    self.staged[slot, span, :] = total.astype(BF16)

                if distance == self.chips - 1:
                    chunks(self.rows, first)
                else:

                    @pl.when(self.has(-way, 1))
                    def _():
                        self.arrival(way, distance).wait_recv()
                        chunks(self.rows, later)

                    @pl.when(jnp.logical_not(self.has(-way, 1)))
                    def _():
                        chunks(self.rows, first)

                self.hop(way, distance).start()

    def finish(self, store):
        below, above = self.has(DOWN, 1), self.has(UP, 1)

        def fill(slots):
            for way in slots:
                self.arrival(way, 0).wait_recv()

            def one(row):
                span = pl.ds(row, CHUNK)
                total = self.both(self.chip, span)
                for way in slots:
                    total = total + self.landed[self.slot(way, 0), span, :].astype(F32)
                store(span, total)

            chunks(self.rows, one)

        @pl.when(below & above)
        def _():
            fill((UP, DOWN))

        @pl.when(jnp.logical_not(above))
        def _():
            fill((UP,))

        @pl.when(jnp.logical_not(below))
        def _():
            fill((DOWN,))

    def drain(self):
        self.swap().wait_send()
        for way in (UP, DOWN):
            for distance in range(1, self.chips):

                @pl.when(self.has(way, distance))
                def _(way=way, distance=distance):
                    self.hop(way, distance).wait_send()


def line_scratch(ndp, rows, columns):
    chips = ndp // 2
    return [
        pltpu.VMEM((chips, rows, columns), BF16),
        pltpu.VMEM((chips, rows, columns), BF16),
        pltpu.VMEM((2 * chips - 2, rows, columns), BF16),
        pltpu.VMEM((2 * chips - 2, rows, columns), BF16),
        pltpu.SemaphoreType.DMA((2 * chips + 1,)),
        pltpu.SemaphoreType.DMA((2 * chips + 1,)),
    ]


RING = 6


def leave_kernel(nbits, tiled, *refs):
    refs = list(refs)

    def take(count):
        taken = refs[:count]
        del refs[:count]
        return taken

    d_norm, tokens, d_middle, gain, own_small, d_gain_mid = take(6)
    pieces = take(2)
    grad_input, sum_y, sum_x, gate_all, small_all = take(5)
    landed, staged, s0, r0 = take(4)
    share = small_all.shape[2]
    gate = LineSum(pieces[0], *take(RING))
    if tiled:
        lines = [LineSum(pieces[1], *take(RING), pl.ds(at, share)) for at in (0, share)]
    else:
        lines = [LineSum(pieces[1], *take(RING))]
    d_gain, gains, gains_landed, small, small_landed = take(5)
    gain_s, gain_r, vec_s, vec_r, join_s, join_r, gate_s, gate_r = take(8)
    rows = tokens.shape[0]
    me = lax.axis_index("tensor")
    chip, core, chips = dp_place()
    peers = [chosen for chosen in subsets(tuple(range(nbits))) if chosen]
    others = [(shift, turn) for shift in range(chips) for turn in range(2)][1:]
    greet_peers(nbits, True, True)
    for line in [gate] + lines:
        line.begin()
    scatter = Scatter(d_norm, landed, staged, rows, nbits, s0, r0)
    scatter.begin()
    d_gain[...] = jnp.zeros_like(d_gain)
    far = list(range(chips - 1, 0, -1))
    for distance in far:
        gate.send(distance)
    for line in lines:
        line.send(far[0])
    scatter.advance(0)
    for distance in far[1:-1]:
        for line in lines:
            line.send(distance)
    for step in range(1, nbits):
        scatter.advance(step)

    def pull(row):
        span = pl.ds(row, CHUNK)
        back, parts = norm_pull(
            tokens[span, :].astype(F32), gain[...], scatter.total(row, CHUNK)
        )
        grad_input[span, :] = d_middle[span, :] + back
        d_gain[...] += eight_rows(parts)

    chunks(rows, pull)
    def store_gate(span, value):
        gate_all[me, chip, core, span, :] = value.astype(BF16)

    def gate_copy(number, ref, target):
        return pltpu.make_async_remote_copy(
            src_ref=ref,
            dst_ref=ref,
            send_sem=gate_s.at[number],
            recv_sem=gate_r.at[number],
            device_id=target,
            device_id_type=MESH,
        )

    def gate_line(shift):
        target = {"dp": dp_index((chip + shift) % chips, core)}
        return gate_copy(shift - 1, gate_all.at[me, chip, core], target)

    def gate_tensor(number, chosen):
        target = {"tensor": flipped(me, chosen)}
        return gate_copy(chips - 1 + number, gate_all.at[me, :, core], target)

    def gate_core():
        target = {"dp": dp_index(chip, 1 - core)}
        return gate_copy(chips - 1 + len(peers), gate_all.at[:, :, core], target)

    def start_gate():
        gate.finish(store_gate)
        for shift in range(1, chips):
            gate_line(shift).start()

    top = jnp.sum(d_gain[...], axis=0, keepdims=True)
    low = jnp.sum(d_gain_mid[...], axis=0, keepdims=True)
    place8 = lax.broadcasted_iota(jnp.int32, (8, share), 0)
    for index in range(1 << nbits):
        span = slice(index * share, (index + 1) * share)
        gains[index] = jnp.where(
            place8 == 6, top[:, span], jnp.where(place8 == 7, low[:, span], 0.0)
        )

    def gain_copy(number, chosen):
        peer = flipped(me, chosen)
        return pltpu.make_async_remote_copy(
            src_ref=gains.at[peer],
            dst_ref=gains_landed.at[number],
            send_sem=gain_s.at[number],
            recv_sem=gain_r.at[number],
            device_id={"tensor": peer},
            device_id_type=MESH,
        )

    for number, chosen in enumerate(peers):
        gain_copy(number, chosen).start()
    start_gate()
    if len(far) > 1:
        for line in lines:
            line.send(far[-1])
    total = own_small[...] + gains[me]
    for number, chosen in enumerate(peers):
        gain_copy(number, chosen).wait_recv()
        total = total + gains_landed[number]
    small[...] = total

    def vec_copy(number, shift, turn):
        other = dp_index((chip + shift) % chips, core + turn * (1 - 2 * core))
        return pltpu.make_async_remote_copy(
            src_ref=small,
            dst_ref=small_landed.at[number],
            send_sem=vec_s.at[number],
            recv_sem=vec_r.at[number],
            device_id={"dp": other},
            device_id_type=MESH,
        )

    for number, (shift, turn) in enumerate(others):
        vec_copy(number, shift, turn).start()

    for shift in range(1, chips):
        gate_line(shift).wait_recv()
    for number, chosen in enumerate(peers):
        gate_tensor(number, chosen).start()
    total = small[...]
    for number, (shift, turn) in enumerate(others):
        vec_copy(number, shift, turn).wait_recv()
        total = total + small_landed[number]
    small_all[me] = total

    def join_copy(number, chosen):
        return pltpu.make_async_remote_copy(
            src_ref=small_all.at[me],
            dst_ref=small_all.at[me],
            send_sem=join_s.at[number],
            recv_sem=join_r.at[number],
            device_id={"tensor": flipped(me, chosen)},
            device_id_type=MESH,
        )

    for number, chosen in enumerate(peers):
        join_copy(number, chosen).start()
    for number, chosen in enumerate(peers):
        gate_tensor(number, chosen).wait_recv()
    gate_core().start()

    def store_in(*targets):
        def store(span, value):
            for number, ref in enumerate(targets):
                ref[span, :] = value[:, number * share : (number + 1) * share]

        return store

    if tiled:
        lines[0].finish(store_in(sum_y))
        lines[1].finish(store_in(sum_x))
    else:
        lines[0].finish(store_in(sum_y, sum_x))
    gate_core().wait()
    for shift in range(1, chips):
        gate_line(shift).wait_send()
    for number, chosen in enumerate(peers):
        gate_tensor(number, chosen).wait_send()
        gain_copy(number, chosen).wait_send()
        join_copy(number, chosen).wait()
    for number, (shift, turn) in enumerate(others):
        vec_copy(number, shift, turn).wait_send()
    scatter.drain()
    for line in [gate] + lines:
        line.drain()


def in_vmem(count):
    return [pl.BlockSpec(memory_space=pltpu.VMEM)] * count


def call_kernel(kernel, outs, scratch, number, *operands, far_in=(), far_out=(), cost_us=1):
    vmem = pl.BlockSpec(memory_space=pltpu.VMEM)
    far = pl.BlockSpec(memory_space=pl.ANY)
    return pl.pallas_call(
        kernel,
        out_shape=outs,
        in_specs=[far if i in far_in else vmem for i in range(len(operands))],
        out_specs=tuple(far if i in far_out else vmem for i in range(len(outs))),
        scratch_shapes=scratch,
        cost_estimate=pl.CostEstimate(
            flops=0, bytes_accessed=cost_us * 1_000_000, transcendentals=0
        ),
        compiler_params=pltpu.CompilerParams(
            collective_id=number, has_side_effects=True, vmem_limit_bytes=VMEM_BYTES
        ),
    )(*operands)


def sigmoid(values):
    return 1.0 / (1.0 + jnp.exp(-values))


def one_minus_exp(values):
    series = values / 7.0 + 1.0
    for order in (6.0, 5.0, 4.0, 3.0, 2.0):
        series = 1.0 + series * values / order
    return jnp.where(values > -0.3, -values * series, 1.0 - jnp.exp(values))


GELU_K = 0.7978845608028654
GELU_C = 0.044715


def gelu_parts(values):
    square = values * values
    bent = jnp.tanh(GELU_K * values * (1.0 + GELU_C * square))
    gelu = 0.5 * values * (1.0 + bent)
    slope = 0.5 * (1.0 + bent) + 0.5 * values * (1.0 - bent * bent) * GELU_K * (
        1.0 + 3.0 * GELU_C * square
    )
    return gelu, slope


def gate_terms(gate_a, gate_x, soft, since):
    sig_a = sigmoid(gate_a)
    sig_x = sigmoid(gate_x)
    log_decay = -8.0 * sig_a * soft
    decay = jnp.exp(log_decay)
    scale = jnp.sqrt(one_minus_exp(2.0 * log_decay))
    keep = since > 0.5
    return sig_a, sig_x, decay, jnp.where(keep, scale, 1.0), keep


def scan_down(decay, value, carry):
    place = lax.broadcasted_iota(jnp.int32, decay.shape, 0)
    for shift in (1, 2, 4):
        past = place >= shift
        moved = pltpu.roll(value, shift, 0)
        value = jnp.where(past, decay * moved + value, value)
        decay = jnp.where(past, decay * pltpu.roll(decay, shift, 0), decay)
    return decay * carry + value


def scan_up(decay, value, carry):
    place = lax.broadcasted_iota(jnp.int32, decay.shape, 0)
    factor = jnp.where(place < 7, pltpu.roll(decay, 7, 0), 1.0)
    for shift in (1, 2, 4):
        past = place < 8 - shift
        moved = pltpu.roll(value, 8 - shift, 0)
        value = jnp.where(past, factor * moved + value, value)
        factor = jnp.where(past, factor * pltpu.roll(factor, 8 - shift, 0), factor)
    return factor * carry + value


def forward_scan(conv_rows, gates, branch_y, soft, since, mixed, states, between=()):
    total_rows, width = states.shape

    def step(i, carry):
        row = pl.multiple_of(i * CHUNK, CHUNK)
        span = pl.ds(row, CHUNK)
        values = conv_rows(span).astype(F32)
        kept = []
        for at in range(0, CHUNK, 8):
            tile = pl.ds(row + at, 8)
            sig_a, sig_x, decay, scale, keep = gate_terms(
                gates[tile, :width], gates[tile, width:], soft[...], since[tile, :]
            )
            given = values[at : at + 8] * sig_x * scale
            state = scan_down(jnp.where(keep, decay, 0.0), given, carry)
            carry = state[7:8]
            states[tile, :] = state
            kept.append(state * gelu_parts(branch_y[tile, :])[0])
        mixed[span, :] = jnp.concatenate(kept, axis=0).astype(BF16)
        return carry

    steps, stretches = total_rows // CHUNK, len(between) + 1
    carry = jnp.zeros((1, width), F32)
    for stretch in range(stretches):
        first, last = stretch * steps // stretches, (stretch + 1) * steps // stretches
        carry = lax.fori_loop(first, last, step, carry)
        if stretch < len(between):
            between[stretch]()


def forward_scan_kernel(conv, gates, branch_y, soft, since, mixed, states):
    forward_scan(lambda span: conv[span, :], gates, branch_y, soft, since, mixed, states)


def backward_scan(
    d_mixed, conv_rows, gates, branch_y, states, soft, slope_soft, since, d_conv, d_gates, d_branch, d_decay
):
    total_rows, width = states.shape
    d_decay[...] = jnp.zeros_like(d_decay)

    def step(i, carry):
        row = pl.multiple_of(total_rows - CHUNK - i * CHUNK, CHUNK)
        span = pl.ds(row, CHUNK)
        values = conv_rows(span).astype(F32)
        kept = []
        for at in range(CHUNK - 8, -1, -8):
            tile = pl.ds(row + at, 8)
            soft_row = soft[...]
            sig_a, sig_x, decay, scale, keep = gate_terms(
                gates[tile, :width], gates[tile, width:], soft_row, since[tile, :]
            )
            value = values[at : at + 8]
            gelu, slope = gelu_parts(branch_y[tile, :])
            state = states[tile, :]
            upper = d_mixed[tile, :]
            held = jnp.where(keep, decay, 0.0)
            lam = scan_up(held, upper * gelu, carry)
            carry = held[0:1] * lam[0:1]
            d_conv[tile, :] = lam * sig_x * scale
            d_x = lam * value * scale * sig_x * (1.0 - sig_x)
            given = value * sig_x
            d_log = lam * (state - given * scale - given * decay * decay / scale)
            d_log = jnp.where(keep, d_log, 0.0)
            d_a = d_log * (-8.0 * soft_row) * sig_a * (1.0 - sig_a)
            d_decay[...] += d_log * (-8.0 * sig_a) * slope_soft[...]
            kept.append((d_a, d_x, upper * state * slope))
        kept = kept[::-1]
        d_gates[span, :width] = jnp.concatenate([k[0] for k in kept], axis=0).astype(BF16)
        d_gates[span, width:] = jnp.concatenate([k[1] for k in kept], axis=0).astype(BF16)
        d_branch[span, :] = jnp.concatenate([k[2] for k in kept], axis=0).astype(BF16)
        return carry

    lax.fori_loop(0, total_rows // CHUNK, step, jnp.zeros((1, width), F32))


def backward_scan_kernel(
    d_mixed, conv, gates, branch_y, states, soft, slope_soft, since, d_conv, d_gates, d_branch, d_decay
):
    backward_scan(
        d_mixed,
        lambda span: conv[span, :],
        gates,
        branch_y,
        states,
        soft,
        slope_soft,
        since,
        d_conv,
        d_gates,
        d_branch,
        d_decay,
    )


def times_transposed(left, right):
    return lax.dot_general(left, right, (((1,), (1,)), ((), ())), preferred_element_type=F32)


class HalfBlocks:
    def __init__(self, channels, block):
        self.odd = lax.axis_index("tensor") % 2
        self.half = block // 2
        self.block = block
        self.count = channels // block + 1
        self.channels = channels
        self.own = pl.multiple_of(self.odd * self.half, self.half)
        self.shared = (1 - self.odd) * (self.count - 1)
        self.mine_in_block = pl.multiple_of(self.odd * self.half, self.half)
        self.other_in_block = pl.multiple_of((1 - self.odd) * self.half, self.half)
        self.mine = pl.multiple_of((1 - self.odd) * (channels - self.half), self.half)
        self.pair = {"tensor": lax.axis_index("tensor") + 1 - 2 * self.odd}

    def full(self, index):
        block = index + self.odd
        return block, pl.multiple_of(index * self.block + self.odd * self.half, self.half)

    def span(self, block):
        return pl.ds(pl.multiple_of(block * self.block, self.block), self.block)

    def shared_part(self, start):
        return pl.ds(pl.multiple_of(self.shared * self.block + start, self.half), self.half)


PART = 256


def parts(rows, body):
    def step(i, carry):
        body(pl.ds(pl.multiple_of(i * PART, PART), PART))
        return carry

    lax.fori_loop(0, rows // PART, step, 0)


def recurrence_kernel(
    taps,
    nbits,
    branches,
    tap_rows,
    soft,
    since,
    weights,
    cot,
    mixed,
    states,
    window,
    gates,
    cot_all,
    send,
    recv,
    *sems,
):
    total_rows, width = states.shape
    block = weights.shape[2]
    place = HalfBlocks(width, block)
    branch_y, branch_x = branches.at[:, :width], branches.at[:, width:]
    greet(tensor_bits(nbits))
    fetch = Fetch(nbits, cot, cot_all, *sems)
    fetch.local.start()

    def conv(i, before):
        row = pl.multiple_of(i * CHUNK, CHUNK)
        kept = []
        for at in range(0, CHUNK, 8):
            tile = pl.ds(row + at, 8)
            values = branch_x[tile, :]
            line = lax.broadcasted_iota(jnp.int32, values.shape, 0)
            total = values * tap_rows[0:1, :]
            for tap in range(1, taps):
                moved = jnp.where(
                    line < tap, pltpu.roll(before, tap, 0), pltpu.roll(values, tap, 0)
                )
                moved = jnp.where(since[tile, :] > tap - 0.5, moved, 0.0)
                total = total + moved * tap_rows[tap : tap + 1, :]
            kept.append(total)
            before = values
        window[pl.ds(row, CHUNK), pl.ds(place.own, width)] = jnp.concatenate(
            kept, axis=0
        ).astype(BF16)
        return before

    lax.fori_loop(0, total_rows // CHUNK, conv, jnp.zeros((8, width), F32))
    source = window.at[:, place.shared_part(place.mine_in_block)]
    away = pl.multiple_of(place.odd * (place.count - 1) * block + place.mine_in_block, place.half)
    rim = pltpu.make_async_remote_copy(
        src_ref=source,
        dst_ref=window.at[:, pl.ds(away, place.half)],
        send_sem=send.at[0],
        recv_sem=recv.at[0],
        device_id=place.pair,
        device_id_type=MESH,
    )
    rim.start()
    fetch.begin()

    def full(span):
        for index in range(place.count - 1):
            number, at = place.full(index)
            cells = window[span, place.span(number)]
            for s in range(2):
                gates[span, pl.ds(s * width + at, block)] = jnp.dot(
                    cells, weights[s, number], preferred_element_type=F32
                )

    parts(total_rows, full)
    rim.wait()

    def shared(span):
        cells = window[span, place.span(place.shared)]
        for s in range(2):
            gates[span, pl.ds(s * width + place.mine, place.half)] = jnp.dot(
                cells,
                weights[s, place.shared, :, pl.ds(place.mine_in_block, place.half)],
                preferred_element_type=F32,
            )

    parts(total_rows, shared)
    forward_scan(
        lambda span: window[span, pl.ds(place.own, width)],
        gates,
        branch_y,
        soft,
        since,
        mixed,
        states,
        [fetch.advance],
    )
    fetch.finish()


def recurrence_back_kernel(
    taps,
    nbits,
    with_ffn,
    d_mixed,
    window,
    gates,
    branches,
    states,
    tap_rows,
    soft,
    slope_soft,
    since,
    weights,
    *refs,
):
    refs = list(refs)

    def take(count):
        taken = refs[:count]
        del refs[:count]
        return taken

    ffn, middle = take(2) if with_ffn else (None, None)
    grad_out = take(1)[0]
    d_branches, gate_grad, own_small, sum_out = take(4)
    mixed = take(1)[0] if with_ffn else None
    d_conv, d_gates, given, taken, sums, send, recv = take(7)
    flow = LineSum(grad_out, *take(RING))
    far = list(range(flow.chips - 1, 0, -1))
    total_rows, width = states.shape
    block = weights.shape[2]
    place = HalfBlocks(width, block)
    half = place.half
    branch_y, branch_x = branches.at[:, :width], branches.at[:, width:]
    d_branch_y, d_branch_x = d_branches.at[:, :width], d_branches.at[:, width:]
    greet_peers(nbits, False, False)
    flow.begin()
    if with_ffn:
        scatter = Scatter(ffn, *take(2), middle.shape[0], nbits, *take(2))
        scatter.begin()
    flow.send(far[0])
    backward_scan(
        d_mixed,
        lambda span: window[span, pl.ds(place.own, width)],
        gates,
        branch_y,
        states,
        soft,
        slope_soft,
        since,
        d_conv,
        d_gates,
        d_branch_y,
        sums.at[taps],
    )

    def to_pair(span):
        total = jnp.zeros((PART, half), F32)
        for s in range(2):
            total = total + times_transposed(
                d_gates[span, pl.ds(s * width + place.mine, half)],
                weights[
                    s,
                    place.shared,
                    pl.ds(place.other_in_block, half),
                    pl.ds(place.mine_in_block, half),
                ],
            )
        given[span, :] = total.astype(BF16)

    parts(total_rows, to_pair)
    rim = pltpu.make_async_remote_copy(
        src_ref=given,
        dst_ref=taken,
        send_sem=send.at[0],
        recv_sem=recv.at[0],
        device_id=place.pair,
        device_id_type=MESH,
    )
    rim.start()
    for distance in far[1:-1]:
        flow.send(distance)

    def full(span):
        for index in range(place.count - 1):
            number, at = place.full(index)
            total = d_conv[span, pl.ds(at, block)]
            for s in range(2):
                total = total + times_transposed(
                    d_gates[span, pl.ds(s * width + at, block)], weights[s, number]
                )
            d_conv[span, pl.ds(at, block)] = total
        total = d_conv[span, pl.ds(place.mine, half)]
        for s in range(2):
            total = total + times_transposed(
                d_gates[span, pl.ds(s * width + place.mine, half)],
                weights[
                    s,
                    place.shared,
                    pl.ds(place.mine_in_block, half),
                    pl.ds(place.mine_in_block, half),
                ],
            )
        d_conv[span, pl.ds(place.mine, half)] = total

    parts(total_rows, full)
    if with_ffn:
        scatter.advance(0)
    units = width // half
    for index in range(units):
        number = (index + place.odd) // 2
        cells = window[:, place.span(number)]
        both = jnp.concatenate(
            [d_gates[:, s * width + index * half : s * width + (index + 1) * half] for s in range(2)],
            axis=1,
        )
        found = lax.dot_general(
            cells, both, (((0,), (0,)), ((), ())), preferred_element_type=F32
        ).astype(BF16)
        gate_grad[2 * index] = found[:, :half]
        gate_grad[2 * index + 1] = found[:, half:]
    rim.wait()
    if len(far) > 1:
        flow.send(far[-1])

    def add(span):
        d_conv[span, pl.ds(place.mine, half)] += taken[span, :].astype(F32)

    parts(total_rows, add)
    for tap in range(taps):
        sums[tap] = jnp.zeros((8, width), F32)

    def conv(i, after):
        row = pl.multiple_of(total_rows - CHUNK - i * CHUNK, CHUNK)
        kept = []
        for at in range(CHUNK - 8, -1, -8):
            tile = pl.ds(row + at, 8)
            values = d_conv[tile, :]
            line = lax.broadcasted_iota(jnp.int32, values.shape, 0)
            below = branch_x[tile, :]
            higher = pl.multiple_of((row + at - 8 + total_rows) % total_rows, 8)
            above = branch_x[pl.ds(higher, 8), :]
            total = values * tap_rows[0:1, :]
            sums[0] += values * below
            masked = []
            for tap in range(1, taps):
                here = jnp.where(since[tile, :] > tap - 0.5, values, 0.0)
                masked.append(here)
                moved = jnp.where(
                    line < 8 - tap,
                    pltpu.roll(here, 8 - tap, 0),
                    pltpu.roll(after[tap - 1], 8 - tap, 0),
                )
                total = total + moved * tap_rows[tap : tap + 1, :]
                source = jnp.where(
                    line < tap, pltpu.roll(above, tap, 0), pltpu.roll(below, tap, 0)
                )
                sums[tap] += here * source
            after = tuple(masked)
            kept.append(total)
        d_branch_x[pl.ds(row, CHUNK), :] = jnp.concatenate(kept[::-1], axis=0).astype(BF16)
        return after

    none = jnp.zeros((8, width), F32)
    lax.fori_loop(0, total_rows // CHUNK, conv, (none,) * (taps - 1))
    line = lax.broadcasted_iota(jnp.int32, (8, width), 0)
    total = jnp.zeros((8, width), F32)
    for tap in range(taps + 1):
        row = jnp.sum(sums[tap], axis=0, keepdims=True)
        total = jnp.where(line == tap, row, total)
    own_small[...] = total
    if with_ffn:
        for step in range(1, nbits):
            scatter.advance(step)

        def result(row):
            span = pl.ds(row, CHUNK)
            mixed[span, :] = (middle[span, :] + scatter.total(row, CHUNK)).astype(BF16)

        chunks(middle.shape[0], result)
        scatter.drain()

    def store(span, value):
        sum_out[span, :] = value

    flow.finish(store)
    flow.drain()


def finish_kernel(
    taps,
    gates,
    small,
    in_out,
    in_y,
    in_x,
    in_grad,
    in_mixed,
    in_both,
    in_down,
    whole,
    out_out,
    out_y,
    out_x,
    out_grad,
    out_mixed,
    out_gate,
    out_up,
    out_down,
    conv,
    decay,
    gain_in,
    gain_mid,
):
    for piece in range(gates.shape[0]):
        for s in range(2):
            whole[s, 0, :, piece * 128 : (piece + 1) * 128] = gates[piece, s].astype(F32)
    out_out[...] = in_out[...]
    out_y[...] = in_y[...]
    out_x[...] = in_x[...]
    out_grad[...] = in_grad[...]
    out_mixed[...] = in_mixed[...]
    units = out_gate.shape[1]
    out_gate[...] = in_both[:, :units].astype(F32)
    out_up[...] = in_both[:, units:].astype(F32)
    out_down[...] = in_down[...].astype(F32)

    @pl.when(pl.program_id(0) == 0)
    def _():
        share = small.shape[2]
        for index in range(small.shape[0]):
            span = slice(index * share, (index + 1) * share)
            conv[:, span] = small[index, :taps, :]
            for at in range(0, share, 128):
                row = (index * share + at) // 128
                decay[row : row + 1, :] = small[index, taps : taps + 1, at : at + 128]
                gain_in[row : row + 1, :] = small[index, 6:7, at : at + 128]
                gain_mid[row : row + 1, :] = small[index, 7:8, at : at + 128]


def finish(gate_all, small_all, sums, grad_input, mixed, both, down, taps, gate_shape):
    _, blocks, block, _ = gate_shape
    unit = gate_all.shape[-1]
    pieces = block // unit
    width = small_all.shape[0] * small_all.shape[2]
    rows, units = down.shape
    own_rows = grad_input.shape[0]
    steps, held = rows // blocks, own_rows // 8
    if unit != 128 or rows % (16 * blocks) or own_rows % 128:
        whole = gate_all.reshape(blocks, pieces, 2, block, unit).transpose(2, 0, 3, 1, 4)
        summed = small_all.transpose(1, 0, 2).reshape(8, width)
        whole = whole.reshape(gate_shape).astype(F32)
        wide = tuple(one.astype(F32) for one in (both[:, :units], both[:, units:], down))
        last = (summed[:taps], summed[taps], summed[6], summed[7])
        return (whole, *sums, grad_input, mixed, *wide, *last)
    shape = jax.ShapeDtypeStruct

    def by_rows(count, columns):
        return pl.BlockSpec((count, columns), lambda n: (n, 0))

    def by_held(columns):
        return pl.BlockSpec((held, columns), lambda n: (jnp.minimum(n, 7), 0))

    def whole_array(*dims):
        return pl.BlockSpec(dims, lambda n: (0,) * len(dims))

    columns = sums[0].shape[1]
    d_width = grad_input.shape[1]
    lines = width // 128
    found = pl.pallas_call(
        partial(finish_kernel, taps),
        grid=(blocks,),
        in_specs=[
            pl.BlockSpec((pieces, 2, block, unit), lambda n: (n, 0, 0, 0)),
            whole_array(*small_all.shape),
        ]
        + [by_rows(steps, columns)] * 3
        + [by_held(d_width)] * 2
        + [by_rows(steps, 2 * units), by_rows(steps, units)],
        out_specs=(
            (pl.BlockSpec((2, 1, block, block), lambda n: (0, n, 0, 0)),)
            + (by_rows(steps, columns),) * 3
            + (by_held(d_width),) * 2
            + (by_rows(steps, units),) * 3
            + (whole_array(taps, width),)
            + (whole_array(lines, 128),) * 3
        ),
        out_shape=(
            (shape(gate_shape, F32),)
            + (shape((rows, columns), F32),) * 3
            + (shape(grad_input.shape, F32), shape(mixed.shape, BF16))
            + (shape((rows, units), F32),) * 3
            + (shape((taps, width), F32),)
            + (shape((lines, 128), F32),) * 3
        ),
        compiler_params=pltpu.CompilerParams(vmem_limit_bytes=VMEM_BYTES),
    )(
        gate_all.reshape(blocks * pieces, 2, block, unit),
        small_all,
        *sums,
        grad_input,
        mixed,
        both,
        down,
    )
    return found[:10] + tuple(one.reshape(width) for one in found[10:])


def scan_call(kernel, outs, *operands):
    return pl.pallas_call(
        kernel,
        out_shape=outs,
        in_specs=in_vmem(len(operands)),
        out_specs=tuple(in_vmem(len(outs))),
        compiler_params=pltpu.CompilerParams(vmem_limit_bytes=VMEM_BYTES),
    )(*operands)


class Rim:
    def __init__(self, route, back, source, first, width, room):
        self.route, self.back = route, back
        self.source, self.first, self.width = source, first, width
        self.room = room

    def fetch(self, values):
        part = lax.dynamic_slice_in_dim(values, self.source, self.width, 1)
        return lax.ppermute(part, "tensor", self.route)

    def give(self, part):
        return lax.ppermute(part, "tensor", self.back)

    def add(self, values, part):
        zeros = jnp.zeros(values.shape, F32)
        return values + lax.dynamic_update_slice_in_dim(
            zeros, part.astype(F32), self.source, 1
        )

    def window(self, channels):
        return (channels // self.width + 4) * self.width


def gate_rims(channels, block_size, ntensor, offset):
    up = [(i, i + 1) for i in range(ntensor - 1)]
    down = [(i + 1, i) for i in range(ntensor - 1)]
    last = jnp.int32(channels - block_size)
    return [
        Rim(up, down, last, offset - block_size, block_size, block_size),
        Rim(down, up, jnp.int32(0), offset + channels, block_size, block_size),
    ]


def same_block(first, count, offset, channels, block_size):
    rows = (first + jnp.arange(count, dtype=jnp.int32))[:, None]
    columns = (offset + jnp.arange(channels, dtype=jnp.int32))[None, :]
    return (rows + block_size) // block_size == (columns + block_size) // block_size


def gate_dense(gate_w, offset, first, count):
    block_size = gate_w.shape[2]
    total = gate_w.shape[1] * block_size
    channels = total // lax.axis_size("tensor")
    columns = gate_w.transpose(2, 0, 1, 3).reshape(block_size, 2, total)
    columns = lax.dynamic_slice_in_dim(columns, offset, channels, 2)
    copies = -(-count // block_size) + 1
    tall = jnp.concatenate([columns] * copies, axis=0)
    tall = lax.dynamic_slice_in_dim(tall, (first + block_size) % block_size, count, 0)
    same = same_block(first, count, offset, channels, block_size)
    dense = jnp.where(same[:, None, :], tall, jnp.zeros_like(tall))
    return dense.reshape(count, 2 * channels)


def doc_starts(seg_ids, seq_len):
    places = jnp.arange(seg_ids.shape[0], dtype=jnp.int32)
    before = jnp.concatenate([seg_ids[:1], seg_ids[:-1]])
    resets = (places % seq_len == 0) | (seg_ids != before)
    starts = lax.cummax(jnp.where(resets, places, jnp.zeros_like(places)), axis=0)
    return starts


def causal_conv(starts, values, kernel):
    places = jnp.arange(values.shape[0], dtype=jnp.int32)
    total = values * kernel[0]
    for offset_k in range(1, kernel.shape[0]):
        moved = jnp.concatenate(
            [jnp.zeros((offset_k, values.shape[1]), values.dtype), values[:-offset_k]], axis=0
        )
        valid = (places - offset_k >= starts)[:, None]
        total = total + jnp.where(valid, moved, jnp.zeros_like(moved)) * kernel[offset_k]
    return total


def geglu(gate_val, up_val):
    return jax.nn.gelu(gate_val, approximate=True) * up_val


def rows_times(left, right):
    return lax.dot_general(left, right, (((1,), (1,)), ((), ())), preferred_element_type=F32)


def rows_back(lefts, rights):
    total = rows_times(lefts[0], rights[0])
    return total + rows_times(lefts[1], rights[1])


def inner_rows(left, right):
    return lax.dot_general(left, right, (((0,), (0,)), ((), ())), preferred_element_type=F32)


def halved(grad, ndp):
    return grad.reshape(ndp // 2, 2, grad.shape[0] // ndp, grad.shape[1])


def body(
    tokens,
    segments,
    cotangent,
    norm_gain,
    w_y,
    w_x,
    conv_w,
    gate_w,
    decay_param,
    w_out,
    mlp_gain,
    w_gate,
    w_up,
    w_down,
):
    ntensor = lax.axis_size("tensor")
    ndp = lax.axis_size("dp")
    nbits = log2_of(ntensor)
    tindex = lax.axis_index("tensor")
    own_rows, width = tokens.shape
    group_rows = own_rows * ntensor
    block_size = gate_w.shape[2]
    nblocks = gate_w.shape[1]
    dp_rows, channels = w_y.shape
    taps = conv_w.shape[0]
    offset = tindex * channels
    shape = jax.ShapeDtypeStruct
    gain_in = norm_gain.reshape(1, width)
    gain_mid = mlp_gain.reshape(1, width)
    seg_rows_of = own_rows // 128
    tiled = channels % 128 == 0
    w_yx = (w_y, w_x) if tiled else (jnp.concatenate([w_y, w_x], axis=1),)
    normed_rows, seg_all, wyx_loc, wout_loc = call_kernel(
        partial(enter_kernel, nbits, len(w_yx)),
        (
            shape((group_rows, width), BF16),
            shape((ntensor, seg_rows_of, 128), jnp.int32),
            shape((dp_rows * ndp, 2 * channels), BF16),
            shape((dp_rows * ndp, channels), BF16),
        ),
        gather_sems(nbits)
        + [pltpu.SemaphoreType.DMA((ntensor - 1,)), pltpu.SemaphoreType.DMA((ntensor - 1,))]
        + [pltpu.SemaphoreType.DMA((1,))]
        + line_sems(ndp) * (len(w_yx) + 1),
        0,
        tokens,
        segments.reshape(seg_rows_of, 128),
        gain_in,
        *w_yx,
        w_out,
        far_in=tuple(range(3, 4 + len(w_yx))),
        far_out=(2, 3),
    )
    units = w_gate.shape[1]
    w_both = jnp.concatenate([w_gate, w_up], axis=1)
    w_both, w_down, normed_rows = lax.optimization_barrier((w_both, w_down, normed_rows))
    both_loc = lax.all_gather(w_both, "dp", axis=0, tiled=True)
    wd_loc = lax.all_gather(w_down, "dp", axis=0, tiled=True)
    seg_rows = seg_all.reshape(group_rows)
    starts = doc_starts(seg_rows, group_rows)
    conv_loc = lax.dynamic_slice_in_dim(conv_w, offset, channels, 1)
    decay_loc = lax.dynamic_slice_in_dim(decay_param, offset, channels, 0).reshape(1, channels)
    soft = jax.nn.softplus(decay_loc)
    slope_soft = jax.nn.sigmoid(decay_loc)
    half_blocks = (
        channels % block_size == block_size // 2 and ntensor % 2 == 0 and block_size % 256 == 0
    )
    since = (jnp.arange(group_rows, dtype=jnp.int32) - starts).astype(F32)[:, None]
    branches = jnp.dot(normed_rows, wyx_loc, preferred_element_type=F32)
    if half_blocks:
        span_blocks = channels // block_size + 1
        w_window = lax.dynamic_slice_in_dim(gate_w, offset // block_size, span_blocks, 1)
        taps_pad = jnp.concatenate([conv_loc, jnp.zeros((8 - taps, channels), F32)], axis=0)
        mixed_low, states, window, gate_pre, cot_rows = call_kernel(
            partial(recurrence_kernel, taps, nbits),
            (
                shape((group_rows, channels), BF16),
                shape((group_rows, channels), F32),
                shape((group_rows, span_blocks * block_size), BF16),
                shape((group_rows, 2 * channels), F32),
                shape((group_rows, width), BF16),
            ),
            [pltpu.SemaphoreType.DMA((1,)), pltpu.SemaphoreType.DMA((1,))]
            + fetch_scratch(nbits),
            5,
            branches,
            taps_pad,
            soft,
            since,
            w_window,
            cotangent,
        )
    else:
        branch_y, branch_x = branches[:, :channels], branches[:, channels:]
        (cot_rows,) = call_kernel(
            partial(fetch_kernel, nbits),
            (shape((group_rows, width), BF16),),
            fetch_scratch(nbits),
            5,
            cotangent,
        )
        rims = gate_rims(channels, block_size, ntensor, offset)
        own_dense = gate_dense(gate_w, offset, offset, channels)
        rim_dense = [gate_dense(gate_w, offset, rim.first, rim.width) for rim in rims]
        conv_out, conv_pull = jax.vjp(partial(causal_conv, starts), branch_x, conv_loc)
        conv_low = conv_out.astype(BF16)
        rim_cells = [rim.fetch(conv_low) for rim in rims]
        gate_pre = jnp.dot(conv_low, own_dense, preferred_element_type=F32)
        for cells, dense in zip(rim_cells, rim_dense):
            gate_pre = gate_pre + jnp.dot(cells, dense, preferred_element_type=F32)
        mixed_low, states = scan_call(
            forward_scan_kernel,
            (shape((group_rows, channels), BF16), shape((group_rows, channels), F32)),
            conv_low,
            gate_pre,
            branch_y,
            soft,
            since,
        )
    middle, mid_rows = call_kernel(
        partial(middle_kernel, nbits),
        (shape((own_rows, width), F32), shape((group_rows, width), BF16)),
        scatter_scratch(own_rows, width, nbits) + gather_sems(nbits),
        1,
        rows_times(mixed_low, wout_loc).astype(BF16),
        tokens,
        gain_mid,
    )
    pre = jnp.dot(mid_rows, both_loc, preferred_element_type=F32)
    hidden, act_pull = jax.vjp(geglu, pre[:, :units], pre[:, units:])
    hidden_low = hidden.astype(BF16)
    grad_wd = inner_rows(cot_rows, hidden_low).astype(BF16)
    sum_wd = lax.psum_scatter(grad_wd, "dp", scatter_dimension=0, tiled=True)
    grad_wd, wd_loc = lax.optimization_barrier((grad_wd, wd_loc))
    d_hidden = jnp.dot(cot_rows, wd_loc, preferred_element_type=F32)
    d_gate, d_up = act_pull(d_hidden)
    d_pre = jnp.concatenate([d_gate.astype(BF16), d_up.astype(BF16)], axis=1)
    grad_both = inner_rows(mid_rows, d_pre).astype(BF16)
    sum_both = lax.psum_scatter(grad_both, "dp", scatter_dimension=0, tiled=True)
    d_pre, grad_both = lax.optimization_barrier((d_pre, grad_both))
    d_mid_part = rows_times(d_pre, both_loc).astype(BF16)
    d_middle, d_mixer, d_gain_mid, ffn_part = call_kernel(
        partial(turn_kernel, nbits),
        (
            shape((own_rows, width), F32),
            shape((group_rows, width), BF16),
            shape((8, width), F32),
            shape((group_rows, width), BF16),
        ),
        scatter_scratch(own_rows, width, nbits) + gather_sems(nbits) + product_scratch(units),
        2,
        d_mid_part,
        cotangent,
        middle,
        gain_mid,
        hidden_low,
        wd_loc,
        far_in=(5,),
    )
    d_mixer, sum_wd = lax.optimization_barrier((d_mixer, sum_wd))
    grad_wout = inner_rows(d_mixer, mixed_low).astype(BF16)
    d_mixed_in = jnp.dot(d_mixer, wout_loc, preferred_element_type=F32)
    unit = math.gcd(channels, block_size)
    merged = half_blocks and nbits <= 2
    if half_blocks:
        found = call_kernel(
            partial(recurrence_back_kernel, taps, nbits, merged),
            (
                shape((group_rows, 2 * channels), BF16),
                shape((channels // unit * 2, block_size, unit), BF16),
                shape((8, channels), F32),
                shape((dp_rows, channels), F32),
            )
            + ((shape((own_rows, width), BF16),) if merged else ()),
            [
                pltpu.VMEM((group_rows, channels), F32),
                pltpu.VMEM((group_rows, 2 * channels), BF16),
                pltpu.VMEM((group_rows, unit), BF16),
                pltpu.VMEM((group_rows, unit), BF16),
                pltpu.VMEM((taps + 1, 8, channels), F32),
                pltpu.SemaphoreType.DMA((1,)),
                pltpu.SemaphoreType.DMA((1,)),
            ]
            + line_scratch(ndp, dp_rows, channels)
            + (scatter_scratch(own_rows, width, nbits) if merged else []),
            6,
            d_mixed_in,
            window,
            gate_pre,
            branches,
            states,
            taps_pad,
            soft,
            slope_soft,
            since,
            w_window,
            *((ffn_part, middle) if merged else ()),
            halved(grad_wout, ndp),
            far_in=(12 if merged else 10,),
        )
        d_branches, gate_grad, own_small, sum_wout = found[:4]
        gate_grad = gate_grad.reshape(channels // unit * 2 * block_size, unit)
    else:
        d_conv, d_gate_low, d_branch_y, d_decay = scan_call(
            backward_scan_kernel,
            (
                shape((group_rows, channels), F32),
                shape((group_rows, 2 * channels), BF16),
                shape((group_rows, channels), BF16),
                shape((8, channels), F32),
            ),
            d_mixed_in,
            conv_low,
            gate_pre,
            branch_y,
            states,
            soft,
            slope_soft,
            since,
        )
        given = [rows_times(d_gate_low, dense).astype(BF16) for dense in rim_dense]
        taken = [rim.give(part) for rim, part in zip(rims, given)]
        d_conv_out = d_conv + rows_times(d_gate_low, own_dense)
        for rim, part in zip(rims, taken):
            d_conv_out = rim.add(d_conv_out, part)
        d_branch_x, grad_conv_loc = conv_pull(d_conv_out)
        d_branches = jnp.concatenate([d_branch_y, d_branch_x.astype(BF16)], axis=1)
        base = offset // block_size * block_size - rims[0].room
        window_rows = rims[0].window(channels)
        picked = jnp.zeros((window_rows, 2 * channels), F32)
        for first, cells in [(offset, conv_low)] + [(r.first, c) for r, c in zip(rims, rim_cells)]:
            part = inner_rows(cells, d_gate_low)
            same = same_block(first, cells.shape[1], offset, channels, block_size)
            part = jnp.where(jnp.concatenate([same, same], axis=1), part, 0.0)
            picked = lax.dynamic_update_slice(picked, part, (first - base, jnp.int32(0)))
        picked = picked.reshape(window_rows // block_size, block_size, 2, channels // unit, unit)
        gate_grad = picked.sum(axis=0).astype(BF16).transpose(2, 1, 0, 3)
        gate_grad = gate_grad.reshape(channels // unit * 2 * block_size, unit)
        own_small = jnp.concatenate(
            [
                grad_conv_loc,
                jnp.sum(d_decay, axis=0, keepdims=True),
                jnp.zeros((7 - taps, channels), F32),
            ],
            axis=0,
        )

    grad_wyx = inner_rows(normed_rows, d_branches).astype(BF16)
    d_normed = rows_times(d_branches, wyx_loc).astype(BF16)
    d_normed, grad_wyx, sum_both = lax.optimization_barrier((d_normed, grad_wyx, sum_both))
    if not half_blocks:
        sum_wout = lax.psum_scatter(grad_wout, "dp", scatter_dimension=0, tiled=True)
        sum_wout = sum_wout.astype(F32)

    pieces = [halved(grad, ndp) for grad in (gate_grad, grad_wyx)]
    peers = ntensor - 1
    gate_rows = gate_grad.shape[0] // ndp
    dma = pltpu.SemaphoreType.DMA
    scratch = scatter_scratch(own_rows, width, nbits)
    scratch += line_scratch(ndp, gate_rows, unit)
    if tiled:
        scratch += line_scratch(ndp, dp_rows, channels) * 2
    else:
        scratch += line_scratch(ndp, dp_rows, 2 * channels)
    scratch += [
        pltpu.VMEM((8, width), F32),
        pltpu.VMEM((ntensor, 8, channels), F32),
        pltpu.VMEM((peers, 8, channels), F32),
        pltpu.VMEM((8, channels), F32),
        pltpu.VMEM((ndp - 1, 8, channels), F32),
    ]
    scratch += [dma((peers,)), dma((peers,)), dma((ndp - 1,)), dma((ndp - 1,))]
    scratch += [dma((peers,)), dma((peers,)), dma((peers + ndp,)), dma((peers + ndp,))]
    grad_input, sum_wy, sum_wx, gate_all, small_all = call_kernel(
        partial(leave_kernel, nbits, tiled),
        (shape((own_rows, width), F32),)
        + (shape((dp_rows, channels), F32),) * 2
        + (
            shape((ntensor, ndp // 2, 2, gate_rows, unit), BF16),
            shape((ntensor, 8, channels), F32),
        ),
        scratch,
        3,
        d_normed,
        tokens,
        d_middle,
        gain_in,
        own_small,
        d_gain_mid,
        *pieces,
        far_in=(6, 7),
    )
    if merged:
        mixed = found[4]
    else:
        (mixed,) = call_kernel(
            partial(result_kernel, nbits),
            (shape((own_rows, width), BF16),),
            scatter_scratch(own_rows, width, nbits),
            4,
            ffn_part,
            middle,
        )
    found = finish(
        gate_all,
        small_all,
        (sum_wout, sum_wy, sum_wx),
        grad_input,
        mixed,
        sum_both,
        sum_wd,
        taps,
        gate_w.shape,
    )
    sum_gate, sum_wout, sum_wy, sum_wx, grad_input, mixed = found[:6]
    sum_wg, sum_wu, sum_wd, sum_conv, sum_decay, sum_gain_in, sum_gain_mid = found[6:]
    return (
        mixed,
        grad_input,
        sum_gain_in,
        sum_wy,
        sum_wx,
        sum_conv,
        sum_gate,
        sum_decay,
        sum_wout,
        sum_gain_mid,
        sum_wg,
        sum_wu,
        sum_wd,
    )


def solution(mesh):
    split = P(("dp", "tensor"), None)
    weight = P("dp", "tensor")
    return jax.shard_map(
        body,
        mesh=mesh,
        in_specs=(
            split,
            P(("dp", "tensor")),
            split,
            P(),
            weight,
            weight,
            P(),
            P(),
            P(),
            weight,
            P(),
            weight,
            weight,
            weight,
        ),
        out_specs=(
            split,
            split,
            P(),
            weight,
            weight,
            P(),
            P(),
            P(),
            weight,
            P(),
            weight,
            weight,
            weight,
        ),
        check_vma=False,
    )
```

```python
import math
from functools import partial

import jax
import jax.numpy as jnp
from jax import lax
from jax.experimental import pallas as pl
from jax.experimental.pallas import tpu as pltpu
from jax.sharding import PartitionSpec as P

EPSILON = 1e-06
MESH = pl.DeviceIdType.MESH
VMEM_BYTES = 56 * 1024 * 1024
CHUNK = 16
F32 = jnp.float32
BF16 = jnp.bfloat16


def subsets(bits):
    found = [()]
    for bit in bits:
        found = found + [chosen + (bit,) for chosen in found]
    return found


def flipped(index, bits):
    for bit in bits:
        mine = (index // (1 << bit)) % 2
        index = index + (1 - 2 * mine) * (1 << bit)
    return index


def log2_of(count):
    assert count & (count - 1) == 0
    return count.bit_length() - 1


def greet(axis_bits):
    barrier = pltpu.get_barrier_semaphore()
    for axis, bit in axis_bits:
        peer = flipped(lax.axis_index(axis), (bit,))
        pl.semaphore_signal(barrier, inc=1, device_id={axis: peer}, device_id_type=MESH)
    pl.semaphore_wait(barrier, len(axis_bits))


def halves_of(nbits, columns):
    half = columns // 2
    ups = tuple(range(nbits))
    return ((ups, 0, half), (ups[::-1], half, half))


class Gather:
    def __init__(self, ref, rows, nbits, send_sems, recv_sems):
        self.ref, self.rows, self.nbits = ref, rows, nbits
        self.sems = (send_sems, recv_sems)
        self.me = lax.axis_index("tensor")
        self.plan = []
        number = 0
        for half, (order, at, width) in enumerate(halves_of(nbits, ref.shape[1])):
            for step, bit in enumerate(order):
                for known in subsets(order[:step]):
                    self.plan.append((half, step, known, bit, at, width, number))
                    number += 1
        self.count = number

    def copy(self, item):
        half, step, known, bit, at, width, number = item
        row = pl.multiple_of(flipped(self.me, known) * self.rows, self.rows)
        piece = self.ref.at[pl.ds(row, self.rows), pl.ds(at, width)]
        return pltpu.make_async_remote_copy(
            src_ref=piece,
            dst_ref=piece,
            send_sem=self.sems[0].at[number],
            recv_sem=self.sems[1].at[number],
            device_id={"tensor": flipped(self.me, (bit,))},
            device_id_type=MESH,
        )

    def begin(self):
        for item in sorted(self.plan, key=lambda it: it[1]):
            if item[2] == ():
                self.copy(item).start()

    def advance(self, step):
        for item in self.plan:
            half, at_step, known, bit, at, width, number = item
            if at_step == step:
                self.copy(item).wait_recv()
                block = known + (bit,)
                for later in self.plan:
                    if later[0] == half and set(later[2]) == set(block):
                        self.copy(later).start()

    def finish(self, step=0):
        for at_step in range(step, self.nbits):
            self.advance(at_step)
        for item in self.plan:
            self.copy(item).wait_send()


def gather_copies(nbits):
    return 2 * ((1 << nbits) - 1)


class Scatter:
    def __init__(self, ref, landed, staged, rows, nbits, send_sems, recv_sems):
        self.ref, self.landed, self.staged = ref, landed, staged
        self.rows, self.nbits = rows, nbits
        self.sems = (send_sems, recv_sems)
        self.me = lax.axis_index("tensor")
        self.plan, self.slot = [], {}
        number = 0
        for half, (order, at, width) in enumerate(halves_of(nbits, ref.shape[1])):
            for step, bit in enumerate(order):
                for rest in subsets(order[step + 1 :])[::-1]:
                    self.plan.append((half, step, rest, bit, at, width, number))
                    if step > 0:
                        self.slot[number] = len(self.slot)
                    number += 1

    def copy(self, item):
        half, step, rest, bit, at, width, number = item
        if step == 0:
            row = pl.multiple_of(flipped(self.me, rest + (bit,)) * self.rows, self.rows)
            source = self.ref.at[pl.ds(row, self.rows), pl.ds(at, width)]
        else:
            source = self.staged.at[self.slot[number]]
        return pltpu.make_async_remote_copy(
            src_ref=source,
            dst_ref=self.landed.at[number],
            send_sem=self.sems[0].at[number],
            recv_sem=self.sems[1].at[number],
            device_id={"tensor": flipped(self.me, (bit,))},
            device_id_type=MESH,
        )

    def begin(self):
        for item in sorted(self.plan, key=lambda it: (len(it[2]) == 0)):
            if item[1] == 0:
                self.copy(item).start()

    def partial_sum(self, half, block, before, row, size):
        at, width = halves_of(self.nbits, self.ref.shape[1])[half][1:]
        base = pl.multiple_of(flipped(self.me, block) * self.rows + row, size)
        total = self.ref[pl.ds(base, size), pl.ds(at, width)].astype(F32)
        for it in self.plan:
            if it[0] == half and it[1] < before and set(it[2]) == set(block):
                total = total + self.landed[it[6], pl.ds(row, size), :].astype(F32)
        return total

    def advance(self, step):
        for half in range(2):
            for item in self.plan:
                if item[0] == half and item[1] == step:
                    self.copy(item).wait_recv()
            for item in self.plan:
                if item[0] == half and item[1] == step + 1:

                    def fill(row, item=item):
                        value = self.partial_sum(
                            item[0], item[2] + (item[3],), item[1], row, CHUNK
                        )
                        where = (self.slot[item[6]], pl.ds(row, CHUNK))
                        self.staged[where + (slice(None),)] = value.astype(BF16)

                    chunks(self.rows, fill)
                    self.copy(item).start()

    def run(self):
        for step in range(self.nbits):
            self.advance(step)

    def total(self, row, size):
        return jnp.concatenate(
            [self.partial_sum(half, (), self.nbits, row, size) for half in range(2)], axis=1
        )

    def drain(self):
        for item in self.plan:
            self.copy(item).wait_send()


def scatter_scratch(rows, columns, nbits):
    copies = gather_copies(nbits)
    later = max(1, copies - (1 << nbits))
    return [
        pltpu.VMEM((copies, rows, columns // 2), BF16),
        pltpu.VMEM((later, rows, columns // 2), BF16),
        pltpu.SemaphoreType.DMA((copies,)),
        pltpu.SemaphoreType.DMA((copies,)),
    ]


def gather_sems(nbits):
    copies = gather_copies(nbits)
    return [pltpu.SemaphoreType.DMA((copies,)), pltpu.SemaphoreType.DMA((copies,))]


def tensor_bits(nbits):
    return [("tensor", bit) for bit in range(nbits)]


def rms_scale_of(values):
    return lax.rsqrt(jnp.mean(values * values, axis=-1, keepdims=True) + EPSILON)


def chunks(rows, body):
    def step(i, carry):
        body(pl.multiple_of(i * CHUNK, CHUNK))
        return carry

    lax.fori_loop(0, rows // CHUNK, step, 0)


def own_row(row, rows):
    return pl.multiple_of(lax.axis_index("tensor") * rows + row, CHUNK)


def dp_place():
    me = lax.axis_index("dp")
    return me // 2, me % 2, lax.axis_size("dp") // 2


def dp_index(chip, core):
    return chip * 2 + core


UP, DOWN = 1, -1


class LineGather:
    def __init__(self, own, whole, send_sems, recv_sems, columns=None):
        self.own, self.whole = own, whole
        self.sems = (send_sems, recv_sems)
        self.chip, self.core, self.chips = dp_place()
        self.rows = own.shape[0]
        self.columns = slice(None) if columns is None else columns

    def block(self, chip):
        row = pl.multiple_of(dp_index(chip, self.core) * self.rows, self.rows)
        return self.whole.at[pl.ds(row, self.rows), self.columns]

    def has(self, way, distance):
        return self.chip >= distance if way == UP else self.chip + distance < self.chips

    def number(self, way, distance):
        return (0 if way == UP else self.chips) + distance

    def along(self, way, distance):
        block = self.block(self.chip - way * distance)
        return pltpu.make_async_remote_copy(
            src_ref=self.own if distance == 0 else block,
            dst_ref=block,
            send_sem=self.sems[0].at[self.number(way, distance)],
            recv_sem=self.sems[1].at[self.number(way, distance + 1)],
            device_id={"dp": dp_index(self.chip + way, self.core)},
            device_id_type=MESH,
        )

    def arrival(self, way, distance):
        block = self.block(self.chip - way * distance)
        return pltpu.make_async_remote_copy(
            src_ref=block,
            dst_ref=block,
            send_sem=self.sems[0].at[self.number(way, distance)],
            recv_sem=self.sems[1].at[self.number(way, distance)],
            device_id={"dp": dp_index(self.chip + way, self.core)},
            device_id_type=MESH,
        )

    def across(self, way, distance):
        block = self.block(self.chip - way * distance)
        number = 2 * self.chips + self.number(way, distance)
        return pltpu.make_async_remote_copy(
            src_ref=self.own if distance == 0 else block,
            dst_ref=block,
            send_sem=self.sems[0].at[number],
            recv_sem=self.sems[1].at[number],
            device_id={"dp": dp_index(self.chip, 1 - self.core)},
            device_id_type=MESH,
        )

    def local(self):
        return pltpu.make_async_copy(
            self.own, self.block(self.chip), self.sems[0].at[4 * self.chips]
        )

    def begin(self):
        for way in (UP, DOWN):

            @pl.when(self.has(-way, 1))
            def _(way=way):
                self.along(way, 0).start()

        self.across(UP, 0).start()
        self.local().start()

    def pass_on(self, distance):
        for way in (UP, DOWN):

            @pl.when(self.has(way, distance))
            def _(way=way):
                self.arrival(way, distance).wait_recv()

                @pl.when(self.has(-way, 1))
                def _():
                    self.along(way, distance).start()

                self.across(way, distance).start()

    def finish(self):
        self.across(UP, 0).wait()
        self.local().wait()
        for way in (UP, DOWN):
            for distance in range(self.chips):

                @pl.when(self.has(way, distance) & self.has(-way, 1))
                def _(way=way, distance=distance):
                    self.along(way, distance).wait_send()

                if distance:

                    @pl.when(self.has(way, distance))
                    def _(way=way, distance=distance):
                        self.across(way, distance).wait()


def line_sems(ndp):
    chips = ndp // 2
    return [pltpu.SemaphoreType.DMA((4 * chips + 1,)), pltpu.SemaphoreType.DMA((4 * chips + 1,))]


def greet_peers(nbits, all_tensor, whole_dp):
    me = lax.axis_index("tensor")
    chip, core, chips = dp_place()
    barrier = pltpu.get_barrier_semaphore()

    def signal(target):
        pl.semaphore_signal(barrier, inc=1, device_id=target, device_id_type=MESH)

    met = 0
    for chosen in subsets(tuple(range(nbits))):
        if chosen and (all_tensor or len(chosen) == 1):
            signal({"tensor": flipped(me, chosen)})
            met += 1
    if whole_dp:
        for shift in range(chips):
            for turn in range(2):
                if (shift, turn) != (0, 0):
                    other = dp_index((chip + shift) % chips, core + turn * (1 - 2 * core))
                    signal({"dp": other})
                    met += 1
    else:
        signal({"dp": dp_index(chip, 1 - core)})
        met += 1

        for shift in sorted({1 % chips, chips - 1} - {0}):
            signal({"dp": dp_index((chip + shift) % chips, core)})
            met += 1

    pl.semaphore_wait(barrier, met)


def enter_kernel(
    nbits, parts_yx, tokens, seg, gain, *refs
):
    w_yx, w_out = refs[:parts_yx], refs[parts_yx]
    normed_all, seg_all, wyx_all, wout_all, s0, r0, s2, r2, l0, *line = refs[parts_yx + 1 :]
    rows = tokens.shape[0]
    me = lax.axis_index("tensor")
    peers = [chosen for chosen in subsets(tuple(range(nbits))) if chosen]
    greet_peers(nbits, True, False)
    width = wyx_all.shape[1] // parts_yx
    lines = [
        LineGather(
            own,
            wyx_all,
            line[2 * number],
            line[2 * number + 1],
            pl.ds(number * width, width) if parts_yx > 1 else None,
        )
        for number, own in enumerate(w_yx)
    ]
    lines.append(LineGather(w_out, wout_all, *line[2 * parts_yx : 2 * parts_yx + 2]))
    for item in lines:
        item.begin()

    def norm(row):
        values = tokens[pl.ds(row, CHUNK), :].astype(F32)
        scaled = values * rms_scale_of(values) * gain[...]
        normed_all[pl.ds(own_row(row, rows), CHUNK), :] = scaled.astype(BF16)

    chunks(rows, norm)
    gather = Gather(normed_all, rows, nbits, s0, r0)
    gather.begin()
    seg_own = pltpu.make_async_copy(seg, seg_all.at[me], l0.at[0])
    seg_own.start()
    seg_copies = [
        pltpu.make_async_remote_copy(
            src_ref=seg,
            dst_ref=seg_all.at[me],
            send_sem=s2.at[number],
            recv_sem=r2.at[number],
            device_id={"tensor": flipped(me, chosen)},
            device_id_type=MESH,
        )
        for number, chosen in enumerate(peers)
    ]
    for copy in seg_copies:
        copy.start()
    chips = lines[0].chips
    for item in lines:
        item.pass_on(1)
    gather.advance(0)
    for distance in range(2, chips):
        for item in lines:
            item.pass_on(distance)
    gather.finish(1)
    for item in lines:
        item.finish()
    for copy in seg_copies:
        copy.wait()
    seg_own.wait()


class Fetch:
    def __init__(self, nbits, cot, cot_all, s0, r0, l0):
        rows = cot.shape[0]
        own = pl.multiple_of(lax.axis_index("tensor") * rows, rows)
        self.local = pltpu.make_async_copy(cot, cot_all.at[pl.ds(own, rows), :], l0.at[0])
        self.gather = Gather(cot_all, rows, nbits, s0, r0)

    def begin(self):
        self.local.wait()
        self.gather.begin()

    def advance(self):
        self.gather.advance(0)

    def finish(self):
        self.gather.finish(1)


def fetch_scratch(nbits):
    return gather_sems(nbits) + [pltpu.SemaphoreType.DMA((1,))]


def fetch_kernel(nbits, cot, cot_all, *sems):
    greet(tensor_bits(nbits))
    fetch = Fetch(nbits, cot, cot_all, *sems)
    fetch.local.start()
    fetch.begin()
    fetch.advance()
    fetch.finish()


def middle_kernel(
    nbits, mixer, tokens, gain, middle, mid_all, landed, staged, s0, r0, s1, r1
):
    rows = tokens.shape[0]
    greet(tensor_bits(nbits))
    scatter = Scatter(mixer, landed, staged, rows, nbits, s0, r0)
    scatter.begin()
    scatter.run()

    def norm(row):
        values = tokens[pl.ds(row, CHUNK), :].astype(F32) + scatter.total(row, CHUNK)
        middle[pl.ds(row, CHUNK), :] = values
        scaled = values * rms_scale_of(values) * gain[...]
        mid_all[pl.ds(own_row(row, rows), CHUNK), :] = scaled.astype(BF16)

    chunks(rows, norm)
    gather = Gather(mid_all, rows, nbits, s1, r1)
    gather.begin()
    gather.finish()
    scatter.drain()


def result_kernel(nbits, ffn, middle, mixed, landed, staged, s0, r0):
    rows = middle.shape[0]
    greet(tensor_bits(nbits))
    scatter = Scatter(ffn, landed, staged, rows, nbits, s0, r0)
    scatter.begin()
    scatter.run()

    def add(row):
        values = middle[pl.ds(row, CHUNK), :] + scatter.total(row, CHUNK)
        mixed[pl.ds(row, CHUNK), :] = values.astype(BF16)

    chunks(rows, add)
    scatter.drain()


def norm_pull(values, gain, cotangent):
    scale = rms_scale_of(values)
    unit = values * scale
    inner = cotangent * gain
    back = scale * (inner - unit * jnp.mean(inner * unit, axis=-1, keepdims=True))
    return back, cotangent * unit


def eight_rows(values):
    total = values[0:8]
    for at in range(8, CHUNK, 8):
        total = total + values[at : at + 8]
    return total


class Product:
    def __init__(self, left, right, out, held, sems):
        self.left, self.right, self.out = left, right, out
        self.held, self.sems = held, sems
        self.width = held.shape[1]
        self.count = right.shape[0] // self.width
        self.done = 0

    def fetch(self, block):
        return pltpu.make_async_copy(
            self.right.at[pl.ds(block * self.width, self.width), :],
            self.held.at[block % 2],
            self.sems.at[block % 2],
        )

    def begin(self):
        self.fetch(0).start()

    def work(self, blocks):
        for block in range(self.done, min(self.done + blocks, self.count)):
            if block + 1 < self.count:
                self.fetch(block + 1).start()
            self.fetch(block).wait()

            def rows(span, block=block):
                found = times_transposed(self.left[span, :], self.held[block % 2])
                at = slice(block * self.width, (block + 1) * self.width)
                self.out[span, at] = found.astype(BF16)

            parts(self.left.shape[0], rows)
        self.done = min(self.done + blocks, self.count)


PRODUCT_BLOCK = 256


def product_scratch(depth):
    return [pltpu.VMEM((2, PRODUCT_BLOCK, depth), BF16), pltpu.SemaphoreType.DMA((2,))]


def turn_kernel(
    nbits,
    d_norm,
    cot,
    middle,
    gain,
    hidden,
    w_down,
    d_middle,
    d_mixer,
    d_gain,
    ffn,
    landed,
    staged,
    s0,
    r0,
    s1,
    r1,
    *product,
):
    rows = middle.shape[0]
    ahead = Product(hidden, w_down, ffn, *product)
    ahead.begin()
    greet(tensor_bits(nbits))
    scatter = Scatter(d_norm, landed, staged, rows, nbits, s0, r0)
    scatter.begin()
    d_gain[...] = jnp.zeros_like(d_gain)
    ahead.work(4)
    for step in range(nbits):
        scatter.advance(step)
        if step + 1 < nbits:
            ahead.work(2)

    def pull(row):
        span = pl.ds(row, CHUNK)
        back, gains = norm_pull(middle[span, :], gain[...], scatter.total(row, CHUNK))
        values = cot[span, :].astype(F32) + back
        d_middle[span, :] = values
        d_mixer[pl.ds(own_row(row, rows), CHUNK), :] = values.astype(BF16)
        d_gain[...] += eight_rows(gains)

    chunks(rows, pull)
    gather = Gather(d_mixer, rows, nbits, s1, r1)
    gather.begin()
    ahead.work(2)
    gather.advance(0)
    ahead.work(ahead.count)
    gather.finish(1)
    scatter.drain()


class LineSum:
    def __init__(self, whole, kept, swapped, staged, landed, send_sems, recv_sems, columns=None):
        self.whole, self.kept, self.swapped = whole, kept, swapped
        self.staged, self.landed = staged, landed
        self.sems = (send_sems, recv_sems)
        self.columns = columns
        self.chip, self.core, self.chips = dp_place()
        self.rows = whole.shape[2]

    def half(self, core):
        if self.columns is None:
            return self.whole.at[:, core]
        return self.whole.at[:, core, :, self.columns]

    def local(self):
        return pltpu.make_async_copy(
            self.half(self.core), self.kept, self.sems[0].at[2 * self.chips]
        )

    def swap(self):
        return pltpu.make_async_remote_copy(
            src_ref=self.half(1 - self.core),
            dst_ref=self.swapped,
            send_sem=self.sems[0].at[0],
            recv_sem=self.sems[1].at[0],
            device_id={"dp": dp_index(self.chip, 1 - self.core)},
            device_id_type=MESH,
        )

    def has(self, way, distance):
        return self.chip + distance < self.chips if way == UP else self.chip >= distance

    def slot(self, way, distance):
        return (0 if way == UP else self.chips - 1) + distance

    def stage(self, way, distance):
        return distance - 1 if way == UP else self.chips - 1 - distance

    def hop(self, way, distance):
        return pltpu.make_async_remote_copy(
            src_ref=self.staged.at[self.stage(way, distance)],
            dst_ref=self.landed.at[self.slot(way, distance - 1)],
            send_sem=self.sems[0].at[1 + self.slot(way, distance - 1)],
            recv_sem=self.sems[1].at[1 + self.slot(way, distance - 1)],
            device_id={"dp": dp_index(self.chip + way, self.core)},
            device_id_type=MESH,
        )

    def arrival(self, way, distance):
        number = self.slot(way, distance)
        return pltpu.make_async_remote_copy(
            src_ref=self.landed.at[number],
            dst_ref=self.landed.at[number],
            send_sem=self.sems[0].at[1 + number],
            recv_sem=self.sems[1].at[1 + number],
            device_id={"dp": dp_index(self.chip - way, self.core)},
            device_id_type=MESH,
        )

    def begin(self):
        self.swap().start()
        self.local().start()

    def both(self, chip, span):
        return self.kept[chip, span, :].astype(F32) + self.swapped[chip, span, :].astype(F32)

    def send(self, distance):
        if distance == self.chips - 1:
            self.local().wait()
            self.swap().wait_recv()
        for way in (UP, DOWN):

            @pl.when(self.has(way, distance))
            def _(way=way):
                chip = self.chip + way * distance
                slot = self.stage(way, distance)

                def first(row):
                    span = pl.ds(row, CHUNK)
                    self.staged[slot, span, :] = self.both(chip, span).astype(BF16)

                def later(row):
                    span = pl.ds(row, CHUNK)
                    total = self.both(chip, span) + self.landed[
                        self.slot(way, distance), span, :
                    ].astype(F32)
                    self.staged[slot, span, :] = total.astype(BF16)

                if distance == self.chips - 1:
                    chunks(self.rows, first)
                else:

                    @pl.when(self.has(-way, 1))
                    def _():
                        self.arrival(way, distance).wait_recv()
                        chunks(self.rows, later)

                    @pl.when(jnp.logical_not(self.has(-way, 1)))
                    def _():
                        chunks(self.rows, first)

                self.hop(way, distance).start()

    def finish(self, store):
        below, above = self.has(DOWN, 1), self.has(UP, 1)

        def fill(slots):
            for way in slots:
                self.arrival(way, 0).wait_recv()

            def one(row):
                span = pl.ds(row, CHUNK)
                total = self.both(self.chip, span)
                for way in slots:
                    total = total + self.landed[self.slot(way, 0), span, :].astype(F32)
                store(span, total)

            chunks(self.rows, one)

        @pl.when(below & above)
        def _():
            fill((UP, DOWN))

        @pl.when(jnp.logical_not(above))
        def _():
            fill((UP,))

        @pl.when(jnp.logical_not(below))
        def _():
            fill((DOWN,))

    def drain(self):
        self.swap().wait_send()
        for way in (UP, DOWN):
            for distance in range(1, self.chips):

                @pl.when(self.has(way, distance))
                def _(way=way, distance=distance):
                    self.hop(way, distance).wait_send()


def line_scratch(ndp, rows, columns):
    chips = ndp // 2
    return [
        pltpu.VMEM((chips, rows, columns), BF16),
        pltpu.VMEM((chips, rows, columns), BF16),
        pltpu.VMEM((chips - 1, rows, columns), BF16),
        pltpu.VMEM((2 * chips - 2, rows, columns), BF16),
        pltpu.SemaphoreType.DMA((2 * chips + 1,)),
        pltpu.SemaphoreType.DMA((2 * chips + 1,)),
    ]


RING = 6


def leave_kernel(nbits, tiled, with_ffn, *refs):
    refs = list(refs)

    def take(count):
        taken = refs[:count]
        del refs[:count]
        return taken

    d_norm, tokens, d_middle, gain, own_small, d_gain_mid = take(6)
    pieces = take(3)
    ffn, middle = take(2) if with_ffn else (None, None)
    grad_input, sum_out, sum_y, sum_x, gate_all, small_all = take(6)
    mixed = take(1)[0] if with_ffn else None
    landed, staged, s0, r0 = take(4)
    share = small_all.shape[2]
    gate = LineSum(pieces[0], *take(RING))
    lines = [LineSum(pieces[1], *take(RING))]
    if tiled:
        lines += [LineSum(pieces[2], *take(RING), pl.ds(at, share)) for at in (0, share)]
    else:
        lines += [LineSum(pieces[2], *take(RING))]
    d_gain, gains, gains_landed, small, small_landed = take(5)
    gain_s, gain_r, vec_s, vec_r, join_s, join_r, gate_s, gate_r = take(8)
    rows = tokens.shape[0]
    me = lax.axis_index("tensor")
    chip, core, chips = dp_place()
    peers = [chosen for chosen in subsets(tuple(range(nbits))) if chosen]
    others = [(shift, turn) for shift in range(chips) for turn in range(2)][1:]
    greet_peers(nbits, True, True)
    for line in [gate] + lines:
        line.begin()
    scatter = Scatter(d_norm, landed, staged, rows, nbits, s0, r0)
    scatter.begin()
    if with_ffn:
        second = Scatter(ffn, *take(2), rows, nbits, *take(2))
    d_gain[...] = jnp.zeros_like(d_gain)
    far = list(range(chips - 1, 0, -1))
    for number in range(max(len(far), len(lines))):
        if number < len(far):
            gate.send(far[number])
        if number < len(lines):
            lines[number].send(far[0])
    scatter.advance(0)
    if with_ffn:
        second.begin()
    for distance in far[1:-1]:
        for line in lines:
            line.send(distance)
    for step in range(1, nbits):
        scatter.advance(step)

    def pull(row):
        span = pl.ds(row, CHUNK)
        back, parts = norm_pull(
            tokens[span, :].astype(F32), gain[...], scatter.total(row, CHUNK)
        )
        grad_input[span, :] = d_middle[span, :] + back
        d_gain[...] += eight_rows(parts)

    chunks(rows, pull)
    def store_gate(span, value):
        gate_all[me, chip, core, span, :] = value.astype(BF16)

    def gate_copy(number, ref, target):
        return pltpu.make_async_remote_copy(
            src_ref=ref,
            dst_ref=ref,
            send_sem=gate_s.at[number],
            recv_sem=gate_r.at[number],
            device_id=target,
            device_id_type=MESH,
        )

    def gate_line(shift):
        target = {"dp": dp_index((chip + shift) % chips, core)}
        return gate_copy(shift - 1, gate_all.at[me, chip, core], target)

    def gate_tensor(number, chosen):
        target = {"tensor": flipped(me, chosen)}
        return gate_copy(chips - 1 + number, gate_all.at[me, :, core], target)

    def gate_core():
        target = {"dp": dp_index(chip, 1 - core)}
        return gate_copy(chips - 1 + len(peers), gate_all.at[:, :, core], target)

    def start_gate():
        gate.finish(store_gate)
        for shift in range(1, chips):
            gate_line(shift).start()

    top = jnp.sum(d_gain[...], axis=0, keepdims=True)
    low = jnp.sum(d_gain_mid[...], axis=0, keepdims=True)
    place8 = lax.broadcasted_iota(jnp.int32, (8, share), 0)
    for index in range(1 << nbits):
        span = slice(index * share, (index + 1) * share)
        gains[index] = jnp.where(
            place8 == 6, top[:, span], jnp.where(place8 == 7, low[:, span], 0.0)
        )

    def gain_copy(number, chosen):
        peer = flipped(me, chosen)
        return pltpu.make_async_remote_copy(
            src_ref=gains.at[peer],
            dst_ref=gains_landed.at[number],
            send_sem=gain_s.at[number],
            recv_sem=gain_r.at[number],
            device_id={"tensor": peer},
            device_id_type=MESH,
        )

    for number, chosen in enumerate(peers):
        gain_copy(number, chosen).start()
    start_gate()
    if len(far) > 1:
        for line in lines:
            line.send(far[-1])
    total = own_small[...] + gains[me]
    for number, chosen in enumerate(peers):
        gain_copy(number, chosen).wait_recv()
        total = total + gains_landed[number]
    small[...] = total

    def vec_copy(number, shift, turn):
        other = dp_index((chip + shift) % chips, core + turn * (1 - 2 * core))
        return pltpu.make_async_remote_copy(
            src_ref=small,
            dst_ref=small_landed.at[number],
            send_sem=vec_s.at[number],
            recv_sem=vec_r.at[number],
            device_id={"dp": other},
            device_id_type=MESH,
        )

    for number, (shift, turn) in enumerate(others):
        vec_copy(number, shift, turn).start()

    for shift in range(1, chips):
        gate_line(shift).wait_recv()
    for number, chosen in enumerate(peers):
        gate_tensor(number, chosen).start()
    total = small[...]
    for number, (shift, turn) in enumerate(others):
        vec_copy(number, shift, turn).wait_recv()
        total = total + small_landed[number]
    small_all[me] = total

    def join_copy(number, chosen):
        return pltpu.make_async_remote_copy(
            src_ref=small_all.at[me],
            dst_ref=small_all.at[me],
            send_sem=join_s.at[number],
            recv_sem=join_r.at[number],
            device_id={"tensor": flipped(me, chosen)},
            device_id_type=MESH,
        )

    for number, chosen in enumerate(peers):
        join_copy(number, chosen).start()
    if with_ffn:
        second.advance(0)
    for number, chosen in enumerate(peers):
        gate_tensor(number, chosen).wait_recv()
    gate_core().start()
    if with_ffn:
        for step in range(1, nbits):
            second.advance(step)

        def add(row):
            span = pl.ds(row, CHUNK)
            mixed[span, :] = (middle[span, :] + second.total(row, CHUNK)).astype(BF16)

        chunks(rows, add)

    def store_in(*targets):
        def store(span, value):
            for number, ref in enumerate(targets):
                ref[span, :] = value[:, number * share : (number + 1) * share]

        return store

    lines[0].finish(store_in(sum_out))
    if tiled:
        lines[1].finish(store_in(sum_y))
        lines[2].finish(store_in(sum_x))
    else:
        lines[1].finish(store_in(sum_y, sum_x))
    gate_core().wait()
    for shift in range(1, chips):
        gate_line(shift).wait_send()
    for number, chosen in enumerate(peers):
        gate_tensor(number, chosen).wait_send()
        gain_copy(number, chosen).wait_send()
        join_copy(number, chosen).wait()
    for number, (shift, turn) in enumerate(others):
        vec_copy(number, shift, turn).wait_send()
    scatter.drain()
    if with_ffn:
        second.drain()
    for line in [gate] + lines:
        line.drain()


def in_vmem(count):
    return [pl.BlockSpec(memory_space=pltpu.VMEM)] * count


def call_kernel(kernel, outs, scratch, number, *operands, far_in=(), far_out=(), cost_us=1, vmem_bytes=VMEM_BYTES):
    vmem = pl.BlockSpec(memory_space=pltpu.VMEM)
    far = pl.BlockSpec(memory_space=pl.ANY)
    return pl.pallas_call(
        kernel,
        out_shape=outs,
        in_specs=[far if i in far_in else vmem for i in range(len(operands))],
        out_specs=tuple(far if i in far_out else vmem for i in range(len(outs))),
        scratch_shapes=scratch,
        cost_estimate=pl.CostEstimate(
            flops=0, bytes_accessed=cost_us * 1_000_000, transcendentals=0
        ),
        compiler_params=pltpu.CompilerParams(
            collective_id=number, has_side_effects=True, vmem_limit_bytes=vmem_bytes
        ),
    )(*operands)


def sigmoid(values):
    return 1.0 / (1.0 + jnp.exp(-values))


def one_minus_exp(values):
    series = values / 7.0 + 1.0
    for order in (6.0, 5.0, 4.0, 3.0, 2.0):
        series = 1.0 + series * values / order
    return jnp.where(values > -0.3, -values * series, 1.0 - jnp.exp(values))


GELU_K = 0.7978845608028654
GELU_C = 0.044715


def gelu_parts(values):
    square = values * values
    bent = jnp.tanh(GELU_K * values * (1.0 + GELU_C * square))
    gelu = 0.5 * values * (1.0 + bent)
    slope = 0.5 * (1.0 + bent) + 0.5 * values * (1.0 - bent * bent) * GELU_K * (
        1.0 + 3.0 * GELU_C * square
    )
    return gelu, slope


def gate_terms(gate_a, gate_x, soft, since):
    sig_a = sigmoid(gate_a)
    sig_x = sigmoid(gate_x)
    log_decay = -8.0 * sig_a * soft
    decay = jnp.exp(log_decay)
    scale = jnp.sqrt(one_minus_exp(2.0 * log_decay))
    keep = since > 0.5
    return sig_a, sig_x, decay, jnp.where(keep, scale, 1.0), keep


def scan_down(decay, value, carry):
    place = lax.broadcasted_iota(jnp.int32, decay.shape, 0)
    for shift in (1, 2, 4):
        past = place >= shift
        moved = pltpu.roll(value, shift, 0)
        value = jnp.where(past, decay * moved + value, value)
        decay = jnp.where(past, decay * pltpu.roll(decay, shift, 0), decay)
    return decay * carry + value


def scan_up(decay, value, carry):
    place = lax.broadcasted_iota(jnp.int32, decay.shape, 0)
    factor = jnp.where(place < 7, pltpu.roll(decay, 7, 0), 1.0)
    for shift in (1, 2, 4):
        past = place < 8 - shift
        moved = pltpu.roll(value, 8 - shift, 0)
        value = jnp.where(past, factor * moved + value, value)
        factor = jnp.where(past, factor * pltpu.roll(factor, 8 - shift, 0), factor)
    return factor * carry + value


def forward_scan(conv_rows, gates, branch_y, soft, since, mixed, states, between=()):
    total_rows, width = states.shape

    def step(i, carry):
        row = pl.multiple_of(i * CHUNK, CHUNK)
        span = pl.ds(row, CHUNK)
        values = conv_rows(span).astype(F32)
        kept = []
        for at in range(0, CHUNK, 8):
            tile = pl.ds(row + at, 8)
            sig_a, sig_x, decay, scale, keep = gate_terms(
                gates[tile, :width], gates[tile, width:], soft[...], since[tile, :]
            )
            given = values[at : at + 8] * sig_x * scale
            state = scan_down(jnp.where(keep, decay, 0.0), given, carry)
            carry = state[7:8]
            states[tile, :] = state
            kept.append(state * gelu_parts(branch_y[tile, :])[0])
        mixed[span, :] = jnp.concatenate(kept, axis=0).astype(BF16)
        return carry

    steps, stretches = total_rows // CHUNK, len(between) + 1
    carry = jnp.zeros((1, width), F32)
    for stretch in range(stretches):
        first, last = stretch * steps // stretches, (stretch + 1) * steps // stretches
        carry = lax.fori_loop(first, last, step, carry)
        if stretch < len(between):
            between[stretch]()


def forward_scan_kernel(conv, gates, branch_y, soft, since, mixed, states):
    forward_scan(lambda span: conv[span, :], gates, branch_y, soft, since, mixed, states)


def backward_scan(
    d_mixed, conv_rows, gates, branch_y, states, soft, slope_soft, since, d_conv, d_gates, d_branch, d_decay
):
    total_rows, width = states.shape
    d_decay[...] = jnp.zeros_like(d_decay)

    def step(i, carry):
        row = pl.multiple_of(total_rows - CHUNK - i * CHUNK, CHUNK)
        span = pl.ds(row, CHUNK)
        values = conv_rows(span).astype(F32)
        kept = []
        for at in range(CHUNK - 8, -1, -8):
            tile = pl.ds(row + at, 8)
            soft_row = soft[...]
            sig_a, sig_x, decay, scale, keep = gate_terms(
                gates[tile, :width], gates[tile, width:], soft_row, since[tile, :]
            )
            value = values[at : at + 8]
            gelu, slope = gelu_parts(branch_y[tile, :])
            state = states[tile, :]
            upper = d_mixed[tile, :]
            held = jnp.where(keep, decay, 0.0)
            lam = scan_up(held, upper * gelu, carry)
            carry = held[0:1] * lam[0:1]
            d_conv[tile, :] = lam * sig_x * scale
            d_x = lam * value * scale * sig_x * (1.0 - sig_x)
            given = value * sig_x
            d_log = lam * (state - given * scale - given * decay * decay / scale)
            d_log = jnp.where(keep, d_log, 0.0)
            d_a = d_log * (-8.0 * soft_row) * sig_a * (1.0 - sig_a)
            d_decay[...] += d_log * (-8.0 * sig_a) * slope_soft[...]
            kept.append((d_a, d_x, upper * state * slope))
        kept = kept[::-1]
        d_gates[span, :width] = jnp.concatenate([k[0] for k in kept], axis=0).astype(BF16)
        d_gates[span, width:] = jnp.concatenate([k[1] for k in kept], axis=0).astype(BF16)
        d_branch[span, :] = jnp.concatenate([k[2] for k in kept], axis=0).astype(BF16)
        return carry

    lax.fori_loop(0, total_rows // CHUNK, step, jnp.zeros((1, width), F32))


def backward_scan_kernel(
    d_mixed, conv, gates, branch_y, states, soft, slope_soft, since, d_conv, d_gates, d_branch, d_decay
):
    backward_scan(
        d_mixed,
        lambda span: conv[span, :],
        gates,
        branch_y,
        states,
        soft,
        slope_soft,
        since,
        d_conv,
        d_gates,
        d_branch,
        d_decay,
    )


def times_transposed(left, right):
    return lax.dot_general(left, right, (((1,), (1,)), ((), ())), preferred_element_type=F32)


class HalfBlocks:
    def __init__(self, channels, block):
        self.odd = lax.axis_index("tensor") % 2
        self.half = block // 2
        self.block = block
        self.count = channels // block + 1
        self.channels = channels
        self.own = pl.multiple_of(self.odd * self.half, self.half)
        self.shared = (1 - self.odd) * (self.count - 1)
        self.mine_in_block = pl.multiple_of(self.odd * self.half, self.half)
        self.other_in_block = pl.multiple_of((1 - self.odd) * self.half, self.half)
        self.mine = pl.multiple_of((1 - self.odd) * (channels - self.half), self.half)
        self.pair = {"tensor": lax.axis_index("tensor") + 1 - 2 * self.odd}

    def full(self, index):
        block = index + self.odd
        return block, pl.multiple_of(index * self.block + self.odd * self.half, self.half)

    def span(self, block):
        return pl.ds(pl.multiple_of(block * self.block, self.block), self.block)

    def shared_part(self, start):
        return pl.ds(pl.multiple_of(self.shared * self.block + start, self.half), self.half)


PART = 256


def parts(rows, body):
    def step(i, carry):
        body(pl.ds(pl.multiple_of(i * PART, PART), PART))
        return carry

    lax.fori_loop(0, rows // PART, step, 0)


def recurrence_kernel(
    taps,
    nbits,
    branches,
    tap_rows,
    soft,
    since,
    weights,
    cot,
    mixed,
    states,
    window,
    gates,
    cot_all,
    send,
    recv,
    *sems,
):
    total_rows, width = states.shape
    block = weights.shape[2]
    place = HalfBlocks(width, block)
    branch_y, branch_x = branches.at[:, :width], branches.at[:, width:]
    greet(tensor_bits(nbits))
    fetch = Fetch(nbits, cot, cot_all, *sems)
    fetch.local.start()

    def conv(i, before):
        row = pl.multiple_of(i * CHUNK, CHUNK)
        kept = []
        for at in range(0, CHUNK, 8):
            tile = pl.ds(row + at, 8)
            values = branch_x[tile, :]
            line = lax.broadcasted_iota(jnp.int32, values.shape, 0)
            total = values * tap_rows[0:1, :]
            for tap in range(1, taps):
                moved = jnp.where(
                    line < tap, pltpu.roll(before, tap, 0), pltpu.roll(values, tap, 0)
                )
                moved = jnp.where(since[tile, :] > tap - 0.5, moved, 0.0)
                total = total + moved * tap_rows[tap : tap + 1, :]
            kept.append(total)
            before = values
        window[pl.ds(row, CHUNK), pl.ds(place.own, width)] = jnp.concatenate(
            kept, axis=0
        ).astype(BF16)
        return before

    lax.fori_loop(0, total_rows // CHUNK, conv, jnp.zeros((8, width), F32))
    source = window.at[:, place.shared_part(place.mine_in_block)]
    away = pl.multiple_of(place.odd * (place.count - 1) * block + place.mine_in_block, place.half)
    rim = pltpu.make_async_remote_copy(
        src_ref=source,
        dst_ref=window.at[:, pl.ds(away, place.half)],
        send_sem=send.at[0],
        recv_sem=recv.at[0],
        device_id=place.pair,
        device_id_type=MESH,
    )
    rim.start()
    fetch.begin()

    def full(span):
        for index in range(place.count - 1):
            number, at = place.full(index)
            cells = window[span, place.span(number)]
            for s in range(2):
                gates[span, pl.ds(s * width + at, block)] = jnp.dot(
                    cells, weights[s, number], preferred_element_type=F32
                )

    parts(total_rows, full)
    rim.wait()

    def shared(span):
        cells = window[span, place.span(place.shared)]
        for s in range(2):
            gates[span, pl.ds(s * width + place.mine, place.half)] = jnp.dot(
                cells,
                weights[s, place.shared, :, pl.ds(place.mine_in_block, place.half)],
                preferred_element_type=F32,
            )

    parts(total_rows, shared)
    forward_scan(
        lambda span: window[span, pl.ds(place.own, width)],
        gates,
        branch_y,
        soft,
        since,
        mixed,
        states,
        [fetch.advance],
    )
    fetch.finish()


def recurrence_back_kernel(
    taps,
    d_mixed,
    window,
    gates,
    branches,
    states,
    tap_rows,
    soft,
    slope_soft,
    since,
    weights,
    d_branches,
    gate_grad,
    own_small,
    d_conv,
    d_gates,
    given,
    taken,
    sums,
    send,
    recv,
):
    total_rows, width = states.shape
    block = weights.shape[2]
    place = HalfBlocks(width, block)
    half = place.half
    branch_y, branch_x = branches.at[:, :width], branches.at[:, width:]
    d_branch_y, d_branch_x = d_branches.at[:, :width], d_branches.at[:, width:]
    greet([("tensor", 0)])
    backward_scan(
        d_mixed,
        lambda span: window[span, pl.ds(place.own, width)],
        gates,
        branch_y,
        states,
        soft,
        slope_soft,
        since,
        d_conv,
        d_gates,
        d_branch_y,
        sums.at[taps],
    )

    def to_pair(span):
        total = jnp.zeros((PART, half), F32)
        for s in range(2):
            total = total + times_transposed(
                d_gates[span, pl.ds(s * width + place.mine, half)],
                weights[
                    s,
                    place.shared,
                    pl.ds(place.other_in_block, half),
                    pl.ds(place.mine_in_block, half),
                ],
            )
        given[span, :] = total.astype(BF16)

    parts(total_rows, to_pair)
    rim = pltpu.make_async_remote_copy(
        src_ref=given,
        dst_ref=taken,
        send_sem=send.at[0],
        recv_sem=recv.at[0],
        device_id=place.pair,
        device_id_type=MESH,
    )
    rim.start()

    def full(span):
        for index in range(place.count - 1):
            number, at = place.full(index)
            total = d_conv[span, pl.ds(at, block)]
            for s in range(2):
                total = total + times_transposed(
                    d_gates[span, pl.ds(s * width + at, block)], weights[s, number]
                )
            d_conv[span, pl.ds(at, block)] = total
        total = d_conv[span, pl.ds(place.mine, half)]
        for s in range(2):
            total = total + times_transposed(
                d_gates[span, pl.ds(s * width + place.mine, half)],
                weights[
                    s,
                    place.shared,
                    pl.ds(place.mine_in_block, half),
                    pl.ds(place.mine_in_block, half),
                ],
            )
        d_conv[span, pl.ds(place.mine, half)] = total

    parts(total_rows, full)
    units = width // half
    for index in range(units):
        number = (index + place.odd) // 2
        cells = window[:, place.span(number)]
        both = jnp.concatenate(
            [d_gates[:, s * width + index * half : s * width + (index + 1) * half] for s in range(2)],
            axis=1,
        )
        found = lax.dot_general(
            cells, both, (((0,), (0,)), ((), ())), preferred_element_type=F32
        ).astype(BF16)
        gate_grad[2 * index] = found[:, :half]
        gate_grad[2 * index + 1] = found[:, half:]
    rim.wait()

    def add(span):
        d_conv[span, pl.ds(place.mine, half)] += taken[span, :].astype(F32)

    parts(total_rows, add)
    for tap in range(taps):
        sums[tap] = jnp.zeros((8, width), F32)

    def conv(i, after):
        row = pl.multiple_of(total_rows - CHUNK - i * CHUNK, CHUNK)
        kept = []
        for at in range(CHUNK - 8, -1, -8):
            tile = pl.ds(row + at, 8)
            values = d_conv[tile, :]
            line = lax.broadcasted_iota(jnp.int32, values.shape, 0)
            below = branch_x[tile, :]
            higher = pl.multiple_of((row + at - 8 + total_rows) % total_rows, 8)
            above = branch_x[pl.ds(higher, 8), :]
            total = values * tap_rows[0:1, :]
            sums[0] += values * below
            masked = []
            for tap in range(1, taps):
                here = jnp.where(since[tile, :] > tap - 0.5, values, 0.0)
                masked.append(here)
                moved = jnp.where(
                    line < 8 - tap,
                    pltpu.roll(here, 8 - tap, 0),
                    pltpu.roll(after[tap - 1], 8 - tap, 0),
                )
                total = total + moved * tap_rows[tap : tap + 1, :]
                source = jnp.where(
                    line < tap, pltpu.roll(above, tap, 0), pltpu.roll(below, tap, 0)
                )
                sums[tap] += here * source
            after = tuple(masked)
            kept.append(total)
        d_branch_x[pl.ds(row, CHUNK), :] = jnp.concatenate(kept[::-1], axis=0).astype(BF16)
        return after

    none = jnp.zeros((8, width), F32)
    lax.fori_loop(0, total_rows // CHUNK, conv, (none,) * (taps - 1))
    line = lax.broadcasted_iota(jnp.int32, (8, width), 0)
    total = jnp.zeros((8, width), F32)
    for tap in range(taps + 1):
        row = jnp.sum(sums[tap], axis=0, keepdims=True)
        total = jnp.where(line == tap, row, total)
    own_small[...] = total


def finish_kernel(
    taps,
    gates,
    small,
    in_out,
    in_y,
    in_x,
    in_grad,
    in_mixed,
    in_both,
    in_down,
    whole,
    out_out,
    out_y,
    out_x,
    out_grad,
    out_mixed,
    out_gate,
    out_up,
    out_down,
    conv,
    decay,
    gain_in,
    gain_mid,
):
    for piece in range(gates.shape[0]):
        for s in range(2):
            whole[s, 0, :, piece * 128 : (piece + 1) * 128] = gates[piece, s].astype(F32)
    out_out[...] = in_out[...]
    out_y[...] = in_y[...]
    out_x[...] = in_x[...]
    out_grad[...] = in_grad[...]
    out_mixed[...] = in_mixed[...]
    units = out_gate.shape[1]
    out_gate[...] = in_both[:, :units].astype(F32)
    out_up[...] = in_both[:, units:].astype(F32)
    out_down[...] = in_down[...].astype(F32)

    @pl.when(pl.program_id(0) == 0)
    def _():
        share = small.shape[2]
        for index in range(small.shape[0]):
            span = slice(index * share, (index + 1) * share)
            conv[:, span] = small[index, :taps, :]
            for at in range(0, share, 128):
                row = (index * share + at) // 128
                decay[row : row + 1, :] = small[index, taps : taps + 1, at : at + 128]
                gain_in[row : row + 1, :] = small[index, 6:7, at : at + 128]
                gain_mid[row : row + 1, :] = small[index, 7:8, at : at + 128]


def finish(gate_all, small_all, sums, grad_input, mixed, both, down, taps, gate_shape):
    _, blocks, block, _ = gate_shape
    unit = gate_all.shape[-1]
    pieces = block // unit
    width = small_all.shape[0] * small_all.shape[2]
    rows, units = down.shape
    own_rows = grad_input.shape[0]
    steps, held = rows // blocks, own_rows // 8
    if unit != 128 or rows % (16 * blocks) or own_rows % 128:
        whole = gate_all.reshape(blocks, pieces, 2, block, unit).transpose(2, 0, 3, 1, 4)
        summed = small_all.transpose(1, 0, 2).reshape(8, width)
        whole = whole.reshape(gate_shape).astype(F32)
        wide = tuple(one.astype(F32) for one in (both[:, :units], both[:, units:], down))
        last = (summed[:taps], summed[taps], summed[6], summed[7])
        return (whole, *sums, grad_input, mixed, *wide, *last)
    shape = jax.ShapeDtypeStruct

    def by_rows(count, columns):
        return pl.BlockSpec((count, columns), lambda n: (n, 0))

    def by_held(columns):
        return pl.BlockSpec((held, columns), lambda n: (jnp.minimum(n, 7), 0))

    def whole_array(*dims):
        return pl.BlockSpec(dims, lambda n: (0,) * len(dims))

    columns = sums[0].shape[1]
    d_width = grad_input.shape[1]
    lines = width // 128
    found = pl.pallas_call(
        partial(finish_kernel, taps),
        grid=(blocks,),
        in_specs=[
            pl.BlockSpec((pieces, 2, block, unit), lambda n: (n, 0, 0, 0)),
            whole_array(*small_all.shape),
        ]
        + [by_rows(steps, columns)] * 3
        + [by_held(d_width)] * 2
        + [by_rows(steps, 2 * units), by_rows(steps, units)],
        out_specs=(
            (pl.BlockSpec((2, 1, block, block), lambda n: (0, n, 0, 0)),)
            + (by_rows(steps, columns),) * 3
            + (by_held(d_width),) * 2
            + (by_rows(steps, units),) * 3
            + (whole_array(taps, width),)
            + (whole_array(lines, 128),) * 3
        ),
        out_shape=(
            (shape(gate_shape, F32),)
            + (shape((rows, columns), F32),) * 3
            + (shape(grad_input.shape, F32), shape(mixed.shape, BF16))
            + (shape((rows, units), F32),) * 3
            + (shape((taps, width), F32),)
            + (shape((lines, 128), F32),) * 3
        ),
        compiler_params=pltpu.CompilerParams(vmem_limit_bytes=VMEM_BYTES),
    )(
        gate_all.reshape(blocks * pieces, 2, block, unit),
        small_all,
        *sums,
        grad_input,
        mixed,
        both,
        down,
    )
    return found[:10] + tuple(one.reshape(width) for one in found[10:])


def scan_call(kernel, outs, *operands):
    return pl.pallas_call(
        kernel,
        out_shape=outs,
        in_specs=in_vmem(len(operands)),
        out_specs=tuple(in_vmem(len(outs))),
        compiler_params=pltpu.CompilerParams(vmem_limit_bytes=VMEM_BYTES),
    )(*operands)


class Rim:
    def __init__(self, route, back, source, first, width, room):
        self.route, self.back = route, back
        self.source, self.first, self.width = source, first, width
        self.room = room

    def fetch(self, values):
        part = lax.dynamic_slice_in_dim(values, self.source, self.width, 1)
        return lax.ppermute(part, "tensor", self.route)

    def give(self, part):
        return lax.ppermute(part, "tensor", self.back)

    def add(self, values, part):
        zeros = jnp.zeros(values.shape, F32)
        return values + lax.dynamic_update_slice_in_dim(
            zeros, part.astype(F32), self.source, 1
        )

    def window(self, channels):
        return (channels // self.width + 4) * self.width


def gate_rims(channels, block_size, ntensor, offset):
    up = [(i, i + 1) for i in range(ntensor - 1)]
    down = [(i + 1, i) for i in range(ntensor - 1)]
    last = jnp.int32(channels - block_size)
    return [
        Rim(up, down, last, offset - block_size, block_size, block_size),
        Rim(down, up, jnp.int32(0), offset + channels, block_size, block_size),
    ]


def same_block(first, count, offset, channels, block_size):
    rows = (first + jnp.arange(count, dtype=jnp.int32))[:, None]
    columns = (offset + jnp.arange(channels, dtype=jnp.int32))[None, :]
    return (rows + block_size) // block_size == (columns + block_size) // block_size


def gate_dense(gate_w, offset, first, count):
    block_size = gate_w.shape[2]
    total = gate_w.shape[1] * block_size
    channels = total // lax.axis_size("tensor")
    columns = gate_w.transpose(2, 0, 1, 3).reshape(block_size, 2, total)
    columns = lax.dynamic_slice_in_dim(columns, offset, channels, 2)
    copies = -(-count // block_size) + 1
    tall = jnp.concatenate([columns] * copies, axis=0)
    tall = lax.dynamic_slice_in_dim(tall, (first + block_size) % block_size, count, 0)
    same = same_block(first, count, offset, channels, block_size)
    dense = jnp.where(same[:, None, :], tall, jnp.zeros_like(tall))
    return dense.reshape(count, 2 * channels)


def doc_starts(seg_ids, seq_len):
    places = jnp.arange(seg_ids.shape[0], dtype=jnp.int32)
    before = jnp.concatenate([seg_ids[:1], seg_ids[:-1]])
    resets = (places % seq_len == 0) | (seg_ids != before)
    starts = lax.cummax(jnp.where(resets, places, jnp.zeros_like(places)), axis=0)
    return starts


def causal_conv(starts, values, kernel):
    places = jnp.arange(values.shape[0], dtype=jnp.int32)
    total = values * kernel[0]
    for offset_k in range(1, kernel.shape[0]):
        moved = jnp.concatenate(
            [jnp.zeros((offset_k, values.shape[1]), values.dtype), values[:-offset_k]], axis=0
        )
        valid = (places - offset_k >= starts)[:, None]
        total = total + jnp.where(valid, moved, jnp.zeros_like(moved)) * kernel[offset_k]
    return total


def geglu(gate_val, up_val):
    return jax.nn.gelu(gate_val, approximate=True) * up_val


def rows_times(left, right):
    return lax.dot_general(left, right, (((1,), (1,)), ((), ())), preferred_element_type=F32)


def rows_back(lefts, rights):
    total = rows_times(lefts[0], rights[0])
    return total + rows_times(lefts[1], rights[1])


def inner_rows(left, right):
    return lax.dot_general(left, right, (((0,), (0,)), ((), ())), preferred_element_type=F32)


def halved(grad, ndp):
    return grad.reshape(ndp // 2, 2, grad.shape[0] // ndp, grad.shape[1])


def body(
    tokens,
    segments,
    cotangent,
    norm_gain,
    w_y,
    w_x,
    conv_w,
    gate_w,
    decay_param,
    w_out,
    mlp_gain,
    w_gate,
    w_up,
    w_down,
):
    ntensor = lax.axis_size("tensor")
    ndp = lax.axis_size("dp")
    nbits = log2_of(ntensor)
    tindex = lax.axis_index("tensor")
    own_rows, width = tokens.shape
    group_rows = own_rows * ntensor
    block_size = gate_w.shape[2]
    nblocks = gate_w.shape[1]
    dp_rows, channels = w_y.shape
    taps = conv_w.shape[0]
    offset = tindex * channels
    shape = jax.ShapeDtypeStruct
    gain_in = norm_gain.reshape(1, width)
    gain_mid = mlp_gain.reshape(1, width)
    seg_rows_of = own_rows // 128
    tiled = channels % 128 == 0
    w_yx = (w_y, w_x) if tiled else (jnp.concatenate([w_y, w_x], axis=1),)
    normed_rows, seg_all, wyx_loc, wout_loc = call_kernel(
        partial(enter_kernel, nbits, len(w_yx)),
        (
            shape((group_rows, width), BF16),
            shape((ntensor, seg_rows_of, 128), jnp.int32),
            shape((dp_rows * ndp, 2 * channels), BF16),
            shape((dp_rows * ndp, channels), BF16),
        ),
        gather_sems(nbits)
        + [pltpu.SemaphoreType.DMA((ntensor - 1,)), pltpu.SemaphoreType.DMA((ntensor - 1,))]
        + [pltpu.SemaphoreType.DMA((1,))]
        + line_sems(ndp) * (len(w_yx) + 1),
        0,
        tokens,
        segments.reshape(seg_rows_of, 128),
        gain_in,
        *w_yx,
        w_out,
        far_in=tuple(range(3, 4 + len(w_yx))),
        far_out=(2, 3),
    )
    units = w_gate.shape[1]
    w_both = jnp.concatenate([w_gate, w_up], axis=1)
    w_both, w_down, normed_rows = lax.optimization_barrier((w_both, w_down, normed_rows))
    both_loc = lax.all_gather(w_both, "dp", axis=0, tiled=True)
    wd_loc = lax.all_gather(w_down, "dp", axis=0, tiled=True)
    seg_rows = seg_all.reshape(group_rows)
    starts = doc_starts(seg_rows, group_rows)
    conv_loc = lax.dynamic_slice_in_dim(conv_w, offset, channels, 1)
    decay_loc = lax.dynamic_slice_in_dim(decay_param, offset, channels, 0).reshape(1, channels)
    soft = jax.nn.softplus(decay_loc)
    slope_soft = jax.nn.sigmoid(decay_loc)
    half_blocks = (
        channels % block_size == block_size // 2 and ntensor % 2 == 0 and block_size % 256 == 0
    )
    since = (jnp.arange(group_rows, dtype=jnp.int32) - starts).astype(F32)[:, None]
    branches = jnp.dot(normed_rows, wyx_loc, preferred_element_type=F32)
    if half_blocks:
        span_blocks = channels // block_size + 1
        w_window = lax.dynamic_slice_in_dim(gate_w, offset // block_size, span_blocks, 1)
        taps_pad = jnp.concatenate([conv_loc, jnp.zeros((8 - taps, channels), F32)], axis=0)
        mixed_low, states, window, gate_pre, cot_rows = call_kernel(
            partial(recurrence_kernel, taps, nbits),
            (
                shape((group_rows, channels), BF16),
                shape((group_rows, channels), F32),
                shape((group_rows, span_blocks * block_size), BF16),
                shape((group_rows, 2 * channels), F32),
                shape((group_rows, width), BF16),
            ),
            [pltpu.SemaphoreType.DMA((1,)), pltpu.SemaphoreType.DMA((1,))]
            + fetch_scratch(nbits),
            5,
            branches,
            taps_pad,
            soft,
            since,
            w_window,
            cotangent,
        )
    else:
        branch_y, branch_x = branches[:, :channels], branches[:, channels:]
        (cot_rows,) = call_kernel(
            partial(fetch_kernel, nbits),
            (shape((group_rows, width), BF16),),
            fetch_scratch(nbits),
            5,
            cotangent,
        )
        rims = gate_rims(channels, block_size, ntensor, offset)
        own_dense = gate_dense(gate_w, offset, offset, channels)
        rim_dense = [gate_dense(gate_w, offset, rim.first, rim.width) for rim in rims]
        conv_out, conv_pull = jax.vjp(partial(causal_conv, starts), branch_x, conv_loc)
        conv_low = conv_out.astype(BF16)
        rim_cells = [rim.fetch(conv_low) for rim in rims]
        gate_pre = jnp.dot(conv_low, own_dense, preferred_element_type=F32)
        for cells, dense in zip(rim_cells, rim_dense):
            gate_pre = gate_pre + jnp.dot(cells, dense, preferred_element_type=F32)
        mixed_low, states = scan_call(
            forward_scan_kernel,
            (shape((group_rows, channels), BF16), shape((group_rows, channels), F32)),
            conv_low,
            gate_pre,
            branch_y,
            soft,
            since,
        )
    middle, mid_rows = call_kernel(
        partial(middle_kernel, nbits),
        (shape((own_rows, width), F32), shape((group_rows, width), BF16)),
        scatter_scratch(own_rows, width, nbits) + gather_sems(nbits),
        1,
        rows_times(mixed_low, wout_loc).astype(BF16),
        tokens,
        gain_mid,
    )
    pre = jnp.dot(mid_rows, both_loc, preferred_element_type=F32)
    hidden, act_pull = jax.vjp(geglu, pre[:, :units], pre[:, units:])
    hidden_low = hidden.astype(BF16)
    grad_wd = inner_rows(cot_rows, hidden_low).astype(BF16)
    sum_wd = lax.psum_scatter(grad_wd, "dp", scatter_dimension=0, tiled=True)
    grad_wd, wd_loc = lax.optimization_barrier((grad_wd, wd_loc))
    d_hidden = jnp.dot(cot_rows, wd_loc, preferred_element_type=F32)
    d_gate, d_up = act_pull(d_hidden)
    d_pre = jnp.concatenate([d_gate.astype(BF16), d_up.astype(BF16)], axis=1)
    grad_both = inner_rows(mid_rows, d_pre).astype(BF16)
    sum_both = lax.psum_scatter(grad_both, "dp", scatter_dimension=0, tiled=True)
    d_pre, grad_both = lax.optimization_barrier((d_pre, grad_both))
    d_mid_part = rows_times(d_pre, both_loc).astype(BF16)
    d_middle, d_mixer, d_gain_mid, ffn_part = call_kernel(
        partial(turn_kernel, nbits),
        (
            shape((own_rows, width), F32),
            shape((group_rows, width), BF16),
            shape((8, width), F32),
            shape((group_rows, width), BF16),
        ),
        scatter_scratch(own_rows, width, nbits) + gather_sems(nbits) + product_scratch(units),
        2,
        d_mid_part,
        cotangent,
        middle,
        gain_mid,
        hidden_low,
        wd_loc,
        far_in=(5,),
    )
    d_mixer, sum_wd = lax.optimization_barrier((d_mixer, sum_wd))
    grad_wout = inner_rows(d_mixer, mixed_low).astype(BF16)
    d_mixed_in = jnp.dot(d_mixer, wout_loc, preferred_element_type=F32)
    unit = math.gcd(channels, block_size)
    merged = nbits <= 2
    if half_blocks:
        d_branches, gate_grad, own_small = call_kernel(
            partial(recurrence_back_kernel, taps),
            (
                shape((group_rows, 2 * channels), BF16),
                shape((channels // unit * 2, block_size, unit), BF16),
                shape((8, channels), F32),
            ),
            [
                pltpu.VMEM((group_rows, channels), F32),
                pltpu.VMEM((group_rows, 2 * channels), BF16),
                pltpu.VMEM((group_rows, unit), BF16),
                pltpu.VMEM((group_rows, unit), BF16),
                pltpu.VMEM((taps + 1, 8, channels), F32),
                pltpu.SemaphoreType.DMA((1,)),
                pltpu.SemaphoreType.DMA((1,)),
            ],
            6,
            d_mixed_in,
            window,
            gate_pre,
            branches,
            states,
            taps_pad,
            soft,
            slope_soft,
            since,
            w_window,
        )
        gate_grad = gate_grad.reshape(channels // unit * 2 * block_size, unit)
    else:
        d_conv, d_gate_low, d_branch_y, d_decay = scan_call(
            backward_scan_kernel,
            (
                shape((group_rows, channels), F32),
                shape((group_rows, 2 * channels), BF16),
                shape((group_rows, channels), BF16),
                shape((8, channels), F32),
            ),
            d_mixed_in,
            conv_low,
            gate_pre,
            branch_y,
            states,
            soft,
            slope_soft,
            since,
        )
        given = [rows_times(d_gate_low, dense).astype(BF16) for dense in rim_dense]
        taken = [rim.give(part) for rim, part in zip(rims, given)]
        d_conv_out = d_conv + rows_times(d_gate_low, own_dense)
        for rim, part in zip(rims, taken):
            d_conv_out = rim.add(d_conv_out, part)
        d_branch_x, grad_conv_loc = conv_pull(d_conv_out)
        d_branches = jnp.concatenate([d_branch_y, d_branch_x.astype(BF16)], axis=1)
        base = offset // block_size * block_size - rims[0].room
        window_rows = rims[0].window(channels)
        picked = jnp.zeros((window_rows, 2 * channels), F32)
        for first, cells in [(offset, conv_low)] + [(r.first, c) for r, c in zip(rims, rim_cells)]:
            part = inner_rows(cells, d_gate_low)
            same = same_block(first, cells.shape[1], offset, channels, block_size)
            part = jnp.where(jnp.concatenate([same, same], axis=1), part, 0.0)
            picked = lax.dynamic_update_slice(picked, part, (first - base, jnp.int32(0)))
        picked = picked.reshape(window_rows // block_size, block_size, 2, channels // unit, unit)
        gate_grad = picked.sum(axis=0).astype(BF16).transpose(2, 1, 0, 3)
        gate_grad = gate_grad.reshape(channels // unit * 2 * block_size, unit)
        own_small = jnp.concatenate(
            [
                grad_conv_loc,
                jnp.sum(d_decay, axis=0, keepdims=True),
                jnp.zeros((7 - taps, channels), F32),
            ],
            axis=0,
        )

    grad_wyx = inner_rows(normed_rows, d_branches).astype(BF16)
    d_normed = rows_times(d_branches, wyx_loc).astype(BF16)

    pieces = [halved(grad, ndp) for grad in (gate_grad, grad_wout, grad_wyx)]
    peers = ntensor - 1
    gate_rows = gate_grad.shape[0] // ndp
    dma = pltpu.SemaphoreType.DMA
    scratch = scatter_scratch(own_rows, width, nbits)
    scratch += line_scratch(ndp, gate_rows, unit) + line_scratch(ndp, dp_rows, channels)
    if tiled:
        scratch += line_scratch(ndp, dp_rows, channels) * 2
    else:
        scratch += line_scratch(ndp, dp_rows, 2 * channels)
    scratch += [
        pltpu.VMEM((8, width), F32),
        pltpu.VMEM((ntensor, 8, channels), F32),
        pltpu.VMEM((peers, 8, channels), F32),
        pltpu.VMEM((8, channels), F32),
        pltpu.VMEM((ndp - 1, 8, channels), F32),
    ]
    scratch += [dma((peers,)), dma((peers,)), dma((ndp - 1,)), dma((ndp - 1,))]
    scratch += [dma((peers,)), dma((peers,)), dma((peers + ndp,)), dma((peers + ndp,))]
    if merged:
        scratch += scatter_scratch(own_rows, width, nbits)
    found = call_kernel(
        partial(leave_kernel, nbits, tiled, merged),
        (shape((own_rows, width), F32),)
        + (shape((dp_rows, channels), F32),) * 3
        + (
            shape((ntensor, ndp // 2, 2, gate_rows, unit), BF16),
            shape((ntensor, 8, channels), F32),
        )
        + ((shape((own_rows, width), BF16),) if merged else ()),
        scratch,
        3,
        d_normed,
        tokens,
        d_middle,
        gain_in,
        own_small,
        d_gain_mid,
        *pieces,
        *((ffn_part, middle) if merged else ()),
        far_in=(6, 7, 8),
        vmem_bytes=60 * 1024 * 1024,
    )
    grad_input, sum_wout, sum_wy, sum_wx, gate_all, small_all = found[:6]
    if merged:
        mixed = found[6]
    else:
        (mixed,) = call_kernel(
            partial(result_kernel, nbits),
            (shape((own_rows, width), BF16),),
            scatter_scratch(own_rows, width, nbits),
            4,
            ffn_part,
            middle,
        )
    gate_all, sum_both = lax.optimization_barrier((gate_all, sum_both))
    found = finish(
        gate_all,
        small_all,
        (sum_wout, sum_wy, sum_wx),
        grad_input,
        mixed,
        sum_both,
        sum_wd,
        taps,
        gate_w.shape,
    )
    sum_gate, sum_wout, sum_wy, sum_wx, grad_input, mixed = found[:6]
    sum_wg, sum_wu, sum_wd, sum_conv, sum_decay, sum_gain_in, sum_gain_mid = found[6:]
    return (
        mixed,
        grad_input,
        sum_gain_in,
        sum_wy,
        sum_wx,
        sum_conv,
        sum_gate,
        sum_decay,
        sum_wout,
        sum_gain_mid,
        sum_wg,
        sum_wu,
        sum_wd,
    )


def solution(mesh):
    split = P(("dp", "tensor"), None)
    weight = P("dp", "tensor")
    return jax.shard_map(
        body,
        mesh=mesh,
        in_specs=(
            split,
            P(("dp", "tensor")),
            split,
            P(),
            weight,
            weight,
            P(),
            P(),
            P(),
            weight,
            P(),
            weight,
            weight,
            weight,
        ),
        out_specs=(
            split,
            split,
            P(),
            weight,
            weight,
            P(),
            P(),
            P(),
            weight,
            P(),
            weight,
            weight,
            weight,
        ),
        check_vma=False,
    )
```

```python
import math
from functools import partial

import jax
import jax.numpy as jnp
from jax import lax
from jax.experimental import pallas as pl
from jax.experimental.pallas import tpu as pltpu
from jax.sharding import PartitionSpec as P

EPSILON = 1e-06
MESH = pl.DeviceIdType.MESH
VMEM_BYTES = 56 * 1024 * 1024
CHUNK = 16
F32 = jnp.float32
BF16 = jnp.bfloat16


def subsets(bits):
    found = [()]
    for bit in bits:
        found = found + [chosen + (bit,) for chosen in found]
    return found


def flipped(index, bits):
    for bit in bits:
        mine = (index // (1 << bit)) % 2
        index = index + (1 - 2 * mine) * (1 << bit)
    return index


def log2_of(count):
    assert count & (count - 1) == 0
    return count.bit_length() - 1


def greet(axis_bits):
    barrier = pltpu.get_barrier_semaphore()
    for axis, bit in axis_bits:
        peer = flipped(lax.axis_index(axis), (bit,))
        pl.semaphore_signal(barrier, inc=1, device_id={axis: peer}, device_id_type=MESH)
    pl.semaphore_wait(barrier, len(axis_bits))


def halves_of(nbits, columns):
    half = columns // 2
    ups = tuple(range(nbits))
    return ((ups, 0, half), (ups[::-1], half, half))


class Gather:
    def __init__(self, ref, rows, nbits, send_sems, recv_sems):
        self.ref, self.rows, self.nbits = ref, rows, nbits
        self.sems = (send_sems, recv_sems)
        self.me = lax.axis_index("tensor")
        self.plan = []
        number = 0
        for half, (order, at, width) in enumerate(halves_of(nbits, ref.shape[1])):
            for step, bit in enumerate(order):
                for known in subsets(order[:step]):
                    self.plan.append((half, step, known, bit, at, width, number))
                    number += 1
        self.count = number

    def copy(self, item):
        half, step, known, bit, at, width, number = item
        row = pl.multiple_of(flipped(self.me, known) * self.rows, self.rows)
        piece = self.ref.at[pl.ds(row, self.rows), pl.ds(at, width)]
        return pltpu.make_async_remote_copy(
            src_ref=piece,
            dst_ref=piece,
            send_sem=self.sems[0].at[number],
            recv_sem=self.sems[1].at[number],
            device_id={"tensor": flipped(self.me, (bit,))},
            device_id_type=MESH,
        )

    def begin(self):
        for item in sorted(self.plan, key=lambda it: it[1]):
            if item[2] == ():
                self.copy(item).start()

    def advance(self, step):
        for item in self.plan:
            half, at_step, known, bit, at, width, number = item
            if at_step == step:
                self.copy(item).wait_recv()
                block = known + (bit,)
                for later in self.plan:
                    if later[0] == half and set(later[2]) == set(block):
                        self.copy(later).start()

    def finish(self, step=0):
        for at_step in range(step, self.nbits):
            self.advance(at_step)
        for item in self.plan:
            self.copy(item).wait_send()


def gather_copies(nbits):
    return 2 * ((1 << nbits) - 1)


class Scatter:
    def __init__(self, ref, landed, staged, rows, nbits, send_sems, recv_sems):
        self.ref, self.landed, self.staged = ref, landed, staged
        self.rows, self.nbits = rows, nbits
        self.sems = (send_sems, recv_sems)
        self.me = lax.axis_index("tensor")
        self.plan, self.slot = [], {}
        number = 0
        for half, (order, at, width) in enumerate(halves_of(nbits, ref.shape[1])):
            for step, bit in enumerate(order):
                for rest in subsets(order[step + 1 :])[::-1]:
                    self.plan.append((half, step, rest, bit, at, width, number))
                    if step > 0:
                        self.slot[number] = len(self.slot)
                    number += 1

    def copy(self, item):
        half, step, rest, bit, at, width, number = item
        if step == 0:
            row = pl.multiple_of(flipped(self.me, rest + (bit,)) * self.rows, self.rows)
            source = self.ref.at[pl.ds(row, self.rows), pl.ds(at, width)]
        else:
            source = self.staged.at[self.slot[number]]
        return pltpu.make_async_remote_copy(
            src_ref=source,
            dst_ref=self.landed.at[number],
            send_sem=self.sems[0].at[number],
            recv_sem=self.sems[1].at[number],
            device_id={"tensor": flipped(self.me, (bit,))},
            device_id_type=MESH,
        )

    def begin(self):
        for item in sorted(self.plan, key=lambda it: (len(it[2]) == 0)):
            if item[1] == 0:
                self.copy(item).start()

    def partial_sum(self, half, block, before, row, size):
        at, width = halves_of(self.nbits, self.ref.shape[1])[half][1:]
        base = pl.multiple_of(flipped(self.me, block) * self.rows + row, size)
        total = self.ref[pl.ds(base, size), pl.ds(at, width)].astype(F32)
        for it in self.plan:
            if it[0] == half and it[1] < before and set(it[2]) == set(block):
                total = total + self.landed[it[6], pl.ds(row, size), :].astype(F32)
        return total

    def advance(self, step):
        for half in range(2):
            for item in self.plan:
                if item[0] == half and item[1] == step:
                    self.copy(item).wait_recv()
            for item in self.plan:
                if item[0] == half and item[1] == step + 1:

                    def fill(row, item=item):
                        value = self.partial_sum(
                            item[0], item[2] + (item[3],), item[1], row, CHUNK
                        )
                        where = (self.slot[item[6]], pl.ds(row, CHUNK))
                        self.staged[where + (slice(None),)] = value.astype(BF16)

                    chunks(self.rows, fill)
                    self.copy(item).start()

    def run(self):
        for step in range(self.nbits):
            self.advance(step)

    def total(self, row, size):
        return jnp.concatenate(
            [self.partial_sum(half, (), self.nbits, row, size) for half in range(2)], axis=1
        )

    def drain(self):
        for item in self.plan:
            self.copy(item).wait_send()


def scatter_scratch(rows, columns, nbits):
    copies = gather_copies(nbits)
    later = max(1, copies - (1 << nbits))
    return [
        pltpu.VMEM((copies, rows, columns // 2), BF16),
        pltpu.VMEM((later, rows, columns // 2), BF16),
        pltpu.SemaphoreType.DMA((copies,)),
        pltpu.SemaphoreType.DMA((copies,)),
    ]


def gather_sems(nbits):
    copies = gather_copies(nbits)
    return [pltpu.SemaphoreType.DMA((copies,)), pltpu.SemaphoreType.DMA((copies,))]


def tensor_bits(nbits):
    return [("tensor", bit) for bit in range(nbits)]


def rms_scale_of(values):
    return lax.rsqrt(jnp.mean(values * values, axis=-1, keepdims=True) + EPSILON)


def chunks(rows, body):
    def step(i, carry):
        body(pl.multiple_of(i * CHUNK, CHUNK))
        return carry

    lax.fori_loop(0, rows // CHUNK, step, 0)


def own_row(row, rows):
    return pl.multiple_of(lax.axis_index("tensor") * rows + row, CHUNK)


def dp_place():
    me = lax.axis_index("dp")
    return me // 2, me % 2, lax.axis_size("dp") // 2


def dp_index(chip, core):
    return chip * 2 + core


UP, DOWN = 1, -1


class LineGather:
    def __init__(self, own, whole, send_sems, recv_sems, columns=None):
        self.own, self.whole = own, whole
        self.sems = (send_sems, recv_sems)
        self.chip, self.core, self.chips = dp_place()
        self.rows = own.shape[0]
        self.columns = slice(None) if columns is None else columns

    def block(self, chip):
        row = pl.multiple_of(dp_index(chip, self.core) * self.rows, self.rows)
        return self.whole.at[pl.ds(row, self.rows), self.columns]

    def has(self, way, distance):
        return self.chip >= distance if way == UP else self.chip + distance < self.chips

    def number(self, way, distance):
        return (0 if way == UP else self.chips) + distance

    def along(self, way, distance):
        block = self.block(self.chip - way * distance)
        return pltpu.make_async_remote_copy(
            src_ref=self.own if distance == 0 else block,
            dst_ref=block,
            send_sem=self.sems[0].at[self.number(way, distance)],
            recv_sem=self.sems[1].at[self.number(way, distance + 1)],
            device_id={"dp": dp_index(self.chip + way, self.core)},
            device_id_type=MESH,
        )

    def arrival(self, way, distance):
        block = self.block(self.chip - way * distance)
        return pltpu.make_async_remote_copy(
            src_ref=block,
            dst_ref=block,
            send_sem=self.sems[0].at[self.number(way, distance)],
            recv_sem=self.sems[1].at[self.number(way, distance)],
            device_id={"dp": dp_index(self.chip + way, self.core)},
            device_id_type=MESH,
        )

    def across(self, way, distance):
        block = self.block(self.chip - way * distance)
        number = 2 * self.chips + self.number(way, distance)
        return pltpu.make_async_remote_copy(
            src_ref=self.own if distance == 0 else block,
            dst_ref=block,
            send_sem=self.sems[0].at[number],
            recv_sem=self.sems[1].at[number],
            device_id={"dp": dp_index(self.chip, 1 - self.core)},
            device_id_type=MESH,
        )

    def local(self):
        return pltpu.make_async_copy(
            self.own, self.block(self.chip), self.sems[0].at[4 * self.chips]
        )

    def begin(self):
        for way in (UP, DOWN):

            @pl.when(self.has(-way, 1))
            def _(way=way):
                self.along(way, 0).start()

        self.across(UP, 0).start()
        self.local().start()

    def pass_on(self, distance):
        for way in (UP, DOWN):

            @pl.when(self.has(way, distance))
            def _(way=way):
                self.arrival(way, distance).wait_recv()

                @pl.when(self.has(-way, 1))
                def _():
                    self.along(way, distance).start()

                self.across(way, distance).start()

    def finish(self):
        self.across(UP, 0).wait()
        self.local().wait()
        for way in (UP, DOWN):
            for distance in range(self.chips):

                @pl.when(self.has(way, distance) & self.has(-way, 1))
                def _(way=way, distance=distance):
                    self.along(way, distance).wait_send()

                if distance:

                    @pl.when(self.has(way, distance))
                    def _(way=way, distance=distance):
                        self.across(way, distance).wait()


def line_sems(ndp):
    chips = ndp // 2
    return [pltpu.SemaphoreType.DMA((4 * chips + 1,)), pltpu.SemaphoreType.DMA((4 * chips + 1,))]


def greet_peers(nbits, all_tensor, whole_dp):
    me = lax.axis_index("tensor")
    chip, core, chips = dp_place()
    barrier = pltpu.get_barrier_semaphore()

    def signal(target):
        pl.semaphore_signal(barrier, inc=1, device_id=target, device_id_type=MESH)

    met = 0
    for chosen in subsets(tuple(range(nbits))):
        if chosen and (all_tensor or len(chosen) == 1):
            signal({"tensor": flipped(me, chosen)})
            met += 1
    if whole_dp:
        for shift in range(chips):
            for turn in range(2):
                if (shift, turn) != (0, 0):
                    other = dp_index((chip + shift) % chips, core + turn * (1 - 2 * core))
                    signal({"dp": other})
                    met += 1
    else:
        signal({"dp": dp_index(chip, 1 - core)})
        met += 1

        for shift in sorted({1 % chips, chips - 1} - {0}):
            signal({"dp": dp_index((chip + shift) % chips, core)})
            met += 1

    pl.semaphore_wait(barrier, met)


def widen(rows, wide):
    for row in range(rows.shape[0]):
        wide[:, row * 128 : (row + 1) * 128] = rows[row : row + 1, :]


def enter_kernel(
    nbits, parts_yx, joins_wide, tokens, seg, gain, *refs
):
    refs = list(refs)
    w_yx, w_out = refs[:parts_yx], refs[parts_yx]
    del refs[: parts_yx + 1]
    joined = refs[:2] if joins_wide else []
    del refs[: len(joined)]
    normed_all, seg_all, wyx_all, wout_all = refs[:4]
    w_both = refs[4] if joins_wide else None
    gain_row, s0, r0, s2, r2, l0, *line = refs[4 + joins_wide :]
    joins = [
        pltpu.make_async_copy(
            one,
            w_both.at[:, pl.ds(number * one.shape[1], one.shape[1])],
            l0.at[1 + number],
        )
        for number, one in enumerate(joined)
    ]
    rows = tokens.shape[0]
    me = lax.axis_index("tensor")
    peers = [chosen for chosen in subsets(tuple(range(nbits))) if chosen]
    greet_peers(nbits, True, False)
    width = wyx_all.shape[1] // parts_yx
    lines = [
        LineGather(
            own,
            wyx_all,
            line[2 * number],
            line[2 * number + 1],
            pl.ds(number * width, width) if parts_yx > 1 else None,
        )
        for number, own in enumerate(w_yx)
    ]
    lines.append(LineGather(w_out, wout_all, *line[2 * parts_yx : 2 * parts_yx + 2]))
    for item in lines:
        item.begin()
    for join in joins:
        join.start()
    widen(gain, gain_row)

    def norm(row):
        values = tokens[pl.ds(row, CHUNK), :].astype(F32)
        scaled = values * rms_scale_of(values) * gain_row[...]
        normed_all[pl.ds(own_row(row, rows), CHUNK), :] = scaled.astype(BF16)

    chunks(rows, norm)
    gather = Gather(normed_all, rows, nbits, s0, r0)
    gather.begin()
    seg_own = pltpu.make_async_copy(seg, seg_all.at[me], l0.at[0])
    seg_own.start()
    seg_copies = [
        pltpu.make_async_remote_copy(
            src_ref=seg,
            dst_ref=seg_all.at[me],
            send_sem=s2.at[number],
            recv_sem=r2.at[number],
            device_id={"tensor": flipped(me, chosen)},
            device_id_type=MESH,
        )
        for number, chosen in enumerate(peers)
    ]
    for copy in seg_copies:
        copy.start()
    chips = lines[0].chips
    for item in lines:
        item.pass_on(1)
    gather.advance(0)
    for distance in range(2, chips):
        for item in lines:
            item.pass_on(distance)
    gather.finish(1)
    for item in lines:
        item.finish()
    for copy in seg_copies:
        copy.wait()
    seg_own.wait()
    for join in joins:
        join.wait()


class Fetch:
    def __init__(self, nbits, cot, cot_all, s0, r0, l0):
        rows = cot.shape[0]
        own = pl.multiple_of(lax.axis_index("tensor") * rows, rows)
        self.local = pltpu.make_async_copy(cot, cot_all.at[pl.ds(own, rows), :], l0.at[0])
        self.gather = Gather(cot_all, rows, nbits, s0, r0)

    def begin(self):
        self.local.wait()
        self.gather.begin()

    def advance(self):
        self.gather.advance(0)

    def finish(self):
        self.gather.finish(1)


def fetch_scratch(nbits):
    return gather_sems(nbits) + [pltpu.SemaphoreType.DMA((1,))]


def fetch_kernel(nbits, cot, cot_all, *sems):
    greet(tensor_bits(nbits))
    fetch = Fetch(nbits, cot, cot_all, *sems)
    fetch.local.start()
    fetch.begin()
    fetch.advance()
    fetch.finish()


def middle_kernel(
    nbits, mixer, tokens, gain, middle, mid_all, landed, staged, s0, r0, s1, r1
):
    rows = tokens.shape[0]
    greet(tensor_bits(nbits))
    scatter = Scatter(mixer, landed, staged, rows, nbits, s0, r0)
    scatter.begin()
    scatter.run()

    def norm(row):
        values = tokens[pl.ds(row, CHUNK), :].astype(F32) + scatter.total(row, CHUNK)
        middle[pl.ds(row, CHUNK), :] = values
        scaled = values * rms_scale_of(values) * gain[...]
        mid_all[pl.ds(own_row(row, rows), CHUNK), :] = scaled.astype(BF16)

    chunks(rows, norm)
    gather = Gather(mid_all, rows, nbits, s1, r1)
    gather.begin()
    gather.finish()
    scatter.drain()


def result_kernel(nbits, ffn, middle, mixed, landed, staged, s0, r0):
    rows = middle.shape[0]
    greet(tensor_bits(nbits))
    scatter = Scatter(ffn, landed, staged, rows, nbits, s0, r0)
    scatter.begin()
    scatter.run()

    def add(row):
        values = middle[pl.ds(row, CHUNK), :] + scatter.total(row, CHUNK)
        mixed[pl.ds(row, CHUNK), :] = values.astype(BF16)

    chunks(rows, add)
    scatter.drain()


def norm_pull(values, gain, cotangent):
    scale = rms_scale_of(values)
    unit = values * scale
    inner = cotangent * gain
    back = scale * (inner - unit * jnp.mean(inner * unit, axis=-1, keepdims=True))
    return back, cotangent * unit


def eight_rows(values):
    total = values[0:8]
    for at in range(8, CHUNK, 8):
        total = total + values[at : at + 8]
    return total


class Product:
    def __init__(self, left, right, out, held, sems):
        self.left, self.right, self.out = left, right, out
        self.held, self.sems = held, sems
        self.width = held.shape[1]
        self.count = right.shape[0] // self.width
        self.done = 0

    def fetch(self, block):
        return pltpu.make_async_copy(
            self.right.at[pl.ds(block * self.width, self.width), :],
            self.held.at[block % 2],
            self.sems.at[block % 2],
        )

    def begin(self):
        self.fetch(0).start()

    def work(self, blocks):
        for block in range(self.done, min(self.done + blocks, self.count)):
            if block + 1 < self.count:
                self.fetch(block + 1).start()
            self.fetch(block).wait()

            def rows(span, block=block):
                found = times_transposed(self.left[span, :], self.held[block % 2])
                at = slice(block * self.width, (block + 1) * self.width)
                self.out[span, at] = found.astype(BF16)

            parts(self.left.shape[0], rows)
        self.done = min(self.done + blocks, self.count)


PRODUCT_BLOCK = 256


def product_scratch(depth):
    return [pltpu.VMEM((2, PRODUCT_BLOCK, depth), BF16), pltpu.SemaphoreType.DMA((2,))]


def turn_kernel(
    nbits,
    d_norm,
    cot,
    middle,
    gain,
    hidden,
    w_down,
    d_middle,
    d_mixer,
    d_gain,
    ffn,
    landed,
    staged,
    s0,
    r0,
    s1,
    r1,
    *product,
):
    rows = middle.shape[0]
    ahead = Product(hidden, w_down, ffn, *product)
    ahead.begin()
    greet(tensor_bits(nbits))
    scatter = Scatter(d_norm, landed, staged, rows, nbits, s0, r0)
    scatter.begin()
    d_gain[...] = jnp.zeros_like(d_gain)
    ahead.work(4)
    for step in range(nbits):
        scatter.advance(step)
        if step + 1 < nbits:
            ahead.work(2)

    def pull(row):
        span = pl.ds(row, CHUNK)
        back, gains = norm_pull(middle[span, :], gain[...], scatter.total(row, CHUNK))
        values = cot[span, :].astype(F32) + back
        d_middle[span, :] = values
        d_mixer[pl.ds(own_row(row, rows), CHUNK), :] = values.astype(BF16)
        d_gain[...] += eight_rows(gains)

    chunks(rows, pull)
    gather = Gather(d_mixer, rows, nbits, s1, r1)
    gather.begin()
    ahead.work(2)
    gather.advance(0)
    ahead.work(ahead.count)
    gather.finish(1)
    scatter.drain()


class LineSum:
    def __init__(self, whole, kept, swapped, staged, landed, send_sems, recv_sems, columns=None):
        self.whole, self.kept, self.swapped = whole, kept, swapped
        self.staged, self.landed = staged, landed
        self.sems = (send_sems, recv_sems)
        self.columns = columns
        self.chip, self.core, self.chips = dp_place()
        self.rows = whole.shape[2]

    def half(self, core):
        if self.columns is None:
            return self.whole.at[:, core]
        return self.whole.at[:, core, :, self.columns]

    def local(self):
        return pltpu.make_async_copy(
            self.half(self.core), self.kept, self.sems[0].at[2 * self.chips]
        )

    def swap(self):
        return pltpu.make_async_remote_copy(
            src_ref=self.half(1 - self.core),
            dst_ref=self.swapped,
            send_sem=self.sems[0].at[0],
            recv_sem=self.sems[1].at[0],
            device_id={"dp": dp_index(self.chip, 1 - self.core)},
            device_id_type=MESH,
        )

    def has(self, way, distance):
        return self.chip + distance < self.chips if way == UP else self.chip >= distance

    def slot(self, way, distance):
        return (0 if way == UP else self.chips - 1) + distance

    def stage(self, way, distance):
        return distance - 1 if way == UP else self.chips - 1 - distance

    def hop(self, way, distance):
        return pltpu.make_async_remote_copy(
            src_ref=self.staged.at[self.stage(way, distance)],
            dst_ref=self.landed.at[self.slot(way, distance - 1)],
            send_sem=self.sems[0].at[1 + self.slot(way, distance - 1)],
            recv_sem=self.sems[1].at[1 + self.slot(way, distance - 1)],
            device_id={"dp": dp_index(self.chip + way, self.core)},
            device_id_type=MESH,
        )

    def arrival(self, way, distance):
        number = self.slot(way, distance)
        return pltpu.make_async_remote_copy(
            src_ref=self.landed.at[number],
            dst_ref=self.landed.at[number],
            send_sem=self.sems[0].at[1 + number],
            recv_sem=self.sems[1].at[1 + number],
            device_id={"dp": dp_index(self.chip - way, self.core)},
            device_id_type=MESH,
        )

    def begin(self):
        self.swap().start()
        self.local().start()

    def both(self, chip, span):
        return self.kept[chip, span, :].astype(F32) + self.swapped[chip, span, :].astype(F32)

    def send(self, distance):
        if distance == self.chips - 1:
            self.local().wait()
            self.swap().wait_recv()
        for way in (UP, DOWN):

            @pl.when(self.has(way, distance))
            def _(way=way):
                chip = self.chip + way * distance
                slot = self.stage(way, distance)

                def first(row):
                    span = pl.ds(row, CHUNK)
                    self.staged[slot, span, :] = self.both(chip, span).astype(BF16)

                def later(row):
                    span = pl.ds(row, CHUNK)
                    total = self.both(chip, span) + self.landed[
                        self.slot(way, distance), span, :
                    ].astype(F32)
                    self.staged[slot, span, :] = total.astype(BF16)

                if distance == self.chips - 1:
                    chunks(self.rows, first)
                else:

                    @pl.when(self.has(-way, 1))
                    def _():
                        self.arrival(way, distance).wait_recv()
                        chunks(self.rows, later)

                    @pl.when(jnp.logical_not(self.has(-way, 1)))
                    def _():
                        chunks(self.rows, first)

                self.hop(way, distance).start()

    def finish(self, store):
        below, above = self.has(DOWN, 1), self.has(UP, 1)

        def fill(slots):
            for way in slots:
                self.arrival(way, 0).wait_recv()

            def one(row):
                span = pl.ds(row, CHUNK)
                total = self.both(self.chip, span)
                for way in slots:
                    total = total + self.landed[self.slot(way, 0), span, :].astype(F32)
                store(span, total)

            chunks(self.rows, one)

        @pl.when(below & above)
        def _():
            fill((UP, DOWN))

        @pl.when(jnp.logical_not(above))
        def _():
            fill((UP,))

        @pl.when(jnp.logical_not(below))
        def _():
            fill((DOWN,))

    def drain(self):
        self.swap().wait_send()
        for way in (UP, DOWN):
            for distance in range(1, self.chips):

                @pl.when(self.has(way, distance))
                def _(way=way, distance=distance):
                    self.hop(way, distance).wait_send()


def line_scratch(ndp, rows, columns):
    chips = ndp // 2
    return [
        pltpu.VMEM((chips, rows, columns), BF16),
        pltpu.VMEM((chips, rows, columns), BF16),
        pltpu.VMEM((chips - 1, rows, columns), BF16),
        pltpu.VMEM((2 * chips - 2, rows, columns), BF16),
        pltpu.SemaphoreType.DMA((2 * chips + 1,)),
        pltpu.SemaphoreType.DMA((2 * chips + 1,)),
    ]


RING = 6


def leave_kernel(nbits, tiled, with_ffn, *refs):
    refs = list(refs)

    def take(count):
        taken = refs[:count]
        del refs[:count]
        return taken

    d_norm, tokens, d_middle, gain, own_small, d_gain_mid = take(6)
    pieces = take(3)
    ffn, middle = take(2) if with_ffn else (None, None)
    grad_input, sum_out, sum_y, sum_x, gate_all, small_all = take(6)
    mixed = take(1)[0] if with_ffn else None
    landed, staged, s0, r0 = take(4)
    share = small_all.shape[2]
    gate = LineSum(pieces[0], *take(RING))
    lines = [LineSum(pieces[1], *take(RING))]
    if tiled:
        lines += [LineSum(pieces[2], *take(RING), pl.ds(at, share)) for at in (0, share)]
    else:
        lines += [LineSum(pieces[2], *take(RING))]
    d_gain, gains, gains_landed, small, small_landed = take(5)
    gain_s, gain_r, vec_s, vec_r, join_s, join_r, gate_s, gate_r = take(8)
    rows = tokens.shape[0]
    me = lax.axis_index("tensor")
    chip, core, chips = dp_place()
    peers = [chosen for chosen in subsets(tuple(range(nbits))) if chosen]
    others = [(shift, turn) for shift in range(chips) for turn in range(2)][1:]
    greet_peers(nbits, True, True)
    for line in [gate] + lines:
        line.begin()
    scatter = Scatter(d_norm, landed, staged, rows, nbits, s0, r0)
    scatter.begin()
    if with_ffn:
        second = Scatter(ffn, *take(2), rows, nbits, *take(2))
    d_gain[...] = jnp.zeros_like(d_gain)
    far = list(range(chips - 1, 0, -1))
    for number in range(max(len(far), len(lines))):
        if number < len(far):
            gate.send(far[number])
        if number < len(lines):
            lines[number].send(far[0])
    scatter.advance(0)
    if with_ffn:
        second.begin()
    for distance in far[1:-1]:
        for line in lines:
            line.send(distance)
    for step in range(1, nbits):
        scatter.advance(step)

    def pull(row):
        span = pl.ds(row, CHUNK)
        back, parts = norm_pull(
            tokens[span, :].astype(F32), gain[...], scatter.total(row, CHUNK)
        )
        grad_input[span, :] = d_middle[span, :] + back
        d_gain[...] += eight_rows(parts)

    chunks(rows, pull)
    def store_gate(span, value):
        gate_all[me, chip, core, span, :] = value.astype(BF16)

    def gate_copy(number, ref, target):
        return pltpu.make_async_remote_copy(
            src_ref=ref,
            dst_ref=ref,
            send_sem=gate_s.at[number],
            recv_sem=gate_r.at[number],
            device_id=target,
            device_id_type=MESH,
        )

    def gate_line(shift):
        target = {"dp": dp_index((chip + shift) % chips, core)}
        return gate_copy(shift - 1, gate_all.at[me, chip, core], target)

    def gate_tensor(number, chosen):
        target = {"tensor": flipped(me, chosen)}
        return gate_copy(chips - 1 + number, gate_all.at[me, :, core], target)

    def gate_core():
        target = {"dp": dp_index(chip, 1 - core)}
        return gate_copy(chips - 1 + len(peers), gate_all.at[:, :, core], target)

    def start_gate():
        gate.finish(store_gate)
        for shift in range(1, chips):
            gate_line(shift).start()

    top = jnp.sum(d_gain[...], axis=0, keepdims=True)
    low = jnp.sum(d_gain_mid[...], axis=0, keepdims=True)
    place8 = lax.broadcasted_iota(jnp.int32, (8, share), 0)
    for index in range(1 << nbits):
        span = slice(index * share, (index + 1) * share)
        gains[index] = jnp.where(
            place8 == 6, top[:, span], jnp.where(place8 == 7, low[:, span], 0.0)
        )

    def gain_copy(number, chosen):
        peer = flipped(me, chosen)
        return pltpu.make_async_remote_copy(
            src_ref=gains.at[peer],
            dst_ref=gains_landed.at[number],
            send_sem=gain_s.at[number],
            recv_sem=gain_r.at[number],
            device_id={"tensor": peer},
            device_id_type=MESH,
        )

    for number, chosen in enumerate(peers):
        gain_copy(number, chosen).start()
    start_gate()
    if len(far) > 1:
        for line in lines:
            line.send(far[-1])
    total = own_small[...] + gains[me]
    for number, chosen in enumerate(peers):
        gain_copy(number, chosen).wait_recv()
        total = total + gains_landed[number]
    small[...] = total

    def vec_copy(number, shift, turn):
        other = dp_index((chip + shift) % chips, core + turn * (1 - 2 * core))
        return pltpu.make_async_remote_copy(
            src_ref=small,
            dst_ref=small_landed.at[number],
            send_sem=vec_s.at[number],
            recv_sem=vec_r.at[number],
            device_id={"dp": other},
            device_id_type=MESH,
        )

    for number, (shift, turn) in enumerate(others):
        vec_copy(number, shift, turn).start()

    for shift in range(1, chips):
        gate_line(shift).wait_recv()
    for number, chosen in enumerate(peers):
        gate_tensor(number, chosen).start()
    total = small[...]
    for number, (shift, turn) in enumerate(others):
        vec_copy(number, shift, turn).wait_recv()
        total = total + small_landed[number]
    small_all[me] = total

    def join_copy(number, chosen):
        return pltpu.make_async_remote_copy(
            src_ref=small_all.at[me],
            dst_ref=small_all.at[me],
            send_sem=join_s.at[number],
            recv_sem=join_r.at[number],
            device_id={"tensor": flipped(me, chosen)},
            device_id_type=MESH,
        )

    for number, chosen in enumerate(peers):
        join_copy(number, chosen).start()
    if with_ffn:
        second.advance(0)
    for number, chosen in enumerate(peers):
        gate_tensor(number, chosen).wait_recv()
    gate_core().start()
    if with_ffn:
        for step in range(1, nbits):
            second.advance(step)

        def add(row):
            span = pl.ds(row, CHUNK)
            mixed[span, :] = (middle[span, :] + second.total(row, CHUNK)).astype(BF16)

        chunks(rows, add)

    def store_in(*targets):
        def store(span, value):
            for number, ref in enumerate(targets):
                ref[span, :] = value[:, number * share : (number + 1) * share]

        return store

    lines[0].finish(store_in(sum_out))
    if tiled:
        lines[1].finish(store_in(sum_y))
        lines[2].finish(store_in(sum_x))
    else:
        lines[1].finish(store_in(sum_y, sum_x))
    gate_core().wait()
    for shift in range(1, chips):
        gate_line(shift).wait_send()
    for number, chosen in enumerate(peers):
        gate_tensor(number, chosen).wait_send()
        gain_copy(number, chosen).wait_send()
        join_copy(number, chosen).wait()
    for number, (shift, turn) in enumerate(others):
        vec_copy(number, shift, turn).wait_send()
    scatter.drain()
    if with_ffn:
        second.drain()
    for line in [gate] + lines:
        line.drain()


def in_vmem(count):
    return [pl.BlockSpec(memory_space=pltpu.VMEM)] * count


def call_kernel(kernel, outs, scratch, number, *operands, far_in=(), far_out=(), cost_us=1, vmem_bytes=VMEM_BYTES):
    vmem = pl.BlockSpec(memory_space=pltpu.VMEM)
    far = pl.BlockSpec(memory_space=pl.ANY)
    return pl.pallas_call(
        kernel,
        out_shape=outs,
        in_specs=[far if i in far_in else vmem for i in range(len(operands))],
        out_specs=tuple(far if i in far_out else vmem for i in range(len(outs))),
        scratch_shapes=scratch,
        cost_estimate=pl.CostEstimate(
            flops=0, bytes_accessed=cost_us * 1_000_000, transcendentals=0
        ),
        compiler_params=pltpu.CompilerParams(
            collective_id=number, has_side_effects=True, vmem_limit_bytes=vmem_bytes
        ),
    )(*operands)


def sigmoid(values):
    return 1.0 / (1.0 + jnp.exp(-values))


def one_minus_exp(values):
    series = values / 7.0 + 1.0
    for order in (6.0, 5.0, 4.0, 3.0, 2.0):
        series = 1.0 + series * values / order
    return jnp.where(values > -0.3, -values * series, 1.0 - jnp.exp(values))


GELU_K = 0.7978845608028654
GELU_C = 0.044715


def gelu_parts(values):
    square = values * values
    bent = jnp.tanh(GELU_K * values * (1.0 + GELU_C * square))
    gelu = 0.5 * values * (1.0 + bent)
    slope = 0.5 * (1.0 + bent) + 0.5 * values * (1.0 - bent * bent) * GELU_K * (
        1.0 + 3.0 * GELU_C * square
    )
    return gelu, slope


def gate_terms(gate_a, gate_x, soft, since):
    sig_a = sigmoid(gate_a)
    sig_x = sigmoid(gate_x)
    log_decay = -8.0 * sig_a * soft
    decay = jnp.exp(log_decay)
    scale = jnp.sqrt(one_minus_exp(2.0 * log_decay))
    keep = since > 0.5
    return sig_a, sig_x, decay, jnp.where(keep, scale, 1.0), keep


def scan_down(decay, value, carry):
    place = lax.broadcasted_iota(jnp.int32, decay.shape, 0)
    for shift in (1, 2, 4):
        past = place >= shift
        moved = pltpu.roll(value, shift, 0)
        value = jnp.where(past, decay * moved + value, value)
        decay = jnp.where(past, decay * pltpu.roll(decay, shift, 0), decay)
    return decay * carry + value


def scan_up(decay, value, carry):
    place = lax.broadcasted_iota(jnp.int32, decay.shape, 0)
    factor = jnp.where(place < 7, pltpu.roll(decay, 7, 0), 1.0)
    for shift in (1, 2, 4):
        past = place < 8 - shift
        moved = pltpu.roll(value, 8 - shift, 0)
        value = jnp.where(past, factor * moved + value, value)
        factor = jnp.where(past, factor * pltpu.roll(factor, 8 - shift, 0), factor)
    return factor * carry + value


def forward_scan(conv_rows, gates, branch_y, soft, since, mixed, states, between=()):
    total_rows, width = states.shape

    def step(i, carry):
        row = pl.multiple_of(i * CHUNK, CHUNK)
        span = pl.ds(row, CHUNK)
        values = conv_rows(span).astype(F32)
        kept = []
        for at in range(0, CHUNK, 8):
            tile = pl.ds(row + at, 8)
            sig_a, sig_x, decay, scale, keep = gate_terms(
                gates[tile, :width], gates[tile, width:], soft[...], since[tile, :]
            )
            given = values[at : at + 8] * sig_x * scale
            state = scan_down(jnp.where(keep, decay, 0.0), given, carry)
            carry = state[7:8]
            states[tile, :] = state
            kept.append(state * gelu_parts(branch_y[tile, :])[0])
        mixed[span, :] = jnp.concatenate(kept, axis=0).astype(BF16)
        return carry

    steps, stretches = total_rows // CHUNK, len(between) + 1
    carry = jnp.zeros((1, width), F32)
    for stretch in range(stretches):
        first, last = stretch * steps // stretches, (stretch + 1) * steps // stretches
        carry = lax.fori_loop(first, last, step, carry)
        if stretch < len(between):
            between[stretch]()


def forward_scan_kernel(conv, gates, branch_y, soft, since, mixed, states):
    forward_scan(lambda span: conv[span, :], gates, branch_y, soft, since, mixed, states)


def backward_scan(
    d_mixed, conv_rows, gates, branch_y, states, soft, slope_soft, since, d_conv, d_gates, d_branch, d_decay
):
    total_rows, width = states.shape
    d_decay[...] = jnp.zeros_like(d_decay)

    def step(i, carry):
        row = pl.multiple_of(total_rows - CHUNK - i * CHUNK, CHUNK)
        span = pl.ds(row, CHUNK)
        values = conv_rows(span).astype(F32)
        kept = []
        for at in range(CHUNK - 8, -1, -8):
            tile = pl.ds(row + at, 8)
            soft_row = soft[...]
            sig_a, sig_x, decay, scale, keep = gate_terms(
                gates[tile, :width], gates[tile, width:], soft_row, since[tile, :]
            )
            value = values[at : at + 8]
            gelu, slope = gelu_parts(branch_y[tile, :])
            state = states[tile, :]
            upper = d_mixed[tile, :]
            held = jnp.where(keep, decay, 0.0)
            lam = scan_up(held, upper * gelu, carry)
            carry = held[0:1] * lam[0:1]
            d_conv[tile, :] = lam * sig_x * scale
            d_x = lam * value * scale * sig_x * (1.0 - sig_x)
            given = value * sig_x
            d_log = lam * (state - given * scale - given * decay * decay / scale)
            d_log = jnp.where(keep, d_log, 0.0)
            d_a = d_log * (-8.0 * soft_row) * sig_a * (1.0 - sig_a)
            d_decay[...] += d_log * (-8.0 * sig_a) * slope_soft[...]
            kept.append((d_a, d_x, upper * state * slope))
        kept = kept[::-1]
        d_gates[span, :width] = jnp.concatenate([k[0] for k in kept], axis=0).astype(BF16)
        d_gates[span, width:] = jnp.concatenate([k[1] for k in kept], axis=0).astype(BF16)
        d_branch[span, :] = jnp.concatenate([k[2] for k in kept], axis=0).astype(BF16)
        return carry

    lax.fori_loop(0, total_rows // CHUNK, step, jnp.zeros((1, width), F32))


def backward_scan_kernel(
    d_mixed, conv, gates, branch_y, states, soft, slope_soft, since, d_conv, d_gates, d_branch, d_decay
):
    backward_scan(
        d_mixed,
        lambda span: conv[span, :],
        gates,
        branch_y,
        states,
        soft,
        slope_soft,
        since,
        d_conv,
        d_gates,
        d_branch,
        d_decay,
    )


def times_transposed(left, right):
    return lax.dot_general(left, right, (((1,), (1,)), ((), ())), preferred_element_type=F32)


class HalfBlocks:
    def __init__(self, channels, block):
        self.odd = lax.axis_index("tensor") % 2
        self.half = block // 2
        self.block = block
        self.count = channels // block + 1
        self.channels = channels
        self.own = pl.multiple_of(self.odd * self.half, self.half)
        self.shared = (1 - self.odd) * (self.count - 1)
        self.mine_in_block = pl.multiple_of(self.odd * self.half, self.half)
        self.other_in_block = pl.multiple_of((1 - self.odd) * self.half, self.half)
        self.mine = pl.multiple_of((1 - self.odd) * (channels - self.half), self.half)
        self.pair = {"tensor": lax.axis_index("tensor") + 1 - 2 * self.odd}

    def full(self, index):
        block = index + self.odd
        return block, pl.multiple_of(index * self.block + self.odd * self.half, self.half)

    def span(self, block):
        return pl.ds(pl.multiple_of(block * self.block, self.block), self.block)

    def shared_part(self, start):
        return pl.ds(pl.multiple_of(self.shared * self.block + start, self.half), self.half)


PART = 256


def parts(rows, body):
    def step(i, carry):
        body(pl.ds(pl.multiple_of(i * PART, PART), PART))
        return carry

    lax.fori_loop(0, rows // PART, step, 0)


def recurrence_kernel(
    taps,
    nbits,
    branches,
    tap_rows,
    soft,
    since,
    weights,
    cot,
    mixed,
    states,
    window,
    gates,
    cot_all,
    send,
    recv,
    *sems,
):
    total_rows, width = states.shape
    block = weights.shape[2]
    place = HalfBlocks(width, block)
    branch_y, branch_x = branches.at[:, :width], branches.at[:, width:]
    greet(tensor_bits(nbits))
    fetch = Fetch(nbits, cot, cot_all, *sems)
    fetch.local.start()

    def conv(i, before):
        row = pl.multiple_of(i * CHUNK, CHUNK)
        kept = []
        for at in range(0, CHUNK, 8):
            tile = pl.ds(row + at, 8)
            values = branch_x[tile, :]
            line = lax.broadcasted_iota(jnp.int32, values.shape, 0)
            total = values * tap_rows[0:1, :]
            for tap in range(1, taps):
                moved = jnp.where(
                    line < tap, pltpu.roll(before, tap, 0), pltpu.roll(values, tap, 0)
                )
                moved = jnp.where(since[tile, :] > tap - 0.5, moved, 0.0)
                total = total + moved * tap_rows[tap : tap + 1, :]
            kept.append(total)
            before = values
        window[pl.ds(row, CHUNK), pl.ds(place.own, width)] = jnp.concatenate(
            kept, axis=0
        ).astype(BF16)
        return before

    lax.fori_loop(0, total_rows // CHUNK, conv, jnp.zeros((8, width), F32))
    source = window.at[:, place.shared_part(place.mine_in_block)]
    away = pl.multiple_of(place.odd * (place.count - 1) * block + place.mine_in_block, place.half)
    rim = pltpu.make_async_remote_copy(
        src_ref=source,
        dst_ref=window.at[:, pl.ds(away, place.half)],
        send_sem=send.at[0],
        recv_sem=recv.at[0],
        device_id=place.pair,
        device_id_type=MESH,
    )
    rim.start()
    fetch.begin()

    def full(span):
        for index in range(place.count - 1):
            number, at = place.full(index)
            cells = window[span, place.span(number)]
            for s in range(2):
                gates[span, pl.ds(s * width + at, block)] = jnp.dot(
                    cells, weights[s, number], preferred_element_type=F32
                )

    parts(total_rows, full)
    rim.wait()

    def shared(span):
        cells = window[span, place.span(place.shared)]
        for s in range(2):
            gates[span, pl.ds(s * width + place.mine, place.half)] = jnp.dot(
                cells,
                weights[s, place.shared, :, pl.ds(place.mine_in_block, place.half)],
                preferred_element_type=F32,
            )

    parts(total_rows, shared)
    forward_scan(
        lambda span: window[span, pl.ds(place.own, width)],
        gates,
        branch_y,
        soft,
        since,
        mixed,
        states,
        [fetch.advance],
    )
    fetch.finish()


def recurrence_back_kernel(
    taps,
    d_mixed,
    window,
    gates,
    branches,
    states,
    tap_rows,
    soft,
    slope_soft,
    since,
    weights,
    d_branches,
    gate_grad,
    own_small,
    d_conv,
    d_gates,
    given,
    taken,
    sums,
    send,
    recv,
):
    total_rows, width = states.shape
    block = weights.shape[2]
    place = HalfBlocks(width, block)
    half = place.half
    branch_y, branch_x = branches.at[:, :width], branches.at[:, width:]
    d_branch_y, d_branch_x = d_branches.at[:, :width], d_branches.at[:, width:]
    greet([("tensor", 0)])
    backward_scan(
        d_mixed,
        lambda span: window[span, pl.ds(place.own, width)],
        gates,
        branch_y,
        states,
        soft,
        slope_soft,
        since,
        d_conv,
        d_gates,
        d_branch_y,
        sums.at[taps],
    )

    def to_pair(span):
        total = jnp.zeros((PART, half), F32)
        for s in range(2):
            total = total + times_transposed(
                d_gates[span, pl.ds(s * width + place.mine, half)],
                weights[
                    s,
                    place.shared,
                    pl.ds(place.other_in_block, half),
                    pl.ds(place.mine_in_block, half),
                ],
            )
        given[span, :] = total.astype(BF16)

    parts(total_rows, to_pair)
    rim = pltpu.make_async_remote_copy(
        src_ref=given,
        dst_ref=taken,
        send_sem=send.at[0],
        recv_sem=recv.at[0],
        device_id=place.pair,
        device_id_type=MESH,
    )
    rim.start()

    def full(span):
        for index in range(place.count - 1):
            number, at = place.full(index)
            total = d_conv[span, pl.ds(at, block)]
            for s in range(2):
                total = total + times_transposed(
                    d_gates[span, pl.ds(s * width + at, block)], weights[s, number]
                )
            d_conv[span, pl.ds(at, block)] = total
        total = d_conv[span, pl.ds(place.mine, half)]
        for s in range(2):
            total = total + times_transposed(
                d_gates[span, pl.ds(s * width + place.mine, half)],
                weights[
                    s,
                    place.shared,
                    pl.ds(place.mine_in_block, half),
                    pl.ds(place.mine_in_block, half),
                ],
            )
        d_conv[span, pl.ds(place.mine, half)] = total

    parts(total_rows, full)
    units = width // half
    for index in range(units):
        number = (index + place.odd) // 2
        cells = window[:, place.span(number)]
        both = jnp.concatenate(
            [d_gates[:, s * width + index * half : s * width + (index + 1) * half] for s in range(2)],
            axis=1,
        )
        found = lax.dot_general(
            cells, both, (((0,), (0,)), ((), ())), preferred_element_type=F32
        ).astype(BF16)
        gate_grad[2 * index] = found[:, :half]
        gate_grad[2 * index + 1] = found[:, half:]
    rim.wait()

    def add(span):
        d_conv[span, pl.ds(place.mine, half)] += taken[span, :].astype(F32)

    parts(total_rows, add)
    for tap in range(taps):
        sums[tap] = jnp.zeros((8, width), F32)

    def conv(i, after):
        row = pl.multiple_of(total_rows - CHUNK - i * CHUNK, CHUNK)
        kept = []
        for at in range(CHUNK - 8, -1, -8):
            tile = pl.ds(row + at, 8)
            values = d_conv[tile, :]
            line = lax.broadcasted_iota(jnp.int32, values.shape, 0)
            below = branch_x[tile, :]
            higher = pl.multiple_of((row + at - 8 + total_rows) % total_rows, 8)
            above = branch_x[pl.ds(higher, 8), :]
            total = values * tap_rows[0:1, :]
            sums[0] += values * below
            masked = []
            for tap in range(1, taps):
                here = jnp.where(since[tile, :] > tap - 0.5, values, 0.0)
                masked.append(here)
                moved = jnp.where(
                    line < 8 - tap,
                    pltpu.roll(here, 8 - tap, 0),
                    pltpu.roll(after[tap - 1], 8 - tap, 0),
                )
                total = total + moved * tap_rows[tap : tap + 1, :]
                source = jnp.where(
                    line < tap, pltpu.roll(above, tap, 0), pltpu.roll(below, tap, 0)
                )
                sums[tap] += here * source
            after = tuple(masked)
            kept.append(total)
        d_branch_x[pl.ds(row, CHUNK), :] = jnp.concatenate(kept[::-1], axis=0).astype(BF16)
        return after

    none = jnp.zeros((8, width), F32)
    lax.fori_loop(0, total_rows // CHUNK, conv, (none,) * (taps - 1))
    line = lax.broadcasted_iota(jnp.int32, (8, width), 0)
    total = jnp.zeros((8, width), F32)
    for tap in range(taps + 1):
        row = jnp.sum(sums[tap], axis=0, keepdims=True)
        total = jnp.where(line == tap, row, total)
    own_small[...] = total


def finish_kernel(
    taps,
    gates,
    small,
    in_out,
    in_y,
    in_x,
    in_grad,
    in_mixed,
    in_both,
    in_down,
    whole,
    out_out,
    out_y,
    out_x,
    out_grad,
    out_mixed,
    out_gate,
    out_up,
    out_down,
    conv,
    decay,
    gain_in,
    gain_mid,
):
    held = whole.shape[1]
    pieces = gates.shape[0] // held

    def block(n, carry):
        for piece in range(pieces):
            for s in range(2):
                whole[s, n, :, piece * 128 : (piece + 1) * 128] = gates[
                    n * pieces + piece, s
                ].astype(F32)
        return carry

    lax.fori_loop(0, held, block, 0)
    units = out_gate.shape[1]

    def copy(row):
        span = pl.ds(row, CHUNK)
        out_out[span, :] = in_out[span, :]
        out_y[span, :] = in_y[span, :]
        out_x[span, :] = in_x[span, :]
        out_gate[span, :] = in_both[span, :units].astype(F32)
        out_up[span, :] = in_both[span, units:].astype(F32)
        out_down[span, :] = in_down[span, :].astype(F32)

    chunks(out_out.shape[0], copy)

    def own(row):
        span = pl.ds(row, CHUNK)
        out_grad[span, :] = in_grad[span, :]
        out_mixed[span, :] = in_mixed[span, :]

    chunks(out_grad.shape[0], own)

    @pl.when(pl.program_id(0) == 0)
    def _():
        share = small.shape[2]
        for index in range(small.shape[0]):
            span = slice(index * share, (index + 1) * share)
            conv[:, span] = small[index, :taps, :]
            for at in range(0, share, 128):
                row = (index * share + at) // 128
                decay[row : row + 1, :] = small[index, taps : taps + 1, at : at + 128]
                gain_in[row : row + 1, :] = small[index, 6:7, at : at + 128]
                gain_mid[row : row + 1, :] = small[index, 7:8, at : at + 128]


def finish(gate_all, small_all, sums, grad_input, mixed, both, down, taps, gate_shape):
    _, blocks, block, _ = gate_shape
    unit = gate_all.shape[-1]
    pieces = block // unit
    width = small_all.shape[0] * small_all.shape[2]
    rows, units = down.shape
    own_rows = grad_input.shape[0]
    grid = 2
    steps, held = rows // grid, own_rows // grid
    if unit != 128 or blocks % grid or rows % (16 * grid) or own_rows % (16 * grid):
        whole = gate_all.reshape(blocks, pieces, 2, block, unit).transpose(2, 0, 3, 1, 4)
        summed = small_all.transpose(1, 0, 2).reshape(8, width)
        whole = whole.reshape(gate_shape).astype(F32)
        wide = tuple(one.astype(F32) for one in (both[:, :units], both[:, units:], down))
        last = (summed[:taps], summed[taps], summed[6], summed[7])
        return (whole, *sums, grad_input, mixed, *wide, *last)
    shape = jax.ShapeDtypeStruct

    def by_rows(count, columns):
        return pl.BlockSpec((count, columns), lambda n: (n, 0))

    def by_held(columns):
        return pl.BlockSpec((held, columns), lambda n: (n, 0))

    def whole_array(*dims):
        return pl.BlockSpec(dims, lambda n: (0,) * len(dims))

    columns = sums[0].shape[1]
    d_width = grad_input.shape[1]
    lines = width // 128
    found = pl.pallas_call(
        partial(finish_kernel, taps),
        grid=(grid,),
        in_specs=[
            pl.BlockSpec((blocks // grid * pieces, 2, block, unit), lambda n: (n, 0, 0, 0)),
            whole_array(*small_all.shape),
        ]
        + [by_rows(steps, columns)] * 3
        + [by_held(d_width)] * 2
        + [by_rows(steps, 2 * units), by_rows(steps, units)],
        out_specs=(
            (pl.BlockSpec((2, blocks // grid, block, block), lambda n: (0, n, 0, 0)),)
            + (by_rows(steps, columns),) * 3
            + (by_held(d_width),) * 2
            + (by_rows(steps, units),) * 3
            + (whole_array(taps, width),)
            + (whole_array(lines, 128),) * 3
        ),
        out_shape=(
            (shape(gate_shape, F32),)
            + (shape((rows, columns), F32),) * 3
            + (shape(grad_input.shape, F32), shape(mixed.shape, BF16))
            + (shape((rows, units), F32),) * 3
            + (shape((taps, width), F32),)
            + (shape((lines, 128), F32),) * 3
        ),
        compiler_params=pltpu.CompilerParams(vmem_limit_bytes=VMEM_BYTES),
    )(
        gate_all.reshape(blocks * pieces, 2, block, unit),
        small_all,
        *sums,
        grad_input,
        mixed,
        both,
        down,
    )
    return found[:10] + tuple(one.reshape(width) for one in found[10:])


def scan_call(kernel, outs, *operands):
    return pl.pallas_call(
        kernel,
        out_shape=outs,
        in_specs=in_vmem(len(operands)),
        out_specs=tuple(in_vmem(len(outs))),
        compiler_params=pltpu.CompilerParams(vmem_limit_bytes=VMEM_BYTES),
    )(*operands)


class Rim:
    def __init__(self, route, back, source, first, width, room):
        self.route, self.back = route, back
        self.source, self.first, self.width = source, first, width
        self.room = room

    def fetch(self, values):
        part = lax.dynamic_slice_in_dim(values, self.source, self.width, 1)
        return lax.ppermute(part, "tensor", self.route)

    def give(self, part):
        return lax.ppermute(part, "tensor", self.back)

    def add(self, values, part):
        zeros = jnp.zeros(values.shape, F32)
        return values + lax.dynamic_update_slice_in_dim(
            zeros, part.astype(F32), self.source, 1
        )

    def window(self, channels):
        return (channels // self.width + 4) * self.width


def gate_rims(channels, block_size, ntensor, offset):
    up = [(i, i + 1) for i in range(ntensor - 1)]
    down = [(i + 1, i) for i in range(ntensor - 1)]
    last = jnp.int32(channels - block_size)
    return [
        Rim(up, down, last, offset - block_size, block_size, block_size),
        Rim(down, up, jnp.int32(0), offset + channels, block_size, block_size),
    ]


def same_block(first, count, offset, channels, block_size):
    rows = (first + jnp.arange(count, dtype=jnp.int32))[:, None]
    columns = (offset + jnp.arange(channels, dtype=jnp.int32))[None, :]
    return (rows + block_size) // block_size == (columns + block_size) // block_size


def gate_dense(gate_w, offset, first, count):
    block_size = gate_w.shape[2]
    total = gate_w.shape[1] * block_size
    channels = total // lax.axis_size("tensor")
    columns = gate_w.transpose(2, 0, 1, 3).reshape(block_size, 2, total)
    columns = lax.dynamic_slice_in_dim(columns, offset, channels, 2)
    copies = -(-count // block_size) + 1
    tall = jnp.concatenate([columns] * copies, axis=0)
    tall = lax.dynamic_slice_in_dim(tall, (first + block_size) % block_size, count, 0)
    same = same_block(first, count, offset, channels, block_size)
    dense = jnp.where(same[:, None, :], tall, jnp.zeros_like(tall))
    return dense.reshape(count, 2 * channels)


def doc_starts(seg_ids, seq_len):
    places = jnp.arange(seg_ids.shape[0], dtype=jnp.int32)
    before = jnp.concatenate([seg_ids[:1], seg_ids[:-1]])
    resets = (places % seq_len == 0) | (seg_ids != before)
    starts = lax.cummax(jnp.where(resets, places, jnp.zeros_like(places)), axis=0)
    return starts


def causal_conv(starts, values, kernel):
    places = jnp.arange(values.shape[0], dtype=jnp.int32)
    total = values * kernel[0]
    for offset_k in range(1, kernel.shape[0]):
        moved = jnp.concatenate(
            [jnp.zeros((offset_k, values.shape[1]), values.dtype), values[:-offset_k]], axis=0
        )
        valid = (places - offset_k >= starts)[:, None]
        total = total + jnp.where(valid, moved, jnp.zeros_like(moved)) * kernel[offset_k]
    return total


def geglu(gate_val, up_val):
    return jax.nn.gelu(gate_val, approximate=True) * up_val


def line_groups():
    ndp = lax.axis_size("dp")
    return [list(range(core, ndp, 2)) for core in range(2)]


def add_cores(grad, after=None):
    core = lax.axis_index("dp") % 2
    ndp = lax.axis_size("dp")
    split = halved(grad, ndp)
    route = [(i, i + 1 - 2 * (i % 2)) for i in range(ndp)]
    away = lax.dynamic_index_in_dim(split, 1 - core, 1, keepdims=False)
    kept = lax.dynamic_index_in_dim(split, core, 1, keepdims=False)
    taken = lax.ppermute(away, "dp", route)
    if after is not None:
        taken, after = lax.optimization_barrier((taken, after))
    both = kept.astype(F32) + taken.astype(F32)
    return both.astype(BF16).reshape(-1, grad.shape[1]), after


def sum_line(both):
    return lax.psum_scatter(
        both, "dp", scatter_dimension=0, axis_index_groups=line_groups(), tiled=True
    )


def rows_times(left, right):
    return lax.dot_general(left, right, (((1,), (1,)), ((), ())), preferred_element_type=F32)


def rows_back(lefts, rights):
    total = rows_times(lefts[0], rights[0])
    return total + rows_times(lefts[1], rights[1])


def inner_rows(left, right):
    return lax.dot_general(left, right, (((0,), (0,)), ((), ())), preferred_element_type=F32)


def halved(grad, ndp):
    return grad.reshape(ndp // 2, 2, grad.shape[0] // ndp, grad.shape[1])


def body(
    tokens,
    segments,
    cotangent,
    norm_gain,
    w_y,
    w_x,
    conv_w,
    gate_w,
    decay_param,
    w_out,
    mlp_gain,
    w_gate,
    w_up,
    w_down,
):
    ntensor = lax.axis_size("tensor")
    ndp = lax.axis_size("dp")
    nbits = log2_of(ntensor)
    tindex = lax.axis_index("tensor")
    own_rows, width = tokens.shape
    group_rows = own_rows * ntensor
    block_size = gate_w.shape[2]
    nblocks = gate_w.shape[1]
    dp_rows, channels = w_y.shape
    taps = conv_w.shape[0]
    offset = tindex * channels
    shape = jax.ShapeDtypeStruct
    gain_in = norm_gain.reshape(1, width)
    gain_mid = mlp_gain.reshape(1, width)
    seg_rows_of = own_rows // 128
    units = w_gate.shape[1]
    joins_wide = units % 128 == 0
    tiled = channels % 128 == 0
    w_yx = (w_y, w_x) if tiled else (jnp.concatenate([w_y, w_x], axis=1),)
    found = call_kernel(
        partial(enter_kernel, nbits, len(w_yx), joins_wide),
        (
            shape((group_rows, width), BF16),
            shape((ntensor, seg_rows_of, 128), jnp.int32),
            shape((dp_rows * ndp, 2 * channels), BF16),
            shape((dp_rows * ndp, channels), BF16),
        )
        + (shape((dp_rows, 2 * units), BF16),) * joins_wide,
        [pltpu.VMEM((1, width), F32)]
        + gather_sems(nbits)
        + [pltpu.SemaphoreType.DMA((ntensor - 1,)), pltpu.SemaphoreType.DMA((ntensor - 1,))]
        + [pltpu.SemaphoreType.DMA((3,))]
        + line_sems(ndp) * (len(w_yx) + 1),
        0,
        tokens,
        segments.reshape(seg_rows_of, 128),
        norm_gain.reshape(width // 128, 128),
        *w_yx,
        w_out,
        *((w_gate, w_up) if joins_wide else ()),
        far_in=tuple(range(3, 4 + 2 * joins_wide + len(w_yx))),
        far_out=(2, 3, 4) if joins_wide else (2, 3),
    )
    normed_rows, seg_all, wyx_loc, wout_loc = found[:4]
    if joins_wide:
        w_both = found[4]
    else:
        w_both = jnp.concatenate([w_gate, w_up], axis=1)
    w_both, w_down, normed_rows = lax.optimization_barrier((w_both, w_down, normed_rows))
    both_loc = lax.all_gather(w_both, "dp", axis=0, tiled=True)
    wd_loc = lax.all_gather(w_down, "dp", axis=0, tiled=True)
    seg_rows = seg_all.reshape(group_rows)
    starts = doc_starts(seg_rows, group_rows)
    conv_loc = lax.dynamic_slice_in_dim(conv_w, offset, channels, 1)
    decay_loc = lax.dynamic_slice_in_dim(decay_param, offset, channels, 0).reshape(1, channels)
    soft = jax.nn.softplus(decay_loc)
    slope_soft = jax.nn.sigmoid(decay_loc)
    half_blocks = (
        channels % block_size == block_size // 2 and ntensor % 2 == 0 and block_size % 256 == 0
    )
    since = (jnp.arange(group_rows, dtype=jnp.int32) - starts).astype(F32)[:, None]
    branches = jnp.dot(normed_rows, wyx_loc, preferred_element_type=F32)
    if half_blocks:
        span_blocks = channels // block_size + 1
        w_window = lax.dynamic_slice_in_dim(gate_w, offset // block_size, span_blocks, 1)
        taps_pad = jnp.concatenate([conv_loc, jnp.zeros((8 - taps, channels), F32)], axis=0)
        mixed_low, states, window, gate_pre, cot_rows = call_kernel(
            partial(recurrence_kernel, taps, nbits),
            (
                shape((group_rows, channels), BF16),
                shape((group_rows, channels), F32),
                shape((group_rows, span_blocks * block_size), BF16),
                shape((group_rows, 2 * channels), F32),
                shape((group_rows, width), BF16),
            ),
            [pltpu.SemaphoreType.DMA((1,)), pltpu.SemaphoreType.DMA((1,))]
            + fetch_scratch(nbits),
            5,
            branches,
            taps_pad,
            soft,
            since,
            w_window,
            cotangent,
        )
    else:
        branch_y, branch_x = branches[:, :channels], branches[:, channels:]
        (cot_rows,) = call_kernel(
            partial(fetch_kernel, nbits),
            (shape((group_rows, width), BF16),),
            fetch_scratch(nbits),
            5,
            cotangent,
        )
        rims = gate_rims(channels, block_size, ntensor, offset)
        own_dense = gate_dense(gate_w, offset, offset, channels)
        rim_dense = [gate_dense(gate_w, offset, rim.first, rim.width) for rim in rims]
        conv_out, conv_pull = jax.vjp(partial(causal_conv, starts), branch_x, conv_loc)
        conv_low = conv_out.astype(BF16)
        rim_cells = [rim.fetch(conv_low) for rim in rims]
        gate_pre = jnp.dot(conv_low, own_dense, preferred_element_type=F32)
        for cells, dense in zip(rim_cells, rim_dense):
            gate_pre = gate_pre + jnp.dot(cells, dense, preferred_element_type=F32)
        mixed_low, states = scan_call(
            forward_scan_kernel,
            (shape((group_rows, channels), BF16), shape((group_rows, channels), F32)),
            conv_low,
            gate_pre,
            branch_y,
            soft,
            since,
        )
    middle, mid_rows = call_kernel(
        partial(middle_kernel, nbits),
        (shape((own_rows, width), F32), shape((group_rows, width), BF16)),
        scatter_scratch(own_rows, width, nbits) + gather_sems(nbits),
        1,
        rows_times(mixed_low, wout_loc).astype(BF16),
        tokens,
        gain_mid,
    )
    pre = jnp.dot(mid_rows, both_loc, preferred_element_type=F32)
    hidden, act_pull = jax.vjp(geglu, pre[:, :units], pre[:, units:])
    hidden_low = hidden.astype(BF16)
    grad_wd = inner_rows(cot_rows, hidden_low).astype(BF16)
    sum_wd = lax.psum_scatter(grad_wd, "dp", scatter_dimension=0, tiled=True)
    grad_wd, wd_loc = lax.optimization_barrier((grad_wd, wd_loc))
    d_hidden = jnp.dot(cot_rows, wd_loc, preferred_element_type=F32)
    d_gate, d_up = act_pull(d_hidden)
    d_pre = jnp.concatenate([d_gate.astype(BF16), d_up.astype(BF16)], axis=1)
    grad_both = inner_rows(mid_rows, d_pre).astype(BF16)
    d_pre, grad_both = lax.optimization_barrier((d_pre, grad_both))
    d_mid_part = rows_times(d_pre, both_loc).astype(BF16)
    both_half, (d_mid_part, sum_wd) = add_cores(grad_both, (d_mid_part, sum_wd))
    sum_both = sum_line(both_half)
    d_mid_part, both_half = lax.optimization_barrier((d_mid_part, both_half))
    d_middle, d_mixer, d_gain_mid, ffn_part = call_kernel(
        partial(turn_kernel, nbits),
        (
            shape((own_rows, width), F32),
            shape((group_rows, width), BF16),
            shape((8, width), F32),
            shape((group_rows, width), BF16),
        ),
        scatter_scratch(own_rows, width, nbits) + gather_sems(nbits) + product_scratch(units),
        2,
        d_mid_part,
        cotangent,
        middle,
        gain_mid,
        hidden_low,
        wd_loc,
        far_in=(5,),
    )
    grad_wout = inner_rows(d_mixer, mixed_low).astype(BF16)
    d_mixed_in = jnp.dot(d_mixer, wout_loc, preferred_element_type=F32)
    unit = math.gcd(channels, block_size)
    merged = nbits <= 2
    if half_blocks:
        d_branches, gate_grad, own_small = call_kernel(
            partial(recurrence_back_kernel, taps),
            (
                shape((group_rows, 2 * channels), BF16),
                shape((channels // unit * 2, block_size, unit), BF16),
                shape((8, channels), F32),
            ),
            [
                pltpu.VMEM((group_rows, channels), F32),
                pltpu.VMEM((group_rows, 2 * channels), BF16),
                pltpu.VMEM((group_rows, unit), BF16),
                pltpu.VMEM((group_rows, unit), BF16),
                pltpu.VMEM((taps + 1, 8, channels), F32),
                pltpu.SemaphoreType.DMA((1,)),
                pltpu.SemaphoreType.DMA((1,)),
            ],
            6,
            d_mixed_in,
            window,
            gate_pre,
            branches,
            states,
            taps_pad,
            soft,
            slope_soft,
            since,
            w_window,
        )
        gate_grad = gate_grad.reshape(channels // unit * 2 * block_size, unit)
    else:
        d_conv, d_gate_low, d_branch_y, d_decay = scan_call(
            backward_scan_kernel,
            (
                shape((group_rows, channels), F32),
                shape((group_rows, 2 * channels), BF16),
                shape((group_rows, channels), BF16),
                shape((8, channels), F32),
            ),
            d_mixed_in,
            conv_low,
            gate_pre,
            branch_y,
            states,
            soft,
            slope_soft,
            since,
        )
        given = [rows_times(d_gate_low, dense).astype(BF16) for dense in rim_dense]
        taken = [rim.give(part) for rim, part in zip(rims, given)]
        d_conv_out = d_conv + rows_times(d_gate_low, own_dense)
        for rim, part in zip(rims, taken):
            d_conv_out = rim.add(d_conv_out, part)
        d_branch_x, grad_conv_loc = conv_pull(d_conv_out)
        d_branches = jnp.concatenate([d_branch_y, d_branch_x.astype(BF16)], axis=1)
        base = offset // block_size * block_size - rims[0].room
        window_rows = rims[0].window(channels)
        picked = jnp.zeros((window_rows, 2 * channels), F32)
        for first, cells in [(offset, conv_low)] + [(r.first, c) for r, c in zip(rims, rim_cells)]:
            part = inner_rows(cells, d_gate_low)
            same = same_block(first, cells.shape[1], offset, channels, block_size)
            part = jnp.where(jnp.concatenate([same, same], axis=1), part, 0.0)
            picked = lax.dynamic_update_slice(picked, part, (first - base, jnp.int32(0)))
        picked = picked.reshape(window_rows // block_size, block_size, 2, channels // unit, unit)
        gate_grad = picked.sum(axis=0).astype(BF16).transpose(2, 1, 0, 3)
        gate_grad = gate_grad.reshape(channels // unit * 2 * block_size, unit)
        own_small = jnp.concatenate(
            [
                grad_conv_loc,
                jnp.sum(d_decay, axis=0, keepdims=True),
                jnp.zeros((7 - taps, channels), F32),
            ],
            axis=0,
        )

    grad_wyx = inner_rows(normed_rows, d_branches).astype(BF16)
    d_normed = rows_times(d_branches, wyx_loc).astype(BF16)

    pieces = [halved(grad, ndp) for grad in (gate_grad, grad_wout, grad_wyx)]
    peers = ntensor - 1
    gate_rows = gate_grad.shape[0] // ndp
    dma = pltpu.SemaphoreType.DMA
    scratch = scatter_scratch(own_rows, width, nbits)
    scratch += line_scratch(ndp, gate_rows, unit) + line_scratch(ndp, dp_rows, channels)
    if tiled:
        scratch += line_scratch(ndp, dp_rows, channels) * 2
    else:
        scratch += line_scratch(ndp, dp_rows, 2 * channels)
    scratch += [
        pltpu.VMEM((8, width), F32),
        pltpu.VMEM((ntensor, 8, channels), F32),
        pltpu.VMEM((peers, 8, channels), F32),
        pltpu.VMEM((8, channels), F32),
        pltpu.VMEM((ndp - 1, 8, channels), F32),
    ]
    scratch += [dma((peers,)), dma((peers,)), dma((ndp - 1,)), dma((ndp - 1,))]
    scratch += [dma((peers,)), dma((peers,)), dma((peers + ndp,)), dma((peers + ndp,))]
    if merged:
        scratch += scatter_scratch(own_rows, width, nbits)
    found = call_kernel(
        partial(leave_kernel, nbits, tiled, merged),
        (shape((own_rows, width), F32),)
        + (shape((dp_rows, channels), F32),) * 3
        + (
            shape((ntensor, ndp // 2, 2, gate_rows, unit), BF16),
            shape((ntensor, 8, channels), F32),
        )
        + ((shape((own_rows, width), BF16),) if merged else ()),
        scratch,
        3,
        d_normed,
        tokens,
        d_middle,
        gain_in,
        own_small,
        d_gain_mid,
        *pieces,
        *((ffn_part, middle) if merged else ()),
        far_in=(6, 7, 8),
        vmem_bytes=60 * 1024 * 1024,
    )
    grad_input, sum_wout, sum_wy, sum_wx, gate_all, small_all = found[:6]
    if merged:
        mixed = found[6]
    else:
        (mixed,) = call_kernel(
            partial(result_kernel, nbits),
            (shape((own_rows, width), BF16),),
            scatter_scratch(own_rows, width, nbits),
            4,
            ffn_part,
            middle,
        )
    gate_all, sum_both = lax.optimization_barrier((gate_all, sum_both))
    found = finish(
        gate_all,
        small_all,
        (sum_wout, sum_wy, sum_wx),
        grad_input,
        mixed,
        sum_both,
        sum_wd,
        taps,
        gate_w.shape,
    )
    sum_gate, sum_wout, sum_wy, sum_wx, grad_input, mixed = found[:6]
    sum_wg, sum_wu, sum_wd, sum_conv, sum_decay, sum_gain_in, sum_gain_mid = found[6:]
    return (
        mixed,
        grad_input,
        sum_gain_in,
        sum_wy,
        sum_wx,
        sum_conv,
        sum_gate,
        sum_decay,
        sum_wout,
        sum_gain_mid,
        sum_wg,
        sum_wu,
        sum_wd,
    )


def solution(mesh):
    split = P(("dp", "tensor"), None)
    weight = P("dp", "tensor")
    return jax.shard_map(
        body,
        mesh=mesh,
        in_specs=(
            split,
            P(("dp", "tensor")),
            split,
            P(),
            weight,
            weight,
            P(),
            P(),
            P(),
            weight,
            P(),
            weight,
            weight,
            weight,
        ),
        out_specs=(
            split,
            split,
            P(),
            weight,
            weight,
            P(),
            P(),
            P(),
            weight,
            P(),
            weight,
            weight,
            weight,
        ),
        check_vma=False,
    )
```

```python
import math
from functools import partial

import jax
import jax.numpy as jnp
from jax import lax
from jax.experimental import pallas as pl
from jax.experimental.pallas import tpu as pltpu
from jax.sharding import PartitionSpec as P

EPSILON = 1e-06
MESH = pl.DeviceIdType.MESH
VMEM_BYTES = 56 * 1024 * 1024
CHUNK = 16
F32 = jnp.float32
BF16 = jnp.bfloat16


def subsets(bits):
    found = [()]
    for bit in bits:
        found = found + [chosen + (bit,) for chosen in found]
    return found


def flipped(index, bits):
    for bit in bits:
        mine = (index // (1 << bit)) % 2
        index = index + (1 - 2 * mine) * (1 << bit)
    return index


def log2_of(count):
    assert count & (count - 1) == 0
    return count.bit_length() - 1


def greet(axis_bits):
    barrier = pltpu.get_barrier_semaphore()
    for axis, bit in axis_bits:
        peer = flipped(lax.axis_index(axis), (bit,))
        pl.semaphore_signal(barrier, inc=1, device_id={axis: peer}, device_id_type=MESH)
    pl.semaphore_wait(barrier, len(axis_bits))


def halves_of(nbits, columns):
    half = columns // 2
    ups = tuple(range(nbits))
    return ((ups, 0, half), (ups[::-1], half, half))


class Gather:
    def __init__(self, ref, rows, nbits, send_sems, recv_sems):
        self.ref, self.rows, self.nbits = ref, rows, nbits
        self.sems = (send_sems, recv_sems)
        self.me = lax.axis_index("tensor")
        self.plan = []
        number = 0
        for half, (order, at, width) in enumerate(halves_of(nbits, ref.shape[1])):
            for step, bit in enumerate(order):
                for known in subsets(order[:step]):
                    self.plan.append((half, step, known, bit, at, width, number))
                    number += 1
        self.count = number

    def copy(self, item):
        half, step, known, bit, at, width, number = item
        row = pl.multiple_of(flipped(self.me, known) * self.rows, self.rows)
        piece = self.ref.at[pl.ds(row, self.rows), pl.ds(at, width)]
        return pltpu.make_async_remote_copy(
            src_ref=piece,
            dst_ref=piece,
            send_sem=self.sems[0].at[number],
            recv_sem=self.sems[1].at[number],
            device_id={"tensor": flipped(self.me, (bit,))},
            device_id_type=MESH,
        )

    def begin(self):
        for item in sorted(self.plan, key=lambda it: it[1]):
            if item[2] == ():
                self.copy(item).start()

    def advance(self, step):
        for item in self.plan:
            half, at_step, known, bit, at, width, number = item
            if at_step == step:
                self.copy(item).wait_recv()
                block = known + (bit,)
                for later in self.plan:
                    if later[0] == half and set(later[2]) == set(block):
                        self.copy(later).start()

    def finish(self, step=0):
        for at_step in range(step, self.nbits):
            self.advance(at_step)
        for item in self.plan:
            self.copy(item).wait_send()


def gather_copies(nbits):
    return 2 * ((1 << nbits) - 1)


class Scatter:
    def __init__(self, ref, landed, staged, rows, nbits, send_sems, recv_sems):
        self.ref, self.landed, self.staged = ref, landed, staged
        self.rows, self.nbits = rows, nbits
        self.sems = (send_sems, recv_sems)
        self.me = lax.axis_index("tensor")
        self.plan, self.slot = [], {}
        number = 0
        for half, (order, at, width) in enumerate(halves_of(nbits, ref.shape[1])):
            for step, bit in enumerate(order):
                for rest in subsets(order[step + 1 :])[::-1]:
                    self.plan.append((half, step, rest, bit, at, width, number))
                    if step > 0:
                        self.slot[number] = len(self.slot)
                    number += 1

    def copy(self, item):
        half, step, rest, bit, at, width, number = item
        if step == 0:
            row = pl.multiple_of(flipped(self.me, rest + (bit,)) * self.rows, self.rows)
            source = self.ref.at[pl.ds(row, self.rows), pl.ds(at, width)]
        else:
            source = self.staged.at[self.slot[number]]
        return pltpu.make_async_remote_copy(
            src_ref=source,
            dst_ref=self.landed.at[number],
            send_sem=self.sems[0].at[number],
            recv_sem=self.sems[1].at[number],
            device_id={"tensor": flipped(self.me, (bit,))},
            device_id_type=MESH,
        )

    def begin(self):
        for item in sorted(self.plan, key=lambda it: (len(it[2]) == 0)):
            if item[1] == 0:
                self.copy(item).start()

    def partial_sum(self, half, block, before, row, size):
        at, width = halves_of(self.nbits, self.ref.shape[1])[half][1:]
        base = pl.multiple_of(flipped(self.me, block) * self.rows + row, size)
        total = self.ref[pl.ds(base, size), pl.ds(at, width)].astype(F32)
        for it in self.plan:
            if it[0] == half and it[1] < before and set(it[2]) == set(block):
                total = total + self.landed[it[6], pl.ds(row, size), :].astype(F32)
        return total

    def advance(self, step):
        for half in range(2):
            for item in self.plan:
                if item[0] == half and item[1] == step:
                    self.copy(item).wait_recv()
            for item in self.plan:
                if item[0] == half and item[1] == step + 1:

                    def fill(row, item=item):
                        value = self.partial_sum(
                            item[0], item[2] + (item[3],), item[1], row, CHUNK
                        )
                        where = (self.slot[item[6]], pl.ds(row, CHUNK))
                        self.staged[where + (slice(None),)] = value.astype(BF16)

                    chunks(self.rows, fill)
                    self.copy(item).start()

    def run(self):
        for step in range(self.nbits):
            self.advance(step)

    def total(self, row, size):
        return jnp.concatenate(
            [self.partial_sum(half, (), self.nbits, row, size) for half in range(2)], axis=1
        )

    def drain(self):
        for item in self.plan:
            self.copy(item).wait_send()


def scatter_scratch(rows, columns, nbits):
    copies = gather_copies(nbits)
    later = max(1, copies - (1 << nbits))
    return [
        pltpu.VMEM((copies, rows, columns // 2), BF16),
        pltpu.VMEM((later, rows, columns // 2), BF16),
        pltpu.SemaphoreType.DMA((copies,)),
        pltpu.SemaphoreType.DMA((copies,)),
    ]


def gather_sems(nbits):
    copies = gather_copies(nbits)
    return [pltpu.SemaphoreType.DMA((copies,)), pltpu.SemaphoreType.DMA((copies,))]


def tensor_bits(nbits):
    return [("tensor", bit) for bit in range(nbits)]


def rms_scale_of(values):
    return lax.rsqrt(jnp.mean(values * values, axis=-1, keepdims=True) + EPSILON)


def chunks(rows, body):
    def step(i, carry):
        body(pl.multiple_of(i * CHUNK, CHUNK))
        return carry

    lax.fori_loop(0, rows // CHUNK, step, 0)


def own_row(row, rows):
    return pl.multiple_of(lax.axis_index("tensor") * rows + row, CHUNK)


def dp_place():
    me = lax.axis_index("dp")
    return me // 2, me % 2, lax.axis_size("dp") // 2


def dp_index(chip, core):
    return chip * 2 + core


UP, DOWN = 1, -1


class LineGather:
    def __init__(self, own, whole, send_sems, recv_sems, columns=None):
        self.own, self.whole = own, whole
        self.sems = (send_sems, recv_sems)
        self.chip, self.core, self.chips = dp_place()
        self.rows = own.shape[0]
        self.columns = slice(None) if columns is None else columns

    def block(self, chip):
        row = pl.multiple_of(dp_index(chip, self.core) * self.rows, self.rows)
        return self.whole.at[pl.ds(row, self.rows), self.columns]

    def has(self, way, distance):
        return self.chip >= distance if way == UP else self.chip + distance < self.chips

    def number(self, way, distance):
        return (0 if way == UP else self.chips) + distance

    def along(self, way, distance):
        block = self.block(self.chip - way * distance)
        return pltpu.make_async_remote_copy(
            src_ref=self.own if distance == 0 else block,
            dst_ref=block,
            send_sem=self.sems[0].at[self.number(way, distance)],
            recv_sem=self.sems[1].at[self.number(way, distance + 1)],
            device_id={"dp": dp_index(self.chip + way, self.core)},
            device_id_type=MESH,
        )

    def arrival(self, way, distance):
        block = self.block(self.chip - way * distance)
        return pltpu.make_async_remote_copy(
            src_ref=block,
            dst_ref=block,
            send_sem=self.sems[0].at[self.number(way, distance)],
            recv_sem=self.sems[1].at[self.number(way, distance)],
            device_id={"dp": dp_index(self.chip + way, self.core)},
            device_id_type=MESH,
        )

    def across(self, way, distance):
        block = self.block(self.chip - way * distance)
        number = 2 * self.chips + self.number(way, distance)
        return pltpu.make_async_remote_copy(
            src_ref=self.own if distance == 0 else block,
            dst_ref=block,
            send_sem=self.sems[0].at[number],
            recv_sem=self.sems[1].at[number],
            device_id={"dp": dp_index(self.chip, 1 - self.core)},
            device_id_type=MESH,
        )

    def local(self):
        return pltpu.make_async_copy(
            self.own, self.block(self.chip), self.sems[0].at[4 * self.chips]
        )

    def begin(self):
        for way in (UP, DOWN):

            @pl.when(self.has(-way, 1))
            def _(way=way):
                self.along(way, 0).start()

        self.across(UP, 0).start()
        self.local().start()

    def pass_on(self, distance):
        for way in (UP, DOWN):

            @pl.when(self.has(way, distance))
            def _(way=way):
                self.arrival(way, distance).wait_recv()

                @pl.when(self.has(-way, 1))
                def _():
                    self.along(way, distance).start()

                self.across(way, distance).start()

    def finish(self):
        self.across(UP, 0).wait()
        self.local().wait()
        for way in (UP, DOWN):
            for distance in range(self.chips):

                @pl.when(self.has(way, distance) & self.has(-way, 1))
                def _(way=way, distance=distance):
                    self.along(way, distance).wait_send()

                if distance:

                    @pl.when(self.has(way, distance))
                    def _(way=way, distance=distance):
                        self.across(way, distance).wait()


def line_sems(ndp):
    chips = ndp // 2
    return [pltpu.SemaphoreType.DMA((4 * chips + 1,)), pltpu.SemaphoreType.DMA((4 * chips + 1,))]


def greet_peers(nbits, all_tensor, whole_dp):
    me = lax.axis_index("tensor")
    chip, core, chips = dp_place()
    barrier = pltpu.get_barrier_semaphore()

    def signal(target):
        pl.semaphore_signal(barrier, inc=1, device_id=target, device_id_type=MESH)

    met = 0
    for chosen in subsets(tuple(range(nbits))):
        if chosen and (all_tensor or len(chosen) == 1):
            signal({"tensor": flipped(me, chosen)})
            met += 1
    if whole_dp:
        for shift in range(chips):
            for turn in range(2):
                if (shift, turn) != (0, 0):
                    other = dp_index((chip + shift) % chips, core + turn * (1 - 2 * core))
                    signal({"dp": other})
                    met += 1
    else:
        signal({"dp": dp_index(chip, 1 - core)})
        met += 1

        for shift in sorted({1 % chips, chips - 1} - {0}):
            signal({"dp": dp_index((chip + shift) % chips, core)})
            met += 1

    pl.semaphore_wait(barrier, met)


def widen(rows, wide):
    for row in range(rows.shape[0]):
        wide[:, row * 128 : (row + 1) * 128] = rows[row : row + 1, :]


def enter_kernel(
    nbits, parts_yx, tokens, seg, gain, *refs
):
    w_yx, w_out = refs[:parts_yx], refs[parts_yx]
    normed_all, seg_all, wyx_all, wout_all, gain_row, s0, r0, s2, r2, l0, *line = refs[
        parts_yx + 1 :
    ]
    rows = tokens.shape[0]
    me = lax.axis_index("tensor")
    peers = [chosen for chosen in subsets(tuple(range(nbits))) if chosen]
    greet_peers(nbits, True, False)
    width = wyx_all.shape[1] // parts_yx
    lines = [
        LineGather(
            own,
            wyx_all,
            line[2 * number],
            line[2 * number + 1],
            pl.ds(number * width, width) if parts_yx > 1 else None,
        )
        for number, own in enumerate(w_yx)
    ]
    lines.append(LineGather(w_out, wout_all, *line[2 * parts_yx : 2 * parts_yx + 2]))
    for item in lines:
        item.begin()
    widen(gain, gain_row)

    def norm(row):
        values = tokens[pl.ds(row, CHUNK), :].astype(F32)
        scaled = values * rms_scale_of(values) * gain_row[...]
        normed_all[pl.ds(own_row(row, rows), CHUNK), :] = scaled.astype(BF16)

    chunks(rows, norm)
    gather = Gather(normed_all, rows, nbits, s0, r0)
    gather.begin()
    seg_own = pltpu.make_async_copy(seg, seg_all.at[me], l0.at[0])
    seg_own.start()
    seg_copies = [
        pltpu.make_async_remote_copy(
            src_ref=seg,
            dst_ref=seg_all.at[me],
            send_sem=s2.at[number],
            recv_sem=r2.at[number],
            device_id={"tensor": flipped(me, chosen)},
            device_id_type=MESH,
        )
        for number, chosen in enumerate(peers)
    ]
    for copy in seg_copies:
        copy.start()
    chips = lines[0].chips
    for item in lines:
        item.pass_on(1)
    gather.advance(0)
    for distance in range(2, chips):
        for item in lines:
            item.pass_on(distance)
    gather.finish(1)
    for item in lines:
        item.finish()
    for copy in seg_copies:
        copy.wait()
    seg_own.wait()


class Fetch:
    def __init__(self, nbits, cot, cot_all, s0, r0, l0):
        rows = cot.shape[0]
        own = pl.multiple_of(lax.axis_index("tensor") * rows, rows)
        self.local = pltpu.make_async_copy(cot, cot_all.at[pl.ds(own, rows), :], l0.at[0])
        self.gather = Gather(cot_all, rows, nbits, s0, r0)

    def begin(self):
        self.local.wait()
        self.gather.begin()

    def advance(self):
        self.gather.advance(0)

    def finish(self):
        self.gather.finish(1)


def fetch_scratch(nbits):
    return gather_sems(nbits) + [pltpu.SemaphoreType.DMA((1,))]


def fetch_kernel(nbits, cot, cot_all, *sems):
    greet(tensor_bits(nbits))
    fetch = Fetch(nbits, cot, cot_all, *sems)
    fetch.local.start()
    fetch.begin()
    fetch.advance()
    fetch.finish()


def middle_kernel(
    nbits, mixer, tokens, gain, middle, mid_all, landed, staged, s0, r0, s1, r1
):
    rows = tokens.shape[0]
    greet(tensor_bits(nbits))
    scatter = Scatter(mixer, landed, staged, rows, nbits, s0, r0)
    scatter.begin()
    scatter.run()

    def norm(row):
        values = tokens[pl.ds(row, CHUNK), :].astype(F32) + scatter.total(row, CHUNK)
        middle[pl.ds(row, CHUNK), :] = values
        scaled = values * rms_scale_of(values) * gain[...]
        mid_all[pl.ds(own_row(row, rows), CHUNK), :] = scaled.astype(BF16)

    chunks(rows, norm)
    gather = Gather(mid_all, rows, nbits, s1, r1)
    gather.begin()
    gather.finish()
    scatter.drain()


def result_kernel(nbits, ffn, middle, mixed, landed, staged, s0, r0):
    rows = middle.shape[0]
    greet(tensor_bits(nbits))
    scatter = Scatter(ffn, landed, staged, rows, nbits, s0, r0)
    scatter.begin()
    scatter.run()

    def add(row):
        values = middle[pl.ds(row, CHUNK), :] + scatter.total(row, CHUNK)
        mixed[pl.ds(row, CHUNK), :] = values.astype(BF16)

    chunks(rows, add)
    scatter.drain()


def norm_pull(values, gain, cotangent):
    scale = rms_scale_of(values)
    unit = values * scale
    inner = cotangent * gain
    back = scale * (inner - unit * jnp.mean(inner * unit, axis=-1, keepdims=True))
    return back, cotangent * unit


def eight_rows(values):
    total = values[0:8]
    for at in range(8, CHUNK, 8):
        total = total + values[at : at + 8]
    return total


class Product:
    def __init__(self, left, right, out, held, sems):
        self.left, self.right, self.out = left, right, out
        self.held, self.sems = held, sems
        self.width = held.shape[1]
        self.count = right.shape[0] // self.width
        self.done = 0

    def fetch(self, block):
        return pltpu.make_async_copy(
            self.right.at[pl.ds(block * self.width, self.width), :],
            self.held.at[block % 2],
            self.sems.at[block % 2],
        )

    def begin(self):
        self.fetch(0).start()

    def work(self, blocks):
        for block in range(self.done, min(self.done + blocks, self.count)):
            if block + 1 < self.count:
                self.fetch(block + 1).start()
            self.fetch(block).wait()

            def rows(span, block=block):
                found = times_transposed(self.left[span, :], self.held[block % 2])
                at = slice(block * self.width, (block + 1) * self.width)
                self.out[span, at] = found.astype(BF16)

            parts(self.left.shape[0], rows)
        self.done = min(self.done + blocks, self.count)


PRODUCT_BLOCK = 256


def product_scratch(depth):
    return [pltpu.VMEM((2, PRODUCT_BLOCK, depth), BF16), pltpu.SemaphoreType.DMA((2,))]


def turn_kernel(
    nbits,
    d_norm,
    cot,
    middle,
    gain,
    hidden,
    w_down,
    d_middle,
    d_mixer,
    d_gain,
    ffn,
    landed,
    staged,
    s0,
    r0,
    s1,
    r1,
    *product,
):
    rows = middle.shape[0]
    ahead = Product(hidden, w_down, ffn, *product)
    ahead.begin()
    greet(tensor_bits(nbits))
    scatter = Scatter(d_norm, landed, staged, rows, nbits, s0, r0)
    scatter.begin()
    d_gain[...] = jnp.zeros_like(d_gain)
    ahead.work(4)
    for step in range(nbits):
        scatter.advance(step)
        if step + 1 < nbits:
            ahead.work(2)

    def pull(row):
        span = pl.ds(row, CHUNK)
        back, gains = norm_pull(middle[span, :], gain[...], scatter.total(row, CHUNK))
        values = cot[span, :].astype(F32) + back
        d_middle[span, :] = values
        d_mixer[pl.ds(own_row(row, rows), CHUNK), :] = values.astype(BF16)
        d_gain[...] += eight_rows(gains)

    chunks(rows, pull)
    gather = Gather(d_mixer, rows, nbits, s1, r1)
    gather.begin()
    ahead.work(2)
    gather.advance(0)
    ahead.work(ahead.count)
    gather.finish(1)
    scatter.drain()


class LineSum:
    def __init__(self, whole, kept, swapped, staged, landed, send_sems, recv_sems, columns=None):
        self.whole, self.kept, self.swapped = whole, kept, swapped
        self.staged, self.landed = staged, landed
        self.sems = (send_sems, recv_sems)
        self.columns = columns
        self.chip, self.core, self.chips = dp_place()
        self.rows = whole.shape[2]

    def half(self, core):
        if self.columns is None:
            return self.whole.at[:, core]
        return self.whole.at[:, core, :, self.columns]

    def local(self):
        return pltpu.make_async_copy(
            self.half(self.core), self.kept, self.sems[0].at[2 * self.chips]
        )

    def swap(self):
        return pltpu.make_async_remote_copy(
            src_ref=self.half(1 - self.core),
            dst_ref=self.swapped,
            send_sem=self.sems[0].at[0],
            recv_sem=self.sems[1].at[0],
            device_id={"dp": dp_index(self.chip, 1 - self.core)},
            device_id_type=MESH,
        )

    def has(self, way, distance):
        return self.chip + distance < self.chips if way == UP else self.chip >= distance

    def slot(self, way, distance):
        return (0 if way == UP else self.chips - 1) + distance

    def hop(self, way, distance):
        return pltpu.make_async_remote_copy(
            src_ref=self.staged.at[self.slot(way, distance - 1)],
            dst_ref=self.landed.at[self.slot(way, distance - 1)],
            send_sem=self.sems[0].at[1 + self.slot(way, distance - 1)],
            recv_sem=self.sems[1].at[1 + self.slot(way, distance - 1)],
            device_id={"dp": dp_index(self.chip + way, self.core)},
            device_id_type=MESH,
        )

    def arrival(self, way, distance):
        number = self.slot(way, distance)
        return pltpu.make_async_remote_copy(
            src_ref=self.landed.at[number],
            dst_ref=self.landed.at[number],
            send_sem=self.sems[0].at[1 + number],
            recv_sem=self.sems[1].at[1 + number],
            device_id={"dp": dp_index(self.chip - way, self.core)},
            device_id_type=MESH,
        )

    def begin(self):
        self.swap().start()
        self.local().start()

    def both(self, chip, span):
        return self.kept[chip, span, :].astype(F32) + self.swapped[chip, span, :].astype(F32)

    def send(self, distance):
        if distance == self.chips - 1:
            self.local().wait()
            self.swap().wait_recv()
        for way in (UP, DOWN):

            @pl.when(self.has(way, distance))
            def _(way=way):
                chip = self.chip + way * distance
                slot = self.slot(way, distance - 1)

                def first(row):
                    span = pl.ds(row, CHUNK)
                    self.staged[slot, span, :] = self.both(chip, span).astype(BF16)

                def later(row):
                    span = pl.ds(row, CHUNK)
                    total = self.both(chip, span) + self.landed[
                        self.slot(way, distance), span, :
                    ].astype(F32)
                    self.staged[slot, span, :] = total.astype(BF16)

                if distance == self.chips - 1:
                    chunks(self.rows, first)
                else:

                    @pl.when(self.has(-way, 1))
                    def _():
                        self.arrival(way, distance).wait_recv()
                        chunks(self.rows, later)

                    @pl.when(jnp.logical_not(self.has(-way, 1)))
                    def _():
                        chunks(self.rows, first)

                self.hop(way, distance).start()

    def finish(self, store):
        below, above = self.has(DOWN, 1), self.has(UP, 1)

        def fill(slots):
            for way in slots:
                self.arrival(way, 0).wait_recv()

            def one(row):
                span = pl.ds(row, CHUNK)
                total = self.both(self.chip, span)
                for way in slots:
                    total = total + self.landed[self.slot(way, 0), span, :].astype(F32)
                store(span, total)

            chunks(self.rows, one)

        @pl.when(below & above)
        def _():
            fill((UP, DOWN))

        @pl.when(jnp.logical_not(above))
        def _():
            fill((UP,))

        @pl.when(jnp.logical_not(below))
        def _():
            fill((DOWN,))

    def drain(self):
        self.swap().wait_send()
        for way in (UP, DOWN):
            for distance in range(1, self.chips):

                @pl.when(self.has(way, distance))
                def _(way=way, distance=distance):
                    self.hop(way, distance).wait_send()


def line_scratch(ndp, rows, columns):
    chips = ndp // 2
    return [
        pltpu.VMEM((chips, rows, columns), BF16),
        pltpu.VMEM((chips, rows, columns), BF16),
        pltpu.VMEM((2 * chips - 2, rows, columns), BF16),
        pltpu.VMEM((2 * chips - 2, rows, columns), BF16),
        pltpu.SemaphoreType.DMA((2 * chips + 1,)),
        pltpu.SemaphoreType.DMA((2 * chips + 1,)),
    ]


RING = 6


def leave_kernel(nbits, tiled, *refs):
    refs = list(refs)

    def take(count):
        taken = refs[:count]
        del refs[:count]
        return taken

    d_norm, tokens, d_middle, gain, own_small, d_gain_mid = take(6)
    pieces = take(2)
    grad_input, sum_y, sum_x, gate_all, small_all = take(5)
    landed, staged, s0, r0 = take(4)
    share = small_all.shape[2]
    gate = LineSum(pieces[0], *take(RING))
    if tiled:
        lines = [LineSum(pieces[1], *take(RING), pl.ds(at, share)) for at in (0, share)]
    else:
        lines = [LineSum(pieces[1], *take(RING))]
    d_gain, gains, gains_landed, small, small_landed = take(5)
    gain_s, gain_r, vec_s, vec_r, join_s, join_r, gate_s, gate_r = take(8)
    rows = tokens.shape[0]
    me = lax.axis_index("tensor")
    chip, core, chips = dp_place()
    peers = [chosen for chosen in subsets(tuple(range(nbits))) if chosen]
    others = [(shift, turn) for shift in range(chips) for turn in range(2)][1:]
    greet_peers(nbits, True, True)
    for line in [gate] + lines:
        line.begin()
    scatter = Scatter(d_norm, landed, staged, rows, nbits, s0, r0)
    scatter.begin()
    d_gain[...] = jnp.zeros_like(d_gain)
    far = list(range(chips - 1, 0, -1))
    for number in range(max(len(far), len(lines))):
        if number < len(far):
            gate.send(far[number])
        if number < len(lines):
            lines[number].send(far[0])
    scatter.advance(0)
    for distance in far[1:-1]:
        for line in lines:
            line.send(distance)
    for step in range(1, nbits):
        scatter.advance(step)

    def pull(row):
        span = pl.ds(row, CHUNK)
        back, parts = norm_pull(
            tokens[span, :].astype(F32), gain[...], scatter.total(row, CHUNK)
        )
        grad_input[span, :] = d_middle[span, :] + back
        d_gain[...] += eight_rows(parts)

    chunks(rows, pull)
    def store_gate(span, value):
        gate_all[me, chip, core, span, :] = value.astype(BF16)

    def gate_copy(number, ref, target):
        return pltpu.make_async_remote_copy(
            src_ref=ref,
            dst_ref=ref,
            send_sem=gate_s.at[number],
            recv_sem=gate_r.at[number],
            device_id=target,
            device_id_type=MESH,
        )

    def gate_line(shift):
        target = {"dp": dp_index((chip + shift) % chips, core)}
        return gate_copy(shift - 1, gate_all.at[me, chip, core], target)

    def gate_tensor(number, chosen):
        target = {"tensor": flipped(me, chosen)}
        return gate_copy(chips - 1 + number, gate_all.at[me, :, core], target)

    def gate_core():
        target = {"dp": dp_index(chip, 1 - core)}
        return gate_copy(chips - 1 + len(peers), gate_all.at[:, :, core], target)

    def start_gate():
        gate.finish(store_gate)
        for shift in range(1, chips):
            gate_line(shift).start()

    top = jnp.sum(d_gain[...], axis=0, keepdims=True)
    low = jnp.sum(d_gain_mid[...], axis=0, keepdims=True)
    place8 = lax.broadcasted_iota(jnp.int32, (8, share), 0)
    for index in range(1 << nbits):
        span = slice(index * share, (index + 1) * share)
        gains[index] = jnp.where(
            place8 == 6, top[:, span], jnp.where(place8 == 7, low[:, span], 0.0)
        )

    def gain_copy(number, chosen):
        peer = flipped(me, chosen)
        return pltpu.make_async_remote_copy(
            src_ref=gains.at[peer],
            dst_ref=gains_landed.at[number],
            send_sem=gain_s.at[number],
            recv_sem=gain_r.at[number],
            device_id={"tensor": peer},
            device_id_type=MESH,
        )

    for number, chosen in enumerate(peers):
        gain_copy(number, chosen).start()
    start_gate()
    if len(far) > 1:
        for line in lines:
            line.send(far[-1])
    total = own_small[...] + gains[me]
    for number, chosen in enumerate(peers):
        gain_copy(number, chosen).wait_recv()
        total = total + gains_landed[number]
    small[...] = total

    def vec_copy(number, shift, turn):
        other = dp_index((chip + shift) % chips, core + turn * (1 - 2 * core))
        return pltpu.make_async_remote_copy(
            src_ref=small,
            dst_ref=small_landed.at[number],
            send_sem=vec_s.at[number],
            recv_sem=vec_r.at[number],
            device_id={"dp": other},
            device_id_type=MESH,
        )

    for number, (shift, turn) in enumerate(others):
        vec_copy(number, shift, turn).start()

    for shift in range(1, chips):
        gate_line(shift).wait_recv()
    for number, chosen in enumerate(peers):
        gate_tensor(number, chosen).start()
    total = small[...]
    for number, (shift, turn) in enumerate(others):
        vec_copy(number, shift, turn).wait_recv()
        total = total + small_landed[number]
    small_all[me] = total

    def join_copy(number, chosen):
        return pltpu.make_async_remote_copy(
            src_ref=small_all.at[me],
            dst_ref=small_all.at[me],
            send_sem=join_s.at[number],
            recv_sem=join_r.at[number],
            device_id={"tensor": flipped(me, chosen)},
            device_id_type=MESH,
        )

    for number, chosen in enumerate(peers):
        join_copy(number, chosen).start()
    for number, chosen in enumerate(peers):
        gate_tensor(number, chosen).wait_recv()
    gate_core().start()

    def store_in(*targets):
        def store(span, value):
            for number, ref in enumerate(targets):
                ref[span, :] = value[:, number * share : (number + 1) * share]

        return store

    if tiled:
        lines[0].finish(store_in(sum_y))
        lines[1].finish(store_in(sum_x))
    else:
        lines[0].finish(store_in(sum_y, sum_x))
    gate_core().wait()
    for shift in range(1, chips):
        gate_line(shift).wait_send()
    for number, chosen in enumerate(peers):
        gate_tensor(number, chosen).wait_send()
        gain_copy(number, chosen).wait_send()
        join_copy(number, chosen).wait()
    for number, (shift, turn) in enumerate(others):
        vec_copy(number, shift, turn).wait_send()
    scatter.drain()
    for line in [gate] + lines:
        line.drain()


def in_vmem(count):
    return [pl.BlockSpec(memory_space=pltpu.VMEM)] * count


def call_kernel(kernel, outs, scratch, number, *operands, far_in=(), far_out=(), cost_us=1):
    vmem = pl.BlockSpec(memory_space=pltpu.VMEM)
    far = pl.BlockSpec(memory_space=pl.ANY)
    return pl.pallas_call(
        kernel,
        out_shape=outs,
        in_specs=[far if i in far_in else vmem for i in range(len(operands))],
        out_specs=tuple(far if i in far_out else vmem for i in range(len(outs))),
        scratch_shapes=scratch,
        cost_estimate=pl.CostEstimate(
            flops=0, bytes_accessed=cost_us * 1_000_000, transcendentals=0
        ),
        compiler_params=pltpu.CompilerParams(
            collective_id=number, has_side_effects=True, vmem_limit_bytes=VMEM_BYTES
        ),
    )(*operands)


def sigmoid(values):
    return 1.0 / (1.0 + jnp.exp(-values))


def one_minus_exp(values):
    series = values / 7.0 + 1.0
    for order in (6.0, 5.0, 4.0, 3.0, 2.0):
        series = 1.0 + series * values / order
    return jnp.where(values > -0.3, -values * series, 1.0 - jnp.exp(values))


GELU_K = 0.7978845608028654
GELU_C = 0.044715


def gelu_parts(values):
    square = values * values
    bent = jnp.tanh(GELU_K * values * (1.0 + GELU_C * square))
    gelu = 0.5 * values * (1.0 + bent)
    slope = 0.5 * (1.0 + bent) + 0.5 * values * (1.0 - bent * bent) * GELU_K * (
        1.0 + 3.0 * GELU_C * square
    )
    return gelu, slope


def gate_terms(gate_a, gate_x, soft, since):
    sig_a = sigmoid(gate_a)
    sig_x = sigmoid(gate_x)
    log_decay = -8.0 * sig_a * soft
    decay = jnp.exp(log_decay)
    scale = jnp.sqrt(one_minus_exp(2.0 * log_decay))
    keep = since > 0.5
    return sig_a, sig_x, decay, jnp.where(keep, scale, 1.0), keep


def scan_down(decay, value, carry):
    place = lax.broadcasted_iota(jnp.int32, decay.shape, 0)
    for shift in (1, 2, 4):
        past = place >= shift
        moved = pltpu.roll(value, shift, 0)
        value = jnp.where(past, decay * moved + value, value)
        decay = jnp.where(past, decay * pltpu.roll(decay, shift, 0), decay)
    return decay * carry + value


def scan_up(decay, value, carry):
    place = lax.broadcasted_iota(jnp.int32, decay.shape, 0)
    factor = jnp.where(place < 7, pltpu.roll(decay, 7, 0), 1.0)
    for shift in (1, 2, 4):
        past = place < 8 - shift
        moved = pltpu.roll(value, 8 - shift, 0)
        value = jnp.where(past, factor * moved + value, value)
        factor = jnp.where(past, factor * pltpu.roll(factor, 8 - shift, 0), factor)
    return factor * carry + value


def forward_scan(conv_rows, gates, branch_y, soft, since, mixed, states, between=()):
    total_rows, width = states.shape

    def step(i, carry):
        row = pl.multiple_of(i * CHUNK, CHUNK)
        span = pl.ds(row, CHUNK)
        values = conv_rows(span).astype(F32)
        kept = []
        for at in range(0, CHUNK, 8):
            tile = pl.ds(row + at, 8)
            sig_a, sig_x, decay, scale, keep = gate_terms(
                gates[tile, :width], gates[tile, width:], soft[...], since[tile, :]
            )
            given = values[at : at + 8] * sig_x * scale
            state = scan_down(jnp.where(keep, decay, 0.0), given, carry)
            carry = state[7:8]
            states[tile, :] = state
            kept.append(state * gelu_parts(branch_y[tile, :])[0])
        mixed[span, :] = jnp.concatenate(kept, axis=0).astype(BF16)
        return carry

    steps, stretches = total_rows // CHUNK, len(between) + 1
    carry = jnp.zeros((1, width), F32)
    for stretch in range(stretches):
        first, last = stretch * steps // stretches, (stretch + 1) * steps // stretches
        carry = lax.fori_loop(first, last, step, carry)
        if stretch < len(between):
            between[stretch]()


def forward_scan_kernel(conv, gates, branch_y, soft, since, mixed, states):
    forward_scan(lambda span: conv[span, :], gates, branch_y, soft, since, mixed, states)


def backward_scan(
    d_mixed, conv_rows, gates, branch_y, states, soft, slope_soft, since, d_conv, d_gates, d_branch, d_decay
):
    total_rows, width = states.shape
    d_decay[...] = jnp.zeros_like(d_decay)

    def step(i, carry):
        row = pl.multiple_of(total_rows - CHUNK - i * CHUNK, CHUNK)
        span = pl.ds(row, CHUNK)
        values = conv_rows(span).astype(F32)
        kept = []
        for at in range(CHUNK - 8, -1, -8):
            tile = pl.ds(row + at, 8)
            soft_row = soft[...]
            sig_a, sig_x, decay, scale, keep = gate_terms(
                gates[tile, :width], gates[tile, width:], soft_row, since[tile, :]
            )
            value = values[at : at + 8]
            gelu, slope = gelu_parts(branch_y[tile, :])
            state = states[tile, :]
            upper = d_mixed[tile, :]
            held = jnp.where(keep, decay, 0.0)
            lam = scan_up(held, upper * gelu, carry)
            carry = held[0:1] * lam[0:1]
            d_conv[tile, :] = lam * sig_x * scale
            d_x = lam * value * scale * sig_x * (1.0 - sig_x)
            given = value * sig_x
            d_log = lam * (state - given * scale - given * decay * decay / scale)
            d_log = jnp.where(keep, d_log, 0.0)
            d_a = d_log * (-8.0 * soft_row) * sig_a * (1.0 - sig_a)
            d_decay[...] += d_log * (-8.0 * sig_a) * slope_soft[...]
            kept.append((d_a, d_x, upper * state * slope))
        kept = kept[::-1]
        d_gates[span, :width] = jnp.concatenate([k[0] for k in kept], axis=0).astype(BF16)
        d_gates[span, width:] = jnp.concatenate([k[1] for k in kept], axis=0).astype(BF16)
        d_branch[span, :] = jnp.concatenate([k[2] for k in kept], axis=0).astype(BF16)
        return carry

    lax.fori_loop(0, total_rows // CHUNK, step, jnp.zeros((1, width), F32))


def backward_scan_kernel(
    d_mixed, conv, gates, branch_y, states, soft, slope_soft, since, d_conv, d_gates, d_branch, d_decay
):
    backward_scan(
        d_mixed,
        lambda span: conv[span, :],
        gates,
        branch_y,
        states,
        soft,
        slope_soft,
        since,
        d_conv,
        d_gates,
        d_branch,
        d_decay,
    )


def times_transposed(left, right):
    return lax.dot_general(left, right, (((1,), (1,)), ((), ())), preferred_element_type=F32)


class HalfBlocks:
    def __init__(self, channels, block):
        self.odd = lax.axis_index("tensor") % 2
        self.half = block // 2
        self.block = block
        self.count = channels // block + 1
        self.channels = channels
        self.own = pl.multiple_of(self.odd * self.half, self.half)
        self.shared = (1 - self.odd) * (self.count - 1)
        self.mine_in_block = pl.multiple_of(self.odd * self.half, self.half)
        self.other_in_block = pl.multiple_of((1 - self.odd) * self.half, self.half)
        self.mine = pl.multiple_of((1 - self.odd) * (channels - self.half), self.half)
        self.pair = {"tensor": lax.axis_index("tensor") + 1 - 2 * self.odd}

    def full(self, index):
        block = index + self.odd
        return block, pl.multiple_of(index * self.block + self.odd * self.half, self.half)

    def span(self, block):
        return pl.ds(pl.multiple_of(block * self.block, self.block), self.block)

    def shared_part(self, start):
        return pl.ds(pl.multiple_of(self.shared * self.block + start, self.half), self.half)


PART = 256


def parts(rows, body):
    def step(i, carry):
        body(pl.ds(pl.multiple_of(i * PART, PART), PART))
        return carry

    lax.fori_loop(0, rows // PART, step, 0)


def recurrence_kernel(
    taps,
    nbits,
    branches,
    tap_rows,
    soft,
    since,
    weights,
    cot,
    mixed,
    states,
    window,
    gates,
    cot_all,
    send,
    recv,
    *sems,
):
    total_rows, width = states.shape
    block = weights.shape[2]
    place = HalfBlocks(width, block)
    branch_y, branch_x = branches.at[:, :width], branches.at[:, width:]
    greet(tensor_bits(nbits))
    fetch = Fetch(nbits, cot, cot_all, *sems)
    fetch.local.start()

    def conv(i, before):
        row = pl.multiple_of(i * CHUNK, CHUNK)
        kept = []
        for at in range(0, CHUNK, 8):
            tile = pl.ds(row + at, 8)
            values = branch_x[tile, :]
            line = lax.broadcasted_iota(jnp.int32, values.shape, 0)
            total = values * tap_rows[0:1, :]
            for tap in range(1, taps):
                moved = jnp.where(
                    line < tap, pltpu.roll(before, tap, 0), pltpu.roll(values, tap, 0)
                )
                moved = jnp.where(since[tile, :] > tap - 0.5, moved, 0.0)
                total = total + moved * tap_rows[tap : tap + 1, :]
            kept.append(total)
            before = values
        window[pl.ds(row, CHUNK), pl.ds(place.own, width)] = jnp.concatenate(
            kept, axis=0
        ).astype(BF16)
        return before

    lax.fori_loop(0, total_rows // CHUNK, conv, jnp.zeros((8, width), F32))
    source = window.at[:, place.shared_part(place.mine_in_block)]
    away = pl.multiple_of(place.odd * (place.count - 1) * block + place.mine_in_block, place.half)
    rim = pltpu.make_async_remote_copy(
        src_ref=source,
        dst_ref=window.at[:, pl.ds(away, place.half)],
        send_sem=send.at[0],
        recv_sem=recv.at[0],
        device_id=place.pair,
        device_id_type=MESH,
    )
    rim.start()
    fetch.begin()

    def full(span):
        for index in range(place.count - 1):
            number, at = place.full(index)
            cells = window[span, place.span(number)]
            for s in range(2):
                gates[span, pl.ds(s * width + at, block)] = jnp.dot(
                    cells, weights[s, number], preferred_element_type=F32
                )

    parts(total_rows, full)
    rim.wait()

    def shared(span):
        cells = window[span, place.span(place.shared)]
        for s in range(2):
            gates[span, pl.ds(s * width + place.mine, place.half)] = jnp.dot(
                cells,
                weights[s, place.shared, :, pl.ds(place.mine_in_block, place.half)],
                preferred_element_type=F32,
            )

    parts(total_rows, shared)
    forward_scan(
        lambda span: window[span, pl.ds(place.own, width)],
        gates,
        branch_y,
        soft,
        since,
        mixed,
        states,
        [fetch.advance],
    )
    fetch.finish()


def recurrence_back_kernel(
    taps,
    nbits,
    with_ffn,
    d_mixed,
    window,
    gates,
    branches,
    states,
    tap_rows,
    soft,
    slope_soft,
    since,
    weights,
    *refs,
):
    refs = list(refs)

    def take(count):
        taken = refs[:count]
        del refs[:count]
        return taken

    ffn, middle = take(2) if with_ffn else (None, None)
    d_branches, gate_grad, own_small = take(3)
    mixed = take(1)[0] if with_ffn else None
    d_conv, d_gates, given, taken, sums, send, recv = take(7)
    total_rows, width = states.shape
    block = weights.shape[2]
    place = HalfBlocks(width, block)
    half = place.half
    branch_y, branch_x = branches.at[:, :width], branches.at[:, width:]
    d_branch_y, d_branch_x = d_branches.at[:, :width], d_branches.at[:, width:]
    greet(tensor_bits(nbits))
    if with_ffn:
        scatter = Scatter(ffn, *take(2), middle.shape[0], nbits, *take(2))
        scatter.begin()
    backward_scan(
        d_mixed,
        lambda span: window[span, pl.ds(place.own, width)],
        gates,
        branch_y,
        states,
        soft,
        slope_soft,
        since,
        d_conv,
        d_gates,
        d_branch_y,
        sums.at[taps],
    )

    def to_pair(span):
        total = jnp.zeros((PART, half), F32)
        for s in range(2):
            total = total + times_transposed(
                d_gates[span, pl.ds(s * width + place.mine, half)],
                weights[
                    s,
                    place.shared,
                    pl.ds(place.other_in_block, half),
                    pl.ds(place.mine_in_block, half),
                ],
            )
        given[span, :] = total.astype(BF16)

    parts(total_rows, to_pair)
    rim = pltpu.make_async_remote_copy(
        src_ref=given,
        dst_ref=taken,
        send_sem=send.at[0],
        recv_sem=recv.at[0],
        device_id=place.pair,
        device_id_type=MESH,
    )
    rim.start()

    def full(span):
        for index in range(place.count - 1):
            number, at = place.full(index)
            total = d_conv[span, pl.ds(at, block)]
            for s in range(2):
                total = total + times_transposed(
                    d_gates[span, pl.ds(s * width + at, block)], weights[s, number]
                )
            d_conv[span, pl.ds(at, block)] = total
        total = d_conv[span, pl.ds(place.mine, half)]
        for s in range(2):
            total = total + times_transposed(
                d_gates[span, pl.ds(s * width + place.mine, half)],
                weights[
                    s,
                    place.shared,
                    pl.ds(place.mine_in_block, half),
                    pl.ds(place.mine_in_block, half),
                ],
            )
        d_conv[span, pl.ds(place.mine, half)] = total

    parts(total_rows, full)
    if with_ffn:
        scatter.advance(0)
    units = width // half
    for index in range(units):
        number = (index + place.odd) // 2
        cells = window[:, place.span(number)]
        both = jnp.concatenate(
            [d_gates[:, s * width + index * half : s * width + (index + 1) * half] for s in range(2)],
            axis=1,
        )
        found = lax.dot_general(
            cells, both, (((0,), (0,)), ((), ())), preferred_element_type=F32
        ).astype(BF16)
        gate_grad[2 * index] = found[:, :half]
        gate_grad[2 * index + 1] = found[:, half:]
    rim.wait()

    def add(span):
        d_conv[span, pl.ds(place.mine, half)] += taken[span, :].astype(F32)

    parts(total_rows, add)
    for tap in range(taps):
        sums[tap] = jnp.zeros((8, width), F32)

    def conv(i, after):
        row = pl.multiple_of(total_rows - CHUNK - i * CHUNK, CHUNK)
        kept = []
        for at in range(CHUNK - 8, -1, -8):
            tile = pl.ds(row + at, 8)
            values = d_conv[tile, :]
            line = lax.broadcasted_iota(jnp.int32, values.shape, 0)
            below = branch_x[tile, :]
            higher = pl.multiple_of((row + at - 8 + total_rows) % total_rows, 8)
            above = branch_x[pl.ds(higher, 8), :]
            total = values * tap_rows[0:1, :]
            sums[0] += values * below
            masked = []
            for tap in range(1, taps):
                here = jnp.where(since[tile, :] > tap - 0.5, values, 0.0)
                masked.append(here)
                moved = jnp.where(
                    line < 8 - tap,
                    pltpu.roll(here, 8 - tap, 0),
                    pltpu.roll(after[tap - 1], 8 - tap, 0),
                )
                total = total + moved * tap_rows[tap : tap + 1, :]
                source = jnp.where(
                    line < tap, pltpu.roll(above, tap, 0), pltpu.roll(below, tap, 0)
                )
                sums[tap] += here * source
            after = tuple(masked)
            kept.append(total)
        d_branch_x[pl.ds(row, CHUNK), :] = jnp.concatenate(kept[::-1], axis=0).astype(BF16)
        return after

    none = jnp.zeros((8, width), F32)
    lax.fori_loop(0, total_rows // CHUNK, conv, (none,) * (taps - 1))
    line = lax.broadcasted_iota(jnp.int32, (8, width), 0)
    total = jnp.zeros((8, width), F32)
    for tap in range(taps + 1):
        row = jnp.sum(sums[tap], axis=0, keepdims=True)
        total = jnp.where(line == tap, row, total)
    own_small[...] = total
    if with_ffn:
        for step in range(1, nbits):
            scatter.advance(step)

        def result(row):
            span = pl.ds(row, CHUNK)
            mixed[span, :] = (middle[span, :] + scatter.total(row, CHUNK)).astype(BF16)

        chunks(middle.shape[0], result)
        scatter.drain()


def finish_kernel(
    taps,
    gates,
    small,
    in_out,
    in_y,
    in_x,
    in_grad,
    in_mixed,
    in_both,
    in_down,
    whole,
    out_out,
    out_y,
    out_x,
    out_grad,
    out_mixed,
    out_gate,
    out_up,
    out_down,
    conv,
    decay,
    gain_in,
    gain_mid,
):
    held = whole.shape[1]
    pieces = gates.shape[0] // held

    def block(n, carry):
        for piece in range(pieces):
            for s in range(2):
                whole[s, n, :, piece * 128 : (piece + 1) * 128] = gates[
                    n * pieces + piece, s
                ].astype(F32)
        return carry

    lax.fori_loop(0, held, block, 0)
    units = out_gate.shape[1]

    def copy(row):
        span = pl.ds(row, CHUNK)
        out_out[span, :] = in_out[span, :].astype(F32)
        out_y[span, :] = in_y[span, :]
        out_x[span, :] = in_x[span, :]
        out_gate[span, :] = in_both[span, :units].astype(F32)
        out_up[span, :] = in_both[span, units:].astype(F32)
        out_down[span, :] = in_down[span, :].astype(F32)

    chunks(out_out.shape[0], copy)

    def own(row):
        span = pl.ds(row, CHUNK)
        out_grad[span, :] = in_grad[span, :]
        out_mixed[span, :] = in_mixed[span, :]

    chunks(out_grad.shape[0], own)

    @pl.when(pl.program_id(0) == 0)
    def _():
        share = small.shape[2]
        for index in range(small.shape[0]):
            span = slice(index * share, (index + 1) * share)
            conv[:, span] = small[index, :taps, :]
            for at in range(0, share, 128):
                row = (index * share + at) // 128
                decay[row : row + 1, :] = small[index, taps : taps + 1, at : at + 128]
                gain_in[row : row + 1, :] = small[index, 6:7, at : at + 128]
                gain_mid[row : row + 1, :] = small[index, 7:8, at : at + 128]


def finish(gate_all, small_all, sums, grad_input, mixed, both, down, taps, gate_shape):
    _, blocks, block, _ = gate_shape
    unit = gate_all.shape[-1]
    pieces = block // unit
    width = small_all.shape[0] * small_all.shape[2]
    rows, units = down.shape
    own_rows = grad_input.shape[0]
    grid = 2
    steps, held = rows // grid, own_rows // grid
    if unit != 128 or blocks % grid or rows % (16 * grid) or own_rows % (16 * grid):
        whole = gate_all.reshape(blocks, pieces, 2, block, unit).transpose(2, 0, 3, 1, 4)
        summed = small_all.transpose(1, 0, 2).reshape(8, width)
        whole = whole.reshape(gate_shape).astype(F32)
        wide = tuple(one.astype(F32) for one in (both[:, :units], both[:, units:], down))
        last = (summed[:taps], summed[taps], summed[6], summed[7])
        sums = tuple(one.astype(F32) for one in sums)
        return (whole, *sums, grad_input, mixed, *wide, *last)
    shape = jax.ShapeDtypeStruct

    def by_rows(count, columns):
        return pl.BlockSpec((count, columns), lambda n: (n, 0))

    def by_held(columns):
        return pl.BlockSpec((held, columns), lambda n: (n, 0))

    def whole_array(*dims):
        return pl.BlockSpec(dims, lambda n: (0,) * len(dims))

    columns = sums[0].shape[1]
    d_width = grad_input.shape[1]
    lines = width // 128
    found = pl.pallas_call(
        partial(finish_kernel, taps),
        grid=(grid,),
        in_specs=[
            pl.BlockSpec((blocks // grid * pieces, 2, block, unit), lambda n: (n, 0, 0, 0)),
            whole_array(*small_all.shape),
        ]
        + [by_rows(steps, columns)] * 3
        + [by_held(d_width)] * 2
        + [by_rows(steps, 2 * units), by_rows(steps, units)],
        out_specs=(
            (pl.BlockSpec((2, blocks // grid, block, block), lambda n: (0, n, 0, 0)),)
            + (by_rows(steps, columns),) * 3
            + (by_held(d_width),) * 2
            + (by_rows(steps, units),) * 3
            + (whole_array(taps, width),)
            + (whole_array(lines, 128),) * 3
        ),
        out_shape=(
            (shape(gate_shape, F32),)
            + (shape((rows, columns), F32),) * 3
            + (shape(grad_input.shape, F32), shape(mixed.shape, BF16))
            + (shape((rows, units), F32),) * 3
            + (shape((taps, width), F32),)
            + (shape((lines, 128), F32),) * 3
        ),
        compiler_params=pltpu.CompilerParams(vmem_limit_bytes=VMEM_BYTES),
    )(
        gate_all.reshape(blocks * pieces, 2, block, unit),
        small_all,
        *sums,
        grad_input,
        mixed,
        both,
        down,
    )
    return found[:10] + tuple(one.reshape(width) for one in found[10:])


def scan_call(kernel, outs, *operands):
    return pl.pallas_call(
        kernel,
        out_shape=outs,
        in_specs=in_vmem(len(operands)),
        out_specs=tuple(in_vmem(len(outs))),
        compiler_params=pltpu.CompilerParams(vmem_limit_bytes=VMEM_BYTES),
    )(*operands)


class Rim:
    def __init__(self, route, back, source, first, width, room):
        self.route, self.back = route, back
        self.source, self.first, self.width = source, first, width
        self.room = room

    def fetch(self, values):
        part = lax.dynamic_slice_in_dim(values, self.source, self.width, 1)
        return lax.ppermute(part, "tensor", self.route)

    def give(self, part):
        return lax.ppermute(part, "tensor", self.back)

    def add(self, values, part):
        zeros = jnp.zeros(values.shape, F32)
        return values + lax.dynamic_update_slice_in_dim(
            zeros, part.astype(F32), self.source, 1
        )

    def window(self, channels):
        return (channels // self.width + 4) * self.width


def gate_rims(channels, block_size, ntensor, offset):
    up = [(i, i + 1) for i in range(ntensor - 1)]
    down = [(i + 1, i) for i in range(ntensor - 1)]
    last = jnp.int32(channels - block_size)
    return [
        Rim(up, down, last, offset - block_size, block_size, block_size),
        Rim(down, up, jnp.int32(0), offset + channels, block_size, block_size),
    ]


def same_block(first, count, offset, channels, block_size):
    rows = (first + jnp.arange(count, dtype=jnp.int32))[:, None]
    columns = (offset + jnp.arange(channels, dtype=jnp.int32))[None, :]
    return (rows + block_size) // block_size == (columns + block_size) // block_size


def gate_dense(gate_w, offset, first, count):
    block_size = gate_w.shape[2]
    total = gate_w.shape[1] * block_size
    channels = total // lax.axis_size("tensor")
    columns = gate_w.transpose(2, 0, 1, 3).reshape(block_size, 2, total)
    columns = lax.dynamic_slice_in_dim(columns, offset, channels, 2)
    copies = -(-count // block_size) + 1
    tall = jnp.concatenate([columns] * copies, axis=0)
    tall = lax.dynamic_slice_in_dim(tall, (first + block_size) % block_size, count, 0)
    same = same_block(first, count, offset, channels, block_size)
    dense = jnp.where(same[:, None, :], tall, jnp.zeros_like(tall))
    return dense.reshape(count, 2 * channels)


def doc_starts(seg_ids, seq_len):
    places = jnp.arange(seg_ids.shape[0], dtype=jnp.int32)
    before = jnp.concatenate([seg_ids[:1], seg_ids[:-1]])
    resets = (places % seq_len == 0) | (seg_ids != before)
    starts = lax.cummax(jnp.where(resets, places, jnp.zeros_like(places)), axis=0)
    return starts


def causal_conv(starts, values, kernel):
    places = jnp.arange(values.shape[0], dtype=jnp.int32)
    total = values * kernel[0]
    for offset_k in range(1, kernel.shape[0]):
        moved = jnp.concatenate(
            [jnp.zeros((offset_k, values.shape[1]), values.dtype), values[:-offset_k]], axis=0
        )
        valid = (places - offset_k >= starts)[:, None]
        total = total + jnp.where(valid, moved, jnp.zeros_like(moved)) * kernel[offset_k]
    return total


def geglu(gate_val, up_val):
    return jax.nn.gelu(gate_val, approximate=True) * up_val


def rows_times(left, right):
    return lax.dot_general(left, right, (((1,), (1,)), ((), ())), preferred_element_type=F32)


def rows_back(lefts, rights):
    total = rows_times(lefts[0], rights[0])
    return total + rows_times(lefts[1], rights[1])


def inner_rows(left, right):
    return lax.dot_general(left, right, (((0,), (0,)), ((), ())), preferred_element_type=F32)


def halved(grad, ndp):
    return grad.reshape(ndp // 2, 2, grad.shape[0] // ndp, grad.shape[1])


def body(
    tokens,
    segments,
    cotangent,
    norm_gain,
    w_y,
    w_x,
    conv_w,
    gate_w,
    decay_param,
    w_out,
    mlp_gain,
    w_gate,
    w_up,
    w_down,
):
    ntensor = lax.axis_size("tensor")
    ndp = lax.axis_size("dp")
    nbits = log2_of(ntensor)
    tindex = lax.axis_index("tensor")
    own_rows, width = tokens.shape
    group_rows = own_rows * ntensor
    block_size = gate_w.shape[2]
    nblocks = gate_w.shape[1]
    dp_rows, channels = w_y.shape
    taps = conv_w.shape[0]
    offset = tindex * channels
    shape = jax.ShapeDtypeStruct
    gain_in = norm_gain.reshape(1, width)
    gain_mid = mlp_gain.reshape(1, width)
    seg_rows_of = own_rows // 128
    tiled = channels % 128 == 0
    w_yx = (w_y, w_x) if tiled else (jnp.concatenate([w_y, w_x], axis=1),)
    normed_rows, seg_all, wyx_loc, wout_loc = call_kernel(
        partial(enter_kernel, nbits, len(w_yx)),
        (
            shape((group_rows, width), BF16),
            shape((ntensor, seg_rows_of, 128), jnp.int32),
            shape((dp_rows * ndp, 2 * channels), BF16),
            shape((dp_rows * ndp, channels), BF16),
        ),
        [pltpu.VMEM((1, width), F32)]
        + gather_sems(nbits)
        + [pltpu.SemaphoreType.DMA((ntensor - 1,)), pltpu.SemaphoreType.DMA((ntensor - 1,))]
        + [pltpu.SemaphoreType.DMA((1,))]
        + line_sems(ndp) * (len(w_yx) + 1),
        0,
        tokens,
        segments.reshape(seg_rows_of, 128),
        norm_gain.reshape(width // 128, 128),
        *w_yx,
        w_out,
        far_in=tuple(range(3, 4 + len(w_yx))),
        far_out=(2, 3),
    )
    units = w_gate.shape[1]
    w_both = jnp.concatenate([w_gate, w_up], axis=1)
    w_both, w_down, normed_rows = lax.optimization_barrier((w_both, w_down, normed_rows))
    both_loc = lax.all_gather(w_both, "dp", axis=0, tiled=True)
    wd_loc = lax.all_gather(w_down, "dp", axis=0, tiled=True)
    seg_rows = seg_all.reshape(group_rows)
    starts = doc_starts(seg_rows, group_rows)
    conv_loc = lax.dynamic_slice_in_dim(conv_w, offset, channels, 1)
    decay_loc = lax.dynamic_slice_in_dim(decay_param, offset, channels, 0).reshape(1, channels)
    soft = jax.nn.softplus(decay_loc)
    slope_soft = jax.nn.sigmoid(decay_loc)
    half_blocks = (
        channels % block_size == block_size // 2 and ntensor % 2 == 0 and block_size % 256 == 0
    )
    since = (jnp.arange(group_rows, dtype=jnp.int32) - starts).astype(F32)[:, None]
    branches = jnp.dot(normed_rows, wyx_loc, preferred_element_type=F32)
    if half_blocks:
        span_blocks = channels // block_size + 1
        w_window = lax.dynamic_slice_in_dim(gate_w, offset // block_size, span_blocks, 1)
        taps_pad = jnp.concatenate([conv_loc, jnp.zeros((8 - taps, channels), F32)], axis=0)
        mixed_low, states, window, gate_pre, cot_rows = call_kernel(
            partial(recurrence_kernel, taps, nbits),
            (
                shape((group_rows, channels), BF16),
                shape((group_rows, channels), F32),
                shape((group_rows, span_blocks * block_size), BF16),
                shape((group_rows, 2 * channels), F32),
                shape((group_rows, width), BF16),
            ),
            [pltpu.SemaphoreType.DMA((1,)), pltpu.SemaphoreType.DMA((1,))]
            + fetch_scratch(nbits),
            5,
            branches,
            taps_pad,
            soft,
            since,
            w_window,
            cotangent,
        )
    else:
        branch_y, branch_x = branches[:, :channels], branches[:, channels:]
        (cot_rows,) = call_kernel(
            partial(fetch_kernel, nbits),
            (shape((group_rows, width), BF16),),
            fetch_scratch(nbits),
            5,
            cotangent,
        )
        rims = gate_rims(channels, block_size, ntensor, offset)
        own_dense = gate_dense(gate_w, offset, offset, channels)
        rim_dense = [gate_dense(gate_w, offset, rim.first, rim.width) for rim in rims]
        conv_out, conv_pull = jax.vjp(partial(causal_conv, starts), branch_x, conv_loc)
        conv_low = conv_out.astype(BF16)
        rim_cells = [rim.fetch(conv_low) for rim in rims]
        gate_pre = jnp.dot(conv_low, own_dense, preferred_element_type=F32)
        for cells, dense in zip(rim_cells, rim_dense):
            gate_pre = gate_pre + jnp.dot(cells, dense, preferred_element_type=F32)
        mixed_low, states = scan_call(
            forward_scan_kernel,
            (shape((group_rows, channels), BF16), shape((group_rows, channels), F32)),
            conv_low,
            gate_pre,
            branch_y,
            soft,
            since,
        )
    middle, mid_rows = call_kernel(
        partial(middle_kernel, nbits),
        (shape((own_rows, width), F32), shape((group_rows, width), BF16)),
        scatter_scratch(own_rows, width, nbits) + gather_sems(nbits),
        1,
        rows_times(mixed_low, wout_loc).astype(BF16),
        tokens,
        gain_mid,
    )
    pre = jnp.dot(mid_rows, both_loc, preferred_element_type=F32)
    hidden, act_pull = jax.vjp(geglu, pre[:, :units], pre[:, units:])
    hidden_low = hidden.astype(BF16)
    grad_wd = inner_rows(cot_rows, hidden_low).astype(BF16)
    sum_wd = lax.psum_scatter(grad_wd, "dp", scatter_dimension=0, tiled=True)
    grad_wd, wd_loc = lax.optimization_barrier((grad_wd, wd_loc))
    d_hidden = jnp.dot(cot_rows, wd_loc, preferred_element_type=F32)
    d_gate, d_up = act_pull(d_hidden)
    d_pre = jnp.concatenate([d_gate.astype(BF16), d_up.astype(BF16)], axis=1)
    grad_both = inner_rows(mid_rows, d_pre).astype(BF16)
    sum_both = lax.psum_scatter(grad_both, "dp", scatter_dimension=0, tiled=True)
    d_pre, grad_both = lax.optimization_barrier((d_pre, grad_both))
    d_mid_part = rows_times(d_pre, both_loc).astype(BF16)
    d_middle, d_mixer, d_gain_mid, ffn_part = call_kernel(
        partial(turn_kernel, nbits),
        (
            shape((own_rows, width), F32),
            shape((group_rows, width), BF16),
            shape((8, width), F32),
            shape((group_rows, width), BF16),
        ),
        scatter_scratch(own_rows, width, nbits) + gather_sems(nbits) + product_scratch(units),
        2,
        d_mid_part,
        cotangent,
        middle,
        gain_mid,
        hidden_low,
        wd_loc,
        far_in=(5,),
    )
    d_mixer, sum_wd = lax.optimization_barrier((d_mixer, sum_wd))
    d_mixed_in = jnp.dot(d_mixer, wout_loc, preferred_element_type=F32)
    unit = math.gcd(channels, block_size)
    merged = half_blocks and nbits <= 2
    if half_blocks:
        found = call_kernel(
            partial(recurrence_back_kernel, taps, nbits, merged),
            (
                shape((group_rows, 2 * channels), BF16),
                shape((channels // unit * 2, block_size, unit), BF16),
                shape((8, channels), F32),
            )
            + ((shape((own_rows, width), BF16),) if merged else ()),
            [
                pltpu.VMEM((group_rows, channels), F32),
                pltpu.VMEM((group_rows, 2 * channels), BF16),
                pltpu.VMEM((group_rows, unit), BF16),
                pltpu.VMEM((group_rows, unit), BF16),
                pltpu.VMEM((taps + 1, 8, channels), F32),
                pltpu.SemaphoreType.DMA((1,)),
                pltpu.SemaphoreType.DMA((1,)),
            ]
            + (scatter_scratch(own_rows, width, nbits) if merged else []),
            6,
            d_mixed_in,
            window,
            gate_pre,
            branches,
            states,
            taps_pad,
            soft,
            slope_soft,
            since,
            w_window,
            *((ffn_part, middle) if merged else ()),
        )
        d_branches, gate_grad, own_small = found[:3]
        gate_grad = gate_grad.reshape(channels // unit * 2 * block_size, unit)
    else:
        d_conv, d_gate_low, d_branch_y, d_decay = scan_call(
            backward_scan_kernel,
            (
                shape((group_rows, channels), F32),
                shape((group_rows, 2 * channels), BF16),
                shape((group_rows, channels), BF16),
                shape((8, channels), F32),
            ),
            d_mixed_in,
            conv_low,
            gate_pre,
            branch_y,
            states,
            soft,
            slope_soft,
            since,
        )
        given = [rows_times(d_gate_low, dense).astype(BF16) for dense in rim_dense]
        taken = [rim.give(part) for rim, part in zip(rims, given)]
        d_conv_out = d_conv + rows_times(d_gate_low, own_dense)
        for rim, part in zip(rims, taken):
            d_conv_out = rim.add(d_conv_out, part)
        d_branch_x, grad_conv_loc = conv_pull(d_conv_out)
        d_branches = jnp.concatenate([d_branch_y, d_branch_x.astype(BF16)], axis=1)
        base = offset // block_size * block_size - rims[0].room
        window_rows = rims[0].window(channels)
        picked = jnp.zeros((window_rows, 2 * channels), F32)
        for first, cells in [(offset, conv_low)] + [(r.first, c) for r, c in zip(rims, rim_cells)]:
            part = inner_rows(cells, d_gate_low)
            same = same_block(first, cells.shape[1], offset, channels, block_size)
            part = jnp.where(jnp.concatenate([same, same], axis=1), part, 0.0)
            picked = lax.dynamic_update_slice(picked, part, (first - base, jnp.int32(0)))
        picked = picked.reshape(window_rows // block_size, block_size, 2, channels // unit, unit)
        gate_grad = picked.sum(axis=0).astype(BF16).transpose(2, 1, 0, 3)
        gate_grad = gate_grad.reshape(channels // unit * 2 * block_size, unit)
        own_small = jnp.concatenate(
            [
                grad_conv_loc,
                jnp.sum(d_decay, axis=0, keepdims=True),
                jnp.zeros((7 - taps, channels), F32),
            ],
            axis=0,
        )

    grad_wout = inner_rows(d_mixer, mixed_low).astype(BF16)
    grad_wyx = inner_rows(normed_rows, d_branches).astype(BF16)
    d_normed = rows_times(d_branches, wyx_loc).astype(BF16)
    d_normed, grad_wyx, grad_wout, sum_both = lax.optimization_barrier(
        (d_normed, grad_wyx, grad_wout, sum_both)
    )
    sum_wout = lax.psum_scatter(grad_wout, "dp", scatter_dimension=0, tiled=True)

    pieces = [halved(grad, ndp) for grad in (gate_grad, grad_wyx)]
    peers = ntensor - 1
    gate_rows = gate_grad.shape[0] // ndp
    dma = pltpu.SemaphoreType.DMA
    scratch = scatter_scratch(own_rows, width, nbits)
    scratch += line_scratch(ndp, gate_rows, unit)
    if tiled:
        scratch += line_scratch(ndp, dp_rows, channels) * 2
    else:
        scratch += line_scratch(ndp, dp_rows, 2 * channels)
    scratch += [
        pltpu.VMEM((8, width), F32),
        pltpu.VMEM((ntensor, 8, channels), F32),
        pltpu.VMEM((peers, 8, channels), F32),
        pltpu.VMEM((8, channels), F32),
        pltpu.VMEM((ndp - 1, 8, channels), F32),
    ]
    scratch += [dma((peers,)), dma((peers,)), dma((ndp - 1,)), dma((ndp - 1,))]
    scratch += [dma((peers,)), dma((peers,)), dma((peers + ndp,)), dma((peers + ndp,))]
    grad_input, sum_wy, sum_wx, gate_all, small_all = call_kernel(
        partial(leave_kernel, nbits, tiled),
        (shape((own_rows, width), F32),)
        + (shape((dp_rows, channels), F32),) * 2
        + (
            shape((ntensor, ndp // 2, 2, gate_rows, unit), BF16),
            shape((ntensor, 8, channels), F32),
        ),
        scratch,
        3,
        d_normed,
        tokens,
        d_middle,
        gain_in,
        own_small,
        d_gain_mid,
        *pieces,
        far_in=(6, 7),
    )
    if merged:
        mixed = found[3]
    else:
        (mixed,) = call_kernel(
            partial(result_kernel, nbits),
            (shape((own_rows, width), BF16),),
            scatter_scratch(own_rows, width, nbits),
            4,
            ffn_part,
            middle,
        )
    found = finish(
        gate_all,
        small_all,
        (sum_wout, sum_wy, sum_wx),
        grad_input,
        mixed,
        sum_both,
        sum_wd,
        taps,
        gate_w.shape,
    )
    sum_gate, sum_wout, sum_wy, sum_wx, grad_input, mixed = found[:6]
    sum_wg, sum_wu, sum_wd, sum_conv, sum_decay, sum_gain_in, sum_gain_mid = found[6:]
    return (
        mixed,
        grad_input,
        sum_gain_in,
        sum_wy,
        sum_wx,
        sum_conv,
        sum_gate,
        sum_decay,
        sum_wout,
        sum_gain_mid,
        sum_wg,
        sum_wu,
        sum_wd,
    )


def solution(mesh):
    split = P(("dp", "tensor"), None)
    weight = P("dp", "tensor")
    return jax.shard_map(
        body,
        mesh=mesh,
        in_specs=(
            split,
            P(("dp", "tensor")),
            split,
            P(),
            weight,
            weight,
            P(),
            P(),
            P(),
            weight,
            P(),
            weight,
            weight,
            weight,
        ),
        out_specs=(
            split,
            split,
            P(),
            weight,
            weight,
            P(),
            P(),
            P(),
            weight,
            P(),
            weight,
            weight,
            weight,
        ),
        check_vma=False,
    )
```

```python
import math
from functools import partial

import jax
import jax.numpy as jnp
from jax import lax
from jax.experimental import pallas as pl
from jax.experimental.pallas import tpu as pltpu
from jax.sharding import PartitionSpec as P

EPSILON = 1e-06
MESH = pl.DeviceIdType.MESH
VMEM_BYTES = 56 * 1024 * 1024
CHUNK = 16
F32 = jnp.float32
BF16 = jnp.bfloat16


def subsets(bits):
    found = [()]
    for bit in bits:
        found = found + [chosen + (bit,) for chosen in found]
    return found


def flipped(index, bits):
    for bit in bits:
        mine = (index // (1 << bit)) % 2
        index = index + (1 - 2 * mine) * (1 << bit)
    return index


def log2_of(count):
    assert count & (count - 1) == 0
    return count.bit_length() - 1


def greet(axis_bits):
    barrier = pltpu.get_barrier_semaphore()
    for axis, bit in axis_bits:
        peer = flipped(lax.axis_index(axis), (bit,))
        pl.semaphore_signal(barrier, inc=1, device_id={axis: peer}, device_id_type=MESH)
    pl.semaphore_wait(barrier, len(axis_bits))


def halves_of(nbits, columns):
    half = columns // 2
    ups = tuple(range(nbits))
    return ((ups, 0, half), (ups[::-1], half, half))


class Gather:
    def __init__(self, ref, rows, nbits, send_sems, recv_sems):
        self.ref, self.rows, self.nbits = ref, rows, nbits
        self.sems = (send_sems, recv_sems)
        self.me = lax.axis_index("tensor")
        self.plan = []
        number = 0
        for half, (order, at, width) in enumerate(halves_of(nbits, ref.shape[1])):
            for step, bit in enumerate(order):
                for known in subsets(order[:step]):
                    self.plan.append((half, step, known, bit, at, width, number))
                    number += 1
        self.count = number

    def copy(self, item):
        half, step, known, bit, at, width, number = item
        row = pl.multiple_of(flipped(self.me, known) * self.rows, self.rows)
        piece = self.ref.at[pl.ds(row, self.rows), pl.ds(at, width)]
        return pltpu.make_async_remote_copy(
            src_ref=piece,
            dst_ref=piece,
            send_sem=self.sems[0].at[number],
            recv_sem=self.sems[1].at[number],
            device_id={"tensor": flipped(self.me, (bit,))},
            device_id_type=MESH,
        )

    def begin(self):
        for item in sorted(self.plan, key=lambda it: it[1]):
            if item[2] == ():
                self.copy(item).start()

    def advance(self, step):
        for item in self.plan:
            half, at_step, known, bit, at, width, number = item
            if at_step == step:
                self.copy(item).wait_recv()
                block = known + (bit,)
                for later in self.plan:
                    if later[0] == half and set(later[2]) == set(block):
                        self.copy(later).start()

    def finish(self, step=0):
        for at_step in range(step, self.nbits):
            self.advance(at_step)
        for item in self.plan:
            self.copy(item).wait_send()


def gather_copies(nbits):
    return 2 * ((1 << nbits) - 1)


class Scatter:
    def __init__(self, ref, landed, staged, rows, nbits, send_sems, recv_sems):
        self.ref, self.landed, self.staged = ref, landed, staged
        self.rows, self.nbits = rows, nbits
        self.sems = (send_sems, recv_sems)
        self.me = lax.axis_index("tensor")
        self.plan, self.slot = [], {}
        number = 0
        for half, (order, at, width) in enumerate(halves_of(nbits, ref.shape[1])):
            for step, bit in enumerate(order):
                for rest in subsets(order[step + 1 :])[::-1]:
                    self.plan.append((half, step, rest, bit, at, width, number))
                    if step > 0:
                        self.slot[number] = len(self.slot)
                    number += 1

    def copy(self, item):
        half, step, rest, bit, at, width, number = item
        if step == 0:
            row = pl.multiple_of(flipped(self.me, rest + (bit,)) * self.rows, self.rows)
            source = self.ref.at[pl.ds(row, self.rows), pl.ds(at, width)]
        else:
            source = self.staged.at[self.slot[number]]
        return pltpu.make_async_remote_copy(
            src_ref=source,
            dst_ref=self.landed.at[number],
            send_sem=self.sems[0].at[number],
            recv_sem=self.sems[1].at[number],
            device_id={"tensor": flipped(self.me, (bit,))},
            device_id_type=MESH,
        )

    def begin(self):
        for item in sorted(self.plan, key=lambda it: (len(it[2]) == 0)):
            if item[1] == 0:
                self.copy(item).start()

    def partial_sum(self, half, block, before, row, size):
        at, width = halves_of(self.nbits, self.ref.shape[1])[half][1:]
        base = pl.multiple_of(flipped(self.me, block) * self.rows + row, size)
        total = self.ref[pl.ds(base, size), pl.ds(at, width)].astype(F32)
        for it in self.plan:
            if it[0] == half and it[1] < before and set(it[2]) == set(block):
                total = total + self.landed[it[6], pl.ds(row, size), :].astype(F32)
        return total

    def advance(self, step):
        for half in range(2):
            for item in self.plan:
                if item[0] == half and item[1] == step:
                    self.copy(item).wait_recv()
            for item in self.plan:
                if item[0] == half and item[1] == step + 1:

                    def fill(row, item=item):
                        value = self.partial_sum(
                            item[0], item[2] + (item[3],), item[1], row, CHUNK
                        )
                        where = (self.slot[item[6]], pl.ds(row, CHUNK))
                        self.staged[where + (slice(None),)] = value.astype(BF16)

                    chunks(self.rows, fill)
                    self.copy(item).start()

    def run(self):
        for step in range(self.nbits):
            self.advance(step)

    def total(self, row, size):
        return jnp.concatenate(
            [self.partial_sum(half, (), self.nbits, row, size) for half in range(2)], axis=1
        )

    def drain(self):
        for item in self.plan:
            self.copy(item).wait_send()


def scatter_scratch(rows, columns, nbits):
    copies = gather_copies(nbits)
    later = max(1, copies - (1 << nbits))
    return [
        pltpu.VMEM((copies, rows, columns // 2), BF16),
        pltpu.VMEM((later, rows, columns // 2), BF16),
        pltpu.SemaphoreType.DMA((copies,)),
        pltpu.SemaphoreType.DMA((copies,)),
    ]


def gather_sems(nbits):
    copies = gather_copies(nbits)
    return [pltpu.SemaphoreType.DMA((copies,)), pltpu.SemaphoreType.DMA((copies,))]


def tensor_bits(nbits):
    return [("tensor", bit) for bit in range(nbits)]


def rms_scale_of(values):
    return lax.rsqrt(jnp.mean(values * values, axis=-1, keepdims=True) + EPSILON)


def chunks(rows, body):
    def step(i, carry):
        body(pl.multiple_of(i * CHUNK, CHUNK))
        return carry

    lax.fori_loop(0, rows // CHUNK, step, 0)


def own_row(row, rows):
    return pl.multiple_of(lax.axis_index("tensor") * rows + row, CHUNK)


def dp_place():
    me = lax.axis_index("dp")
    return me // 2, me % 2, lax.axis_size("dp") // 2


def dp_index(chip, core):
    return chip * 2 + core


UP, DOWN = 1, -1


class LineGather:
    def __init__(self, own, whole, send_sems, recv_sems, columns=None):
        self.own, self.whole = own, whole
        self.sems = (send_sems, recv_sems)
        self.chip, self.core, self.chips = dp_place()
        self.rows = own.shape[0]
        self.columns = slice(None) if columns is None else columns

    def block(self, chip):
        row = pl.multiple_of(dp_index(chip, self.core) * self.rows, self.rows)
        return self.whole.at[pl.ds(row, self.rows), self.columns]

    def has(self, way, distance):
        return self.chip >= distance if way == UP else self.chip + distance < self.chips

    def number(self, way, distance):
        return (0 if way == UP else self.chips) + distance

    def along(self, way, distance):
        block = self.block(self.chip - way * distance)
        return pltpu.make_async_remote_copy(
            src_ref=self.own if distance == 0 else block,
            dst_ref=block,
            send_sem=self.sems[0].at[self.number(way, distance)],
            recv_sem=self.sems[1].at[self.number(way, distance + 1)],
            device_id={"dp": dp_index(self.chip + way, self.core)},
            device_id_type=MESH,
        )

    def arrival(self, way, distance):
        block = self.block(self.chip - way * distance)
        return pltpu.make_async_remote_copy(
            src_ref=block,
            dst_ref=block,
            send_sem=self.sems[0].at[self.number(way, distance)],
            recv_sem=self.sems[1].at[self.number(way, distance)],
            device_id={"dp": dp_index(self.chip + way, self.core)},
            device_id_type=MESH,
        )

    def across(self, way, distance):
        block = self.block(self.chip - way * distance)
        number = 2 * self.chips + self.number(way, distance)
        return pltpu.make_async_remote_copy(
            src_ref=self.own if distance == 0 else block,
            dst_ref=block,
            send_sem=self.sems[0].at[number],
            recv_sem=self.sems[1].at[number],
            device_id={"dp": dp_index(self.chip, 1 - self.core)},
            device_id_type=MESH,
        )

    def local(self):
        return pltpu.make_async_copy(
            self.own, self.block(self.chip), self.sems[0].at[4 * self.chips]
        )

    def begin(self):
        for way in (UP, DOWN):

            @pl.when(self.has(-way, 1))
            def _(way=way):
                self.along(way, 0).start()

        self.across(UP, 0).start()
        self.local().start()

    def pass_on(self, distance):
        for way in (UP, DOWN):

            @pl.when(self.has(way, distance))
            def _(way=way):
                self.arrival(way, distance).wait_recv()

                @pl.when(self.has(-way, 1))
                def _():
                    self.along(way, distance).start()

                self.across(way, distance).start()

    def finish(self):
        self.across(UP, 0).wait()
        self.local().wait()
        for way in (UP, DOWN):
            for distance in range(self.chips):

                @pl.when(self.has(way, distance) & self.has(-way, 1))
                def _(way=way, distance=distance):
                    self.along(way, distance).wait_send()

                if distance:

                    @pl.when(self.has(way, distance))
                    def _(way=way, distance=distance):
                        self.across(way, distance).wait()


def line_sems(ndp):
    chips = ndp // 2
    return [pltpu.SemaphoreType.DMA((4 * chips + 1,)), pltpu.SemaphoreType.DMA((4 * chips + 1,))]


def greet_peers(nbits, all_tensor, whole_dp):
    me = lax.axis_index("tensor")
    chip, core, chips = dp_place()
    barrier = pltpu.get_barrier_semaphore()

    def signal(target):
        pl.semaphore_signal(barrier, inc=1, device_id=target, device_id_type=MESH)

    met = 0
    for chosen in subsets(tuple(range(nbits))):
        if chosen and (all_tensor or len(chosen) == 1):
            signal({"tensor": flipped(me, chosen)})
            met += 1
    if whole_dp:
        for shift in range(chips):
            for turn in range(2):
                if (shift, turn) != (0, 0):
                    other = dp_index((chip + shift) % chips, core + turn * (1 - 2 * core))
                    signal({"dp": other})
                    met += 1
    else:
        signal({"dp": dp_index(chip, 1 - core)})
        met += 1

        for shift in sorted({1 % chips, chips - 1} - {0}):
            signal({"dp": dp_index((chip + shift) % chips, core)})
            met += 1

    pl.semaphore_wait(barrier, met)


def widen(rows, wide):
    for row in range(rows.shape[0]):
        wide[:, row * 128 : (row + 1) * 128] = rows[row : row + 1, :]


def enter_kernel(
    nbits, parts_yx, tokens, seg, gain, *refs
):
    w_yx, w_out = refs[:parts_yx], refs[parts_yx]
    normed_all, seg_all, wyx_all, wout_all, gain_row, s0, r0, s2, r2, l0, *line = refs[
        parts_yx + 1 :
    ]
    rows = tokens.shape[0]
    me = lax.axis_index("tensor")
    peers = [chosen for chosen in subsets(tuple(range(nbits))) if chosen]
    greet_peers(nbits, True, False)
    width = wyx_all.shape[1] // parts_yx
    lines = [
        LineGather(
            own,
            wyx_all,
            line[2 * number],
            line[2 * number + 1],
            pl.ds(number * width, width) if parts_yx > 1 else None,
        )
        for number, own in enumerate(w_yx)
    ]
    lines.append(LineGather(w_out, wout_all, *line[2 * parts_yx : 2 * parts_yx + 2]))
    for item in lines:
        item.begin()
    widen(gain, gain_row)

    def norm(row):
        values = tokens[pl.ds(row, CHUNK), :].astype(F32)
        scaled = values * rms_scale_of(values) * gain_row[...]
        normed_all[pl.ds(own_row(row, rows), CHUNK), :] = scaled.astype(BF16)

    chunks(rows, norm)
    gather = Gather(normed_all, rows, nbits, s0, r0)
    gather.begin()
    seg_own = pltpu.make_async_copy(seg, seg_all.at[me], l0.at[0])
    seg_own.start()
    seg_copies = [
        pltpu.make_async_remote_copy(
            src_ref=seg,
            dst_ref=seg_all.at[me],
            send_sem=s2.at[number],
            recv_sem=r2.at[number],
            device_id={"tensor": flipped(me, chosen)},
            device_id_type=MESH,
        )
        for number, chosen in enumerate(peers)
    ]
    for copy in seg_copies:
        copy.start()
    chips = lines[0].chips
    for item in lines:
        item.pass_on(1)
    gather.advance(0)
    for distance in range(2, chips):
        for item in lines:
            item.pass_on(distance)
    gather.finish(1)
    for item in lines:
        item.finish()
    for copy in seg_copies:
        copy.wait()
    seg_own.wait()


class Fetch:
    def __init__(self, nbits, cot, cot_all, s0, r0, l0):
        rows = cot.shape[0]
        own = pl.multiple_of(lax.axis_index("tensor") * rows, rows)
        self.local = pltpu.make_async_copy(cot, cot_all.at[pl.ds(own, rows), :], l0.at[0])
        self.gather = Gather(cot_all, rows, nbits, s0, r0)

    def begin(self):
        self.local.wait()
        self.gather.begin()

    def advance(self):
        self.gather.advance(0)

    def finish(self):
        self.gather.finish(1)


def fetch_scratch(nbits):
    return gather_sems(nbits) + [pltpu.SemaphoreType.DMA((1,))]


def fetch_kernel(nbits, cot, cot_all, *sems):
    greet(tensor_bits(nbits))
    fetch = Fetch(nbits, cot, cot_all, *sems)
    fetch.local.start()
    fetch.begin()
    fetch.advance()
    fetch.finish()


def middle_kernel(
    nbits, mixer, tokens, gain, middle, mid_all, landed, staged, s0, r0, s1, r1
):
    rows = tokens.shape[0]
    greet(tensor_bits(nbits))
    scatter = Scatter(mixer, landed, staged, rows, nbits, s0, r0)
    scatter.begin()
    scatter.run()

    def norm(row):
        values = tokens[pl.ds(row, CHUNK), :].astype(F32) + scatter.total(row, CHUNK)
        middle[pl.ds(row, CHUNK), :] = values
        scaled = values * rms_scale_of(values) * gain[...]
        mid_all[pl.ds(own_row(row, rows), CHUNK), :] = scaled.astype(BF16)

    chunks(rows, norm)
    gather = Gather(mid_all, rows, nbits, s1, r1)
    gather.begin()
    gather.finish()
    scatter.drain()


def result_kernel(nbits, ffn, middle, mixed, landed, staged, s0, r0):
    rows = middle.shape[0]
    greet(tensor_bits(nbits))
    scatter = Scatter(ffn, landed, staged, rows, nbits, s0, r0)
    scatter.begin()
    scatter.run()

    def add(row):
        values = middle[pl.ds(row, CHUNK), :] + scatter.total(row, CHUNK)
        mixed[pl.ds(row, CHUNK), :] = values.astype(BF16)

    chunks(rows, add)
    scatter.drain()


def norm_pull(values, gain, cotangent):
    scale = rms_scale_of(values)
    unit = values * scale
    inner = cotangent * gain
    back = scale * (inner - unit * jnp.mean(inner * unit, axis=-1, keepdims=True))
    return back, cotangent * unit


def eight_rows(values):
    total = values[0:8]
    for at in range(8, CHUNK, 8):
        total = total + values[at : at + 8]
    return total


class Product:
    def __init__(self, left, right, out, held, sems):
        self.left, self.right, self.out = left, right, out
        self.held, self.sems = held, sems
        self.width = held.shape[1]
        self.count = right.shape[0] // self.width
        self.done = 0

    def fetch(self, block):
        return pltpu.make_async_copy(
            self.right.at[pl.ds(block * self.width, self.width), :],
            self.held.at[block % 2],
            self.sems.at[block % 2],
        )

    def begin(self):
        self.fetch(0).start()

    def work(self, blocks):
        for block in range(self.done, min(self.done + blocks, self.count)):
            if block + 1 < self.count:
                self.fetch(block + 1).start()
            self.fetch(block).wait()

            def rows(span, block=block):
                found = times_transposed(self.left[span, :], self.held[block % 2])
                at = slice(block * self.width, (block + 1) * self.width)
                self.out[span, at] = found.astype(BF16)

            parts(self.left.shape[0], rows)
        self.done = min(self.done + blocks, self.count)


PRODUCT_BLOCK = 256


def product_scratch(depth):
    return [pltpu.VMEM((2, PRODUCT_BLOCK, depth), BF16), pltpu.SemaphoreType.DMA((2,))]


def turn_kernel(
    nbits,
    d_norm,
    cot,
    middle,
    gain,
    hidden,
    w_down,
    d_middle,
    d_mixer,
    d_gain,
    ffn,
    landed,
    staged,
    s0,
    r0,
    s1,
    r1,
    *product,
):
    rows = middle.shape[0]
    ahead = Product(hidden, w_down, ffn, *product)
    ahead.begin()
    greet(tensor_bits(nbits))
    scatter = Scatter(d_norm, landed, staged, rows, nbits, s0, r0)
    scatter.begin()
    d_gain[...] = jnp.zeros_like(d_gain)
    ahead.work(4)
    for step in range(nbits):
        scatter.advance(step)
        if step + 1 < nbits:
            ahead.work(2)

    def pull(row):
        span = pl.ds(row, CHUNK)
        back, gains = norm_pull(middle[span, :], gain[...], scatter.total(row, CHUNK))
        values = cot[span, :].astype(F32) + back
        d_middle[span, :] = values
        d_mixer[pl.ds(own_row(row, rows), CHUNK), :] = values.astype(BF16)
        d_gain[...] += eight_rows(gains)

    chunks(rows, pull)
    gather = Gather(d_mixer, rows, nbits, s1, r1)
    gather.begin()
    ahead.work(2)
    gather.advance(0)
    ahead.work(ahead.count)
    gather.finish(1)
    scatter.drain()


class LineSum:
    def __init__(self, whole, kept, swapped, staged, landed, send_sems, recv_sems, columns=None):
        self.whole, self.kept, self.swapped = whole, kept, swapped
        self.staged, self.landed = staged, landed
        self.sems = (send_sems, recv_sems)
        self.columns = columns
        self.chip, self.core, self.chips = dp_place()
        self.rows = whole.shape[2]

    def half(self, core):
        if self.columns is None:
            return self.whole.at[:, core]
        return self.whole.at[:, core, :, self.columns]

    def local(self):
        return pltpu.make_async_copy(
            self.half(self.core), self.kept, self.sems[0].at[2 * self.chips]
        )

    def swap(self):
        return pltpu.make_async_remote_copy(
            src_ref=self.half(1 - self.core),
            dst_ref=self.swapped,
            send_sem=self.sems[0].at[0],
            recv_sem=self.sems[1].at[0],
            device_id={"dp": dp_index(self.chip, 1 - self.core)},
            device_id_type=MESH,
        )

    def has(self, way, distance):
        return self.chip + distance < self.chips if way == UP else self.chip >= distance

    def slot(self, way, distance):
        return (0 if way == UP else self.chips - 1) + distance

    def hop(self, way, distance):
        return pltpu.make_async_remote_copy(
            src_ref=self.staged.at[self.slot(way, distance - 1)],
            dst_ref=self.landed.at[self.slot(way, distance - 1)],
            send_sem=self.sems[0].at[1 + self.slot(way, distance - 1)],
            recv_sem=self.sems[1].at[1 + self.slot(way, distance - 1)],
            device_id={"dp": dp_index(self.chip + way, self.core)},
            device_id_type=MESH,
        )

    def arrival(self, way, distance):
        number = self.slot(way, distance)
        return pltpu.make_async_remote_copy(
            src_ref=self.landed.at[number],
            dst_ref=self.landed.at[number],
            send_sem=self.sems[0].at[1 + number],
            recv_sem=self.sems[1].at[1 + number],
            device_id={"dp": dp_index(self.chip - way, self.core)},
            device_id_type=MESH,
        )

    def begin(self):
        self.swap().start()
        self.local().start()

    def both(self, chip, span):
        return self.kept[chip, span, :].astype(F32) + self.swapped[chip, span, :].astype(F32)

    def send(self, distance):
        if distance == self.chips - 1:
            self.local().wait()
            self.swap().wait_recv()
        for way in (UP, DOWN):

            @pl.when(self.has(way, distance))
            def _(way=way):
                chip = self.chip + way * distance
                slot = self.slot(way, distance - 1)

                def first(row):
                    span = pl.ds(row, CHUNK)
                    self.staged[slot, span, :] = self.both(chip, span).astype(BF16)

                def later(row):
                    span = pl.ds(row, CHUNK)
                    total = self.both(chip, span) + self.landed[
                        self.slot(way, distance), span, :
                    ].astype(F32)
                    self.staged[slot, span, :] = total.astype(BF16)

                if distance == self.chips - 1:
                    chunks(self.rows, first)
                else:

                    @pl.when(self.has(-way, 1))
                    def _():
                        self.arrival(way, distance).wait_recv()
                        chunks(self.rows, later)

                    @pl.when(jnp.logical_not(self.has(-way, 1)))
                    def _():
                        chunks(self.rows, first)

                self.hop(way, distance).start()

    def finish(self, store):
        below, above = self.has(DOWN, 1), self.has(UP, 1)

        def fill(slots):
            for way in slots:
                self.arrival(way, 0).wait_recv()

            def one(row):
                span = pl.ds(row, CHUNK)
                total = self.both(self.chip, span)
                for way in slots:
                    total = total + self.landed[self.slot(way, 0), span, :].astype(F32)
                store(span, total)

            chunks(self.rows, one)

        @pl.when(below & above)
        def _():
            fill((UP, DOWN))

        @pl.when(jnp.logical_not(above))
        def _():
            fill((UP,))

        @pl.when(jnp.logical_not(below))
        def _():
            fill((DOWN,))

    def drain(self):
        self.swap().wait_send()
        for way in (UP, DOWN):
            for distance in range(1, self.chips):

                @pl.when(self.has(way, distance))
                def _(way=way, distance=distance):
                    self.hop(way, distance).wait_send()


def line_scratch(ndp, rows, columns):
    chips = ndp // 2
    return [
        pltpu.VMEM((chips, rows, columns), BF16),
        pltpu.VMEM((chips, rows, columns), BF16),
        pltpu.VMEM((2 * chips - 2, rows, columns), BF16),
        pltpu.VMEM((2 * chips - 2, rows, columns), BF16),
        pltpu.SemaphoreType.DMA((2 * chips + 1,)),
        pltpu.SemaphoreType.DMA((2 * chips + 1,)),
    ]


RING = 6


def leave_kernel(nbits, tiled, *refs):
    refs = list(refs)

    def take(count):
        taken = refs[:count]
        del refs[:count]
        return taken

    d_norm, tokens, d_middle, gain, own_small, d_gain_mid = take(6)
    pieces = take(3)
    grad_input, sum_out, sum_y, sum_x, gate_all, small_all = take(6)
    landed, staged, s0, r0 = take(4)
    share = small_all.shape[2]
    gate = LineSum(pieces[0], *take(RING))
    lines = [LineSum(pieces[1], *take(RING))]
    if tiled:
        lines += [LineSum(pieces[2], *take(RING), pl.ds(at, share)) for at in (0, share)]
    else:
        lines += [LineSum(pieces[2], *take(RING))]
    d_gain, gains, gains_landed, small, small_landed = take(5)
    gain_s, gain_r, vec_s, vec_r, join_s, join_r, gate_s, gate_r = take(8)
    rows = tokens.shape[0]
    me = lax.axis_index("tensor")
    chip, core, chips = dp_place()
    peers = [chosen for chosen in subsets(tuple(range(nbits))) if chosen]
    others = [(shift, turn) for shift in range(chips) for turn in range(2)][1:]
    greet_peers(nbits, True, True)
    for line in [gate] + lines:
        line.begin()
    scatter = Scatter(d_norm, landed, staged, rows, nbits, s0, r0)
    scatter.begin()
    d_gain[...] = jnp.zeros_like(d_gain)
    far = list(range(chips - 1, 0, -1))
    for number in range(max(len(far), len(lines))):
        if number < len(far):
            gate.send(far[number])
        if number < len(lines):
            lines[number].send(far[0])
    scatter.advance(0)
    for distance in far[1:-1]:
        for line in lines:
            line.send(distance)
    for step in range(1, nbits):
        scatter.advance(step)

    def pull(row):
        span = pl.ds(row, CHUNK)
        back, parts = norm_pull(
            tokens[span, :].astype(F32), gain[...], scatter.total(row, CHUNK)
        )
        grad_input[span, :] = d_middle[span, :] + back
        d_gain[...] += eight_rows(parts)

    chunks(rows, pull)
    def store_gate(span, value):
        gate_all[me, chip, core, span, :] = value.astype(BF16)

    def gate_copy(number, ref, target):
        return pltpu.make_async_remote_copy(
            src_ref=ref,
            dst_ref=ref,
            send_sem=gate_s.at[number],
            recv_sem=gate_r.at[number],
            device_id=target,
            device_id_type=MESH,
        )

    def gate_line(shift):
        target = {"dp": dp_index((chip + shift) % chips, core)}
        return gate_copy(shift - 1, gate_all.at[me, chip, core], target)

    def gate_tensor(number, chosen):
        target = {"tensor": flipped(me, chosen)}
        return gate_copy(chips - 1 + number, gate_all.at[me, :, core], target)

    def gate_core():
        target = {"dp": dp_index(chip, 1 - core)}
        return gate_copy(chips - 1 + len(peers), gate_all.at[:, :, core], target)

    def start_gate():
        gate.finish(store_gate)
        for shift in range(1, chips):
            gate_line(shift).start()

    top = jnp.sum(d_gain[...], axis=0, keepdims=True)
    low = jnp.sum(d_gain_mid[...], axis=0, keepdims=True)
    place8 = lax.broadcasted_iota(jnp.int32, (8, share), 0)
    for index in range(1 << nbits):
        span = slice(index * share, (index + 1) * share)
        gains[index] = jnp.where(
            place8 == 6, top[:, span], jnp.where(place8 == 7, low[:, span], 0.0)
        )

    def gain_copy(number, chosen):
        peer = flipped(me, chosen)
        return pltpu.make_async_remote_copy(
            src_ref=gains.at[peer],
            dst_ref=gains_landed.at[number],
            send_sem=gain_s.at[number],
            recv_sem=gain_r.at[number],
            device_id={"tensor": peer},
            device_id_type=MESH,
        )

    for number, chosen in enumerate(peers):
        gain_copy(number, chosen).start()
    start_gate()
    if len(far) > 1:
        for line in lines:
            line.send(far[-1])
    total = own_small[...] + gains[me]
    for number, chosen in enumerate(peers):
        gain_copy(number, chosen).wait_recv()
        total = total + gains_landed[number]
    small[...] = total

    def vec_copy(number, shift, turn):
        other = dp_index((chip + shift) % chips, core + turn * (1 - 2 * core))
        return pltpu.make_async_remote_copy(
            src_ref=small,
            dst_ref=small_landed.at[number],
            send_sem=vec_s.at[number],
            recv_sem=vec_r.at[number],
            device_id={"dp": other},
            device_id_type=MESH,
        )

    for number, (shift, turn) in enumerate(others):
        vec_copy(number, shift, turn).start()

    for shift in range(1, chips):
        gate_line(shift).wait_recv()
    for number, chosen in enumerate(peers):
        gate_tensor(number, chosen).start()
    total = small[...]
    for number, (shift, turn) in enumerate(others):
        vec_copy(number, shift, turn).wait_recv()
        total = total + small_landed[number]
    small_all[me] = total

    def join_copy(number, chosen):
        return pltpu.make_async_remote_copy(
            src_ref=small_all.at[me],
            dst_ref=small_all.at[me],
            send_sem=join_s.at[number],
            recv_sem=join_r.at[number],
            device_id={"tensor": flipped(me, chosen)},
            device_id_type=MESH,
        )

    for number, chosen in enumerate(peers):
        join_copy(number, chosen).start()
    for number, chosen in enumerate(peers):
        gate_tensor(number, chosen).wait_recv()
    gate_core().start()

    def store_in(*targets):
        def store(span, value):
            for number, ref in enumerate(targets):
                ref[span, :] = value[:, number * share : (number + 1) * share]

        return store

    lines[0].finish(store_in(sum_out))
    if tiled:
        lines[1].finish(store_in(sum_y))
        lines[2].finish(store_in(sum_x))
    else:
        lines[1].finish(store_in(sum_y, sum_x))
    gate_core().wait()
    for shift in range(1, chips):
        gate_line(shift).wait_send()
    for number, chosen in enumerate(peers):
        gate_tensor(number, chosen).wait_send()
        gain_copy(number, chosen).wait_send()
        join_copy(number, chosen).wait()
    for number, (shift, turn) in enumerate(others):
        vec_copy(number, shift, turn).wait_send()
    scatter.drain()
    for line in [gate] + lines:
        line.drain()


def in_vmem(count):
    return [pl.BlockSpec(memory_space=pltpu.VMEM)] * count


def call_kernel(kernel, outs, scratch, number, *operands, far_in=(), far_out=(), cost_us=1):
    vmem = pl.BlockSpec(memory_space=pltpu.VMEM)
    far = pl.BlockSpec(memory_space=pl.ANY)
    return pl.pallas_call(
        kernel,
        out_shape=outs,
        in_specs=[far if i in far_in else vmem for i in range(len(operands))],
        out_specs=tuple(far if i in far_out else vmem for i in range(len(outs))),
        scratch_shapes=scratch,
        cost_estimate=pl.CostEstimate(
            flops=0, bytes_accessed=cost_us * 1_000_000, transcendentals=0
        ),
        compiler_params=pltpu.CompilerParams(
            collective_id=number, has_side_effects=True, vmem_limit_bytes=VMEM_BYTES
        ),
    )(*operands)


def sigmoid(values):
    return 1.0 / (1.0 + jnp.exp(-values))


def one_minus_exp(values):
    series = values / 7.0 + 1.0
    for order in (6.0, 5.0, 4.0, 3.0, 2.0):
        series = 1.0 + series * values / order
    return jnp.where(values > -0.3, -values * series, 1.0 - jnp.exp(values))


GELU_K = 0.7978845608028654
GELU_C = 0.044715


def gelu_parts(values):
    square = values * values
    bent = jnp.tanh(GELU_K * values * (1.0 + GELU_C * square))
    gelu = 0.5 * values * (1.0 + bent)
    slope = 0.5 * (1.0 + bent) + 0.5 * values * (1.0 - bent * bent) * GELU_K * (
        1.0 + 3.0 * GELU_C * square
    )
    return gelu, slope


def gate_terms(gate_a, gate_x, soft, since):
    sig_a = sigmoid(gate_a)
    sig_x = sigmoid(gate_x)
    log_decay = -8.0 * sig_a * soft
    decay = jnp.exp(log_decay)
    scale = jnp.sqrt(one_minus_exp(2.0 * log_decay))
    keep = since > 0.5
    return sig_a, sig_x, decay, jnp.where(keep, scale, 1.0), keep


def scan_down(decay, value, carry):
    place = lax.broadcasted_iota(jnp.int32, decay.shape, 0)
    for shift in (1, 2, 4):
        past = place >= shift
        moved = pltpu.roll(value, shift, 0)
        value = jnp.where(past, decay * moved + value, value)
        decay = jnp.where(past, decay * pltpu.roll(decay, shift, 0), decay)
    return decay * carry + value


def scan_up(decay, value, carry):
    place = lax.broadcasted_iota(jnp.int32, decay.shape, 0)
    factor = jnp.where(place < 7, pltpu.roll(decay, 7, 0), 1.0)
    for shift in (1, 2, 4):
        past = place < 8 - shift
        moved = pltpu.roll(value, 8 - shift, 0)
        value = jnp.where(past, factor * moved + value, value)
        factor = jnp.where(past, factor * pltpu.roll(factor, 8 - shift, 0), factor)
    return factor * carry + value


def forward_scan(conv_rows, gates, branch_y, soft, since, mixed, states, between=()):
    total_rows, width = states.shape

    def step(i, carry):
        row = pl.multiple_of(i * CHUNK, CHUNK)
        span = pl.ds(row, CHUNK)
        values = conv_rows(span).astype(F32)
        kept = []
        for at in range(0, CHUNK, 8):
            tile = pl.ds(row + at, 8)
            sig_a, sig_x, decay, scale, keep = gate_terms(
                gates[tile, :width], gates[tile, width:], soft[...], since[tile, :]
            )
            given = values[at : at + 8] * sig_x * scale
            state = scan_down(jnp.where(keep, decay, 0.0), given, carry)
            carry = state[7:8]
            states[tile, :] = state
            kept.append(state * gelu_parts(branch_y[tile, :])[0])
        mixed[span, :] = jnp.concatenate(kept, axis=0).astype(BF16)
        return carry

    steps, stretches = total_rows // CHUNK, len(between) + 1
    carry = jnp.zeros((1, width), F32)
    for stretch in range(stretches):
        first, last = stretch * steps // stretches, (stretch + 1) * steps // stretches
        carry = lax.fori_loop(first, last, step, carry)
        if stretch < len(between):
            between[stretch]()


def forward_scan_kernel(conv, gates, branch_y, soft, since, mixed, states):
    forward_scan(lambda span: conv[span, :], gates, branch_y, soft, since, mixed, states)


def backward_scan(
    d_mixed, conv_rows, gates, branch_y, states, soft, slope_soft, since, d_conv, d_gates, d_branch, d_decay
):
    total_rows, width = states.shape
    d_decay[...] = jnp.zeros_like(d_decay)

    def step(i, carry):
        row = pl.multiple_of(total_rows - CHUNK - i * CHUNK, CHUNK)
        span = pl.ds(row, CHUNK)
        values = conv_rows(span).astype(F32)
        kept = []
        for at in range(CHUNK - 8, -1, -8):
            tile = pl.ds(row + at, 8)
            soft_row = soft[...]
            sig_a, sig_x, decay, scale, keep = gate_terms(
                gates[tile, :width], gates[tile, width:], soft_row, since[tile, :]
            )
            value = values[at : at + 8]
            gelu, slope = gelu_parts(branch_y[tile, :])
            state = states[tile, :]
            upper = d_mixed[tile, :]
            held = jnp.where(keep, decay, 0.0)
            lam = scan_up(held, upper * gelu, carry)
            carry = held[0:1] * lam[0:1]
            d_conv[tile, :] = lam * sig_x * scale
            d_x = lam * value * scale * sig_x * (1.0 - sig_x)
            given = value * sig_x
            d_log = lam * (state - given * scale - given * decay * decay / scale)
            d_log = jnp.where(keep, d_log, 0.0)
            d_a = d_log * (-8.0 * soft_row) * sig_a * (1.0 - sig_a)
            d_decay[...] += d_log * (-8.0 * sig_a) * slope_soft[...]
            kept.append((d_a, d_x, upper * state * slope))
        kept = kept[::-1]
        d_gates[span, :width] = jnp.concatenate([k[0] for k in kept], axis=0).astype(BF16)
        d_gates[span, width:] = jnp.concatenate([k[1] for k in kept], axis=0).astype(BF16)
        d_branch[span, :] = jnp.concatenate([k[2] for k in kept], axis=0).astype(BF16)
        return carry

    lax.fori_loop(0, total_rows // CHUNK, step, jnp.zeros((1, width), F32))


def backward_scan_kernel(
    d_mixed, conv, gates, branch_y, states, soft, slope_soft, since, d_conv, d_gates, d_branch, d_decay
):
    backward_scan(
        d_mixed,
        lambda span: conv[span, :],
        gates,
        branch_y,
        states,
        soft,
        slope_soft,
        since,
        d_conv,
        d_gates,
        d_branch,
        d_decay,
    )


def times_transposed(left, right):
    return lax.dot_general(left, right, (((1,), (1,)), ((), ())), preferred_element_type=F32)


class HalfBlocks:
    def __init__(self, channels, block):
        self.odd = lax.axis_index("tensor") % 2
        self.half = block // 2
        self.block = block
        self.count = channels // block + 1
        self.channels = channels
        self.own = pl.multiple_of(self.odd * self.half, self.half)
        self.shared = (1 - self.odd) * (self.count - 1)
        self.mine_in_block = pl.multiple_of(self.odd * self.half, self.half)
        self.other_in_block = pl.multiple_of((1 - self.odd) * self.half, self.half)
        self.mine = pl.multiple_of((1 - self.odd) * (channels - self.half), self.half)
        self.pair = {"tensor": lax.axis_index("tensor") + 1 - 2 * self.odd}

    def full(self, index):
        block = index + self.odd
        return block, pl.multiple_of(index * self.block + self.odd * self.half, self.half)

    def span(self, block):
        return pl.ds(pl.multiple_of(block * self.block, self.block), self.block)

    def shared_part(self, start):
        return pl.ds(pl.multiple_of(self.shared * self.block + start, self.half), self.half)


PART = 256


def parts(rows, body):
    def step(i, carry):
        body(pl.ds(pl.multiple_of(i * PART, PART), PART))
        return carry

    lax.fori_loop(0, rows // PART, step, 0)


def recurrence_kernel(
    taps,
    nbits,
    branches,
    tap_rows,
    soft,
    since,
    weights,
    cot,
    mixed,
    states,
    window,
    gates,
    cot_all,
    send,
    recv,
    *sems,
):
    total_rows, width = states.shape
    block = weights.shape[2]
    place = HalfBlocks(width, block)
    branch_y, branch_x = branches.at[:, :width], branches.at[:, width:]
    greet(tensor_bits(nbits))
    fetch = Fetch(nbits, cot, cot_all, *sems)
    fetch.local.start()

    def conv(i, before):
        row = pl.multiple_of(i * CHUNK, CHUNK)
        kept = []
        for at in range(0, CHUNK, 8):
            tile = pl.ds(row + at, 8)
            values = branch_x[tile, :]
            line = lax.broadcasted_iota(jnp.int32, values.shape, 0)
            total = values * tap_rows[0:1, :]
            for tap in range(1, taps):
                moved = jnp.where(
                    line < tap, pltpu.roll(before, tap, 0), pltpu.roll(values, tap, 0)
                )
                moved = jnp.where(since[tile, :] > tap - 0.5, moved, 0.0)
                total = total + moved * tap_rows[tap : tap + 1, :]
            kept.append(total)
            before = values
        window[pl.ds(row, CHUNK), pl.ds(place.own, width)] = jnp.concatenate(
            kept, axis=0
        ).astype(BF16)
        return before

    lax.fori_loop(0, total_rows // CHUNK, conv, jnp.zeros((8, width), F32))
    source = window.at[:, place.shared_part(place.mine_in_block)]
    away = pl.multiple_of(place.odd * (place.count - 1) * block + place.mine_in_block, place.half)
    rim = pltpu.make_async_remote_copy(
        src_ref=source,
        dst_ref=window.at[:, pl.ds(away, place.half)],
        send_sem=send.at[0],
        recv_sem=recv.at[0],
        device_id=place.pair,
        device_id_type=MESH,
    )
    rim.start()
    fetch.begin()

    def full(span):
        for index in range(place.count - 1):
            number, at = place.full(index)
            cells = window[span, place.span(number)]
            for s in range(2):
                gates[span, pl.ds(s * width + at, block)] = jnp.dot(
                    cells, weights[s, number], preferred_element_type=F32
                )

    parts(total_rows, full)
    rim.wait()

    def shared(span):
        cells = window[span, place.span(place.shared)]
        for s in range(2):
            gates[span, pl.ds(s * width + place.mine, place.half)] = jnp.dot(
                cells,
                weights[s, place.shared, :, pl.ds(place.mine_in_block, place.half)],
                preferred_element_type=F32,
            )

    parts(total_rows, shared)
    forward_scan(
        lambda span: window[span, pl.ds(place.own, width)],
        gates,
        branch_y,
        soft,
        since,
        mixed,
        states,
        [fetch.advance],
    )
    fetch.finish()


def recurrence_back_kernel(
    taps,
    nbits,
    with_ffn,
    d_mixed,
    window,
    gates,
    branches,
    states,
    tap_rows,
    soft,
    slope_soft,
    since,
    weights,
    *refs,
):
    refs = list(refs)

    def take(count):
        taken = refs[:count]
        del refs[:count]
        return taken

    ffn, middle = take(2) if with_ffn else (None, None)
    d_branches, gate_grad, own_small = take(3)
    mixed = take(1)[0] if with_ffn else None
    d_conv, d_gates, given, taken, sums, send, recv = take(7)
    total_rows, width = states.shape
    block = weights.shape[2]
    place = HalfBlocks(width, block)
    half = place.half
    branch_y, branch_x = branches.at[:, :width], branches.at[:, width:]
    d_branch_y, d_branch_x = d_branches.at[:, :width], d_branches.at[:, width:]
    greet(tensor_bits(nbits))
    if with_ffn:
        scatter = Scatter(ffn, *take(2), middle.shape[0], nbits, *take(2))
        scatter.begin()
    backward_scan(
        d_mixed,
        lambda span: window[span, pl.ds(place.own, width)],
        gates,
        branch_y,
        states,
        soft,
        slope_soft,
        since,
        d_conv,
        d_gates,
        d_branch_y,
        sums.at[taps],
    )

    def to_pair(span):
        total = jnp.zeros((PART, half), F32)
        for s in range(2):
            total = total + times_transposed(
                d_gates[span, pl.ds(s * width + place.mine, half)],
                weights[
                    s,
                    place.shared,
                    pl.ds(place.other_in_block, half),
                    pl.ds(place.mine_in_block, half),
                ],
            )
        given[span, :] = total.astype(BF16)

    parts(total_rows, to_pair)
    rim = pltpu.make_async_remote_copy(
        src_ref=given,
        dst_ref=taken,
        send_sem=send.at[0],
        recv_sem=recv.at[0],
        device_id=place.pair,
        device_id_type=MESH,
    )
    rim.start()

    def full(span):
        for index in range(place.count - 1):
            number, at = place.full(index)
            total = d_conv[span, pl.ds(at, block)]
            for s in range(2):
                total = total + times_transposed(
                    d_gates[span, pl.ds(s * width + at, block)], weights[s, number]
                )
            d_conv[span, pl.ds(at, block)] = total
        total = d_conv[span, pl.ds(place.mine, half)]
        for s in range(2):
            total = total + times_transposed(
                d_gates[span, pl.ds(s * width + place.mine, half)],
                weights[
                    s,
                    place.shared,
                    pl.ds(place.mine_in_block, half),
                    pl.ds(place.mine_in_block, half),
                ],
            )
        d_conv[span, pl.ds(place.mine, half)] = total

    parts(total_rows, full)
    if with_ffn:
        scatter.advance(0)
    units = width // half
    for index in range(units):
        number = (index + place.odd) // 2
        cells = window[:, place.span(number)]
        both = jnp.concatenate(
            [d_gates[:, s * width + index * half : s * width + (index + 1) * half] for s in range(2)],
            axis=1,
        )
        found = lax.dot_general(
            cells, both, (((0,), (0,)), ((), ())), preferred_element_type=F32
        ).astype(BF16)
        gate_grad[2 * index] = found[:, :half]
        gate_grad[2 * index + 1] = found[:, half:]
    rim.wait()

    def add(span):
        d_conv[span, pl.ds(place.mine, half)] += taken[span, :].astype(F32)

    parts(total_rows, add)
    for tap in range(taps):
        sums[tap] = jnp.zeros((8, width), F32)

    def conv(i, after):
        row = pl.multiple_of(total_rows - CHUNK - i * CHUNK, CHUNK)
        kept = []
        for at in range(CHUNK - 8, -1, -8):
            tile = pl.ds(row + at, 8)
            values = d_conv[tile, :]
            line = lax.broadcasted_iota(jnp.int32, values.shape, 0)
            below = branch_x[tile, :]
            higher = pl.multiple_of((row + at - 8 + total_rows) % total_rows, 8)
            above = branch_x[pl.ds(higher, 8), :]
            total = values * tap_rows[0:1, :]
            sums[0] += values * below
            masked = []
            for tap in range(1, taps):
                here = jnp.where(since[tile, :] > tap - 0.5, values, 0.0)
                masked.append(here)
                moved = jnp.where(
                    line < 8 - tap,
                    pltpu.roll(here, 8 - tap, 0),
                    pltpu.roll(after[tap - 1], 8 - tap, 0),
                )
                total = total + moved * tap_rows[tap : tap + 1, :]
                source = jnp.where(
                    line < tap, pltpu.roll(above, tap, 0), pltpu.roll(below, tap, 0)
                )
                sums[tap] += here * source
            after = tuple(masked)
            kept.append(total)
        d_branch_x[pl.ds(row, CHUNK), :] = jnp.concatenate(kept[::-1], axis=0).astype(BF16)
        return after

    none = jnp.zeros((8, width), F32)
    lax.fori_loop(0, total_rows // CHUNK, conv, (none,) * (taps - 1))
    line = lax.broadcasted_iota(jnp.int32, (8, width), 0)
    total = jnp.zeros((8, width), F32)
    for tap in range(taps + 1):
        row = jnp.sum(sums[tap], axis=0, keepdims=True)
        total = jnp.where(line == tap, row, total)
    own_small[...] = total
    if with_ffn:
        for step in range(1, nbits):
            scatter.advance(step)

        def result(row):
            span = pl.ds(row, CHUNK)
            mixed[span, :] = (middle[span, :] + scatter.total(row, CHUNK)).astype(BF16)

        chunks(middle.shape[0], result)
        scatter.drain()


def finish_kernel(
    taps,
    gates,
    small,
    in_out,
    in_y,
    in_x,
    in_grad,
    in_mixed,
    in_both,
    in_down,
    whole,
    out_out,
    out_y,
    out_x,
    out_grad,
    out_mixed,
    out_gate,
    out_up,
    out_down,
    conv,
    decay,
    gain_in,
    gain_mid,
):
    held = whole.shape[1]
    pieces = gates.shape[0] // held

    def block(n, carry):
        for piece in range(pieces):
            for s in range(2):
                whole[s, n, :, piece * 128 : (piece + 1) * 128] = gates[
                    n * pieces + piece, s
                ].astype(F32)
        return carry

    lax.fori_loop(0, held, block, 0)
    units = out_gate.shape[1]

    def copy(row):
        span = pl.ds(row, CHUNK)
        out_out[span, :] = in_out[span, :].astype(F32)
        out_y[span, :] = in_y[span, :]
        out_x[span, :] = in_x[span, :]
        out_gate[span, :] = in_both[span, :units].astype(F32)
        out_up[span, :] = in_both[span, units:].astype(F32)
        out_down[span, :] = in_down[span, :].astype(F32)

    chunks(out_out.shape[0], copy)

    def own(row):
        span = pl.ds(row, CHUNK)
        out_grad[span, :] = in_grad[span, :]
        out_mixed[span, :] = in_mixed[span, :]

    chunks(out_grad.shape[0], own)

    @pl.when(pl.program_id(0) == 0)
    def _():
        share = small.shape[2]
        for index in range(small.shape[0]):
            span = slice(index * share, (index + 1) * share)
            conv[:, span] = small[index, :taps, :]
            for at in range(0, share, 128):
                row = (index * share + at) // 128
                decay[row : row + 1, :] = small[index, taps : taps + 1, at : at + 128]
                gain_in[row : row + 1, :] = small[index, 6:7, at : at + 128]
                gain_mid[row : row + 1, :] = small[index, 7:8, at : at + 128]


def finish(gate_all, small_all, sums, grad_input, mixed, both, down, taps, gate_shape):
    _, blocks, block, _ = gate_shape
    unit = gate_all.shape[-1]
    pieces = block // unit
    width = small_all.shape[0] * small_all.shape[2]
    rows, units = down.shape
    own_rows = grad_input.shape[0]
    grid = 2
    steps, held = rows // grid, own_rows // grid
    if unit != 128 or blocks % grid or rows % (16 * grid) or own_rows % (16 * grid):
        whole = gate_all.reshape(blocks, pieces, 2, block, unit).transpose(2, 0, 3, 1, 4)
        summed = small_all.transpose(1, 0, 2).reshape(8, width)
        whole = whole.reshape(gate_shape).astype(F32)
        wide = tuple(one.astype(F32) for one in (both[:, :units], both[:, units:], down))
        last = (summed[:taps], summed[taps], summed[6], summed[7])
        sums = tuple(one.astype(F32) for one in sums)
        return (whole, *sums, grad_input, mixed, *wide, *last)
    shape = jax.ShapeDtypeStruct

    def by_rows(count, columns):
        return pl.BlockSpec((count, columns), lambda n: (n, 0))

    def by_held(columns):
        return pl.BlockSpec((held, columns), lambda n: (n, 0))

    def whole_array(*dims):
        return pl.BlockSpec(dims, lambda n: (0,) * len(dims))

    columns = sums[0].shape[1]
    d_width = grad_input.shape[1]
    lines = width // 128
    found = pl.pallas_call(
        partial(finish_kernel, taps),
        grid=(grid,),
        in_specs=[
            pl.BlockSpec((blocks // grid * pieces, 2, block, unit), lambda n: (n, 0, 0, 0)),
            whole_array(*small_all.shape),
        ]
        + [by_rows(steps, columns)] * 3
        + [by_held(d_width)] * 2
        + [by_rows(steps, 2 * units), by_rows(steps, units)],
        out_specs=(
            (pl.BlockSpec((2, blocks // grid, block, block), lambda n: (0, n, 0, 0)),)
            + (by_rows(steps, columns),) * 3
            + (by_held(d_width),) * 2
            + (by_rows(steps, units),) * 3
            + (whole_array(taps, width),)
            + (whole_array(lines, 128),) * 3
        ),
        out_shape=(
            (shape(gate_shape, F32),)
            + (shape((rows, columns), F32),) * 3
            + (shape(grad_input.shape, F32), shape(mixed.shape, BF16))
            + (shape((rows, units), F32),) * 3
            + (shape((taps, width), F32),)
            + (shape((lines, 128), F32),) * 3
        ),
        compiler_params=pltpu.CompilerParams(vmem_limit_bytes=VMEM_BYTES),
    )(
        gate_all.reshape(blocks * pieces, 2, block, unit),
        small_all,
        *sums,
        grad_input,
        mixed,
        both,
        down,
    )
    return found[:10] + tuple(one.reshape(width) for one in found[10:])


def scan_call(kernel, outs, *operands):
    return pl.pallas_call(
        kernel,
        out_shape=outs,
        in_specs=in_vmem(len(operands)),
        out_specs=tuple(in_vmem(len(outs))),
        compiler_params=pltpu.CompilerParams(vmem_limit_bytes=VMEM_BYTES),
    )(*operands)


class Rim:
    def __init__(self, route, back, source, first, width, room):
        self.route, self.back = route, back
        self.source, self.first, self.width = source, first, width
        self.room = room

    def fetch(self, values):
        part = lax.dynamic_slice_in_dim(values, self.source, self.width, 1)
        return lax.ppermute(part, "tensor", self.route)

    def give(self, part):
        return lax.ppermute(part, "tensor", self.back)

    def add(self, values, part):
        zeros = jnp.zeros(values.shape, F32)
        return values + lax.dynamic_update_slice_in_dim(
            zeros, part.astype(F32), self.source, 1
        )

    def window(self, channels):
        return (channels // self.width + 4) * self.width


def gate_rims(channels, block_size, ntensor, offset):
    up = [(i, i + 1) for i in range(ntensor - 1)]
    down = [(i + 1, i) for i in range(ntensor - 1)]
    last = jnp.int32(channels - block_size)
    return [
        Rim(up, down, last, offset - block_size, block_size, block_size),
        Rim(down, up, jnp.int32(0), offset + channels, block_size, block_size),
    ]


def same_block(first, count, offset, channels, block_size):
    rows = (first + jnp.arange(count, dtype=jnp.int32))[:, None]
    columns = (offset + jnp.arange(channels, dtype=jnp.int32))[None, :]
    return (rows + block_size) // block_size == (columns + block_size) // block_size


def gate_dense(gate_w, offset, first, count):
    block_size = gate_w.shape[2]
    total = gate_w.shape[1] * block_size
    channels = total // lax.axis_size("tensor")
    columns = gate_w.transpose(2, 0, 1, 3).reshape(block_size, 2, total)
    columns = lax.dynamic_slice_in_dim(columns, offset, channels, 2)
    copies = -(-count // block_size) + 1
    tall = jnp.concatenate([columns] * copies, axis=0)
    tall = lax.dynamic_slice_in_dim(tall, (first + block_size) % block_size, count, 0)
    same = same_block(first, count, offset, channels, block_size)
    dense = jnp.where(same[:, None, :], tall, jnp.zeros_like(tall))
    return dense.reshape(count, 2 * channels)


def doc_starts(seg_ids, seq_len):
    places = jnp.arange(seg_ids.shape[0], dtype=jnp.int32)
    before = jnp.concatenate([seg_ids[:1], seg_ids[:-1]])
    resets = (places % seq_len == 0) | (seg_ids != before)
    starts = lax.cummax(jnp.where(resets, places, jnp.zeros_like(places)), axis=0)
    return starts


def causal_conv(starts, values, kernel):
    places = jnp.arange(values.shape[0], dtype=jnp.int32)
    total = values * kernel[0]
    for offset_k in range(1, kernel.shape[0]):
        moved = jnp.concatenate(
            [jnp.zeros((offset_k, values.shape[1]), values.dtype), values[:-offset_k]], axis=0
        )
        valid = (places - offset_k >= starts)[:, None]
        total = total + jnp.where(valid, moved, jnp.zeros_like(moved)) * kernel[offset_k]
    return total


def geglu(gate_val, up_val):
    return jax.nn.gelu(gate_val, approximate=True) * up_val


def rows_times(left, right):
    return lax.dot_general(left, right, (((1,), (1,)), ((), ())), preferred_element_type=F32)


def rows_back(lefts, rights):
    total = rows_times(lefts[0], rights[0])
    return total + rows_times(lefts[1], rights[1])


def inner_rows(left, right):
    return lax.dot_general(left, right, (((0,), (0,)), ((), ())), preferred_element_type=F32)


def halved(grad, ndp):
    return grad.reshape(ndp // 2, 2, grad.shape[0] // ndp, grad.shape[1])


def body(
    tokens,
    segments,
    cotangent,
    norm_gain,
    w_y,
    w_x,
    conv_w,
    gate_w,
    decay_param,
    w_out,
    mlp_gain,
    w_gate,
    w_up,
    w_down,
):
    ntensor = lax.axis_size("tensor")
    ndp = lax.axis_size("dp")
    nbits = log2_of(ntensor)
    tindex = lax.axis_index("tensor")
    own_rows, width = tokens.shape
    group_rows = own_rows * ntensor
    block_size = gate_w.shape[2]
    nblocks = gate_w.shape[1]
    dp_rows, channels = w_y.shape
    taps = conv_w.shape[0]
    offset = tindex * channels
    shape = jax.ShapeDtypeStruct
    gain_in = norm_gain.reshape(1, width)
    gain_mid = mlp_gain.reshape(1, width)
    seg_rows_of = own_rows // 128
    tiled = channels % 128 == 0
    w_yx = (w_y, w_x) if tiled else (jnp.concatenate([w_y, w_x], axis=1),)
    normed_rows, seg_all, wyx_loc, wout_loc = call_kernel(
        partial(enter_kernel, nbits, len(w_yx)),
        (
            shape((group_rows, width), BF16),
            shape((ntensor, seg_rows_of, 128), jnp.int32),
            shape((dp_rows * ndp, 2 * channels), BF16),
            shape((dp_rows * ndp, channels), BF16),
        ),
        [pltpu.VMEM((1, width), F32)]
        + gather_sems(nbits)
        + [pltpu.SemaphoreType.DMA((ntensor - 1,)), pltpu.SemaphoreType.DMA((ntensor - 1,))]
        + [pltpu.SemaphoreType.DMA((1,))]
        + line_sems(ndp) * (len(w_yx) + 1),
        0,
        tokens,
        segments.reshape(seg_rows_of, 128),
        norm_gain.reshape(width // 128, 128),
        *w_yx,
        w_out,
        far_in=tuple(range(3, 4 + len(w_yx))),
        far_out=(2, 3),
    )
    units = w_gate.shape[1]
    w_both = jnp.concatenate([w_gate, w_up], axis=1)
    w_both, w_down, normed_rows = lax.optimization_barrier((w_both, w_down, normed_rows))
    both_loc = lax.all_gather(w_both, "dp", axis=0, tiled=True)
    wd_loc = lax.all_gather(w_down, "dp", axis=0, tiled=True)
    seg_rows = seg_all.reshape(group_rows)
    starts = doc_starts(seg_rows, group_rows)
    conv_loc = lax.dynamic_slice_in_dim(conv_w, offset, channels, 1)
    decay_loc = lax.dynamic_slice_in_dim(decay_param, offset, channels, 0).reshape(1, channels)
    soft = jax.nn.softplus(decay_loc)
    slope_soft = jax.nn.sigmoid(decay_loc)
    half_blocks = (
        channels % block_size == block_size // 2 and ntensor % 2 == 0 and block_size % 256 == 0
    )
    since = (jnp.arange(group_rows, dtype=jnp.int32) - starts).astype(F32)[:, None]
    branches = jnp.dot(normed_rows, wyx_loc, preferred_element_type=F32)
    if half_blocks:
        span_blocks = channels // block_size + 1
        w_window = lax.dynamic_slice_in_dim(gate_w, offset // block_size, span_blocks, 1)
        taps_pad = jnp.concatenate([conv_loc, jnp.zeros((8 - taps, channels), F32)], axis=0)
        mixed_low, states, window, gate_pre, cot_rows = call_kernel(
            partial(recurrence_kernel, taps, nbits),
            (
                shape((group_rows, channels), BF16),
                shape((group_rows, channels), F32),
                shape((group_rows, span_blocks * block_size), BF16),
                shape((group_rows, 2 * channels), F32),
                shape((group_rows, width), BF16),
            ),
            [pltpu.SemaphoreType.DMA((1,)), pltpu.SemaphoreType.DMA((1,))]
            + fetch_scratch(nbits),
            5,
            branches,
            taps_pad,
            soft,
            since,
            w_window,
            cotangent,
        )
    else:
        branch_y, branch_x = branches[:, :channels], branches[:, channels:]
        (cot_rows,) = call_kernel(
            partial(fetch_kernel, nbits),
            (shape((group_rows, width), BF16),),
            fetch_scratch(nbits),
            5,
            cotangent,
        )
        rims = gate_rims(channels, block_size, ntensor, offset)
        own_dense = gate_dense(gate_w, offset, offset, channels)
        rim_dense = [gate_dense(gate_w, offset, rim.first, rim.width) for rim in rims]
        conv_out, conv_pull = jax.vjp(partial(causal_conv, starts), branch_x, conv_loc)
        conv_low = conv_out.astype(BF16)
        rim_cells = [rim.fetch(conv_low) for rim in rims]
        gate_pre = jnp.dot(conv_low, own_dense, preferred_element_type=F32)
        for cells, dense in zip(rim_cells, rim_dense):
            gate_pre = gate_pre + jnp.dot(cells, dense, preferred_element_type=F32)
        mixed_low, states = scan_call(
            forward_scan_kernel,
            (shape((group_rows, channels), BF16), shape((group_rows, channels), F32)),
            conv_low,
            gate_pre,
            branch_y,
            soft,
            since,
        )
    middle, mid_rows = call_kernel(
        partial(middle_kernel, nbits),
        (shape((own_rows, width), F32), shape((group_rows, width), BF16)),
        scatter_scratch(own_rows, width, nbits) + gather_sems(nbits),
        1,
        rows_times(mixed_low, wout_loc).astype(BF16),
        tokens,
        gain_mid,
    )
    pre = jnp.dot(mid_rows, both_loc, preferred_element_type=F32)
    hidden, act_pull = jax.vjp(geglu, pre[:, :units], pre[:, units:])
    hidden_low = hidden.astype(BF16)
    grad_wd = inner_rows(cot_rows, hidden_low).astype(BF16)
    sum_wd = lax.psum_scatter(grad_wd, "dp", scatter_dimension=0, tiled=True)
    grad_wd, wd_loc = lax.optimization_barrier((grad_wd, wd_loc))
    d_hidden = jnp.dot(cot_rows, wd_loc, preferred_element_type=F32)
    d_gate, d_up = act_pull(d_hidden)
    d_pre = jnp.concatenate([d_gate.astype(BF16), d_up.astype(BF16)], axis=1)
    grad_both = inner_rows(mid_rows, d_pre).astype(BF16)
    sum_both = lax.psum_scatter(grad_both, "dp", scatter_dimension=0, tiled=True)
    d_pre, grad_both = lax.optimization_barrier((d_pre, grad_both))
    d_mid_part = rows_times(d_pre, both_loc).astype(BF16)
    d_middle, d_mixer, d_gain_mid, ffn_part = call_kernel(
        partial(turn_kernel, nbits),
        (
            shape((own_rows, width), F32),
            shape((group_rows, width), BF16),
            shape((8, width), F32),
            shape((group_rows, width), BF16),
        ),
        scatter_scratch(own_rows, width, nbits) + gather_sems(nbits) + product_scratch(units),
        2,
        d_mid_part,
        cotangent,
        middle,
        gain_mid,
        hidden_low,
        wd_loc,
        far_in=(5,),
    )
    d_mixer, sum_wd = lax.optimization_barrier((d_mixer, sum_wd))
    d_mixed_in = jnp.dot(d_mixer, wout_loc, preferred_element_type=F32)
    unit = math.gcd(channels, block_size)
    merged = half_blocks and nbits <= 2
    if half_blocks:
        found = call_kernel(
            partial(recurrence_back_kernel, taps, nbits, merged),
            (
                shape((group_rows, 2 * channels), BF16),
                shape((channels // unit * 2, block_size, unit), BF16),
                shape((8, channels), F32),
            )
            + ((shape((own_rows, width), BF16),) if merged else ()),
            [
                pltpu.VMEM((group_rows, channels), F32),
                pltpu.VMEM((group_rows, 2 * channels), BF16),
                pltpu.VMEM((group_rows, unit), BF16),
                pltpu.VMEM((group_rows, unit), BF16),
                pltpu.VMEM((taps + 1, 8, channels), F32),
                pltpu.SemaphoreType.DMA((1,)),
                pltpu.SemaphoreType.DMA((1,)),
            ]
            + (scatter_scratch(own_rows, width, nbits) if merged else []),
            6,
            d_mixed_in,
            window,
            gate_pre,
            branches,
            states,
            taps_pad,
            soft,
            slope_soft,
            since,
            w_window,
            *((ffn_part, middle) if merged else ()),
        )
        d_branches, gate_grad, own_small = found[:3]
        gate_grad = gate_grad.reshape(channels // unit * 2 * block_size, unit)
    else:
        d_conv, d_gate_low, d_branch_y, d_decay = scan_call(
            backward_scan_kernel,
            (
                shape((group_rows, channels), F32),
                shape((group_rows, 2 * channels), BF16),
                shape((group_rows, channels), BF16),
                shape((8, channels), F32),
            ),
            d_mixed_in,
            conv_low,
            gate_pre,
            branch_y,
            states,
            soft,
            slope_soft,
            since,
        )
        given = [rows_times(d_gate_low, dense).astype(BF16) for dense in rim_dense]
        taken = [rim.give(part) for rim, part in zip(rims, given)]
        d_conv_out = d_conv + rows_times(d_gate_low, own_dense)
        for rim, part in zip(rims, taken):
            d_conv_out = rim.add(d_conv_out, part)
        d_branch_x, grad_conv_loc = conv_pull(d_conv_out)
        d_branches = jnp.concatenate([d_branch_y, d_branch_x.astype(BF16)], axis=1)
        base = offset // block_size * block_size - rims[0].room
        window_rows = rims[0].window(channels)
        picked = jnp.zeros((window_rows, 2 * channels), F32)
        for first, cells in [(offset, conv_low)] + [(r.first, c) for r, c in zip(rims, rim_cells)]:
            part = inner_rows(cells, d_gate_low)
            same = same_block(first, cells.shape[1], offset, channels, block_size)
            part = jnp.where(jnp.concatenate([same, same], axis=1), part, 0.0)
            picked = lax.dynamic_update_slice(picked, part, (first - base, jnp.int32(0)))
        picked = picked.reshape(window_rows // block_size, block_size, 2, channels // unit, unit)
        gate_grad = picked.sum(axis=0).astype(BF16).transpose(2, 1, 0, 3)
        gate_grad = gate_grad.reshape(channels // unit * 2 * block_size, unit)
        own_small = jnp.concatenate(
            [
                grad_conv_loc,
                jnp.sum(d_decay, axis=0, keepdims=True),
                jnp.zeros((7 - taps, channels), F32),
            ],
            axis=0,
        )

    grad_wout = inner_rows(d_mixer, mixed_low).astype(BF16)
    grad_wyx = inner_rows(normed_rows, d_branches).astype(BF16)
    d_normed = rows_times(d_branches, wyx_loc).astype(BF16)
    d_normed, grad_wyx, sum_both = lax.optimization_barrier((d_normed, grad_wyx, sum_both))

    pieces = [halved(grad, ndp) for grad in (gate_grad, grad_wout, grad_wyx)]
    peers = ntensor - 1
    gate_rows = gate_grad.shape[0] // ndp
    dma = pltpu.SemaphoreType.DMA
    scratch = scatter_scratch(own_rows, width, nbits)
    scratch += line_scratch(ndp, gate_rows, unit) + line_scratch(ndp, dp_rows, channels)
    if tiled:
        scratch += line_scratch(ndp, dp_rows, channels) * 2
    else:
        scratch += line_scratch(ndp, dp_rows, 2 * channels)
    scratch += [
        pltpu.VMEM((8, width), F32),
        pltpu.VMEM((ntensor, 8, channels), F32),
        pltpu.VMEM((peers, 8, channels), F32),
        pltpu.VMEM((8, channels), F32),
        pltpu.VMEM((ndp - 1, 8, channels), F32),
    ]
    scratch += [dma((peers,)), dma((peers,)), dma((ndp - 1,)), dma((ndp - 1,))]
    scratch += [dma((peers,)), dma((peers,)), dma((peers + ndp,)), dma((peers + ndp,))]
    grad_input, sum_wout, sum_wy, sum_wx, gate_all, small_all = call_kernel(
        partial(leave_kernel, nbits, tiled),
        (shape((own_rows, width), F32),)
        + (shape((dp_rows, channels), F32),) * 3
        + (
            shape((ntensor, ndp // 2, 2, gate_rows, unit), BF16),
            shape((ntensor, 8, channels), F32),
        ),
        scratch,
        3,
        d_normed,
        tokens,
        d_middle,
        gain_in,
        own_small,
        d_gain_mid,
        *pieces,
        far_in=(6, 7, 8),
    )
    if merged:
        mixed = found[3]
    else:
        (mixed,) = call_kernel(
            partial(result_kernel, nbits),
            (shape((own_rows, width), BF16),),
            scatter_scratch(own_rows, width, nbits),
            4,
            ffn_part,
            middle,
        )
    found = finish(
        gate_all,
        small_all,
        (sum_wout, sum_wy, sum_wx),
        grad_input,
        mixed,
        sum_both,
        sum_wd,
        taps,
        gate_w.shape,
    )
    sum_gate, sum_wout, sum_wy, sum_wx, grad_input, mixed = found[:6]
    sum_wg, sum_wu, sum_wd, sum_conv, sum_decay, sum_gain_in, sum_gain_mid = found[6:]
    return (
        mixed,
        grad_input,
        sum_gain_in,
        sum_wy,
        sum_wx,
        sum_conv,
        sum_gate,
        sum_decay,
        sum_wout,
        sum_gain_mid,
        sum_wg,
        sum_wu,
        sum_wd,
    )


def solution(mesh):
    split = P(("dp", "tensor"), None)
    weight = P("dp", "tensor")
    return jax.shard_map(
        body,
        mesh=mesh,
        in_specs=(
            split,
            P(("dp", "tensor")),
            split,
            P(),
            weight,
            weight,
            P(),
            P(),
            P(),
            weight,
            P(),
            weight,
            weight,
            weight,
        ),
        out_specs=(
            split,
            split,
            P(),
            weight,
            weight,
            P(),
            P(),
            P(),
            weight,
            P(),
            weight,
            weight,
            weight,
        ),
        check_vma=False,
    )
```

```python
import math
from functools import partial

import jax
import jax.numpy as jnp
from jax import lax
from jax.experimental import pallas as pl
from jax.experimental.pallas import tpu as pltpu
from jax.sharding import PartitionSpec as P

EPSILON = 1e-06
MESH = pl.DeviceIdType.MESH
VMEM_BYTES = 56 * 1024 * 1024
CHUNK = 16
F32 = jnp.float32
BF16 = jnp.bfloat16


def subsets(bits):
    found = [()]
    for bit in bits:
        found = found + [chosen + (bit,) for chosen in found]
    return found


def flipped(index, bits):
    for bit in bits:
        mine = (index // (1 << bit)) % 2
        index = index + (1 - 2 * mine) * (1 << bit)
    return index


def log2_of(count):
    assert count & (count - 1) == 0
    return count.bit_length() - 1


def greet(axis_bits):
    barrier = pltpu.get_barrier_semaphore()
    for axis, bit in axis_bits:
        peer = flipped(lax.axis_index(axis), (bit,))
        pl.semaphore_signal(barrier, inc=1, device_id={axis: peer}, device_id_type=MESH)
    pl.semaphore_wait(barrier, len(axis_bits))


def halves_of(nbits, columns):
    half = columns // 2
    ups = tuple(range(nbits))
    return ((ups, 0, half), (ups[::-1], half, half))


class Gather:
    def __init__(self, ref, rows, nbits, send_sems, recv_sems):
        self.ref, self.rows, self.nbits = ref, rows, nbits
        self.sems = (send_sems, recv_sems)
        self.me = lax.axis_index("tensor")
        self.plan = []
        number = 0
        for half, (order, at, width) in enumerate(halves_of(nbits, ref.shape[1])):
            for step, bit in enumerate(order):
                for known in subsets(order[:step]):
                    self.plan.append((half, step, known, bit, at, width, number))
                    number += 1
        self.count = number

    def copy(self, item):
        half, step, known, bit, at, width, number = item
        row = pl.multiple_of(flipped(self.me, known) * self.rows, self.rows)
        piece = self.ref.at[pl.ds(row, self.rows), pl.ds(at, width)]
        return pltpu.make_async_remote_copy(
            src_ref=piece,
            dst_ref=piece,
            send_sem=self.sems[0].at[number],
            recv_sem=self.sems[1].at[number],
            device_id={"tensor": flipped(self.me, (bit,))},
            device_id_type=MESH,
        )

    def begin(self):
        for item in sorted(self.plan, key=lambda it: it[1]):
            if item[2] == ():
                self.copy(item).start()

    def advance(self, step):
        for item in self.plan:
            half, at_step, known, bit, at, width, number = item
            if at_step == step:
                self.copy(item).wait_recv()
                block = known + (bit,)
                for later in self.plan:
                    if later[0] == half and set(later[2]) == set(block):
                        self.copy(later).start()

    def finish(self, step=0):
        for at_step in range(step, self.nbits):
            self.advance(at_step)
        for item in self.plan:
            self.copy(item).wait_send()


def gather_copies(nbits):
    return 2 * ((1 << nbits) - 1)


class Scatter:
    def __init__(self, ref, landed, staged, rows, nbits, send_sems, recv_sems):
        self.ref, self.landed, self.staged = ref, landed, staged
        self.rows, self.nbits = rows, nbits
        self.sems = (send_sems, recv_sems)
        self.me = lax.axis_index("tensor")
        self.plan, self.slot = [], {}
        number = 0
        for half, (order, at, width) in enumerate(halves_of(nbits, ref.shape[1])):
            for step, bit in enumerate(order):
                for rest in subsets(order[step + 1 :])[::-1]:
                    self.plan.append((half, step, rest, bit, at, width, number))
                    if step > 0:
                        self.slot[number] = len(self.slot)
                    number += 1

    def copy(self, item):
        half, step, rest, bit, at, width, number = item
        if step == 0:
            row = pl.multiple_of(flipped(self.me, rest + (bit,)) * self.rows, self.rows)
            source = self.ref.at[pl.ds(row, self.rows), pl.ds(at, width)]
        else:
            source = self.staged.at[self.slot[number]]
        return pltpu.make_async_remote_copy(
            src_ref=source,
            dst_ref=self.landed.at[number],
            send_sem=self.sems[0].at[number],
            recv_sem=self.sems[1].at[number],
            device_id={"tensor": flipped(self.me, (bit,))},
            device_id_type=MESH,
        )

    def begin(self):
        for item in sorted(self.plan, key=lambda it: (len(it[2]) == 0)):
            if item[1] == 0:
                self.copy(item).start()

    def partial_sum(self, half, block, before, row, size):
        at, width = halves_of(self.nbits, self.ref.shape[1])[half][1:]
        base = pl.multiple_of(flipped(self.me, block) * self.rows + row, size)
        total = self.ref[pl.ds(base, size), pl.ds(at, width)].astype(F32)
        for it in self.plan:
            if it[0] == half and it[1] < before and set(it[2]) == set(block):
                total = total + self.landed[it[6], pl.ds(row, size), :].astype(F32)
        return total

    def advance(self, step):
        for half in range(2):
            for item in self.plan:
                if item[0] == half and item[1] == step:
                    self.copy(item).wait_recv()
            for item in self.plan:
                if item[0] == half and item[1] == step + 1:

                    def fill(row, item=item):
                        value = self.partial_sum(
                            item[0], item[2] + (item[3],), item[1], row, CHUNK
                        )
                        where = (self.slot[item[6]], pl.ds(row, CHUNK))
                        self.staged[where + (slice(None),)] = value.astype(BF16)

                    chunks(self.rows, fill)
                    self.copy(item).start()

    def run(self):
        for step in range(self.nbits):
            self.advance(step)

    def total(self, row, size):
        return jnp.concatenate(
            [self.partial_sum(half, (), self.nbits, row, size) for half in range(2)], axis=1
        )

    def drain(self):
        for item in self.plan:
            self.copy(item).wait_send()


def scatter_scratch(rows, columns, nbits):
    copies = gather_copies(nbits)
    later = max(1, copies - (1 << nbits))
    return [
        pltpu.VMEM((copies, rows, columns // 2), BF16),
        pltpu.VMEM((later, rows, columns // 2), BF16),
        pltpu.SemaphoreType.DMA((copies,)),
        pltpu.SemaphoreType.DMA((copies,)),
    ]


def gather_sems(nbits):
    copies = gather_copies(nbits)
    return [pltpu.SemaphoreType.DMA((copies,)), pltpu.SemaphoreType.DMA((copies,))]


def tensor_bits(nbits):
    return [("tensor", bit) for bit in range(nbits)]


def rms_scale_of(values):
    return lax.rsqrt(jnp.mean(values * values, axis=-1, keepdims=True) + EPSILON)


def chunks(rows, body):
    def step(i, carry):
        body(pl.multiple_of(i * CHUNK, CHUNK))
        return carry

    lax.fori_loop(0, rows // CHUNK, step, 0)


def own_row(row, rows):
    return pl.multiple_of(lax.axis_index("tensor") * rows + row, CHUNK)


def dp_place():
    me = lax.axis_index("dp")
    return me // 2, me % 2, lax.axis_size("dp") // 2


def dp_index(chip, core):
    return chip * 2 + core


UP, DOWN = 1, -1


class LineGather:
    def __init__(self, own, whole, send_sems, recv_sems, columns=None):
        self.own, self.whole = own, whole
        self.sems = (send_sems, recv_sems)
        self.chip, self.core, self.chips = dp_place()
        self.rows = own.shape[0]
        self.columns = slice(None) if columns is None else columns

    def block(self, chip):
        row = pl.multiple_of(dp_index(chip, self.core) * self.rows, self.rows)
        return self.whole.at[pl.ds(row, self.rows), self.columns]

    def has(self, way, distance):
        return self.chip >= distance if way == UP else self.chip + distance < self.chips

    def number(self, way, distance):
        return (0 if way == UP else self.chips) + distance

    def along(self, way, distance):
        block = self.block(self.chip - way * distance)
        return pltpu.make_async_remote_copy(
            src_ref=self.own if distance == 0 else block,
            dst_ref=block,
            send_sem=self.sems[0].at[self.number(way, distance)],
            recv_sem=self.sems[1].at[self.number(way, distance + 1)],
            device_id={"dp": dp_index(self.chip + way, self.core)},
            device_id_type=MESH,
        )

    def arrival(self, way, distance):
        block = self.block(self.chip - way * distance)
        return pltpu.make_async_remote_copy(
            src_ref=block,
            dst_ref=block,
            send_sem=self.sems[0].at[self.number(way, distance)],
            recv_sem=self.sems[1].at[self.number(way, distance)],
            device_id={"dp": dp_index(self.chip + way, self.core)},
            device_id_type=MESH,
        )

    def across(self, way, distance):
        block = self.block(self.chip - way * distance)
        number = 2 * self.chips + self.number(way, distance)
        return pltpu.make_async_remote_copy(
            src_ref=self.own if distance == 0 else block,
            dst_ref=block,
            send_sem=self.sems[0].at[number],
            recv_sem=self.sems[1].at[number],
            device_id={"dp": dp_index(self.chip, 1 - self.core)},
            device_id_type=MESH,
        )

    def local(self):
        return pltpu.make_async_copy(
            self.own, self.block(self.chip), self.sems[0].at[4 * self.chips]
        )

    def begin(self):
        for way in (UP, DOWN):

            @pl.when(self.has(-way, 1))
            def _(way=way):
                self.along(way, 0).start()

        self.across(UP, 0).start()
        self.local().start()

    def pass_on(self, distance):
        for way in (UP, DOWN):

            @pl.when(self.has(way, distance))
            def _(way=way):
                self.arrival(way, distance).wait_recv()

                @pl.when(self.has(-way, 1))
                def _():
                    self.along(way, distance).start()

                self.across(way, distance).start()

    def finish(self):
        self.across(UP, 0).wait()
        self.local().wait()
        for way in (UP, DOWN):
            for distance in range(self.chips):

                @pl.when(self.has(way, distance) & self.has(-way, 1))
                def _(way=way, distance=distance):
                    self.along(way, distance).wait_send()

                if distance:

                    @pl.when(self.has(way, distance))
                    def _(way=way, distance=distance):
                        self.across(way, distance).wait()


def line_sems(ndp):
    chips = ndp // 2
    return [pltpu.SemaphoreType.DMA((4 * chips + 1,)), pltpu.SemaphoreType.DMA((4 * chips + 1,))]


def greet_peers(nbits, all_tensor, whole_dp):
    me = lax.axis_index("tensor")
    chip, core, chips = dp_place()
    barrier = pltpu.get_barrier_semaphore()

    def signal(target):
        pl.semaphore_signal(barrier, inc=1, device_id=target, device_id_type=MESH)

    met = 0
    for chosen in subsets(tuple(range(nbits))):
        if chosen and (all_tensor or len(chosen) == 1):
            signal({"tensor": flipped(me, chosen)})
            met += 1
    if whole_dp:
        for shift in range(chips):
            for turn in range(2):
                if (shift, turn) != (0, 0):
                    other = dp_index((chip + shift) % chips, core + turn * (1 - 2 * core))
                    signal({"dp": other})
                    met += 1
    else:
        signal({"dp": dp_index(chip, 1 - core)})
        met += 1

        for shift in sorted({1 % chips, chips - 1} - {0}):
            signal({"dp": dp_index((chip + shift) % chips, core)})
            met += 1

    pl.semaphore_wait(barrier, met)


def widen(rows, wide):
    for row in range(rows.shape[0]):
        wide[:, row * 128 : (row + 1) * 128] = rows[row : row + 1, :]


def enter_kernel(
    nbits, parts_yx, tokens, seg, gain, *refs
):
    w_yx, w_out = refs[:parts_yx], refs[parts_yx]
    normed_all, seg_all, wyx_all, wout_all, gain_row, s0, r0, s2, r2, l0, *line = refs[
        parts_yx + 1 :
    ]
    rows = tokens.shape[0]
    me = lax.axis_index("tensor")
    peers = [chosen for chosen in subsets(tuple(range(nbits))) if chosen]
    greet_peers(nbits, True, False)
    width = wyx_all.shape[1] // parts_yx
    lines = [
        LineGather(
            own,
            wyx_all,
            line[2 * number],
            line[2 * number + 1],
            pl.ds(number * width, width) if parts_yx > 1 else None,
        )
        for number, own in enumerate(w_yx)
    ]
    lines.append(LineGather(w_out, wout_all, *line[2 * parts_yx : 2 * parts_yx + 2]))
    for item in lines:
        item.begin()
    widen(gain, gain_row)

    def norm(row):
        values = tokens[pl.ds(row, CHUNK), :].astype(F32)
        scaled = values * rms_scale_of(values) * gain_row[...]
        normed_all[pl.ds(own_row(row, rows), CHUNK), :] = scaled.astype(BF16)

    chunks(rows, norm)
    gather = Gather(normed_all, rows, nbits, s0, r0)
    gather.begin()
    seg_own = pltpu.make_async_copy(seg, seg_all.at[me], l0.at[0])
    seg_own.start()
    seg_copies = [
        pltpu.make_async_remote_copy(
            src_ref=seg,
            dst_ref=seg_all.at[me],
            send_sem=s2.at[number],
            recv_sem=r2.at[number],
            device_id={"tensor": flipped(me, chosen)},
            device_id_type=MESH,
        )
        for number, chosen in enumerate(peers)
    ]
    for copy in seg_copies:
        copy.start()
    chips = lines[0].chips
    for item in lines:
        item.pass_on(1)
    gather.advance(0)
    for distance in range(2, chips):
        for item in lines:
            item.pass_on(distance)
    gather.finish(1)
    for item in lines:
        item.finish()
    for copy in seg_copies:
        copy.wait()
    seg_own.wait()


class Fetch:
    def __init__(self, nbits, cot, cot_all, s0, r0, l0):
        rows = cot.shape[0]
        own = pl.multiple_of(lax.axis_index("tensor") * rows, rows)
        self.local = pltpu.make_async_copy(cot, cot_all.at[pl.ds(own, rows), :], l0.at[0])
        self.gather = Gather(cot_all, rows, nbits, s0, r0)

    def begin(self):
        self.local.wait()
        self.gather.begin()

    def advance(self):
        self.gather.advance(0)

    def finish(self):
        self.gather.finish(1)


def fetch_scratch(nbits):
    return gather_sems(nbits) + [pltpu.SemaphoreType.DMA((1,))]


def fetch_kernel(nbits, cot, cot_all, *sems):
    greet(tensor_bits(nbits))
    fetch = Fetch(nbits, cot, cot_all, *sems)
    fetch.local.start()
    fetch.begin()
    fetch.advance()
    fetch.finish()


def middle_kernel(
    nbits, mixer, tokens, gain, middle, mid_all, landed, staged, s0, r0, s1, r1
):
    rows = tokens.shape[0]
    greet(tensor_bits(nbits))
    scatter = Scatter(mixer, landed, staged, rows, nbits, s0, r0)
    scatter.begin()
    scatter.run()

    def norm(row):
        values = tokens[pl.ds(row, CHUNK), :].astype(F32) + scatter.total(row, CHUNK)
        middle[pl.ds(row, CHUNK), :] = values
        scaled = values * rms_scale_of(values) * gain[...]
        mid_all[pl.ds(own_row(row, rows), CHUNK), :] = scaled.astype(BF16)

    chunks(rows, norm)
    gather = Gather(mid_all, rows, nbits, s1, r1)
    gather.begin()
    gather.finish()
    scatter.drain()


def result_kernel(nbits, ffn, middle, mixed, landed, staged, s0, r0):
    rows = middle.shape[0]
    greet(tensor_bits(nbits))
    scatter = Scatter(ffn, landed, staged, rows, nbits, s0, r0)
    scatter.begin()
    scatter.run()

    def add(row):
        values = middle[pl.ds(row, CHUNK), :] + scatter.total(row, CHUNK)
        mixed[pl.ds(row, CHUNK), :] = values.astype(BF16)

    chunks(rows, add)
    scatter.drain()


def norm_pull(values, gain, cotangent):
    scale = rms_scale_of(values)
    unit = values * scale
    inner = cotangent * gain
    back = scale * (inner - unit * jnp.mean(inner * unit, axis=-1, keepdims=True))
    return back, cotangent * unit


def eight_rows(values):
    total = values[0:8]
    for at in range(8, CHUNK, 8):
        total = total + values[at : at + 8]
    return total


class Product:
    def __init__(self, left, right, out, held, sems):
        self.left, self.right, self.out = left, right, out
        self.held, self.sems = held, sems
        self.width = held.shape[1]
        self.count = right.shape[0] // self.width
        self.done = 0

    def fetch(self, block):
        return pltpu.make_async_copy(
            self.right.at[pl.ds(block * self.width, self.width), :],
            self.held.at[block % 2],
            self.sems.at[block % 2],
        )

    def begin(self):
        self.fetch(0).start()

    def work(self, blocks):
        for block in range(self.done, min(self.done + blocks, self.count)):
            if block + 1 < self.count:
                self.fetch(block + 1).start()
            self.fetch(block).wait()

            def rows(span, block=block):
                found = times_transposed(self.left[span, :], self.held[block % 2])
                at = slice(block * self.width, (block + 1) * self.width)
                self.out[span, at] = found.astype(BF16)

            parts(self.left.shape[0], rows)
        self.done = min(self.done + blocks, self.count)


PRODUCT_BLOCK = 256


def product_scratch(depth):
    return [pltpu.VMEM((2, PRODUCT_BLOCK, depth), BF16), pltpu.SemaphoreType.DMA((2,))]


def turn_kernel(
    nbits,
    d_norm,
    cot,
    middle,
    gain,
    hidden,
    w_down,
    d_middle,
    d_mixer,
    d_gain,
    ffn,
    landed,
    staged,
    s0,
    r0,
    s1,
    r1,
    *product,
):
    rows = middle.shape[0]
    ahead = Product(hidden, w_down, ffn, *product)
    ahead.begin()
    greet(tensor_bits(nbits))
    scatter = Scatter(d_norm, landed, staged, rows, nbits, s0, r0)
    scatter.begin()
    d_gain[...] = jnp.zeros_like(d_gain)
    ahead.work(4)
    for step in range(nbits):
        scatter.advance(step)
        if step + 1 < nbits:
            ahead.work(2)

    def pull(row):
        span = pl.ds(row, CHUNK)
        back, gains = norm_pull(middle[span, :], gain[...], scatter.total(row, CHUNK))
        values = cot[span, :].astype(F32) + back
        d_middle[span, :] = values
        d_mixer[pl.ds(own_row(row, rows), CHUNK), :] = values.astype(BF16)
        d_gain[...] += eight_rows(gains)

    chunks(rows, pull)
    gather = Gather(d_mixer, rows, nbits, s1, r1)
    gather.begin()
    ahead.work(2)
    gather.advance(0)
    ahead.work(ahead.count)
    gather.finish(1)
    scatter.drain()


class LineSum:
    def __init__(self, whole, kept, swapped, staged, landed, send_sems, recv_sems, columns=None):
        self.whole, self.kept, self.swapped = whole, kept, swapped
        self.staged, self.landed = staged, landed
        self.sems = (send_sems, recv_sems)
        self.columns = columns
        self.chip, self.core, self.chips = dp_place()
        self.rows = whole.shape[2]

    def half(self, core):
        if self.columns is None:
            return self.whole.at[:, core]
        return self.whole.at[:, core, :, self.columns]

    def local(self):
        return pltpu.make_async_copy(
            self.half(self.core), self.kept, self.sems[0].at[2 * self.chips]
        )

    def swap(self):
        return pltpu.make_async_remote_copy(
            src_ref=self.half(1 - self.core),
            dst_ref=self.swapped,
            send_sem=self.sems[0].at[0],
            recv_sem=self.sems[1].at[0],
            device_id={"dp": dp_index(self.chip, 1 - self.core)},
            device_id_type=MESH,
        )

    def has(self, way, distance):
        return self.chip + distance < self.chips if way == UP else self.chip >= distance

    def slot(self, way, distance):
        return (0 if way == UP else self.chips - 1) + distance

    def hop(self, way, distance):
        return pltpu.make_async_remote_copy(
            src_ref=self.staged.at[self.slot(way, distance - 1)],
            dst_ref=self.landed.at[self.slot(way, distance - 1)],
            send_sem=self.sems[0].at[1 + self.slot(way, distance - 1)],
            recv_sem=self.sems[1].at[1 + self.slot(way, distance - 1)],
            device_id={"dp": dp_index(self.chip + way, self.core)},
            device_id_type=MESH,
        )

    def arrival(self, way, distance):
        number = self.slot(way, distance)
        return pltpu.make_async_remote_copy(
            src_ref=self.landed.at[number],
            dst_ref=self.landed.at[number],
            send_sem=self.sems[0].at[1 + number],
            recv_sem=self.sems[1].at[1 + number],
            device_id={"dp": dp_index(self.chip - way, self.core)},
            device_id_type=MESH,
        )

    def begin(self):
        self.swap().start()
        self.local().start()

    def both(self, chip, span):
        return self.kept[chip, span, :].astype(F32) + self.swapped[chip, span, :].astype(F32)

    def send(self, distance):
        if distance == self.chips - 1:
            self.local().wait()
            self.swap().wait_recv()
        for way in (UP, DOWN):

            @pl.when(self.has(way, distance))
            def _(way=way):
                chip = self.chip + way * distance
                slot = self.slot(way, distance - 1)

                def first(row):
                    span = pl.ds(row, CHUNK)
                    self.staged[slot, span, :] = self.both(chip, span).astype(BF16)

                def later(row):
                    span = pl.ds(row, CHUNK)
                    total = self.both(chip, span) + self.landed[
                        self.slot(way, distance), span, :
                    ].astype(F32)
                    self.staged[slot, span, :] = total.astype(BF16)

                if distance == self.chips - 1:
                    chunks(self.rows, first)
                else:

                    @pl.when(self.has(-way, 1))
                    def _():
                        self.arrival(way, distance).wait_recv()
                        chunks(self.rows, later)

                    @pl.when(jnp.logical_not(self.has(-way, 1)))
                    def _():
                        chunks(self.rows, first)

                self.hop(way, distance).start()

    def finish(self, store):
        below, above = self.has(DOWN, 1), self.has(UP, 1)

        def fill(slots):
            for way in slots:
                self.arrival(way, 0).wait_recv()

            def one(row):
                span = pl.ds(row, CHUNK)
                total = self.both(self.chip, span)
                for way in slots:
                    total = total + self.landed[self.slot(way, 0), span, :].astype(F32)
                store(span, total)

            chunks(self.rows, one)

        @pl.when(below & above)
        def _():
            fill((UP, DOWN))

        @pl.when(jnp.logical_not(above))
        def _():
            fill((UP,))

        @pl.when(jnp.logical_not(below))
        def _():
            fill((DOWN,))

    def drain(self):
        self.swap().wait_send()
        for way in (UP, DOWN):
            for distance in range(1, self.chips):

                @pl.when(self.has(way, distance))
                def _(way=way, distance=distance):
                    self.hop(way, distance).wait_send()


def line_scratch(ndp, rows, columns):
    chips = ndp // 2
    return [
        pltpu.VMEM((chips, rows, columns), BF16),
        pltpu.VMEM((chips, rows, columns), BF16),
        pltpu.VMEM((2 * chips - 2, rows, columns), BF16),
        pltpu.VMEM((2 * chips - 2, rows, columns), BF16),
        pltpu.SemaphoreType.DMA((2 * chips + 1,)),
        pltpu.SemaphoreType.DMA((2 * chips + 1,)),
    ]


RING = 6


def leave_kernel(nbits, tiled, *refs):
    refs = list(refs)

    def take(count):
        taken = refs[:count]
        del refs[:count]
        return taken

    d_norm, tokens, d_middle, gain, own_small, d_gain_mid = take(6)
    pieces = take(3)
    grad_input, sum_out, sum_y, sum_x, gate_all, small_all = take(6)
    landed, staged, s0, r0 = take(4)
    share = small_all.shape[2]
    gate = LineSum(pieces[0], *take(RING))
    lines = [LineSum(pieces[1], *take(RING))]
    if tiled:
        lines += [LineSum(pieces[2], *take(RING), pl.ds(at, share)) for at in (0, share)]
    else:
        lines += [LineSum(pieces[2], *take(RING))]
    d_gain, gains, gains_landed, small, small_landed = take(5)
    gain_s, gain_r, vec_s, vec_r, join_s, join_r, gate_s, gate_r = take(8)
    rows = tokens.shape[0]
    me = lax.axis_index("tensor")
    chip, core, chips = dp_place()
    peers = [chosen for chosen in subsets(tuple(range(nbits))) if chosen]
    others = [(shift, turn) for shift in range(chips) for turn in range(2)][1:]
    greet_peers(nbits, True, True)
    for line in [gate] + lines:
        line.begin()
    scatter = Scatter(d_norm, landed, staged, rows, nbits, s0, r0)
    scatter.begin()
    d_gain[...] = jnp.zeros_like(d_gain)
    far = list(range(chips - 1, 0, -1))
    for number in range(max(len(far), len(lines))):
        if number < len(far):
            gate.send(far[number])
        if number < len(lines):
            lines[number].send(far[0])
    scatter.advance(0)
    for distance in far[1:-1]:
        for line in lines:
            line.send(distance)
    for step in range(1, nbits):
        scatter.advance(step)

    def pull(row):
        span = pl.ds(row, CHUNK)
        back, parts = norm_pull(
            tokens[span, :].astype(F32), gain[...], scatter.total(row, CHUNK)
        )
        grad_input[span, :] = d_middle[span, :] + back
        d_gain[...] += eight_rows(parts)

    chunks(rows, pull)
    def store_gate(span, value):
        gate_all[me, chip, core, span, :] = value.astype(BF16)

    def gate_copy(number, ref, target):
        return pltpu.make_async_remote_copy(
            src_ref=ref,
            dst_ref=ref,
            send_sem=gate_s.at[number],
            recv_sem=gate_r.at[number],
            device_id=target,
            device_id_type=MESH,
        )

    def gate_line(shift):
        target = {"dp": dp_index((chip + shift) % chips, core)}
        return gate_copy(shift - 1, gate_all.at[me, chip, core], target)

    def gate_tensor(number, chosen):
        target = {"tensor": flipped(me, chosen)}
        return gate_copy(chips - 1 + number, gate_all.at[me, :, core], target)

    def gate_core():
        target = {"dp": dp_index(chip, 1 - core)}
        return gate_copy(chips - 1 + len(peers), gate_all.at[:, :, core], target)

    def start_gate():
        gate.finish(store_gate)
        for shift in range(1, chips):
            gate_line(shift).start()

    top = jnp.sum(d_gain[...], axis=0, keepdims=True)
    low = jnp.sum(d_gain_mid[...], axis=0, keepdims=True)
    place8 = lax.broadcasted_iota(jnp.int32, (8, share), 0)
    for index in range(1 << nbits):
        span = slice(index * share, (index + 1) * share)
        gains[index] = jnp.where(
            place8 == 6, top[:, span], jnp.where(place8 == 7, low[:, span], 0.0)
        )

    def gain_copy(number, chosen):
        peer = flipped(me, chosen)
        return pltpu.make_async_remote_copy(
            src_ref=gains.at[peer],
            dst_ref=gains_landed.at[number],
            send_sem=gain_s.at[number],
            recv_sem=gain_r.at[number],
            device_id={"tensor": peer},
            device_id_type=MESH,
        )

    for number, chosen in enumerate(peers):
        gain_copy(number, chosen).start()
    if len(far) > 1:
        for line in lines:
            line.send(far[-1])
    start_gate()
    total = own_small[...] + gains[me]
    for number, chosen in enumerate(peers):
        gain_copy(number, chosen).wait_recv()
        total = total + gains_landed[number]
    small[...] = total

    def vec_copy(number, shift, turn):
        other = dp_index((chip + shift) % chips, core + turn * (1 - 2 * core))
        return pltpu.make_async_remote_copy(
            src_ref=small,
            dst_ref=small_landed.at[number],
            send_sem=vec_s.at[number],
            recv_sem=vec_r.at[number],
            device_id={"dp": other},
            device_id_type=MESH,
        )

    for number, (shift, turn) in enumerate(others):
        vec_copy(number, shift, turn).start()

    for shift in range(1, chips):
        gate_line(shift).wait_recv()
    for number, chosen in enumerate(peers):
        gate_tensor(number, chosen).start()
    total = small[...]
    for number, (shift, turn) in enumerate(others):
        vec_copy(number, shift, turn).wait_recv()
        total = total + small_landed[number]
    small_all[me] = total

    def join_copy(number, chosen):
        return pltpu.make_async_remote_copy(
            src_ref=small_all.at[me],
            dst_ref=small_all.at[me],
            send_sem=join_s.at[number],
            recv_sem=join_r.at[number],
            device_id={"tensor": flipped(me, chosen)},
            device_id_type=MESH,
        )

    for number, chosen in enumerate(peers):
        join_copy(number, chosen).start()
    for number, chosen in enumerate(peers):
        gate_tensor(number, chosen).wait_recv()
    gate_core().start()

    def store_in(*targets):
        def store(span, value):
            for number, ref in enumerate(targets):
                ref[span, :] = value[:, number * share : (number + 1) * share]

        return store

    lines[0].finish(store_in(sum_out))
    if tiled:
        lines[1].finish(store_in(sum_y))
        lines[2].finish(store_in(sum_x))
    else:
        lines[1].finish(store_in(sum_y, sum_x))
    gate_core().wait()
    for shift in range(1, chips):
        gate_line(shift).wait_send()
    for number, chosen in enumerate(peers):
        gate_tensor(number, chosen).wait_send()
        gain_copy(number, chosen).wait_send()
        join_copy(number, chosen).wait()
    for number, (shift, turn) in enumerate(others):
        vec_copy(number, shift, turn).wait_send()
    scatter.drain()
    for line in [gate] + lines:
        line.drain()


def in_vmem(count):
    return [pl.BlockSpec(memory_space=pltpu.VMEM)] * count


def call_kernel(kernel, outs, scratch, number, *operands, far_in=(), far_out=(), cost_us=1):
    vmem = pl.BlockSpec(memory_space=pltpu.VMEM)
    far = pl.BlockSpec(memory_space=pl.ANY)
    return pl.pallas_call(
        kernel,
        out_shape=outs,
        in_specs=[far if i in far_in else vmem for i in range(len(operands))],
        out_specs=tuple(far if i in far_out else vmem for i in range(len(outs))),
        scratch_shapes=scratch,
        cost_estimate=pl.CostEstimate(
            flops=0, bytes_accessed=cost_us * 1_000_000, transcendentals=0
        ),
        compiler_params=pltpu.CompilerParams(
            collective_id=number, has_side_effects=True, vmem_limit_bytes=VMEM_BYTES
        ),
    )(*operands)


def sigmoid(values):
    return 1.0 / (1.0 + jnp.exp(-values))


def one_minus_exp(values):
    series = values / 7.0 + 1.0
    for order in (6.0, 5.0, 4.0, 3.0, 2.0):
        series = 1.0 + series * values / order
    return jnp.where(values > -0.3, -values * series, 1.0 - jnp.exp(values))


GELU_K = 0.7978845608028654
GELU_C = 0.044715


def gelu_parts(values):
    square = values * values
    bent = jnp.tanh(GELU_K * values * (1.0 + GELU_C * square))
    gelu = 0.5 * values * (1.0 + bent)
    slope = 0.5 * (1.0 + bent) + 0.5 * values * (1.0 - bent * bent) * GELU_K * (
        1.0 + 3.0 * GELU_C * square
    )
    return gelu, slope


def gate_terms(gate_a, gate_x, soft, since):
    sig_a = sigmoid(gate_a)
    sig_x = sigmoid(gate_x)
    log_decay = -8.0 * sig_a * soft
    decay = jnp.exp(log_decay)
    scale = jnp.sqrt(one_minus_exp(2.0 * log_decay))
    keep = since > 0.5
    return sig_a, sig_x, decay, jnp.where(keep, scale, 1.0), keep


def scan_down(decay, value, carry):
    place = lax.broadcasted_iota(jnp.int32, decay.shape, 0)
    for shift in (1, 2, 4):
        past = place >= shift
        moved = pltpu.roll(value, shift, 0)
        value = jnp.where(past, decay * moved + value, value)
        decay = jnp.where(past, decay * pltpu.roll(decay, shift, 0), decay)
    return decay * carry + value


def scan_up(decay, value, carry):
    place = lax.broadcasted_iota(jnp.int32, decay.shape, 0)
    factor = jnp.where(place < 7, pltpu.roll(decay, 7, 0), 1.0)
    for shift in (1, 2, 4):
        past = place < 8 - shift
        moved = pltpu.roll(value, 8 - shift, 0)
        value = jnp.where(past, factor * moved + value, value)
        factor = jnp.where(past, factor * pltpu.roll(factor, 8 - shift, 0), factor)
    return factor * carry + value


def forward_scan(conv_rows, gates, branch_y, soft, since, mixed, states, between=()):
    total_rows, width = states.shape

    def step(i, carry):
        row = pl.multiple_of(i * CHUNK, CHUNK)
        span = pl.ds(row, CHUNK)
        values = conv_rows(span).astype(F32)
        kept = []
        for at in range(0, CHUNK, 8):
            tile = pl.ds(row + at, 8)
            sig_a, sig_x, decay, scale, keep = gate_terms(
                gates[tile, :width], gates[tile, width:], soft[...], since[tile, :]
            )
            given = values[at : at + 8] * sig_x * scale
            state = scan_down(jnp.where(keep, decay, 0.0), given, carry)
            carry = state[7:8]
            states[tile, :] = state
            kept.append(state * gelu_parts(branch_y[tile, :])[0])
        mixed[span, :] = jnp.concatenate(kept, axis=0).astype(BF16)
        return carry

    steps, stretches = total_rows // CHUNK, len(between) + 1
    carry = jnp.zeros((1, width), F32)
    for stretch in range(stretches):
        first, last = stretch * steps // stretches, (stretch + 1) * steps // stretches
        carry = lax.fori_loop(first, last, step, carry)
        if stretch < len(between):
            between[stretch]()


def forward_scan_kernel(conv, gates, branch_y, soft, since, mixed, states):
    forward_scan(lambda span: conv[span, :], gates, branch_y, soft, since, mixed, states)


def backward_scan(
    d_mixed, conv_rows, gates, branch_y, states, soft, slope_soft, since, d_conv, d_gates, d_branch, d_decay
):
    total_rows, width = states.shape
    d_decay[...] = jnp.zeros_like(d_decay)

    def step(i, carry):
        row = pl.multiple_of(total_rows - CHUNK - i * CHUNK, CHUNK)
        span = pl.ds(row, CHUNK)
        values = conv_rows(span).astype(F32)
        kept = []
        for at in range(CHUNK - 8, -1, -8):
            tile = pl.ds(row + at, 8)
            soft_row = soft[...]
            sig_a, sig_x, decay, scale, keep = gate_terms(
                gates[tile, :width], gates[tile, width:], soft_row, since[tile, :]
            )
            value = values[at : at + 8]
            gelu, slope = gelu_parts(branch_y[tile, :])
            state = states[tile, :]
            upper = d_mixed[tile, :]
            held = jnp.where(keep, decay, 0.0)
            lam = scan_up(held, upper * gelu, carry)
            carry = held[0:1] * lam[0:1]
            d_conv[tile, :] = lam * sig_x * scale
            d_x = lam * value * scale * sig_x * (1.0 - sig_x)
            given = value * sig_x
            d_log = lam * (state - given * scale - given * decay * decay / scale)
            d_log = jnp.where(keep, d_log, 0.0)
            d_a = d_log * (-8.0 * soft_row) * sig_a * (1.0 - sig_a)
            d_decay[...] += d_log * (-8.0 * sig_a) * slope_soft[...]
            kept.append((d_a, d_x, upper * state * slope))
        kept = kept[::-1]
        d_gates[span, :width] = jnp.concatenate([k[0] for k in kept], axis=0).astype(BF16)
        d_gates[span, width:] = jnp.concatenate([k[1] for k in kept], axis=0).astype(BF16)
        d_branch[span, :] = jnp.concatenate([k[2] for k in kept], axis=0).astype(BF16)
        return carry

    lax.fori_loop(0, total_rows // CHUNK, step, jnp.zeros((1, width), F32))


def backward_scan_kernel(
    d_mixed, conv, gates, branch_y, states, soft, slope_soft, since, d_conv, d_gates, d_branch, d_decay
):
    backward_scan(
        d_mixed,
        lambda span: conv[span, :],
        gates,
        branch_y,
        states,
        soft,
        slope_soft,
        since,
        d_conv,
        d_gates,
        d_branch,
        d_decay,
    )


def times_transposed(left, right):
    return lax.dot_general(left, right, (((1,), (1,)), ((), ())), preferred_element_type=F32)


class HalfBlocks:
    def __init__(self, channels, block):
        self.odd = lax.axis_index("tensor") % 2
        self.half = block // 2
        self.block = block
        self.count = channels // block + 1
        self.channels = channels
        self.own = pl.multiple_of(self.odd * self.half, self.half)
        self.shared = (1 - self.odd) * (self.count - 1)
        self.mine_in_block = pl.multiple_of(self.odd * self.half, self.half)
        self.other_in_block = pl.multiple_of((1 - self.odd) * self.half, self.half)
        self.mine = pl.multiple_of((1 - self.odd) * (channels - self.half), self.half)
        self.pair = {"tensor": lax.axis_index("tensor") + 1 - 2 * self.odd}

    def full(self, index):
        block = index + self.odd
        return block, pl.multiple_of(index * self.block + self.odd * self.half, self.half)

    def span(self, block):
        return pl.ds(pl.multiple_of(block * self.block, self.block), self.block)

    def shared_part(self, start):
        return pl.ds(pl.multiple_of(self.shared * self.block + start, self.half), self.half)


PART = 256


def parts(rows, body):
    def step(i, carry):
        body(pl.ds(pl.multiple_of(i * PART, PART), PART))
        return carry

    lax.fori_loop(0, rows // PART, step, 0)


def recurrence_kernel(
    taps,
    nbits,
    branches,
    tap_rows,
    soft,
    since,
    weights,
    cot,
    mixed,
    states,
    window,
    gates,
    cot_all,
    send,
    recv,
    *sems,
):
    total_rows, width = states.shape
    block = weights.shape[2]
    place = HalfBlocks(width, block)
    branch_y, branch_x = branches.at[:, :width], branches.at[:, width:]
    greet(tensor_bits(nbits))
    fetch = Fetch(nbits, cot, cot_all, *sems)
    fetch.local.start()

    def conv(i, before):
        row = pl.multiple_of(i * CHUNK, CHUNK)
        kept = []
        for at in range(0, CHUNK, 8):
            tile = pl.ds(row + at, 8)
            values = branch_x[tile, :]
            line = lax.broadcasted_iota(jnp.int32, values.shape, 0)
            total = values * tap_rows[0:1, :]
            for tap in range(1, taps):
                moved = jnp.where(
                    line < tap, pltpu.roll(before, tap, 0), pltpu.roll(values, tap, 0)
                )
                moved = jnp.where(since[tile, :] > tap - 0.5, moved, 0.0)
                total = total + moved * tap_rows[tap : tap + 1, :]
            kept.append(total)
            before = values
        window[pl.ds(row, CHUNK), pl.ds(place.own, width)] = jnp.concatenate(
            kept, axis=0
        ).astype(BF16)
        return before

    lax.fori_loop(0, total_rows // CHUNK, conv, jnp.zeros((8, width), F32))
    source = window.at[:, place.shared_part(place.mine_in_block)]
    away = pl.multiple_of(place.odd * (place.count - 1) * block + place.mine_in_block, place.half)
    rim = pltpu.make_async_remote_copy(
        src_ref=source,
        dst_ref=window.at[:, pl.ds(away, place.half)],
        send_sem=send.at[0],
        recv_sem=recv.at[0],
        device_id=place.pair,
        device_id_type=MESH,
    )
    rim.start()
    fetch.begin()

    def full(span):
        for index in range(place.count - 1):
            number, at = place.full(index)
            cells = window[span, place.span(number)]
            for s in range(2):
                gates[span, pl.ds(s * width + at, block)] = jnp.dot(
                    cells, weights[s, number], preferred_element_type=F32
                )

    parts(total_rows, full)
    rim.wait()

    def shared(span):
        cells = window[span, place.span(place.shared)]
        for s in range(2):
            gates[span, pl.ds(s * width + place.mine, place.half)] = jnp.dot(
                cells,
                weights[s, place.shared, :, pl.ds(place.mine_in_block, place.half)],
                preferred_element_type=F32,
            )

    parts(total_rows, shared)
    forward_scan(
        lambda span: window[span, pl.ds(place.own, width)],
        gates,
        branch_y,
        soft,
        since,
        mixed,
        states,
        [fetch.advance],
    )
    fetch.finish()


def recurrence_back_kernel(
    taps,
    nbits,
    with_ffn,
    d_mixed,
    window,
    gates,
    branches,
    states,
    tap_rows,
    soft,
    slope_soft,
    since,
    weights,
    *refs,
):
    refs = list(refs)

    def take(count):
        taken = refs[:count]
        del refs[:count]
        return taken

    ffn, middle = take(2) if with_ffn else (None, None)
    d_branches, gate_grad, own_small = take(3)
    mixed = take(1)[0] if with_ffn else None
    d_conv, d_gates, given, taken, sums, send, recv = take(7)
    total_rows, width = states.shape
    block = weights.shape[2]
    place = HalfBlocks(width, block)
    half = place.half
    branch_y, branch_x = branches.at[:, :width], branches.at[:, width:]
    d_branch_y, d_branch_x = d_branches.at[:, :width], d_branches.at[:, width:]
    greet(tensor_bits(nbits))
    if with_ffn:
        scatter = Scatter(ffn, *take(2), middle.shape[0], nbits, *take(2))
        scatter.begin()
    backward_scan(
        d_mixed,
        lambda span: window[span, pl.ds(place.own, width)],
        gates,
        branch_y,
        states,
        soft,
        slope_soft,
        since,
        d_conv,
        d_gates,
        d_branch_y,
        sums.at[taps],
    )

    def to_pair(span):
        total = jnp.zeros((PART, half), F32)
        for s in range(2):
            total = total + times_transposed(
                d_gates[span, pl.ds(s * width + place.mine, half)],
                weights[
                    s,
                    place.shared,
                    pl.ds(place.other_in_block, half),
                    pl.ds(place.mine_in_block, half),
                ],
            )
        given[span, :] = total.astype(BF16)

    parts(total_rows, to_pair)
    rim = pltpu.make_async_remote_copy(
        src_ref=given,
        dst_ref=taken,
        send_sem=send.at[0],
        recv_sem=recv.at[0],
        device_id=place.pair,
        device_id_type=MESH,
    )
    rim.start()

    def full(span):
        for index in range(place.count - 1):
            number, at = place.full(index)
            total = d_conv[span, pl.ds(at, block)]
            for s in range(2):
                total = total + times_transposed(
                    d_gates[span, pl.ds(s * width + at, block)], weights[s, number]
                )
            d_conv[span, pl.ds(at, block)] = total
        total = d_conv[span, pl.ds(place.mine, half)]
        for s in range(2):
            total = total + times_transposed(
                d_gates[span, pl.ds(s * width + place.mine, half)],
                weights[
                    s,
                    place.shared,
                    pl.ds(place.mine_in_block, half),
                    pl.ds(place.mine_in_block, half),
                ],
            )
        d_conv[span, pl.ds(place.mine, half)] = total

    parts(total_rows, full)
    if with_ffn:
        scatter.advance(0)
    units = width // half
    for index in range(units):
        number = (index + place.odd) // 2
        cells = window[:, place.span(number)]
        both = jnp.concatenate(
            [d_gates[:, s * width + index * half : s * width + (index + 1) * half] for s in range(2)],
            axis=1,
        )
        found = lax.dot_general(
            cells, both, (((0,), (0,)), ((), ())), preferred_element_type=F32
        ).astype(BF16)
        gate_grad[2 * index] = found[:, :half]
        gate_grad[2 * index + 1] = found[:, half:]
    rim.wait()

    def add(span):
        d_conv[span, pl.ds(place.mine, half)] += taken[span, :].astype(F32)

    parts(total_rows, add)
    for tap in range(taps):
        sums[tap] = jnp.zeros((8, width), F32)

    def conv(i, after):
        row = pl.multiple_of(total_rows - CHUNK - i * CHUNK, CHUNK)
        kept = []
        for at in range(CHUNK - 8, -1, -8):
            tile = pl.ds(row + at, 8)
            values = d_conv[tile, :]
            line = lax.broadcasted_iota(jnp.int32, values.shape, 0)
            below = branch_x[tile, :]
            higher = pl.multiple_of((row + at - 8 + total_rows) % total_rows, 8)
            above = branch_x[pl.ds(higher, 8), :]
            total = values * tap_rows[0:1, :]
            sums[0] += values * below
            masked = []
            for tap in range(1, taps):
                here = jnp.where(since[tile, :] > tap - 0.5, values, 0.0)
                masked.append(here)
                moved = jnp.where(
                    line < 8 - tap,
                    pltpu.roll(here, 8 - tap, 0),
                    pltpu.roll(after[tap - 1], 8 - tap, 0),
                )
                total = total + moved * tap_rows[tap : tap + 1, :]
                source = jnp.where(
                    line < tap, pltpu.roll(above, tap, 0), pltpu.roll(below, tap, 0)
                )
                sums[tap] += here * source
            after = tuple(masked)
            kept.append(total)
        d_branch_x[pl.ds(row, CHUNK), :] = jnp.concatenate(kept[::-1], axis=0).astype(BF16)
        return after

    none = jnp.zeros((8, width), F32)
    lax.fori_loop(0, total_rows // CHUNK, conv, (none,) * (taps - 1))
    line = lax.broadcasted_iota(jnp.int32, (8, width), 0)
    total = jnp.zeros((8, width), F32)
    for tap in range(taps + 1):
        row = jnp.sum(sums[tap], axis=0, keepdims=True)
        total = jnp.where(line == tap, row, total)
    own_small[...] = total
    if with_ffn:
        for step in range(1, nbits):
            scatter.advance(step)

        def result(row):
            span = pl.ds(row, CHUNK)
            mixed[span, :] = (middle[span, :] + scatter.total(row, CHUNK)).astype(BF16)

        chunks(middle.shape[0], result)
        scatter.drain()


def finish_kernel(
    taps,
    gates,
    small,
    in_out,
    in_y,
    in_x,
    in_grad,
    in_mixed,
    in_both,
    in_down,
    whole,
    out_out,
    out_y,
    out_x,
    out_grad,
    out_mixed,
    out_gate,
    out_up,
    out_down,
    conv,
    decay,
    gain_in,
    gain_mid,
):
    held = whole.shape[1]
    pieces = gates.shape[0] // held

    def block(n, carry):
        for piece in range(pieces):
            for s in range(2):
                whole[s, n, :, piece * 128 : (piece + 1) * 128] = gates[
                    n * pieces + piece, s
                ].astype(F32)
        return carry

    lax.fori_loop(0, held, block, 0)
    units = out_gate.shape[1]

    def copy(row):
        span = pl.ds(row, CHUNK)
        out_out[span, :] = in_out[span, :].astype(F32)
        out_y[span, :] = in_y[span, :]
        out_x[span, :] = in_x[span, :]
        out_gate[span, :] = in_both[span, :units].astype(F32)
        out_up[span, :] = in_both[span, units:].astype(F32)
        out_down[span, :] = in_down[span, :].astype(F32)

    chunks(out_out.shape[0], copy)

    def own(row):
        span = pl.ds(row, CHUNK)
        out_grad[span, :] = in_grad[span, :]
        out_mixed[span, :] = in_mixed[span, :]

    chunks(out_grad.shape[0], own)

    @pl.when(pl.program_id(0) == 0)
    def _():
        share = small.shape[2]
        for index in range(small.shape[0]):
            span = slice(index * share, (index + 1) * share)
            conv[:, span] = small[index, :taps, :]
            for at in range(0, share, 128):
                row = (index * share + at) // 128
                decay[row : row + 1, :] = small[index, taps : taps + 1, at : at + 128]
                gain_in[row : row + 1, :] = small[index, 6:7, at : at + 128]
                gain_mid[row : row + 1, :] = small[index, 7:8, at : at + 128]


def finish(gate_all, small_all, sums, grad_input, mixed, both, down, taps, gate_shape):
    _, blocks, block, _ = gate_shape
    unit = gate_all.shape[-1]
    pieces = block // unit
    width = small_all.shape[0] * small_all.shape[2]
    rows, units = down.shape
    own_rows = grad_input.shape[0]
    grid = 2
    steps, held = rows // grid, own_rows // grid
    if unit != 128 or blocks % grid or rows % (16 * grid) or own_rows % (16 * grid):
        whole = gate_all.reshape(blocks, pieces, 2, block, unit).transpose(2, 0, 3, 1, 4)
        summed = small_all.transpose(1, 0, 2).reshape(8, width)
        whole = whole.reshape(gate_shape).astype(F32)
        wide = tuple(one.astype(F32) for one in (both[:, :units], both[:, units:], down))
        last = (summed[:taps], summed[taps], summed[6], summed[7])
        sums = tuple(one.astype(F32) for one in sums)
        return (whole, *sums, grad_input, mixed, *wide, *last)
    shape = jax.ShapeDtypeStruct

    def by_rows(count, columns):
        return pl.BlockSpec((count, columns), lambda n: (n, 0))

    def by_held(columns):
        return pl.BlockSpec((held, columns), lambda n: (n, 0))

    def whole_array(*dims):
        return pl.BlockSpec(dims, lambda n: (0,) * len(dims))

    columns = sums[0].shape[1]
    d_width = grad_input.shape[1]
    lines = width // 128
    found = pl.pallas_call(
        partial(finish_kernel, taps),
        grid=(grid,),
        in_specs=[
            pl.BlockSpec((blocks // grid * pieces, 2, block, unit), lambda n: (n, 0, 0, 0)),
            whole_array(*small_all.shape),
        ]
        + [by_rows(steps, columns)] * 3
        + [by_held(d_width)] * 2
        + [by_rows(steps, 2 * units), by_rows(steps, units)],
        out_specs=(
            (pl.BlockSpec((2, blocks // grid, block, block), lambda n: (0, n, 0, 0)),)
            + (by_rows(steps, columns),) * 3
            + (by_held(d_width),) * 2
            + (by_rows(steps, units),) * 3
            + (whole_array(taps, width),)
            + (whole_array(lines, 128),) * 3
        ),
        out_shape=(
            (shape(gate_shape, F32),)
            + (shape((rows, columns), F32),) * 3
            + (shape(grad_input.shape, F32), shape(mixed.shape, BF16))
            + (shape((rows, units), F32),) * 3
            + (shape((taps, width), F32),)
            + (shape((lines, 128), F32),) * 3
        ),
        compiler_params=pltpu.CompilerParams(vmem_limit_bytes=VMEM_BYTES),
    )(
        gate_all.reshape(blocks * pieces, 2, block, unit),
        small_all,
        *sums,
        grad_input,
        mixed,
        both,
        down,
    )
    return found[:10] + tuple(one.reshape(width) for one in found[10:])


def scan_call(kernel, outs, *operands):
    return pl.pallas_call(
        kernel,
        out_shape=outs,
        in_specs=in_vmem(len(operands)),
        out_specs=tuple(in_vmem(len(outs))),
        compiler_params=pltpu.CompilerParams(vmem_limit_bytes=VMEM_BYTES),
    )(*operands)


class Rim:
    def __init__(self, route, back, source, first, width, room):
        self.route, self.back = route, back
        self.source, self.first, self.width = source, first, width
        self.room = room

    def fetch(self, values):
        part = lax.dynamic_slice_in_dim(values, self.source, self.width, 1)
        return lax.ppermute(part, "tensor", self.route)

    def give(self, part):
        return lax.ppermute(part, "tensor", self.back)

    def add(self, values, part):
        zeros = jnp.zeros(values.shape, F32)
        return values + lax.dynamic_update_slice_in_dim(
            zeros, part.astype(F32), self.source, 1
        )

    def window(self, channels):
        return (channels // self.width + 4) * self.width


def gate_rims(channels, block_size, ntensor, offset):
    up = [(i, i + 1) for i in range(ntensor - 1)]
    down = [(i + 1, i) for i in range(ntensor - 1)]
    last = jnp.int32(channels - block_size)
    return [
        Rim(up, down, last, offset - block_size, block_size, block_size),
        Rim(down, up, jnp.int32(0), offset + channels, block_size, block_size),
    ]


def same_block(first, count, offset, channels, block_size):
    rows = (first + jnp.arange(count, dtype=jnp.int32))[:, None]
    columns = (offset + jnp.arange(channels, dtype=jnp.int32))[None, :]
    return (rows + block_size) // block_size == (columns + block_size) // block_size


def gate_dense(gate_w, offset, first, count):
    block_size = gate_w.shape[2]
    total = gate_w.shape[1] * block_size
    channels = total // lax.axis_size("tensor")
    columns = gate_w.transpose(2, 0, 1, 3).reshape(block_size, 2, total)
    columns = lax.dynamic_slice_in_dim(columns, offset, channels, 2)
    copies = -(-count // block_size) + 1
    tall = jnp.concatenate([columns] * copies, axis=0)
    tall = lax.dynamic_slice_in_dim(tall, (first + block_size) % block_size, count, 0)
    same = same_block(first, count, offset, channels, block_size)
    dense = jnp.where(same[:, None, :], tall, jnp.zeros_like(tall))
    return dense.reshape(count, 2 * channels)


def doc_starts(seg_ids, seq_len):
    places = jnp.arange(seg_ids.shape[0], dtype=jnp.int32)
    before = jnp.concatenate([seg_ids[:1], seg_ids[:-1]])
    resets = (places % seq_len == 0) | (seg_ids != before)
    starts = lax.cummax(jnp.where(resets, places, jnp.zeros_like(places)), axis=0)
    return starts


def causal_conv(starts, values, kernel):
    places = jnp.arange(values.shape[0], dtype=jnp.int32)
    total = values * kernel[0]
    for offset_k in range(1, kernel.shape[0]):
        moved = jnp.concatenate(
            [jnp.zeros((offset_k, values.shape[1]), values.dtype), values[:-offset_k]], axis=0
        )
        valid = (places - offset_k >= starts)[:, None]
        total = total + jnp.where(valid, moved, jnp.zeros_like(moved)) * kernel[offset_k]
    return total


def geglu(gate_val, up_val):
    return jax.nn.gelu(gate_val, approximate=True) * up_val


def rows_times(left, right):
    return lax.dot_general(left, right, (((1,), (1,)), ((), ())), preferred_element_type=F32)


def rows_back(lefts, rights):
    total = rows_times(lefts[0], rights[0])
    return total + rows_times(lefts[1], rights[1])


def inner_rows(left, right):
    return lax.dot_general(left, right, (((0,), (0,)), ((), ())), preferred_element_type=F32)


def halved(grad, ndp):
    return grad.reshape(ndp // 2, 2, grad.shape[0] // ndp, grad.shape[1])


def body(
    tokens,
    segments,
    cotangent,
    norm_gain,
    w_y,
    w_x,
    conv_w,
    gate_w,
    decay_param,
    w_out,
    mlp_gain,
    w_gate,
    w_up,
    w_down,
):
    ntensor = lax.axis_size("tensor")
    ndp = lax.axis_size("dp")
    nbits = log2_of(ntensor)
    tindex = lax.axis_index("tensor")
    own_rows, width = tokens.shape
    group_rows = own_rows * ntensor
    block_size = gate_w.shape[2]
    nblocks = gate_w.shape[1]
    dp_rows, channels = w_y.shape
    taps = conv_w.shape[0]
    offset = tindex * channels
    shape = jax.ShapeDtypeStruct
    gain_in = norm_gain.reshape(1, width)
    gain_mid = mlp_gain.reshape(1, width)
    seg_rows_of = own_rows // 128
    tiled = channels % 128 == 0
    w_yx = (w_y, w_x) if tiled else (jnp.concatenate([w_y, w_x], axis=1),)
    normed_rows, seg_all, wyx_loc, wout_loc = call_kernel(
        partial(enter_kernel, nbits, len(w_yx)),
        (
            shape((group_rows, width), BF16),
            shape((ntensor, seg_rows_of, 128), jnp.int32),
            shape((dp_rows * ndp, 2 * channels), BF16),
            shape((dp_rows * ndp, channels), BF16),
        ),
        [pltpu.VMEM((1, width), F32)]
        + gather_sems(nbits)
        + [pltpu.SemaphoreType.DMA((ntensor - 1,)), pltpu.SemaphoreType.DMA((ntensor - 1,))]
        + [pltpu.SemaphoreType.DMA((1,))]
        + line_sems(ndp) * (len(w_yx) + 1),
        0,
        tokens,
        segments.reshape(seg_rows_of, 128),
        norm_gain.reshape(width // 128, 128),
        *w_yx,
        w_out,
        far_in=tuple(range(3, 4 + len(w_yx))),
        far_out=(2, 3),
    )
    units = w_gate.shape[1]
    w_both = jnp.concatenate([w_gate, w_up], axis=1)
    w_both, w_down, normed_rows = lax.optimization_barrier((w_both, w_down, normed_rows))
    both_loc = lax.all_gather(w_both, "dp", axis=0, tiled=True)
    wd_loc = lax.all_gather(w_down, "dp", axis=0, tiled=True)
    seg_rows = seg_all.reshape(group_rows)
    starts = doc_starts(seg_rows, group_rows)
    conv_loc = lax.dynamic_slice_in_dim(conv_w, offset, channels, 1)
    decay_loc = lax.dynamic_slice_in_dim(decay_param, offset, channels, 0).reshape(1, channels)
    soft = jax.nn.softplus(decay_loc)
    slope_soft = jax.nn.sigmoid(decay_loc)
    half_blocks = (
        channels % block_size == block_size // 2 and ntensor % 2 == 0 and block_size % 256 == 0
    )
    since = (jnp.arange(group_rows, dtype=jnp.int32) - starts).astype(F32)[:, None]
    branches = jnp.dot(normed_rows, wyx_loc, preferred_element_type=F32)
    if half_blocks:
        span_blocks = channels // block_size + 1
        w_window = lax.dynamic_slice_in_dim(gate_w, offset // block_size, span_blocks, 1)
        taps_pad = jnp.concatenate([conv_loc, jnp.zeros((8 - taps, channels), F32)], axis=0)
        mixed_low, states, window, gate_pre, cot_rows = call_kernel(
            partial(recurrence_kernel, taps, nbits),
            (
                shape((group_rows, channels), BF16),
                shape((group_rows, channels), F32),
                shape((group_rows, span_blocks * block_size), BF16),
                shape((group_rows, 2 * channels), F32),
                shape((group_rows, width), BF16),
            ),
            [pltpu.SemaphoreType.DMA((1,)), pltpu.SemaphoreType.DMA((1,))]
            + fetch_scratch(nbits),
            5,
            branches,
            taps_pad,
            soft,
            since,
            w_window,
            cotangent,
        )
    else:
        branch_y, branch_x = branches[:, :channels], branches[:, channels:]
        (cot_rows,) = call_kernel(
            partial(fetch_kernel, nbits),
            (shape((group_rows, width), BF16),),
            fetch_scratch(nbits),
            5,
            cotangent,
        )
        rims = gate_rims(channels, block_size, ntensor, offset)
        own_dense = gate_dense(gate_w, offset, offset, channels)
        rim_dense = [gate_dense(gate_w, offset, rim.first, rim.width) for rim in rims]
        conv_out, conv_pull = jax.vjp(partial(causal_conv, starts), branch_x, conv_loc)
        conv_low = conv_out.astype(BF16)
        rim_cells = [rim.fetch(conv_low) for rim in rims]
        gate_pre = jnp.dot(conv_low, own_dense, preferred_element_type=F32)
        for cells, dense in zip(rim_cells, rim_dense):
            gate_pre = gate_pre + jnp.dot(cells, dense, preferred_element_type=F32)
        mixed_low, states = scan_call(
            forward_scan_kernel,
            (shape((group_rows, channels), BF16), shape((group_rows, channels), F32)),
            conv_low,
            gate_pre,
            branch_y,
            soft,
            since,
        )
    middle, mid_rows = call_kernel(
        partial(middle_kernel, nbits),
        (shape((own_rows, width), F32), shape((group_rows, width), BF16)),
        scatter_scratch(own_rows, width, nbits) + gather_sems(nbits),
        1,
        rows_times(mixed_low, wout_loc).astype(BF16),
        tokens,
        gain_mid,
    )
    pre = jnp.dot(mid_rows, both_loc, preferred_element_type=F32)
    hidden, act_pull = jax.vjp(geglu, pre[:, :units], pre[:, units:])
    hidden_low = hidden.astype(BF16)
    grad_wd = inner_rows(cot_rows, hidden_low).astype(BF16)
    sum_wd = lax.psum_scatter(grad_wd, "dp", scatter_dimension=0, tiled=True)
    grad_wd, wd_loc = lax.optimization_barrier((grad_wd, wd_loc))
    d_hidden = jnp.dot(cot_rows, wd_loc, preferred_element_type=F32)
    d_gate, d_up = act_pull(d_hidden)
    d_pre = jnp.concatenate([d_gate.astype(BF16), d_up.astype(BF16)], axis=1)
    grad_both = inner_rows(mid_rows, d_pre).astype(BF16)
    sum_both = lax.psum_scatter(grad_both, "dp", scatter_dimension=0, tiled=True)
    d_pre, grad_both = lax.optimization_barrier((d_pre, grad_both))
    d_mid_part = rows_times(d_pre, both_loc).astype(BF16)
    d_middle, d_mixer, d_gain_mid, ffn_part = call_kernel(
        partial(turn_kernel, nbits),
        (
            shape((own_rows, width), F32),
            shape((group_rows, width), BF16),
            shape((8, width), F32),
            shape((group_rows, width), BF16),
        ),
        scatter_scratch(own_rows, width, nbits) + gather_sems(nbits) + product_scratch(units),
        2,
        d_mid_part,
        cotangent,
        middle,
        gain_mid,
        hidden_low,
        wd_loc,
        far_in=(5,),
    )
    d_mixer, sum_wd = lax.optimization_barrier((d_mixer, sum_wd))
    d_mixed_in = jnp.dot(d_mixer, wout_loc, preferred_element_type=F32)
    unit = math.gcd(channels, block_size)
    merged = half_blocks and nbits <= 2
    if half_blocks:
        found = call_kernel(
            partial(recurrence_back_kernel, taps, nbits, merged),
            (
                shape((group_rows, 2 * channels), BF16),
                shape((channels // unit * 2, block_size, unit), BF16),
                shape((8, channels), F32),
            )
            + ((shape((own_rows, width), BF16),) if merged else ()),
            [
                pltpu.VMEM((group_rows, channels), F32),
                pltpu.VMEM((group_rows, 2 * channels), BF16),
                pltpu.VMEM((group_rows, unit), BF16),
                pltpu.VMEM((group_rows, unit), BF16),
                pltpu.VMEM((taps + 1, 8, channels), F32),
                pltpu.SemaphoreType.DMA((1,)),
                pltpu.SemaphoreType.DMA((1,)),
            ]
            + (scatter_scratch(own_rows, width, nbits) if merged else []),
            6,
            d_mixed_in,
            window,
            gate_pre,
            branches,
            states,
            taps_pad,
            soft,
            slope_soft,
            since,
            w_window,
            *((ffn_part, middle) if merged else ()),
        )
        d_branches, gate_grad, own_small = found[:3]
        gate_grad = gate_grad.reshape(channels // unit * 2 * block_size, unit)
    else:
        d_conv, d_gate_low, d_branch_y, d_decay = scan_call(
            backward_scan_kernel,
            (
                shape((group_rows, channels), F32),
                shape((group_rows, 2 * channels), BF16),
                shape((group_rows, channels), BF16),
                shape((8, channels), F32),
            ),
            d_mixed_in,
            conv_low,
            gate_pre,
            branch_y,
            states,
            soft,
            slope_soft,
            since,
        )
        given = [rows_times(d_gate_low, dense).astype(BF16) for dense in rim_dense]
        taken = [rim.give(part) for rim, part in zip(rims, given)]
        d_conv_out = d_conv + rows_times(d_gate_low, own_dense)
        for rim, part in zip(rims, taken):
            d_conv_out = rim.add(d_conv_out, part)
        d_branch_x, grad_conv_loc = conv_pull(d_conv_out)
        d_branches = jnp.concatenate([d_branch_y, d_branch_x.astype(BF16)], axis=1)
        base = offset // block_size * block_size - rims[0].room
        window_rows = rims[0].window(channels)
        picked = jnp.zeros((window_rows, 2 * channels), F32)
        for first, cells in [(offset, conv_low)] + [(r.first, c) for r, c in zip(rims, rim_cells)]:
            part = inner_rows(cells, d_gate_low)
            same = same_block(first, cells.shape[1], offset, channels, block_size)
            part = jnp.where(jnp.concatenate([same, same], axis=1), part, 0.0)
            picked = lax.dynamic_update_slice(picked, part, (first - base, jnp.int32(0)))
        picked = picked.reshape(window_rows // block_size, block_size, 2, channels // unit, unit)
        gate_grad = picked.sum(axis=0).astype(BF16).transpose(2, 1, 0, 3)
        gate_grad = gate_grad.reshape(channels // unit * 2 * block_size, unit)
        own_small = jnp.concatenate(
            [
                grad_conv_loc,
                jnp.sum(d_decay, axis=0, keepdims=True),
                jnp.zeros((7 - taps, channels), F32),
            ],
            axis=0,
        )

    grad_wout = inner_rows(d_mixer, mixed_low).astype(BF16)
    grad_wyx = inner_rows(normed_rows, d_branches).astype(BF16)
    d_normed = rows_times(d_branches, wyx_loc).astype(BF16)
    d_normed, grad_wyx, sum_both = lax.optimization_barrier((d_normed, grad_wyx, sum_both))

    pieces = [halved(grad, ndp) for grad in (gate_grad, grad_wout, grad_wyx)]
    peers = ntensor - 1
    gate_rows = gate_grad.shape[0] // ndp
    dma = pltpu.SemaphoreType.DMA
    scratch = scatter_scratch(own_rows, width, nbits)
    scratch += line_scratch(ndp, gate_rows, unit) + line_scratch(ndp, dp_rows, channels)
    if tiled:
        scratch += line_scratch(ndp, dp_rows, channels) * 2
    else:
        scratch += line_scratch(ndp, dp_rows, 2 * channels)
    scratch += [
        pltpu.VMEM((8, width), F32),
        pltpu.VMEM((ntensor, 8, channels), F32),
        pltpu.VMEM((peers, 8, channels), F32),
        pltpu.VMEM((8, channels), F32),
        pltpu.VMEM((ndp - 1, 8, channels), F32),
    ]
    scratch += [dma((peers,)), dma((peers,)), dma((ndp - 1,)), dma((ndp - 1,))]
    scratch += [dma((peers,)), dma((peers,)), dma((peers + ndp,)), dma((peers + ndp,))]
    grad_input, sum_wout, sum_wy, sum_wx, gate_all, small_all = call_kernel(
        partial(leave_kernel, nbits, tiled),
        (shape((own_rows, width), F32),)
        + (shape((dp_rows, channels), F32),) * 3
        + (
            shape((ntensor, ndp // 2, 2, gate_rows, unit), BF16),
            shape((ntensor, 8, channels), F32),
        ),
        scratch,
        3,
        d_normed,
        tokens,
        d_middle,
        gain_in,
        own_small,
        d_gain_mid,
        *pieces,
        far_in=(6, 7, 8),
    )
    if merged:
        mixed = found[3]
    else:
        (mixed,) = call_kernel(
            partial(result_kernel, nbits),
            (shape((own_rows, width), BF16),),
            scatter_scratch(own_rows, width, nbits),
            4,
            ffn_part,
            middle,
        )
    found = finish(
        gate_all,
        small_all,
        (sum_wout, sum_wy, sum_wx),
        grad_input,
        mixed,
        sum_both,
        sum_wd,
        taps,
        gate_w.shape,
    )
    sum_gate, sum_wout, sum_wy, sum_wx, grad_input, mixed = found[:6]
    sum_wg, sum_wu, sum_wd, sum_conv, sum_decay, sum_gain_in, sum_gain_mid = found[6:]
    return (
        mixed,
        grad_input,
        sum_gain_in,
        sum_wy,
        sum_wx,
        sum_conv,
        sum_gate,
        sum_decay,
        sum_wout,
        sum_gain_mid,
        sum_wg,
        sum_wu,
        sum_wd,
    )


def solution(mesh):
    split = P(("dp", "tensor"), None)
    weight = P("dp", "tensor")
    return jax.shard_map(
        body,
        mesh=mesh,
        in_specs=(
            split,
            P(("dp", "tensor")),
            split,
            P(),
            weight,
            weight,
            P(),
            P(),
            P(),
            weight,
            P(),
            weight,
            weight,
            weight,
        ),
        out_specs=(
            split,
            split,
            P(),
            weight,
            weight,
            P(),
            P(),
            P(),
            weight,
            P(),
            weight,
            weight,
            weight,
        ),
        check_vma=False,
    )
```
